32 devices in a mesh: seq: 8 (over z, core), fsdp: 4 (over y, x).
Axes of the slice: x: 2, y: 2, z: 4, core: 2. Of those that a mesh axis runs over, the one named last changes fastest.
Arguments:
- hidden: bfloat16 [4, 1280, 2048], P('fsdp', 'seq'), may hold values from -6 to 6
- lengths: int32 [4, 4], replicated, may hold values from 1 to 1024, 1280 in all within a row
- w_input: bfloat16 [2048, 2048], P(None, 'fsdp'), may hold values from -0.125 to 0.125
- w_forget: bfloat16 [2048, 2048], P(None, 'fsdp'), may hold values from -0.125 to 0.125
- w_gate_out: bfloat16 [2048, 2048], P(None, 'fsdp'), may hold values from -0.125 to 0.125
- w_output: bfloat16 [2048, 2048], P('fsdp'), may hold values from -0.25 to 0.25
- norm_gain: float32 [2048], replicated, may hold values from 0.5 to 1.5
- gate_gain: float32 [2048], replicated, may hold values from 0.5 to 1.5
- glu_gain: float32 [2048], replicated, may hold values from 0.5 to 1.5
- lower_table: float32 [24, 2048], replicated, may hold values from -12 to 12
- w_glu_gate: bfloat16 [2048, 5632], P(None, 'fsdp'), may hold values from -0.125 to 0.125
- w_glu_up: bfloat16 [2048, 5632], P(None, 'fsdp'), may hold values from -0.125 to 0.125
- w_glu_down: bfloat16 [5632, 2048], P('fsdp'), may hold values from -0.15625 to 0.15625
- cotangent: bfloat16 [4, 1280, 2048], P('fsdp', 'seq'), may hold values from -6 to 6
Outputs:
- output: bfloat16 [4, 1280, 2048], P('fsdp', 'seq')
- grad_hidden: bfloat16 [4, 1280, 2048], P('fsdp', 'seq')
- grad_w_input: float32 [2048, 2048], P('seq', 'fsdp')
- grad_w_forget: float32 [2048, 2048], P('seq', 'fsdp')
- grad_w_gate_out: float32 [2048, 2048], P('seq', 'fsdp')
- grad_w_output: float32 [2048, 2048], P('fsdp', 'seq')
- grad_norm_gain: float32 [2048], replicated
- grad_gate_gain: float32 [2048], replicated
- grad_glu_gain: float32 [2048], replicated
- grad_lower_table: float32 [24, 2048], replicated
- grad_glu_gate: float32 [2048, 5632], P('seq', 'fsdp')
- grad_glu_up: float32 [2048, 5632], P('seq', 'fsdp')
- grad_glu_down: float32 [5632, 2048], P('fsdp', 'seq')
The draws below stay inside these ranges and needn't reach their ends.
Inputs may be any that keep to these rules, and one draw needn't show every extreme that they name: Each row holds the lengths of one group's 4 sequences; they sum to 1280 and the largest is 1024.
All inputs are finite; a program needn't handle non-finite values.
Results may differ from the reference program's by a relative error of at most 0.017.
Values may be sent and summed in bfloat16 or wider, within the bound.
A program may use at most 256 MiB of HBM per device.

```python
import math
import jax
import jax.numpy as jnp
import numpy as np
from jax import lax

D = 2048
FF = 5632
LAYERS = 24
LAYER = 12
SEQS = 4
NGROUPS = 4
GROUP = 1280
LONGEST = 1024


def level_of(key, extent, shards, low, top_value):
    level, own = 1.0, jax.random.fold_in(key, 6)
    for dim, blocks in shards:
        draws = jnp.exp(jax.random.uniform(jax.random.fold_in(own, dim), (blocks,), jnp.float32, low / len(shards), top_value / len(shards)))
        level = level * jnp.repeat(draws, extent[dim] // blocks).reshape([-1 if axis == dim else 1 for axis in range(len(extent))])
    return level


def profile(count, total, reach, slope):
    loads = [(1 << 20) // math.isqrt(standing ** slope) + 1 for standing in range(2, count + 1)]
    rest, counts = total - reach - (count - 1), [1] * (count - 1)
    while rest > 0:
        candidates = [i for i in range(count - 1) if counts[i] < reach]
        mass, remaining = sum([loads[i] for i in candidates]), rest
        for i in candidates:
            extra = min(reach - counts[i], max(1, remaining * loads[i] // mass), rest)
            counts[i] = counts[i] + extra
            rest = rest - extra
    return np.array([reach] + counts)


def uneven(own_key, number_of, total, limit, lean):
    if number_of == 2:
        one = jax.random.randint(own_key, (), max(1, total - limit), min(limit, total - 1) + 1)
        return jnp.stack([one, total - one])
    sizes = jnp.asarray(profile(number_of, total, limit, lean), jnp.int32)
    twos = (number_of - 1) // 2
    source_of, sink = sizes[1:1 + 2 * twos:2], sizes[2:2 + 2 * twos:2]
    margin = jnp.minimum(source_of - 1, limit - sink)
    passed = jax.random.randint(jax.random.fold_in(own_key, 1), (twos,), 0, 1 << 20) % (margin + 1)
    sizes = sizes.at[1:1 + 2 * twos:2].set(source_of - passed).at[2:2 + 2 * twos:2].set(sink + passed)
    return sizes[jax.random.permutation(jax.random.fold_in(own_key, 2), number_of)]


def normal_values(rng, extent, scale, bound, shards=(), kind=jnp.bfloat16):
    entries = jax.random.normal(rng, extent, jnp.float32) * scale
    if len(shards) > 0:
        entries = level_of(rng, extent, shards, -0.22, 0.18) * entries
    return jnp.clip(entries, min=-bound, max=bound).astype(kind)


def setup_inputs(seed: int = 0) -> dict:
    arg_keys = jax.random.split(jax.random.key(seed), 15)
    return {
        "hidden": normal_values(arg_keys[0], (NGROUPS, GROUP, D), 1.0, 6.0, ((0, 4), (1, 8))),
        "lengths": jax.vmap(lambda own: uneven(own, SEQS, GROUP, LONGEST, 2))(jax.random.split(arg_keys[1], NGROUPS)).reshape((NGROUPS, SEQS)).astype(jnp.int32),
        "w_input": normal_values(arg_keys[2], (D, D), D ** -0.5, 0.125, ((1, 4),)),
        "w_forget": normal_values(arg_keys[3], (D, D), D ** -0.5, 0.125, ((1, 4),)),
        "w_gate_out": normal_values(arg_keys[4], (D, D), D ** -0.5, 0.125, ((1, 4),)),
        "w_output": normal_values(arg_keys[5], (D, D), (D // 4) ** -0.5, 0.25, ((0, 4),)),
        "norm_gain": jnp.clip(1.0 + 0.1 * jax.random.normal(arg_keys[6], (D,), jnp.float32), 0.5, 1.5),
        "gate_gain": jnp.clip(1.0 + 0.1 * jax.random.normal(arg_keys[7], (D,), jnp.float32), 0.5, 1.5),
        "glu_gain": jnp.clip(1.0 + 0.1 * jax.random.normal(arg_keys[8], (D,), jnp.float32), 0.5, 1.5),
        "lower_table": normal_values(arg_keys[9], (LAYERS, D), 3.0, 12.0, (), jnp.float32),
        "w_glu_gate": normal_values(arg_keys[10], (D, FF), D ** -0.5, 0.125, ((1, 4),)),
        "w_glu_up": normal_values(arg_keys[11], (D, FF), D ** -0.5, 0.125, ((1, 4),)),
        "w_glu_down": normal_values(arg_keys[12], (FF, D), (FF // 4) ** -0.5, 0.15625, ((0, 4),)),
        "cotangent": normal_values(arg_keys[13], (NGROUPS, GROUP, D), 1.0, 6.0, ((0, 4), (1, 8))),
    }


epsilon = 1e-06
highest = lax.Precision.HIGHEST

@jax.custom_vjp
def low(v):
    return lax.optimization_barrier(v.astype(jnp.bfloat16)).astype(jnp.float32)

@jax.custom_vjp
def low_back(v):
    return v

def low_keep(v):
    return (low(v), None)

def low_pass(kept, grad):
    return (grad,)

def back_keep(v):
    return (v, None)

def back_low(kept, grad):
    return (low(grad),)
low.defvjp(low_keep, low_pass)
low_back.defvjp(back_keep, back_low)

def matmul(left, right):
    return jnp.dot(left, right, precision=highest, preferred_element_type=jnp.float32)

def rms_scale(values, gain):
    return values * lax.rsqrt(lax.optimization_barrier(jnp.mean(values * values, -1, keepdims=True)) + epsilon) * gain

def lower_bound(table):
    soft = jax.nn.softmax(table, axis=0)
    totals = jnp.cumsum(soft, axis=0)
    return totals[LAYER] - totals[0]

def combine(earlier, later):
    return (earlier[0] * later[0], later[0] * earlier[1] + later[1])

def group_block(hidden_f, keep, w_input, w_forget, w_gate_out, w_output, norm_gain, gate_gain, glu_gain, lower_table, w_glu_gate, w_glu_up, w_glu_down):
    normed = low(rms_scale(hidden_f, norm_gain))
    in_raw = low_back(low(matmul(normed, w_input)))
    forget_raw = low_back(low(matmul(normed, w_forget)))
    gate_raw = low_back(matmul(normed, w_gate_out))
    bounds = lower_bound(lower_table)
    forget = bounds + (1.0 - bounds) * jax.nn.sigmoid(forget_raw)
    inflow = jax.nn.silu(in_raw) * (1.0 - forget)
    states = lax.associative_scan(combine, (forget * keep[:, None], inflow), axis=0)[1]
    state_b = low_back(low(states))
    scaled = state_b * lax.rsqrt(lax.optimization_barrier(jnp.mean(state_b * state_b, -1, keepdims=True)) + epsilon)
    out_gate = low(scaled * gate_gain * jax.nn.silu(gate_raw))
    mixed = low_back(matmul(out_gate, w_output))
    middle = hidden_f + mixed
    normed_two = low(rms_scale(middle, glu_gain))
    gate_val = low_back(matmul(normed_two, w_glu_gate))
    up_val = low_back(matmul(normed_two, w_glu_up))
    activity = low(jax.nn.silu(gate_val) * up_val)
    return middle + matmul(activity, w_glu_down)

def reference(hidden, lengths, w_input, w_forget, w_gate_out, w_output, norm_gain, gate_gain, glu_gain, lower_table, w_glu_gate, w_glu_up, w_glu_down, cotangent):
    seq_starts = jnp.cumsum(lengths, axis=1) - lengths
    places = jnp.arange(GROUP, dtype=jnp.int32)
    keep = jnp.where(jnp.any(places[None, :, None] == seq_starts[:, None, :], axis=-1), 0.0, 1.0).astype(jnp.float32)
    params = tuple((item.astype(jnp.float32) for item in (w_input, w_forget, w_gate_out, w_output, norm_gain, gate_gain, glu_gain, lower_table, w_glu_gate, w_glu_up, w_glu_down)))

    def forward(hidden_f, *weights):
        block = jax.checkpoint(group_block)
        return lax.map(lambda pair: block(pair[0], pair[1], *weights), (hidden_f, keep))
    result, pull = jax.vjp(forward, hidden.astype(jnp.float32), *params)
    grads = pull(cotangent.astype(jnp.float32))
    return (result.astype(jnp.bfloat16), grads[0].astype(jnp.bfloat16), grads[1], grads[2], grads[3], grads[4], grads[5], grads[6], grads[7], grads[8], grads[9], grads[10], grads[11])
```

```python
import functools

import jax
import jax.numpy as jnp
from jax import lax
from jax.experimental import pallas as pl
from jax.experimental.pallas import tpu as pltpu
from jax.sharding import PartitionSpec as P

LAYER = 12
MESH = pl.DeviceIdType.MESH
F32 = jnp.float32
BF16 = jnp.bfloat16

epsilon = 1e-06

VMEM = pl.BlockSpec(memory_space=pltpu.VMEM)
ANY = pl.BlockSpec(memory_space=pl.ANY)


def lower_bound(table):
    soft = jax.nn.softmax(table, axis=0)
    totals = jnp.cumsum(soft, axis=0)
    return totals[LAYER] - totals[0]


def silu_slope(value, sigma):
    return sigma * (1.0 + value * (1.0 - sigma))


def params(collective_id):
    return pltpu.CompilerParams(
        collective_id=collective_id, has_side_effects=True, vmem_limit_bytes=56 << 20
    )


def round_up(value, unit):
    return -(-value // unit) * unit


def plane():
    s = lax.axis_index("seq")
    f = lax.axis_index("fsdp")
    y, x = f // 2, f % 2
    fx = y * 2 + (1 - x)
    fy = (1 - y) * 2 + x
    fd = (1 - y) * 2 + (1 - x)
    return s, f, fx, fy, fd


def enter(devices):
    barrier = pltpu.get_barrier_semaphore()
    for device in devices:
        pl.semaphore_signal(barrier, inc=1, device_id=device, device_id_type=MESH)
    pl.semaphore_wait(barrier, len(devices))


def remote(src, dst, send, recv, device):
    return pltpu.make_async_remote_copy(
        src_ref=src,
        dst_ref=dst,
        send_sem=send,
        recv_sem=recv,
        device_id=device,
        device_id_type=MESH,
    )


def gather_kernel(x, small, out, out_small, local_sem, send, recv):
    s, f, fx, fy, fd = plane()
    half = x.shape[0] // 2
    enter([(s, fx), (s, fy), (s, fd)])
    top, bottom = pl.ds(0, half), pl.ds(half, half)
    own = [
        remote(x.at[top], out.at[f, top], send.at[0], recv.at[0], (s, fx)),
        remote(x.at[bottom], out.at[f, bottom], send.at[1], recv.at[1], (s, fy)),
        remote(x.at[bottom], out.at[f, bottom], send.at[2], recv.at[2], (s, fx)),
        remote(x.at[top], out.at[f, top], send.at[3], recv.at[3], (s, fy)),
        remote(small, out_small.at[f], send.at[6], recv.at[6], (s, fx)),
        remote(small, out_small.at[f], send.at[7], recv.at[7], (s, fy)),
        remote(small, out_small.at[f], send.at[8], recv.at[8], (s, fd)),
    ]
    for copy in own:
        copy.start()
    local = pltpu.make_async_copy(x, out.at[f], local_sem)
    local.start()
    out_small[pl.ds(f, 1)] = small[...][None]
    own[0].wait_recv()
    on_y = remote(out.at[fx, top], out.at[fx, top], send.at[4], recv.at[4], (s, fy))
    on_y.start()
    own[1].wait_recv()
    on_x = remote(out.at[fy, bottom], out.at[fy, bottom], send.at[5], recv.at[5], (s, fx))
    on_x.start()
    own[0].wait_send()
    own[1].wait_send()
    for copy in own[2:]:
        copy.wait()
    on_y.wait()
    on_x.wait()
    local.wait()


def gather(x, small, collective_id):
    n = lax.axis_size("fsdp")
    if n != 4:
        return lax.all_gather(x, "fsdp"), lax.all_gather(small, "fsdp")
    rows, width = x.shape
    return pl.pallas_call(
        gather_kernel,
        out_shape=(
            jax.ShapeDtypeStruct((n, rows, width), x.dtype),
            jax.ShapeDtypeStruct((n,) + small.shape, F32),
        ),
        in_specs=[ANY, VMEM],
        out_specs=(ANY, VMEM),
        scratch_shapes=[
            pltpu.SemaphoreType.DMA,
            pltpu.SemaphoreType.DMA((9,)),
            pltpu.SemaphoreType.DMA((9,)),
        ],
        compiler_params=params(collective_id),
        name="gather_rows",
    )(x, small)


def reduce_kernel(p, small, out, out_small, from_x, from_y, pass_x, pass_y, small_in, send, recv):
    s, f, fx, fy, fd = plane()
    half = p.shape[1] // 2
    enter([(s, fx), (s, fy), (s, fd)])
    top, bottom = pl.ds(0, half), pl.ds(half, half)
    own = [
        remote(p.at[fd, top], from_x.at[0], send.at[0], recv.at[0], (s, fx)),
        remote(p.at[fd, bottom], from_y.at[0], send.at[1], recv.at[1], (s, fy)),
        remote(p.at[fx, top], from_x.at[1], send.at[2], recv.at[2], (s, fx)),
        remote(p.at[fy, bottom], from_y.at[1], send.at[3], recv.at[3], (s, fy)),
        remote(small, small_in.at[0], send.at[6], recv.at[6], (s, fx)),
        remote(small, small_in.at[1], send.at[7], recv.at[7], (s, fy)),
        remote(small, small_in.at[2], send.at[8], recv.at[8], (s, fd)),
    ]
    for copy in own:
        copy.start()
    own[0].wait_recv()
    pass_y[...] = (from_x[0].astype(F32) + p[pl.ds(fy, 1), :half][0].astype(F32)).astype(BF16)
    on_y = remote(pass_y, from_y.at[2], send.at[4], recv.at[4], (s, fy))
    on_y.start()
    own[1].wait_recv()
    pass_x[...] = (from_y[0].astype(F32) + p[pl.ds(fx, 1), half:][0].astype(F32)).astype(BF16)
    on_x = remote(pass_x, from_x.at[2], send.at[5], recv.at[5], (s, fx))
    on_x.start()
    own[2].wait_recv()
    own[3].wait_recv()
    out[:half] = p[pl.ds(f, 1), :half][0].astype(F32) + from_x[1].astype(F32)
    out[half:] = p[pl.ds(f, 1), half:][0].astype(F32) + from_y[1].astype(F32)
    for copy in own[4:]:
        copy.wait_recv()
    out_small[...] = (small[...] + small_in[0]) + (small_in[1] + small_in[2])
    on_y.wait_recv()
    out[:half] += from_y[2].astype(F32)
    on_x.wait_recv()
    out[half:] += from_x[2].astype(F32)
    for copy in own:
        copy.wait_send()
    on_y.wait_send()
    on_x.wait_send()


def reduce_rows(p, small, collective_id):
    n = lax.axis_size("fsdp")
    if n != 4:
        total = lax.psum_scatter(p, "fsdp", scatter_dimension=0, tiled=True)[0]
        return total.astype(F32), lax.psum(small, "fsdp")
    _, rows, width = p.shape
    half = (rows // 2, width)
    return pl.pallas_call(
        reduce_kernel,
        out_shape=(
            jax.ShapeDtypeStruct((rows, width), F32),
            jax.ShapeDtypeStruct(small.shape, F32),
        ),
        in_specs=[VMEM, VMEM],
        out_specs=(VMEM, VMEM),
        scratch_shapes=[
            pltpu.VMEM((3,) + half, BF16),
            pltpu.VMEM((3,) + half, BF16),
            pltpu.VMEM(half, BF16),
            pltpu.VMEM(half, BF16),
            pltpu.VMEM((3,) + small.shape, F32),
            pltpu.SemaphoreType.DMA((9,)),
            pltpu.SemaphoreType.DMA((9,)),
        ],
        compiler_params=params(collective_id),
        name="reduce_rows",
    )(p, small)


def start_exchange(total, gathered, send, recv, n_seq):
    s = lax.axis_index("seq")
    f = lax.axis_index("fsdp")
    copies = []
    for k in range(1, n_seq):
        peer = lax.rem(s + k, n_seq)
        copy = remote(total, gathered.at[s], send.at[k], recv.at[k], (peer, f))
        copy.start()
        copies.append(copy)
    gathered[pl.ds(s, 1)] = total[...][None]
    return copies


def seq_peers(n_seq):
    s = lax.axis_index("seq")
    f = lax.axis_index("fsdp")
    return [(lax.rem(s + k, n_seq), f) for k in range(1, n_seq)]


def lane_blocks(groups, chans):
    return [(g, slice(c, c + 128)) for g in range(groups) for c in range(0, chans, 128)]


def forward_scan_kernel(
    n_seq, in_raw, forget_raw, bounds, keep, state_b, before, a_ref, b_ref, total, gathered, send, recv
):
    groups, rows, chans = in_raw.shape
    part = rows // 8
    blocks = lane_blocks(groups, chans)
    s = lax.axis_index("seq")
    barrier = pltpu.get_barrier_semaphore()
    for peer in seq_peers(n_seq):
        pl.semaphore_signal(barrier, inc=1, device_id=peer, device_id_type=MESH)
    for n, (g, lanes) in enumerate(blocks):
        bound = bounds[:, lanes]
        forget = bound + (1.0 - bound) * jax.nn.sigmoid(forget_raw[g, :, lanes].astype(F32))
        value = in_raw[g, :, lanes].astype(F32)
        a_ref[n] = forget * keep[g]
        b_ref[n] = value * jax.nn.sigmoid(value) * (1.0 - forget)

    def step(i, carry):
        new = []
        at = pl.ds(i, 8, stride=part)
        for n, (product, state) in enumerate(carry):
            a = a_ref[n, at, :]
            state = a * state + b_ref[n, at, :]
            product = product * a
            a_ref[n, at, :] = product
            b_ref[n, at, :] = state
            new.append((product, state))
        return tuple(new)

    start = tuple((jnp.ones((8, 128), F32), jnp.zeros((8, 128), F32)) for _ in blocks)
    ends = lax.fori_loop(0, part, step, start)
    for n, (product, state) in enumerate(ends):
        p_all, s_all = product[0:1], state[0:1]
        for j in range(1, 8):
            p_all, s_all = p_all * product[j : j + 1], state[j : j + 1] + product[j : j + 1] * s_all
        total[2 * n : 2 * n + 1] = p_all
        total[2 * n + 1 : 2 * n + 2] = s_all
    pl.semaphore_wait(barrier, n_seq - 1)
    copies = start_exchange(total, gathered, send, recv, n_seq)
    for copy in copies:
        copy.wait()
    for n, (g, lanes) in enumerate(blocks):
        carry = jnp.zeros((1, 128), F32)
        for j in range(n_seq - 1):
            p_j = gathered[j, 2 * n : 2 * n + 1]
            s_j = gathered[j, 2 * n + 1 : 2 * n + 2]
            carry = jnp.where(j < s, s_j + p_j * carry, carry)
        before[g, 0:1, lanes] = carry
        product, state = ends[n]
        carries = [carry]
        for j in range(7):
            carries.append(state[j : j + 1] + product[j : j + 1] * carries[-1])
        for j in range(8):
            at = slice(j * part, (j + 1) * part)
            b_ref[n, at] = b_ref[n, at] + a_ref[n, at] * carries[j]
        state_b[g, :, lanes] = b_ref[n].astype(BF16)
        before[g, 1:rows, lanes] = b_ref[n, 0 : rows - 1]


def forward_scan(in_raw, forget_raw, bounds, keep, collective_id):
    n_seq = lax.axis_size("seq")
    groups, rows, chans = in_raw.shape
    blocks = groups * chans // 128
    return pl.pallas_call(
        functools.partial(forward_scan_kernel, n_seq),
        out_shape=(
            jax.ShapeDtypeStruct(in_raw.shape, BF16),
            jax.ShapeDtypeStruct(in_raw.shape, F32),
        ),
        in_specs=[VMEM] * 4,
        out_specs=(VMEM, VMEM),
        scratch_shapes=[
            pltpu.VMEM((blocks, rows, 128), F32),
            pltpu.VMEM((blocks, rows, 128), F32),
            pltpu.VMEM((2 * blocks, 128), F32),
            pltpu.VMEM((n_seq, 2 * blocks, 128), F32),
            pltpu.SemaphoreType.DMA((n_seq,)),
            pltpu.SemaphoreType.DMA((n_seq,)),
        ],
        compiler_params=params(collective_id),
        name="forward_scan",
    )(in_raw, forget_raw, bounds, keep)


def backward_scan_kernel(
    n_seq,
    d_state,
    in_raw,
    forget_raw,
    before,
    bounds,
    keep,
    d_in,
    d_forget_raw,
    d_bounds,
    p_ref,
    q_ref,
    total,
    gathered,
    send,
    recv,
):
    groups, rows, chans = in_raw.shape
    part = rows // 8
    blocks = lane_blocks(groups, chans)
    s = lax.axis_index("seq")
    barrier = pltpu.get_barrier_semaphore()
    for peer in seq_peers(n_seq):
        pl.semaphore_signal(barrier, inc=1, device_id=peer, device_id_type=MESH)
    for n, (g, lanes) in enumerate(blocks):
        bound = bounds[:, lanes]
        forget = bound + (1.0 - bound) * jax.nn.sigmoid(forget_raw[g, :, lanes].astype(F32))
        p_ref[n] = forget * keep[g]
        q_ref[n] = d_state[g, :, lanes].astype(F32)

    def step(i, carry):
        new = []
        at = pl.ds(part - 1 - i, 8, stride=part)
        for n, (product, message) in enumerate(carry):
            a = p_ref[n, at, :]
            acc = q_ref[n, at, :] + message
            p_ref[n, at, :] = product
            q_ref[n, at, :] = acc
            new.append((product * a, a * acc))
        return tuple(new)

    start = tuple((jnp.ones((8, 128), F32), jnp.zeros((8, 128), F32)) for _ in blocks)
    ends = lax.fori_loop(0, part, step, start)
    for n, (product, message) in enumerate(ends):
        p_all, m_all = product[7:8], message[7:8]
        for j in range(6, -1, -1):
            p_all, m_all = p_all * product[j : j + 1], message[j : j + 1] + product[j : j + 1] * m_all
        total[2 * n : 2 * n + 1] = p_all
        total[2 * n + 1 : 2 * n + 2] = m_all
    pl.semaphore_wait(barrier, n_seq - 1)
    copies = start_exchange(total, gathered, send, recv, n_seq)
    for copy in copies:
        copy.wait()
    d_bounds[...] = jnp.zeros((1, chans), F32)
    for n, (g, lanes) in enumerate(blocks):
        carry = jnp.zeros((1, 128), F32)
        for j in range(n_seq - 1, 0, -1):
            p_j = gathered[j, 2 * n : 2 * n + 1]
            m_j = gathered[j, 2 * n + 1 : 2 * n + 2]
            carry = jnp.where(j > s, m_j + p_j * carry, carry)
        product, message = ends[n]
        carries = [carry]
        for j in range(7, 0, -1):
            carries.append(message[j : j + 1] + product[j : j + 1] * carries[-1])
        carries = carries[::-1]
        for j in range(8):
            at = slice(j * part, (j + 1) * part)
            q_ref[n, at] = q_ref[n, at] + p_ref[n, at] * carries[j]
        acc = q_ref[n]
        bound = bounds[:, lanes]
        sigma_f = jax.nn.sigmoid(forget_raw[g, :, lanes].astype(F32))
        forget = bound + (1.0 - bound) * sigma_f
        value = in_raw[g, :, lanes].astype(F32)
        sigma_i = jax.nn.sigmoid(value)
        d_forget = acc * (before[g, :, lanes] * keep[g] - value * sigma_i)
        d_in[g, :, lanes] = (acc * (1.0 - forget) * silu_slope(value, sigma_i)).astype(BF16)
        d_sigma = d_forget * (1.0 - sigma_f)
        d_forget_raw[g, :, lanes] = (d_sigma * (1.0 - bound) * sigma_f).astype(BF16)
        d_bounds[:, lanes] += jnp.sum(d_sigma, 0, keepdims=True)


def backward_scan(d_state, in_raw, forget_raw, before, bounds, keep, collective_id):
    n_seq = lax.axis_size("seq")
    groups, rows, chans = in_raw.shape
    blocks = groups * chans // 128
    return pl.pallas_call(
        functools.partial(backward_scan_kernel, n_seq),
        out_shape=(
            jax.ShapeDtypeStruct(in_raw.shape, BF16),
            jax.ShapeDtypeStruct(in_raw.shape, BF16),
            jax.ShapeDtypeStruct((1, chans), F32),
        ),
        in_specs=[VMEM] * 6,
        out_specs=(VMEM, VMEM, VMEM),
        scratch_shapes=[
            pltpu.VMEM((blocks, rows, 128), F32),
            pltpu.VMEM((blocks, rows, 128), F32),
            pltpu.VMEM((2 * blocks, 128), F32),
            pltpu.VMEM((n_seq, 2 * blocks, 128), F32),
            pltpu.SemaphoreType.DMA((n_seq,)),
            pltpu.SemaphoreType.DMA((n_seq,)),
        ],
        compiler_params=params(collective_id),
        name="backward_scan",
    )(d_state, in_raw, forget_raw, before, bounds, keep)


def sum_all_kernel(n_seq, n_fsdp, x, out, middle, over_seq, over_fsdp, send, recv):
    s = lax.axis_index("seq")
    f = lax.axis_index("fsdp")
    along = [(lax.rem(s + k, n_seq), f) for k in range(1, n_seq)]
    across = [(s, lax.rem(f + k, n_fsdp)) for k in range(1, n_fsdp)]
    enter(along + across)
    copies = []
    for k, peer in enumerate(along):
        copy = remote(x, over_seq.at[k], send.at[k], recv.at[k], peer)
        copy.start()
        copies.append(copy)
    total = x[...]
    for k, copy in enumerate(copies):
        copy.wait_recv()
        total = total + over_seq[k]
    middle[...] = total
    later = []
    for k, peer in enumerate(across):
        slot = n_seq - 1 + k
        copy = remote(middle, over_fsdp.at[k], send.at[slot], recv.at[slot], peer)
        copy.start()
        later.append(copy)
    for k, copy in enumerate(later):
        copy.wait_recv()
        total = total + over_fsdp[k]
    out[...] = total
    for copy in copies + later:
        copy.wait_send()


def sum_all(x, collective_id):
    n_seq, n_fsdp = lax.axis_size("seq"), lax.axis_size("fsdp")
    count = n_seq + n_fsdp - 2
    return pl.pallas_call(
        functools.partial(sum_all_kernel, n_seq, n_fsdp),
        out_shape=jax.ShapeDtypeStruct(x.shape, F32),
        in_specs=[VMEM],
        out_specs=VMEM,
        scratch_shapes=[
            pltpu.VMEM(x.shape, F32),
            pltpu.VMEM((n_seq - 1,) + x.shape, F32),
            pltpu.VMEM((n_fsdp - 1,) + x.shape, F32),
            pltpu.SemaphoreType.DMA((count,)),
            pltpu.SemaphoreType.DMA((count,)),
        ],
        compiler_params=params(collective_id),
        name="sum_all",
    )(x)


def sum_over_seq(part):
    return lax.psum_scatter(part.astype(BF16), "seq", scatter_dimension=0, tiled=True).astype(F32)


def per_device(
    hidden,
    lengths,
    w_input,
    w_forget,
    w_gate_out,
    w_output,
    norm_gain,
    gate_gain,
    glu_gain,
    lower_table,
    w_glu_gate,
    w_glu_up,
    w_glu_down,
    cotangent,
):
    seq_index = lax.axis_index("seq")
    fsdp_index = lax.axis_index("fsdp")
    groups = lax.axis_size("fsdp")
    _, rows, width = hidden.shape
    chans = w_input.shape[1]
    units = w_glu_gate.shape[1]
    tokens = groups * rows
    small_shape = (round_up(groups, 8), round_up(rows, 128))

    def to_small(value):
        return jnp.pad(
            value, ((0, small_shape[0] - value.shape[0]), (0, small_shape[1] - value.shape[1]))
        )

    def dot(left, right):
        return jnp.dot(left, right, preferred_element_type=F32)

    def dot_t(left, right):
        return lax.dot_general(left, right, (((1,), (1,)), ((), ())), preferred_element_type=F32)

    def over_tokens(left, right):
        return lax.dot_general(left, right, (((0,), (0,)), ((), ())), preferred_element_type=F32)

    cotangent_all = lax.all_gather(cotangent[0], "fsdp").reshape(tokens, width)

    hidden_f = hidden[0].astype(F32)
    scale_one = lax.rsqrt(jnp.mean(hidden_f * hidden_f, -1, keepdims=True) + epsilon)
    normed = (hidden_f * scale_one * norm_gain).astype(BF16)
    normed_all, _ = gather(normed, jnp.zeros((8, 128), F32), 0)
    normed_all = normed_all.reshape(tokens, width)
    in_raw = dot(normed_all, w_input).astype(BF16).reshape(groups, rows, chans)
    forget_raw = dot(normed_all, w_forget).astype(BF16).reshape(groups, rows, chans)
    gate_raw = dot(normed_all, w_gate_out)

    bounds_full = lower_bound(lower_table)
    bounds = lax.dynamic_slice_in_dim(bounds_full, fsdp_index * chans, chans)[None]
    seq_starts = jnp.cumsum(lengths, axis=1) - lengths
    places = seq_index * rows + jnp.arange(rows, dtype=jnp.int32)
    starts = jnp.any(places[None, :, None] == seq_starts[:, None, :], axis=-1)
    keep = jnp.where(starts, 0.0, 1.0).astype(F32)[:, :, None]
    state_b, before = forward_scan(in_raw, forget_raw, bounds, keep, 1)

    state_f = state_b.astype(F32).reshape(tokens, chans)
    gain_slice = lax.dynamic_slice_in_dim(gate_gain, fsdp_index * chans, chans)
    sigma_g = jax.nn.sigmoid(gate_raw)
    silu_gate = gate_raw * sigma_g
    out_raw = (state_f * gain_slice * silu_gate).astype(BF16)
    squares = jnp.sum(state_f * state_f, -1).reshape(groups, rows)
    mixed_part = dot(out_raw, w_output).astype(BF16).reshape(groups, rows, width)
    mixed_raw, square_sum = reduce_rows(mixed_part, to_small(squares), 2)
    state_scale = lax.rsqrt(square_sum[:groups, :rows] / width + epsilon)
    own_scale = lax.dynamic_slice_in_dim(state_scale, fsdp_index, 1, 0)[0][:, None]
    scale_g = state_scale.reshape(tokens, 1)
    middle = hidden_f + own_scale * mixed_raw
    scale_two = lax.rsqrt(jnp.mean(middle * middle, -1, keepdims=True) + epsilon)
    normed_two = (middle * scale_two * glu_gain).astype(BF16)
    normed_two_all, _ = gather(normed_two, jnp.zeros((8, 128), F32), 3)
    normed_two_all = normed_two_all.reshape(tokens, width)

    gate_val = dot(normed_two_all, w_glu_gate)
    up_val = dot(normed_two_all, w_glu_up)
    sigma_u = jax.nn.sigmoid(gate_val)
    silu_u = gate_val * sigma_u
    activity = (silu_u * up_val).astype(BF16)
    down_grad = sum_over_seq(over_tokens(cotangent_all, activity))
    d_act = dot_t(cotangent_all, w_glu_down)
    d_gate = (d_act * up_val * silu_slope(gate_val, sigma_u)).astype(BF16)
    d_up = (d_act * silu_u).astype(BF16)
    pair_grad = sum_over_seq(
        jnp.concatenate(
            [
                over_tokens(normed_two_all, d_gate).astype(BF16),
                over_tokens(normed_two_all, d_up).astype(BF16),
            ],
            1,
        )
    )
    d_two_part = (dot_t(d_gate, w_glu_gate) + dot_t(d_up, w_glu_up)).astype(BF16)
    no_small = jnp.zeros((8, 128), F32)
    d_normed_two, _ = reduce_rows(d_two_part.reshape(groups, rows, width), no_small, 4)
    glu_part = dot(activity, w_glu_down).astype(BF16).reshape(groups, rows, width)
    glu_result = lax.psum_scatter(glu_part, "fsdp", scatter_dimension=0, tiled=True)[0]
    output = (middle + glu_result.astype(F32)).astype(BF16)[None]

    cotangent_f = cotangent[0].astype(F32)
    scaled_two = glu_gain * d_normed_two
    d_middle = (
        cotangent_f
        + scale_two * scaled_two
        - middle * scale_two**3 * jnp.mean(scaled_two * middle, -1, keepdims=True)
    )
    d_glu_gain = jnp.sum(d_normed_two * middle * scale_two, 0)
    d_mixed = d_middle.astype(BF16)
    own_dot = jnp.sum(d_mixed.astype(F32) * mixed_raw, -1)[None]
    d_mixed_all, dots = gather(d_mixed, to_small(own_dot), 5)
    d_mixed_all = d_mixed_all.reshape(tokens, width)
    dot_rows = dots[:, 0, :rows].reshape(tokens, 1)

    d_out = dot_t(d_mixed_all, w_output)
    scaled_state = state_f * scale_g
    d_gain_slice = jnp.sum(d_out * scaled_state * silu_gate, 0)
    d_scaled = d_out * gain_slice * silu_gate
    d_gate_raw = (d_out * scaled_state * gain_slice * silu_slope(gate_raw, sigma_g)).astype(BF16)
    d_state = scale_g * d_scaled - state_f * (scale_g**3 * (dot_rows / width))
    d_state = d_state.astype(BF16).reshape(groups, rows, chans)
    d_in, d_forget_raw, d_bounds = backward_scan(
        d_state, in_raw, forget_raw, before, bounds, keep, 6
    )
    d_in = d_in.reshape(tokens, chans)
    d_forget_raw = d_forget_raw.reshape(tokens, chans)

    d_normed_part = dot_t(d_in, w_input) + dot_t(d_forget_raw, w_forget)
    d_normed_part = (d_normed_part + dot_t(d_gate_raw, w_gate_out)).astype(BF16)
    out_gate = (out_raw.astype(F32) * scale_g).astype(BF16)
    mixer_grad = sum_over_seq(
        jnp.concatenate(
            [
                over_tokens(d_mixed_all, out_gate).astype(BF16),
                over_tokens(normed_all, d_in).astype(BF16),
                over_tokens(normed_all, d_forget_raw).astype(BF16),
                over_tokens(normed_all, d_gate_raw).astype(BF16),
            ],
            1,
        )
    )
    d_normed, _ = reduce_rows(d_normed_part.reshape(groups, rows, width), no_small, 7)
    scaled_one = norm_gain * d_normed
    d_hidden = (
        d_middle
        + scale_one * scaled_one
        - hidden_f * scale_one**3 * jnp.mean(scaled_one * hidden_f, -1, keepdims=True)
    )
    d_norm_gain = jnp.sum(d_normed * hidden_f * scale_one, 0)
    d_gain_full = lax.dynamic_update_slice(
        jnp.zeros((width,), F32), d_gain_slice, (fsdp_index * chans,)
    )
    d_bounds_full = lax.dynamic_update_slice(
        jnp.zeros((width,), F32), d_bounds[0], (fsdp_index * chans,)
    )
    sums = jnp.stack([d_norm_gain, d_glu_gain, d_gain_full, d_bounds_full])
    totals = sum_all(sums.reshape(8, width // 2), 8).reshape(4, width)
    _, bounds_pull = jax.vjp(lower_bound, lower_table)
    d_table = bounds_pull(totals[3])[0]
    return (
        output,
        d_hidden.astype(BF16)[None],
        mixer_grad[:, chans : 2 * chans],
        mixer_grad[:, 2 * chans : 3 * chans],
        mixer_grad[:, 3 * chans :],
        mixer_grad[:, :chans].T,
        totals[0],
        totals[2],
        totals[1],
        d_table,
        pair_grad[:, :units],
        pair_grad[:, units:],
        down_grad.T,
    )


def solution(mesh):
    rows_spec = P("fsdp", "seq", None)
    columns = P(None, "fsdp")
    placed = (
        rows_spec,
        P(),
        columns,
        columns,
        columns,
        P("fsdp", None),
        P(),
        P(),
        P(),
        P(),
        columns,
        columns,
        P("fsdp", None),
        rows_spec,
    )
    by_rows, by_columns = P("seq", "fsdp"), P("fsdp", "seq")
    return jax.shard_map(
        per_device,
        mesh=mesh,
        in_specs=placed,
        out_specs=(
            rows_spec,
            rows_spec,
            by_rows,
            by_rows,
            by_rows,
            by_columns,
            P(),
            P(),
            P(),
            P(),
            by_rows,
            by_rows,
            by_columns,
        ),
        check_vma=False,
    )
```

```python
import functools

import jax
import jax.numpy as jnp
from jax import lax
from jax.experimental import pallas as pl
from jax.experimental.pallas import tpu as pltpu
from jax.sharding import PartitionSpec as P

LAYER = 12
MESH = pl.DeviceIdType.MESH
F32 = jnp.float32
BF16 = jnp.bfloat16

epsilon = 1e-06

VMEM = pl.BlockSpec(memory_space=pltpu.VMEM)
ANY = pl.BlockSpec(memory_space=pl.ANY)


def lower_bound(table):
    soft = jax.nn.softmax(table, axis=0)
    totals = jnp.cumsum(soft, axis=0)
    return totals[LAYER] - totals[0]


def silu_slope(value, sigma):
    return sigma * (1.0 + value * (1.0 - sigma))


def params(collective_id):
    return pltpu.CompilerParams(
        collective_id=collective_id, has_side_effects=True, vmem_limit_bytes=56 << 20
    )


def round_up(value, unit):
    return -(-value // unit) * unit


def plane():
    s = lax.axis_index("seq")
    f = lax.axis_index("fsdp")
    y, x = f // 2, f % 2
    fx = y * 2 + (1 - x)
    fy = (1 - y) * 2 + x
    fd = (1 - y) * 2 + (1 - x)
    return s, f, fx, fy, fd


def enter(devices):
    barrier = pltpu.get_barrier_semaphore()
    for device in devices:
        pl.semaphore_signal(barrier, inc=1, device_id=device, device_id_type=MESH)
    pl.semaphore_wait(barrier, len(devices))


def remote(src, dst, send, recv, device):
    return pltpu.make_async_remote_copy(
        src_ref=src,
        dst_ref=dst,
        send_sem=send,
        recv_sem=recv,
        device_id=device,
        device_id_type=MESH,
    )


def gather(x, small, collective_id):
    return lax.all_gather(x, "fsdp"), lax.all_gather(small, "fsdp")


def reduce_rows(p, small, collective_id):
    total = lax.psum_scatter(p, "fsdp", scatter_dimension=0, tiled=True)[0]
    return total.astype(F32), lax.psum(small, "fsdp")


def start_exchange(total, gathered, send, recv, n_seq):
    s = lax.axis_index("seq")
    f = lax.axis_index("fsdp")
    copies = []
    for k in range(1, n_seq):
        peer = lax.rem(s + k, n_seq)
        copy = remote(total, gathered.at[s], send.at[k], recv.at[k], (peer, f))
        copy.start()
        copies.append(copy)
    gathered[pl.ds(s, 1)] = total[...][None]
    return copies


def seq_peers(n_seq):
    s = lax.axis_index("seq")
    f = lax.axis_index("fsdp")
    return [(lax.rem(s + k, n_seq), f) for k in range(1, n_seq)]


def lane_blocks(groups, chans):
    return [(g, slice(c, c + 128)) for g in range(groups) for c in range(0, chans, 128)]


def forward_scan_kernel(
    n_seq, in_raw, forget_raw, bounds, keep, state_b, before, a_ref, b_ref, total, gathered, send, recv
):
    groups, rows, chans = in_raw.shape
    part = rows // 8
    blocks = lane_blocks(groups, chans)
    s = lax.axis_index("seq")
    barrier = pltpu.get_barrier_semaphore()
    for peer in seq_peers(n_seq):
        pl.semaphore_signal(barrier, inc=1, device_id=peer, device_id_type=MESH)
    for n, (g, lanes) in enumerate(blocks):
        bound = bounds[:, lanes]
        forget = bound + (1.0 - bound) * jax.nn.sigmoid(forget_raw[g, :, lanes].astype(F32))
        value = in_raw[g, :, lanes].astype(F32)
        a_ref[n] = forget * keep[g]
        b_ref[n] = value * jax.nn.sigmoid(value) * (1.0 - forget)

    def step(i, carry):
        new = []
        at = pl.ds(i, 8, stride=part)
        for n, (product, state) in enumerate(carry):
            a = a_ref[n, at, :]
            state = a * state + b_ref[n, at, :]
            product = product * a
            a_ref[n, at, :] = product
            b_ref[n, at, :] = state
            new.append((product, state))
        return tuple(new)

    start = tuple((jnp.ones((8, 128), F32), jnp.zeros((8, 128), F32)) for _ in blocks)
    ends = lax.fori_loop(0, part, step, start)
    for n, (product, state) in enumerate(ends):
        p_all, s_all = product[0:1], state[0:1]
        for j in range(1, 8):
            p_all, s_all = p_all * product[j : j + 1], state[j : j + 1] + product[j : j + 1] * s_all
        total[2 * n : 2 * n + 1] = p_all
        total[2 * n + 1 : 2 * n + 2] = s_all
    pl.semaphore_wait(barrier, n_seq - 1)
    copies = start_exchange(total, gathered, send, recv, n_seq)
    for copy in copies:
        copy.wait()
    for n, (g, lanes) in enumerate(blocks):
        carry = jnp.zeros((1, 128), F32)
        for j in range(n_seq - 1):
            p_j = gathered[j, 2 * n : 2 * n + 1]
            s_j = gathered[j, 2 * n + 1 : 2 * n + 2]
            carry = jnp.where(j < s, s_j + p_j * carry, carry)
        before[g, 0:1, lanes] = carry
        product, state = ends[n]
        carries = [carry]
        for j in range(7):
            carries.append(state[j : j + 1] + product[j : j + 1] * carries[-1])
        for j in range(8):
            at = slice(j * part, (j + 1) * part)
            b_ref[n, at] = b_ref[n, at] + a_ref[n, at] * carries[j]
        state_b[g, :, lanes] = b_ref[n].astype(BF16)
        before[g, 1:rows, lanes] = b_ref[n, 0 : rows - 1]


def forward_scan(in_raw, forget_raw, bounds, keep, collective_id):
    n_seq = lax.axis_size("seq")
    groups, rows, chans = in_raw.shape
    blocks = groups * chans // 128
    return pl.pallas_call(
        functools.partial(forward_scan_kernel, n_seq),
        out_shape=(
            jax.ShapeDtypeStruct(in_raw.shape, BF16),
            jax.ShapeDtypeStruct(in_raw.shape, F32),
        ),
        in_specs=[VMEM] * 4,
        out_specs=(VMEM, VMEM),
        scratch_shapes=[
            pltpu.VMEM((blocks, rows, 128), F32),
            pltpu.VMEM((blocks, rows, 128), F32),
            pltpu.VMEM((2 * blocks, 128), F32),
            pltpu.VMEM((n_seq, 2 * blocks, 128), F32),
            pltpu.SemaphoreType.DMA((n_seq,)),
            pltpu.SemaphoreType.DMA((n_seq,)),
        ],
        compiler_params=params(collective_id),
        name="forward_scan",
    )(in_raw, forget_raw, bounds, keep)


def backward_scan_kernel(
    n_seq,
    d_state,
    in_raw,
    forget_raw,
    before,
    bounds,
    keep,
    d_in,
    d_forget_raw,
    d_bounds,
    p_ref,
    q_ref,
    total,
    gathered,
    send,
    recv,
):
    groups, rows, chans = in_raw.shape
    part = rows // 8
    blocks = lane_blocks(groups, chans)
    s = lax.axis_index("seq")
    barrier = pltpu.get_barrier_semaphore()
    for peer in seq_peers(n_seq):
        pl.semaphore_signal(barrier, inc=1, device_id=peer, device_id_type=MESH)
    for n, (g, lanes) in enumerate(blocks):
        bound = bounds[:, lanes]
        forget = bound + (1.0 - bound) * jax.nn.sigmoid(forget_raw[g, :, lanes].astype(F32))
        p_ref[n] = forget * keep[g]
        q_ref[n] = d_state[g, :, lanes].astype(F32)

    def step(i, carry):
        new = []
        at = pl.ds(part - 1 - i, 8, stride=part)
        for n, (product, message) in enumerate(carry):
            a = p_ref[n, at, :]
            acc = q_ref[n, at, :] + message
            p_ref[n, at, :] = product
            q_ref[n, at, :] = acc
            new.append((product * a, a * acc))
        return tuple(new)

    start = tuple((jnp.ones((8, 128), F32), jnp.zeros((8, 128), F32)) for _ in blocks)
    ends = lax.fori_loop(0, part, step, start)
    for n, (product, message) in enumerate(ends):
        p_all, m_all = product[7:8], message[7:8]
        for j in range(6, -1, -1):
            p_all, m_all = p_all * product[j : j + 1], message[j : j + 1] + product[j : j + 1] * m_all
        total[2 * n : 2 * n + 1] = p_all
        total[2 * n + 1 : 2 * n + 2] = m_all
    pl.semaphore_wait(barrier, n_seq - 1)
    copies = start_exchange(total, gathered, send, recv, n_seq)
    for copy in copies:
        copy.wait()
    d_bounds[...] = jnp.zeros((1, chans), F32)
    for n, (g, lanes) in enumerate(blocks):
        carry = jnp.zeros((1, 128), F32)
        for j in range(n_seq - 1, 0, -1):
            p_j = gathered[j, 2 * n : 2 * n + 1]
            m_j = gathered[j, 2 * n + 1 : 2 * n + 2]
            carry = jnp.where(j > s, m_j + p_j * carry, carry)
        product, message = ends[n]
        carries = [carry]
        for j in range(7, 0, -1):
            carries.append(message[j : j + 1] + product[j : j + 1] * carries[-1])
        carries = carries[::-1]
        for j in range(8):
            at = slice(j * part, (j + 1) * part)
            q_ref[n, at] = q_ref[n, at] + p_ref[n, at] * carries[j]
        acc = q_ref[n]
        bound = bounds[:, lanes]
        sigma_f = jax.nn.sigmoid(forget_raw[g, :, lanes].astype(F32))
        forget = bound + (1.0 - bound) * sigma_f
        value = in_raw[g, :, lanes].astype(F32)
        sigma_i = jax.nn.sigmoid(value)
        d_forget = acc * (before[g, :, lanes] * keep[g] - value * sigma_i)
        d_in[g, :, lanes] = (acc * (1.0 - forget) * silu_slope(value, sigma_i)).astype(BF16)
        d_sigma = d_forget * (1.0 - sigma_f)
        d_forget_raw[g, :, lanes] = (d_sigma * (1.0 - bound) * sigma_f).astype(BF16)
        d_bounds[:, lanes] += jnp.sum(d_sigma, 0, keepdims=True)


def backward_scan(d_state, in_raw, forget_raw, before, bounds, keep, collective_id):
    n_seq = lax.axis_size("seq")
    groups, rows, chans = in_raw.shape
    blocks = groups * chans // 128
    return pl.pallas_call(
        functools.partial(backward_scan_kernel, n_seq),
        out_shape=(
            jax.ShapeDtypeStruct(in_raw.shape, BF16),
            jax.ShapeDtypeStruct(in_raw.shape, BF16),
            jax.ShapeDtypeStruct((1, chans), F32),
        ),
        in_specs=[VMEM] * 6,
        out_specs=(VMEM, VMEM, VMEM),
        scratch_shapes=[
            pltpu.VMEM((blocks, rows, 128), F32),
            pltpu.VMEM((blocks, rows, 128), F32),
            pltpu.VMEM((2 * blocks, 128), F32),
            pltpu.VMEM((n_seq, 2 * blocks, 128), F32),
            pltpu.SemaphoreType.DMA((n_seq,)),
            pltpu.SemaphoreType.DMA((n_seq,)),
        ],
        compiler_params=params(collective_id),
        name="backward_scan",
    )(d_state, in_raw, forget_raw, before, bounds, keep)


def sum_all_kernel(n_seq, n_fsdp, x, out, middle, over_seq, over_fsdp, send, recv):
    s = lax.axis_index("seq")
    f = lax.axis_index("fsdp")
    along = [(lax.rem(s + k, n_seq), f) for k in range(1, n_seq)]
    across = [(s, lax.rem(f + k, n_fsdp)) for k in range(1, n_fsdp)]
    enter(along + across)
    copies = []
    for k, peer in enumerate(along):
        copy = remote(x, over_seq.at[k], send.at[k], recv.at[k], peer)
        copy.start()
        copies.append(copy)
    total = x[...]
    for k, copy in enumerate(copies):
        copy.wait_recv()
        total = total + over_seq[k]
    middle[...] = total
    later = []
    for k, peer in enumerate(across):
        slot = n_seq - 1 + k
        copy = remote(middle, over_fsdp.at[k], send.at[slot], recv.at[slot], peer)
        copy.start()
        later.append(copy)
    for k, copy in enumerate(later):
        copy.wait_recv()
        total = total + over_fsdp[k]
    out[...] = total
    for copy in copies + later:
        copy.wait_send()


def sum_all(x, collective_id):
    n_seq, n_fsdp = lax.axis_size("seq"), lax.axis_size("fsdp")
    count = n_seq + n_fsdp - 2
    return pl.pallas_call(
        functools.partial(sum_all_kernel, n_seq, n_fsdp),
        out_shape=jax.ShapeDtypeStruct(x.shape, F32),
        in_specs=[VMEM],
        out_specs=VMEM,
        scratch_shapes=[
            pltpu.VMEM(x.shape, F32),
            pltpu.VMEM((n_seq - 1,) + x.shape, F32),
            pltpu.VMEM((n_fsdp - 1,) + x.shape, F32),
            pltpu.SemaphoreType.DMA((count,)),
            pltpu.SemaphoreType.DMA((count,)),
        ],
        compiler_params=params(collective_id),
        name="sum_all",
    )(x)


def sum_over_seq(part):
    return lax.psum_scatter(part.astype(BF16), "seq", scatter_dimension=0, tiled=True).astype(F32)


def per_device(
    hidden,
    lengths,
    w_input,
    w_forget,
    w_gate_out,
    w_output,
    norm_gain,
    gate_gain,
    glu_gain,
    lower_table,
    w_glu_gate,
    w_glu_up,
    w_glu_down,
    cotangent,
):
    seq_index = lax.axis_index("seq")
    fsdp_index = lax.axis_index("fsdp")
    groups = lax.axis_size("fsdp")
    _, rows, width = hidden.shape
    chans = w_input.shape[1]
    units = w_glu_gate.shape[1]
    tokens = groups * rows
    small_shape = (round_up(groups, 8), round_up(rows, 128))

    def to_small(value):
        return jnp.pad(
            value, ((0, small_shape[0] - value.shape[0]), (0, small_shape[1] - value.shape[1]))
        )

    def dot(left, right):
        return jnp.dot(left, right, preferred_element_type=F32)

    def dot_t(left, right):
        return lax.dot_general(left, right, (((1,), (1,)), ((), ())), preferred_element_type=F32)

    def over_tokens(left, right):
        return lax.dot_general(left, right, (((0,), (0,)), ((), ())), preferred_element_type=F32)

    cotangent_all = lax.all_gather(cotangent[0], "fsdp").reshape(tokens, width)

    hidden_f = hidden[0].astype(F32)
    scale_one = lax.rsqrt(jnp.mean(hidden_f * hidden_f, -1, keepdims=True) + epsilon)
    normed = (hidden_f * scale_one * norm_gain).astype(BF16)
    normed_all, _ = gather(normed, jnp.zeros((8, 128), F32), 0)
    normed_all = normed_all.reshape(tokens, width)
    in_raw = dot(normed_all, w_input).astype(BF16).reshape(groups, rows, chans)
    forget_raw = dot(normed_all, w_forget).astype(BF16).reshape(groups, rows, chans)
    gate_raw = dot(normed_all, w_gate_out)

    bounds_full = lower_bound(lower_table)
    bounds = lax.dynamic_slice_in_dim(bounds_full, fsdp_index * chans, chans)[None]
    seq_starts = jnp.cumsum(lengths, axis=1) - lengths
    places = seq_index * rows + jnp.arange(rows, dtype=jnp.int32)
    starts = jnp.any(places[None, :, None] == seq_starts[:, None, :], axis=-1)
    keep = jnp.where(starts, 0.0, 1.0).astype(F32)[:, :, None]
    state_b, before = forward_scan(in_raw, forget_raw, bounds, keep, 1)

    state_f = state_b.astype(F32).reshape(tokens, chans)
    gain_slice = lax.dynamic_slice_in_dim(gate_gain, fsdp_index * chans, chans)
    sigma_g = jax.nn.sigmoid(gate_raw)
    silu_gate = gate_raw * sigma_g
    out_raw = (state_f * gain_slice * silu_gate).astype(BF16)
    squares = jnp.sum(state_f * state_f, -1).reshape(groups, rows)
    mixed_part = dot(out_raw, w_output).astype(BF16).reshape(groups, rows, width)
    mixed_raw, square_sum = reduce_rows(mixed_part, to_small(squares), 2)
    state_scale = lax.rsqrt(square_sum[:groups, :rows] / width + epsilon)
    own_scale = lax.dynamic_slice_in_dim(state_scale, fsdp_index, 1, 0)[0][:, None]
    scale_g = state_scale.reshape(tokens, 1)
    middle = hidden_f + own_scale * mixed_raw
    scale_two = lax.rsqrt(jnp.mean(middle * middle, -1, keepdims=True) + epsilon)
    normed_two = (middle * scale_two * glu_gain).astype(BF16)
    normed_two_all, _ = gather(normed_two, jnp.zeros((8, 128), F32), 3)
    normed_two_all = normed_two_all.reshape(tokens, width)

    gate_val = dot(normed_two_all, w_glu_gate)
    up_val = dot(normed_two_all, w_glu_up)
    sigma_u = jax.nn.sigmoid(gate_val)
    silu_u = gate_val * sigma_u
    activity = (silu_u * up_val).astype(BF16)
    down_grad = sum_over_seq(over_tokens(cotangent_all, activity))
    d_act = dot_t(cotangent_all, w_glu_down)
    d_gate = (d_act * up_val * silu_slope(gate_val, sigma_u)).astype(BF16)
    d_up = (d_act * silu_u).astype(BF16)
    pair_grad = sum_over_seq(
        jnp.concatenate(
            [
                over_tokens(normed_two_all, d_gate).astype(BF16),
                over_tokens(normed_two_all, d_up).astype(BF16),
            ],
            1,
        )
    )
    d_two_part = (dot_t(d_gate, w_glu_gate) + dot_t(d_up, w_glu_up)).astype(BF16)
    no_small = jnp.zeros((8, 128), F32)
    d_normed_two, _ = reduce_rows(d_two_part.reshape(groups, rows, width), no_small, 4)
    glu_part = dot(activity, w_glu_down).astype(BF16).reshape(groups, rows, width)
    glu_result = lax.psum_scatter(glu_part, "fsdp", scatter_dimension=0, tiled=True)[0]
    output = (middle + glu_result.astype(F32)).astype(BF16)[None]

    cotangent_f = cotangent[0].astype(F32)
    scaled_two = glu_gain * d_normed_two
    d_middle = (
        cotangent_f
        + scale_two * scaled_two
        - middle * scale_two**3 * jnp.mean(scaled_two * middle, -1, keepdims=True)
    )
    d_glu_gain = jnp.sum(d_normed_two * middle * scale_two, 0)
    d_mixed = d_middle.astype(BF16)
    own_dot = jnp.sum(d_mixed.astype(F32) * mixed_raw, -1)[None]
    d_mixed_all, dots = gather(d_mixed, to_small(own_dot), 5)
    d_mixed_all = d_mixed_all.reshape(tokens, width)
    dot_rows = dots[:, 0, :rows].reshape(tokens, 1)

    d_out = dot_t(d_mixed_all, w_output)
    scaled_state = state_f * scale_g
    d_gain_slice = jnp.sum(d_out * scaled_state * silu_gate, 0)
    d_scaled = d_out * gain_slice * silu_gate
    d_gate_raw = (d_out * scaled_state * gain_slice * silu_slope(gate_raw, sigma_g)).astype(BF16)
    d_state = scale_g * d_scaled - state_f * (scale_g**3 * (dot_rows / width))
    d_state = d_state.astype(BF16).reshape(groups, rows, chans)
    d_in, d_forget_raw, d_bounds = backward_scan(
        d_state, in_raw, forget_raw, before, bounds, keep, 6
    )
    d_in = d_in.reshape(tokens, chans)
    d_forget_raw = d_forget_raw.reshape(tokens, chans)

    d_normed_part = dot_t(d_in, w_input) + dot_t(d_forget_raw, w_forget)
    d_normed_part = (d_normed_part + dot_t(d_gate_raw, w_gate_out)).astype(BF16)
    out_gate = (out_raw.astype(F32) * scale_g).astype(BF16)
    mixer_grad = sum_over_seq(
        jnp.concatenate(
            [
                over_tokens(d_mixed_all, out_gate).astype(BF16),
                over_tokens(normed_all, d_in).astype(BF16),
                over_tokens(normed_all, d_forget_raw).astype(BF16),
                over_tokens(normed_all, d_gate_raw).astype(BF16),
            ],
            1,
        )
    )
    d_normed, _ = reduce_rows(d_normed_part.reshape(groups, rows, width), no_small, 7)
    scaled_one = norm_gain * d_normed
    d_hidden = (
        d_middle
        + scale_one * scaled_one
        - hidden_f * scale_one**3 * jnp.mean(scaled_one * hidden_f, -1, keepdims=True)
    )
    d_norm_gain = jnp.sum(d_normed * hidden_f * scale_one, 0)
    d_gain_full = lax.dynamic_update_slice(
        jnp.zeros((width,), F32), d_gain_slice, (fsdp_index * chans,)
    )
    d_bounds_full = lax.dynamic_update_slice(
        jnp.zeros((width,), F32), d_bounds[0], (fsdp_index * chans,)
    )
    sums = jnp.stack([d_norm_gain, d_glu_gain, d_gain_full, d_bounds_full])
    totals = sum_all(sums.reshape(8, width // 2), 8).reshape(4, width)
    _, bounds_pull = jax.vjp(lower_bound, lower_table)
    d_table = bounds_pull(totals[3])[0]
    return (
        output,
        d_hidden.astype(BF16)[None],
        mixer_grad[:, chans : 2 * chans],
        mixer_grad[:, 2 * chans : 3 * chans],
        mixer_grad[:, 3 * chans :],
        mixer_grad[:, :chans].T,
        totals[0],
        totals[2],
        totals[1],
        d_table,
        pair_grad[:, :units],
        pair_grad[:, units:],
        down_grad.T,
    )


def copy_in(src, dst, sem):
    copy = pltpu.make_async_copy(src, dst, sem)
    copy.start()
    return copy


class Links:
    def __init__(self, send, recv):
        self.send, self.recv, self.used = send, recv, 0

    def start(self, src, dst, device):
        copy = remote(src, dst, self.send.at[self.used], self.recv.at[self.used], device)
        self.used += 1
        copy.start()
        return copy


class Locals:
    def __init__(self, sems):
        self.sems, self.used = sems, 0

    def start(self, src, dst):
        copy = copy_in(src, dst, self.sems.at[self.used])
        self.used += 1
        return copy


def row_slots(rows):
    half = rows // 2
    top = [pl.ds(k * rows, half) for k in range(4)]
    bottom = [pl.ds(k * rows + half, half) for k in range(4)]
    return top, bottom


def gather_start(links, src, dst, rows, s, fx, fy):
    half = rows // 2
    top, bottom = row_slots(rows)
    here = (pl.ds(0, half), pl.ds(half, half))
    return [
        links.start(src.at[here[0]], dst.at[top[1]], (s, fx)),
        links.start(src.at[here[1]], dst.at[bottom[2]], (s, fy)),
        links.start(src.at[here[1]], dst.at[bottom[1]], (s, fx)),
        links.start(src.at[here[0]], dst.at[top[2]], (s, fy)),
    ]


def gather_forward(links, own, dst, rows, s, fx, fy):
    top, bottom = row_slots(rows)
    own[0].wait_recv()
    on_y = links.start(dst.at[top[1]], dst.at[top[3]], (s, fy))
    own[1].wait_recv()
    on_x = links.start(dst.at[bottom[2]], dst.at[bottom[3]], (s, fx))
    return [on_y, on_x]


def gather_middle(own):
    own[2].wait_recv()
    own[3].wait_recv()


def gather_far(later):
    for copy in later:
        copy.wait_recv()


def sends_done(*lists):
    for copies in lists:
        for copy in copies:
            copy.wait_send()


def wait_all(*lists):
    for copies in lists:
        for copy in copies:
            copy.wait()


def reduce_start_far(links, part, from_x, from_y, rows, s, fx, fy):
    top, bottom = row_slots(rows)
    return [
        links.start(part.at[top[3]], from_x.at[0], (s, fx)),
        links.start(part.at[bottom[3]], from_y.at[0], (s, fy)),
    ]


def reduce_start_near(links, part, from_x, from_y, rows, s, fx, fy):
    top, bottom = row_slots(rows)
    return [
        links.start(part.at[top[1]], from_x.at[1], (s, fx)),
        links.start(part.at[bottom[2]], from_y.at[1], (s, fy)),
    ]


def reduce_pass(links, far, part, from_x, from_y, pass_x, pass_y, rows, s, fx, fy):
    top, bottom = row_slots(rows)
    far[0].wait_recv()
    pass_y[...] = (from_x[0].astype(F32) + part[top[2]].astype(F32)).astype(BF16)
    on_y = links.start(pass_y, from_y.at[2], (s, fy))
    far[1].wait_recv()
    pass_x[...] = (from_y[0].astype(F32) + part[bottom[1]].astype(F32)).astype(BF16)
    on_x = links.start(pass_x, from_x.at[2], (s, fx))
    return [on_y, on_x]


def mm(left, right):
    return jnp.dot(left, right, preferred_element_type=F32)


def mm_t(left, right):
    return lax.dot_general(left, right, (((1,), (1,)), ((), ())), preferred_element_type=F32)


def tile(n, width):
    return pl.ds(pl.multiple_of(n * width, width), width)


def bounds_slice(table, first, count):
    rows = table[:, pl.ds(pl.multiple_of(first, 128), count)]
    powers = jnp.exp(rows - jnp.max(rows, 0, keepdims=True))
    return jnp.sum(powers[1 : LAYER + 1], 0, keepdims=True) / jnp.sum(powers, 0, keepdims=True)


def keep_rows(lengths, group, first, rows):
    places = first + lax.broadcasted_iota(jnp.int32, (rows, 128), 0)
    start = jnp.int32(0)
    keep = jnp.where(places == start, 0.0, 1.0)
    for i in range(lengths.shape[1] - 1):
        start = start + lengths[group, i]
        keep = jnp.where(places == start, 0.0, keep)
    return keep.astype(F32)


def segment_totals(end_p, end_s, blocks, order):
    first, rest = order[0], order[1:]
    p_all = end_p[pl.ds(first, blocks, stride=8), :]
    s_all = end_s[pl.ds(first, blocks, stride=8), :]
    for j in rest:
        p_j = end_p[pl.ds(j, blocks, stride=8), :]
        s_all = end_s[pl.ds(j, blocks, stride=8), :] + p_j * s_all
        p_all = p_all * p_j
    return p_all, s_all


def spread_carry(carry, carr, end_p, end_s, blocks, order):
    for i, j in enumerate(order):
        carr[pl.ds(j, blocks, stride=8), :] = carry
        if i < 7:
            carry = end_s[pl.ds(j, blocks, stride=8), :] + end_p[pl.ds(j, blocks, stride=8), :] * carry


def mixer_kernel(
    n_seq,
    lengths,
    hidden,
    cot,
    norm_gain,
    gate_gain,
    glu_gain,
    table,
    w_in,
    w_fg,
    w_gt,
    w_out,
    normed_half,
    cot_out,
    in_out,
    fg_out,
    gate_out,
    state_out,
    raw_out,
    before_out,
    scale_out,
    middle,
    two,
    wv,
    wo,
    rows_all,
    stage,
    in_ref,
    fg_ref,
    gate_ref,
    a_ref,
    b_ref,
    shifted,
    keep_ref,
    end_p,
    end_s,
    carr,
    total,
    gathered,
    state_ref,
    raw_ref,
    squares,
    squares_in,
    part,
    from_x,
    from_y,
    pass_x,
    pass_y,
    send,
    recv,
    exchange_send,
    exchange_recv,
    local_sems,
):
    rows, width = hidden.shape
    chans = w_in.shape[1]
    lanes_of = [slice(c, c + 128) for c in range(0, chans, 128)]
    count = len(lanes_of)
    blocks = 4 * count
    step_len = rows // 8
    s, f, fx, fy, fd = plane()
    groups = [f, fx, fy, fd]
    links, local = Links(send, recv), Locals(local_sems)

    weights = [
        local.start(w, wv.at[:, pl.ds(i * chans, chans)]) for i, w in enumerate((w_in, w_fg, w_gt))
    ]
    weights.append(local.start(w_out, wo))
    barrier = pltpu.get_barrier_semaphore()
    peers = [(s, fx), (s, fy), (s, fd)] + seq_peers(n_seq)
    for peer in peers:
        pl.semaphore_signal(barrier, inc=1, device_id=peer, device_id_type=MESH)

    def norm_rows(i, _):
        at = pl.ds(pl.multiple_of(i * 16, 16), 16)
        value = hidden[at].astype(F32)
        scale = lax.rsqrt(jnp.mean(value * value, -1, keepdims=True) + epsilon)
        rows_all[at] = (value * scale * norm_gain[...]).astype(BF16)
        return 0

    lax.fori_loop(0, rows // 16, norm_rows, 0)
    pl.semaphore_wait(barrier, len(peers))
    own = gather_start(links, rows_all, rows_all, rows, s, fx, fy)
    bound = bounds_slice(table, f * chans, chans)
    for k in range(4):
        keep_ref[k] = keep_rows(lengths, groups[k], s * rows, rows)
    squares[...] = jnp.zeros_like(squares)
    for copy in weights[:3]:
        copy.wait()

    def project(first, slots):
        def tile_of(n, _):
            cols = tile(n, 256)
            stage[: slots * rows, cols] = mm(
                rows_all[first * rows : (first + slots) * rows], wv[:, cols]
            )
            return 0

        lax.fori_loop(0, 3 * chans // 256, tile_of, 0)
        for k in range(slots):
            at = slice(k * rows, (k + 1) * rows)
            for c, lanes in enumerate(lanes_of):
                n = (first + k) * count + c
                value = stage[at, lanes].astype(BF16)
                in_ref[first + k, :, lanes] = value
                value = value.astype(F32)
                raw = stage[at, chans + c * 128 : chans + (c + 1) * 128].astype(BF16)
                fg_ref[first + k, :, lanes] = raw
                edge = bound[:, lanes]
                forget = edge + (1.0 - edge) * jax.nn.sigmoid(raw.astype(F32))
                a_ref[n] = forget * keep_ref[first + k]
                b_ref[n] = value * jax.nn.sigmoid(value) * (1.0 - forget)
            gate_ref[first + k] = stage[at, 2 * chans :]

    project(0, 1)
    later = gather_forward(links, own, rows_all, rows, s, fx, fy)
    gather_middle(own)
    project(1, 2)
    gather_far(later)
    cot_own = gather_start(links, cot, cot_out, rows, s, fx, fy)
    core = s % 2
    swaps, outs = swap_columns(
        links, local, rows_all, normed_half, n_seq, core, (s + 1 - 2 * core, f)
    )
    outs.append(local.start(cot, cot_out.at[pl.ds(0, rows)]))
    project(3, 1)
    outs += [
        local.start(in_ref, in_out),
        local.start(fg_ref, fg_out),
        local.start(gate_ref, gate_out),
    ]

    def scan_step(i, carry):
        new = []
        at = pl.ds(i, 8, stride=step_len)
        for n, (product, state) in enumerate(carry):
            a = a_ref[n, at, :]
            state = a * state + b_ref[n, at, :]
            product = product * a
            a_ref[n, at, :] = product
            b_ref[n, at, :] = state
            new.append((product, state))
        return tuple(new)

    start = tuple((jnp.ones((8, 128), F32), jnp.zeros((8, 128), F32)) for _ in range(blocks))
    ends = lax.fori_loop(0, step_len, scan_step, start)
    for n, (product, state) in enumerate(ends):
        end_p[8 * n : 8 * n + 8] = product
        end_s[8 * n : 8 * n + 8] = state
    p_all, s_all = segment_totals(end_p, end_s, blocks, range(8))
    total[:blocks] = p_all
    total[blocks:] = s_all
    copies = start_exchange(total, gathered, exchange_send, exchange_recv, n_seq)
    wait_all(copies)
    carry = jnp.zeros((blocks, 128), F32)
    for j in range(n_seq - 1):
        carry = jnp.where(j < s, gathered[j, blocks:] + gathered[j, :blocks] * carry, carry)
    for n in range(blocks):
        shifted[n, 0:1] = carry[n : n + 1]
    spread_carry(carry, carr, end_p, end_s, blocks, range(8))

    def finish(n, _):
        enter_state = carr[pl.ds(pl.multiple_of(n * 8, 8), 8)]
        for i in range(step_len):
            at = pl.ds(i, 8, stride=step_len)
            state = b_ref[n, at, :] + a_ref[n, at, :] * enter_state
            b_ref[n, at, :] = state
            shifted[n, pl.ds(i + 1, 8, stride=step_len), :] = state
        return 0

    lax.fori_loop(0, blocks, finish, 0)
    outs.append(local.start(shifted.at[:, pl.ds(0, rows)], before_out))

    lane = lax.broadcasted_iota(jnp.int32, (rows, 128), 1)
    for k in (3, 1, 2, 0):
        square = jnp.zeros((rows, 1), F32)
        for c, lanes in enumerate(lanes_of):
            state_b = b_ref[k * count + c].astype(BF16)
            state_ref[k, :, lanes] = state_b
            state = state_b.astype(F32)
            square = square + jnp.sum(state * state, -1, keepdims=True)
            gate = gate_ref[k, :, lanes]
            gain = gate_gain[:, pl.ds(pl.multiple_of(f * chans + c * 128, 128), 128)]
            raw_ref[k * rows : (k + 1) * rows, lanes] = (
                state * gain * gate * jax.nn.sigmoid(gate)
            ).astype(BF16)
        squares[...] = jnp.where(lane == groups[k], square, squares[...])
    square_copies = [
        links.start(squares, squares_in.at[i], (s, peer)) for i, peer in enumerate((fx, fy, fd))
    ]
    outs += [local.start(state_ref, state_out), local.start(raw_ref, raw_out)]
    cot_later = gather_forward(links, cot_own, cot_out, rows, s, fx, fy)
    weights[3].wait()

    def output_part(first, slots):
        at = slice(first * rows, (first + slots) * rows)

        def tile_of(n, _):
            cols = tile(n, 512)
            part[at, cols] = mm(raw_ref[at], wo[:, cols]).astype(BF16)
            return 0

        lax.fori_loop(0, width // 512, tile_of, 0)

    output_part(3, 1)
    far = reduce_start_far(links, part, from_x, from_y, rows, s, fx, fy)
    output_part(1, 2)
    near = reduce_start_near(links, part, from_x, from_y, rows, s, fx, fy)
    output_part(0, 1)
    passed = reduce_pass(links, far, part, from_x, from_y, pass_x, pass_y, rows, s, fx, fy)
    for copy in square_copies:
        copy.wait_recv()
    all_squares = (squares[...] + squares_in[0]) + (squares_in[1] + squares_in[2])
    scales = lax.rsqrt(all_squares / width + epsilon)
    for k in range(4):
        scale_out[k] = jnp.sum(jnp.where(lane == groups[k], scales, 0.0), -1, keepdims=True)
    for copy in near + passed:
        copy.wait_recv()
    half = rows // 2
    for first, one, other in ((0, from_x.at[1], from_y.at[2]), (half, from_y.at[1], from_x.at[2])):

        def sum_rows(i, _):
            here = pl.ds(pl.multiple_of(i * 16, 16), 16)
            at = pl.ds(pl.multiple_of(first + i * 16, 16), 16)
            mixed = part[at].astype(F32) + one[here].astype(F32) + other[here].astype(F32)
            value = hidden[at].astype(F32) + scale_out[0, at] * mixed
            middle[at] = value
            scale = lax.rsqrt(jnp.mean(value * value, -1, keepdims=True) + epsilon)
            two[at] = (value * scale * glu_gain[...]).astype(BF16)
            return 0

        lax.fori_loop(0, half // 16, sum_rows, 0)
    gather_middle(cot_own)
    gather_far(cot_later)
    sends_done(own, later, cot_own, cot_later, square_copies, far, near, passed)
    wait_all(swaps, outs)


def mixer_forward(lengths, hidden, cot, gains, table, weights, collective_id):
    n_seq = lax.axis_size("seq")
    rows, width = hidden.shape
    chans = weights[0].shape[1]
    blocks = 4 * chans // 128
    tokens = 4 * rows
    half = rows // 2
    shape = jax.ShapeDtypeStruct
    wide = shape((tokens, width), BF16)
    narrow = shape((4, rows, chans), BF16)
    return pl.pallas_call(
        functools.partial(mixer_kernel, n_seq),
        out_shape=(
            shape((2, tokens, width // 2), BF16),
            wide,
            narrow,
            narrow,
            shape((4, rows, chans), F32),
            narrow,
            shape((tokens, chans), BF16),
            shape((blocks, rows, 128), F32),
            shape((4, rows, 1), F32),
            shape((rows, width), F32),
            shape((rows, width), BF16),
        ),
        in_specs=[pl.BlockSpec(memory_space=pltpu.SMEM), VMEM, VMEM, VMEM, VMEM, VMEM, VMEM]
        + [ANY] * 4,
        out_specs=(ANY,) * 8 + (VMEM,) * 3,
        scratch_shapes=[
            pltpu.VMEM((width, 3 * chans), BF16),
            pltpu.VMEM((chans, width), BF16),
            pltpu.VMEM((tokens, width), BF16),
            pltpu.VMEM((2 * rows, 3 * chans), F32),
            pltpu.VMEM((4, rows, chans), BF16),
            pltpu.VMEM((4, rows, chans), BF16),
            pltpu.VMEM((4, rows, chans), F32),
            pltpu.VMEM((blocks, rows, 128), F32),
            pltpu.VMEM((blocks, rows, 128), F32),
            pltpu.VMEM((blocks, rows + 8, 128), F32),
            pltpu.VMEM((4, rows, 128), F32),
            pltpu.VMEM((8 * blocks, 128), F32),
            pltpu.VMEM((8 * blocks, 128), F32),
            pltpu.VMEM((8 * blocks, 128), F32),
            pltpu.VMEM((2 * blocks, 128), F32),
            pltpu.VMEM((n_seq, 2 * blocks, 128), F32),
            pltpu.VMEM((4, rows, chans), BF16),
            pltpu.VMEM((tokens, chans), BF16),
            pltpu.VMEM((rows, 128), F32),
            pltpu.VMEM((3, rows, 128), F32),
            pltpu.VMEM((tokens, width), BF16),
            pltpu.VMEM((3, half, width), BF16),
            pltpu.VMEM((3, half, width), BF16),
            pltpu.VMEM((half, width), BF16),
            pltpu.VMEM((half, width), BF16),
            pltpu.SemaphoreType.DMA((21 + n_seq // 2,)),
            pltpu.SemaphoreType.DMA((21 + n_seq // 2,)),
            pltpu.SemaphoreType.DMA((n_seq,)),
            pltpu.SemaphoreType.DMA((n_seq,)),
            pltpu.SemaphoreType.DMA((11 + n_seq // 2,)),
        ],
        compiler_params=params(collective_id),
        name="mixer_forward",
    )(lengths, hidden, cot, *gains, table, *weights)


def swap_columns(links, local, src, dst, n_seq, core, mate):
    part = src.shape[1] // n_seq
    copies, stays = [], []
    for z in range(n_seq // 2):
        to = pl.ds(z * part, part)
        theirs = pl.ds(pl.multiple_of((2 * z + 1 - core) * part, part), part)
        ours = pl.ds(pl.multiple_of((2 * z + core) * part, part), part)
        copies.append(links.start(src.at[:, theirs], dst.at[1, :, to], mate))
        stays.append(local.start(src.at[:, ours], dst.at[0, :, to]))
    return copies, stays


def swap_rows(links, local, src, dst, at, mate):
    copy = links.start(src.at[at], dst.at[1, at], mate)
    return copy, local.start(src.at[at], dst.at[0, at])


def glu_kernel(
    n_seq,
    two,
    cot_all,
    w_gate,
    w_up,
    w_down,
    two_half,
    cot_half,
    act_pair,
    gate_pair,
    up_pair,
    wv,
    wd,
    cot_ref,
    two_ref,
    d_act,
    stage,
    act,
    d_gate,
    d_up,
    send,
    recv,
    local_sems,
):
    rows = two.shape[0]
    units = w_gate.shape[1]
    s, f, fx, fy, fd = plane()
    core = s % 2
    mate = (s + 1 - 2 * core, f)
    links, local = Links(send, recv), Locals(local_sems)
    loads = [
        local.start(w_down, wd),
        local.start(cot_all, cot_ref),
        local.start(w_gate, wv.at[:, pl.ds(0, units)]),
        local.start(w_up, wv.at[:, pl.ds(units, units)]),
    ]
    two_ref[:rows] = two[...]
    enter([(s, fx), (s, fy), mate])
    own = gather_start(links, two_ref, two_ref, rows, s, fx, fy)
    loads[0].wait()
    loads[1].wait()
    swaps, stays = swap_columns(links, local, cot_ref, cot_half, n_seq, core, mate)

    def act_tile(n, _):
        cols = tile(n, 256)
        d_act[:, cols] = mm_t(cot_ref[...], wd[cols])
        return 0

    lax.fori_loop(0, units // 256, act_tile, 0)
    if units % 256:
        rest = slice(units // 256 * 256, units)
        d_act[:, rest] = mm_t(cot_ref[...], wd[rest])
    later = gather_forward(links, own, two_ref, rows, s, fx, fy)
    loads[2].wait()
    loads[3].wait()

    def slots(first, number):
        nonlocal swaps, stays
        base = first * rows

        def tile_of(n, _):
            cols = tile(n, 256)
            stage[: number * rows, cols] = mm(two_ref[base : base + number * rows], wv[:, cols])
            return 0

        lax.fori_loop(0, 2 * units // 256, tile_of, 0)

        def rows_of(i, _):
            at = pl.ds(pl.multiple_of(i * 16, 16), 16)
            to = pl.ds(pl.multiple_of(base + i * 16, 16), 16)
            gate, up = stage[at, :units], stage[at, units:]
            sigma = jax.nn.sigmoid(gate)
            silu = gate * sigma
            act[to] = (silu * up).astype(BF16)
            d = d_act[to]
            d_gate[to] = (d * up * silu_slope(gate, sigma)).astype(BF16)
            d_up[to] = (d * silu).astype(BF16)
            return 0

        lax.fori_loop(0, number * rows // 16, rows_of, 0)
        at = pl.ds(base, number * rows)
        for src, dst in ((act, act_pair), (d_gate, gate_pair), (d_up, up_pair)):
            sent, stayed = swap_rows(links, local, src, dst, at, mate)
            swaps, stays = swaps + [sent], stays + [stayed]

    slots(0, 1)
    gather_middle(own)
    slots(1, 2)
    gather_far(later)
    more, keeps = swap_columns(links, local, two_ref, two_half, n_seq, core, mate)
    slots(3, 1)
    sends_done(own, later)
    wait_all(swaps, stays, more, keeps)


def glu(two, cot_all, w_gate, w_up, w_down, collective_id):
    n_seq = lax.axis_size("seq")
    rows, width = two.shape
    units = w_gate.shape[1]
    tokens = 4 * rows
    shape = jax.ShapeDtypeStruct
    half = shape((2, tokens, width // 2), BF16)
    pair = shape((2, tokens, units), BF16)
    remote_count = 6 + n_seq + 9
    return pl.pallas_call(
        functools.partial(glu_kernel, n_seq),
        out_shape=(half, half, pair, pair, pair),
        in_specs=[VMEM] + [ANY] * 4,
        out_specs=(ANY,) * 5,
        scratch_shapes=[
            pltpu.VMEM((width, 2 * units), BF16),
            pltpu.VMEM((units, width), BF16),
            pltpu.VMEM((tokens, width), BF16),
            pltpu.VMEM((tokens, width), BF16),
            pltpu.VMEM((tokens, units), F32),
            pltpu.VMEM((2 * rows, 2 * units), F32),
            pltpu.VMEM((tokens, units), BF16),
            pltpu.VMEM((tokens, units), BF16),
            pltpu.VMEM((tokens, units), BF16),
            pltpu.SemaphoreType.DMA((remote_count,)),
            pltpu.SemaphoreType.DMA((remote_count,)),
            pltpu.SemaphoreType.DMA((4 + n_seq + 9,)),
        ],
        compiler_params=params(collective_id),
        name="glu",
    )(two, cot_all, w_gate, w_up, w_down)


def slot_gather_kernel(x, small, out, out_small, send, recv, local_sems):
    s, f, fx, fy, fd = plane()
    rows = x.shape[0]
    links, local = Links(send, recv), Locals(local_sems)
    enter([(s, fx), (s, fy), (s, fd)])
    own = gather_start(links, x, out, rows, s, fx, fy)
    smalls = [
        links.start(small, out_small.at[k], (s, peer))
        for k, peer in ((1, fx), (2, fy), (3, fd))
    ]
    stay = local.start(x, out.at[pl.ds(0, rows)])
    out_small[0] = small[...]
    later = gather_forward(links, own, out, rows, s, fx, fy)
    gather_middle(own)
    gather_far(later)
    sends_done(own, later)
    wait_all(smalls, [stay])


def slot_gather(x, small, collective_id):
    rows, width = x.shape
    return pl.pallas_call(
        slot_gather_kernel,
        out_shape=(
            jax.ShapeDtypeStruct((4 * rows, width), BF16),
            jax.ShapeDtypeStruct((4,) + small.shape, F32),
        ),
        in_specs=[VMEM, VMEM],
        out_specs=(ANY, VMEM),
        scratch_shapes=[
            pltpu.SemaphoreType.DMA((9,)),
            pltpu.SemaphoreType.DMA((9,)),
            pltpu.SemaphoreType.DMA((1,)),
        ],
        compiler_params=params(collective_id),
        name="slot_gather",
    )(x, small)


def slot_reduce_kernel(part, out, from_x, from_y, pass_x, pass_y, send, recv):
    s, f, fx, fy, fd = plane()
    rows = out.shape[0]
    half = rows // 2
    links = Links(send, recv)
    enter([(s, fx), (s, fy)])
    far = reduce_start_far(links, part, from_x, from_y, rows, s, fx, fy)
    near = reduce_start_near(links, part, from_x, from_y, rows, s, fx, fy)
    passed = reduce_pass(links, far, part, from_x, from_y, pass_x, pass_y, rows, s, fx, fy)
    for copy in near + passed:
        copy.wait_recv()
    out[:half] = part[:half].astype(F32) + from_x[1].astype(F32) + from_y[2].astype(F32)
    out[half:] = part[half:rows].astype(F32) + from_y[1].astype(F32) + from_x[2].astype(F32)
    sends_done(far, near, passed)


def slot_reduce(part, collective_id):
    tokens, width = part.shape
    rows = tokens // 4
    half = (rows // 2, width)
    return pl.pallas_call(
        slot_reduce_kernel,
        out_shape=jax.ShapeDtypeStruct((rows, width), F32),
        in_specs=[VMEM],
        out_specs=VMEM,
        scratch_shapes=[
            pltpu.VMEM((3,) + half, BF16),
            pltpu.VMEM((3,) + half, BF16),
            pltpu.VMEM(half, BF16),
            pltpu.VMEM(half, BF16),
            pltpu.SemaphoreType.DMA((6,)),
            pltpu.SemaphoreType.DMA((6,)),
        ],
        compiler_params=params(collective_id),
        name="slot_reduce",
    )(part)


def mixer_backward_kernel(
    n_seq,
    lengths,
    d_state,
    in_raw,
    fg_raw,
    before,
    table,
    d_gate_raw,
    out_gate,
    d_mixed_all,
    in_pair,
    fg_pair,
    gate_pair,
    out_pair,
    mixed_half,
    d_bounds,
    p_ref,
    q_ref,
    end_p,
    end_s,
    carr,
    total,
    gathered,
    keep_ref,
    d_in,
    d_fg,
    send,
    recv,
    exchange_send,
    exchange_recv,
    local_sems,
):
    _, rows, chans = in_raw.shape
    lanes_of = [slice(c, c + 128) for c in range(0, chans, 128)]
    count = len(lanes_of)
    blocks = 4 * count
    step_len = rows // 8
    s, f, fx, fy, fd = plane()
    groups = [f, fx, fy, fd]
    core = s % 2
    mate = (s + 1 - 2 * core, f)
    links, local = Links(send, recv), Locals(local_sems)
    barrier = pltpu.get_barrier_semaphore()
    peers = seq_peers(n_seq)
    for peer in peers:
        pl.semaphore_signal(barrier, inc=1, device_id=peer, device_id_type=MESH)
    bound = bounds_slice(table, f * chans, chans)
    for k in range(4):
        keep_ref[k] = keep_rows(lengths, groups[k], s * rows, rows)
        for c, lanes in enumerate(lanes_of):
            edge = bound[:, lanes]
            forget = edge + (1.0 - edge) * jax.nn.sigmoid(fg_raw[k, :, lanes].astype(F32))
            p_ref[k * count + c] = forget * keep_ref[k]
            q_ref[k * count + c] = d_state[k, :, lanes].astype(F32)

    def scan_step(i, carry):
        new = []
        at = pl.ds(step_len - 1 - i, 8, stride=step_len)
        for n, (product, message) in enumerate(carry):
            a = p_ref[n, at, :]
            acc = q_ref[n, at, :] + message
            p_ref[n, at, :] = product
            q_ref[n, at, :] = acc
            new.append((product * a, a * acc))
        return tuple(new)

    start = tuple((jnp.ones((8, 128), F32), jnp.zeros((8, 128), F32)) for _ in range(blocks))
    ends = lax.fori_loop(0, step_len, scan_step, start)
    for n, (product, message) in enumerate(ends):
        end_p[8 * n : 8 * n + 8] = product
        end_s[8 * n : 8 * n + 8] = message
    p_all, s_all = segment_totals(end_p, end_s, blocks, range(7, -1, -1))
    total[:blocks] = p_all
    total[blocks:] = s_all
    pl.semaphore_wait(barrier, len(peers))
    copies = start_exchange(total, gathered, exchange_send, exchange_recv, n_seq)
    wait_all(copies)
    everything = pl.ds(0, 4 * rows)
    swaps, stays = swap_columns(links, local, d_mixed_all, mixed_half, n_seq, core, mate)
    for src, dst in ((d_gate_raw, gate_pair), (out_gate, out_pair)):
        sent, stayed = swap_rows(links, local, src, dst, everything, mate)
        swaps, stays = swaps + [sent], stays + [stayed]
    carry = jnp.zeros((blocks, 128), F32)
    for j in range(n_seq - 1, 0, -1):
        carry = jnp.where(j > s, gathered[j, blocks:] + gathered[j, :blocks] * carry, carry)
    spread_carry(carry, carr, end_p, end_s, blocks, range(7, -1, -1))

    def finish(n, _):
        enter_state = carr[pl.ds(pl.multiple_of(n * 8, 8), 8)]
        for i in range(step_len):
            at = pl.ds(i, 8, stride=step_len)
            q_ref[n, at, :] = q_ref[n, at, :] + p_ref[n, at, :] * enter_state
        return 0

    lax.fori_loop(0, blocks, finish, 0)
    d_bounds[...] = jnp.zeros_like(d_bounds)
    for k in range(4):
        at = slice(k * rows, (k + 1) * rows)
        for c, lanes in enumerate(lanes_of):
            acc = q_ref[k * count + c]
            edge = bound[:, lanes]
            sigma_f = jax.nn.sigmoid(fg_raw[k, :, lanes].astype(F32))
            forget = edge + (1.0 - edge) * sigma_f
            value = in_raw[k, :, lanes].astype(F32)
            sigma_i = jax.nn.sigmoid(value)
            d_forget = acc * (before[k * count + c] * keep_ref[k] - value * sigma_i)
            d_in[at, lanes] = (acc * (1.0 - forget) * silu_slope(value, sigma_i)).astype(BF16)
            d_sigma = d_forget * (1.0 - sigma_f)
            d_fg[at, lanes] = (d_sigma * (1.0 - edge) * sigma_f).astype(BF16)
            d_bounds[:, lanes] += jnp.sum(d_sigma, 0, keepdims=True)
    for src, dst in ((d_in, in_pair), (d_fg, fg_pair)):
        sent, stayed = swap_rows(links, local, src, dst, everything, mate)
        swaps, stays = swaps + [sent], stays + [stayed]
    wait_all(swaps, stays)


def mixer_backward(
    lengths, d_state, in_raw, fg_raw, before, table, d_gate_raw, out_gate, d_mixed_all, collective_id
):
    n_seq = lax.axis_size("seq")
    _, rows, chans = in_raw.shape
    width = d_mixed_all.shape[1]
    tokens = 4 * rows
    blocks = 4 * chans // 128
    shape = jax.ShapeDtypeStruct
    pair = shape((2, tokens, chans), BF16)
    remote_count = n_seq // 2 + 4
    return pl.pallas_call(
        functools.partial(mixer_backward_kernel, n_seq),
        out_shape=(
            pair,
            pair,
            pair,
            pair,
            shape((2, tokens, width // 2), BF16),
            shape((1, chans), F32),
        ),
        in_specs=[pl.BlockSpec(memory_space=pltpu.SMEM)] + [VMEM] * 8,
        out_specs=(ANY,) * 5 + (VMEM,),
        scratch_shapes=[
            pltpu.VMEM((blocks, rows, 128), F32),
            pltpu.VMEM((blocks, rows, 128), F32),
            pltpu.VMEM((8 * blocks, 128), F32),
            pltpu.VMEM((8 * blocks, 128), F32),
            pltpu.VMEM((8 * blocks, 128), F32),
            pltpu.VMEM((2 * blocks, 128), F32),
            pltpu.VMEM((n_seq, 2 * blocks, 128), F32),
            pltpu.VMEM((4, rows, 128), F32),
            pltpu.VMEM((tokens, chans), BF16),
            pltpu.VMEM((tokens, chans), BF16),
            pltpu.SemaphoreType.DMA((remote_count,)),
            pltpu.SemaphoreType.DMA((remote_count,)),
            pltpu.SemaphoreType.DMA((n_seq,)),
            pltpu.SemaphoreType.DMA((n_seq,)),
            pltpu.SemaphoreType.DMA((remote_count,)),
        ],
        compiler_params=params(collective_id),
        name="mixer_backward",
    )(lengths, d_state, in_raw, fg_raw, before, table, d_gate_raw, out_gate, d_mixed_all)


def sum_over_z(part):
    n_seq = lax.axis_size("seq")
    cores = [list(range(core, n_seq, 2)) for core in range(2)]
    return lax.psum_scatter(
        part, "seq", scatter_dimension=0, tiled=True, axis_index_groups=cores
    )


def plane_device(
    hidden,
    lengths,
    w_input,
    w_forget,
    w_gate_out,
    w_output,
    norm_gain,
    gate_gain,
    glu_gain,
    lower_table,
    w_glu_gate,
    w_glu_up,
    w_glu_down,
    cotangent,
):
    fsdp_index = lax.axis_index("fsdp")
    hidden, cotangent = hidden[0], cotangent[0]
    rows, width = hidden.shape
    chans = w_input.shape[1]
    units = w_glu_gate.shape[1]
    tokens = 4 * rows
    small_shape = (8, round_up(rows, 128))

    def over_pairs(left, right):
        left, right = left.reshape(2 * tokens, -1), right.reshape(2 * tokens, -1)
        return lax.dot_general(
            left, right, (((0,), (0,)), ((), ())), preferred_element_type=F32
        ).astype(BF16)

    gains = (norm_gain[None], gate_gain[None], glu_gain[None])
    (
        normed_half,
        cot_all,
        in_raw,
        fg_raw,
        gate_raw,
        state_b,
        out_raw,
        before,
        scale_g,
        middle,
        normed_two,
    ) = mixer_forward(
        lengths,
        hidden,
        cotangent,
        gains,
        lower_table,
        (w_input, w_forget, w_gate_out, w_output),
        0,
    )
    two_half, cot_half, act_pair, gate_pair, up_pair = glu(
        normed_two, cot_all, w_glu_gate, w_glu_up, w_glu_down, 1
    )
    down_part = over_pairs(cot_half, act_pair)
    down_grad = sum_over_z(down_part)
    d_gate, d_up = gate_pair[0], up_pair[0]
    gate_pair, up_pair, down_part = lax.optimization_barrier((gate_pair, up_pair, down_part))
    pair_part = jnp.concatenate([over_pairs(two_half, gate_pair), over_pairs(two_half, up_pair)], 1)
    d_gate, d_up, down_part = lax.optimization_barrier((d_gate, d_up, down_part))
    d_two_part = (mm_t(d_gate, w_glu_gate) + mm_t(d_up, w_glu_up)).astype(BF16)
    d_normed_two = slot_reduce(d_two_part, 2)
    pair_part, down_grad, d_normed_two = lax.optimization_barrier(
        (pair_part, down_grad, d_normed_two)
    )
    pair_grad = sum_over_z(pair_part)

    hidden_f = hidden.astype(F32)
    cotangent_f = cotangent.astype(F32)
    scale_two = lax.rsqrt(jnp.mean(middle * middle, -1, keepdims=True) + epsilon)
    scaled_two = glu_gain * d_normed_two
    d_middle = (
        cotangent_f
        + scale_two * scaled_two
        - middle * scale_two**3 * jnp.mean(scaled_two * middle, -1, keepdims=True)
    )
    d_glu_gain = jnp.sum(d_normed_two * middle * scale_two, 0)
    d_mixed = d_middle.astype(BF16)
    own_dot = jnp.sum(d_mixed.astype(F32) * (middle - hidden_f), -1)[None]
    own_dot = jnp.pad(own_dot, ((0, 7), (0, small_shape[1] - rows)))
    d_mixed_all, dots = slot_gather(d_mixed, own_dot, 3)
    dot_rows = dots[:, 0, :rows].reshape(tokens, 1)

    scale_g = scale_g.reshape(tokens, 1)
    gate_raw = gate_raw.reshape(tokens, chans)
    state_f = state_b.astype(F32).reshape(tokens, chans)
    gain_slice = lax.dynamic_slice_in_dim(gate_gain, fsdp_index * chans, chans)
    sigma_g = jax.nn.sigmoid(gate_raw)
    silu_gate = gate_raw * sigma_g
    d_out = mm_t(d_mixed_all, w_output)
    scaled_state = state_f * scale_g
    d_gain_slice = jnp.sum(d_out * scaled_state * silu_gate, 0)
    d_scaled = d_out * gain_slice * silu_gate
    d_gate_raw = (d_out * scaled_state * gain_slice * silu_slope(gate_raw, sigma_g)).astype(BF16)
    d_state = scale_g * d_scaled - state_f * (scale_g**2 * (dot_rows / width))
    d_state = d_state.astype(BF16).reshape(4, rows, chans)
    out_gate = (out_raw.astype(F32) * scale_g).astype(BF16)
    in_pair, fg_pair, gate_raw_pair, out_pair, mixed_half, d_bounds = mixer_backward(
        lengths, d_state, in_raw, fg_raw, before, lower_table, d_gate_raw, out_gate, d_mixed_all, 4
    )
    mixer_part = jnp.concatenate(
        [
            over_pairs(mixed_half, out_pair),
            over_pairs(normed_half, in_pair),
            over_pairs(normed_half, fg_pair),
            over_pairs(normed_half, gate_raw_pair),
        ],
        1,
    )
    mixer_ready, in_pair, fg_pair, d_gate_raw = lax.optimization_barrier(
        (mixer_part, in_pair, fg_pair, d_gate_raw)
    )
    d_normed_part = mm_t(in_pair[0], w_input) + mm_t(fg_pair[0], w_forget)
    d_normed_part = (d_normed_part + mm_t(d_gate_raw, w_gate_out)).astype(BF16)
    d_normed = slot_reduce(d_normed_part, 5)
    mixer_ready, pair_grad, d_normed = lax.optimization_barrier((mixer_ready, pair_grad, d_normed))
    mixer_grad = sum_over_z(mixer_ready).astype(F32)

    scale_one = lax.rsqrt(jnp.mean(hidden_f * hidden_f, -1, keepdims=True) + epsilon)
    scaled_one = norm_gain * d_normed
    d_hidden = (
        d_middle
        + scale_one * scaled_one
        - hidden_f * scale_one**3 * jnp.mean(scaled_one * hidden_f, -1, keepdims=True)
    )
    d_norm_gain = jnp.sum(d_normed * hidden_f * scale_one, 0)
    d_gain_full = lax.dynamic_update_slice(
        jnp.zeros((width,), F32), d_gain_slice, (fsdp_index * chans,)
    )
    d_bounds_full = lax.dynamic_update_slice(
        jnp.zeros((width,), F32), d_bounds[0], (fsdp_index * chans,)
    )
    sums = jnp.stack([d_norm_gain, d_glu_gain, d_gain_full, d_bounds_full])
    totals = sum_all(sums.reshape(8, width // 2), 6).reshape(4, width)
    _, bounds_pull = jax.vjp(lower_bound, lower_table)
    d_table = bounds_pull(totals[3])[0]

    act, _ = lax.optimization_barrier((act_pair[0], d_normed))
    glu_part = mm(act, w_glu_down).astype(BF16)
    output = (middle + slot_reduce(glu_part, 7)).astype(BF16)
    pair_grad, down_grad = pair_grad.astype(F32), down_grad.astype(F32)
    return (
        output[None],
        d_hidden.astype(BF16)[None],
        mixer_grad[:, chans : 2 * chans],
        mixer_grad[:, 2 * chans : 3 * chans],
        mixer_grad[:, 3 * chans :],
        mixer_grad[:, :chans].T,
        totals[0],
        totals[2],
        totals[1],
        d_table,
        pair_grad[:, :units],
        pair_grad[:, units:],
        down_grad.T,
    )


def fits_plane(mesh):
    return mesh.shape["fsdp"] == 4 and mesh.shape["seq"] % 2 == 0


def solution(mesh):
    rows_spec = P("fsdp", "seq", None)
    columns = P(None, "fsdp")
    placed = (
        rows_spec,
        P(),
        columns,
        columns,
        columns,
        P("fsdp", None),
        P(),
        P(),
        P(),
        P(),
        columns,
        columns,
        P("fsdp", None),
        rows_spec,
    )
    by_rows, by_columns = P("seq", "fsdp"), P("fsdp", "seq")
    return jax.shard_map(
        plane_device if fits_plane(mesh) else per_device,
        mesh=mesh,
        in_specs=placed,
        out_specs=(
            rows_spec,
            rows_spec,
            by_rows,
            by_rows,
            by_rows,
            by_columns,
            P(),
            P(),
            P(),
            P(),
            by_rows,
            by_rows,
            by_columns,
        ),
        check_vma=False,
    )
```

```python
import functools

import jax
import jax.numpy as jnp
from jax import lax
from jax.experimental import pallas as pl
from jax.experimental.pallas import tpu as pltpu
from jax.sharding import PartitionSpec as P

LAYER = 12
MESH = pl.DeviceIdType.MESH
F32 = jnp.float32
BF16 = jnp.bfloat16

epsilon = 1e-06

VMEM = pl.BlockSpec(memory_space=pltpu.VMEM)
ANY = pl.BlockSpec(memory_space=pl.ANY)


def lower_bound(table):
    soft = jax.nn.softmax(table, axis=0)
    totals = jnp.cumsum(soft, axis=0)
    return totals[LAYER] - totals[0]


def silu_slope(value, sigma):
    return sigma * (1.0 + value * (1.0 - sigma))


def params(collective_id):
    return pltpu.CompilerParams(
        collective_id=collective_id, has_side_effects=True, vmem_limit_bytes=56 << 20
    )


def round_up(value, unit):
    return -(-value // unit) * unit


def plane():
    s = lax.axis_index("seq")
    f = lax.axis_index("fsdp")
    y, x = f // 2, f % 2
    fx = y * 2 + (1 - x)
    fy = (1 - y) * 2 + x
    fd = (1 - y) * 2 + (1 - x)
    return s, f, fx, fy, fd


def enter(devices):
    barrier = pltpu.get_barrier_semaphore()
    for device in devices:
        pl.semaphore_signal(barrier, inc=1, device_id=device, device_id_type=MESH)
    pl.semaphore_wait(barrier, len(devices))


def remote(src, dst, send, recv, device):
    return pltpu.make_async_remote_copy(
        src_ref=src,
        dst_ref=dst,
        send_sem=send,
        recv_sem=recv,
        device_id=device,
        device_id_type=MESH,
    )


def gather(x, small, collective_id):
    return lax.all_gather(x, "fsdp"), lax.all_gather(small, "fsdp")


def reduce_rows(p, small, collective_id):
    total = lax.psum_scatter(p, "fsdp", scatter_dimension=0, tiled=True)[0]
    return total.astype(F32), lax.psum(small, "fsdp")


def start_exchange(total, gathered, send, recv, n_seq):
    s = lax.axis_index("seq")
    f = lax.axis_index("fsdp")
    copies = []
    for k in range(1, n_seq):
        peer = lax.rem(s + k, n_seq)
        copy = remote(total, gathered.at[s], send.at[k], recv.at[k], (peer, f))
        copy.start()
        copies.append(copy)
    gathered[pl.ds(s, 1)] = total[...][None]
    return copies


def seq_peers(n_seq):
    s = lax.axis_index("seq")
    f = lax.axis_index("fsdp")
    return [(lax.rem(s + k, n_seq), f) for k in range(1, n_seq)]


def lane_blocks(groups, chans):
    return [(g, slice(c, c + 128)) for g in range(groups) for c in range(0, chans, 128)]


def forward_scan_kernel(
    n_seq, in_raw, forget_raw, bounds, keep, state_b, before, a_ref, b_ref, total, gathered, send, recv
):
    groups, rows, chans = in_raw.shape
    part = rows // 8
    blocks = lane_blocks(groups, chans)
    s = lax.axis_index("seq")
    barrier = pltpu.get_barrier_semaphore()
    for peer in seq_peers(n_seq):
        pl.semaphore_signal(barrier, inc=1, device_id=peer, device_id_type=MESH)
    for n, (g, lanes) in enumerate(blocks):
        bound = bounds[:, lanes]
        forget = bound + (1.0 - bound) * jax.nn.sigmoid(forget_raw[g, :, lanes].astype(F32))
        value = in_raw[g, :, lanes].astype(F32)
        a_ref[n] = forget * keep[g]
        b_ref[n] = value * jax.nn.sigmoid(value) * (1.0 - forget)

    def step(i, carry):
        new = []
        at = pl.ds(i, 8, stride=part)
        for n, (product, state) in enumerate(carry):
            a = a_ref[n, at, :]
            state = a * state + b_ref[n, at, :]
            product = product * a
            a_ref[n, at, :] = product
            b_ref[n, at, :] = state
            new.append((product, state))
        return tuple(new)

    start = tuple((jnp.ones((8, 128), F32), jnp.zeros((8, 128), F32)) for _ in blocks)
    ends = lax.fori_loop(0, part, step, start)
    for n, (product, state) in enumerate(ends):
        p_all, s_all = product[0:1], state[0:1]
        for j in range(1, 8):
            p_all, s_all = p_all * product[j : j + 1], state[j : j + 1] + product[j : j + 1] * s_all
        total[2 * n : 2 * n + 1] = p_all
        total[2 * n + 1 : 2 * n + 2] = s_all
    pl.semaphore_wait(barrier, n_seq - 1)
    copies = start_exchange(total, gathered, send, recv, n_seq)
    for copy in copies:
        copy.wait()
    for n, (g, lanes) in enumerate(blocks):
        carry = jnp.zeros((1, 128), F32)
        for j in range(n_seq - 1):
            p_j = gathered[j, 2 * n : 2 * n + 1]
            s_j = gathered[j, 2 * n + 1 : 2 * n + 2]
            carry = jnp.where(j < s, s_j + p_j * carry, carry)
        before[g, 0:1, lanes] = carry
        product, state = ends[n]
        carries = [carry]
        for j in range(7):
            carries.append(state[j : j + 1] + product[j : j + 1] * carries[-1])
        for j in range(8):
            at = slice(j * part, (j + 1) * part)
            b_ref[n, at] = b_ref[n, at] + a_ref[n, at] * carries[j]
        state_b[g, :, lanes] = b_ref[n].astype(BF16)
        before[g, 1:rows, lanes] = b_ref[n, 0 : rows - 1]


def forward_scan(in_raw, forget_raw, bounds, keep, collective_id):
    n_seq = lax.axis_size("seq")
    groups, rows, chans = in_raw.shape
    blocks = groups * chans // 128
    return pl.pallas_call(
        functools.partial(forward_scan_kernel, n_seq),
        out_shape=(
            jax.ShapeDtypeStruct(in_raw.shape, BF16),
            jax.ShapeDtypeStruct(in_raw.shape, F32),
        ),
        in_specs=[VMEM] * 4,
        out_specs=(VMEM, VMEM),
        scratch_shapes=[
            pltpu.VMEM((blocks, rows, 128), F32),
            pltpu.VMEM((blocks, rows, 128), F32),
            pltpu.VMEM((2 * blocks, 128), F32),
            pltpu.VMEM((n_seq, 2 * blocks, 128), F32),
            pltpu.SemaphoreType.DMA((n_seq,)),
            pltpu.SemaphoreType.DMA((n_seq,)),
        ],
        compiler_params=params(collective_id),
        name="forward_scan",
    )(in_raw, forget_raw, bounds, keep)


def backward_scan_kernel(
    n_seq,
    d_state,
    in_raw,
    forget_raw,
    before,
    bounds,
    keep,
    d_in,
    d_forget_raw,
    d_bounds,
    p_ref,
    q_ref,
    total,
    gathered,
    send,
    recv,
):
    groups, rows, chans = in_raw.shape
    part = rows // 8
    blocks = lane_blocks(groups, chans)
    s = lax.axis_index("seq")
    barrier = pltpu.get_barrier_semaphore()
    for peer in seq_peers(n_seq):
        pl.semaphore_signal(barrier, inc=1, device_id=peer, device_id_type=MESH)
    for n, (g, lanes) in enumerate(blocks):
        bound = bounds[:, lanes]
        forget = bound + (1.0 - bound) * jax.nn.sigmoid(forget_raw[g, :, lanes].astype(F32))
        p_ref[n] = forget * keep[g]
        q_ref[n] = d_state[g, :, lanes].astype(F32)

    def step(i, carry):
        new = []
        at = pl.ds(part - 1 - i, 8, stride=part)
        for n, (product, message) in enumerate(carry):
            a = p_ref[n, at, :]
            acc = q_ref[n, at, :] + message
            p_ref[n, at, :] = product
            q_ref[n, at, :] = acc
            new.append((product * a, a * acc))
        return tuple(new)

    start = tuple((jnp.ones((8, 128), F32), jnp.zeros((8, 128), F32)) for _ in blocks)
    ends = lax.fori_loop(0, part, step, start)
    for n, (product, message) in enumerate(ends):
        p_all, m_all = product[7:8], message[7:8]
        for j in range(6, -1, -1):
            p_all, m_all = p_all * product[j : j + 1], message[j : j + 1] + product[j : j + 1] * m_all
        total[2 * n : 2 * n + 1] = p_all
        total[2 * n + 1 : 2 * n + 2] = m_all
    pl.semaphore_wait(barrier, n_seq - 1)
    copies = start_exchange(total, gathered, send, recv, n_seq)
    for copy in copies:
        copy.wait()
    d_bounds[...] = jnp.zeros((1, chans), F32)
    for n, (g, lanes) in enumerate(blocks):
        carry = jnp.zeros((1, 128), F32)
        for j in range(n_seq - 1, 0, -1):
            p_j = gathered[j, 2 * n : 2 * n + 1]
            m_j = gathered[j, 2 * n + 1 : 2 * n + 2]
            carry = jnp.where(j > s, m_j + p_j * carry, carry)
        product, message = ends[n]
        carries = [carry]
        for j in range(7, 0, -1):
            carries.append(message[j : j + 1] + product[j : j + 1] * carries[-1])
        carries = carries[::-1]
        for j in range(8):
            at = slice(j * part, (j + 1) * part)
            q_ref[n, at] = q_ref[n, at] + p_ref[n, at] * carries[j]
        acc = q_ref[n]
        bound = bounds[:, lanes]
        sigma_f = jax.nn.sigmoid(forget_raw[g, :, lanes].astype(F32))
        forget = bound + (1.0 - bound) * sigma_f
        value = in_raw[g, :, lanes].astype(F32)
        sigma_i = jax.nn.sigmoid(value)
        d_forget = acc * (before[g, :, lanes] * keep[g] - value * sigma_i)
        d_in[g, :, lanes] = (acc * (1.0 - forget) * silu_slope(value, sigma_i)).astype(BF16)
        d_sigma = d_forget * (1.0 - sigma_f)
        d_forget_raw[g, :, lanes] = (d_sigma * (1.0 - bound) * sigma_f).astype(BF16)
        d_bounds[:, lanes] += jnp.sum(d_sigma, 0, keepdims=True)


def backward_scan(d_state, in_raw, forget_raw, before, bounds, keep, collective_id):
    n_seq = lax.axis_size("seq")
    groups, rows, chans = in_raw.shape
    blocks = groups * chans // 128
    return pl.pallas_call(
        functools.partial(backward_scan_kernel, n_seq),
        out_shape=(
            jax.ShapeDtypeStruct(in_raw.shape, BF16),
            jax.ShapeDtypeStruct(in_raw.shape, BF16),
            jax.ShapeDtypeStruct((1, chans), F32),
        ),
        in_specs=[VMEM] * 6,
        out_specs=(VMEM, VMEM, VMEM),
        scratch_shapes=[
            pltpu.VMEM((blocks, rows, 128), F32),
            pltpu.VMEM((blocks, rows, 128), F32),
            pltpu.VMEM((2 * blocks, 128), F32),
            pltpu.VMEM((n_seq, 2 * blocks, 128), F32),
            pltpu.SemaphoreType.DMA((n_seq,)),
            pltpu.SemaphoreType.DMA((n_seq,)),
        ],
        compiler_params=params(collective_id),
        name="backward_scan",
    )(d_state, in_raw, forget_raw, before, bounds, keep)


def sum_all_kernel(n_seq, n_fsdp, x, out, middle, over_seq, over_fsdp, send, recv):
    s = lax.axis_index("seq")
    f = lax.axis_index("fsdp")
    along = [(lax.rem(s + k, n_seq), f) for k in range(1, n_seq)]
    across = [(s, lax.rem(f + k, n_fsdp)) for k in range(1, n_fsdp)]
    enter(along + across)
    copies = []
    for k, peer in enumerate(along):
        copy = remote(x, over_seq.at[k], send.at[k], recv.at[k], peer)
        copy.start()
        copies.append(copy)
    total = x[...]
    for k, copy in enumerate(copies):
        copy.wait_recv()
        total = total + over_seq[k]
    middle[...] = total
    later = []
    for k, peer in enumerate(across):
        slot = n_seq - 1 + k
        copy = remote(middle, over_fsdp.at[k], send.at[slot], recv.at[slot], peer)
        copy.start()
        later.append(copy)
    for k, copy in enumerate(later):
        copy.wait_recv()
        total = total + over_fsdp[k]
    out[...] = total
    for copy in copies + later:
        copy.wait_send()


def sum_all(x, collective_id):
    n_seq, n_fsdp = lax.axis_size("seq"), lax.axis_size("fsdp")
    count = n_seq + n_fsdp - 2
    return pl.pallas_call(
        functools.partial(sum_all_kernel, n_seq, n_fsdp),
        out_shape=jax.ShapeDtypeStruct(x.shape, F32),
        in_specs=[VMEM],
        out_specs=VMEM,
        scratch_shapes=[
            pltpu.VMEM(x.shape, F32),
            pltpu.VMEM((n_seq - 1,) + x.shape, F32),
            pltpu.VMEM((n_fsdp - 1,) + x.shape, F32),
            pltpu.SemaphoreType.DMA((count,)),
            pltpu.SemaphoreType.DMA((count,)),
        ],
        compiler_params=params(collective_id),
        name="sum_all",
    )(x)


def sum_over_seq(part):
    return lax.psum_scatter(part.astype(BF16), "seq", scatter_dimension=0, tiled=True).astype(F32)


def per_device(
    hidden,
    lengths,
    w_input,
    w_forget,
    w_gate_out,
    w_output,
    norm_gain,
    gate_gain,
    glu_gain,
    lower_table,
    w_glu_gate,
    w_glu_up,
    w_glu_down,
    cotangent,
):
    seq_index = lax.axis_index("seq")
    fsdp_index = lax.axis_index("fsdp")
    groups = lax.axis_size("fsdp")
    _, rows, width = hidden.shape
    chans = w_input.shape[1]
    units = w_glu_gate.shape[1]
    tokens = groups * rows
    small_shape = (round_up(groups, 8), round_up(rows, 128))

    def to_small(value):
        return jnp.pad(
            value, ((0, small_shape[0] - value.shape[0]), (0, small_shape[1] - value.shape[1]))
        )

    def dot(left, right):
        return jnp.dot(left, right, preferred_element_type=F32)

    def dot_t(left, right):
        return lax.dot_general(left, right, (((1,), (1,)), ((), ())), preferred_element_type=F32)

    def over_tokens(left, right):
        return lax.dot_general(left, right, (((0,), (0,)), ((), ())), preferred_element_type=F32)

    cotangent_all = lax.all_gather(cotangent[0], "fsdp").reshape(tokens, width)

    hidden_f = hidden[0].astype(F32)
    scale_one = lax.rsqrt(jnp.mean(hidden_f * hidden_f, -1, keepdims=True) + epsilon)
    normed = (hidden_f * scale_one * norm_gain).astype(BF16)
    normed_all, _ = gather(normed, jnp.zeros((8, 128), F32), 0)
    normed_all = normed_all.reshape(tokens, width)
    in_raw = dot(normed_all, w_input).astype(BF16).reshape(groups, rows, chans)
    forget_raw = dot(normed_all, w_forget).astype(BF16).reshape(groups, rows, chans)
    gate_raw = dot(normed_all, w_gate_out)

    bounds_full = lower_bound(lower_table)
    bounds = lax.dynamic_slice_in_dim(bounds_full, fsdp_index * chans, chans)[None]
    seq_starts = jnp.cumsum(lengths, axis=1) - lengths
    places = seq_index * rows + jnp.arange(rows, dtype=jnp.int32)
    starts = jnp.any(places[None, :, None] == seq_starts[:, None, :], axis=-1)
    keep = jnp.where(starts, 0.0, 1.0).astype(F32)[:, :, None]
    state_b, before = forward_scan(in_raw, forget_raw, bounds, keep, 1)

    state_f = state_b.astype(F32).reshape(tokens, chans)
    gain_slice = lax.dynamic_slice_in_dim(gate_gain, fsdp_index * chans, chans)
    sigma_g = jax.nn.sigmoid(gate_raw)
    silu_gate = gate_raw * sigma_g
    out_raw = (state_f * gain_slice * silu_gate).astype(BF16)
    squares = jnp.sum(state_f * state_f, -1).reshape(groups, rows)
    mixed_part = dot(out_raw, w_output).astype(BF16).reshape(groups, rows, width)
    mixed_raw, square_sum = reduce_rows(mixed_part, to_small(squares), 2)
    state_scale = lax.rsqrt(square_sum[:groups, :rows] / width + epsilon)
    own_scale = lax.dynamic_slice_in_dim(state_scale, fsdp_index, 1, 0)[0][:, None]
    scale_g = state_scale.reshape(tokens, 1)
    middle = hidden_f + own_scale * mixed_raw
    scale_two = lax.rsqrt(jnp.mean(middle * middle, -1, keepdims=True) + epsilon)
    normed_two = (middle * scale_two * glu_gain).astype(BF16)
    normed_two_all, _ = gather(normed_two, jnp.zeros((8, 128), F32), 3)
    normed_two_all = normed_two_all.reshape(tokens, width)

    gate_val = dot(normed_two_all, w_glu_gate)
    up_val = dot(normed_two_all, w_glu_up)
    sigma_u = jax.nn.sigmoid(gate_val)
    silu_u = gate_val * sigma_u
    activity = (silu_u * up_val).astype(BF16)
    down_grad = sum_over_seq(over_tokens(cotangent_all, activity))
    d_act = dot_t(cotangent_all, w_glu_down)
    d_gate = (d_act * up_val * silu_slope(gate_val, sigma_u)).astype(BF16)
    d_up = (d_act * silu_u).astype(BF16)
    pair_grad = sum_over_seq(
        jnp.concatenate(
            [
                over_tokens(normed_two_all, d_gate).astype(BF16),
                over_tokens(normed_two_all, d_up).astype(BF16),
            ],
            1,
        )
    )
    d_two_part = (dot_t(d_gate, w_glu_gate) + dot_t(d_up, w_glu_up)).astype(BF16)
    no_small = jnp.zeros((8, 128), F32)
    d_normed_two, _ = reduce_rows(d_two_part.reshape(groups, rows, width), no_small, 4)
    glu_part = dot(activity, w_glu_down).astype(BF16).reshape(groups, rows, width)
    glu_result = lax.psum_scatter(glu_part, "fsdp", scatter_dimension=0, tiled=True)[0]
    output = (middle + glu_result.astype(F32)).astype(BF16)[None]

    cotangent_f = cotangent[0].astype(F32)
    scaled_two = glu_gain * d_normed_two
    d_middle = (
        cotangent_f
        + scale_two * scaled_two
        - middle * scale_two**3 * jnp.mean(scaled_two * middle, -1, keepdims=True)
    )
    d_glu_gain = jnp.sum(d_normed_two * middle * scale_two, 0)
    d_mixed = d_middle.astype(BF16)
    own_dot = jnp.sum(d_mixed.astype(F32) * mixed_raw, -1)[None]
    d_mixed_all, dots = gather(d_mixed, to_small(own_dot), 5)
    d_mixed_all = d_mixed_all.reshape(tokens, width)
    dot_rows = dots[:, 0, :rows].reshape(tokens, 1)

    d_out = dot_t(d_mixed_all, w_output)
    scaled_state = state_f * scale_g
    d_gain_slice = jnp.sum(d_out * scaled_state * silu_gate, 0)
    d_scaled = d_out * gain_slice * silu_gate
    d_gate_raw = (d_out * scaled_state * gain_slice * silu_slope(gate_raw, sigma_g)).astype(BF16)
    d_state = scale_g * d_scaled - state_f * (scale_g**3 * (dot_rows / width))
    d_state = d_state.astype(BF16).reshape(groups, rows, chans)
    d_in, d_forget_raw, d_bounds = backward_scan(
        d_state, in_raw, forget_raw, before, bounds, keep, 6
    )
    d_in = d_in.reshape(tokens, chans)
    d_forget_raw = d_forget_raw.reshape(tokens, chans)

    d_normed_part = dot_t(d_in, w_input) + dot_t(d_forget_raw, w_forget)
    d_normed_part = (d_normed_part + dot_t(d_gate_raw, w_gate_out)).astype(BF16)
    out_gate = (out_raw.astype(F32) * scale_g).astype(BF16)
    mixer_grad = sum_over_seq(
        jnp.concatenate(
            [
                over_tokens(d_mixed_all, out_gate).astype(BF16),
                over_tokens(normed_all, d_in).astype(BF16),
                over_tokens(normed_all, d_forget_raw).astype(BF16),
                over_tokens(normed_all, d_gate_raw).astype(BF16),
            ],
            1,
        )
    )
    d_normed, _ = reduce_rows(d_normed_part.reshape(groups, rows, width), no_small, 7)
    scaled_one = norm_gain * d_normed
    d_hidden = (
        d_middle
        + scale_one * scaled_one
        - hidden_f * scale_one**3 * jnp.mean(scaled_one * hidden_f, -1, keepdims=True)
    )
    d_norm_gain = jnp.sum(d_normed * hidden_f * scale_one, 0)
    d_gain_full = lax.dynamic_update_slice(
        jnp.zeros((width,), F32), d_gain_slice, (fsdp_index * chans,)
    )
    d_bounds_full = lax.dynamic_update_slice(
        jnp.zeros((width,), F32), d_bounds[0], (fsdp_index * chans,)
    )
    sums = jnp.stack([d_norm_gain, d_glu_gain, d_gain_full, d_bounds_full])
    totals = sum_all(sums.reshape(8, width // 2), 8).reshape(4, width)
    _, bounds_pull = jax.vjp(lower_bound, lower_table)
    d_table = bounds_pull(totals[3])[0]
    return (
        output,
        d_hidden.astype(BF16)[None],
        mixer_grad[:, chans : 2 * chans],
        mixer_grad[:, 2 * chans : 3 * chans],
        mixer_grad[:, 3 * chans :],
        mixer_grad[:, :chans].T,
        totals[0],
        totals[2],
        totals[1],
        d_table,
        pair_grad[:, :units],
        pair_grad[:, units:],
        down_grad.T,
    )


def copy_in(src, dst, sem):
    copy = pltpu.make_async_copy(src, dst, sem)
    copy.start()
    return copy


class Links:
    def __init__(self, send, recv):
        self.send, self.recv, self.used = send, recv, 0

    def start(self, src, dst, device):
        copy = remote(src, dst, self.send.at[self.used], self.recv.at[self.used], device)
        self.used += 1
        copy.start()
        return copy


class Locals:
    def __init__(self, sems):
        self.sems, self.used = sems, 0

    def start(self, src, dst):
        copy = copy_in(src, dst, self.sems.at[self.used])
        self.used += 1
        return copy


def row_slots(rows):
    half = rows // 2
    top = [pl.ds(k * rows, half) for k in range(4)]
    bottom = [pl.ds(k * rows + half, half) for k in range(4)]
    return top, bottom


def gather_start(links, src, dst, rows, s, fx, fy):
    half = rows // 2
    top, bottom = row_slots(rows)
    here = (pl.ds(0, half), pl.ds(half, half))
    return [
        links.start(src.at[here[0]], dst.at[top[1]], (s, fx)),
        links.start(src.at[here[1]], dst.at[bottom[2]], (s, fy)),
        links.start(src.at[here[1]], dst.at[bottom[1]], (s, fx)),
        links.start(src.at[here[0]], dst.at[top[2]], (s, fy)),
    ]


def gather_forward(links, own, dst, rows, s, fx, fy):
    top, bottom = row_slots(rows)
    own[0].wait_recv()
    on_y = links.start(dst.at[top[1]], dst.at[top[3]], (s, fy))
    own[1].wait_recv()
    on_x = links.start(dst.at[bottom[2]], dst.at[bottom[3]], (s, fx))
    return [on_y, on_x]


def gather_middle(own):
    own[2].wait_recv()
    own[3].wait_recv()


def gather_far(later):
    for copy in later:
        copy.wait_recv()


def sends_done(*lists):
    for copies in lists:
        for copy in copies:
            copy.wait_send()


def wait_all(*lists):
    for copies in lists:
        for copy in copies:
            copy.wait()


def reduce_start_far(links, part, from_x, from_y, rows, s, fx, fy):
    top, bottom = row_slots(rows)
    return [
        links.start(part.at[top[3]], from_x.at[0], (s, fx)),
        links.start(part.at[bottom[3]], from_y.at[0], (s, fy)),
    ]


def reduce_start_near(links, part, from_x, from_y, rows, s, fx, fy):
    top, bottom = row_slots(rows)
    return [
        links.start(part.at[top[1]], from_x.at[1], (s, fx)),
        links.start(part.at[bottom[2]], from_y.at[1], (s, fy)),
    ]


def reduce_pass(links, far, part, from_x, from_y, pass_x, pass_y, rows, s, fx, fy):
    top, bottom = row_slots(rows)
    far[0].wait_recv()
    pass_y[...] = (from_x[0].astype(F32) + part[top[2]].astype(F32)).astype(BF16)
    on_y = links.start(pass_y, from_y.at[2], (s, fy))
    far[1].wait_recv()
    pass_x[...] = (from_y[0].astype(F32) + part[bottom[1]].astype(F32)).astype(BF16)
    on_x = links.start(pass_x, from_x.at[2], (s, fx))
    return [on_y, on_x]


def mm(left, right):
    return jnp.dot(left, right, preferred_element_type=F32)


def mm_t(left, right):
    return lax.dot_general(left, right, (((1,), (1,)), ((), ())), preferred_element_type=F32)


def tile(n, width):
    return pl.ds(pl.multiple_of(n * width, width), width)


def bounds_slice(table, first, count):
    rows = table[:, pl.ds(pl.multiple_of(first, 128), count)]
    powers = jnp.exp(rows - jnp.max(rows, 0, keepdims=True))
    return jnp.sum(powers[1 : LAYER + 1], 0, keepdims=True) / jnp.sum(powers, 0, keepdims=True)


def keep_rows(lengths, group, first, rows):
    places = first + lax.broadcasted_iota(jnp.int32, (rows, 128), 0)
    start = jnp.int32(0)
    keep = jnp.where(places == start, 0.0, 1.0)
    for i in range(lengths.shape[1] - 1):
        start = start + lengths[group, i]
        keep = jnp.where(places == start, 0.0, keep)
    return keep.astype(F32)


def segment_totals(end_p, end_s, blocks, order):
    first, rest = order[0], order[1:]
    p_all = end_p[pl.ds(first, blocks, stride=8), :]
    s_all = end_s[pl.ds(first, blocks, stride=8), :]
    for j in rest:
        p_j = end_p[pl.ds(j, blocks, stride=8), :]
        s_all = end_s[pl.ds(j, blocks, stride=8), :] + p_j * s_all
        p_all = p_all * p_j
    return p_all, s_all


def spread_carry(carry, carr, end_p, end_s, blocks, order):
    for i, j in enumerate(order):
        carr[pl.ds(j, blocks, stride=8), :] = carry
        if i < 7:
            carry = end_s[pl.ds(j, blocks, stride=8), :] + end_p[pl.ds(j, blocks, stride=8), :] * carry


def mixer_kernel(
    n_seq,
    lengths,
    hidden,
    cot,
    norm_gain,
    gate_gain,
    glu_gain,
    table,
    w_in,
    w_fg,
    w_gt,
    w_out,
    normed_half,
    cot_out,
    in_out,
    fg_out,
    gate_out,
    state_out,
    raw_out,
    before_out,
    scale_out,
    middle,
    two,
    wv,
    wo,
    rows_all,
    stage,
    in_ref,
    fg_ref,
    gate_ref,
    a_ref,
    b_ref,
    shifted,
    keep_ref,
    end_p,
    end_s,
    carr,
    total,
    gathered,
    state_ref,
    raw_ref,
    squares,
    squares_in,
    part,
    from_x,
    from_y,
    pass_x,
    pass_y,
    send,
    recv,
    exchange_send,
    exchange_recv,
    local_sems,
):
    rows, width = hidden.shape
    chans = w_in.shape[1]
    lanes_of = [slice(c, c + 128) for c in range(0, chans, 128)]
    count = len(lanes_of)
    blocks = 4 * count
    step_len = rows // 8
    s, f, fx, fy, fd = plane()
    groups = [f, fx, fy, fd]
    links, local = Links(send, recv), Locals(local_sems)

    weights = [
        local.start(w, wv.at[:, pl.ds(i * chans, chans)]) for i, w in enumerate((w_in, w_fg, w_gt))
    ]
    weights.append(local.start(w_out, wo))
    barrier = pltpu.get_barrier_semaphore()
    peers = [(s, fx), (s, fy), (s, fd)] + seq_peers(n_seq)
    for peer in peers:
        pl.semaphore_signal(barrier, inc=1, device_id=peer, device_id_type=MESH)

    def norm_rows(i, _):
        at = pl.ds(pl.multiple_of(i * 16, 16), 16)
        value = hidden[at].astype(F32)
        scale = lax.rsqrt(jnp.mean(value * value, -1, keepdims=True) + epsilon)
        rows_all[at] = (value * scale * norm_gain[...]).astype(BF16)
        return 0

    lax.fori_loop(0, rows // 16, norm_rows, 0)
    pl.semaphore_wait(barrier, len(peers))
    own = gather_start(links, rows_all, rows_all, rows, s, fx, fy)
    bound = bounds_slice(table, f * chans, chans)
    for k in range(4):
        keep_ref[k] = keep_rows(lengths, groups[k], s * rows, rows)
    squares[...] = jnp.zeros_like(squares)
    for copy in weights[:3]:
        copy.wait()

    def project(first, slots):
        def tile_of(n, _):
            cols = tile(n, 256)
            stage[: slots * rows, cols] = mm(
                rows_all[first * rows : (first + slots) * rows], wv[:, cols]
            )
            return 0

        lax.fori_loop(0, 3 * chans // 256, tile_of, 0)
        for k in range(slots):
            at = slice(k * rows, (k + 1) * rows)
            for c, lanes in enumerate(lanes_of):
                n = (first + k) * count + c
                value = stage[at, lanes].astype(BF16)
                in_ref[first + k, :, lanes] = value
                value = value.astype(F32)
                raw = stage[at, chans + c * 128 : chans + (c + 1) * 128].astype(BF16)
                fg_ref[first + k, :, lanes] = raw
                edge = bound[:, lanes]
                forget = edge + (1.0 - edge) * jax.nn.sigmoid(raw.astype(F32))
                a_ref[n] = forget * keep_ref[first + k]
                b_ref[n] = value * jax.nn.sigmoid(value) * (1.0 - forget)
            gate_ref[first + k] = stage[at, 2 * chans :]

    project(0, 1)
    later = gather_forward(links, own, rows_all, rows, s, fx, fy)
    gather_middle(own)
    project(1, 2)
    gather_far(later)
    cot_own = gather_start(links, cot, cot_out, rows, s, fx, fy)
    core = s % 2
    swaps, outs = swap_columns(
        links, local, rows_all, normed_half, n_seq, core, (s + 1 - 2 * core, f)
    )
    outs.append(local.start(cot, cot_out.at[pl.ds(0, rows)]))
    project(3, 1)
    outs += [
        local.start(in_ref, in_out),
        local.start(fg_ref, fg_out),
        local.start(gate_ref, gate_out),
    ]

    def scan_step(i, carry):
        new = []
        at = pl.ds(i, 8, stride=step_len)
        for n, (product, state) in enumerate(carry):
            a = a_ref[n, at, :]
            state = a * state + b_ref[n, at, :]
            product = product * a
            a_ref[n, at, :] = product
            b_ref[n, at, :] = state
            new.append((product, state))
        return tuple(new)

    start = tuple((jnp.ones((8, 128), F32), jnp.zeros((8, 128), F32)) for _ in range(blocks))
    ends = lax.fori_loop(0, step_len, scan_step, start)
    for n, (product, state) in enumerate(ends):
        end_p[8 * n : 8 * n + 8] = product
        end_s[8 * n : 8 * n + 8] = state
    p_all, s_all = segment_totals(end_p, end_s, blocks, range(8))
    total[:blocks] = p_all
    total[blocks:] = s_all
    copies = start_exchange(total, gathered, exchange_send, exchange_recv, n_seq)
    wait_all(copies)
    carry = jnp.zeros((blocks, 128), F32)
    for j in range(n_seq - 1):
        carry = jnp.where(j < s, gathered[j, blocks:] + gathered[j, :blocks] * carry, carry)
    for n in range(blocks):
        shifted[n, 0:1] = carry[n : n + 1]
    spread_carry(carry, carr, end_p, end_s, blocks, range(8))

    def finish(n, _):
        enter_state = carr[pl.ds(pl.multiple_of(n * 8, 8), 8)]
        for i in range(step_len):
            at = pl.ds(i, 8, stride=step_len)
            state = b_ref[n, at, :] + a_ref[n, at, :] * enter_state
            b_ref[n, at, :] = state
            shifted[n, pl.ds(i + 1, 8, stride=step_len), :] = state
        return 0

    lax.fori_loop(0, blocks, finish, 0)
    outs.append(local.start(shifted.at[:, pl.ds(0, rows)], before_out))

    lane = lax.broadcasted_iota(jnp.int32, (rows, 128), 1)
    for k in (3, 1, 2, 0):
        square = jnp.zeros((rows, 1), F32)
        for c, lanes in enumerate(lanes_of):
            state_b = b_ref[k * count + c].astype(BF16)
            state_ref[k, :, lanes] = state_b
            state = state_b.astype(F32)
            square = square + jnp.sum(state * state, -1, keepdims=True)
            gate = gate_ref[k, :, lanes]
            gain = gate_gain[:, pl.ds(pl.multiple_of(f * chans + c * 128, 128), 128)]
            raw_ref[k * rows : (k + 1) * rows, lanes] = (
                state * gain * gate * jax.nn.sigmoid(gate)
            ).astype(BF16)
        squares[...] = jnp.where(lane == groups[k], square, squares[...])
    square_copies = [
        links.start(squares, squares_in.at[i], (s, peer)) for i, peer in enumerate((fx, fy, fd))
    ]
    outs += [local.start(state_ref, state_out), local.start(raw_ref, raw_out)]
    cot_later = gather_forward(links, cot_own, cot_out, rows, s, fx, fy)
    weights[3].wait()

    def output_part(first, slots):
        at = slice(first * rows, (first + slots) * rows)

        def tile_of(n, _):
            cols = tile(n, 512)
            part[at, cols] = mm(raw_ref[at], wo[:, cols]).astype(BF16)
            return 0

        lax.fori_loop(0, width // 512, tile_of, 0)

    output_part(3, 1)
    far = reduce_start_far(links, part, from_x, from_y, rows, s, fx, fy)
    output_part(1, 2)
    near = reduce_start_near(links, part, from_x, from_y, rows, s, fx, fy)
    output_part(0, 1)
    passed = reduce_pass(links, far, part, from_x, from_y, pass_x, pass_y, rows, s, fx, fy)
    for copy in square_copies:
        copy.wait_recv()
    all_squares = (squares[...] + squares_in[0]) + (squares_in[1] + squares_in[2])
    scales = lax.rsqrt(all_squares / width + epsilon)
    for k in range(4):
        scale_out[k] = jnp.sum(jnp.where(lane == groups[k], scales, 0.0), -1, keepdims=True)
    for copy in near + passed:
        copy.wait_recv()
    half = rows // 2
    for first, one, other in ((0, from_x.at[1], from_y.at[2]), (half, from_y.at[1], from_x.at[2])):

        def sum_rows(i, _):
            here = pl.ds(pl.multiple_of(i * 16, 16), 16)
            at = pl.ds(pl.multiple_of(first + i * 16, 16), 16)
            mixed = part[at].astype(F32) + one[here].astype(F32) + other[here].astype(F32)
            value = hidden[at].astype(F32) + scale_out[0, at] * mixed
            middle[at] = value
            scale = lax.rsqrt(jnp.mean(value * value, -1, keepdims=True) + epsilon)
            two[at] = (value * scale * glu_gain[...]).astype(BF16)
            return 0

        lax.fori_loop(0, half // 16, sum_rows, 0)
    gather_middle(cot_own)
    gather_far(cot_later)
    sends_done(own, later, cot_own, cot_later, square_copies, far, near, passed)
    wait_all(swaps, outs)


def mixer_forward(lengths, hidden, cot, gains, table, weights, collective_id):
    n_seq = lax.axis_size("seq")
    rows, width = hidden.shape
    chans = weights[0].shape[1]
    blocks = 4 * chans // 128
    tokens = 4 * rows
    half = rows // 2
    shape = jax.ShapeDtypeStruct
    wide = shape((tokens, width), BF16)
    narrow = shape((4, rows, chans), BF16)
    return pl.pallas_call(
        functools.partial(mixer_kernel, n_seq),
        out_shape=(
            shape((2, tokens, width // 2), BF16),
            wide,
            narrow,
            narrow,
            shape((4, rows, chans), F32),
            narrow,
            shape((tokens, chans), BF16),
            shape((blocks, rows, 128), F32),
            shape((4, rows, 1), F32),
            shape((rows, width), F32),
            shape((rows, width), BF16),
        ),
        in_specs=[pl.BlockSpec(memory_space=pltpu.SMEM), VMEM, VMEM, VMEM, VMEM, VMEM, VMEM]
        + [ANY] * 4,
        out_specs=(ANY,) * 8 + (VMEM,) * 3,
        scratch_shapes=[
            pltpu.VMEM((width, 3 * chans), BF16),
            pltpu.VMEM((chans, width), BF16),
            pltpu.VMEM((tokens, width), BF16),
            pltpu.VMEM((2 * rows, 3 * chans), F32),
            pltpu.VMEM((4, rows, chans), BF16),
            pltpu.VMEM((4, rows, chans), BF16),
            pltpu.VMEM((4, rows, chans), F32),
            pltpu.VMEM((blocks, rows, 128), F32),
            pltpu.VMEM((blocks, rows, 128), F32),
            pltpu.VMEM((blocks, rows + 8, 128), F32),
            pltpu.VMEM((4, rows, 128), F32),
            pltpu.VMEM((8 * blocks, 128), F32),
            pltpu.VMEM((8 * blocks, 128), F32),
            pltpu.VMEM((8 * blocks, 128), F32),
            pltpu.VMEM((2 * blocks, 128), F32),
            pltpu.VMEM((n_seq, 2 * blocks, 128), F32),
            pltpu.VMEM((4, rows, chans), BF16),
            pltpu.VMEM((tokens, chans), BF16),
            pltpu.VMEM((rows, 128), F32),
            pltpu.VMEM((3, rows, 128), F32),
            pltpu.VMEM((tokens, width), BF16),
            pltpu.VMEM((3, half, width), BF16),
            pltpu.VMEM((3, half, width), BF16),
            pltpu.VMEM((half, width), BF16),
            pltpu.VMEM((half, width), BF16),
            pltpu.SemaphoreType.DMA((21 + n_seq // 2,)),
            pltpu.SemaphoreType.DMA((21 + n_seq // 2,)),
            pltpu.SemaphoreType.DMA((n_seq,)),
            pltpu.SemaphoreType.DMA((n_seq,)),
            pltpu.SemaphoreType.DMA((11 + n_seq // 2,)),
        ],
        compiler_params=params(collective_id),
        name="mixer_forward",
    )(lengths, hidden, cot, *gains, table, *weights)


def swap_columns(links, local, src, dst, n_seq, core, mate):
    part = src.shape[1] // n_seq
    copies, stays = [], []
    for z in range(n_seq // 2):
        to = pl.ds(z * part, part)
        theirs = pl.ds(pl.multiple_of((2 * z + 1 - core) * part, part), part)
        ours = pl.ds(pl.multiple_of((2 * z + core) * part, part), part)
        copies.append(links.start(src.at[:, theirs], dst.at[1, :, to], mate))
        stays.append(local.start(src.at[:, ours], dst.at[0, :, to]))
    return copies, stays


def swap_rows(links, local, src, dst, at, mate):
    copy = links.start(src.at[at], dst.at[1, at], mate)
    return copy, local.start(src.at[at], dst.at[0, at])


def glu_kernel(
    n_seq,
    two,
    cot_all,
    w_gate,
    w_up,
    w_down,
    two_half,
    cot_half,
    act_pair,
    gate_pair,
    up_pair,
    wv,
    wd,
    cot_ref,
    two_ref,
    d_act,
    stage,
    act,
    d_gate,
    d_up,
    send,
    recv,
    local_sems,
):
    rows = two.shape[0]
    units = w_gate.shape[1]
    s, f, fx, fy, fd = plane()
    core = s % 2
    mate = (s + 1 - 2 * core, f)
    links, local = Links(send, recv), Locals(local_sems)
    loads = [
        local.start(w_down, wd),
        local.start(cot_all, cot_ref),
        local.start(w_gate, wv.at[:, pl.ds(0, units)]),
        local.start(w_up, wv.at[:, pl.ds(units, units)]),
    ]
    two_ref[:rows] = two[...]
    enter([(s, fx), (s, fy), mate])
    own = gather_start(links, two_ref, two_ref, rows, s, fx, fy)
    loads[0].wait()
    loads[1].wait()
    swaps, stays = swap_columns(links, local, cot_ref, cot_half, n_seq, core, mate)

    def act_tile(n, _):
        cols = tile(n, 256)
        d_act[:, cols] = mm_t(cot_ref[...], wd[cols])
        return 0

    lax.fori_loop(0, units // 256, act_tile, 0)
    if units % 256:
        rest = slice(units // 256 * 256, units)
        d_act[:, rest] = mm_t(cot_ref[...], wd[rest])
    later = gather_forward(links, own, two_ref, rows, s, fx, fy)
    loads[2].wait()
    loads[3].wait()

    def slots(first, number):
        nonlocal swaps, stays
        base = first * rows

        def tile_of(n, _):
            cols = tile(n, 256)
            stage[: number * rows, cols] = mm(two_ref[base : base + number * rows], wv[:, cols])
            return 0

        lax.fori_loop(0, 2 * units // 256, tile_of, 0)

        def rows_of(i, _):
            at = pl.ds(pl.multiple_of(i * 16, 16), 16)
            to = pl.ds(pl.multiple_of(base + i * 16, 16), 16)
            gate, up = stage[at, :units], stage[at, units:]
            sigma = jax.nn.sigmoid(gate)
            silu = gate * sigma
            act[to] = (silu * up).astype(BF16)
            d = d_act[to]
            d_gate[to] = (d * up * silu_slope(gate, sigma)).astype(BF16)
            d_up[to] = (d * silu).astype(BF16)
            return 0

        lax.fori_loop(0, number * rows // 16, rows_of, 0)
        at = pl.ds(base, number * rows)
        for src, dst in ((act, act_pair), (d_gate, gate_pair), (d_up, up_pair)):
            sent, stayed = swap_rows(links, local, src, dst, at, mate)
            swaps, stays = swaps + [sent], stays + [stayed]

    slots(0, 1)
    gather_middle(own)
    slots(1, 2)
    gather_far(later)
    more, keeps = swap_columns(links, local, two_ref, two_half, n_seq, core, mate)
    slots(3, 1)
    sends_done(own, later)
    wait_all(swaps, stays, more, keeps)


def glu(two, cot_all, w_gate, w_up, w_down, collective_id):
    n_seq = lax.axis_size("seq")
    rows, width = two.shape
    units = w_gate.shape[1]
    tokens = 4 * rows
    shape = jax.ShapeDtypeStruct
    half = shape((2, tokens, width // 2), BF16)
    pair = shape((2, tokens, units), BF16)
    remote_count = 6 + n_seq + 9
    return pl.pallas_call(
        functools.partial(glu_kernel, n_seq),
        out_shape=(half, half, pair, pair, pair),
        in_specs=[VMEM] + [ANY] * 4,
        out_specs=(ANY,) * 5,
        scratch_shapes=[
            pltpu.VMEM((width, 2 * units), BF16),
            pltpu.VMEM((units, width), BF16),
            pltpu.VMEM((tokens, width), BF16),
            pltpu.VMEM((tokens, width), BF16),
            pltpu.VMEM((tokens, units), F32),
            pltpu.VMEM((2 * rows, 2 * units), F32),
            pltpu.VMEM((tokens, units), BF16),
            pltpu.VMEM((tokens, units), BF16),
            pltpu.VMEM((tokens, units), BF16),
            pltpu.SemaphoreType.DMA((remote_count,)),
            pltpu.SemaphoreType.DMA((remote_count,)),
            pltpu.SemaphoreType.DMA((4 + n_seq + 9,)),
        ],
        compiler_params=params(collective_id),
        name="glu",
    )(two, cot_all, w_gate, w_up, w_down)


def slot_gather_kernel(x, small, out, out_small, send, recv, local_sems):
    s, f, fx, fy, fd = plane()
    rows = x.shape[0]
    links, local = Links(send, recv), Locals(local_sems)
    enter([(s, fx), (s, fy), (s, fd)])
    own = gather_start(links, x, out, rows, s, fx, fy)
    smalls = [
        links.start(small, out_small.at[k], (s, peer))
        for k, peer in ((1, fx), (2, fy), (3, fd))
    ]
    stay = local.start(x, out.at[pl.ds(0, rows)])
    out_small[0] = small[...]
    later = gather_forward(links, own, out, rows, s, fx, fy)
    gather_middle(own)
    gather_far(later)
    sends_done(own, later)
    wait_all(smalls, [stay])


def slot_gather(x, small, collective_id):
    rows, width = x.shape
    return pl.pallas_call(
        slot_gather_kernel,
        out_shape=(
            jax.ShapeDtypeStruct((4 * rows, width), BF16),
            jax.ShapeDtypeStruct((4,) + small.shape, F32),
        ),
        in_specs=[VMEM, VMEM],
        out_specs=(ANY, VMEM),
        scratch_shapes=[
            pltpu.SemaphoreType.DMA((9,)),
            pltpu.SemaphoreType.DMA((9,)),
            pltpu.SemaphoreType.DMA((1,)),
        ],
        compiler_params=params(collective_id),
        name="slot_gather",
    )(x, small)


def slot_reduce_kernel(part, out, from_x, from_y, pass_x, pass_y, send, recv):
    s, f, fx, fy, fd = plane()
    rows = out.shape[0]
    half = rows // 2
    links = Links(send, recv)
    enter([(s, fx), (s, fy)])
    far = reduce_start_far(links, part, from_x, from_y, rows, s, fx, fy)
    near = reduce_start_near(links, part, from_x, from_y, rows, s, fx, fy)
    passed = reduce_pass(links, far, part, from_x, from_y, pass_x, pass_y, rows, s, fx, fy)
    for copy in near + passed:
        copy.wait_recv()
    out[:half] = part[:half].astype(F32) + from_x[1].astype(F32) + from_y[2].astype(F32)
    out[half:] = part[half:rows].astype(F32) + from_y[1].astype(F32) + from_x[2].astype(F32)
    sends_done(far, near, passed)


def slot_reduce(part, collective_id):
    tokens, width = part.shape
    rows = tokens // 4
    half = (rows // 2, width)
    return pl.pallas_call(
        slot_reduce_kernel,
        out_shape=jax.ShapeDtypeStruct((rows, width), F32),
        in_specs=[VMEM],
        out_specs=VMEM,
        scratch_shapes=[
            pltpu.VMEM((3,) + half, BF16),
            pltpu.VMEM((3,) + half, BF16),
            pltpu.VMEM(half, BF16),
            pltpu.VMEM(half, BF16),
            pltpu.SemaphoreType.DMA((6,)),
            pltpu.SemaphoreType.DMA((6,)),
        ],
        compiler_params=params(collective_id),
        name="slot_reduce",
    )(part)


def mixer_backward_kernel(
    n_seq,
    lengths,
    d_state,
    in_raw,
    fg_raw,
    before,
    table,
    d_gate_raw,
    out_gate,
    d_mixed_all,
    in_pair,
    fg_pair,
    gate_pair,
    out_pair,
    mixed_half,
    d_bounds,
    p_ref,
    q_ref,
    end_p,
    end_s,
    carr,
    total,
    gathered,
    keep_ref,
    d_in,
    d_fg,
    send,
    recv,
    exchange_send,
    exchange_recv,
    local_sems,
):
    _, rows, chans = in_raw.shape
    lanes_of = [slice(c, c + 128) for c in range(0, chans, 128)]
    count = len(lanes_of)
    blocks = 4 * count
    step_len = rows // 8
    s, f, fx, fy, fd = plane()
    groups = [f, fx, fy, fd]
    core = s % 2
    mate = (s + 1 - 2 * core, f)
    links, local = Links(send, recv), Locals(local_sems)
    barrier = pltpu.get_barrier_semaphore()
    peers = seq_peers(n_seq)
    for peer in peers:
        pl.semaphore_signal(barrier, inc=1, device_id=peer, device_id_type=MESH)
    bound = bounds_slice(table, f * chans, chans)
    for k in range(4):
        keep_ref[k] = keep_rows(lengths, groups[k], s * rows, rows)
        for c, lanes in enumerate(lanes_of):
            edge = bound[:, lanes]
            forget = edge + (1.0 - edge) * jax.nn.sigmoid(fg_raw[k, :, lanes].astype(F32))
            p_ref[k * count + c] = forget * keep_ref[k]
            q_ref[k * count + c] = d_state[k, :, lanes].astype(F32)

    def scan_step(i, carry):
        new = []
        at = pl.ds(step_len - 1 - i, 8, stride=step_len)
        for n, (product, message) in enumerate(carry):
            a = p_ref[n, at, :]
            acc = q_ref[n, at, :] + message
            p_ref[n, at, :] = product
            q_ref[n, at, :] = acc
            new.append((product * a, a * acc))
        return tuple(new)

    start = tuple((jnp.ones((8, 128), F32), jnp.zeros((8, 128), F32)) for _ in range(blocks))
    ends = lax.fori_loop(0, step_len, scan_step, start)
    for n, (product, message) in enumerate(ends):
        end_p[8 * n : 8 * n + 8] = product
        end_s[8 * n : 8 * n + 8] = message
    p_all, s_all = segment_totals(end_p, end_s, blocks, range(7, -1, -1))
    total[:blocks] = p_all
    total[blocks:] = s_all
    pl.semaphore_wait(barrier, len(peers))
    copies = start_exchange(total, gathered, exchange_send, exchange_recv, n_seq)
    wait_all(copies)
    everything = pl.ds(0, 4 * rows)
    swaps, stays = swap_columns(links, local, d_mixed_all, mixed_half, n_seq, core, mate)
    for src, dst in ((d_gate_raw, gate_pair), (out_gate, out_pair)):
        sent, stayed = swap_rows(links, local, src, dst, everything, mate)
        swaps, stays = swaps + [sent], stays + [stayed]
    carry = jnp.zeros((blocks, 128), F32)
    for j in range(n_seq - 1, 0, -1):
        carry = jnp.where(j > s, gathered[j, blocks:] + gathered[j, :blocks] * carry, carry)
    spread_carry(carry, carr, end_p, end_s, blocks, range(7, -1, -1))

    def finish(n, _):
        enter_state = carr[pl.ds(pl.multiple_of(n * 8, 8), 8)]
        for i in range(step_len):
            at = pl.ds(i, 8, stride=step_len)
            q_ref[n, at, :] = q_ref[n, at, :] + p_ref[n, at, :] * enter_state
        return 0

    lax.fori_loop(0, blocks, finish, 0)
    d_bounds[...] = jnp.zeros_like(d_bounds)
    for k in range(4):
        at = slice(k * rows, (k + 1) * rows)
        for c, lanes in enumerate(lanes_of):
            acc = q_ref[k * count + c]
            edge = bound[:, lanes]
            sigma_f = jax.nn.sigmoid(fg_raw[k, :, lanes].astype(F32))
            forget = edge + (1.0 - edge) * sigma_f
            value = in_raw[k, :, lanes].astype(F32)
            sigma_i = jax.nn.sigmoid(value)
            d_forget = acc * (before[k * count + c] * keep_ref[k] - value * sigma_i)
            d_in[at, lanes] = (acc * (1.0 - forget) * silu_slope(value, sigma_i)).astype(BF16)
            d_sigma = d_forget * (1.0 - sigma_f)
            d_fg[at, lanes] = (d_sigma * (1.0 - edge) * sigma_f).astype(BF16)
            d_bounds[:, lanes] += jnp.sum(d_sigma, 0, keepdims=True)
    for src, dst in ((d_in, in_pair), (d_fg, fg_pair)):
        sent, stayed = swap_rows(links, local, src, dst, everything, mate)
        swaps, stays = swaps + [sent], stays + [stayed]
    wait_all(swaps, stays)


def mixer_backward(
    lengths, d_state, in_raw, fg_raw, before, table, d_gate_raw, out_gate, d_mixed_all, collective_id
):
    n_seq = lax.axis_size("seq")
    _, rows, chans = in_raw.shape
    width = d_mixed_all.shape[1]
    tokens = 4 * rows
    blocks = 4 * chans // 128
    shape = jax.ShapeDtypeStruct
    pair = shape((2, tokens, chans), BF16)
    remote_count = n_seq // 2 + 4
    return pl.pallas_call(
        functools.partial(mixer_backward_kernel, n_seq),
        out_shape=(
            pair,
            pair,
            pair,
            pair,
            shape((2, tokens, width // 2), BF16),
            shape((1, chans), F32),
        ),
        in_specs=[pl.BlockSpec(memory_space=pltpu.SMEM)] + [VMEM] * 8,
        out_specs=(ANY,) * 5 + (VMEM,),
        scratch_shapes=[
            pltpu.VMEM((blocks, rows, 128), F32),
            pltpu.VMEM((blocks, rows, 128), F32),
            pltpu.VMEM((8 * blocks, 128), F32),
            pltpu.VMEM((8 * blocks, 128), F32),
            pltpu.VMEM((8 * blocks, 128), F32),
            pltpu.VMEM((2 * blocks, 128), F32),
            pltpu.VMEM((n_seq, 2 * blocks, 128), F32),
            pltpu.VMEM((4, rows, 128), F32),
            pltpu.VMEM((tokens, chans), BF16),
            pltpu.VMEM((tokens, chans), BF16),
            pltpu.SemaphoreType.DMA((remote_count,)),
            pltpu.SemaphoreType.DMA((remote_count,)),
            pltpu.SemaphoreType.DMA((n_seq,)),
            pltpu.SemaphoreType.DMA((n_seq,)),
            pltpu.SemaphoreType.DMA((remote_count,)),
        ],
        compiler_params=params(collective_id),
        name="mixer_backward",
    )(lengths, d_state, in_raw, fg_raw, before, table, d_gate_raw, out_gate, d_mixed_all)


class ZLine:
    def __init__(self, part, buf, sems, n_seq, width, lag):
        self.part, self.buf, self.width, self.lag = part, buf, width, lag
        self.send_up, self.recv_up, self.send_down, self.recv_down = sems
        self.s, self.f = lax.axis_index("seq"), lax.axis_index("fsdp")
        self.n_seq, self.nz = n_seq, n_seq // 2
        self.z = self.s // 2
        self.block = part.shape[0] // self.nz
        self.chunks = part.shape[1] // width
        self.steps = (self.nz - 1) * self.chunks
        self.calls = self.steps + lag * (self.nz - 2)

    def rows(self, t):
        return pl.ds(pl.multiple_of(t * self.block, self.block), self.block)

    def move(self, up, k, j):
        t = self.nz - 1 - k if up else k
        landing = t + 1 if up else t
        cols = tile(j, self.width)
        slot = k * self.chunks + j
        peer = lax.rem(self.s + (2 if up else self.n_seq - 2), self.n_seq)
        send, recv = (
            (self.send_up, self.recv_up) if up else (self.send_down, self.recv_down)
        )
        return remote(
            self.part.at[self.rows(t), cols],
            self.buf.at[self.rows(landing), cols],
            send.at[slot],
            recv.at[slot],
            (peer, self.f),
        )

    def feed(self, q):
        inside = q < self.steps
        q = jnp.minimum(q, self.steps - 1)
        k = q // self.chunks
        j = q - k * self.chunks

        @pl.when(inside & (self.z == 0))
        def _():
            self.move(True, k, j).start()

        @pl.when(inside & (self.z == self.nz - 1))
        def _():
            self.move(False, k, j).start()

    def serve_one(self, up, q):
        z, nz = self.z, self.nz
        hops = z if up else nz - 1 - z
        q = q - self.lag * (hops - 1)
        inside = (hops >= 1) & (q >= 0) & (q < self.steps)
        q = jnp.clip(q, 0, self.steps - 1)
        k = q // self.chunks
        j = q - k * self.chunks
        left = nz - 1 - k - hops
        cols = tile(j, self.width)

        @pl.when(inside & (left >= 0))
        def _():
            self.move(up, k, j).wait_recv()

        @pl.when(inside & (left > 0))
        def _():
            t = nz - 1 - k if up else k
            landing = t + 1 if up else t
            own = self.part[self.rows(t), cols].astype(F32)
            came = self.buf[self.rows(landing), cols].astype(F32)
            self.part[self.rows(t), cols] = (own + came).astype(BF16)
            self.move(up, k, j).start()

    def serve(self, q):
        self.serve_one(True, q)
        self.serve_one(False, q)

    def serve_range(self, first, last):
        def step(q, _):
            self.feed(q + FEED)
            self.serve(q)
            return 0

        lax.fori_loop(first, last, step, 0)

    def finish(self, store, cols):
        own = self.part[self.rows(self.z), cols].astype(F32)
        above = self.buf[self.rows(self.z), cols].astype(F32)
        below = self.buf[self.rows(self.z + 1), cols].astype(F32)

        @pl.when(self.z == 0)
        def _():
            store(own + above)

        @pl.when((self.z > 0) & (self.z < self.nz - 1))
        def _():
            store(own + above + below)

        @pl.when(self.z == self.nz - 1)
        def _():
            store(own + below)

    def drain(self):
        for k in range(self.nz - 1):
            for up in (True, False):
                hops = self.z if up else self.nz - 1 - self.z

                @pl.when(hops < self.nz - 1 - k)
                def _():
                    def step(j, _):
                        self.move(up, k, j).wait_send()
                        return 0

                    lax.fori_loop(0, self.chunks, step, 0)


FEED = 6


def line_sems(n_seq, columns, width):
    count = (n_seq // 2 - 1) * (columns // width)
    return [pltpu.SemaphoreType.DMA((count,)) for _ in range(4)]


def z_peers(n_seq):
    s = lax.axis_index("seq")
    f = lax.axis_index("fsdp")
    return [(lax.rem(s + 2 * k, n_seq), f) for k in range(1, n_seq // 2)]


def mm_tokens(left, right):
    return lax.dot_general(left, right, (((0,), (0,)), ((), ())), preferred_element_type=F32)


def down_kernel(
    n_seq,
    cot_half,
    act_pair,
    two_half,
    gate_pair,
    up_pair,
    w_gate,
    w_up,
    d_two,
    pair_part,
    down_out,
    cot_ref,
    act_ref,
    two_ref,
    gate_ref,
    up_ref,
    wg,
    wu,
    part,
    buf,
    rows_part,
    from_x,
    from_y,
    pass_x,
    pass_y,
    pair_ref,
    send,
    recv,
    local_sems,
    *line,
):
    rows, width = d_two.shape
    units = act_pair.shape[1]
    s, f, fx, fy, fd = plane()
    links, local = Links(send, recv), Locals(local_sems)
    moves = (
        (cot_half, cot_ref),
        (act_pair, act_ref),
        (w_gate, wg),
        (w_up, wu),
        (gate_pair, gate_ref),
        (up_pair, up_ref),
        (two_half, two_ref),
    )
    loads = [local.start(src, dst) for src, dst in moves]
    enter([(s, fx), (s, fy)] + z_peers(n_seq))
    z_sum = ZLine(part, buf, line, n_seq, 128, 3)
    block = z_sum.block
    loads[0].wait()
    loads[1].wait()

    def down_tile(i, _):
        t = jnp.where(z_sum.z < z_sum.nz // 2, z_sum.nz - 1 - i, i)
        part[z_sum.rows(t)] = mm_tokens(cot_ref[:, tile(t, block)], act_ref[...]).astype(BF16)
        return 0

    down_tile(jnp.int32(0), 0)
    for q in range(FEED):
        z_sum.feed(jnp.int32(q))
    lax.fori_loop(1, z_sum.nz, down_tile, 0)
    for copy in loads[2:]:
        copy.wait()

    def two_part(first, slots, base):
        at = slice(first * rows, (first + slots) * rows)

        def tile_of(n, _):
            cols = tile(n, 512)
            total = mm_t(gate_ref[at], wg[cols]) + mm_t(up_ref[at], wu[cols])
            rows_part[at, cols] = total.astype(BF16)
            z_sum.feed(base + n + FEED)
            z_sum.serve(base + n)
            return 0

        lax.fori_loop(0, width // 512, tile_of, 0)

    count = width // 512
    two_part(3, 1, 0)
    far = reduce_start_far(links, rows_part, from_x, from_y, rows, s, fx, fy)
    two_part(1, 2, count)
    near = reduce_start_near(links, rows_part, from_x, from_y, rows, s, fx, fy)
    two_part(0, 1, 2 * count)
    served = 3 * count

    def pair_tiles(right, first, base):
        def tile_of(t, _):
            pair_ref[z_sum.rows(t), pl.ds(first, units)] = mm_tokens(
                two_ref[:, tile(t, block)], right[...]
            ).astype(BF16)
            z_sum.serve_range(base + 2 * t, base + 2 * t + 2)
            return 0

        lax.fori_loop(0, z_sum.nz, tile_of, 0)

    pair_tiles(gate_ref, 0, served)
    served += 2 * z_sum.nz
    passed = reduce_pass(links, far, rows_part, from_x, from_y, pass_x, pass_y, rows, s, fx, fy)
    pair_tiles(up_ref, units, served)
    served += 2 * z_sum.nz
    stay = local.start(pair_ref, pair_part)
    for copy in near + passed:
        copy.wait_recv()
    half = rows // 2
    d_two[:half] = rows_part[:half].astype(F32) + from_x[1].astype(F32) + from_y[2].astype(F32)
    d_two[half:] = rows_part[half:rows].astype(F32) + from_y[1].astype(F32) + from_x[2].astype(F32)
    z_sum.serve_range(served, z_sum.calls)

    def out_tile(n, _):
        def store(value):
            down_out[tile(n, 128)] = value.T

        z_sum.finish(store, tile(n, 128))
        return 0

    lax.fori_loop(0, units // 128, out_tile, 0)
    z_sum.drain()
    sends_done(far, near, passed)
    stay.wait()


def down_sum(cot_half, act_pair, two_half, gate_pair, up_pair, w_gate, w_up, collective_id):
    n_seq = lax.axis_size("seq")
    tokens, units = act_pair.shape
    width = w_gate.shape[0]
    rows = tokens // 8
    half = (rows // 2, width)
    own = cot_half.shape[1]
    block = width // n_seq
    shape = jax.ShapeDtypeStruct
    return pl.pallas_call(
        functools.partial(down_kernel, n_seq),
        out_shape=(
            shape((rows, width), F32),
            shape((own, 2 * units), BF16),
            shape((units, block), F32),
        ),
        in_specs=[ANY] * 7,
        out_specs=(VMEM, ANY, VMEM),
        scratch_shapes=[
            pltpu.VMEM((tokens, own), BF16),
            pltpu.VMEM((tokens, units), BF16),
            pltpu.VMEM((tokens, own), BF16),
            pltpu.VMEM((tokens, units), BF16),
            pltpu.VMEM((tokens, units), BF16),
            pltpu.VMEM((width, units), BF16),
            pltpu.VMEM((width, units), BF16),
            pltpu.VMEM((own, units), BF16),
            pltpu.VMEM((own + block, units), BF16),
            pltpu.VMEM((tokens // 2, width), BF16),
            pltpu.VMEM((3,) + half, BF16),
            pltpu.VMEM((3,) + half, BF16),
            pltpu.VMEM(half, BF16),
            pltpu.VMEM(half, BF16),
            pltpu.VMEM((own, 2 * units), BF16),
            pltpu.SemaphoreType.DMA((6,)),
            pltpu.SemaphoreType.DMA((6,)),
            pltpu.SemaphoreType.DMA((8,)),
        ]
        + line_sems(n_seq, units, 128),
        compiler_params=params(collective_id),
        name="down_sum",
    )(cot_half, act_pair, two_half, gate_pair, up_pair, w_gate, w_up)


def sum_over_z(part):
    n_seq = lax.axis_size("seq")
    cores = [list(range(core, n_seq, 2)) for core in range(2)]
    return lax.psum_scatter(
        part, "seq", scatter_dimension=0, tiled=True, axis_index_groups=cores
    )


def plane_device(
    hidden,
    lengths,
    w_input,
    w_forget,
    w_gate_out,
    w_output,
    norm_gain,
    gate_gain,
    glu_gain,
    lower_table,
    w_glu_gate,
    w_glu_up,
    w_glu_down,
    cotangent,
):
    fsdp_index = lax.axis_index("fsdp")
    hidden, cotangent = hidden[0], cotangent[0]
    rows, width = hidden.shape
    chans = w_input.shape[1]
    units = w_glu_gate.shape[1]
    tokens = 4 * rows
    small_shape = (8, round_up(rows, 128))

    def over_pairs(left, right):
        left, right = left.reshape(2 * tokens, -1), right.reshape(2 * tokens, -1)
        return lax.dot_general(
            left, right, (((0,), (0,)), ((), ())), preferred_element_type=F32
        ).astype(BF16)

    gains = (norm_gain[None], gate_gain[None], glu_gain[None])
    (
        normed_half,
        cot_all,
        in_raw,
        fg_raw,
        gate_raw,
        state_b,
        out_raw,
        before,
        scale_g,
        middle,
        normed_two,
    ) = mixer_forward(
        lengths,
        hidden,
        cotangent,
        gains,
        lower_table,
        (w_input, w_forget, w_gate_out, w_output),
        0,
    )
    two_half, cot_half, act_pair, gate_pair, up_pair = glu(
        normed_two, cot_all, w_glu_gate, w_glu_up, w_glu_down, 1
    )
    d_normed_two, pair_part, down_grad = down_sum(
        *(x.reshape(2 * tokens, -1) for x in (cot_half, act_pair, two_half, gate_pair, up_pair)),
        w_glu_gate,
        w_glu_up,
        2,
    )
    pair_grad = sum_over_z(pair_part)

    hidden_f = hidden.astype(F32)
    cotangent_f = cotangent.astype(F32)
    scale_two = lax.rsqrt(jnp.mean(middle * middle, -1, keepdims=True) + epsilon)
    scaled_two = glu_gain * d_normed_two
    d_middle = (
        cotangent_f
        + scale_two * scaled_two
        - middle * scale_two**3 * jnp.mean(scaled_two * middle, -1, keepdims=True)
    )
    d_glu_gain = jnp.sum(d_normed_two * middle * scale_two, 0)
    d_mixed = d_middle.astype(BF16)
    own_dot = jnp.sum(d_mixed.astype(F32) * (middle - hidden_f), -1)[None]
    own_dot = jnp.pad(own_dot, ((0, 7), (0, small_shape[1] - rows)))
    d_mixed_all, dots = slot_gather(d_mixed, own_dot, 3)
    dot_rows = dots[:, 0, :rows].reshape(tokens, 1)

    scale_g = scale_g.reshape(tokens, 1)
    gate_raw = gate_raw.reshape(tokens, chans)
    state_f = state_b.astype(F32).reshape(tokens, chans)
    gain_slice = lax.dynamic_slice_in_dim(gate_gain, fsdp_index * chans, chans)
    sigma_g = jax.nn.sigmoid(gate_raw)
    silu_gate = gate_raw * sigma_g
    d_out = mm_t(d_mixed_all, w_output)
    scaled_state = state_f * scale_g
    d_gain_slice = jnp.sum(d_out * scaled_state * silu_gate, 0)
    d_scaled = d_out * gain_slice * silu_gate
    d_gate_raw = (d_out * scaled_state * gain_slice * silu_slope(gate_raw, sigma_g)).astype(BF16)
    d_state = scale_g * d_scaled - state_f * (scale_g**2 * (dot_rows / width))
    d_state = d_state.astype(BF16).reshape(4, rows, chans)
    out_gate = (out_raw.astype(F32) * scale_g).astype(BF16)
    in_pair, fg_pair, gate_raw_pair, out_pair, mixed_half, d_bounds = mixer_backward(
        lengths, d_state, in_raw, fg_raw, before, lower_table, d_gate_raw, out_gate, d_mixed_all, 4
    )
    mixer_part = jnp.concatenate(
        [
            over_pairs(mixed_half, out_pair),
            over_pairs(normed_half, in_pair),
            over_pairs(normed_half, fg_pair),
            over_pairs(normed_half, gate_raw_pair),
        ],
        1,
    )
    mixer_ready, in_pair, fg_pair, d_gate_raw = lax.optimization_barrier(
        (mixer_part, in_pair, fg_pair, d_gate_raw)
    )
    d_normed_part = mm_t(in_pair[0], w_input) + mm_t(fg_pair[0], w_forget)
    d_normed_part = (d_normed_part + mm_t(d_gate_raw, w_gate_out)).astype(BF16)
    d_normed = slot_reduce(d_normed_part, 5)
    mixer_ready, pair_grad, d_normed = lax.optimization_barrier((mixer_ready, pair_grad, d_normed))
    mixer_grad = sum_over_z(mixer_ready).astype(F32)

    scale_one = lax.rsqrt(jnp.mean(hidden_f * hidden_f, -1, keepdims=True) + epsilon)
    scaled_one = norm_gain * d_normed
    d_hidden = (
        d_middle
        + scale_one * scaled_one
        - hidden_f * scale_one**3 * jnp.mean(scaled_one * hidden_f, -1, keepdims=True)
    )
    d_norm_gain = jnp.sum(d_normed * hidden_f * scale_one, 0)
    d_gain_full = lax.dynamic_update_slice(
        jnp.zeros((width,), F32), d_gain_slice, (fsdp_index * chans,)
    )
    d_bounds_full = lax.dynamic_update_slice(
        jnp.zeros((width,), F32), d_bounds[0], (fsdp_index * chans,)
    )
    sums = jnp.stack([d_norm_gain, d_glu_gain, d_gain_full, d_bounds_full])
    totals = sum_all(sums.reshape(8, width // 2), 6).reshape(4, width)
    _, bounds_pull = jax.vjp(lower_bound, lower_table)
    d_table = bounds_pull(totals[3])[0]

    act, _ = lax.optimization_barrier((act_pair[0], d_normed))
    glu_part = mm(act, w_glu_down).astype(BF16)
    output = (middle + slot_reduce(glu_part, 7)).astype(BF16)
    pair_grad = pair_grad.astype(F32)
    return (
        output[None],
        d_hidden.astype(BF16)[None],
        mixer_grad[:, chans : 2 * chans],
        mixer_grad[:, 2 * chans : 3 * chans],
        mixer_grad[:, 3 * chans :],
        mixer_grad[:, :chans].T,
        totals[0],
        totals[2],
        totals[1],
        d_table,
        pair_grad[:, :units],
        pair_grad[:, units:],
        down_grad,
    )


def fits_plane(mesh):
    return mesh.shape["fsdp"] == 4 and mesh.shape["seq"] % 2 == 0


def solution(mesh):
    rows_spec = P("fsdp", "seq", None)
    columns = P(None, "fsdp")
    placed = (
        rows_spec,
        P(),
        columns,
        columns,
        columns,
        P("fsdp", None),
        P(),
        P(),
        P(),
        P(),
        columns,
        columns,
        P("fsdp", None),
        rows_spec,
    )
    by_rows, by_columns = P("seq", "fsdp"), P("fsdp", "seq")
    return jax.shard_map(
        plane_device if fits_plane(mesh) else per_device,
        mesh=mesh,
        in_specs=placed,
        out_specs=(
            rows_spec,
            rows_spec,
            by_rows,
            by_rows,
            by_rows,
            by_columns,
            P(),
            P(),
            P(),
            P(),
            by_rows,
            by_rows,
            by_columns,
        ),
        check_vma=False,
    )
```

```python
import functools

import jax
import jax.numpy as jnp
from jax import lax
from jax.experimental import pallas as pl
from jax.experimental.pallas import tpu as pltpu
from jax.sharding import PartitionSpec as P

LAYER = 12
MESH = pl.DeviceIdType.MESH
F32 = jnp.float32
BF16 = jnp.bfloat16

epsilon = 1e-06

VMEM = pl.BlockSpec(memory_space=pltpu.VMEM)
ANY = pl.BlockSpec(memory_space=pl.ANY)


def lower_bound(table):
    soft = jax.nn.softmax(table, axis=0)
    totals = jnp.cumsum(soft, axis=0)
    return totals[LAYER] - totals[0]


def silu_slope(value, sigma):
    return sigma * (1.0 + value * (1.0 - sigma))


def params(collective_id):
    return pltpu.CompilerParams(
        collective_id=collective_id, has_side_effects=True, vmem_limit_bytes=56 << 20
    )


def round_up(value, unit):
    return -(-value // unit) * unit


def plane():
    s = lax.axis_index("seq")
    f = lax.axis_index("fsdp")
    y, x = f // 2, f % 2
    fx = y * 2 + (1 - x)
    fy = (1 - y) * 2 + x
    fd = (1 - y) * 2 + (1 - x)
    return s, f, fx, fy, fd


def enter(devices):
    barrier = pltpu.get_barrier_semaphore()
    for device in devices:
        pl.semaphore_signal(barrier, inc=1, device_id=device, device_id_type=MESH)
    pl.semaphore_wait(barrier, len(devices))


def remote(src, dst, send, recv, device):
    return pltpu.make_async_remote_copy(
        src_ref=src,
        dst_ref=dst,
        send_sem=send,
        recv_sem=recv,
        device_id=device,
        device_id_type=MESH,
    )


def gather(x, small, collective_id):
    return lax.all_gather(x, "fsdp"), lax.all_gather(small, "fsdp")


def reduce_rows(p, small, collective_id):
    total = lax.psum_scatter(p, "fsdp", scatter_dimension=0, tiled=True)[0]
    return total.astype(F32), lax.psum(small, "fsdp")


def start_exchange(total, gathered, send, recv, n_seq):
    s = lax.axis_index("seq")
    f = lax.axis_index("fsdp")
    copies = []
    for k in range(1, n_seq):
        peer = lax.rem(s + k, n_seq)
        copy = remote(total, gathered.at[s], send.at[k], recv.at[k], (peer, f))
        copy.start()
        copies.append(copy)
    gathered[pl.ds(s, 1)] = total[...][None]
    return copies


def seq_peers(n_seq):
    s = lax.axis_index("seq")
    f = lax.axis_index("fsdp")
    return [(lax.rem(s + k, n_seq), f) for k in range(1, n_seq)]


def lane_blocks(groups, chans):
    return [(g, slice(c, c + 128)) for g in range(groups) for c in range(0, chans, 128)]


def forward_scan_kernel(
    n_seq, in_raw, forget_raw, bounds, keep, state_b, before, a_ref, b_ref, total, gathered, send, recv
):
    groups, rows, chans = in_raw.shape
    part = rows // 8
    blocks = lane_blocks(groups, chans)
    s = lax.axis_index("seq")
    barrier = pltpu.get_barrier_semaphore()
    for peer in seq_peers(n_seq):
        pl.semaphore_signal(barrier, inc=1, device_id=peer, device_id_type=MESH)
    for n, (g, lanes) in enumerate(blocks):
        bound = bounds[:, lanes]
        forget = bound + (1.0 - bound) * jax.nn.sigmoid(forget_raw[g, :, lanes].astype(F32))
        value = in_raw[g, :, lanes].astype(F32)
        a_ref[n] = forget * keep[g]
        b_ref[n] = value * jax.nn.sigmoid(value) * (1.0 - forget)

    def step(i, carry):
        new = []
        at = pl.ds(i, 8, stride=part)
        for n, (product, state) in enumerate(carry):
            a = a_ref[n, at, :]
            state = a * state + b_ref[n, at, :]
            product = product * a
            a_ref[n, at, :] = product
            b_ref[n, at, :] = state
            new.append((product, state))
        return tuple(new)

    start = tuple((jnp.ones((8, 128), F32), jnp.zeros((8, 128), F32)) for _ in blocks)
    ends = lax.fori_loop(0, part, step, start)
    for n, (product, state) in enumerate(ends):
        p_all, s_all = product[0:1], state[0:1]
        for j in range(1, 8):
            p_all, s_all = p_all * product[j : j + 1], state[j : j + 1] + product[j : j + 1] * s_all
        total[2 * n : 2 * n + 1] = p_all
        total[2 * n + 1 : 2 * n + 2] = s_all
    pl.semaphore_wait(barrier, n_seq - 1)
    copies = start_exchange(total, gathered, send, recv, n_seq)
    for copy in copies:
        copy.wait()
    for n, (g, lanes) in enumerate(blocks):
        carry = jnp.zeros((1, 128), F32)
        for j in range(n_seq - 1):
            p_j = gathered[j, 2 * n : 2 * n + 1]
            s_j = gathered[j, 2 * n + 1 : 2 * n + 2]
            carry = jnp.where(j < s, s_j + p_j * carry, carry)
        before[g, 0:1, lanes] = carry
        product, state = ends[n]
        carries = [carry]
        for j in range(7):
            carries.append(state[j : j + 1] + product[j : j + 1] * carries[-1])
        for j in range(8):
            at = slice(j * part, (j + 1) * part)
            b_ref[n, at] = b_ref[n, at] + a_ref[n, at] * carries[j]
        state_b[g, :, lanes] = b_ref[n].astype(BF16)
        before[g, 1:rows, lanes] = b_ref[n, 0 : rows - 1]


def forward_scan(in_raw, forget_raw, bounds, keep, collective_id):
    n_seq = lax.axis_size("seq")
    groups, rows, chans = in_raw.shape
    blocks = groups * chans // 128
    return pl.pallas_call(
        functools.partial(forward_scan_kernel, n_seq),
        out_shape=(
            jax.ShapeDtypeStruct(in_raw.shape, BF16),
            jax.ShapeDtypeStruct(in_raw.shape, F32),
        ),
        in_specs=[VMEM] * 4,
        out_specs=(VMEM, VMEM),
        scratch_shapes=[
            pltpu.VMEM((blocks, rows, 128), F32),
            pltpu.VMEM((blocks, rows, 128), F32),
            pltpu.VMEM((2 * blocks, 128), F32),
            pltpu.VMEM((n_seq, 2 * blocks, 128), F32),
            pltpu.SemaphoreType.DMA((n_seq,)),
            pltpu.SemaphoreType.DMA((n_seq,)),
        ],
        compiler_params=params(collective_id),
        name="forward_scan",
    )(in_raw, forget_raw, bounds, keep)


def backward_scan_kernel(
    n_seq,
    d_state,
    in_raw,
    forget_raw,
    before,
    bounds,
    keep,
    d_in,
    d_forget_raw,
    d_bounds,
    p_ref,
    q_ref,
    total,
    gathered,
    send,
    recv,
):
    groups, rows, chans = in_raw.shape
    part = rows // 8
    blocks = lane_blocks(groups, chans)
    s = lax.axis_index("seq")
    barrier = pltpu.get_barrier_semaphore()
    for peer in seq_peers(n_seq):
        pl.semaphore_signal(barrier, inc=1, device_id=peer, device_id_type=MESH)
    for n, (g, lanes) in enumerate(blocks):
        bound = bounds[:, lanes]
        forget = bound + (1.0 - bound) * jax.nn.sigmoid(forget_raw[g, :, lanes].astype(F32))
        p_ref[n] = forget * keep[g]
        q_ref[n] = d_state[g, :, lanes].astype(F32)

    def step(i, carry):
        new = []
        at = pl.ds(part - 1 - i, 8, stride=part)
        for n, (product, message) in enumerate(carry):
            a = p_ref[n, at, :]
            acc = q_ref[n, at, :] + message
            p_ref[n, at, :] = product
            q_ref[n, at, :] = acc
            new.append((product * a, a * acc))
        return tuple(new)

    start = tuple((jnp.ones((8, 128), F32), jnp.zeros((8, 128), F32)) for _ in blocks)
    ends = lax.fori_loop(0, part, step, start)
    for n, (product, message) in enumerate(ends):
        p_all, m_all = product[7:8], message[7:8]
        for j in range(6, -1, -1):
            p_all, m_all = p_all * product[j : j + 1], message[j : j + 1] + product[j : j + 1] * m_all
        total[2 * n : 2 * n + 1] = p_all
        total[2 * n + 1 : 2 * n + 2] = m_all
    pl.semaphore_wait(barrier, n_seq - 1)
    copies = start_exchange(total, gathered, send, recv, n_seq)
    for copy in copies:
        copy.wait()
    d_bounds[...] = jnp.zeros((1, chans), F32)
    for n, (g, lanes) in enumerate(blocks):
        carry = jnp.zeros((1, 128), F32)
        for j in range(n_seq - 1, 0, -1):
            p_j = gathered[j, 2 * n : 2 * n + 1]
            m_j = gathered[j, 2 * n + 1 : 2 * n + 2]
            carry = jnp.where(j > s, m_j + p_j * carry, carry)
        product, message = ends[n]
        carries = [carry]
        for j in range(7, 0, -1):
            carries.append(message[j : j + 1] + product[j : j + 1] * carries[-1])
        carries = carries[::-1]
        for j in range(8):
            at = slice(j * part, (j + 1) * part)
            q_ref[n, at] = q_ref[n, at] + p_ref[n, at] * carries[j]
        acc = q_ref[n]
        bound = bounds[:, lanes]
        sigma_f = jax.nn.sigmoid(forget_raw[g, :, lanes].astype(F32))
        forget = bound + (1.0 - bound) * sigma_f
        value = in_raw[g, :, lanes].astype(F32)
        sigma_i = jax.nn.sigmoid(value)
        d_forget = acc * (before[g, :, lanes] * keep[g] - value * sigma_i)
        d_in[g, :, lanes] = (acc * (1.0 - forget) * silu_slope(value, sigma_i)).astype(BF16)
        d_sigma = d_forget * (1.0 - sigma_f)
        d_forget_raw[g, :, lanes] = (d_sigma * (1.0 - bound) * sigma_f).astype(BF16)
        d_bounds[:, lanes] += jnp.sum(d_sigma, 0, keepdims=True)


def backward_scan(d_state, in_raw, forget_raw, before, bounds, keep, collective_id):
    n_seq = lax.axis_size("seq")
    groups, rows, chans = in_raw.shape
    blocks = groups * chans // 128
    return pl.pallas_call(
        functools.partial(backward_scan_kernel, n_seq),
        out_shape=(
            jax.ShapeDtypeStruct(in_raw.shape, BF16),
            jax.ShapeDtypeStruct(in_raw.shape, BF16),
            jax.ShapeDtypeStruct((1, chans), F32),
        ),
        in_specs=[VMEM] * 6,
        out_specs=(VMEM, VMEM, VMEM),
        scratch_shapes=[
            pltpu.VMEM((blocks, rows, 128), F32),
            pltpu.VMEM((blocks, rows, 128), F32),
            pltpu.VMEM((2 * blocks, 128), F32),
            pltpu.VMEM((n_seq, 2 * blocks, 128), F32),
            pltpu.SemaphoreType.DMA((n_seq,)),
            pltpu.SemaphoreType.DMA((n_seq,)),
        ],
        compiler_params=params(collective_id),
        name="backward_scan",
    )(d_state, in_raw, forget_raw, before, bounds, keep)


def sum_all_kernel(n_seq, n_fsdp, x, out, middle, over_seq, over_fsdp, send, recv):
    s = lax.axis_index("seq")
    f = lax.axis_index("fsdp")
    along = [(lax.rem(s + k, n_seq), f) for k in range(1, n_seq)]
    across = [(s, lax.rem(f + k, n_fsdp)) for k in range(1, n_fsdp)]
    enter(along + across)
    copies = []
    for k, peer in enumerate(along):
        copy = remote(x, over_seq.at[k], send.at[k], recv.at[k], peer)
        copy.start()
        copies.append(copy)
    total = x[...]
    for k, copy in enumerate(copies):
        copy.wait_recv()
        total = total + over_seq[k]
    middle[...] = total
    later = []
    for k, peer in enumerate(across):
        slot = n_seq - 1 + k
        copy = remote(middle, over_fsdp.at[k], send.at[slot], recv.at[slot], peer)
        copy.start()
        later.append(copy)
    for k, copy in enumerate(later):
        copy.wait_recv()
        total = total + over_fsdp[k]
    out[...] = total
    for copy in copies + later:
        copy.wait_send()


def sum_all(x, collective_id):
    n_seq, n_fsdp = lax.axis_size("seq"), lax.axis_size("fsdp")
    count = n_seq + n_fsdp - 2
    return pl.pallas_call(
        functools.partial(sum_all_kernel, n_seq, n_fsdp),
        out_shape=jax.ShapeDtypeStruct(x.shape, F32),
        in_specs=[VMEM],
        out_specs=VMEM,
        scratch_shapes=[
            pltpu.VMEM(x.shape, F32),
            pltpu.VMEM((n_seq - 1,) + x.shape, F32),
            pltpu.VMEM((n_fsdp - 1,) + x.shape, F32),
            pltpu.SemaphoreType.DMA((count,)),
            pltpu.SemaphoreType.DMA((count,)),
        ],
        compiler_params=params(collective_id),
        name="sum_all",
    )(x)


def sum_over_seq(part):
    return lax.psum_scatter(part.astype(BF16), "seq", scatter_dimension=0, tiled=True).astype(F32)


def per_device(
    hidden,
    lengths,
    w_input,
    w_forget,
    w_gate_out,
    w_output,
    norm_gain,
    gate_gain,
    glu_gain,
    lower_table,
    w_glu_gate,
    w_glu_up,
    w_glu_down,
    cotangent,
):
    seq_index = lax.axis_index("seq")
    fsdp_index = lax.axis_index("fsdp")
    groups = lax.axis_size("fsdp")
    _, rows, width = hidden.shape
    chans = w_input.shape[1]
    units = w_glu_gate.shape[1]
    tokens = groups * rows
    small_shape = (round_up(groups, 8), round_up(rows, 128))

    def to_small(value):
        return jnp.pad(
            value, ((0, small_shape[0] - value.shape[0]), (0, small_shape[1] - value.shape[1]))
        )

    def dot(left, right):
        return jnp.dot(left, right, preferred_element_type=F32)

    def dot_t(left, right):
        return lax.dot_general(left, right, (((1,), (1,)), ((), ())), preferred_element_type=F32)

    def over_tokens(left, right):
        return lax.dot_general(left, right, (((0,), (0,)), ((), ())), preferred_element_type=F32)

    cotangent_all = lax.all_gather(cotangent[0], "fsdp").reshape(tokens, width)

    hidden_f = hidden[0].astype(F32)
    scale_one = lax.rsqrt(jnp.mean(hidden_f * hidden_f, -1, keepdims=True) + epsilon)
    normed = (hidden_f * scale_one * norm_gain).astype(BF16)
    normed_all, _ = gather(normed, jnp.zeros((8, 128), F32), 0)
    normed_all = normed_all.reshape(tokens, width)
    in_raw = dot(normed_all, w_input).astype(BF16).reshape(groups, rows, chans)
    forget_raw = dot(normed_all, w_forget).astype(BF16).reshape(groups, rows, chans)
    gate_raw = dot(normed_all, w_gate_out)

    bounds_full = lower_bound(lower_table)
    bounds = lax.dynamic_slice_in_dim(bounds_full, fsdp_index * chans, chans)[None]
    seq_starts = jnp.cumsum(lengths, axis=1) - lengths
    places = seq_index * rows + jnp.arange(rows, dtype=jnp.int32)
    starts = jnp.any(places[None, :, None] == seq_starts[:, None, :], axis=-1)
    keep = jnp.where(starts, 0.0, 1.0).astype(F32)[:, :, None]
    state_b, before = forward_scan(in_raw, forget_raw, bounds, keep, 1)

    state_f = state_b.astype(F32).reshape(tokens, chans)
    gain_slice = lax.dynamic_slice_in_dim(gate_gain, fsdp_index * chans, chans)
    sigma_g = jax.nn.sigmoid(gate_raw)
    silu_gate = gate_raw * sigma_g
    out_raw = (state_f * gain_slice * silu_gate).astype(BF16)
    squares = jnp.sum(state_f * state_f, -1).reshape(groups, rows)
    mixed_part = dot(out_raw, w_output).astype(BF16).reshape(groups, rows, width)
    mixed_raw, square_sum = reduce_rows(mixed_part, to_small(squares), 2)
    state_scale = lax.rsqrt(square_sum[:groups, :rows] / width + epsilon)
    own_scale = lax.dynamic_slice_in_dim(state_scale, fsdp_index, 1, 0)[0][:, None]
    scale_g = state_scale.reshape(tokens, 1)
    middle = hidden_f + own_scale * mixed_raw
    scale_two = lax.rsqrt(jnp.mean(middle * middle, -1, keepdims=True) + epsilon)
    normed_two = (middle * scale_two * glu_gain).astype(BF16)
    normed_two_all, _ = gather(normed_two, jnp.zeros((8, 128), F32), 3)
    normed_two_all = normed_two_all.reshape(tokens, width)

    gate_val = dot(normed_two_all, w_glu_gate)
    up_val = dot(normed_two_all, w_glu_up)
    sigma_u = jax.nn.sigmoid(gate_val)
    silu_u = gate_val * sigma_u
    activity = (silu_u * up_val).astype(BF16)
    down_grad = sum_over_seq(over_tokens(cotangent_all, activity))
    d_act = dot_t(cotangent_all, w_glu_down)
    d_gate = (d_act * up_val * silu_slope(gate_val, sigma_u)).astype(BF16)
    d_up = (d_act * silu_u).astype(BF16)
    pair_grad = sum_over_seq(
        jnp.concatenate(
            [
                over_tokens(normed_two_all, d_gate).astype(BF16),
                over_tokens(normed_two_all, d_up).astype(BF16),
            ],
            1,
        )
    )
    d_two_part = (dot_t(d_gate, w_glu_gate) + dot_t(d_up, w_glu_up)).astype(BF16)
    no_small = jnp.zeros((8, 128), F32)
    d_normed_two, _ = reduce_rows(d_two_part.reshape(groups, rows, width), no_small, 4)
    glu_part = dot(activity, w_glu_down).astype(BF16).reshape(groups, rows, width)
    glu_result = lax.psum_scatter(glu_part, "fsdp", scatter_dimension=0, tiled=True)[0]
    output = (middle + glu_result.astype(F32)).astype(BF16)[None]

    cotangent_f = cotangent[0].astype(F32)
    scaled_two = glu_gain * d_normed_two
    d_middle = (
        cotangent_f
        + scale_two * scaled_two
        - middle * scale_two**3 * jnp.mean(scaled_two * middle, -1, keepdims=True)
    )
    d_glu_gain = jnp.sum(d_normed_two * middle * scale_two, 0)
    d_mixed = d_middle.astype(BF16)
    own_dot = jnp.sum(d_mixed.astype(F32) * mixed_raw, -1)[None]
    d_mixed_all, dots = gather(d_mixed, to_small(own_dot), 5)
    d_mixed_all = d_mixed_all.reshape(tokens, width)
    dot_rows = dots[:, 0, :rows].reshape(tokens, 1)

    d_out = dot_t(d_mixed_all, w_output)
    scaled_state = state_f * scale_g
    d_gain_slice = jnp.sum(d_out * scaled_state * silu_gate, 0)
    d_scaled = d_out * gain_slice * silu_gate
    d_gate_raw = (d_out * scaled_state * gain_slice * silu_slope(gate_raw, sigma_g)).astype(BF16)
    d_state = scale_g * d_scaled - state_f * (scale_g**3 * (dot_rows / width))
    d_state = d_state.astype(BF16).reshape(groups, rows, chans)
    d_in, d_forget_raw, d_bounds = backward_scan(
        d_state, in_raw, forget_raw, before, bounds, keep, 6
    )
    d_in = d_in.reshape(tokens, chans)
    d_forget_raw = d_forget_raw.reshape(tokens, chans)

    d_normed_part = dot_t(d_in, w_input) + dot_t(d_forget_raw, w_forget)
    d_normed_part = (d_normed_part + dot_t(d_gate_raw, w_gate_out)).astype(BF16)
    out_gate = (out_raw.astype(F32) * scale_g).astype(BF16)
    mixer_grad = sum_over_seq(
        jnp.concatenate(
            [
                over_tokens(d_mixed_all, out_gate).astype(BF16),
                over_tokens(normed_all, d_in).astype(BF16),
                over_tokens(normed_all, d_forget_raw).astype(BF16),
                over_tokens(normed_all, d_gate_raw).astype(BF16),
            ],
            1,
        )
    )
    d_normed, _ = reduce_rows(d_normed_part.reshape(groups, rows, width), no_small, 7)
    scaled_one = norm_gain * d_normed
    d_hidden = (
        d_middle
        + scale_one * scaled_one
        - hidden_f * scale_one**3 * jnp.mean(scaled_one * hidden_f, -1, keepdims=True)
    )
    d_norm_gain = jnp.sum(d_normed * hidden_f * scale_one, 0)
    d_gain_full = lax.dynamic_update_slice(
        jnp.zeros((width,), F32), d_gain_slice, (fsdp_index * chans,)
    )
    d_bounds_full = lax.dynamic_update_slice(
        jnp.zeros((width,), F32), d_bounds[0], (fsdp_index * chans,)
    )
    sums = jnp.stack([d_norm_gain, d_glu_gain, d_gain_full, d_bounds_full])
    totals = sum_all(sums.reshape(8, width // 2), 8).reshape(4, width)
    _, bounds_pull = jax.vjp(lower_bound, lower_table)
    d_table = bounds_pull(totals[3])[0]
    return (
        output,
        d_hidden.astype(BF16)[None],
        mixer_grad[:, chans : 2 * chans],
        mixer_grad[:, 2 * chans : 3 * chans],
        mixer_grad[:, 3 * chans :],
        mixer_grad[:, :chans].T,
        totals[0],
        totals[2],
        totals[1],
        d_table,
        pair_grad[:, :units],
        pair_grad[:, units:],
        down_grad.T,
    )


def copy_in(src, dst, sem):
    copy = pltpu.make_async_copy(src, dst, sem)
    copy.start()
    return copy


class Links:
    def __init__(self, send, recv):
        self.send, self.recv, self.used = send, recv, 0

    def start(self, src, dst, device):
        copy = remote(src, dst, self.send.at[self.used], self.recv.at[self.used], device)
        self.used += 1
        copy.start()
        return copy


class Locals:
    def __init__(self, sems):
        self.sems, self.used = sems, 0

    def start(self, src, dst):
        copy = copy_in(src, dst, self.sems.at[self.used])
        self.used += 1
        return copy


def row_slots(rows):
    half = rows // 2
    top = [pl.ds(k * rows, half) for k in range(4)]
    bottom = [pl.ds(k * rows + half, half) for k in range(4)]
    return top, bottom


def gather_start(links, src, dst, rows, s, fx, fy):
    half = rows // 2
    top, bottom = row_slots(rows)
    here = (pl.ds(0, half), pl.ds(half, half))
    return [
        links.start(src.at[here[0]], dst.at[top[1]], (s, fx)),
        links.start(src.at[here[1]], dst.at[bottom[2]], (s, fy)),
        links.start(src.at[here[1]], dst.at[bottom[1]], (s, fx)),
        links.start(src.at[here[0]], dst.at[top[2]], (s, fy)),
    ]


def gather_forward(links, own, dst, rows, s, fx, fy):
    top, bottom = row_slots(rows)
    own[0].wait_recv()
    on_y = links.start(dst.at[top[1]], dst.at[top[3]], (s, fy))
    own[1].wait_recv()
    on_x = links.start(dst.at[bottom[2]], dst.at[bottom[3]], (s, fx))
    return [on_y, on_x]


def gather_middle(own):
    own[2].wait_recv()
    own[3].wait_recv()


def gather_far(later):
    for copy in later:
        copy.wait_recv()


def sends_done(*lists):
    for copies in lists:
        for copy in copies:
            copy.wait_send()


def wait_all(*lists):
    for copies in lists:
        for copy in copies:
            copy.wait()


def reduce_start_far(links, part, from_x, from_y, rows, s, fx, fy):
    top, bottom = row_slots(rows)
    return [
        links.start(part.at[top[3]], from_x.at[0], (s, fx)),
        links.start(part.at[bottom[3]], from_y.at[0], (s, fy)),
    ]


def reduce_start_near(links, part, from_x, from_y, rows, s, fx, fy):
    top, bottom = row_slots(rows)
    return [
        links.start(part.at[top[1]], from_x.at[1], (s, fx)),
        links.start(part.at[bottom[2]], from_y.at[1], (s, fy)),
    ]


def reduce_pass(links, far, part, from_x, from_y, pass_x, pass_y, rows, s, fx, fy):
    top, bottom = row_slots(rows)
    far[0].wait_recv()
    pass_y[...] = (from_x[0].astype(F32) + part[top[2]].astype(F32)).astype(BF16)
    on_y = links.start(pass_y, from_y.at[2], (s, fy))
    far[1].wait_recv()
    pass_x[...] = (from_y[0].astype(F32) + part[bottom[1]].astype(F32)).astype(BF16)
    on_x = links.start(pass_x, from_x.at[2], (s, fx))
    return [on_y, on_x]


def mm(left, right):
    return jnp.dot(left, right, preferred_element_type=F32)


def mm_t(left, right):
    return lax.dot_general(left, right, (((1,), (1,)), ((), ())), preferred_element_type=F32)


def tile(n, width):
    return pl.ds(pl.multiple_of(n * width, width), width)


def bounds_slice(table, first, count):
    rows = table[:, pl.ds(pl.multiple_of(first, 128), count)]
    powers = jnp.exp(rows - jnp.max(rows, 0, keepdims=True))
    return jnp.sum(powers[1 : LAYER + 1], 0, keepdims=True) / jnp.sum(powers, 0, keepdims=True)


def keep_rows(lengths, group, first, rows):
    places = first + lax.broadcasted_iota(jnp.int32, (rows, 128), 0)
    start = jnp.int32(0)
    keep = jnp.where(places == start, 0.0, 1.0)
    for i in range(lengths.shape[1] - 1):
        start = start + lengths[group, i]
        keep = jnp.where(places == start, 0.0, keep)
    return keep.astype(F32)


def segment_totals(end_p, end_s, blocks, order):
    first, rest = order[0], order[1:]
    p_all = end_p[pl.ds(first, blocks, stride=8), :]
    s_all = end_s[pl.ds(first, blocks, stride=8), :]
    for j in rest:
        p_j = end_p[pl.ds(j, blocks, stride=8), :]
        s_all = end_s[pl.ds(j, blocks, stride=8), :] + p_j * s_all
        p_all = p_all * p_j
    return p_all, s_all


def spread_carry(carry, carr, end_p, end_s, blocks, order):
    for i, j in enumerate(order):
        carr[pl.ds(j, blocks, stride=8), :] = carry
        if i < 7:
            carry = end_s[pl.ds(j, blocks, stride=8), :] + end_p[pl.ds(j, blocks, stride=8), :] * carry


def mixer_kernel(
    n_seq,
    lengths,
    hidden,
    cot,
    norm_gain,
    gate_gain,
    glu_gain,
    table,
    w_in,
    w_fg,
    w_gt,
    w_out,
    normed_half,
    cot_out,
    in_out,
    fg_out,
    gate_out,
    state_out,
    raw_out,
    before_out,
    scale_out,
    middle,
    two,
    wv,
    wo,
    rows_all,
    stage,
    in_ref,
    fg_ref,
    gate_ref,
    a_ref,
    b_ref,
    shifted,
    keep_ref,
    end_p,
    end_s,
    carr,
    total,
    gathered,
    state_ref,
    raw_ref,
    squares,
    squares_in,
    part,
    from_x,
    from_y,
    pass_x,
    pass_y,
    send,
    recv,
    exchange_send,
    exchange_recv,
    local_sems,
):
    rows, width = hidden.shape
    chans = w_in.shape[1]
    lanes_of = [slice(c, c + 128) for c in range(0, chans, 128)]
    count = len(lanes_of)
    blocks = 4 * count
    step_len = rows // 8
    s, f, fx, fy, fd = plane()
    groups = [f, fx, fy, fd]
    links, local = Links(send, recv), Locals(local_sems)

    weights = [
        local.start(w, wv.at[:, pl.ds(i * chans, chans)]) for i, w in enumerate((w_in, w_fg, w_gt))
    ]
    weights.append(local.start(w_out, wo))
    barrier = pltpu.get_barrier_semaphore()
    peers = [(s, fx), (s, fy), (s, fd)] + seq_peers(n_seq)
    for peer in peers:
        pl.semaphore_signal(barrier, inc=1, device_id=peer, device_id_type=MESH)

    def norm_rows(i, _):
        at = pl.ds(pl.multiple_of(i * 16, 16), 16)
        value = hidden[at].astype(F32)
        scale = lax.rsqrt(jnp.mean(value * value, -1, keepdims=True) + epsilon)
        rows_all[at] = (value * scale * norm_gain[...]).astype(BF16)
        return 0

    lax.fori_loop(0, rows // 16, norm_rows, 0)
    pl.semaphore_wait(barrier, len(peers))
    own = gather_start(links, rows_all, rows_all, rows, s, fx, fy)
    bound = bounds_slice(table, f * chans, chans)
    for k in range(4):
        keep_ref[k] = keep_rows(lengths, groups[k], s * rows, rows)
    squares[...] = jnp.zeros_like(squares)
    for copy in weights[:3]:
        copy.wait()

    def project(first, slots):
        def tile_of(n, _):
            cols = tile(n, 256)
            stage[: slots * rows, cols] = mm(
                rows_all[first * rows : (first + slots) * rows], wv[:, cols]
            )
            return 0

        lax.fori_loop(0, 3 * chans // 256, tile_of, 0)
        for k in range(slots):
            at = slice(k * rows, (k + 1) * rows)
            for c, lanes in enumerate(lanes_of):
                n = (first + k) * count + c
                value = stage[at, lanes].astype(BF16)
                in_ref[first + k, :, lanes] = value
                value = value.astype(F32)
                raw = stage[at, chans + c * 128 : chans + (c + 1) * 128].astype(BF16)
                fg_ref[first + k, :, lanes] = raw
                edge = bound[:, lanes]
                forget = edge + (1.0 - edge) * jax.nn.sigmoid(raw.astype(F32))
                a_ref[n] = forget * keep_ref[first + k]
                b_ref[n] = value * jax.nn.sigmoid(value) * (1.0 - forget)
            gate_ref[first + k] = stage[at, 2 * chans :]

    project(0, 1)
    later = gather_forward(links, own, rows_all, rows, s, fx, fy)
    gather_middle(own)
    project(1, 2)
    gather_far(later)
    cot_own = gather_start(links, cot, cot_out, rows, s, fx, fy)
    core = s % 2
    swaps, outs = swap_columns(
        links, local, rows_all, normed_half, n_seq, core, (s + 1 - 2 * core, f)
    )
    outs.append(local.start(cot, cot_out.at[pl.ds(0, rows)]))
    project(3, 1)
    outs += [
        local.start(in_ref, in_out),
        local.start(fg_ref, fg_out),
        local.start(gate_ref, gate_out),
    ]

    def scan_step(i, carry):
        new = []
        at = pl.ds(i, 8, stride=step_len)
        for n, (product, state) in enumerate(carry):
            a = a_ref[n, at, :]
            state = a * state + b_ref[n, at, :]
            product = product * a
            a_ref[n, at, :] = product
            b_ref[n, at, :] = state
            new.append((product, state))
        return tuple(new)

    start = tuple((jnp.ones((8, 128), F32), jnp.zeros((8, 128), F32)) for _ in range(blocks))
    ends = lax.fori_loop(0, step_len, scan_step, start)
    for n, (product, state) in enumerate(ends):
        end_p[8 * n : 8 * n + 8] = product
        end_s[8 * n : 8 * n + 8] = state
    p_all, s_all = segment_totals(end_p, end_s, blocks, range(8))
    total[:blocks] = p_all
    total[blocks:] = s_all
    copies = start_exchange(total, gathered, exchange_send, exchange_recv, n_seq)
    wait_all(copies)
    carry = jnp.zeros((blocks, 128), F32)
    for j in range(n_seq - 1):
        carry = jnp.where(j < s, gathered[j, blocks:] + gathered[j, :blocks] * carry, carry)
    for n in range(blocks):
        shifted[n, 0:1] = carry[n : n + 1]
    spread_carry(carry, carr, end_p, end_s, blocks, range(8))

    def finish(n, _):
        enter_state = carr[pl.ds(pl.multiple_of(n * 8, 8), 8)]
        for i in range(step_len):
            at = pl.ds(i, 8, stride=step_len)
            state = b_ref[n, at, :] + a_ref[n, at, :] * enter_state
            b_ref[n, at, :] = state
            shifted[n, pl.ds(i + 1, 8, stride=step_len), :] = state
        return 0

    lax.fori_loop(0, blocks, finish, 0)
    outs.append(local.start(shifted.at[:, pl.ds(0, rows)], before_out))

    lane = lax.broadcasted_iota(jnp.int32, (rows, 128), 1)
    for k in (3, 1, 2, 0):
        square = jnp.zeros((rows, 1), F32)
        for c, lanes in enumerate(lanes_of):
            state_b = b_ref[k * count + c].astype(BF16)
            state_ref[k, :, lanes] = state_b
            state = state_b.astype(F32)
            square = square + jnp.sum(state * state, -1, keepdims=True)
            gate = gate_ref[k, :, lanes]
            gain = gate_gain[:, pl.ds(pl.multiple_of(f * chans + c * 128, 128), 128)]
            raw_ref[k * rows : (k + 1) * rows, lanes] = (
                state * gain * gate * jax.nn.sigmoid(gate)
            ).astype(BF16)
        squares[...] = jnp.where(lane == groups[k], square, squares[...])
    square_copies = [
        links.start(squares, squares_in.at[i], (s, peer)) for i, peer in enumerate((fx, fy, fd))
    ]
    outs += [local.start(state_ref, state_out), local.start(raw_ref, raw_out)]
    cot_later = gather_forward(links, cot_own, cot_out, rows, s, fx, fy)
    weights[3].wait()

    def output_part(first, slots):
        at = slice(first * rows, (first + slots) * rows)

        def tile_of(n, _):
            cols = tile(n, 512)
            part[at, cols] = mm(raw_ref[at], wo[:, cols]).astype(BF16)
            return 0

        lax.fori_loop(0, width // 512, tile_of, 0)

    output_part(3, 1)
    far = reduce_start_far(links, part, from_x, from_y, rows, s, fx, fy)
    output_part(1, 2)
    near = reduce_start_near(links, part, from_x, from_y, rows, s, fx, fy)
    output_part(0, 1)
    passed = reduce_pass(links, far, part, from_x, from_y, pass_x, pass_y, rows, s, fx, fy)
    for copy in square_copies:
        copy.wait_recv()
    all_squares = (squares[...] + squares_in[0]) + (squares_in[1] + squares_in[2])
    scales = lax.rsqrt(all_squares / width + epsilon)
    for k in range(4):
        scale_out[k] = jnp.sum(jnp.where(lane == groups[k], scales, 0.0), -1, keepdims=True)
    for copy in near + passed:
        copy.wait_recv()
    half = rows // 2
    for first, one, other in ((0, from_x.at[1], from_y.at[2]), (half, from_y.at[1], from_x.at[2])):

        def sum_rows(i, _):
            here = pl.ds(pl.multiple_of(i * 16, 16), 16)
            at = pl.ds(pl.multiple_of(first + i * 16, 16), 16)
            mixed = part[at].astype(F32) + one[here].astype(F32) + other[here].astype(F32)
            value = hidden[at].astype(F32) + scale_out[0, at] * mixed
            middle[at] = value
            scale = lax.rsqrt(jnp.mean(value * value, -1, keepdims=True) + epsilon)
            two[at] = (value * scale * glu_gain[...]).astype(BF16)
            return 0

        lax.fori_loop(0, half // 16, sum_rows, 0)
    gather_middle(cot_own)
    gather_far(cot_later)
    sends_done(own, later, cot_own, cot_later, square_copies, far, near, passed)
    wait_all(swaps, outs)


def mixer_forward(lengths, hidden, cot, gains, table, weights, collective_id):
    n_seq = lax.axis_size("seq")
    rows, width = hidden.shape
    chans = weights[0].shape[1]
    blocks = 4 * chans // 128
    tokens = 4 * rows
    half = rows // 2
    shape = jax.ShapeDtypeStruct
    wide = shape((tokens, width), BF16)
    narrow = shape((4, rows, chans), BF16)
    return pl.pallas_call(
        functools.partial(mixer_kernel, n_seq),
        out_shape=(
            shape((2, tokens, width // 2), BF16),
            wide,
            narrow,
            narrow,
            shape((4, rows, chans), F32),
            narrow,
            shape((tokens, chans), BF16),
            shape((blocks, rows, 128), F32),
            shape((4, rows, 1), F32),
            shape((rows, width), F32),
            shape((rows, width), BF16),
        ),
        in_specs=[pl.BlockSpec(memory_space=pltpu.SMEM), VMEM, VMEM, VMEM, VMEM, VMEM, VMEM]
        + [ANY] * 4,
        out_specs=(ANY,) * 8 + (VMEM,) * 3,
        scratch_shapes=[
            pltpu.VMEM((width, 3 * chans), BF16),
            pltpu.VMEM((chans, width), BF16),
            pltpu.VMEM((tokens, width), BF16),
            pltpu.VMEM((2 * rows, 3 * chans), F32),
            pltpu.VMEM((4, rows, chans), BF16),
            pltpu.VMEM((4, rows, chans), BF16),
            pltpu.VMEM((4, rows, chans), F32),
            pltpu.VMEM((blocks, rows, 128), F32),
            pltpu.VMEM((blocks, rows, 128), F32),
            pltpu.VMEM((blocks, rows + 8, 128), F32),
            pltpu.VMEM((4, rows, 128), F32),
            pltpu.VMEM((8 * blocks, 128), F32),
            pltpu.VMEM((8 * blocks, 128), F32),
            pltpu.VMEM((8 * blocks, 128), F32),
            pltpu.VMEM((2 * blocks, 128), F32),
            pltpu.VMEM((n_seq, 2 * blocks, 128), F32),
            pltpu.VMEM((4, rows, chans), BF16),
            pltpu.VMEM((tokens, chans), BF16),
            pltpu.VMEM((rows, 128), F32),
            pltpu.VMEM((3, rows, 128), F32),
            pltpu.VMEM((tokens, width), BF16),
            pltpu.VMEM((3, half, width), BF16),
            pltpu.VMEM((3, half, width), BF16),
            pltpu.VMEM((half, width), BF16),
            pltpu.VMEM((half, width), BF16),
            pltpu.SemaphoreType.DMA((21 + n_seq // 2,)),
            pltpu.SemaphoreType.DMA((21 + n_seq // 2,)),
            pltpu.SemaphoreType.DMA((n_seq,)),
            pltpu.SemaphoreType.DMA((n_seq,)),
            pltpu.SemaphoreType.DMA((11 + n_seq // 2,)),
        ],
        compiler_params=params(collective_id),
        name="mixer_forward",
    )(lengths, hidden, cot, *gains, table, *weights)


def swap_columns(links, local, src, dst, n_seq, core, mate):
    part = src.shape[1] // n_seq
    copies, stays = [], []
    for z in range(n_seq // 2):
        to = pl.ds(z * part, part)
        theirs = pl.ds(pl.multiple_of((2 * z + 1 - core) * part, part), part)
        ours = pl.ds(pl.multiple_of((2 * z + core) * part, part), part)
        copies.append(links.start(src.at[:, theirs], dst.at[1, :, to], mate))
        stays.append(local.start(src.at[:, ours], dst.at[0, :, to]))
    return copies, stays


def swap_rows(links, local, src, dst, at, mate):
    copy = links.start(src.at[at], dst.at[1, at], mate)
    return copy, local.start(src.at[at], dst.at[0, at])


def glu_kernel(
    n_seq,
    two,
    cot_all,
    w_gate,
    w_up,
    w_down,
    two_half,
    cot_half,
    act_pair,
    gate_pair,
    up_pair,
    wv,
    wd,
    cot_ref,
    two_ref,
    d_act,
    stage,
    act,
    d_gate,
    d_up,
    send,
    recv,
    local_sems,
):
    rows = two.shape[0]
    units = w_gate.shape[1]
    s, f, fx, fy, fd = plane()
    core = s % 2
    mate = (s + 1 - 2 * core, f)
    links, local = Links(send, recv), Locals(local_sems)
    loads = [
        local.start(w_down, wd),
        local.start(cot_all, cot_ref),
        local.start(w_gate, wv.at[:, pl.ds(0, units)]),
        local.start(w_up, wv.at[:, pl.ds(units, units)]),
    ]
    two_ref[:rows] = two[...]
    enter([(s, fx), (s, fy), mate])
    own = gather_start(links, two_ref, two_ref, rows, s, fx, fy)
    loads[0].wait()
    loads[1].wait()
    swaps, stays = swap_columns(links, local, cot_ref, cot_half, n_seq, core, mate)

    def act_tile(n, _):
        cols = tile(n, 256)
        d_act[:, cols] = mm_t(cot_ref[...], wd[cols])
        return 0

    lax.fori_loop(0, units // 256, act_tile, 0)
    if units % 256:
        rest = slice(units // 256 * 256, units)
        d_act[:, rest] = mm_t(cot_ref[...], wd[rest])
    later = gather_forward(links, own, two_ref, rows, s, fx, fy)
    loads[2].wait()
    loads[3].wait()

    def slots(first, number):
        nonlocal swaps, stays
        base = first * rows

        def tile_of(n, _):
            cols = tile(n, 256)
            stage[: number * rows, cols] = mm(two_ref[base : base + number * rows], wv[:, cols])
            return 0

        lax.fori_loop(0, 2 * units // 256, tile_of, 0)

        def rows_of(i, _):
            at = pl.ds(pl.multiple_of(i * 16, 16), 16)
            to = pl.ds(pl.multiple_of(base + i * 16, 16), 16)
            gate, up = stage[at, :units], stage[at, units:]
            sigma = jax.nn.sigmoid(gate)
            silu = gate * sigma
            act[to] = (silu * up).astype(BF16)
            d = d_act[to]
            d_gate[to] = (d * up * silu_slope(gate, sigma)).astype(BF16)
            d_up[to] = (d * silu).astype(BF16)
            return 0

        lax.fori_loop(0, number * rows // 16, rows_of, 0)
        at = pl.ds(base, number * rows)
        for src, dst in ((act, act_pair), (d_gate, gate_pair), (d_up, up_pair)):
            sent, stayed = swap_rows(links, local, src, dst, at, mate)
            swaps, stays = swaps + [sent], stays + [stayed]

    slots(0, 1)
    gather_middle(own)
    slots(1, 2)
    gather_far(later)
    more, keeps = swap_columns(links, local, two_ref, two_half, n_seq, core, mate)
    slots(3, 1)
    sends_done(own, later)
    wait_all(swaps, stays, more, keeps)


def glu(two, cot_all, w_gate, w_up, w_down, collective_id):
    n_seq = lax.axis_size("seq")
    rows, width = two.shape
    units = w_gate.shape[1]
    tokens = 4 * rows
    shape = jax.ShapeDtypeStruct
    half = shape((2, tokens, width // 2), BF16)
    pair = shape((2, tokens, units), BF16)
    remote_count = 6 + n_seq + 9
    return pl.pallas_call(
        functools.partial(glu_kernel, n_seq),
        out_shape=(half, half, pair, pair, pair),
        in_specs=[VMEM] + [ANY] * 4,
        out_specs=(ANY,) * 5,
        scratch_shapes=[
            pltpu.VMEM((width, 2 * units), BF16),
            pltpu.VMEM((units, width), BF16),
            pltpu.VMEM((tokens, width), BF16),
            pltpu.VMEM((tokens, width), BF16),
            pltpu.VMEM((tokens, units), F32),
            pltpu.VMEM((2 * rows, 2 * units), F32),
            pltpu.VMEM((tokens, units), BF16),
            pltpu.VMEM((tokens, units), BF16),
            pltpu.VMEM((tokens, units), BF16),
            pltpu.SemaphoreType.DMA((remote_count,)),
            pltpu.SemaphoreType.DMA((remote_count,)),
            pltpu.SemaphoreType.DMA((4 + n_seq + 9,)),
        ],
        compiler_params=params(collective_id),
        name="glu",
    )(two, cot_all, w_gate, w_up, w_down)


class ZLine:
    def __init__(self, part, buf, sems, n_seq, width, lag, ahead):
        self.part, self.buf, self.width, self.lag, self.ahead = part, buf, width, lag, ahead
        self.send_up, self.recv_up, self.send_down, self.recv_down = sems
        self.s, self.f = lax.axis_index("seq"), lax.axis_index("fsdp")
        self.n_seq, self.nz = n_seq, n_seq // 2
        self.z = self.s // 2
        self.block = part.shape[0] // self.nz
        self.chunks = part.shape[1] // width
        self.steps = (self.nz - 1) * self.chunks
        self.calls = self.steps + lag * (self.nz - 2)

    def rows(self, t):
        return pl.ds(pl.multiple_of(t * self.block, self.block), self.block)

    def move(self, up, k, j):
        t = self.nz - 1 - k if up else k
        landing = t + 1 if up else t
        cols = tile(j, self.width)
        slot = k * self.chunks + j
        peer = lax.rem(self.s + (2 if up else self.n_seq - 2), self.n_seq)
        send, recv = (
            (self.send_up, self.recv_up) if up else (self.send_down, self.recv_down)
        )
        return remote(
            self.part.at[self.rows(t), cols],
            self.buf.at[self.rows(landing), cols],
            send.at[slot],
            recv.at[slot],
            (peer, self.f),
        )

    def feed(self, q):
        inside = q < self.steps
        q = jnp.minimum(q, self.steps - 1)
        k = q // self.chunks
        j = q - k * self.chunks

        @pl.when(inside & (self.z == 0))
        def _():
            self.move(True, k, j).start()

        @pl.when(inside & (self.z == self.nz - 1))
        def _():
            self.move(False, k, j).start()

    def feed_first(self):
        def step(q, _):
            self.feed(q)
            return 0

        lax.fori_loop(0, self.ahead, step, 0)

    def serve_one(self, up, q):
        z, nz = self.z, self.nz
        hops = z if up else nz - 1 - z
        q = q - self.lag * (hops - 1)
        inside = (hops >= 1) & (q >= 0) & (q < self.steps)
        q = jnp.clip(q, 0, self.steps - 1)
        k = q // self.chunks
        j = q - k * self.chunks
        left = nz - 1 - k - hops
        cols = tile(j, self.width)

        @pl.when(inside & (left >= 0))
        def _():
            self.move(up, k, j).wait_recv()

        @pl.when(inside & (left > 0))
        def _():
            t = nz - 1 - k if up else k
            landing = t + 1 if up else t
            own = self.part[self.rows(t), cols].astype(F32)
            came = self.buf[self.rows(landing), cols].astype(F32)
            self.part[self.rows(t), cols] = (own + came).astype(BF16)
            self.move(up, k, j).start()

    def serve(self, q):
        self.serve_one(True, q)
        self.serve_one(False, q)

    def serve_range(self, first, last):
        def step(q, _):
            self.feed(q + self.ahead)
            self.serve(q)
            return 0

        lax.fori_loop(first, last, step, 0)

    def finish(self, store, cols):
        own = self.part[self.rows(self.z), cols].astype(F32)
        above = self.buf[self.rows(self.z), cols].astype(F32)
        below = self.buf[self.rows(self.z + 1), cols].astype(F32)

        @pl.when(self.z == 0)
        def _():
            store(own + above)

        @pl.when((self.z > 0) & (self.z < self.nz - 1))
        def _():
            store(own + above + below)

        @pl.when(self.z == self.nz - 1)
        def _():
            store(own + below)

    def drain(self):
        for k in range(self.nz - 1):
            for up in (True, False):
                hops = self.z if up else self.nz - 1 - self.z

                @pl.when(hops < self.nz - 1 - k)
                def _():
                    def step(j, _):
                        self.move(up, k, j).wait_send()
                        return 0

                    lax.fori_loop(0, self.chunks, step, 0)


def line_sems(n_seq, columns, width):
    count = (n_seq // 2 - 1) * (columns // width)
    return [pltpu.SemaphoreType.DMA((count,)) for _ in range(4)]


def z_peers(n_seq):
    s = lax.axis_index("seq")
    f = lax.axis_index("fsdp")
    return [(lax.rem(s + 2 * k, n_seq), f) for k in range(1, n_seq // 2)]


def mm_tokens(left, right):
    return lax.dot_general(left, right, (((0,), (0,)), ((), ())), preferred_element_type=F32)


def down_kernel(
    n_seq,
    cot_half,
    act_pair,
    two_half,
    gate_pair,
    up_pair,
    w_gate,
    w_up,
    d_two,
    pair_part,
    down_out,
    cot_ref,
    act_ref,
    two_ref,
    gate_ref,
    up_ref,
    wg,
    wu,
    part,
    buf,
    rows_part,
    from_x,
    from_y,
    pass_x,
    pass_y,
    pair_ref,
    send,
    recv,
    local_sems,
    *line,
):
    rows, width = d_two.shape
    units = act_pair.shape[1]
    s, f, fx, fy, fd = plane()
    links, local = Links(send, recv), Locals(local_sems)
    moves = (
        (cot_half, cot_ref),
        (act_pair, act_ref),
        (w_gate, wg),
        (w_up, wu),
        (gate_pair, gate_ref),
        (up_pair, up_ref),
        (two_half, two_ref),
    )
    loads = [local.start(src, dst) for src, dst in moves]
    enter([(s, fx), (s, fy)] + z_peers(n_seq))
    z_sum = ZLine(part, buf, line, n_seq, 128, 3, 11)
    block = z_sum.block
    loads[0].wait()
    loads[1].wait()

    def down_tile(i, _):
        t = jnp.where(z_sum.z < z_sum.nz // 2, z_sum.nz - 1 - i, i)
        part[z_sum.rows(t)] = mm_tokens(cot_ref[:, tile(t, block)], act_ref[...]).astype(BF16)
        return 0

    down_tile(jnp.int32(0), 0)
    z_sum.feed_first()
    lax.fori_loop(1, z_sum.nz, down_tile, 0)
    for copy in loads[2:]:
        copy.wait()

    def two_part(first, slots, base):
        at = slice(first * rows, (first + slots) * rows)

        def tile_of(n, _):
            cols = tile(n, 512)
            total = mm_t(gate_ref[at], wg[cols]) + mm_t(up_ref[at], wu[cols])
            rows_part[at, cols] = total.astype(BF16)
            z_sum.feed(base + n + z_sum.ahead)
            z_sum.serve(base + n)
            return 0

        lax.fori_loop(0, width // 512, tile_of, 0)

    count = width // 512
    two_part(3, 1, 0)
    far = reduce_start_far(links, rows_part, from_x, from_y, rows, s, fx, fy)
    two_part(1, 2, count)
    near = reduce_start_near(links, rows_part, from_x, from_y, rows, s, fx, fy)
    two_part(0, 1, 2 * count)
    served = 3 * count

    def pair_tiles(right, first, base):
        def tile_of(t, _):
            pair_ref[z_sum.rows(t), pl.ds(first, units)] = mm_tokens(
                two_ref[:, tile(t, block)], right[...]
            ).astype(BF16)
            z_sum.serve_range(base + 2 * t, base + 2 * t + 2)
            return 0

        lax.fori_loop(0, z_sum.nz, tile_of, 0)

    pair_tiles(gate_ref, 0, served)
    served += 2 * z_sum.nz
    passed = reduce_pass(links, far, rows_part, from_x, from_y, pass_x, pass_y, rows, s, fx, fy)
    pair_tiles(up_ref, units, served)
    served += 2 * z_sum.nz
    stay = local.start(pair_ref, pair_part)
    for copy in near + passed:
        copy.wait_recv()
    half = rows // 2
    d_two[:half] = rows_part[:half].astype(F32) + from_x[1].astype(F32) + from_y[2].astype(F32)
    d_two[half:] = rows_part[half:rows].astype(F32) + from_y[1].astype(F32) + from_x[2].astype(F32)
    z_sum.serve_range(served, z_sum.calls)

    def out_tile(n, _):
        def store(value):
            down_out[tile(n, 128)] = value.T

        z_sum.finish(store, tile(n, 128))
        return 0

    lax.fori_loop(0, units // 128, out_tile, 0)
    z_sum.drain()
    sends_done(far, near, passed)
    stay.wait()


def down_sum(cot_half, act_pair, two_half, gate_pair, up_pair, w_gate, w_up, collective_id):
    n_seq = lax.axis_size("seq")
    tokens, units = act_pair.shape
    width = w_gate.shape[0]
    rows = tokens // 8
    half = (rows // 2, width)
    own = cot_half.shape[1]
    block = width // n_seq
    shape = jax.ShapeDtypeStruct
    return pl.pallas_call(
        functools.partial(down_kernel, n_seq),
        out_shape=(
            shape((rows, width), F32),
            shape((own, 2 * units), BF16),
            shape((units, block), F32),
        ),
        in_specs=[ANY] * 7,
        out_specs=(VMEM, ANY, VMEM),
        scratch_shapes=[
            pltpu.VMEM((tokens, own), BF16),
            pltpu.VMEM((tokens, units), BF16),
            pltpu.VMEM((tokens, own), BF16),
            pltpu.VMEM((tokens, units), BF16),
            pltpu.VMEM((tokens, units), BF16),
            pltpu.VMEM((width, units), BF16),
            pltpu.VMEM((width, units), BF16),
            pltpu.VMEM((own, units), BF16),
            pltpu.VMEM((own + block, units), BF16),
            pltpu.VMEM((tokens // 2, width), BF16),
            pltpu.VMEM((3,) + half, BF16),
            pltpu.VMEM((3,) + half, BF16),
            pltpu.VMEM(half, BF16),
            pltpu.VMEM(half, BF16),
            pltpu.VMEM((own, 2 * units), BF16),
            pltpu.SemaphoreType.DMA((6,)),
            pltpu.SemaphoreType.DMA((6,)),
            pltpu.SemaphoreType.DMA((8,)),
        ]
        + line_sems(n_seq, units, 128),
        compiler_params=params(collective_id),
        name="down_sum",
    )(cot_half, act_pair, two_half, gate_pair, up_pair, w_gate, w_up)


def pair_kernel(
    n_seq,
    lengths,
    hidden,
    cot,
    glu_gain,
    gate_gain,
    table,
    scale_g,
    d_two,
    middle,
    pair_part,
    w_out,
    w_in,
    w_fg,
    w_gt,
    gate_raw,
    state_b,
    out_raw,
    in_raw,
    fg_raw,
    before_in,
    normed_half,
    gate_grad,
    up_grad,
    mixer_part,
    d_normed,
    d_middle,
    d_glu_gain,
    d_gain,
    d_bounds,
    part,
    buf,
    wo,
    wv,
    mixed_all,
    mixed_mate,
    normed_ref,
    d_proj,
    out_gate,
    gate_ref,
    state_ref,
    raw_ref,
    in_ref,
    fg_ref,
    before,
    p_ref,
    q_ref,
    stage,
    rows_part,
    from_x,
    from_y,
    pass_x,
    pass_y,
    dots,
    keep_ref,
    end_p,
    end_s,
    carr,
    total,
    gathered,
    send,
    recv,
    exchange_send,
    exchange_recv,
    local_sems,
    tile_sems,
    *line,
):
    rows, width = hidden.shape
    chans = w_in.shape[1]
    units = gate_grad.shape[1]
    tokens = 4 * rows
    lanes_of = [slice(c, c + 128) for c in range(0, chans, 128)]
    count = len(lanes_of)
    blocks = 4 * count
    step_len = rows // 8
    s, f, fx, fy, fd = plane()
    groups = [f, fx, fy, fd]
    core = s % 2
    mate = (s + 1 - 2 * core, f)
    links, local = Links(send, recv), Locals(local_sems)
    rows_in = [local.start(d_two, d_middle), local.start(middle, d_normed)]
    loads = [local.start(pair_part, part), local.start(w_out, wo)]
    loads += [
        local.start(src, dst)
        for src, dst in (
            (gate_raw, gate_ref),
            (state_b, state_ref),
            (out_raw, raw_ref),
            (in_raw, in_ref),
            (fg_raw, fg_ref),
            (before_in, before),
        )
    ]
    weights = [
        local.start(w, wv.at[:, pl.ds(i * chans, chans)]) for i, w in enumerate((w_in, w_fg, w_gt))
    ]
    weights.append(local.start(normed_half, normed_ref))
    enter([(s, fx), (s, fy), (s, fd)] + seq_peers(n_seq))
    z_sum = ZLine(part, buf, line, n_seq, 256, 2, 11)
    loads[0].wait()
    z_sum.feed_first()
    served = 0

    def serve(number):
        nonlocal served
        z_sum.serve_range(served, served + number)
        served += number

    d_glu_gain[...] = jnp.zeros_like(d_glu_gain)
    wait_all(rows_in)

    def middle_rows(i, _):
        at = pl.ds(pl.multiple_of(i * 16, 16), 16)
        value, came = d_normed[at], d_middle[at]
        scale = lax.rsqrt(jnp.mean(value * value, -1, keepdims=True) + epsilon)
        scaled = glu_gain[...] * came
        mean = jnp.mean(scaled * value, -1, keepdims=True)
        grad = cot[at].astype(F32) + scale * scaled - value * (scale**3 * mean)
        d_middle[at] = grad
        grad_b = grad.astype(BF16)
        mixed_all[at] = grad_b
        own_dot = jnp.sum(
            grad_b.astype(F32) * (value - hidden[at].astype(F32)), -1, keepdims=True
        )
        dots[0, at] = jnp.broadcast_to(own_dot, (16, 128))
        d_glu_gain[...] += jnp.sum(came * value * scale, 0, keepdims=True)
        return 0

    lax.fori_loop(0, rows // 16, middle_rows, 0)
    own = gather_start(links, mixed_all, mixed_all, rows, s, fx, fy)
    dot_copies = [
        links.start(dots.at[0], dots.at[k], (s, peer)) for k, peer in ((1, fx), (2, fy), (3, fd))
    ]
    bound = bounds_slice(table, f * chans, chans)
    for k in range(4):
        keep_ref[k] = keep_rows(lengths, groups[k], s * rows, rows)
    d_gain[...] = jnp.zeros_like(d_gain)
    serve(1)
    for copy in loads[1:]:
        copy.wait()

    def out_rows(first, slots):
        stage[: slots * rows] = mm_t(mixed_all[first * rows : (first + slots) * rows], wo[...])
        for i in range(slots):
            k = first + i
            scale = scale_g[k]
            for c, lanes in enumerate(lanes_of):
                n = k * count + c
                gain = gate_gain[:, pl.ds(pl.multiple_of(f * chans + c * 128, 128), 128)]
                d_out = stage[i * rows : (i + 1) * rows, lanes]
                gate = gate_ref[k, :, lanes]
                sigma = jax.nn.sigmoid(gate)
                silu = gate * sigma
                state = state_ref[k, :, lanes].astype(F32)
                weighed = d_out * (state * scale)
                d_gain[:, lanes] += jnp.sum(weighed * silu, 0, keepdims=True)
                at = slice(k * rows, (k + 1) * rows)
                d_proj[at, 2 * chans + c * 128 : 2 * chans + (c + 1) * 128] = (
                    weighed * gain * silu_slope(gate, sigma)
                ).astype(BF16)
                out_gate[at, lanes] = (raw_ref[at, lanes].astype(F32) * scale).astype(BF16)
                d_state = scale * (d_out * gain * silu) - state * (
                    scale * scale * (dots[k] / width)
                )
                q_ref[n] = d_state.astype(BF16).astype(F32)
                edge = bound[:, lanes]
                forget = edge + (1.0 - edge) * jax.nn.sigmoid(fg_ref[k, :, lanes].astype(F32))
                p_ref[n] = forget * keep_ref[k]

    out_rows(0, 1)
    later = gather_forward(links, own, mixed_all, rows, s, fx, fy)
    serve(2)
    gather_middle(own)
    for copy in dot_copies:
        copy.wait_recv()
    out_rows(1, 2)
    serve(3)
    gather_far(later)
    out_rows(3, 1)
    serve(2)
    own_rows, mate_rows = pl.ds(0, tokens), pl.ds(tokens, tokens)
    last = pl.ds(2 * chans, chans)
    swaps = [
        links.start(out_gate.at[own_rows], out_gate.at[mate_rows], mate),
        links.start(d_proj.at[own_rows, last], d_proj.at[mate_rows, last], mate),
    ]
    wide = z_sum.block
    for t in range(n_seq // 2):
        theirs = pl.ds(pl.multiple_of((2 * t + 1 - core) * wide, wide), wide)
        swaps.append(
            links.start(mixed_all.at[:, theirs], mixed_mate.at[:, pl.ds(t * wide, wide)], mate)
        )

    def scan_step(i, carry):
        new = []
        at = pl.ds(step_len - 1 - i, 8, stride=step_len)
        for n, (product, message) in enumerate(carry):
            a = p_ref[n, at, :]
            acc = q_ref[n, at, :] + message
            p_ref[n, at, :] = product
            q_ref[n, at, :] = acc
            new.append((product * a, a * acc))
        return tuple(new)

    start = tuple((jnp.ones((8, 128), F32), jnp.zeros((8, 128), F32)) for _ in range(blocks))
    ends = lax.fori_loop(0, step_len, scan_step, start)
    for n, (product, message) in enumerate(ends):
        end_p[8 * n : 8 * n + 8] = product
        end_s[8 * n : 8 * n + 8] = message
    p_all, s_all = segment_totals(end_p, end_s, blocks, range(7, -1, -1))
    total[:blocks] = p_all
    total[blocks:] = s_all
    copies = start_exchange(total, gathered, exchange_send, exchange_recv, n_seq)
    serve(2)
    wait_all(copies)
    carry = jnp.zeros((blocks, 128), F32)
    for j in range(n_seq - 1, 0, -1):
        carry = jnp.where(j > s, gathered[j, blocks:] + gathered[j, :blocks] * carry, carry)
    spread_carry(carry, carr, end_p, end_s, blocks, range(7, -1, -1))

    def finish(n, _):
        enter_state = carr[pl.ds(pl.multiple_of(n * 8, 8), 8)]
        for i in range(step_len):
            at = pl.ds(i, 8, stride=step_len)
            q_ref[n, at, :] = q_ref[n, at, :] + p_ref[n, at, :] * enter_state
        return 0

    lax.fori_loop(0, blocks, finish, 0)
    d_bounds[...] = jnp.zeros_like(d_bounds)
    for k in range(4):
        at = slice(k * rows, (k + 1) * rows)
        for c, lanes in enumerate(lanes_of):
            acc = q_ref[k * count + c]
            edge = bound[:, lanes]
            sigma_f = jax.nn.sigmoid(fg_ref[k, :, lanes].astype(F32))
            forget = edge + (1.0 - edge) * sigma_f
            value = in_ref[k, :, lanes].astype(F32)
            sigma_i = jax.nn.sigmoid(value)
            d_forget = acc * (before[k * count + c] * keep_ref[k] - value * sigma_i)
            d_proj[at, lanes] = (acc * (1.0 - forget) * silu_slope(value, sigma_i)).astype(BF16)
            d_sigma = d_forget * (1.0 - sigma_f)
            d_proj[at, chans + c * 128 : chans + (c + 1) * 128] = (
                d_sigma * (1.0 - edge) * sigma_f
            ).astype(BF16)
            d_bounds[:, lanes] += jnp.sum(d_sigma, 0, keepdims=True)
    first = pl.ds(0, 2 * chans)
    swaps.append(links.start(d_proj.at[own_rows, first], d_proj.at[mate_rows, first], mate))
    serve(2)
    for copy in weights:
        copy.wait()

    def normed_part(first_slot, slots):
        at = slice(first_slot * rows, (first_slot + slots) * rows)

        def tile_of(n, _):
            cols = tile(n, 512)
            rows_part[at, cols] = mm_t(d_proj[at], wv[cols]).astype(BF16)
            return 0

        lax.fori_loop(0, width // 512, tile_of, 0)

    normed_part(3, 1)
    far = reduce_start_far(links, rows_part, from_x, from_y, rows, s, fx, fy)
    normed_part(1, 2)
    near = reduce_start_near(links, rows_part, from_x, from_y, rows, s, fx, fy)
    normed_part(0, 1)
    serve(3)
    for copy in swaps:
        copy.wait_recv()

    def tile_out(t):
        slot = lax.rem(t, 2)
        return pltpu.make_async_copy(
            wo.at[tile(slot, wide)], mixer_part.at[z_sum.rows(t)], tile_sems.at[slot]
        )

    def mixer_tile(t, _):
        @pl.when(t >= 2)
        def _():
            tile_out(t - 2).wait()

        at = tile(lax.rem(t, 2), wide)
        ours = mixed_all[:, tile(2 * t + core, wide)]
        out_part = mm_tokens(ours, out_gate[:tokens])
        out_part = out_part + mm_tokens(mixed_mate[:, tile(t, wide)], out_gate[tokens:])
        wo[at, :chans] = out_part.astype(BF16)
        wo[at, chans:] = mm_tokens(normed_ref[:, tile(t, wide)], d_proj[...]).astype(BF16)
        tile_out(t).start()
        return 0

    lax.fori_loop(0, 1, mixer_tile, 0)
    passed = reduce_pass(links, far, rows_part, from_x, from_y, pass_x, pass_y, rows, s, fx, fy)
    serve(1)
    lax.fori_loop(1, z_sum.nz, mixer_tile, 0)
    serve(2)
    for copy in near + passed:
        copy.wait_recv()
    half = rows // 2
    d_normed[:half] = rows_part[:half].astype(F32) + from_x[1].astype(F32) + from_y[2].astype(F32)
    d_normed[half:] = (
        rows_part[half:rows].astype(F32) + from_y[1].astype(F32) + from_x[2].astype(F32)
    )
    z_sum.serve_range(served, z_sum.calls)

    def out_tile(n, _):
        def store_gate(value):
            gate_grad[:, tile(n, 128)] = value

        def store_up(value):
            up_grad[:, tile(n, 128)] = value

        z_sum.finish(store_gate, tile(n, 128))
        z_sum.finish(store_up, pl.ds(pl.multiple_of(units + n * 128, 128), 128))
        return 0

    lax.fori_loop(0, units // 128, out_tile, 0)
    z_sum.drain()
    sends_done(own, later, dot_copies, swaps, far, near, passed)
    for t in range(z_sum.nz - 2, z_sum.nz):
        tile_out(jnp.int32(t)).wait()


def pair_sum(
    lengths, own_rows, gains, table, scale_g, float_rows, pair_part, weights, saved, normed_half, cid
):
    n_seq = lax.axis_size("seq")
    rows, width = own_rows[0].shape
    chans = weights[1].shape[1]
    own, columns = pair_part.shape
    tokens = 4 * rows
    blocks = 4 * chans // 128
    block = width // n_seq
    half = (rows // 2, width)
    shape = jax.ShapeDtypeStruct
    exchange = pltpu.SemaphoreType.DMA((n_seq,))
    count = 18 + n_seq // 2
    return pl.pallas_call(
        functools.partial(pair_kernel, n_seq),
        out_shape=(
            shape((block, columns // 2), F32),
            shape((block, columns // 2), F32),
            shape((own, 4 * chans), BF16),
            shape((rows, width), F32),
            shape((rows, width), F32),
            shape((1, width), F32),
            shape((1, chans), F32),
            shape((1, chans), F32),
        ),
        in_specs=[pl.BlockSpec(memory_space=pltpu.SMEM)] + [VMEM] * 6 + [ANY] * 14,
        out_specs=(VMEM, VMEM, ANY) + (VMEM,) * 5,
        scratch_shapes=[
            pltpu.VMEM((own, columns), BF16),
            pltpu.VMEM((own + block, columns), BF16),
            pltpu.VMEM((chans, width), BF16),
            pltpu.VMEM((width, 3 * chans), BF16),
            pltpu.VMEM((tokens, width), BF16),
            pltpu.VMEM((tokens, width // 2), BF16),
            pltpu.VMEM((2 * tokens, width // 2), BF16),
            pltpu.VMEM((2 * tokens, 3 * chans), BF16),
            pltpu.VMEM((2 * tokens, chans), BF16),
            pltpu.VMEM((4, rows, chans), F32),
            pltpu.VMEM((4, rows, chans), BF16),
            pltpu.VMEM((tokens, chans), BF16),
            pltpu.VMEM((4, rows, chans), BF16),
            pltpu.VMEM((4, rows, chans), BF16),
            pltpu.VMEM((blocks, rows, 128), F32),
            pltpu.VMEM((blocks, rows, 128), F32),
            pltpu.VMEM((blocks, rows, 128), F32),
            pltpu.VMEM((2 * rows, chans), F32),
            pltpu.VMEM((tokens, width), BF16),
            pltpu.VMEM((3,) + half, BF16),
            pltpu.VMEM((3,) + half, BF16),
            pltpu.VMEM(half, BF16),
            pltpu.VMEM(half, BF16),
            pltpu.VMEM((4, rows, 128), F32),
            pltpu.VMEM((4, rows, 128), F32),
            pltpu.VMEM((8 * blocks, 128), F32),
            pltpu.VMEM((8 * blocks, 128), F32),
            pltpu.VMEM((8 * blocks, 128), F32),
            pltpu.VMEM((2 * blocks, 128), F32),
            pltpu.VMEM((n_seq, 2 * blocks, 128), F32),
            pltpu.SemaphoreType.DMA((count,)),
            pltpu.SemaphoreType.DMA((count,)),
            exchange,
            exchange,
            pltpu.SemaphoreType.DMA((14,)),
            pltpu.SemaphoreType.DMA((2,)),
        ]
        + line_sems(n_seq, columns, 256),
        compiler_params=params(cid),
        name="pair_sum",
    )(
        lengths,
        *own_rows,
        *gains,
        table,
        scale_g,
        *float_rows,
        pair_part,
        *weights,
        *saved,
        normed_half,
    )


def final_kernel(
    n_seq,
    n_fsdp,
    d_normed,
    d_middle,
    hidden,
    middle,
    norm_gain,
    d_glu_gain,
    d_gain,
    d_bounds,
    table,
    mixer_part,
    act_pair,
    w_down,
    output,
    d_hidden,
    out_grad,
    in_grad,
    fg_grad,
    gt_grad,
    sums,
    d_table,
    part,
    buf,
    act,
    wd,
    rows_part,
    from_x,
    from_y,
    pass_x,
    pass_y,
    norm_sum,
    terms,
    over_seq,
    along_sum,
    over_fsdp,
    send,
    recv,
    local_sems,
    *line,
):
    rows, width = middle.shape
    chans = d_gain.shape[1]
    tokens = 4 * rows
    s, f, fx, fy, fd = plane()
    links, local = Links(send, recv), Locals(local_sems)
    loads = [
        local.start(mixer_part, part),
        local.start(act_pair.at[pl.ds(0, tokens)], act),
        local.start(w_down, wd),
    ]
    along = seq_peers(n_seq)
    across = [(s, fx), (s, fy), (s, fd)]
    enter(across + along)
    z_sum = ZLine(part, buf, line, n_seq, 256, 2, 11)
    loads[0].wait()
    z_sum.feed_first()
    served = 0

    def serve(number):
        nonlocal served
        z_sum.serve_range(served, served + number)
        served += number

    norm_sum[...] = jnp.zeros_like(norm_sum)

    def hidden_rows(i, _):
        at = pl.ds(pl.multiple_of(i * 16, 16), 16)
        value, came = hidden[at].astype(F32), d_normed[at]
        scale = lax.rsqrt(jnp.mean(value * value, -1, keepdims=True) + epsilon)
        scaled = norm_gain[...] * came
        mean = jnp.mean(scaled * value, -1, keepdims=True)
        d_hidden[at] = (d_middle[at] + scale * scaled - value * (scale**3 * mean)).astype(BF16)
        norm_sum[...] += jnp.sum(came * value * scale, 0, keepdims=True)
        return 0

    loads[1].wait()
    loads[2].wait()

    def glu_part(first, slots):
        at = slice(first * rows, (first + slots) * rows)

        def tile_of(n, _):
            cols = tile(n, 512)
            rows_part[at, cols] = mm(act[at], wd[:, cols]).astype(BF16)
            return 0

        lax.fori_loop(0, width // 512, tile_of, 0)

    glu_part(3, 1)
    far = reduce_start_far(links, rows_part, from_x, from_y, rows, s, fx, fy)
    glu_part(1, 2)
    near = reduce_start_near(links, rows_part, from_x, from_y, rows, s, fx, fy)
    glu_part(0, 1)
    serve(2)
    lax.fori_loop(0, rows // 16, hidden_rows, 0)
    half = width // 2
    terms[...] = jnp.zeros_like(terms)
    terms[0:1] = norm_sum[:, :half]
    terms[4:5] = norm_sum[:, half:]
    terms[1:2] = d_glu_gain[:, :half]
    terms[5:6] = d_glu_gain[:, half:]
    high = f * chans // half
    at = pl.ds(pl.multiple_of(f * chans - high * half, 128), chans)
    terms[pl.ds(2 + 4 * high, 1), at] = d_gain[...]
    terms[pl.ds(3 + 4 * high, 1), at] = d_bounds[...]
    seq_copies = [links.start(terms, over_seq.at[k], peer) for k, peer in enumerate(along)]
    serve(1)
    passed = reduce_pass(links, far, rows_part, from_x, from_y, pass_x, pass_y, rows, s, fx, fy)
    serve(2)
    total = terms[...]
    for k, copy in enumerate(seq_copies):
        copy.wait_recv()
        total = total + over_seq[k]
    along_sum[...] = total
    fsdp_copies = [links.start(along_sum, over_fsdp.at[k], peer) for k, peer in enumerate(across)]
    serve(2)
    for copy in near + passed:
        copy.wait_recv()
    middle_half = rows // 2
    for first, one, other in (
        (0, from_x.at[1], from_y.at[2]),
        (middle_half, from_y.at[1], from_x.at[2]),
    ):
        at = slice(first, first + middle_half)
        added = rows_part[at].astype(F32) + one[...].astype(F32) + other[...].astype(F32)
        output[at] = (middle[at] + added).astype(BF16)
    serve(1)
    total = along_sum[...]
    for k, copy in enumerate(fsdp_copies):
        copy.wait_recv()
        total = total + over_fsdp[k]
    for r in range(4):
        sums[r : r + 1, :half] = total[r : r + 1]
        sums[r : r + 1, half:] = total[r + 4 : r + 5]
    powers = jnp.exp(table[...] - jnp.max(table[...], 0, keepdims=True))
    soft = powers / jnp.sum(powers, 0, keepdims=True)
    row = lax.broadcasted_iota(jnp.int32, soft.shape, 0)
    chosen = jnp.where((row >= 1) & (row <= LAYER), 1.0, 0.0)
    bound = jnp.sum(soft * chosen, 0, keepdims=True)
    d_table[...] = soft * (chosen - bound) * sums[3:4]
    z_sum.serve_range(served, z_sum.calls)

    for m, grad in enumerate((out_grad, in_grad, fg_grad, gt_grad)):

        def out_tile(n, _):
            cols = tile(n, 128)

            def store(value):
                if m == 0:
                    grad[cols] = value.T
                else:
                    grad[:, cols] = value

            z_sum.finish(store, pl.ds(pl.multiple_of(m * chans + n * 128, 128), 128))
            return 0

        lax.fori_loop(0, chans // 128, out_tile, 0)
    z_sum.drain()
    sends_done(far, near, passed, seq_copies, fsdp_copies)


def final_sum(rows_in, gains, table, mixer_part, act_pair, w_down, cid):
    n_seq, n_fsdp = lax.axis_size("seq"), lax.axis_size("fsdp")
    rows, width = rows_in[0].shape
    own, columns = mixer_part.shape
    units = w_down.shape[0]
    chans = columns // 4
    tokens = 4 * rows
    block = width // n_seq
    half = (rows // 2, width)
    terms = (8, width // 2)
    shape = jax.ShapeDtypeStruct
    count = 6 + n_seq + n_fsdp - 2
    return pl.pallas_call(
        functools.partial(final_kernel, n_seq, n_fsdp),
        out_shape=(
            shape((rows, width), BF16),
            shape((rows, width), BF16),
            shape((chans, block), F32),
            shape((block, chans), F32),
            shape((block, chans), F32),
            shape((block, chans), F32),
            shape((4, width), F32),
            shape(table.shape, F32),
        ),
        in_specs=[VMEM] * 9 + [ANY] * 3,
        out_specs=(VMEM,) * 8,
        scratch_shapes=[
            pltpu.VMEM((own, columns), BF16),
            pltpu.VMEM((own + block, columns), BF16),
            pltpu.VMEM((tokens, units), BF16),
            pltpu.VMEM((units, width), BF16),
            pltpu.VMEM((tokens, width), BF16),
            pltpu.VMEM((3,) + half, BF16),
            pltpu.VMEM((3,) + half, BF16),
            pltpu.VMEM(half, BF16),
            pltpu.VMEM(half, BF16),
            pltpu.VMEM((1, width), F32),
            pltpu.VMEM(terms, F32),
            pltpu.VMEM((n_seq - 1,) + terms, F32),
            pltpu.VMEM(terms, F32),
            pltpu.VMEM((n_fsdp - 1,) + terms, F32),
            pltpu.SemaphoreType.DMA((count,)),
            pltpu.SemaphoreType.DMA((count,)),
            pltpu.SemaphoreType.DMA((3,)),
        ]
        + line_sems(n_seq, columns, 256),
        compiler_params=params(cid),
        name="final_sum",
    )(*rows_in, *gains, table, mixer_part, act_pair, w_down)


def hand_over_kernel(count, *refs):
    sources, targets = refs[:count], refs[count : 2 * count]
    kept, arrived, left = refs[2 * count : 3 * count], refs[3 * count], refs[3 * count + 1]
    loads = [copy_in(src, keep, arrived.at[i]) for i, (src, keep) in enumerate(zip(sources, kept))]
    stores = []
    for i, load in enumerate(loads):
        load.wait()
        stores.append(copy_in(kept[i], targets[i], left.at[i]))
    for store in stores:
        store.wait()


def hand_over(arrays):
    count = len(arrays)
    return pl.pallas_call(
        functools.partial(hand_over_kernel, count),
        out_shape=tuple(jax.ShapeDtypeStruct(x.shape, x.dtype) for x in arrays),
        in_specs=[ANY] * count,
        out_specs=(ANY,) * count,
        scratch_shapes=[pltpu.VMEM(x.shape, x.dtype) for x in arrays]
        + [pltpu.SemaphoreType.DMA((count,))] * 2,
        compiler_params=pltpu.CompilerParams(vmem_limit_bytes=56 << 20),
        name="hand_over",
    )(*arrays)


def plane_device(
    hidden,
    lengths,
    w_input,
    w_forget,
    w_gate_out,
    w_output,
    norm_gain,
    gate_gain,
    glu_gain,
    lower_table,
    w_glu_gate,
    w_glu_up,
    w_glu_down,
    cotangent,
):
    hidden, cotangent = hidden[0], cotangent[0]
    tokens = 4 * hidden.shape[0]
    gains = (norm_gain[None], gate_gain[None], glu_gain[None])
    (
        normed_half,
        cot_all,
        in_raw,
        fg_raw,
        gate_raw,
        state_b,
        out_raw,
        before,
        scale_g,
        middle,
        normed_two,
    ) = mixer_forward(
        lengths,
        hidden,
        cotangent,
        gains,
        lower_table,
        (w_input, w_forget, w_gate_out, w_output),
        0,
    )
    two_half, cot_half, act_pair, gate_pair, up_pair = glu(
        normed_two, cot_all, w_glu_gate, w_glu_up, w_glu_down, 1
    )
    d_normed_two, pair_part, down_grad = down_sum(
        *(x.reshape(2 * tokens, -1) for x in (cot_half, act_pair, two_half, gate_pair, up_pair)),
        w_glu_gate,
        w_glu_up,
        2,
    )
    gate_grad, up_grad, mixer_part, d_normed, d_middle, d_glu_gain, d_gain, d_bounds = pair_sum(
        lengths,
        (hidden, cotangent),
        (gains[2], gains[1]),
        lower_table,
        scale_g,
        (d_normed_two, middle),
        pair_part,
        (w_output, w_input, w_forget, w_gate_out),
        (gate_raw, state_b, out_raw, in_raw, fg_raw, before),
        normed_half.reshape(2 * tokens, -1),
        3,
    )
    output, d_hidden, out_grad, in_grad, fg_grad, gt_grad, sums, d_table = final_sum(
        (d_normed, d_middle, hidden, middle),
        (gains[0], d_glu_gain, d_gain, d_bounds),
        lower_table,
        mixer_part,
        act_pair.reshape(2 * tokens, -1),
        w_glu_down,
        4,
    )
    (
        down_grad,
        gate_grad,
        up_grad,
        output,
        d_hidden,
        out_grad,
        in_grad,
        fg_grad,
        gt_grad,
        d_table,
    ) = hand_over(
        (
            down_grad,
            gate_grad,
            up_grad,
            output,
            d_hidden,
            out_grad,
            in_grad,
            fg_grad,
            gt_grad,
            d_table,
        )
    )
    return (
        output[None],
        d_hidden[None],
        in_grad,
        fg_grad,
        gt_grad,
        out_grad,
        sums[0],
        sums[2],
        sums[1],
        d_table,
        gate_grad,
        up_grad,
        down_grad,
    )


def fits_plane(mesh):
    return mesh.shape["fsdp"] == 4 and mesh.shape["seq"] % 2 == 0


def solution(mesh):
    rows_spec = P("fsdp", "seq", None)
    columns = P(None, "fsdp")
    placed = (
        rows_spec,
        P(),
        columns,
        columns,
        columns,
        P("fsdp", None),
        P(),
        P(),
        P(),
        P(),
        columns,
        columns,
        P("fsdp", None),
        rows_spec,
    )
    by_rows, by_columns = P("seq", "fsdp"), P("fsdp", "seq")
    return jax.shard_map(
        plane_device if fits_plane(mesh) else per_device,
        mesh=mesh,
        in_specs=placed,
        out_specs=(
            rows_spec,
            rows_spec,
            by_rows,
            by_rows,
            by_rows,
            by_columns,
            P(),
            P(),
            P(),
            P(),
            by_rows,
            by_rows,
            by_columns,
        ),
        check_vma=False,
    )
```

```python
import functools

import jax
import jax.numpy as jnp
from jax import lax
from jax.experimental import pallas as pl
from jax.experimental.pallas import tpu as pltpu
from jax.sharding import PartitionSpec as P

LAYER = 12
MESH = pl.DeviceIdType.MESH
F32 = jnp.float32
BF16 = jnp.bfloat16

epsilon = 1e-06

VMEM = pl.BlockSpec(memory_space=pltpu.VMEM)
ANY = pl.BlockSpec(memory_space=pl.ANY)


def lower_bound(table):
    soft = jax.nn.softmax(table, axis=0)
    totals = jnp.cumsum(soft, axis=0)
    return totals[LAYER] - totals[0]


def silu_slope(value, sigma):
    return sigma * (1.0 + value * (1.0 - sigma))


def params(collective_id):
    return pltpu.CompilerParams(
        collective_id=collective_id, has_side_effects=True, vmem_limit_bytes=56 << 20
    )


def round_up(value, unit):
    return -(-value // unit) * unit


def plane():
    s = lax.axis_index("seq")
    f = lax.axis_index("fsdp")
    y, x = f // 2, f % 2
    fx = y * 2 + (1 - x)
    fy = (1 - y) * 2 + x
    fd = (1 - y) * 2 + (1 - x)
    return s, f, fx, fy, fd


def enter(devices):
    barrier = pltpu.get_barrier_semaphore()
    for device in devices:
        pl.semaphore_signal(barrier, inc=1, device_id=device, device_id_type=MESH)
    pl.semaphore_wait(barrier, len(devices))


def remote(src, dst, send, recv, device):
    return pltpu.make_async_remote_copy(
        src_ref=src,
        dst_ref=dst,
        send_sem=send,
        recv_sem=recv,
        device_id=device,
        device_id_type=MESH,
    )


def gather(x, small, collective_id):
    return lax.all_gather(x, "fsdp"), lax.all_gather(small, "fsdp")


def reduce_rows(p, small, collective_id):
    total = lax.psum_scatter(p, "fsdp", scatter_dimension=0, tiled=True)[0]
    return total.astype(F32), lax.psum(small, "fsdp")


def start_exchange(total, gathered, send, recv, n_seq):
    s = lax.axis_index("seq")
    f = lax.axis_index("fsdp")
    copies = []
    for k in range(1, n_seq):
        peer = lax.rem(s + k, n_seq)
        copy = remote(total, gathered.at[s], send.at[k], recv.at[k], (peer, f))
        copy.start()
        copies.append(copy)
    gathered[pl.ds(s, 1)] = total[...][None]
    return copies


def seq_peers(n_seq):
    s = lax.axis_index("seq")
    f = lax.axis_index("fsdp")
    return [(lax.rem(s + k, n_seq), f) for k in range(1, n_seq)]


def lane_blocks(groups, chans):
    return [(g, slice(c, c + 128)) for g in range(groups) for c in range(0, chans, 128)]


def forward_scan_kernel(
    n_seq, in_raw, forget_raw, bounds, keep, state_b, before, a_ref, b_ref, total, gathered, send, recv
):
    groups, rows, chans = in_raw.shape
    part = rows // 8
    blocks = lane_blocks(groups, chans)
    s = lax.axis_index("seq")
    barrier = pltpu.get_barrier_semaphore()
    for peer in seq_peers(n_seq):
        pl.semaphore_signal(barrier, inc=1, device_id=peer, device_id_type=MESH)
    for n, (g, lanes) in enumerate(blocks):
        bound = bounds[:, lanes]
        forget = bound + (1.0 - bound) * jax.nn.sigmoid(forget_raw[g, :, lanes].astype(F32))
        value = in_raw[g, :, lanes].astype(F32)
        a_ref[n] = forget * keep[g]
        b_ref[n] = value * jax.nn.sigmoid(value) * (1.0 - forget)

    def step(i, carry):
        new = []
        at = pl.ds(i, 8, stride=part)
        for n, (product, state) in enumerate(carry):
            a = a_ref[n, at, :]
            state = a * state + b_ref[n, at, :]
            product = product * a
            a_ref[n, at, :] = product
            b_ref[n, at, :] = state
            new.append((product, state))
        return tuple(new)

    start = tuple((jnp.ones((8, 128), F32), jnp.zeros((8, 128), F32)) for _ in blocks)
    ends = lax.fori_loop(0, part, step, start)
    for n, (product, state) in enumerate(ends):
        p_all, s_all = product[0:1], state[0:1]
        for j in range(1, 8):
            p_all, s_all = p_all * product[j : j + 1], state[j : j + 1] + product[j : j + 1] * s_all
        total[2 * n : 2 * n + 1] = p_all
        total[2 * n + 1 : 2 * n + 2] = s_all
    pl.semaphore_wait(barrier, n_seq - 1)
    copies = start_exchange(total, gathered, send, recv, n_seq)
    for copy in copies:
        copy.wait()
    for n, (g, lanes) in enumerate(blocks):
        carry = jnp.zeros((1, 128), F32)
        for j in range(n_seq - 1):
            p_j = gathered[j, 2 * n : 2 * n + 1]
            s_j = gathered[j, 2 * n + 1 : 2 * n + 2]
            carry = jnp.where(j < s, s_j + p_j * carry, carry)
        before[g, 0:1, lanes] = carry
        product, state = ends[n]
        carries = [carry]
        for j in range(7):
            carries.append(state[j : j + 1] + product[j : j + 1] * carries[-1])
        for j in range(8):
            at = slice(j * part, (j + 1) * part)
            b_ref[n, at] = b_ref[n, at] + a_ref[n, at] * carries[j]
        state_b[g, :, lanes] = b_ref[n].astype(BF16)
        before[g, 1:rows, lanes] = b_ref[n, 0 : rows - 1]


def forward_scan(in_raw, forget_raw, bounds, keep, collective_id):
    n_seq = lax.axis_size("seq")
    groups, rows, chans = in_raw.shape
    blocks = groups * chans // 128
    return pl.pallas_call(
        functools.partial(forward_scan_kernel, n_seq),
        out_shape=(
            jax.ShapeDtypeStruct(in_raw.shape, BF16),
            jax.ShapeDtypeStruct(in_raw.shape, F32),
        ),
        in_specs=[VMEM] * 4,
        out_specs=(VMEM, VMEM),
        scratch_shapes=[
            pltpu.VMEM((blocks, rows, 128), F32),
            pltpu.VMEM((blocks, rows, 128), F32),
            pltpu.VMEM((2 * blocks, 128), F32),
            pltpu.VMEM((n_seq, 2 * blocks, 128), F32),
            pltpu.SemaphoreType.DMA((n_seq,)),
            pltpu.SemaphoreType.DMA((n_seq,)),
        ],
        compiler_params=params(collective_id),
        name="forward_scan",
    )(in_raw, forget_raw, bounds, keep)


def backward_scan_kernel(
    n_seq,
    d_state,
    in_raw,
    forget_raw,
    before,
    bounds,
    keep,
    d_in,
    d_forget_raw,
    d_bounds,
    p_ref,
    q_ref,
    total,
    gathered,
    send,
    recv,
):
    groups, rows, chans = in_raw.shape
    part = rows // 8
    blocks = lane_blocks(groups, chans)
    s = lax.axis_index("seq")
    barrier = pltpu.get_barrier_semaphore()
    for peer in seq_peers(n_seq):
        pl.semaphore_signal(barrier, inc=1, device_id=peer, device_id_type=MESH)
    for n, (g, lanes) in enumerate(blocks):
        bound = bounds[:, lanes]
        forget = bound + (1.0 - bound) * jax.nn.sigmoid(forget_raw[g, :, lanes].astype(F32))
        p_ref[n] = forget * keep[g]
        q_ref[n] = d_state[g, :, lanes].astype(F32)

    def step(i, carry):
        new = []
        at = pl.ds(part - 1 - i, 8, stride=part)
        for n, (product, message) in enumerate(carry):
            a = p_ref[n, at, :]
            acc = q_ref[n, at, :] + message
            p_ref[n, at, :] = product
            q_ref[n, at, :] = acc
            new.append((product * a, a * acc))
        return tuple(new)

    start = tuple((jnp.ones((8, 128), F32), jnp.zeros((8, 128), F32)) for _ in blocks)
    ends = lax.fori_loop(0, part, step, start)
    for n, (product, message) in enumerate(ends):
        p_all, m_all = product[7:8], message[7:8]
        for j in range(6, -1, -1):
            p_all, m_all = p_all * product[j : j + 1], message[j : j + 1] + product[j : j + 1] * m_all
        total[2 * n : 2 * n + 1] = p_all
        total[2 * n + 1 : 2 * n + 2] = m_all
    pl.semaphore_wait(barrier, n_seq - 1)
    copies = start_exchange(total, gathered, send, recv, n_seq)
    for copy in copies:
        copy.wait()
    d_bounds[...] = jnp.zeros((1, chans), F32)
    for n, (g, lanes) in enumerate(blocks):
        carry = jnp.zeros((1, 128), F32)
        for j in range(n_seq - 1, 0, -1):
            p_j = gathered[j, 2 * n : 2 * n + 1]
            m_j = gathered[j, 2 * n + 1 : 2 * n + 2]
            carry = jnp.where(j > s, m_j + p_j * carry, carry)
        product, message = ends[n]
        carries = [carry]
        for j in range(7, 0, -1):
            carries.append(message[j : j + 1] + product[j : j + 1] * carries[-1])
        carries = carries[::-1]
        for j in range(8):
            at = slice(j * part, (j + 1) * part)
            q_ref[n, at] = q_ref[n, at] + p_ref[n, at] * carries[j]
        acc = q_ref[n]
        bound = bounds[:, lanes]
        sigma_f = jax.nn.sigmoid(forget_raw[g, :, lanes].astype(F32))
        forget = bound + (1.0 - bound) * sigma_f
        value = in_raw[g, :, lanes].astype(F32)
        sigma_i = jax.nn.sigmoid(value)
        d_forget = acc * (before[g, :, lanes] * keep[g] - value * sigma_i)
        d_in[g, :, lanes] = (acc * (1.0 - forget) * silu_slope(value, sigma_i)).astype(BF16)
        d_sigma = d_forget * (1.0 - sigma_f)
        d_forget_raw[g, :, lanes] = (d_sigma * (1.0 - bound) * sigma_f).astype(BF16)
        d_bounds[:, lanes] += jnp.sum(d_sigma, 0, keepdims=True)


def backward_scan(d_state, in_raw, forget_raw, before, bounds, keep, collective_id):
    n_seq = lax.axis_size("seq")
    groups, rows, chans = in_raw.shape
    blocks = groups * chans // 128
    return pl.pallas_call(
        functools.partial(backward_scan_kernel, n_seq),
        out_shape=(
            jax.ShapeDtypeStruct(in_raw.shape, BF16),
            jax.ShapeDtypeStruct(in_raw.shape, BF16),
            jax.ShapeDtypeStruct((1, chans), F32),
        ),
        in_specs=[VMEM] * 6,
        out_specs=(VMEM, VMEM, VMEM),
        scratch_shapes=[
            pltpu.VMEM((blocks, rows, 128), F32),
            pltpu.VMEM((blocks, rows, 128), F32),
            pltpu.VMEM((2 * blocks, 128), F32),
            pltpu.VMEM((n_seq, 2 * blocks, 128), F32),
            pltpu.SemaphoreType.DMA((n_seq,)),
            pltpu.SemaphoreType.DMA((n_seq,)),
        ],
        compiler_params=params(collective_id),
        name="backward_scan",
    )(d_state, in_raw, forget_raw, before, bounds, keep)


def sum_all_kernel(n_seq, n_fsdp, x, out, middle, over_seq, over_fsdp, send, recv):
    s = lax.axis_index("seq")
    f = lax.axis_index("fsdp")
    along = [(lax.rem(s + k, n_seq), f) for k in range(1, n_seq)]
    across = [(s, lax.rem(f + k, n_fsdp)) for k in range(1, n_fsdp)]
    enter(along + across)
    copies = []
    for k, peer in enumerate(along):
        copy = remote(x, over_seq.at[k], send.at[k], recv.at[k], peer)
        copy.start()
        copies.append(copy)
    total = x[...]
    for k, copy in enumerate(copies):
        copy.wait_recv()
        total = total + over_seq[k]
    middle[...] = total
    later = []
    for k, peer in enumerate(across):
        slot = n_seq - 1 + k
        copy = remote(middle, over_fsdp.at[k], send.at[slot], recv.at[slot], peer)
        copy.start()
        later.append(copy)
    for k, copy in enumerate(later):
        copy.wait_recv()
        total = total + over_fsdp[k]
    out[...] = total
    for copy in copies + later:
        copy.wait_send()


def sum_all(x, collective_id):
    n_seq, n_fsdp = lax.axis_size("seq"), lax.axis_size("fsdp")
    count = n_seq + n_fsdp - 2
    return pl.pallas_call(
        functools.partial(sum_all_kernel, n_seq, n_fsdp),
        out_shape=jax.ShapeDtypeStruct(x.shape, F32),
        in_specs=[VMEM],
        out_specs=VMEM,
        scratch_shapes=[
            pltpu.VMEM(x.shape, F32),
            pltpu.VMEM((n_seq - 1,) + x.shape, F32),
            pltpu.VMEM((n_fsdp - 1,) + x.shape, F32),
            pltpu.SemaphoreType.DMA((count,)),
            pltpu.SemaphoreType.DMA((count,)),
        ],
        compiler_params=params(collective_id),
        name="sum_all",
    )(x)


def sum_over_seq(part):
    return lax.psum_scatter(part.astype(BF16), "seq", scatter_dimension=0, tiled=True).astype(F32)


def per_device(
    hidden,
    lengths,
    w_input,
    w_forget,
    w_gate_out,
    w_output,
    norm_gain,
    gate_gain,
    glu_gain,
    lower_table,
    w_glu_gate,
    w_glu_up,
    w_glu_down,
    cotangent,
):
    seq_index = lax.axis_index("seq")
    fsdp_index = lax.axis_index("fsdp")
    groups = lax.axis_size("fsdp")
    _, rows, width = hidden.shape
    chans = w_input.shape[1]
    units = w_glu_gate.shape[1]
    tokens = groups * rows
    small_shape = (round_up(groups, 8), round_up(rows, 128))

    def to_small(value):
        return jnp.pad(
            value, ((0, small_shape[0] - value.shape[0]), (0, small_shape[1] - value.shape[1]))
        )

    def dot(left, right):
        return jnp.dot(left, right, preferred_element_type=F32)

    def dot_t(left, right):
        return lax.dot_general(left, right, (((1,), (1,)), ((), ())), preferred_element_type=F32)

    def over_tokens(left, right):
        return lax.dot_general(left, right, (((0,), (0,)), ((), ())), preferred_element_type=F32)

    cotangent_all = lax.all_gather(cotangent[0], "fsdp").reshape(tokens, width)

    hidden_f = hidden[0].astype(F32)
    scale_one = lax.rsqrt(jnp.mean(hidden_f * hidden_f, -1, keepdims=True) + epsilon)
    normed = (hidden_f * scale_one * norm_gain).astype(BF16)
    normed_all, _ = gather(normed, jnp.zeros((8, 128), F32), 0)
    normed_all = normed_all.reshape(tokens, width)
    in_raw = dot(normed_all, w_input).astype(BF16).reshape(groups, rows, chans)
    forget_raw = dot(normed_all, w_forget).astype(BF16).reshape(groups, rows, chans)
    gate_raw = dot(normed_all, w_gate_out)

    bounds_full = lower_bound(lower_table)
    bounds = lax.dynamic_slice_in_dim(bounds_full, fsdp_index * chans, chans)[None]
    seq_starts = jnp.cumsum(lengths, axis=1) - lengths
    places = seq_index * rows + jnp.arange(rows, dtype=jnp.int32)
    starts = jnp.any(places[None, :, None] == seq_starts[:, None, :], axis=-1)
    keep = jnp.where(starts, 0.0, 1.0).astype(F32)[:, :, None]
    state_b, before = forward_scan(in_raw, forget_raw, bounds, keep, 1)

    state_f = state_b.astype(F32).reshape(tokens, chans)
    gain_slice = lax.dynamic_slice_in_dim(gate_gain, fsdp_index * chans, chans)
    sigma_g = jax.nn.sigmoid(gate_raw)
    silu_gate = gate_raw * sigma_g
    out_raw = (state_f * gain_slice * silu_gate).astype(BF16)
    squares = jnp.sum(state_f * state_f, -1).reshape(groups, rows)
    mixed_part = dot(out_raw, w_output).astype(BF16).reshape(groups, rows, width)
    mixed_raw, square_sum = reduce_rows(mixed_part, to_small(squares), 2)
    state_scale = lax.rsqrt(square_sum[:groups, :rows] / width + epsilon)
    own_scale = lax.dynamic_slice_in_dim(state_scale, fsdp_index, 1, 0)[0][:, None]
    scale_g = state_scale.reshape(tokens, 1)
    middle = hidden_f + own_scale * mixed_raw
    scale_two = lax.rsqrt(jnp.mean(middle * middle, -1, keepdims=True) + epsilon)
    normed_two = (middle * scale_two * glu_gain).astype(BF16)
    normed_two_all, _ = gather(normed_two, jnp.zeros((8, 128), F32), 3)
    normed_two_all = normed_two_all.reshape(tokens, width)

    gate_val = dot(normed_two_all, w_glu_gate)
    up_val = dot(normed_two_all, w_glu_up)
    sigma_u = jax.nn.sigmoid(gate_val)
    silu_u = gate_val * sigma_u
    activity = (silu_u * up_val).astype(BF16)
    down_grad = sum_over_seq(over_tokens(cotangent_all, activity))
    d_act = dot_t(cotangent_all, w_glu_down)
    d_gate = (d_act * up_val * silu_slope(gate_val, sigma_u)).astype(BF16)
    d_up = (d_act * silu_u).astype(BF16)
    pair_grad = sum_over_seq(
        jnp.concatenate(
            [
                over_tokens(normed_two_all, d_gate).astype(BF16),
                over_tokens(normed_two_all, d_up).astype(BF16),
            ],
            1,
        )
    )
    d_two_part = (dot_t(d_gate, w_glu_gate) + dot_t(d_up, w_glu_up)).astype(BF16)
    no_small = jnp.zeros((8, 128), F32)
    d_normed_two, _ = reduce_rows(d_two_part.reshape(groups, rows, width), no_small, 4)
    glu_part = dot(activity, w_glu_down).astype(BF16).reshape(groups, rows, width)
    glu_result = lax.psum_scatter(glu_part, "fsdp", scatter_dimension=0, tiled=True)[0]
    output = (middle + glu_result.astype(F32)).astype(BF16)[None]

    cotangent_f = cotangent[0].astype(F32)
    scaled_two = glu_gain * d_normed_two
    d_middle = (
        cotangent_f
        + scale_two * scaled_two
        - middle * scale_two**3 * jnp.mean(scaled_two * middle, -1, keepdims=True)
    )
    d_glu_gain = jnp.sum(d_normed_two * middle * scale_two, 0)
    d_mixed = d_middle.astype(BF16)
    own_dot = jnp.sum(d_mixed.astype(F32) * mixed_raw, -1)[None]
    d_mixed_all, dots = gather(d_mixed, to_small(own_dot), 5)
    d_mixed_all = d_mixed_all.reshape(tokens, width)
    dot_rows = dots[:, 0, :rows].reshape(tokens, 1)

    d_out = dot_t(d_mixed_all, w_output)
    scaled_state = state_f * scale_g
    d_gain_slice = jnp.sum(d_out * scaled_state * silu_gate, 0)
    d_scaled = d_out * gain_slice * silu_gate
    d_gate_raw = (d_out * scaled_state * gain_slice * silu_slope(gate_raw, sigma_g)).astype(BF16)
    d_state = scale_g * d_scaled - state_f * (scale_g**3 * (dot_rows / width))
    d_state = d_state.astype(BF16).reshape(groups, rows, chans)
    d_in, d_forget_raw, d_bounds = backward_scan(
        d_state, in_raw, forget_raw, before, bounds, keep, 6
    )
    d_in = d_in.reshape(tokens, chans)
    d_forget_raw = d_forget_raw.reshape(tokens, chans)

    d_normed_part = dot_t(d_in, w_input) + dot_t(d_forget_raw, w_forget)
    d_normed_part = (d_normed_part + dot_t(d_gate_raw, w_gate_out)).astype(BF16)
    out_gate = (out_raw.astype(F32) * scale_g).astype(BF16)
    mixer_grad = sum_over_seq(
        jnp.concatenate(
            [
                over_tokens(d_mixed_all, out_gate).astype(BF16),
                over_tokens(normed_all, d_in).astype(BF16),
                over_tokens(normed_all, d_forget_raw).astype(BF16),
                over_tokens(normed_all, d_gate_raw).astype(BF16),
            ],
            1,
        )
    )
    d_normed, _ = reduce_rows(d_normed_part.reshape(groups, rows, width), no_small, 7)
    scaled_one = norm_gain * d_normed
    d_hidden = (
        d_middle
        + scale_one * scaled_one
        - hidden_f * scale_one**3 * jnp.mean(scaled_one * hidden_f, -1, keepdims=True)
    )
    d_norm_gain = jnp.sum(d_normed * hidden_f * scale_one, 0)
    d_gain_full = lax.dynamic_update_slice(
        jnp.zeros((width,), F32), d_gain_slice, (fsdp_index * chans,)
    )
    d_bounds_full = lax.dynamic_update_slice(
        jnp.zeros((width,), F32), d_bounds[0], (fsdp_index * chans,)
    )
    sums = jnp.stack([d_norm_gain, d_glu_gain, d_gain_full, d_bounds_full])
    totals = sum_all(sums.reshape(8, width // 2), 8).reshape(4, width)
    _, bounds_pull = jax.vjp(lower_bound, lower_table)
    d_table = bounds_pull(totals[3])[0]
    return (
        output,
        d_hidden.astype(BF16)[None],
        mixer_grad[:, chans : 2 * chans],
        mixer_grad[:, 2 * chans : 3 * chans],
        mixer_grad[:, 3 * chans :],
        mixer_grad[:, :chans].T,
        totals[0],
        totals[2],
        totals[1],
        d_table,
        pair_grad[:, :units],
        pair_grad[:, units:],
        down_grad.T,
    )


def copy_in(src, dst, sem):
    copy = pltpu.make_async_copy(src, dst, sem)
    copy.start()
    return copy


class Links:
    def __init__(self, send, recv):
        self.send, self.recv, self.used = send, recv, 0

    def start(self, src, dst, device):
        copy = remote(src, dst, self.send.at[self.used], self.recv.at[self.used], device)
        self.used += 1
        copy.start()
        return copy


class Locals:
    def __init__(self, sems):
        self.sems, self.used = sems, 0

    def start(self, src, dst):
        copy = copy_in(src, dst, self.sems.at[self.used])
        self.used += 1
        return copy


def row_slots(rows):
    half = rows // 2
    top = [pl.ds(k * rows, half) for k in range(4)]
    bottom = [pl.ds(k * rows + half, half) for k in range(4)]
    return top, bottom


def gather_start(links, src, dst, rows, s, fx, fy):
    half = rows // 2
    top, bottom = row_slots(rows)
    here = (pl.ds(0, half), pl.ds(half, half))
    return [
        links.start(src.at[here[0]], dst.at[top[1]], (s, fx)),
        links.start(src.at[here[1]], dst.at[bottom[2]], (s, fy)),
        links.start(src.at[here[1]], dst.at[bottom[1]], (s, fx)),
        links.start(src.at[here[0]], dst.at[top[2]], (s, fy)),
    ]


def gather_forward(links, own, dst, rows, s, fx, fy):
    top, bottom = row_slots(rows)
    own[0].wait_recv()
    on_y = links.start(dst.at[top[1]], dst.at[top[3]], (s, fy))
    own[1].wait_recv()
    on_x = links.start(dst.at[bottom[2]], dst.at[bottom[3]], (s, fx))
    return [on_y, on_x]


def gather_middle(own):
    own[2].wait_recv()
    own[3].wait_recv()


def gather_far(later):
    for copy in later:
        copy.wait_recv()


def sends_done(*lists):
    for copies in lists:
        for copy in copies:
            copy.wait_send()


def wait_all(*lists):
    for copies in lists:
        for copy in copies:
            copy.wait()


def reduce_start_far(links, part, from_x, from_y, rows, s, fx, fy):
    top, bottom = row_slots(rows)
    return [
        links.start(part.at[top[3]], from_x.at[0], (s, fx)),
        links.start(part.at[bottom[3]], from_y.at[0], (s, fy)),
    ]


def reduce_start_near(links, part, from_x, from_y, rows, s, fx, fy):
    top, bottom = row_slots(rows)
    return [
        links.start(part.at[top[1]], from_x.at[1], (s, fx)),
        links.start(part.at[bottom[2]], from_y.at[1], (s, fy)),
    ]


def reduce_pass(links, far, part, from_x, from_y, pass_x, pass_y, rows, s, fx, fy):
    top, bottom = row_slots(rows)
    far[0].wait_recv()
    pass_y[...] = (from_x[0].astype(F32) + part[top[2]].astype(F32)).astype(BF16)
    on_y = links.start(pass_y, from_y.at[2], (s, fy))
    far[1].wait_recv()
    pass_x[...] = (from_y[0].astype(F32) + part[bottom[1]].astype(F32)).astype(BF16)
    on_x = links.start(pass_x, from_x.at[2], (s, fx))
    return [on_y, on_x]


def mm(left, right):
    return jnp.dot(left, right, preferred_element_type=F32)


def mm_t(left, right):
    return lax.dot_general(left, right, (((1,), (1,)), ((), ())), preferred_element_type=F32)


def tile(n, width):
    return pl.ds(pl.multiple_of(n * width, width), width)


def bounds_slice(table, first, count):
    rows = table[:, pl.ds(pl.multiple_of(first, 128), count)]
    powers = jnp.exp(rows - jnp.max(rows, 0, keepdims=True))
    return jnp.sum(powers[1 : LAYER + 1], 0, keepdims=True) / jnp.sum(powers, 0, keepdims=True)


def keep_rows(lengths, group, first, rows):
    places = first + lax.broadcasted_iota(jnp.int32, (rows, 128), 0)
    start = jnp.int32(0)
    keep = jnp.where(places == start, 0.0, 1.0)
    for i in range(lengths.shape[1] - 1):
        start = start + lengths[group, i]
        keep = jnp.where(places == start, 0.0, keep)
    return keep.astype(F32)


def segment_totals(end_p, end_s, blocks, order):
    first, rest = order[0], order[1:]
    p_all = end_p[pl.ds(first, blocks, stride=8), :]
    s_all = end_s[pl.ds(first, blocks, stride=8), :]
    for j in rest:
        p_j = end_p[pl.ds(j, blocks, stride=8), :]
        s_all = end_s[pl.ds(j, blocks, stride=8), :] + p_j * s_all
        p_all = p_all * p_j
    return p_all, s_all


def spread_carry(carry, carr, end_p, end_s, blocks, order):
    for i, j in enumerate(order):
        carr[pl.ds(j, blocks, stride=8), :] = carry
        if i < 7:
            carry = end_s[pl.ds(j, blocks, stride=8), :] + end_p[pl.ds(j, blocks, stride=8), :] * carry


def mixer_kernel(
    n_seq,
    lengths,
    hidden,
    cot,
    norm_gain,
    gate_gain,
    glu_gain,
    table,
    w_in,
    w_fg,
    w_gt,
    w_out,
    normed_half,
    cot_out,
    in_out,
    fg_out,
    gate_out,
    state_out,
    raw_out,
    before_out,
    scale_out,
    middle,
    two,
    wv,
    wo,
    rows_all,
    stage,
    in_ref,
    fg_ref,
    gate_ref,
    a_ref,
    b_ref,
    shifted,
    keep_ref,
    end_p,
    end_s,
    carr,
    total,
    gathered,
    state_ref,
    raw_ref,
    squares,
    squares_t,
    packed,
    squares_in,
    part,
    from_x,
    from_y,
    pass_x,
    pass_y,
    send,
    recv,
    exchange_send,
    exchange_recv,
    local_sems,
):
    rows, width = hidden.shape
    chans = w_in.shape[1]
    lanes_of = [slice(c, c + 128) for c in range(0, chans, 128)]
    count = len(lanes_of)
    blocks = 4 * count
    step_len = rows // 8
    s, f, fx, fy, fd = plane()
    groups = [f, fx, fy, fd]
    links, local = Links(send, recv), Locals(local_sems)

    weights = [
        local.start(w, wv.at[:, pl.ds(i * chans, chans)]) for i, w in enumerate((w_in, w_fg, w_gt))
    ]
    weights.append(local.start(w_out, wo))
    barrier = pltpu.get_barrier_semaphore()
    peers = [(s, fx), (s, fy), (s, fd)] + seq_peers(n_seq)
    for peer in peers:
        pl.semaphore_signal(barrier, inc=1, device_id=peer, device_id_type=MESH)

    def norm_rows(i, _):
        at = pl.ds(pl.multiple_of(i * 16, 16), 16)
        value = hidden[at].astype(F32)
        scale = lax.rsqrt(jnp.mean(value * value, -1, keepdims=True) + epsilon)
        rows_all[at] = (value * scale * norm_gain[...]).astype(BF16)
        return 0

    lax.fori_loop(0, rows // 16, norm_rows, 0)
    pl.semaphore_wait(barrier, len(peers))
    own = gather_start(links, rows_all, rows_all, rows, s, fx, fy)
    bound = bounds_slice(table, f * chans, chans)
    for k in range(4):
        keep_ref[k] = keep_rows(lengths, groups[k], s * rows, rows)
    squares[...] = jnp.zeros_like(squares)
    squares_t[...] = jnp.zeros_like(squares_t)
    for copy in weights[:3]:
        copy.wait()

    def project(first, slots):
        def tile_of(n, _):
            cols = tile(n, 256)
            stage[: slots * rows, cols] = mm(
                rows_all[first * rows : (first + slots) * rows], wv[:, cols]
            )
            return 0

        lax.fori_loop(0, 3 * chans // 256, tile_of, 0)
        for k in range(slots):
            at = slice(k * rows, (k + 1) * rows)
            for c, lanes in enumerate(lanes_of):
                n = (first + k) * count + c
                value = stage[at, lanes].astype(BF16)
                in_ref[first + k, :, lanes] = value
                value = value.astype(F32)
                raw = stage[at, chans + c * 128 : chans + (c + 1) * 128].astype(BF16)
                fg_ref[first + k, :, lanes] = raw
                edge = bound[:, lanes]
                forget = edge + (1.0 - edge) * jax.nn.sigmoid(raw.astype(F32))
                a_ref[n] = forget * keep_ref[first + k]
                b_ref[n] = value * jax.nn.sigmoid(value) * (1.0 - forget)
            gate_ref[first + k] = stage[at, 2 * chans :]

    project(0, 1)
    later = gather_forward(links, own, rows_all, rows, s, fx, fy)
    gather_middle(own)
    project(1, 2)
    gather_far(later)
    cot_own = gather_start(links, cot, cot_out, rows, s, fx, fy)
    core = s % 2
    swaps, outs = swap_columns(
        links, local, rows_all, normed_half, n_seq, core, (s + 1 - 2 * core, f)
    )
    outs.append(local.start(cot, cot_out.at[pl.ds(0, rows)]))
    project(3, 1)
    outs += [
        local.start(in_ref, in_out),
        local.start(fg_ref, fg_out),
        local.start(gate_ref, gate_out),
    ]

    def scan_step(i, carry):
        new = []
        at = pl.ds(i, 8, stride=step_len)
        for n, (product, state) in enumerate(carry):
            a = a_ref[n, at, :]
            state = a * state + b_ref[n, at, :]
            product = product * a
            a_ref[n, at, :] = product
            b_ref[n, at, :] = state
            new.append((product, state))
        return tuple(new)

    start = tuple((jnp.ones((8, 128), F32), jnp.zeros((8, 128), F32)) for _ in range(blocks))
    ends = lax.fori_loop(0, step_len, scan_step, start)
    for n, (product, state) in enumerate(ends):
        end_p[8 * n : 8 * n + 8] = product
        end_s[8 * n : 8 * n + 8] = state
    p_all, s_all = segment_totals(end_p, end_s, blocks, range(8))
    total[:blocks] = p_all
    total[blocks:] = s_all
    copies = start_exchange(total, gathered, exchange_send, exchange_recv, n_seq)
    wait_all(copies)
    carry = jnp.zeros((blocks, 128), F32)
    for j in range(n_seq - 1):
        carry = jnp.where(j < s, gathered[j, blocks:] + gathered[j, :blocks] * carry, carry)
    for n in range(blocks):
        shifted[n, 0:1] = carry[n : n + 1]
    spread_carry(carry, carr, end_p, end_s, blocks, range(8))

    def finish(n, _):
        enter_state = carr[pl.ds(pl.multiple_of(n * 8, 8), 8)]
        for i in range(step_len):
            at = pl.ds(i, 8, stride=step_len)
            state = b_ref[n, at, :] + a_ref[n, at, :] * enter_state
            b_ref[n, at, :] = state
            shifted[n, pl.ds(i + 1, 8, stride=step_len), :] = state
        return 0

    lax.fori_loop(0, blocks, finish, 0)
    outs.append(local.start(shifted.at[:, pl.ds(0, rows)], before_out))

    lane = lax.broadcasted_iota(jnp.int32, (rows, 128), 1)
    for k in (3, 1, 2, 0):
        square = jnp.zeros((rows, 1), F32)
        for c, lanes in enumerate(lanes_of):
            state_b = b_ref[k * count + c].astype(BF16)
            state_ref[k, :, lanes] = state_b
            state = state_b.astype(F32)
            square = square + jnp.sum(state * state, -1, keepdims=True)
            gate = gate_ref[k, :, lanes]
            gain = gate_gain[:, pl.ds(pl.multiple_of(f * chans + c * 128, 128), 128)]
            raw_ref[k * rows : (k + 1) * rows, lanes] = (
                state * gain * gate * jax.nn.sigmoid(gate)
            ).astype(BF16)
        squares[:rows] = jnp.where(lane == groups[k], square, squares[:rows])
    packed[...] = squares[...].T[:8]
    square_copies = [
        links.start(packed, squares_in.at[i], (s, peer)) for i, peer in enumerate((fx, fy, fd))
    ]
    outs += [local.start(state_ref, state_out), local.start(raw_ref, raw_out)]
    cot_later = gather_forward(links, cot_own, cot_out, rows, s, fx, fy)
    weights[3].wait()

    def output_part(first, slots):
        at = slice(first * rows, (first + slots) * rows)

        def tile_of(n, _):
            cols = tile(n, 512)
            part[at, cols] = mm(raw_ref[at], wo[:, cols]).astype(BF16)
            return 0

        lax.fori_loop(0, width // 512, tile_of, 0)

    output_part(3, 1)
    far = reduce_start_far(links, part, from_x, from_y, rows, s, fx, fy)
    output_part(1, 2)
    near = reduce_start_near(links, part, from_x, from_y, rows, s, fx, fy)
    output_part(0, 1)
    passed = reduce_pass(links, far, part, from_x, from_y, pass_x, pass_y, rows, s, fx, fy)
    for copy in square_copies:
        copy.wait_recv()
    all_squares = (packed[...] + squares_in[0]) + (squares_in[1] + squares_in[2])
    squares_t[:8] = lax.rsqrt(all_squares / width + epsilon)
    scales = squares_t[...].T[:rows]
    for k in range(4):
        scale_out[k] = jnp.sum(jnp.where(lane == groups[k], scales, 0.0), -1, keepdims=True)
    for copy in near + passed:
        copy.wait_recv()
    half = rows // 2
    for first, one, other in ((0, from_x.at[1], from_y.at[2]), (half, from_y.at[1], from_x.at[2])):

        def sum_rows(i, _):
            here = pl.ds(pl.multiple_of(i * 16, 16), 16)
            at = pl.ds(pl.multiple_of(first + i * 16, 16), 16)
            mixed = part[at].astype(F32) + one[here].astype(F32) + other[here].astype(F32)
            value = hidden[at].astype(F32) + scale_out[0, at] * mixed
            middle[at] = value
            scale = lax.rsqrt(jnp.mean(value * value, -1, keepdims=True) + epsilon)
            two[at] = (value * scale * glu_gain[...]).astype(BF16)
            return 0

        lax.fori_loop(0, half // 16, sum_rows, 0)
    gather_middle(cot_own)
    gather_far(cot_later)
    sends_done(own, later, cot_own, cot_later, square_copies, far, near, passed)
    wait_all(swaps, outs)


def mixer_forward(lengths, hidden, cot, gains, table, weights, collective_id):
    n_seq = lax.axis_size("seq")
    rows, width = hidden.shape
    chans = weights[0].shape[1]
    blocks = 4 * chans // 128
    tokens = 4 * rows
    half = rows // 2
    shape = jax.ShapeDtypeStruct
    wide = shape((tokens, width), BF16)
    narrow = shape((4, rows, chans), BF16)
    long_rows = round_up(rows, 128)
    return pl.pallas_call(
        functools.partial(mixer_kernel, n_seq),
        out_shape=(
            shape((2, tokens, width // 2), BF16),
            wide,
            narrow,
            narrow,
            shape((4, rows, chans), F32),
            narrow,
            shape((tokens, chans), BF16),
            shape((blocks, rows, 128), F32),
            shape((4, rows, 1), F32),
            shape((rows, width), F32),
            shape((rows, width), BF16),
        ),
        in_specs=[pl.BlockSpec(memory_space=pltpu.SMEM), VMEM, VMEM, VMEM, VMEM, VMEM, VMEM]
        + [ANY] * 4,
        out_specs=(ANY,) * 8 + (VMEM,) * 3,
        scratch_shapes=[
            pltpu.VMEM((width, 3 * chans), BF16),
            pltpu.VMEM((chans, width), BF16),
            pltpu.VMEM((tokens, width), BF16),
            pltpu.VMEM((2 * rows, 3 * chans), F32),
            pltpu.VMEM((4, rows, chans), BF16),
            pltpu.VMEM((4, rows, chans), BF16),
            pltpu.VMEM((4, rows, chans), F32),
            pltpu.VMEM((blocks, rows, 128), F32),
            pltpu.VMEM((blocks, rows, 128), F32),
            pltpu.VMEM((blocks, rows + 8, 128), F32),
            pltpu.VMEM((4, rows, 128), F32),
            pltpu.VMEM((8 * blocks, 128), F32),
            pltpu.VMEM((8 * blocks, 128), F32),
            pltpu.VMEM((8 * blocks, 128), F32),
            pltpu.VMEM((2 * blocks, 128), F32),
            pltpu.VMEM((n_seq, 2 * blocks, 128), F32),
            pltpu.VMEM((4, rows, chans), BF16),
            pltpu.VMEM((tokens, chans), BF16),
            pltpu.VMEM((long_rows, 128), F32),
            pltpu.VMEM((128, long_rows), F32),
            pltpu.VMEM((8, long_rows), F32),
            pltpu.VMEM((3, 8, long_rows), F32),
            pltpu.VMEM((tokens, width), BF16),
            pltpu.VMEM((3, half, width), BF16),
            pltpu.VMEM((3, half, width), BF16),
            pltpu.VMEM((half, width), BF16),
            pltpu.VMEM((half, width), BF16),
            pltpu.SemaphoreType.DMA((21 + n_seq // 2,)),
            pltpu.SemaphoreType.DMA((21 + n_seq // 2,)),
            pltpu.SemaphoreType.DMA((n_seq,)),
            pltpu.SemaphoreType.DMA((n_seq,)),
            pltpu.SemaphoreType.DMA((11 + n_seq // 2,)),
        ],
        compiler_params=params(collective_id),
        name="mixer_forward",
    )(lengths, hidden, cot, *gains, table, *weights)


def swap_columns(links, local, src, dst, n_seq, core, mate):
    part = src.shape[1] // n_seq
    copies, stays = [], []
    for z in range(n_seq // 2):
        to = pl.ds(z * part, part)
        theirs = pl.ds(pl.multiple_of((2 * z + 1 - core) * part, part), part)
        ours = pl.ds(pl.multiple_of((2 * z + core) * part, part), part)
        copies.append(links.start(src.at[:, theirs], dst.at[1, :, to], mate))
        stays.append(local.start(src.at[:, ours], dst.at[0, :, to]))
    return copies, stays


def swap_rows(links, local, src, dst, at, mate):
    copy = links.start(src.at[at], dst.at[1, at], mate)
    return copy, local.start(src.at[at], dst.at[0, at])


def glu_kernel(
    n_seq,
    two,
    cot_all,
    w_gate,
    w_up,
    w_down,
    two_half,
    cot_half,
    act_pair,
    gate_pair,
    up_pair,
    wv,
    wd,
    cot_ref,
    two_ref,
    d_act,
    stage,
    act,
    d_gate,
    d_up,
    send,
    recv,
    local_sems,
):
    rows = two.shape[0]
    units = w_gate.shape[1]
    s, f, fx, fy, fd = plane()
    core = s % 2
    mate = (s + 1 - 2 * core, f)
    links, local = Links(send, recv), Locals(local_sems)
    loads = [
        local.start(w_down, wd),
        local.start(cot_all, cot_ref),
        local.start(w_gate, wv.at[:, pl.ds(0, units)]),
        local.start(w_up, wv.at[:, pl.ds(units, units)]),
    ]
    two_ref[:rows] = two[...]
    enter([(s, fx), (s, fy), mate])
    own = gather_start(links, two_ref, two_ref, rows, s, fx, fy)
    loads[0].wait()
    loads[1].wait()
    swaps, stays = swap_columns(links, local, cot_ref, cot_half, n_seq, core, mate)

    def act_tile(n, _):
        cols = tile(n, 256)
        d_act[:, cols] = mm_t(cot_ref[...], wd[cols])
        return 0

    lax.fori_loop(0, units // 256, act_tile, 0)
    if units % 256:
        rest = slice(units // 256 * 256, units)
        d_act[:, rest] = mm_t(cot_ref[...], wd[rest])
    later = gather_forward(links, own, two_ref, rows, s, fx, fy)
    loads[2].wait()
    loads[3].wait()

    def slots(first, number):
        nonlocal swaps, stays
        base = first * rows

        def tile_of(n, _):
            cols = tile(n, 256)
            stage[: number * rows, cols] = mm(two_ref[base : base + number * rows], wv[:, cols])
            return 0

        lax.fori_loop(0, 2 * units // 256, tile_of, 0)

        def rows_of(i, _):
            at = pl.ds(pl.multiple_of(i * 16, 16), 16)
            to = pl.ds(pl.multiple_of(base + i * 16, 16), 16)
            gate, up = stage[at, :units], stage[at, units:]
            sigma = jax.nn.sigmoid(gate)
            silu = gate * sigma
            act[to] = (silu * up).astype(BF16)
            d = d_act[to]
            d_gate[to] = (d * up * silu_slope(gate, sigma)).astype(BF16)
            d_up[to] = (d * silu).astype(BF16)
            return 0

        lax.fori_loop(0, number * rows // 16, rows_of, 0)
        at = pl.ds(base, number * rows)
        for src, dst in ((act, act_pair), (d_gate, gate_pair), (d_up, up_pair)):
            sent, stayed = swap_rows(links, local, src, dst, at, mate)
            swaps, stays = swaps + [sent], stays + [stayed]

    slots(0, 1)
    gather_middle(own)
    slots(1, 2)
    gather_far(later)
    more, keeps = swap_columns(links, local, two_ref, two_half, n_seq, core, mate)
    slots(3, 1)
    sends_done(own, later)
    wait_all(swaps, stays, more, keeps)


def glu(two, cot_all, w_gate, w_up, w_down, collective_id):
    n_seq = lax.axis_size("seq")
    rows, width = two.shape
    units = w_gate.shape[1]
    tokens = 4 * rows
    shape = jax.ShapeDtypeStruct
    half = shape((2, tokens, width // 2), BF16)
    pair = shape((2, tokens, units), BF16)
    remote_count = 6 + n_seq + 9
    return pl.pallas_call(
        functools.partial(glu_kernel, n_seq),
        out_shape=(half, half, pair, pair, pair),
        in_specs=[VMEM] + [ANY] * 4,
        out_specs=(ANY,) * 5,
        scratch_shapes=[
            pltpu.VMEM((width, 2 * units), BF16),
            pltpu.VMEM((units, width), BF16),
            pltpu.VMEM((tokens, width), BF16),
            pltpu.VMEM((tokens, width), BF16),
            pltpu.VMEM((tokens, units), F32),
            pltpu.VMEM((2 * rows, 2 * units), F32),
            pltpu.VMEM((tokens, units), BF16),
            pltpu.VMEM((tokens, units), BF16),
            pltpu.VMEM((tokens, units), BF16),
            pltpu.SemaphoreType.DMA((remote_count,)),
            pltpu.SemaphoreType.DMA((remote_count,)),
            pltpu.SemaphoreType.DMA((4 + n_seq + 9,)),
        ],
        compiler_params=params(collective_id),
        name="glu",
    )(two, cot_all, w_gate, w_up, w_down)


class ZLine:
    def __init__(self, part, buf, sems, n_seq, width, lag, ahead, store=None, leave=None):
        self.part, self.buf, self.width, self.lag, self.ahead = part, buf, width, lag, ahead
        self.send_up, self.recv_up, self.send_down, self.recv_down = sems[:4]
        self.store, self.leave = store, leave
        self.s, self.f = lax.axis_index("seq"), lax.axis_index("fsdp")
        self.n_seq, self.nz = n_seq, n_seq // 2
        self.z = self.s // 2
        self.block = part.shape[0] // self.nz
        self.chunks = part.shape[1] // width
        self.steps = (self.nz - 1) * self.chunks
        self.calls = self.steps + lag * (self.nz - 2)

    def rows(self, t):
        return pl.ds(pl.multiple_of(t * self.block, self.block), self.block)

    def move(self, up, k, j):
        t = self.nz - 1 - k if up else k
        landing = t + 1 if up else t
        cols = tile(j, self.width)
        slot = k * self.chunks + j
        peer = lax.rem(self.s + (2 if up else self.n_seq - 2), self.n_seq)
        send, recv = (
            (self.send_up, self.recv_up) if up else (self.send_down, self.recv_down)
        )
        return remote(
            self.part.at[self.rows(t), cols],
            self.buf.at[self.rows(landing), cols],
            send.at[slot],
            recv.at[slot],
            (peer, self.f),
        )

    def feed(self, q):
        inside = q < self.steps
        q = jnp.minimum(q, self.steps - 1)
        k = q // self.chunks
        j = q - k * self.chunks

        @pl.when(inside & (self.z == 0))
        def _():
            self.move(True, k, j).start()

        @pl.when(inside & (self.z == self.nz - 1))
        def _():
            self.move(False, k, j).start()

    def nth(self, i):
        return jnp.where(self.z < self.nz // 2, self.nz - 1 - i, i)

    def load(self, local, src):
        order = [self.rows(self.nth(i)) for i in range(self.nz)]
        return [local.start(src.at[at], self.part.at[at]) for at in order]

    def feed_first(self):
        def step(q, _):
            self.feed(q)
            return 0

        lax.fori_loop(0, self.ahead, step, 0)

    def serve_one(self, up, q):
        z, nz = self.z, self.nz
        hops = z if up else nz - 1 - z
        q = q - self.lag * (hops - 1)
        inside = (hops >= 1) & (q >= 0) & (q < self.steps)
        q = jnp.clip(q, 0, self.steps - 1)
        k = q // self.chunks
        j = q - k * self.chunks
        left = nz - 1 - k - hops
        cols = tile(j, self.width)

        @pl.when(inside & (left >= 0))
        def _():
            self.move(up, k, j).wait_recv()

        @pl.when(inside & (left > 0))
        def _():
            t = nz - 1 - k if up else k
            landing = t + 1 if up else t
            own = self.part[self.rows(t), cols].astype(F32)
            came = self.buf[self.rows(landing), cols].astype(F32)
            self.part[self.rows(t), cols] = (own + came).astype(BF16)
            self.move(up, k, j).start()

        if up:
            latest = (z == nz - 1) | (2 * z < nz - 1)
        else:
            latest = (z == 0) | (2 * z > nz - 1)

        @pl.when(inside & (left == 0) & latest)
        def _():
            self.finish(j)

    def serve(self, q):
        self.serve_one(True, q)
        self.serve_one(False, q)

    def serve_range(self, first, last):
        def step(q, _):
            self.feed(q + self.ahead)
            self.serve(q)
            return 0

        lax.fori_loop(first, last, step, 0)

    def finish(self, j):
        cols = tile(j, self.width)

        def add(*at):
            value = self.part[self.rows(self.z), cols].astype(F32)
            for t in at:
                value = value + self.buf[self.rows(t), cols].astype(F32)
            self.store(j, value)

        @pl.when(self.z == 0)
        def _():
            add(self.z)

        @pl.when((self.z > 0) & (self.z < self.nz - 1))
        def _():
            add(self.z, self.z + 1)

        @pl.when(self.z == self.nz - 1)
        def _():
            add(self.z + 1)

        self.leave(j, True)

    def drain(self):
        for k in range(self.nz - 1):
            for up in (True, False):
                hops = self.z if up else self.nz - 1 - self.z

                @pl.when(hops < self.nz - 1 - k)
                def _():
                    def step(j, _):
                        self.move(up, k, j).wait_send()
                        return 0

                    lax.fori_loop(0, self.chunks, step, 0)

        def left(j, _):
            self.leave(j, False)
            return 0

        lax.fori_loop(0, self.chunks, left, 0)


def start_or_wait(copy, start):
    if start:
        copy.start()
    else:
        copy.wait()


def line_sems(n_seq, columns, width):
    count = (n_seq // 2 - 1) * (columns // width)
    leave = pltpu.SemaphoreType.DMA((columns // width,))
    return [pltpu.SemaphoreType.DMA((count,)) for _ in range(4)] + [leave]


def z_peers(n_seq):
    s = lax.axis_index("seq")
    f = lax.axis_index("fsdp")
    return [(lax.rem(s + 2 * k, n_seq), f) for k in range(1, n_seq // 2)]


def mm_tokens(left, right):
    return lax.dot_general(left, right, (((0,), (0,)), ((), ())), preferred_element_type=F32)


def down_kernel(
    n_seq,
    cot_half,
    act_pair,
    two_half,
    gate_pair,
    up_pair,
    w_gate,
    w_up,
    d_two,
    pair_part,
    down_out,
    cot_ref,
    act_ref,
    two_ref,
    gate_ref,
    up_ref,
    wg,
    wu,
    part,
    buf,
    rows_part,
    from_x,
    from_y,
    pass_x,
    pass_y,
    pair_ref,
    down_ref,
    send,
    recv,
    local_sems,
    *line,
):
    rows, width = d_two.shape
    units = act_pair.shape[1]
    s, f, fx, fy, fd = plane()
    links, local = Links(send, recv), Locals(local_sems)
    moves = (
        (cot_half, cot_ref),
        (act_pair, act_ref),
        (w_gate, wg),
        (w_up, wu),
        (gate_pair, gate_ref),
        (up_pair, up_ref),
        (two_half, two_ref),
    )
    loads = [local.start(src, dst) for src, dst in moves]
    enter([(s, fx), (s, fy)] + z_peers(n_seq))

    def store(j, value):
        down_ref[tile(j, 128)] = value.T

    def leave(j, start):
        at = tile(j, 128)
        copy = pltpu.make_async_copy(down_ref.at[at], down_out.at[at], line[4].at[j])
        start_or_wait(copy, start)

    z_sum = ZLine(part, buf, line, n_seq, 128, 3, 11, store, leave)
    block = z_sum.block
    loads[0].wait()
    loads[1].wait()

    def down_tile(i, _):
        t = z_sum.nth(i)
        part[z_sum.rows(t)] = mm_tokens(cot_ref[:, tile(t, block)], act_ref[...]).astype(BF16)
        return 0

    down_tile(jnp.int32(0), 0)
    z_sum.feed_first()
    lax.fori_loop(1, z_sum.nz, down_tile, 0)
    for copy in loads[2:]:
        copy.wait()

    def two_part(first, slots, base):
        at = slice(first * rows, (first + slots) * rows)

        def tile_of(n, _):
            cols = tile(n, 512)
            total = mm_t(gate_ref[at], wg[cols]) + mm_t(up_ref[at], wu[cols])
            rows_part[at, cols] = total.astype(BF16)
            z_sum.feed(base + n + z_sum.ahead)
            z_sum.serve(base + n)
            return 0

        lax.fori_loop(0, width // 512, tile_of, 0)

    count = width // 512
    two_part(3, 1, 0)
    far = reduce_start_far(links, rows_part, from_x, from_y, rows, s, fx, fy)
    two_part(1, 2, count)
    near = reduce_start_near(links, rows_part, from_x, from_y, rows, s, fx, fy)
    two_part(0, 1, 2 * count)
    served = 3 * count

    def pair_tiles(right, first, base):
        def tile_of(t, _):
            pair_ref[z_sum.rows(t), pl.ds(first, units)] = mm_tokens(
                two_ref[:, tile(t, block)], right[...]
            ).astype(BF16)
            z_sum.serve_range(base + 2 * t, base + 2 * t + 2)
            return 0

        lax.fori_loop(0, z_sum.nz, tile_of, 0)

    pair_tiles(gate_ref, 0, served)
    served += 2 * z_sum.nz
    passed = reduce_pass(links, far, rows_part, from_x, from_y, pass_x, pass_y, rows, s, fx, fy)
    pair_tiles(up_ref, units, served)
    served += 2 * z_sum.nz
    stay = local.start(pair_ref, pair_part)
    for copy in near + passed:
        copy.wait_recv()
    half = rows // 2
    d_two[:half] = rows_part[:half].astype(F32) + from_x[1].astype(F32) + from_y[2].astype(F32)
    d_two[half:] = rows_part[half:rows].astype(F32) + from_y[1].astype(F32) + from_x[2].astype(F32)
    z_sum.serve_range(served, z_sum.calls)
    z_sum.drain()
    sends_done(far, near, passed)
    stay.wait()


def down_sum(cot_half, act_pair, two_half, gate_pair, up_pair, w_gate, w_up, collective_id):
    n_seq = lax.axis_size("seq")
    tokens, units = act_pair.shape
    width = w_gate.shape[0]
    rows = tokens // 8
    half = (rows // 2, width)
    own = cot_half.shape[1]
    block = width // n_seq
    shape = jax.ShapeDtypeStruct
    return pl.pallas_call(
        functools.partial(down_kernel, n_seq),
        out_shape=(
            shape((rows, width), F32),
            shape((own, 2 * units), BF16),
            shape((units, block), F32),
        ),
        in_specs=[ANY] * 7,
        out_specs=(VMEM, ANY, ANY),
        scratch_shapes=[
            pltpu.VMEM((tokens, own), BF16),
            pltpu.VMEM((tokens, units), BF16),
            pltpu.VMEM((tokens, own), BF16),
            pltpu.VMEM((tokens, units), BF16),
            pltpu.VMEM((tokens, units), BF16),
            pltpu.VMEM((width, units), BF16),
            pltpu.VMEM((width, units), BF16),
            pltpu.VMEM((own, units), BF16),
            pltpu.VMEM((own + block, units), BF16),
            pltpu.VMEM((tokens // 2, width), BF16),
            pltpu.VMEM((3,) + half, BF16),
            pltpu.VMEM((3,) + half, BF16),
            pltpu.VMEM(half, BF16),
            pltpu.VMEM(half, BF16),
            pltpu.VMEM((own, 2 * units), BF16),
            pltpu.VMEM((units, block), F32),
            pltpu.SemaphoreType.DMA((6,)),
            pltpu.SemaphoreType.DMA((6,)),
            pltpu.SemaphoreType.DMA((8,)),
        ]
        + line_sems(n_seq, units, 128),
        compiler_params=params(collective_id),
        name="down_sum",
    )(cot_half, act_pair, two_half, gate_pair, up_pair, w_gate, w_up)


def pair_kernel(
    n_seq,
    lengths,
    hidden,
    cot,
    glu_gain,
    gate_gain,
    table,
    scale_g,
    d_two,
    middle,
    pair_part,
    w_out,
    w_in,
    w_fg,
    w_gt,
    gate_raw,
    state_b,
    out_raw,
    in_raw,
    fg_raw,
    before_in,
    normed_half,
    pair_grad,
    mixer_part,
    d_normed_out,
    d_middle_out,
    d_glu_gain,
    d_gain,
    d_bounds,
    d_normed,
    d_middle,
    pair_ref,
    part,
    buf,
    wo,
    wv,
    mixed_all,
    mixed_mate,
    normed_ref,
    d_proj,
    out_gate,
    gate_ref,
    state_ref,
    raw_ref,
    in_ref,
    fg_ref,
    before,
    p_ref,
    q_ref,
    stage,
    rows_part,
    from_x,
    from_y,
    pass_x,
    pass_y,
    dots,
    keep_ref,
    end_p,
    end_s,
    carr,
    total,
    gathered,
    send,
    recv,
    exchange_send,
    exchange_recv,
    local_sems,
    tile_sems,
    *line,
):
    rows, width = hidden.shape
    chans = w_in.shape[1]
    tokens = 4 * rows
    lanes_of = [slice(c, c + 128) for c in range(0, chans, 128)]
    count = len(lanes_of)
    blocks = 4 * count
    step_len = rows // 8
    s, f, fx, fy, fd = plane()
    groups = [f, fx, fy, fd]
    core = s % 2
    mate = (s + 1 - 2 * core, f)
    links, local = Links(send, recv), Locals(local_sems)

    def store(j, value):
        pair_ref[:, tile(j, 256)] = value

    def leave(j, start):
        at = tile(j, 256)
        copy = pltpu.make_async_copy(pair_ref.at[:, at], pair_grad.at[:, at], line[4].at[j])
        start_or_wait(copy, start)

    z_sum = ZLine(part, buf, line, n_seq, 256, 2, 11, store, leave)
    blocks_in = z_sum.load(local, pair_part)
    rows_in = [local.start(d_two, d_middle), local.start(middle, d_normed)]
    loads = [local.start(w_out, wo)]
    loads += [
        local.start(src, dst)
        for src, dst in (
            (gate_raw, gate_ref),
            (state_b, state_ref),
            (out_raw, raw_ref),
            (in_raw, in_ref),
            (fg_raw, fg_ref),
            (before_in, before),
        )
    ]
    weights = [
        local.start(w, wv.at[:, pl.ds(i * chans, chans)]) for i, w in enumerate((w_in, w_fg, w_gt))
    ]
    weights.append(local.start(normed_half, normed_ref))
    enter([(s, fx), (s, fy), (s, fd)] + seq_peers(n_seq))
    blocks_in[0].wait()
    z_sum.feed_first()
    served = 0

    def serve(number):
        nonlocal served
        z_sum.serve_range(served, served + number)
        served += number

    d_glu_gain[...] = jnp.zeros_like(d_glu_gain)
    wait_all(rows_in, blocks_in[1:])

    def middle_rows(i, _):
        at = pl.ds(pl.multiple_of(i * 16, 16), 16)
        value, came = d_normed[at], d_middle[at]
        scale = lax.rsqrt(jnp.mean(value * value, -1, keepdims=True) + epsilon)
        scaled = glu_gain[...] * came
        mean = jnp.mean(scaled * value, -1, keepdims=True)
        grad = cot[at].astype(F32) + scale * scaled - value * (scale**3 * mean)
        d_middle[at] = grad
        grad_b = grad.astype(BF16)
        mixed_all[at] = grad_b
        own_dot = jnp.sum(
            grad_b.astype(F32) * (value - hidden[at].astype(F32)), -1, keepdims=True
        )
        dots[0, at] = jnp.broadcast_to(own_dot, (16, 128))
        d_glu_gain[...] += jnp.sum(came * value * scale, 0, keepdims=True)
        return 0

    lax.fori_loop(0, rows // 16, middle_rows, 0)
    outs = [local.start(d_middle, d_middle_out)]
    own = gather_start(links, mixed_all, mixed_all, rows, s, fx, fy)
    dot_copies = [
        links.start(dots.at[0], dots.at[k], (s, peer)) for k, peer in ((1, fx), (2, fy), (3, fd))
    ]
    bound = bounds_slice(table, f * chans, chans)
    for k in range(4):
        keep_ref[k] = keep_rows(lengths, groups[k], s * rows, rows)
    d_gain[...] = jnp.zeros_like(d_gain)
    serve(1)
    for copy in loads:
        copy.wait()

    def out_rows(first, slots):
        stage[: slots * rows] = mm_t(mixed_all[first * rows : (first + slots) * rows], wo[...])
        for i in range(slots):
            k = first + i
            scale = scale_g[k]
            for c, lanes in enumerate(lanes_of):
                n = k * count + c
                gain = gate_gain[:, pl.ds(pl.multiple_of(f * chans + c * 128, 128), 128)]
                d_out = stage[i * rows : (i + 1) * rows, lanes]
                gate = gate_ref[k, :, lanes]
                sigma = jax.nn.sigmoid(gate)
                silu = gate * sigma
                state = state_ref[k, :, lanes].astype(F32)
                weighed = d_out * (state * scale)
                d_gain[:, lanes] += jnp.sum(weighed * silu, 0, keepdims=True)
                at = slice(k * rows, (k + 1) * rows)
                d_proj[at, 2 * chans + c * 128 : 2 * chans + (c + 1) * 128] = (
                    weighed * gain * silu_slope(gate, sigma)
                ).astype(BF16)
                out_gate[at, lanes] = (raw_ref[at, lanes].astype(F32) * scale).astype(BF16)
                d_state = scale * (d_out * gain * silu) - state * (
                    scale * scale * (dots[k] / width)
                )
                q_ref[n] = d_state.astype(BF16).astype(F32)
                edge = bound[:, lanes]
                forget = edge + (1.0 - edge) * jax.nn.sigmoid(fg_ref[k, :, lanes].astype(F32))
                p_ref[n] = forget * keep_ref[k]

    out_rows(0, 1)
    later = gather_forward(links, own, mixed_all, rows, s, fx, fy)
    serve(2)
    gather_middle(own)
    for copy in dot_copies:
        copy.wait_recv()
    out_rows(1, 2)
    serve(3)
    gather_far(later)
    out_rows(3, 1)
    serve(2)
    own_rows, mate_rows = pl.ds(0, tokens), pl.ds(tokens, tokens)
    last = pl.ds(2 * chans, chans)
    swaps = [
        links.start(out_gate.at[own_rows], out_gate.at[mate_rows], mate),
        links.start(d_proj.at[own_rows, last], d_proj.at[mate_rows, last], mate),
    ]
    wide = z_sum.block
    for t in range(n_seq // 2):
        theirs = pl.ds(pl.multiple_of((2 * t + 1 - core) * wide, wide), wide)
        swaps.append(
            links.start(mixed_all.at[:, theirs], mixed_mate.at[:, pl.ds(t * wide, wide)], mate)
        )

    def scan_step(i, carry):
        new = []
        at = pl.ds(step_len - 1 - i, 8, stride=step_len)
        for n, (product, message) in enumerate(carry):
            a = p_ref[n, at, :]
            acc = q_ref[n, at, :] + message
            p_ref[n, at, :] = product
            q_ref[n, at, :] = acc
            new.append((product * a, a * acc))
        return tuple(new)

    start = tuple((jnp.ones((8, 128), F32), jnp.zeros((8, 128), F32)) for _ in range(blocks))
    ends = lax.fori_loop(0, step_len, scan_step, start)
    for n, (product, message) in enumerate(ends):
        end_p[8 * n : 8 * n + 8] = product
        end_s[8 * n : 8 * n + 8] = message
    p_all, s_all = segment_totals(end_p, end_s, blocks, range(7, -1, -1))
    total[:blocks] = p_all
    total[blocks:] = s_all
    copies = start_exchange(total, gathered, exchange_send, exchange_recv, n_seq)
    serve(2)
    wait_all(copies)
    carry = jnp.zeros((blocks, 128), F32)
    for j in range(n_seq - 1, 0, -1):
        carry = jnp.where(j > s, gathered[j, blocks:] + gathered[j, :blocks] * carry, carry)
    spread_carry(carry, carr, end_p, end_s, blocks, range(7, -1, -1))

    def finish(n, _):
        enter_state = carr[pl.ds(pl.multiple_of(n * 8, 8), 8)]
        for i in range(step_len):
            at = pl.ds(i, 8, stride=step_len)
            q_ref[n, at, :] = q_ref[n, at, :] + p_ref[n, at, :] * enter_state
        return 0

    lax.fori_loop(0, blocks, finish, 0)
    d_bounds[...] = jnp.zeros_like(d_bounds)
    for k in range(4):
        at = slice(k * rows, (k + 1) * rows)
        for c, lanes in enumerate(lanes_of):
            acc = q_ref[k * count + c]
            edge = bound[:, lanes]
            sigma_f = jax.nn.sigmoid(fg_ref[k, :, lanes].astype(F32))
            forget = edge + (1.0 - edge) * sigma_f
            value = in_ref[k, :, lanes].astype(F32)
            sigma_i = jax.nn.sigmoid(value)
            d_forget = acc * (before[k * count + c] * keep_ref[k] - value * sigma_i)
            d_proj[at, lanes] = (acc * (1.0 - forget) * silu_slope(value, sigma_i)).astype(BF16)
            d_sigma = d_forget * (1.0 - sigma_f)
            d_proj[at, chans + c * 128 : chans + (c + 1) * 128] = (
                d_sigma * (1.0 - edge) * sigma_f
            ).astype(BF16)
            d_bounds[:, lanes] += jnp.sum(d_sigma, 0, keepdims=True)
    first = pl.ds(0, 2 * chans)
    swaps.append(links.start(d_proj.at[own_rows, first], d_proj.at[mate_rows, first], mate))
    serve(2)
    for copy in weights:
        copy.wait()

    def normed_part(first_slot, slots):
        at = slice(first_slot * rows, (first_slot + slots) * rows)

        def tile_of(n, _):
            cols = tile(n, 512)
            rows_part[at, cols] = mm_t(d_proj[at], wv[cols]).astype(BF16)
            return 0

        lax.fori_loop(0, width // 512, tile_of, 0)

    normed_part(3, 1)
    far = reduce_start_far(links, rows_part, from_x, from_y, rows, s, fx, fy)
    normed_part(1, 2)
    near = reduce_start_near(links, rows_part, from_x, from_y, rows, s, fx, fy)
    normed_part(0, 1)
    serve(3)
    for copy in swaps:
        copy.wait_recv()

    def tile_out(t):
        slot = lax.rem(t, 2)
        return pltpu.make_async_copy(
            wo.at[tile(slot, wide)], mixer_part.at[z_sum.rows(t)], tile_sems.at[slot]
        )

    def mixer_tile(t, _):
        @pl.when(t >= 2)
        def _():
            tile_out(t - 2).wait()

        at = tile(lax.rem(t, 2), wide)
        ours = mixed_all[:, tile(2 * t + core, wide)]
        out_part = mm_tokens(ours, out_gate[:tokens])
        out_part = out_part + mm_tokens(mixed_mate[:, tile(t, wide)], out_gate[tokens:])
        wo[at, :chans] = out_part.astype(BF16)
        wo[at, chans:] = mm_tokens(normed_ref[:, tile(t, wide)], d_proj[...]).astype(BF16)
        tile_out(t).start()
        return 0

    lax.fori_loop(0, 1, mixer_tile, 0)
    passed = reduce_pass(links, far, rows_part, from_x, from_y, pass_x, pass_y, rows, s, fx, fy)
    serve(1)
    lax.fori_loop(1, z_sum.nz, mixer_tile, 0)
    serve(2)
    for copy in near + passed:
        copy.wait_recv()
    half = rows // 2
    d_normed[:half] = rows_part[:half].astype(F32) + from_x[1].astype(F32) + from_y[2].astype(F32)
    d_normed[half:] = (
        rows_part[half:rows].astype(F32) + from_y[1].astype(F32) + from_x[2].astype(F32)
    )
    outs.append(local.start(d_normed, d_normed_out))
    z_sum.serve_range(served, z_sum.calls)
    z_sum.drain()
    sends_done(own, later, dot_copies, swaps, far, near, passed)
    for t in range(z_sum.nz - 2, z_sum.nz):
        tile_out(jnp.int32(t)).wait()
    wait_all(outs)


def pair_sum(
    lengths, own_rows, gains, table, scale_g, float_rows, pair_part, weights, saved, normed_half, cid
):
    n_seq = lax.axis_size("seq")
    rows, width = own_rows[0].shape
    chans = weights[1].shape[1]
    own, columns = pair_part.shape
    tokens = 4 * rows
    blocks = 4 * chans // 128
    block = width // n_seq
    half = (rows // 2, width)
    shape = jax.ShapeDtypeStruct
    exchange = pltpu.SemaphoreType.DMA((n_seq,))
    count = 18 + n_seq // 2
    return pl.pallas_call(
        functools.partial(pair_kernel, n_seq),
        out_shape=(
            shape((block, columns), F32),
            shape((own, 4 * chans), BF16),
            shape((rows, width), F32),
            shape((rows, width), F32),
            shape((1, width), F32),
            shape((1, chans), F32),
            shape((1, chans), F32),
        ),
        in_specs=[pl.BlockSpec(memory_space=pltpu.SMEM)] + [VMEM] * 6 + [ANY] * 14,
        out_specs=(ANY,) * 4 + (VMEM,) * 3,
        scratch_shapes=[
            pltpu.VMEM((rows, width), F32),
            pltpu.VMEM((rows, width), F32),
            pltpu.VMEM((block, columns), F32),
            pltpu.VMEM((own, columns), BF16),
            pltpu.VMEM((own + block, columns), BF16),
            pltpu.VMEM((chans, width), BF16),
            pltpu.VMEM((width, 3 * chans), BF16),
            pltpu.VMEM((tokens, width), BF16),
            pltpu.VMEM((tokens, width // 2), BF16),
            pltpu.VMEM((2 * tokens, width // 2), BF16),
            pltpu.VMEM((2 * tokens, 3 * chans), BF16),
            pltpu.VMEM((2 * tokens, chans), BF16),
            pltpu.VMEM((4, rows, chans), F32),
            pltpu.VMEM((4, rows, chans), BF16),
            pltpu.VMEM((tokens, chans), BF16),
            pltpu.VMEM((4, rows, chans), BF16),
            pltpu.VMEM((4, rows, chans), BF16),
            pltpu.VMEM((blocks, rows, 128), F32),
            pltpu.VMEM((blocks, rows, 128), F32),
            pltpu.VMEM((blocks, rows, 128), F32),
            pltpu.VMEM((2 * rows, chans), F32),
            pltpu.VMEM((tokens, width), BF16),
            pltpu.VMEM((3,) + half, BF16),
            pltpu.VMEM((3,) + half, BF16),
            pltpu.VMEM(half, BF16),
            pltpu.VMEM(half, BF16),
            pltpu.VMEM((4, rows, 128), F32),
            pltpu.VMEM((4, rows, 128), F32),
            pltpu.VMEM((8 * blocks, 128), F32),
            pltpu.VMEM((8 * blocks, 128), F32),
            pltpu.VMEM((8 * blocks, 128), F32),
            pltpu.VMEM((2 * blocks, 128), F32),
            pltpu.VMEM((n_seq, 2 * blocks, 128), F32),
            pltpu.SemaphoreType.DMA((count,)),
            pltpu.SemaphoreType.DMA((count,)),
            exchange,
            exchange,
            pltpu.SemaphoreType.DMA((15 + n_seq // 2,)),
            pltpu.SemaphoreType.DMA((2,)),
        ]
        + line_sems(n_seq, columns, 256),
        compiler_params=params(cid),
        name="pair_sum",
    )(
        lengths,
        *own_rows,
        *gains,
        table,
        scale_g,
        *float_rows,
        pair_part,
        *weights,
        *saved,
        normed_half,
    )


def final_kernel(
    n_seq,
    n_fsdp,
    d_normed,
    d_middle,
    hidden,
    middle,
    norm_gain,
    d_glu_gain,
    d_gain,
    d_bounds,
    table,
    mixer_part,
    act_pair,
    w_down,
    output,
    d_hidden,
    out_grad,
    rest_grad,
    sums,
    d_table,
    out_ref,
    rest_ref,
    part,
    buf,
    act,
    wd,
    rows_part,
    from_x,
    from_y,
    pass_x,
    pass_y,
    norm_sum,
    terms,
    quarters_in,
    terms_q,
    over_seq,
    along_sum,
    over_fsdp,
    send,
    recv,
    local_sems,
    *line,
):
    rows, width = middle.shape
    chans = d_gain.shape[1]
    tokens = 4 * rows
    s, f, fx, fy, fd = plane()
    links, local = Links(send, recv), Locals(local_sems)
    head = chans // 256

    def store(j, value):
        @pl.when(j < head)
        def _():
            out_ref[tile(j, 256)] = value.T

        @pl.when(j >= head)
        def _():
            rest_ref[:, tile(j - head, 256)] = value

    def leave(j, start):
        @pl.when(j < head)
        def _():
            at = tile(j, 256)
            copy = pltpu.make_async_copy(out_ref.at[at], out_grad.at[at], line[4].at[j])
            start_or_wait(copy, start)

        @pl.when(j >= head)
        def _():
            at = tile(j - head, 256)
            copy = pltpu.make_async_copy(rest_ref.at[:, at], rest_grad.at[:, at], line[4].at[j])
            start_or_wait(copy, start)

    z_sum = ZLine(part, buf, line, n_seq, 256, 2, 8, store, leave)
    blocks_in = z_sum.load(local, mixer_part)
    loads = [
        local.start(act_pair.at[pl.ds(0, tokens)], act),
        local.start(w_down, wd),
    ]
    along = seq_peers(n_seq)
    across = [(s, fx), (s, fy), (s, fd)]
    enter(across + along)
    blocks_in[0].wait()
    z_sum.feed_first()
    served = 0

    def serve(number):
        nonlocal served
        z_sum.serve_range(served, served + number)
        served += number

    norm_sum[...] = jnp.zeros_like(norm_sum)

    def hidden_rows(i, _):
        at = pl.ds(pl.multiple_of(i * 16, 16), 16)
        value, came = hidden[at].astype(F32), d_normed[at]
        scale = lax.rsqrt(jnp.mean(value * value, -1, keepdims=True) + epsilon)
        scaled = norm_gain[...] * came
        mean = jnp.mean(scaled * value, -1, keepdims=True)
        d_hidden[at] = (d_middle[at] + scale * scaled - value * (scale**3 * mean)).astype(BF16)
        norm_sum[...] += jnp.sum(came * value * scale, 0, keepdims=True)
        return 0

    wait_all(blocks_in[1:], loads)

    def glu_part(first, slots):
        at = slice(first * rows, (first + slots) * rows)

        def tile_of(n, _):
            cols = tile(n, 512)
            rows_part[at, cols] = mm(act[at], wd[:, cols]).astype(BF16)
            return 0

        lax.fori_loop(0, width // 512, tile_of, 0)

    glu_part(3, 1)
    far = reduce_start_far(links, rows_part, from_x, from_y, rows, s, fx, fy)
    glu_part(1, 2)
    near = reduce_start_near(links, rows_part, from_x, from_y, rows, s, fx, fy)
    glu_part(0, 1)
    serve(2)
    lax.fori_loop(0, rows // 16, hidden_rows, 0)
    terms[...] = jnp.zeros_like(terms)
    for q in range(4):
        terms[q, 0:1] = norm_sum[:, q * chans : (q + 1) * chans]
        terms[q, 1:2] = d_glu_gain[:, q * chans : (q + 1) * chans]
    quarter_copies = [
        links.start(terms.at[peer], quarters_in.at[k], (s, peer))
        for k, peer in enumerate((fx, fy, fd))
    ]
    serve(1)
    passed = reduce_pass(links, far, rows_part, from_x, from_y, pass_x, pass_y, rows, s, fx, fy)
    serve(2)
    quarter = terms[pl.ds(f, 1)][0]
    for k, copy in enumerate(quarter_copies):
        copy.wait_recv()
        quarter = quarter + quarters_in[k]
    half = chans // 2
    for first, cols in ((0, slice(0, half)), (4, slice(half, chans))):
        terms_q[first : first + 2] = quarter[:2, cols]
        terms_q[first + 2 : first + 3] = d_gain[:, cols]
        terms_q[first + 3 : first + 4] = d_bounds[:, cols]
    seq_copies = [links.start(terms_q, over_seq.at[k], peer) for k, peer in enumerate(along)]
    serve(1)
    total = terms_q[...]
    for k, copy in enumerate(seq_copies):
        copy.wait_recv()
        total = total + over_seq[k]
    along_sum[...] = total
    fsdp_copies = [links.start(along_sum, over_fsdp.at[k], peer) for k, peer in enumerate(across)]
    serve(2)
    for copy in near + passed:
        copy.wait_recv()
    middle_half = rows // 2
    for first, one, other in (
        (0, from_x.at[1], from_y.at[2]),
        (middle_half, from_y.at[1], from_x.at[2]),
    ):
        at = slice(first, first + middle_half)
        added = rows_part[at].astype(F32) + one[...].astype(F32) + other[...].astype(F32)
        output[at] = (middle[at] + added).astype(BF16)
    serve(1)
    for copy in fsdp_copies:
        copy.wait_recv()
    for k, group in enumerate((f, fx, fy, fd)):
        total = along_sum[...] if k == 0 else over_fsdp[k - 1]
        for i in range(2):
            at = pl.ds(pl.multiple_of(group * chans + i * half, 128), half)
            sums[:, at] = total[4 * i : 4 * i + 4]
    powers = jnp.exp(table[...] - jnp.max(table[...], 0, keepdims=True))
    soft = powers / jnp.sum(powers, 0, keepdims=True)
    row = lax.broadcasted_iota(jnp.int32, soft.shape, 0)
    chosen = jnp.where((row >= 1) & (row <= LAYER), 1.0, 0.0)
    bound = jnp.sum(soft * chosen, 0, keepdims=True)
    d_table[...] = soft * (chosen - bound) * sums[3:4]
    z_sum.serve_range(served, z_sum.calls)
    z_sum.drain()
    sends_done(far, near, passed, quarter_copies, seq_copies, fsdp_copies)


def final_sum(rows_in, gains, table, mixer_part, act_pair, w_down, cid):
    n_seq, n_fsdp = lax.axis_size("seq"), lax.axis_size("fsdp")
    rows, width = rows_in[0].shape
    own, columns = mixer_part.shape
    units = w_down.shape[0]
    chans = columns // 4
    tokens = 4 * rows
    block = width // n_seq
    half = (rows // 2, width)
    terms = (8, chans // 2)
    shape = jax.ShapeDtypeStruct
    count = 6 + n_seq - 1 + 2 * (n_fsdp - 1)
    return pl.pallas_call(
        functools.partial(final_kernel, n_seq, n_fsdp),
        out_shape=(
            shape((rows, width), BF16),
            shape((rows, width), BF16),
            shape((chans, block), F32),
            shape((block, 3 * chans), F32),
            shape((4, width), F32),
            shape(table.shape, F32),
        ),
        in_specs=[VMEM] * 9 + [ANY] * 3,
        out_specs=(VMEM, VMEM, ANY, ANY, VMEM, VMEM),
        scratch_shapes=[
            pltpu.VMEM((chans, block), F32),
            pltpu.VMEM((block, 3 * chans), F32),
            pltpu.VMEM((own, columns), BF16),
            pltpu.VMEM((own + block, columns), BF16),
            pltpu.VMEM((tokens, units), BF16),
            pltpu.VMEM((units, width), BF16),
            pltpu.VMEM((tokens, width), BF16),
            pltpu.VMEM((3,) + half, BF16),
            pltpu.VMEM((3,) + half, BF16),
            pltpu.VMEM(half, BF16),
            pltpu.VMEM(half, BF16),
            pltpu.VMEM((1, width), F32),
            pltpu.VMEM((n_fsdp, 8, chans), F32),
            pltpu.VMEM((n_fsdp - 1, 8, chans), F32),
            pltpu.VMEM(terms, F32),
            pltpu.VMEM((n_seq - 1,) + terms, F32),
            pltpu.VMEM(terms, F32),
            pltpu.VMEM((n_fsdp - 1,) + terms, F32),
            pltpu.SemaphoreType.DMA((count,)),
            pltpu.SemaphoreType.DMA((count,)),
            pltpu.SemaphoreType.DMA((2 + n_seq // 2,)),
        ]
        + line_sems(n_seq, columns, 256),
        compiler_params=params(cid),
        name="final_sum",
    )(*rows_in, *gains, table, mixer_part, act_pair, w_down)


def hand_over_kernel(count, pieces, *refs):
    sources, targets = refs[: len(refs) - 2 * count - 2], refs[len(refs) - 2 * count - 2 :]
    kept, arrived, left = targets[count : 2 * count], targets[2 * count], targets[2 * count + 1]
    loads, stores = [], []
    for n, (i, source, first, rows, column) in enumerate(pieces):
        at = pl.ds(first, rows)
        src = sources[source].at[at, pl.ds(column, kept[i].shape[1])]
        loads.append(copy_in(src, kept[i].at[at], arrived.at[n]))
    for n, (i, source, first, rows, column) in enumerate(pieces):
        at = pl.ds(first, rows)
        loads[n].wait()
        stores.append(copy_in(kept[i].at[at], targets[i].at[at], left.at[n]))
    for store in stores:
        store.wait()


def hand_over(arrays, wanted):
    pieces, shapes = [], []
    for i, (source, column, columns) in enumerate(wanted):
        x = arrays[source]
        height = x.shape[0]
        parts = max(1, height * columns * x.dtype.itemsize >> 18)
        parts = parts if height % (parts * 16) == 0 else 1
        rows = height // parts
        pieces += [(i, source, n * rows, rows, column) for n in range(parts)]
        shapes.append(((height, columns), x.dtype))
    return pl.pallas_call(
        functools.partial(hand_over_kernel, len(wanted), tuple(pieces)),
        out_shape=tuple(jax.ShapeDtypeStruct(*x) for x in shapes),
        in_specs=[ANY] * len(arrays),
        out_specs=(ANY,) * len(wanted),
        scratch_shapes=[pltpu.VMEM(*x) for x in shapes]
        + [pltpu.SemaphoreType.DMA((len(pieces),))] * 2,
        compiler_params=pltpu.CompilerParams(vmem_limit_bytes=56 << 20),
        name="hand_over",
    )(*arrays)


def plane_device(
    hidden,
    lengths,
    w_input,
    w_forget,
    w_gate_out,
    w_output,
    norm_gain,
    gate_gain,
    glu_gain,
    lower_table,
    w_glu_gate,
    w_glu_up,
    w_glu_down,
    cotangent,
):
    hidden, cotangent = hidden[0], cotangent[0]
    tokens = 4 * hidden.shape[0]
    gains = (norm_gain[None], gate_gain[None], glu_gain[None])
    (
        normed_half,
        cot_all,
        in_raw,
        fg_raw,
        gate_raw,
        state_b,
        out_raw,
        before,
        scale_g,
        middle,
        normed_two,
    ) = mixer_forward(
        lengths,
        hidden,
        cotangent,
        gains,
        lower_table,
        (w_input, w_forget, w_gate_out, w_output),
        0,
    )
    two_half, cot_half, act_pair, gate_pair, up_pair = glu(
        normed_two, cot_all, w_glu_gate, w_glu_up, w_glu_down, 1
    )
    d_normed_two, pair_part, down_grad = down_sum(
        *(x.reshape(2 * tokens, -1) for x in (cot_half, act_pair, two_half, gate_pair, up_pair)),
        w_glu_gate,
        w_glu_up,
        2,
    )
    pair_grad, mixer_part, d_normed, d_middle, d_glu_gain, d_gain, d_bounds = pair_sum(
        lengths,
        (hidden, cotangent),
        (gains[2], gains[1]),
        lower_table,
        scale_g,
        (d_normed_two, middle),
        pair_part,
        (w_output, w_input, w_forget, w_gate_out),
        (gate_raw, state_b, out_raw, in_raw, fg_raw, before),
        normed_half.reshape(2 * tokens, -1),
        3,
    )
    output, d_hidden, out_grad, rest_grad, sums, d_table = final_sum(
        (d_normed, d_middle, hidden, middle),
        (gains[0], d_glu_gain, d_gain, d_bounds),
        lower_table,
        mixer_part,
        act_pair.reshape(2 * tokens, -1),
        w_glu_down,
        4,
    )
    width, chans, units = hidden.shape[1], w_input.shape[1], w_glu_gate.shape[1]
    block = down_grad.shape[1]
    (
        down_grad,
        gate_grad,
        up_grad,
        output,
        d_hidden,
        d_table,
        out_grad,
        in_grad,
        fg_grad,
        gt_grad,
    ) = hand_over(
        (down_grad, pair_grad, output, d_hidden, d_table, out_grad, rest_grad),
        (
            (0, 0, block),
            (1, 0, units),
            (1, units, units),
            (2, 0, width),
            (3, 0, width),
            (4, 0, width),
            (5, 0, block),
            (6, 0, chans),
            (6, chans, chans),
            (6, 2 * chans, chans),
        ),
    )
    return (
        output[None],
        d_hidden[None],
        in_grad,
        fg_grad,
        gt_grad,
        out_grad,
        sums[0],
        sums[2],
        sums[1],
        d_table,
        gate_grad,
        up_grad,
        down_grad,
    )


def fits_plane(mesh):
    return mesh.shape["fsdp"] == 4 and mesh.shape["seq"] % 2 == 0


def solution(mesh):
    rows_spec = P("fsdp", "seq", None)
    columns = P(None, "fsdp")
    placed = (
        rows_spec,
        P(),
        columns,
        columns,
        columns,
        P("fsdp", None),
        P(),
        P(),
        P(),
        P(),
        columns,
        columns,
        P("fsdp", None),
        rows_spec,
    )
    by_rows, by_columns = P("seq", "fsdp"), P("fsdp", "seq")
    return jax.shard_map(
        plane_device if fits_plane(mesh) else per_device,
        mesh=mesh,
        in_specs=placed,
        out_specs=(
            rows_spec,
            rows_spec,
            by_rows,
            by_rows,
            by_rows,
            by_columns,
            P(),
            P(),
            P(),
            P(),
            by_rows,
            by_rows,
            by_columns,
        ),
        check_vma=False,
    )
```

```python
import functools

import jax
import jax.numpy as jnp
from jax import lax
from jax.experimental import pallas as pl
from jax.experimental.pallas import tpu as pltpu
from jax.sharding import PartitionSpec as P

LAYER = 12
MESH = pl.DeviceIdType.MESH
F32 = jnp.float32
BF16 = jnp.bfloat16

epsilon = 1e-06

VMEM = pl.BlockSpec(memory_space=pltpu.VMEM)
ANY = pl.BlockSpec(memory_space=pl.ANY)


def lower_bound(table):
    soft = jax.nn.softmax(table, axis=0)
    totals = jnp.cumsum(soft, axis=0)
    return totals[LAYER] - totals[0]


def silu_slope(value, sigma):
    return sigma * (1.0 + value * (1.0 - sigma))


def params(collective_id):
    return pltpu.CompilerParams(
        collective_id=collective_id, has_side_effects=True, vmem_limit_bytes=56 << 20
    )


def round_up(value, unit):
    return -(-value // unit) * unit


def plane():
    s = lax.axis_index("seq")
    f = lax.axis_index("fsdp")
    y, x = f // 2, f % 2
    fx = y * 2 + (1 - x)
    fy = (1 - y) * 2 + x
    fd = (1 - y) * 2 + (1 - x)
    return s, f, fx, fy, fd


def enter(devices):
    barrier = pltpu.get_barrier_semaphore()
    for device in devices:
        pl.semaphore_signal(barrier, inc=1, device_id=device, device_id_type=MESH)
    pl.semaphore_wait(barrier, len(devices))


def remote(src, dst, send, recv, device):
    return pltpu.make_async_remote_copy(
        src_ref=src,
        dst_ref=dst,
        send_sem=send,
        recv_sem=recv,
        device_id=device,
        device_id_type=MESH,
    )


def gather(x, small, collective_id):
    return lax.all_gather(x, "fsdp"), lax.all_gather(small, "fsdp")


def reduce_rows(p, small, collective_id):
    total = lax.psum_scatter(p, "fsdp", scatter_dimension=0, tiled=True)[0]
    return total.astype(F32), lax.psum(small, "fsdp")


def start_exchange(total, gathered, send, recv, n_seq):
    s = lax.axis_index("seq")
    f = lax.axis_index("fsdp")
    copies = []
    for k in range(1, n_seq):
        peer = lax.rem(s + k, n_seq)
        copy = remote(total, gathered.at[s], send.at[k], recv.at[k], (peer, f))
        copy.start()
        copies.append(copy)
    gathered[pl.ds(s, 1)] = total[...][None]
    return copies


def seq_peers(n_seq):
    s = lax.axis_index("seq")
    f = lax.axis_index("fsdp")
    return [(lax.rem(s + k, n_seq), f) for k in range(1, n_seq)]


def lane_blocks(groups, chans):
    return [(g, slice(c, c + 128)) for g in range(groups) for c in range(0, chans, 128)]


def forward_scan_kernel(
    n_seq, in_raw, forget_raw, bounds, keep, state_b, before, a_ref, b_ref, total, gathered, send, recv
):
    groups, rows, chans = in_raw.shape
    part = rows // 8
    blocks = lane_blocks(groups, chans)
    s = lax.axis_index("seq")
    barrier = pltpu.get_barrier_semaphore()
    for peer in seq_peers(n_seq):
        pl.semaphore_signal(barrier, inc=1, device_id=peer, device_id_type=MESH)
    for n, (g, lanes) in enumerate(blocks):
        bound = bounds[:, lanes]
        forget = bound + (1.0 - bound) * jax.nn.sigmoid(forget_raw[g, :, lanes].astype(F32))
        value = in_raw[g, :, lanes].astype(F32)
        a_ref[n] = forget * keep[g]
        b_ref[n] = value * jax.nn.sigmoid(value) * (1.0 - forget)

    def step(i, carry):
        new = []
        at = pl.ds(i, 8, stride=part)
        for n, (product, state) in enumerate(carry):
            a = a_ref[n, at, :]
            state = a * state + b_ref[n, at, :]
            product = product * a
            a_ref[n, at, :] = product
            b_ref[n, at, :] = state
            new.append((product, state))
        return tuple(new)

    start = tuple((jnp.ones((8, 128), F32), jnp.zeros((8, 128), F32)) for _ in blocks)
    ends = lax.fori_loop(0, part, step, start)
    for n, (product, state) in enumerate(ends):
        p_all, s_all = product[0:1], state[0:1]
        for j in range(1, 8):
            p_all, s_all = p_all * product[j : j + 1], state[j : j + 1] + product[j : j + 1] * s_all
        total[2 * n : 2 * n + 1] = p_all
        total[2 * n + 1 : 2 * n + 2] = s_all
    pl.semaphore_wait(barrier, n_seq - 1)
    copies = start_exchange(total, gathered, send, recv, n_seq)
    for copy in copies:
        copy.wait()
    for n, (g, lanes) in enumerate(blocks):
        carry = jnp.zeros((1, 128), F32)
        for j in range(n_seq - 1):
            p_j = gathered[j, 2 * n : 2 * n + 1]
            s_j = gathered[j, 2 * n + 1 : 2 * n + 2]
            carry = jnp.where(j < s, s_j + p_j * carry, carry)
        before[g, 0:1, lanes] = carry
        product, state = ends[n]
        carries = [carry]
        for j in range(7):
            carries.append(state[j : j + 1] + product[j : j + 1] * carries[-1])
        for j in range(8):
            at = slice(j * part, (j + 1) * part)
            b_ref[n, at] = b_ref[n, at] + a_ref[n, at] * carries[j]
        state_b[g, :, lanes] = b_ref[n].astype(BF16)
        before[g, 1:rows, lanes] = b_ref[n, 0 : rows - 1]


def forward_scan(in_raw, forget_raw, bounds, keep, collective_id):
    n_seq = lax.axis_size("seq")
    groups, rows, chans = in_raw.shape
    blocks = groups * chans // 128
    return pl.pallas_call(
        functools.partial(forward_scan_kernel, n_seq),
        out_shape=(
            jax.ShapeDtypeStruct(in_raw.shape, BF16),
            jax.ShapeDtypeStruct(in_raw.shape, F32),
        ),
        in_specs=[VMEM] * 4,
        out_specs=(VMEM, VMEM),
        scratch_shapes=[
            pltpu.VMEM((blocks, rows, 128), F32),
            pltpu.VMEM((blocks, rows, 128), F32),
            pltpu.VMEM((2 * blocks, 128), F32),
            pltpu.VMEM((n_seq, 2 * blocks, 128), F32),
            pltpu.SemaphoreType.DMA((n_seq,)),
            pltpu.SemaphoreType.DMA((n_seq,)),
        ],
        compiler_params=params(collective_id),
        name="forward_scan",
    )(in_raw, forget_raw, bounds, keep)


def backward_scan_kernel(
    n_seq,
    d_state,
    in_raw,
    forget_raw,
    before,
    bounds,
    keep,
    d_in,
    d_forget_raw,
    d_bounds,
    p_ref,
    q_ref,
    total,
    gathered,
    send,
    recv,
):
    groups, rows, chans = in_raw.shape
    part = rows // 8
    blocks = lane_blocks(groups, chans)
    s = lax.axis_index("seq")
    barrier = pltpu.get_barrier_semaphore()
    for peer in seq_peers(n_seq):
        pl.semaphore_signal(barrier, inc=1, device_id=peer, device_id_type=MESH)
    for n, (g, lanes) in enumerate(blocks):
        bound = bounds[:, lanes]
        forget = bound + (1.0 - bound) * jax.nn.sigmoid(forget_raw[g, :, lanes].astype(F32))
        p_ref[n] = forget * keep[g]
        q_ref[n] = d_state[g, :, lanes].astype(F32)

    def step(i, carry):
        new = []
        at = pl.ds(part - 1 - i, 8, stride=part)
        for n, (product, message) in enumerate(carry):
            a = p_ref[n, at, :]
            acc = q_ref[n, at, :] + message
            p_ref[n, at, :] = product
            q_ref[n, at, :] = acc
            new.append((product * a, a * acc))
        return tuple(new)

    start = tuple((jnp.ones((8, 128), F32), jnp.zeros((8, 128), F32)) for _ in blocks)
    ends = lax.fori_loop(0, part, step, start)
    for n, (product, message) in enumerate(ends):
        p_all, m_all = product[7:8], message[7:8]
        for j in range(6, -1, -1):
            p_all, m_all = p_all * product[j : j + 1], message[j : j + 1] + product[j : j + 1] * m_all
        total[2 * n : 2 * n + 1] = p_all
        total[2 * n + 1 : 2 * n + 2] = m_all
    pl.semaphore_wait(barrier, n_seq - 1)
    copies = start_exchange(total, gathered, send, recv, n_seq)
    for copy in copies:
        copy.wait()
    d_bounds[...] = jnp.zeros((1, chans), F32)
    for n, (g, lanes) in enumerate(blocks):
        carry = jnp.zeros((1, 128), F32)
        for j in range(n_seq - 1, 0, -1):
            p_j = gathered[j, 2 * n : 2 * n + 1]
            m_j = gathered[j, 2 * n + 1 : 2 * n + 2]
            carry = jnp.where(j > s, m_j + p_j * carry, carry)
        product, message = ends[n]
        carries = [carry]
        for j in range(7, 0, -1):
            carries.append(message[j : j + 1] + product[j : j + 1] * carries[-1])
        carries = carries[::-1]
        for j in range(8):
            at = slice(j * part, (j + 1) * part)
            q_ref[n, at] = q_ref[n, at] + p_ref[n, at] * carries[j]
        acc = q_ref[n]
        bound = bounds[:, lanes]
        sigma_f = jax.nn.sigmoid(forget_raw[g, :, lanes].astype(F32))
        forget = bound + (1.0 - bound) * sigma_f
        value = in_raw[g, :, lanes].astype(F32)
        sigma_i = jax.nn.sigmoid(value)
        d_forget = acc * (before[g, :, lanes] * keep[g] - value * sigma_i)
        d_in[g, :, lanes] = (acc * (1.0 - forget) * silu_slope(value, sigma_i)).astype(BF16)
        d_sigma = d_forget * (1.0 - sigma_f)
        d_forget_raw[g, :, lanes] = (d_sigma * (1.0 - bound) * sigma_f).astype(BF16)
        d_bounds[:, lanes] += jnp.sum(d_sigma, 0, keepdims=True)


def backward_scan(d_state, in_raw, forget_raw, before, bounds, keep, collective_id):
    n_seq = lax.axis_size("seq")
    groups, rows, chans = in_raw.shape
    blocks = groups * chans // 128
    return pl.pallas_call(
        functools.partial(backward_scan_kernel, n_seq),
        out_shape=(
            jax.ShapeDtypeStruct(in_raw.shape, BF16),
            jax.ShapeDtypeStruct(in_raw.shape, BF16),
            jax.ShapeDtypeStruct((1, chans), F32),
        ),
        in_specs=[VMEM] * 6,
        out_specs=(VMEM, VMEM, VMEM),
        scratch_shapes=[
            pltpu.VMEM((blocks, rows, 128), F32),
            pltpu.VMEM((blocks, rows, 128), F32),
            pltpu.VMEM((2 * blocks, 128), F32),
            pltpu.VMEM((n_seq, 2 * blocks, 128), F32),
            pltpu.SemaphoreType.DMA((n_seq,)),
            pltpu.SemaphoreType.DMA((n_seq,)),
        ],
        compiler_params=params(collective_id),
        name="backward_scan",
    )(d_state, in_raw, forget_raw, before, bounds, keep)


def sum_all_kernel(n_seq, n_fsdp, x, out, middle, over_seq, over_fsdp, send, recv):
    s = lax.axis_index("seq")
    f = lax.axis_index("fsdp")
    along = [(lax.rem(s + k, n_seq), f) for k in range(1, n_seq)]
    across = [(s, lax.rem(f + k, n_fsdp)) for k in range(1, n_fsdp)]
    enter(along + across)
    copies = []
    for k, peer in enumerate(along):
        copy = remote(x, over_seq.at[k], send.at[k], recv.at[k], peer)
        copy.start()
        copies.append(copy)
    total = x[...]
    for k, copy in enumerate(copies):
        copy.wait_recv()
        total = total + over_seq[k]
    middle[...] = total
    later = []
    for k, peer in enumerate(across):
        slot = n_seq - 1 + k
        copy = remote(middle, over_fsdp.at[k], send.at[slot], recv.at[slot], peer)
        copy.start()
        later.append(copy)
    for k, copy in enumerate(later):
        copy.wait_recv()
        total = total + over_fsdp[k]
    out[...] = total
    for copy in copies + later:
        copy.wait_send()


def sum_all(x, collective_id):
    n_seq, n_fsdp = lax.axis_size("seq"), lax.axis_size("fsdp")
    count = n_seq + n_fsdp - 2
    return pl.pallas_call(
        functools.partial(sum_all_kernel, n_seq, n_fsdp),
        out_shape=jax.ShapeDtypeStruct(x.shape, F32),
        in_specs=[VMEM],
        out_specs=VMEM,
        scratch_shapes=[
            pltpu.VMEM(x.shape, F32),
            pltpu.VMEM((n_seq - 1,) + x.shape, F32),
            pltpu.VMEM((n_fsdp - 1,) + x.shape, F32),
            pltpu.SemaphoreType.DMA((count,)),
            pltpu.SemaphoreType.DMA((count,)),
        ],
        compiler_params=params(collective_id),
        name="sum_all",
    )(x)


def sum_over_seq(part):
    return lax.psum_scatter(part.astype(BF16), "seq", scatter_dimension=0, tiled=True).astype(F32)


def per_device(
    hidden,
    lengths,
    w_input,
    w_forget,
    w_gate_out,
    w_output,
    norm_gain,
    gate_gain,
    glu_gain,
    lower_table,
    w_glu_gate,
    w_glu_up,
    w_glu_down,
    cotangent,
):
    seq_index = lax.axis_index("seq")
    fsdp_index = lax.axis_index("fsdp")
    groups = lax.axis_size("fsdp")
    _, rows, width = hidden.shape
    chans = w_input.shape[1]
    units = w_glu_gate.shape[1]
    tokens = groups * rows
    small_shape = (round_up(groups, 8), round_up(rows, 128))

    def to_small(value):
        return jnp.pad(
            value, ((0, small_shape[0] - value.shape[0]), (0, small_shape[1] - value.shape[1]))
        )

    def dot(left, right):
        return jnp.dot(left, right, preferred_element_type=F32)

    def dot_t(left, right):
        return lax.dot_general(left, right, (((1,), (1,)), ((), ())), preferred_element_type=F32)

    def over_tokens(left, right):
        return lax.dot_general(left, right, (((0,), (0,)), ((), ())), preferred_element_type=F32)

    cotangent_all = lax.all_gather(cotangent[0], "fsdp").reshape(tokens, width)

    hidden_f = hidden[0].astype(F32)
    scale_one = lax.rsqrt(jnp.mean(hidden_f * hidden_f, -1, keepdims=True) + epsilon)
    normed = (hidden_f * scale_one * norm_gain).astype(BF16)
    normed_all, _ = gather(normed, jnp.zeros((8, 128), F32), 0)
    normed_all = normed_all.reshape(tokens, width)
    in_raw = dot(normed_all, w_input).astype(BF16).reshape(groups, rows, chans)
    forget_raw = dot(normed_all, w_forget).astype(BF16).reshape(groups, rows, chans)
    gate_raw = dot(normed_all, w_gate_out)

    bounds_full = lower_bound(lower_table)
    bounds = lax.dynamic_slice_in_dim(bounds_full, fsdp_index * chans, chans)[None]
    seq_starts = jnp.cumsum(lengths, axis=1) - lengths
    places = seq_index * rows + jnp.arange(rows, dtype=jnp.int32)
    starts = jnp.any(places[None, :, None] == seq_starts[:, None, :], axis=-1)
    keep = jnp.where(starts, 0.0, 1.0).astype(F32)[:, :, None]
    state_b, before = forward_scan(in_raw, forget_raw, bounds, keep, 1)

    state_f = state_b.astype(F32).reshape(tokens, chans)
    gain_slice = lax.dynamic_slice_in_dim(gate_gain, fsdp_index * chans, chans)
    sigma_g = jax.nn.sigmoid(gate_raw)
    silu_gate = gate_raw * sigma_g
    out_raw = (state_f * gain_slice * silu_gate).astype(BF16)
    squares = jnp.sum(state_f * state_f, -1).reshape(groups, rows)
    mixed_part = dot(out_raw, w_output).astype(BF16).reshape(groups, rows, width)
    mixed_raw, square_sum = reduce_rows(mixed_part, to_small(squares), 2)
    state_scale = lax.rsqrt(square_sum[:groups, :rows] / width + epsilon)
    own_scale = lax.dynamic_slice_in_dim(state_scale, fsdp_index, 1, 0)[0][:, None]
    scale_g = state_scale.reshape(tokens, 1)
    middle = hidden_f + own_scale * mixed_raw
    scale_two = lax.rsqrt(jnp.mean(middle * middle, -1, keepdims=True) + epsilon)
    normed_two = (middle * scale_two * glu_gain).astype(BF16)
    normed_two_all, _ = gather(normed_two, jnp.zeros((8, 128), F32), 3)
    normed_two_all = normed_two_all.reshape(tokens, width)

    gate_val = dot(normed_two_all, w_glu_gate)
    up_val = dot(normed_two_all, w_glu_up)
    sigma_u = jax.nn.sigmoid(gate_val)
    silu_u = gate_val * sigma_u
    activity = (silu_u * up_val).astype(BF16)
    down_grad = sum_over_seq(over_tokens(cotangent_all, activity))
    d_act = dot_t(cotangent_all, w_glu_down)
    d_gate = (d_act * up_val * silu_slope(gate_val, sigma_u)).astype(BF16)
    d_up = (d_act * silu_u).astype(BF16)
    pair_grad = sum_over_seq(
        jnp.concatenate(
            [
                over_tokens(normed_two_all, d_gate).astype(BF16),
                over_tokens(normed_two_all, d_up).astype(BF16),
            ],
            1,
        )
    )
    d_two_part = (dot_t(d_gate, w_glu_gate) + dot_t(d_up, w_glu_up)).astype(BF16)
    no_small = jnp.zeros((8, 128), F32)
    d_normed_two, _ = reduce_rows(d_two_part.reshape(groups, rows, width), no_small, 4)
    glu_part = dot(activity, w_glu_down).astype(BF16).reshape(groups, rows, width)
    glu_result = lax.psum_scatter(glu_part, "fsdp", scatter_dimension=0, tiled=True)[0]
    output = (middle + glu_result.astype(F32)).astype(BF16)[None]

    cotangent_f = cotangent[0].astype(F32)
    scaled_two = glu_gain * d_normed_two
    d_middle = (
        cotangent_f
        + scale_two * scaled_two
        - middle * scale_two**3 * jnp.mean(scaled_two * middle, -1, keepdims=True)
    )
    d_glu_gain = jnp.sum(d_normed_two * middle * scale_two, 0)
    d_mixed = d_middle.astype(BF16)
    own_dot = jnp.sum(d_mixed.astype(F32) * mixed_raw, -1)[None]
    d_mixed_all, dots = gather(d_mixed, to_small(own_dot), 5)
    d_mixed_all = d_mixed_all.reshape(tokens, width)
    dot_rows = dots[:, 0, :rows].reshape(tokens, 1)

    d_out = dot_t(d_mixed_all, w_output)
    scaled_state = state_f * scale_g
    d_gain_slice = jnp.sum(d_out * scaled_state * silu_gate, 0)
    d_scaled = d_out * gain_slice * silu_gate
    d_gate_raw = (d_out * scaled_state * gain_slice * silu_slope(gate_raw, sigma_g)).astype(BF16)
    d_state = scale_g * d_scaled - state_f * (scale_g**3 * (dot_rows / width))
    d_state = d_state.astype(BF16).reshape(groups, rows, chans)
    d_in, d_forget_raw, d_bounds = backward_scan(
        d_state, in_raw, forget_raw, before, bounds, keep, 6
    )
    d_in = d_in.reshape(tokens, chans)
    d_forget_raw = d_forget_raw.reshape(tokens, chans)

    d_normed_part = dot_t(d_in, w_input) + dot_t(d_forget_raw, w_forget)
    d_normed_part = (d_normed_part + dot_t(d_gate_raw, w_gate_out)).astype(BF16)
    out_gate = (out_raw.astype(F32) * scale_g).astype(BF16)
    mixer_grad = sum_over_seq(
        jnp.concatenate(
            [
                over_tokens(d_mixed_all, out_gate).astype(BF16),
                over_tokens(normed_all, d_in).astype(BF16),
                over_tokens(normed_all, d_forget_raw).astype(BF16),
                over_tokens(normed_all, d_gate_raw).astype(BF16),
            ],
            1,
        )
    )
    d_normed, _ = reduce_rows(d_normed_part.reshape(groups, rows, width), no_small, 7)
    scaled_one = norm_gain * d_normed
    d_hidden = (
        d_middle
        + scale_one * scaled_one
        - hidden_f * scale_one**3 * jnp.mean(scaled_one * hidden_f, -1, keepdims=True)
    )
    d_norm_gain = jnp.sum(d_normed * hidden_f * scale_one, 0)
    d_gain_full = lax.dynamic_update_slice(
        jnp.zeros((width,), F32), d_gain_slice, (fsdp_index * chans,)
    )
    d_bounds_full = lax.dynamic_update_slice(
        jnp.zeros((width,), F32), d_bounds[0], (fsdp_index * chans,)
    )
    sums = jnp.stack([d_norm_gain, d_glu_gain, d_gain_full, d_bounds_full])
    totals = sum_all(sums.reshape(8, width // 2), 8).reshape(4, width)
    _, bounds_pull = jax.vjp(lower_bound, lower_table)
    d_table = bounds_pull(totals[3])[0]
    return (
        output,
        d_hidden.astype(BF16)[None],
        mixer_grad[:, chans : 2 * chans],
        mixer_grad[:, 2 * chans : 3 * chans],
        mixer_grad[:, 3 * chans :],
        mixer_grad[:, :chans].T,
        totals[0],
        totals[2],
        totals[1],
        d_table,
        pair_grad[:, :units],
        pair_grad[:, units:],
        down_grad.T,
    )


def copy_in(src, dst, sem):
    copy = pltpu.make_async_copy(src, dst, sem)
    copy.start()
    return copy


class Links:
    def __init__(self, send, recv):
        self.send, self.recv, self.used = send, recv, 0

    def start(self, src, dst, device):
        copy = remote(src, dst, self.send.at[self.used], self.recv.at[self.used], device)
        self.used += 1
        copy.start()
        return copy


class Locals:
    def __init__(self, sems):
        self.sems, self.used = sems, 0

    def start(self, src, dst):
        copy = copy_in(src, dst, self.sems.at[self.used])
        self.used += 1
        return copy


def row_slots(rows):
    half = rows // 2
    top = [pl.ds(k * rows, half) for k in range(4)]
    bottom = [pl.ds(k * rows + half, half) for k in range(4)]
    return top, bottom


def gather_start(links, src, dst, rows, s, fx, fy):
    half = rows // 2
    top, bottom = row_slots(rows)
    here = (pl.ds(0, half), pl.ds(half, half))
    return [
        links.start(src.at[here[0]], dst.at[top[1]], (s, fx)),
        links.start(src.at[here[1]], dst.at[bottom[2]], (s, fy)),
        links.start(src.at[here[1]], dst.at[bottom[1]], (s, fx)),
        links.start(src.at[here[0]], dst.at[top[2]], (s, fy)),
    ]


def gather_forward(links, own, dst, rows, s, fx, fy):
    top, bottom = row_slots(rows)
    own[0].wait_recv()
    on_y = links.start(dst.at[top[1]], dst.at[top[3]], (s, fy))
    own[1].wait_recv()
    on_x = links.start(dst.at[bottom[2]], dst.at[bottom[3]], (s, fx))
    return [on_y, on_x]


def gather_middle(own):
    own[2].wait_recv()
    own[3].wait_recv()


def gather_far(later):
    for copy in later:
        copy.wait_recv()


def sends_done(*lists):
    for copies in lists:
        for copy in copies:
            copy.wait_send()


def wait_all(*lists):
    for copies in lists:
        for copy in copies:
            copy.wait()


def reduce_start_far(links, part, from_x, from_y, rows, s, fx, fy):
    top, bottom = row_slots(rows)
    return [
        links.start(part.at[top[3]], from_x.at[0], (s, fx)),
        links.start(part.at[bottom[3]], from_y.at[0], (s, fy)),
    ]


def reduce_start_near(links, part, from_x, from_y, rows, s, fx, fy):
    top, bottom = row_slots(rows)
    return [
        links.start(part.at[top[1]], from_x.at[1], (s, fx)),
        links.start(part.at[bottom[2]], from_y.at[1], (s, fy)),
    ]


def reduce_pass(links, far, part, from_x, from_y, pass_x, pass_y, rows, s, fx, fy):
    top, bottom = row_slots(rows)
    far[0].wait_recv()
    pass_y[...] = (from_x[0].astype(F32) + part[top[2]].astype(F32)).astype(BF16)
    on_y = links.start(pass_y, from_y.at[2], (s, fy))
    far[1].wait_recv()
    pass_x[...] = (from_y[0].astype(F32) + part[bottom[1]].astype(F32)).astype(BF16)
    on_x = links.start(pass_x, from_x.at[2], (s, fx))
    return [on_y, on_x]


def mm(left, right):
    return jnp.dot(left, right, preferred_element_type=F32)


def mm_t(left, right):
    return lax.dot_general(left, right, (((1,), (1,)), ((), ())), preferred_element_type=F32)


def tile(n, width):
    return pl.ds(pl.multiple_of(n * width, width), width)


def bounds_slice(table, first, count):
    rows = table[:, pl.ds(pl.multiple_of(first, 128), count)]
    powers = jnp.exp(rows - jnp.max(rows, 0, keepdims=True))
    return jnp.sum(powers[1 : LAYER + 1], 0, keepdims=True) / jnp.sum(powers, 0, keepdims=True)


def keep_rows(lengths, group, first, rows):
    places = first + lax.broadcasted_iota(jnp.int32, (rows, 128), 0)
    start = jnp.int32(0)
    keep = jnp.where(places == start, 0.0, 1.0)
    for i in range(lengths.shape[1] - 1):
        start = start + lengths[group, i]
        keep = jnp.where(places == start, 0.0, keep)
    return keep.astype(F32)


def segment_totals(end_p, end_s, blocks, order):
    first, rest = order[0], order[1:]
    p_all = end_p[pl.ds(first, blocks, stride=8), :]
    s_all = end_s[pl.ds(first, blocks, stride=8), :]
    for j in rest:
        p_j = end_p[pl.ds(j, blocks, stride=8), :]
        s_all = end_s[pl.ds(j, blocks, stride=8), :] + p_j * s_all
        p_all = p_all * p_j
    return p_all, s_all


def spread_carry(carry, carr, end_p, end_s, blocks, order):
    for i, j in enumerate(order):
        carr[pl.ds(j, blocks, stride=8), :] = carry
        if i < 7:
            carry = end_s[pl.ds(j, blocks, stride=8), :] + end_p[pl.ds(j, blocks, stride=8), :] * carry


def mixer_kernel(
    n_seq,
    lengths,
    hidden,
    cot,
    norm_gain,
    gate_gain,
    glu_gain,
    table,
    w_in,
    w_fg,
    w_gt,
    w_out,
    normed_half,
    cot_out,
    in_out,
    fg_out,
    gate_out,
    state_out,
    raw_out,
    before_out,
    scale_out,
    middle,
    two,
    wv,
    wo,
    rows_all,
    stage,
    in_ref,
    fg_ref,
    gate_ref,
    a_ref,
    b_ref,
    shifted,
    keep_ref,
    end_p,
    end_s,
    carr,
    total,
    gathered,
    state_ref,
    raw_ref,
    squares,
    squares_t,
    packed,
    squares_in,
    part,
    from_x,
    from_y,
    pass_x,
    pass_y,
    send,
    recv,
    exchange_send,
    exchange_recv,
    local_sems,
):
    rows, width = hidden.shape
    chans = w_in.shape[1]
    lanes_of = [slice(c, c + 128) for c in range(0, chans, 128)]
    count = len(lanes_of)
    blocks = 4 * count
    step_len = rows // 8
    s, f, fx, fy, fd = plane()
    groups = [f, fx, fy, fd]
    links, local = Links(send, recv), Locals(local_sems)

    weights = [
        local.start(w, wv.at[:, pl.ds(i * chans, chans)]) for i, w in enumerate((w_in, w_fg, w_gt))
    ]
    weights.append(local.start(w_out, wo))
    barrier = pltpu.get_barrier_semaphore()
    peers = [(s, fx), (s, fy), (s, fd)] + seq_peers(n_seq)
    for peer in peers:
        pl.semaphore_signal(barrier, inc=1, device_id=peer, device_id_type=MESH)

    def norm_rows(i, _):
        at = pl.ds(pl.multiple_of(i * 16, 16), 16)
        value = hidden[at].astype(F32)
        scale = lax.rsqrt(jnp.mean(value * value, -1, keepdims=True) + epsilon)
        rows_all[at] = (value * scale * norm_gain[...]).astype(BF16)
        return 0

    lax.fori_loop(0, rows // 16, norm_rows, 0)
    pl.semaphore_wait(barrier, len(peers))
    own = gather_start(links, rows_all, rows_all, rows, s, fx, fy)
    bound = bounds_slice(table, f * chans, chans)
    for k in range(4):
        keep_ref[k] = keep_rows(lengths, groups[k], s * rows, rows)
    squares[...] = jnp.zeros_like(squares)
    squares_t[...] = jnp.zeros_like(squares_t)
    for copy in weights[:3]:
        copy.wait()

    def project(first, slots):
        def tile_of(n, _):
            cols = tile(n, 256)
            stage[: slots * rows, cols] = mm(
                rows_all[first * rows : (first + slots) * rows], wv[:, cols]
            )
            return 0

        lax.fori_loop(0, 3 * chans // 256, tile_of, 0)
        for k in range(slots):
            at = slice(k * rows, (k + 1) * rows)
            for c, lanes in enumerate(lanes_of):
                n = (first + k) * count + c
                value = stage[at, lanes].astype(BF16)
                in_ref[first + k, :, lanes] = value
                value = value.astype(F32)
                raw = stage[at, chans + c * 128 : chans + (c + 1) * 128].astype(BF16)
                fg_ref[first + k, :, lanes] = raw
                edge = bound[:, lanes]
                forget = edge + (1.0 - edge) * jax.nn.sigmoid(raw.astype(F32))
                a_ref[n] = forget * keep_ref[first + k]
                b_ref[n] = value * jax.nn.sigmoid(value) * (1.0 - forget)
            gate_ref[first + k] = stage[at, 2 * chans :]

    project(0, 1)
    later = gather_forward(links, own, rows_all, rows, s, fx, fy)
    gather_middle(own)
    project(1, 2)
    gather_far(later)
    cot_own = gather_start(links, cot, cot_out, rows, s, fx, fy)
    core = s % 2
    swaps, outs = swap_columns(
        links, local, rows_all, normed_half, n_seq, core, (s + 1 - 2 * core, f)
    )
    outs.append(local.start(cot, cot_out.at[pl.ds(0, rows)]))
    project(3, 1)
    outs += [
        local.start(in_ref, in_out),
        local.start(fg_ref, fg_out),
        local.start(gate_ref, gate_out),
    ]

    def scan_step(i, carry):
        new = []
        at = pl.ds(i, 8, stride=step_len)
        for n, (product, state) in enumerate(carry):
            a = a_ref[n, at, :]
            state = a * state + b_ref[n, at, :]
            product = product * a
            a_ref[n, at, :] = product
            b_ref[n, at, :] = state
            new.append((product, state))
        return tuple(new)

    start = tuple((jnp.ones((8, 128), F32), jnp.zeros((8, 128), F32)) for _ in range(blocks))
    ends = lax.fori_loop(0, step_len, scan_step, start)
    for n, (product, state) in enumerate(ends):
        end_p[8 * n : 8 * n + 8] = product
        end_s[8 * n : 8 * n + 8] = state
    p_all, s_all = segment_totals(end_p, end_s, blocks, range(8))
    total[:blocks] = p_all
    total[blocks:] = s_all
    copies = start_exchange(total, gathered, exchange_send, exchange_recv, n_seq)
    wait_all(copies)
    carry = jnp.zeros((blocks, 128), F32)
    for j in range(n_seq - 1):
        carry = jnp.where(j < s, gathered[j, blocks:] + gathered[j, :blocks] * carry, carry)
    for n in range(blocks):
        shifted[n, 0:1] = carry[n : n + 1]
    spread_carry(carry, carr, end_p, end_s, blocks, range(8))

    def finish(n, _):
        enter_state = carr[pl.ds(pl.multiple_of(n * 8, 8), 8)]
        for i in range(step_len):
            at = pl.ds(i, 8, stride=step_len)
            state = b_ref[n, at, :] + a_ref[n, at, :] * enter_state
            b_ref[n, at, :] = state
            shifted[n, pl.ds(i + 1, 8, stride=step_len), :] = state
        return 0

    lax.fori_loop(0, blocks, finish, 0)
    outs.append(local.start(shifted.at[:, pl.ds(0, rows)], before_out))

    lane = lax.broadcasted_iota(jnp.int32, (rows, 128), 1)
    for k in (3, 1, 2, 0):
        square = jnp.zeros((rows, 1), F32)
        for c, lanes in enumerate(lanes_of):
            state_b = b_ref[k * count + c].astype(BF16)
            state_ref[k, :, lanes] = state_b
            state = state_b.astype(F32)
            square = square + jnp.sum(state * state, -1, keepdims=True)
            gate = gate_ref[k, :, lanes]
            gain = gate_gain[:, pl.ds(pl.multiple_of(f * chans + c * 128, 128), 128)]
            raw_ref[k * rows : (k + 1) * rows, lanes] = (
                state * gain * gate * jax.nn.sigmoid(gate)
            ).astype(BF16)
        squares[:rows] = jnp.where(lane == groups[k], square, squares[:rows])
    packed[...] = squares[...].T[:8]
    square_copies = [
        links.start(packed, squares_in.at[i], (s, peer)) for i, peer in enumerate((fx, fy, fd))
    ]
    outs += [local.start(state_ref, state_out), local.start(raw_ref, raw_out)]
    cot_later = gather_forward(links, cot_own, cot_out, rows, s, fx, fy)
    weights[3].wait()

    def output_part(first, slots):
        at = slice(first * rows, (first + slots) * rows)

        def tile_of(n, _):
            cols = tile(n, 512)
            part[at, cols] = mm(raw_ref[at], wo[:, cols]).astype(BF16)
            return 0

        lax.fori_loop(0, width // 512, tile_of, 0)

    output_part(3, 1)
    far = reduce_start_far(links, part, from_x, from_y, rows, s, fx, fy)
    output_part(1, 2)
    near = reduce_start_near(links, part, from_x, from_y, rows, s, fx, fy)
    output_part(0, 1)
    passed = reduce_pass(links, far, part, from_x, from_y, pass_x, pass_y, rows, s, fx, fy)
    for copy in square_copies:
        copy.wait_recv()
    all_squares = (packed[...] + squares_in[0]) + (squares_in[1] + squares_in[2])
    squares_t[:8] = lax.rsqrt(all_squares / width + epsilon)
    scales = squares_t[...].T[:rows]
    for k in range(4):
        scale_out[k] = jnp.sum(jnp.where(lane == groups[k], scales, 0.0), -1, keepdims=True)
    for copy in near + passed:
        copy.wait_recv()
    half = rows // 2
    for first, one, other in ((0, from_x.at[1], from_y.at[2]), (half, from_y.at[1], from_x.at[2])):

        def sum_rows(i, _):
            here = pl.ds(pl.multiple_of(i * 16, 16), 16)
            at = pl.ds(pl.multiple_of(first + i * 16, 16), 16)
            mixed = part[at].astype(F32) + one[here].astype(F32) + other[here].astype(F32)
            value = hidden[at].astype(F32) + scale_out[0, at] * mixed
            middle[at] = value
            scale = lax.rsqrt(jnp.mean(value * value, -1, keepdims=True) + epsilon)
            two[at] = (value * scale * glu_gain[...]).astype(BF16)
            return 0

        lax.fori_loop(0, half // 16, sum_rows, 0)
    gather_middle(cot_own)
    gather_far(cot_later)
    sends_done(own, later, cot_own, cot_later, square_copies, far, near, passed)
    wait_all(swaps, outs)


def mixer_forward(lengths, hidden, cot, gains, table, weights, collective_id):
    n_seq = lax.axis_size("seq")
    rows, width = hidden.shape
    chans = weights[0].shape[1]
    blocks = 4 * chans // 128
    tokens = 4 * rows
    half = rows // 2
    shape = jax.ShapeDtypeStruct
    wide = shape((tokens, width), BF16)
    narrow = shape((4, rows, chans), BF16)
    long_rows = round_up(rows, 128)
    return pl.pallas_call(
        functools.partial(mixer_kernel, n_seq),
        out_shape=(
            shape((2, tokens, width // 2), BF16),
            wide,
            narrow,
            narrow,
            shape((4, rows, chans), F32),
            narrow,
            shape((tokens, chans), BF16),
            shape((blocks, rows, 128), F32),
            shape((4, rows, 1), F32),
            shape((rows, width), F32),
            shape((rows, width), BF16),
        ),
        in_specs=[pl.BlockSpec(memory_space=pltpu.SMEM), VMEM, VMEM, VMEM, VMEM, VMEM, VMEM]
        + [ANY] * 4,
        out_specs=(ANY,) * 8 + (VMEM,) * 3,
        scratch_shapes=[
            pltpu.VMEM((width, 3 * chans), BF16),
            pltpu.VMEM((chans, width), BF16),
            pltpu.VMEM((tokens, width), BF16),
            pltpu.VMEM((2 * rows, 3 * chans), F32),
            pltpu.VMEM((4, rows, chans), BF16),
            pltpu.VMEM((4, rows, chans), BF16),
            pltpu.VMEM((4, rows, chans), F32),
            pltpu.VMEM((blocks, rows, 128), F32),
            pltpu.VMEM((blocks, rows, 128), F32),
            pltpu.VMEM((blocks, rows + 8, 128), F32),
            pltpu.VMEM((4, rows, 128), F32),
            pltpu.VMEM((8 * blocks, 128), F32),
            pltpu.VMEM((8 * blocks, 128), F32),
            pltpu.VMEM((8 * blocks, 128), F32),
            pltpu.VMEM((2 * blocks, 128), F32),
            pltpu.VMEM((n_seq, 2 * blocks, 128), F32),
            pltpu.VMEM((4, rows, chans), BF16),
            pltpu.VMEM((tokens, chans), BF16),
            pltpu.VMEM((long_rows, 128), F32),
            pltpu.VMEM((128, long_rows), F32),
            pltpu.VMEM((8, long_rows), F32),
            pltpu.VMEM((3, 8, long_rows), F32),
            pltpu.VMEM((tokens, width), BF16),
            pltpu.VMEM((3, half, width), BF16),
            pltpu.VMEM((3, half, width), BF16),
            pltpu.VMEM((half, width), BF16),
            pltpu.VMEM((half, width), BF16),
            pltpu.SemaphoreType.DMA((21 + n_seq // 2,)),
            pltpu.SemaphoreType.DMA((21 + n_seq // 2,)),
            pltpu.SemaphoreType.DMA((n_seq,)),
            pltpu.SemaphoreType.DMA((n_seq,)),
            pltpu.SemaphoreType.DMA((11 + n_seq // 2,)),
        ],
        compiler_params=params(collective_id),
        name="mixer_forward",
    )(lengths, hidden, cot, *gains, table, *weights)


def swap_columns(links, local, src, dst, n_seq, core, mate):
    part = src.shape[1] // n_seq
    copies, stays = [], []
    for z in range(n_seq // 2):
        to = pl.ds(z * part, part)
        theirs = pl.ds(pl.multiple_of((2 * z + 1 - core) * part, part), part)
        ours = pl.ds(pl.multiple_of((2 * z + core) * part, part), part)
        copies.append(links.start(src.at[:, theirs], dst.at[1, :, to], mate))
        stays.append(local.start(src.at[:, ours], dst.at[0, :, to]))
    return copies, stays


def swap_rows(links, local, src, dst, at, mate):
    copy = links.start(src.at[at], dst.at[1, at], mate)
    return copy, local.start(src.at[at], dst.at[0, at])


def glu_kernel(
    n_seq,
    two,
    cot_all,
    w_gate,
    w_up,
    w_down,
    two_half,
    cot_half,
    act_pair,
    gate_pair,
    up_pair,
    wv,
    wd,
    cot_ref,
    two_ref,
    d_act,
    stage,
    act,
    d_gate,
    d_up,
    send,
    recv,
    local_sems,
):
    rows = two.shape[0]
    units = w_gate.shape[1]
    s, f, fx, fy, fd = plane()
    core = s % 2
    mate = (s + 1 - 2 * core, f)
    links, local = Links(send, recv), Locals(local_sems)
    loads = [
        local.start(w_down, wd),
        local.start(cot_all, cot_ref),
        local.start(w_gate, wv.at[:, pl.ds(0, units)]),
        local.start(w_up, wv.at[:, pl.ds(units, units)]),
    ]
    two_ref[:rows] = two[...]
    enter([(s, fx), (s, fy), mate])
    own = gather_start(links, two_ref, two_ref, rows, s, fx, fy)
    loads[0].wait()
    loads[1].wait()
    swaps, stays = swap_columns(links, local, cot_ref, cot_half, n_seq, core, mate)

    def act_tile(n, _):
        cols = tile(n, 256)
        d_act[:, cols] = mm_t(cot_ref[...], wd[cols])
        return 0

    lax.fori_loop(0, units // 256, act_tile, 0)
    if units % 256:
        rest = slice(units // 256 * 256, units)
        d_act[:, rest] = mm_t(cot_ref[...], wd[rest])
    later = gather_forward(links, own, two_ref, rows, s, fx, fy)
    loads[2].wait()
    loads[3].wait()

    def slots(first, number):
        nonlocal swaps, stays
        base = first * rows

        def tile_of(n, _):
            cols = tile(n, 256)
            stage[: number * rows, cols] = mm(two_ref[base : base + number * rows], wv[:, cols])
            return 0

        lax.fori_loop(0, 2 * units // 256, tile_of, 0)

        def rows_of(i, _):
            at = pl.ds(pl.multiple_of(i * 16, 16), 16)
            to = pl.ds(pl.multiple_of(base + i * 16, 16), 16)
            gate, up = stage[at, :units], stage[at, units:]
            sigma = jax.nn.sigmoid(gate)
            silu = gate * sigma
            act[to] = (silu * up).astype(BF16)
            d = d_act[to]
            d_gate[to] = (d * up * silu_slope(gate, sigma)).astype(BF16)
            d_up[to] = (d * silu).astype(BF16)
            return 0

        lax.fori_loop(0, number * rows // 16, rows_of, 0)
        at = pl.ds(base, number * rows)
        for src, dst in ((act, act_pair), (d_gate, gate_pair), (d_up, up_pair)):
            sent, stayed = swap_rows(links, local, src, dst, at, mate)
            swaps, stays = swaps + [sent], stays + [stayed]

    slots(0, 1)
    gather_middle(own)
    slots(1, 2)
    gather_far(later)
    more, keeps = swap_columns(links, local, two_ref, two_half, n_seq, core, mate)
    slots(3, 1)
    sends_done(own, later)
    wait_all(swaps, stays, more, keeps)


def glu(two, cot_all, w_gate, w_up, w_down, collective_id):
    n_seq = lax.axis_size("seq")
    rows, width = two.shape
    units = w_gate.shape[1]
    tokens = 4 * rows
    shape = jax.ShapeDtypeStruct
    half = shape((2, tokens, width // 2), BF16)
    pair = shape((2, tokens, units), BF16)
    remote_count = 6 + n_seq + 9
    return pl.pallas_call(
        functools.partial(glu_kernel, n_seq),
        out_shape=(half, half, pair, pair, pair),
        in_specs=[VMEM] + [ANY] * 4,
        out_specs=(ANY,) * 5,
        scratch_shapes=[
            pltpu.VMEM((width, 2 * units), BF16),
            pltpu.VMEM((units, width), BF16),
            pltpu.VMEM((tokens, width), BF16),
            pltpu.VMEM((tokens, width), BF16),
            pltpu.VMEM((tokens, units), F32),
            pltpu.VMEM((2 * rows, 2 * units), F32),
            pltpu.VMEM((tokens, units), BF16),
            pltpu.VMEM((tokens, units), BF16),
            pltpu.VMEM((tokens, units), BF16),
            pltpu.SemaphoreType.DMA((remote_count,)),
            pltpu.SemaphoreType.DMA((remote_count,)),
            pltpu.SemaphoreType.DMA((4 + n_seq + 9,)),
        ],
        compiler_params=params(collective_id),
        name="glu",
    )(two, cot_all, w_gate, w_up, w_down)


class ZLine:
    def __init__(self, part, buf, sems, n_seq, width, lag, ahead, store=None, leave=None):
        self.part, self.buf, self.width, self.lag, self.ahead = part, buf, width, lag, ahead
        self.send_up, self.recv_up, self.send_down, self.recv_down = sems[:4]
        self.store, self.leave = store, leave
        self.s, self.f = lax.axis_index("seq"), lax.axis_index("fsdp")
        self.n_seq, self.nz = n_seq, n_seq // 2
        self.z = self.s // 2
        self.block = part.shape[0] // self.nz
        self.chunks = part.shape[1] // width
        self.steps = (self.nz - 1) * self.chunks
        self.calls = self.steps + lag * (self.nz - 2)

    def rows(self, t):
        return pl.ds(pl.multiple_of(t * self.block, self.block), self.block)

    def move(self, up, k, j):
        t = self.nz - 1 - k if up else k
        landing = t + 1 if up else t
        cols = tile(j, self.width)
        slot = k * self.chunks + j
        peer = lax.rem(self.s + (2 if up else self.n_seq - 2), self.n_seq)
        send, recv = (
            (self.send_up, self.recv_up) if up else (self.send_down, self.recv_down)
        )
        return remote(
            self.part.at[self.rows(t), cols],
            self.buf.at[self.rows(landing), cols],
            send.at[slot],
            recv.at[slot],
            (peer, self.f),
        )

    def feed(self, q):
        inside = q < self.steps
        q = jnp.minimum(q, self.steps - 1)
        k = q // self.chunks
        j = q - k * self.chunks

        @pl.when(inside & (self.z == 0))
        def _():
            self.move(True, k, j).start()

        @pl.when(inside & (self.z == self.nz - 1))
        def _():
            self.move(False, k, j).start()

    def nth(self, i):
        return jnp.where(self.z < self.nz // 2, self.nz - 1 - i, i)

    def load(self, local, src):
        order = [self.rows(self.nth(i)) for i in range(self.nz)]
        return [local.start(src.at[at], self.part.at[at]) for at in order]

    def feed_first(self):
        def step(q, _):
            self.feed(q)
            return 0

        lax.fori_loop(0, self.ahead, step, 0)

    def serve_one(self, up, q):
        z, nz = self.z, self.nz
        hops = z if up else nz - 1 - z
        q = q - self.lag * (hops - 1)
        inside = (hops >= 1) & (q >= 0) & (q < self.steps)
        q = jnp.clip(q, 0, self.steps - 1)
        k = q // self.chunks
        j = q - k * self.chunks
        left = nz - 1 - k - hops
        cols = tile(j, self.width)

        @pl.when(inside & (left >= 0))
        def _():
            self.move(up, k, j).wait_recv()

        @pl.when(inside & (left > 0))
        def _():
            t = nz - 1 - k if up else k
            landing = t + 1 if up else t
            own = self.part[self.rows(t), cols].astype(F32)
            came = self.buf[self.rows(landing), cols].astype(F32)
            self.part[self.rows(t), cols] = (own + came).astype(BF16)
            self.move(up, k, j).start()

    def serve(self, q, done=False):
        self.serve_one(True, q)
        self.serve_one(False, q)
        if done:
            j = q - (self.nz - 2) * self.chunks

            @pl.when((j >= 0) & (j < self.chunks))
            def _():
                self.finish(j)

    def serve_range(self, first, last, done=False):
        def step(q, _):
            self.feed(q + self.ahead)
            self.serve(q, done)
            return 0

        lax.fori_loop(first, last, step, 0)

    def finish(self, j):
        cols = tile(j, self.width)
        above = self.buf[self.rows(self.z), cols].astype(F32)
        below = self.buf[self.rows(self.z + 1), cols].astype(F32)
        own = self.part[self.rows(self.z), cols].astype(F32)
        own = own + jnp.where(self.z < self.nz - 1, above, 0.0)
        self.store(j, own + jnp.where(self.z > 0, below, 0.0))
        self.leave(j, True)

    def drain(self):
        for k in range(self.nz - 1):
            for up in (True, False):
                hops = self.z if up else self.nz - 1 - self.z

                @pl.when(hops < self.nz - 1 - k)
                def _():
                    def step(j, _):
                        self.move(up, k, j).wait_send()
                        return 0

                    lax.fori_loop(0, self.chunks, step, 0)

        def left(j, _):
            self.leave(j, False)
            return 0

        lax.fori_loop(0, self.chunks, left, 0)


def start_or_wait(copy, start):
    if start:
        copy.start()
    else:
        copy.wait()


def line_sems(n_seq, columns, width):
    count = (n_seq // 2 - 1) * (columns // width)
    leave = pltpu.SemaphoreType.DMA((columns // width,))
    return [pltpu.SemaphoreType.DMA((count,)) for _ in range(4)] + [leave]


def z_peers(n_seq):
    s = lax.axis_index("seq")
    f = lax.axis_index("fsdp")
    return [(lax.rem(s + 2 * k, n_seq), f) for k in range(1, n_seq // 2)]


def mm_tokens(left, right):
    return lax.dot_general(left, right, (((0,), (0,)), ((), ())), preferred_element_type=F32)


def down_kernel(
    n_seq,
    cot_half,
    act_pair,
    two_half,
    gate_pair,
    up_pair,
    w_gate,
    w_up,
    d_two,
    pair_part,
    down_out,
    cot_ref,
    act_ref,
    two_ref,
    gate_ref,
    up_ref,
    wg,
    wu,
    part,
    buf,
    rows_part,
    from_x,
    from_y,
    pass_x,
    pass_y,
    pair_ref,
    down_ref,
    send,
    recv,
    local_sems,
    *line,
):
    rows, width = d_two.shape
    units = act_pair.shape[1]
    s, f, fx, fy, fd = plane()
    links, local = Links(send, recv), Locals(local_sems)
    moves = (
        (cot_half, cot_ref),
        (act_pair, act_ref),
        (w_gate, wg),
        (w_up, wu),
        (gate_pair, gate_ref),
        (up_pair, up_ref),
        (two_half, two_ref),
    )
    loads = [local.start(src, dst) for src, dst in moves]
    enter([(s, fx), (s, fy)] + z_peers(n_seq))

    def store(j, value):
        down_ref[tile(j, 128)] = value.T

    def leave(j, start):
        at = tile(j, 128)
        copy = pltpu.make_async_copy(down_ref.at[at], down_out.at[at], line[4].at[j])
        start_or_wait(copy, start)

    z_sum = ZLine(part, buf, line, n_seq, 128, 3, 11, store, leave)
    block = z_sum.block
    loads[0].wait()
    loads[1].wait()

    def down_tile(i, _):
        t = z_sum.nth(i)
        part[z_sum.rows(t)] = mm_tokens(cot_ref[:, tile(t, block)], act_ref[...]).astype(BF16)
        return 0

    down_tile(jnp.int32(0), 0)
    z_sum.feed_first()
    lax.fori_loop(1, z_sum.nz, down_tile, 0)
    for copy in loads[2:]:
        copy.wait()

    def two_part(first, slots, base):
        at = slice(first * rows, (first + slots) * rows)

        def tile_of(n, _):
            cols = tile(n, 512)
            total = mm_t(gate_ref[at], wg[cols]) + mm_t(up_ref[at], wu[cols])
            rows_part[at, cols] = total.astype(BF16)
            z_sum.feed(base + n + z_sum.ahead)
            z_sum.serve(base + n)
            return 0

        lax.fori_loop(0, width // 512, tile_of, 0)

    count = width // 512
    two_part(3, 1, 0)
    far = reduce_start_far(links, rows_part, from_x, from_y, rows, s, fx, fy)
    two_part(1, 2, count)
    near = reduce_start_near(links, rows_part, from_x, from_y, rows, s, fx, fy)
    two_part(0, 1, 2 * count)
    served = 3 * count

    def pair_tiles(right, first, base):
        def tile_of(t, _):
            pair_ref[z_sum.rows(t), pl.ds(first, units)] = mm_tokens(
                two_ref[:, tile(t, block)], right[...]
            ).astype(BF16)
            z_sum.serve_range(base + 2 * t, base + 2 * t + 2, True)
            return 0

        lax.fori_loop(0, z_sum.nz, tile_of, 0)

    pair_tiles(gate_ref, 0, served)
    served += 2 * z_sum.nz
    passed = reduce_pass(links, far, rows_part, from_x, from_y, pass_x, pass_y, rows, s, fx, fy)
    pair_tiles(up_ref, units, served)
    served += 2 * z_sum.nz
    stay = local.start(pair_ref, pair_part)
    for copy in near + passed:
        copy.wait_recv()
    half = rows // 2
    d_two[:half] = rows_part[:half].astype(F32) + from_x[1].astype(F32) + from_y[2].astype(F32)
    d_two[half:] = rows_part[half:rows].astype(F32) + from_y[1].astype(F32) + from_x[2].astype(F32)
    z_sum.serve_range(served, z_sum.calls, True)
    z_sum.drain()
    sends_done(far, near, passed)
    stay.wait()


def down_sum(cot_half, act_pair, two_half, gate_pair, up_pair, w_gate, w_up, collective_id):
    n_seq = lax.axis_size("seq")
    tokens, units = act_pair.shape
    width = w_gate.shape[0]
    rows = tokens // 8
    half = (rows // 2, width)
    own = cot_half.shape[1]
    block = width // n_seq
    shape = jax.ShapeDtypeStruct
    return pl.pallas_call(
        functools.partial(down_kernel, n_seq),
        out_shape=(
            shape((rows, width), F32),
            shape((own, 2 * units), BF16),
            shape((units, block), F32),
        ),
        in_specs=[ANY] * 7,
        out_specs=(VMEM, ANY, ANY),
        scratch_shapes=[
            pltpu.VMEM((tokens, own), BF16),
            pltpu.VMEM((tokens, units), BF16),
            pltpu.VMEM((tokens, own), BF16),
            pltpu.VMEM((tokens, units), BF16),
            pltpu.VMEM((tokens, units), BF16),
            pltpu.VMEM((width, units), BF16),
            pltpu.VMEM((width, units), BF16),
            pltpu.VMEM((own, units), BF16),
            pltpu.VMEM((own + block, units), BF16),
            pltpu.VMEM((tokens // 2, width), BF16),
            pltpu.VMEM((3,) + half, BF16),
            pltpu.VMEM((3,) + half, BF16),
            pltpu.VMEM(half, BF16),
            pltpu.VMEM(half, BF16),
            pltpu.VMEM((own, 2 * units), BF16),
            pltpu.VMEM((units, block), F32),
            pltpu.SemaphoreType.DMA((6,)),
            pltpu.SemaphoreType.DMA((6,)),
            pltpu.SemaphoreType.DMA((8,)),
        ]
        + line_sems(n_seq, units, 128),
        compiler_params=params(collective_id),
        name="down_sum",
    )(cot_half, act_pair, two_half, gate_pair, up_pair, w_gate, w_up)


def pair_kernel(
    n_seq,
    lengths,
    hidden,
    cot,
    glu_gain,
    gate_gain,
    table,
    scale_g,
    d_two,
    middle,
    pair_part,
    w_out,
    w_in,
    w_fg,
    w_gt,
    gate_raw,
    state_b,
    out_raw,
    in_raw,
    fg_raw,
    before_in,
    normed_half,
    pair_grad,
    mixer_part,
    d_normed_out,
    d_middle_out,
    d_glu_gain,
    d_gain,
    d_bounds,
    d_normed,
    d_middle,
    pair_ref,
    part,
    buf,
    wo,
    wv,
    mixed_all,
    mixed_mate,
    normed_ref,
    d_proj,
    out_gate,
    gate_ref,
    state_ref,
    raw_ref,
    in_ref,
    fg_ref,
    before,
    p_ref,
    q_ref,
    stage,
    rows_part,
    from_x,
    from_y,
    pass_x,
    pass_y,
    dots,
    keep_ref,
    end_p,
    end_s,
    carr,
    total,
    gathered,
    send,
    recv,
    exchange_send,
    exchange_recv,
    local_sems,
    tile_sems,
    *line,
):
    rows, width = hidden.shape
    chans = w_in.shape[1]
    tokens = 4 * rows
    lanes_of = [slice(c, c + 128) for c in range(0, chans, 128)]
    count = len(lanes_of)
    blocks = 4 * count
    step_len = rows // 8
    s, f, fx, fy, fd = plane()
    groups = [f, fx, fy, fd]
    core = s % 2
    mate = (s + 1 - 2 * core, f)
    links, local = Links(send, recv), Locals(local_sems)

    def store(j, value):
        pair_ref[:, tile(j, 256)] = value

    def leave(j, start):
        at = tile(j, 256)
        copy = pltpu.make_async_copy(pair_ref.at[:, at], pair_grad.at[:, at], line[4].at[j])
        start_or_wait(copy, start)

    z_sum = ZLine(part, buf, line, n_seq, 256, 2, 11, store, leave)
    blocks_in = z_sum.load(local, pair_part)
    rows_in = [local.start(d_two, d_middle), local.start(middle, d_normed)]
    loads = [local.start(w_out, wo)]
    loads += [
        local.start(src, dst)
        for src, dst in (
            (gate_raw, gate_ref),
            (state_b, state_ref),
            (out_raw, raw_ref),
            (in_raw, in_ref),
            (fg_raw, fg_ref),
            (before_in, before),
        )
    ]
    weights = [
        local.start(w, wv.at[:, pl.ds(i * chans, chans)]) for i, w in enumerate((w_in, w_fg, w_gt))
    ]
    weights.append(local.start(normed_half, normed_ref))
    enter([(s, fx), (s, fy), (s, fd)] + seq_peers(n_seq))
    blocks_in[0].wait()
    z_sum.feed_first()
    served = 0

    def serve(number):
        nonlocal served
        z_sum.serve_range(served, served + number)
        served += number

    d_glu_gain[...] = jnp.zeros_like(d_glu_gain)
    wait_all(rows_in, blocks_in[1:])

    def middle_rows(i, _):
        at = pl.ds(pl.multiple_of(i * 16, 16), 16)
        value, came = d_normed[at], d_middle[at]
        scale = lax.rsqrt(jnp.mean(value * value, -1, keepdims=True) + epsilon)
        scaled = glu_gain[...] * came
        mean = jnp.mean(scaled * value, -1, keepdims=True)
        grad = cot[at].astype(F32) + scale * scaled - value * (scale**3 * mean)
        d_middle[at] = grad
        grad_b = grad.astype(BF16)
        mixed_all[at] = grad_b
        own_dot = jnp.sum(
            grad_b.astype(F32) * (value - hidden[at].astype(F32)), -1, keepdims=True
        )
        dots[0, at] = jnp.broadcast_to(own_dot, (16, 128))
        d_glu_gain[...] += jnp.sum(came * value * scale, 0, keepdims=True)
        return 0

    lax.fori_loop(0, rows // 16, middle_rows, 0)
    outs = [local.start(d_middle, d_middle_out)]
    own = gather_start(links, mixed_all, mixed_all, rows, s, fx, fy)
    dot_copies = [
        links.start(dots.at[0], dots.at[k], (s, peer)) for k, peer in ((1, fx), (2, fy), (3, fd))
    ]
    bound = bounds_slice(table, f * chans, chans)
    for k in range(4):
        keep_ref[k] = keep_rows(lengths, groups[k], s * rows, rows)
    d_gain[...] = jnp.zeros_like(d_gain)
    serve(1)
    for copy in loads:
        copy.wait()

    def out_rows(first, slots):
        stage[: slots * rows] = mm_t(mixed_all[first * rows : (first + slots) * rows], wo[...])
        for i in range(slots):
            k = first + i
            scale = scale_g[k]
            for c, lanes in enumerate(lanes_of):
                n = k * count + c
                gain = gate_gain[:, pl.ds(pl.multiple_of(f * chans + c * 128, 128), 128)]
                d_out = stage[i * rows : (i + 1) * rows, lanes]
                gate = gate_ref[k, :, lanes]
                sigma = jax.nn.sigmoid(gate)
                silu = gate * sigma
                state = state_ref[k, :, lanes].astype(F32)
                weighed = d_out * (state * scale)
                d_gain[:, lanes] += jnp.sum(weighed * silu, 0, keepdims=True)
                at = slice(k * rows, (k + 1) * rows)
                d_proj[at, 2 * chans + c * 128 : 2 * chans + (c + 1) * 128] = (
                    weighed * gain * silu_slope(gate, sigma)
                ).astype(BF16)
                out_gate[at, lanes] = (raw_ref[at, lanes].astype(F32) * scale).astype(BF16)
                d_state = scale * (d_out * gain * silu) - state * (
                    scale * scale * (dots[k] / width)
                )
                q_ref[n] = d_state.astype(BF16).astype(F32)
                edge = bound[:, lanes]
                forget = edge + (1.0 - edge) * jax.nn.sigmoid(fg_ref[k, :, lanes].astype(F32))
                p_ref[n] = forget * keep_ref[k]

    out_rows(0, 1)
    later = gather_forward(links, own, mixed_all, rows, s, fx, fy)
    serve(2)
    gather_middle(own)
    for copy in dot_copies:
        copy.wait_recv()
    out_rows(1, 2)
    serve(3)
    gather_far(later)
    out_rows(3, 1)
    serve(2)
    own_rows, mate_rows = pl.ds(0, tokens), pl.ds(tokens, tokens)
    last = pl.ds(2 * chans, chans)
    swaps = [
        links.start(out_gate.at[own_rows], out_gate.at[mate_rows], mate),
        links.start(d_proj.at[own_rows, last], d_proj.at[mate_rows, last], mate),
    ]
    wide = z_sum.block
    for t in range(n_seq // 2):
        theirs = pl.ds(pl.multiple_of((2 * t + 1 - core) * wide, wide), wide)
        swaps.append(
            links.start(mixed_all.at[:, theirs], mixed_mate.at[:, pl.ds(t * wide, wide)], mate)
        )

    def scan_step(i, carry):
        new = []
        at = pl.ds(step_len - 1 - i, 8, stride=step_len)
        for n, (product, message) in enumerate(carry):
            a = p_ref[n, at, :]
            acc = q_ref[n, at, :] + message
            p_ref[n, at, :] = product
            q_ref[n, at, :] = acc
            new.append((product * a, a * acc))
        return tuple(new)

    start = tuple((jnp.ones((8, 128), F32), jnp.zeros((8, 128), F32)) for _ in range(blocks))
    ends = lax.fori_loop(0, step_len, scan_step, start)
    for n, (product, message) in enumerate(ends):
        end_p[8 * n : 8 * n + 8] = product
        end_s[8 * n : 8 * n + 8] = message
    p_all, s_all = segment_totals(end_p, end_s, blocks, range(7, -1, -1))
    total[:blocks] = p_all
    total[blocks:] = s_all
    copies = start_exchange(total, gathered, exchange_send, exchange_recv, n_seq)
    serve(2)
    wait_all(copies)
    carry = jnp.zeros((blocks, 128), F32)
    for j in range(n_seq - 1, 0, -1):
        carry = jnp.where(j > s, gathered[j, blocks:] + gathered[j, :blocks] * carry, carry)
    spread_carry(carry, carr, end_p, end_s, blocks, range(7, -1, -1))

    def finish(n, _):
        enter_state = carr[pl.ds(pl.multiple_of(n * 8, 8), 8)]
        for i in range(step_len):
            at = pl.ds(i, 8, stride=step_len)
            q_ref[n, at, :] = q_ref[n, at, :] + p_ref[n, at, :] * enter_state
        return 0

    lax.fori_loop(0, blocks, finish, 0)
    d_bounds[...] = jnp.zeros_like(d_bounds)
    for k in range(4):
        at = slice(k * rows, (k + 1) * rows)
        for c, lanes in enumerate(lanes_of):
            acc = q_ref[k * count + c]
            edge = bound[:, lanes]
            sigma_f = jax.nn.sigmoid(fg_ref[k, :, lanes].astype(F32))
            forget = edge + (1.0 - edge) * sigma_f
            value = in_ref[k, :, lanes].astype(F32)
            sigma_i = jax.nn.sigmoid(value)
            d_forget = acc * (before[k * count + c] * keep_ref[k] - value * sigma_i)
            d_proj[at, lanes] = (acc * (1.0 - forget) * silu_slope(value, sigma_i)).astype(BF16)
            d_sigma = d_forget * (1.0 - sigma_f)
            d_proj[at, chans + c * 128 : chans + (c + 1) * 128] = (
                d_sigma * (1.0 - edge) * sigma_f
            ).astype(BF16)
            d_bounds[:, lanes] += jnp.sum(d_sigma, 0, keepdims=True)
    first = pl.ds(0, 2 * chans)
    swaps.append(links.start(d_proj.at[own_rows, first], d_proj.at[mate_rows, first], mate))
    serve(2)
    for copy in weights:
        copy.wait()

    def normed_part(first_slot, slots):
        at = slice(first_slot * rows, (first_slot + slots) * rows)

        def tile_of(n, _):
            cols = tile(n, 512)
            rows_part[at, cols] = mm_t(d_proj[at], wv[cols]).astype(BF16)
            return 0

        lax.fori_loop(0, width // 512, tile_of, 0)

    normed_part(3, 1)
    far = reduce_start_far(links, rows_part, from_x, from_y, rows, s, fx, fy)
    normed_part(1, 2)
    near = reduce_start_near(links, rows_part, from_x, from_y, rows, s, fx, fy)
    normed_part(0, 1)
    serve(3)
    for copy in swaps:
        copy.wait_recv()

    def tile_out(t):
        slot = lax.rem(t, 2)
        return pltpu.make_async_copy(
            wo.at[tile(slot, wide)], mixer_part.at[z_sum.rows(t)], tile_sems.at[slot]
        )

    def mixer_tile(t, _):
        @pl.when(t >= 2)
        def _():
            tile_out(t - 2).wait()

        at = tile(lax.rem(t, 2), wide)
        ours = mixed_all[:, tile(2 * t + core, wide)]
        out_part = mm_tokens(ours, out_gate[:tokens])
        out_part = out_part + mm_tokens(mixed_mate[:, tile(t, wide)], out_gate[tokens:])
        wo[at, :chans] = out_part.astype(BF16)
        wo[at, chans:] = mm_tokens(normed_ref[:, tile(t, wide)], d_proj[...]).astype(BF16)
        tile_out(t).start()
        return 0

    lax.fori_loop(0, 1, mixer_tile, 0)
    passed = reduce_pass(links, far, rows_part, from_x, from_y, pass_x, pass_y, rows, s, fx, fy)
    serve(1)
    lax.fori_loop(1, z_sum.nz, mixer_tile, 0)
    serve(2)
    for copy in near + passed:
        copy.wait_recv()
    half = rows // 2
    d_normed[:half] = rows_part[:half].astype(F32) + from_x[1].astype(F32) + from_y[2].astype(F32)
    d_normed[half:] = (
        rows_part[half:rows].astype(F32) + from_y[1].astype(F32) + from_x[2].astype(F32)
    )
    outs.append(local.start(d_normed, d_normed_out))
    z_sum.serve_range(served, z_sum.calls, True)
    z_sum.drain()
    sends_done(own, later, dot_copies, swaps, far, near, passed)
    for t in range(z_sum.nz - 2, z_sum.nz):
        tile_out(jnp.int32(t)).wait()
    wait_all(outs)


def pair_sum(
    lengths, own_rows, gains, table, scale_g, float_rows, pair_part, weights, saved, normed_half, cid
):
    n_seq = lax.axis_size("seq")
    rows, width = own_rows[0].shape
    chans = weights[1].shape[1]
    own, columns = pair_part.shape
    tokens = 4 * rows
    blocks = 4 * chans // 128
    block = width // n_seq
    half = (rows // 2, width)
    shape = jax.ShapeDtypeStruct
    exchange = pltpu.SemaphoreType.DMA((n_seq,))
    count = 18 + n_seq // 2
    return pl.pallas_call(
        functools.partial(pair_kernel, n_seq),
        out_shape=(
            shape((block, columns), F32),
            shape((own, 4 * chans), BF16),
            shape((rows, width), F32),
            shape((rows, width), F32),
            shape((1, width), F32),
            shape((1, chans), F32),
            shape((1, chans), F32),
        ),
        in_specs=[pl.BlockSpec(memory_space=pltpu.SMEM)] + [VMEM] * 6 + [ANY] * 14,
        out_specs=(ANY,) * 4 + (VMEM,) * 3,
        scratch_shapes=[
            pltpu.VMEM((rows, width), F32),
            pltpu.VMEM((rows, width), F32),
            pltpu.VMEM((block, columns), F32),
            pltpu.VMEM((own, columns), BF16),
            pltpu.VMEM((own + block, columns), BF16),
            pltpu.VMEM((chans, width), BF16),
            pltpu.VMEM((width, 3 * chans), BF16),
            pltpu.VMEM((tokens, width), BF16),
            pltpu.VMEM((tokens, width // 2), BF16),
            pltpu.VMEM((2 * tokens, width // 2), BF16),
            pltpu.VMEM((2 * tokens, 3 * chans), BF16),
            pltpu.VMEM((2 * tokens, chans), BF16),
            pltpu.VMEM((4, rows, chans), F32),
            pltpu.VMEM((4, rows, chans), BF16),
            pltpu.VMEM((tokens, chans), BF16),
            pltpu.VMEM((4, rows, chans), BF16),
            pltpu.VMEM((4, rows, chans), BF16),
            pltpu.VMEM((blocks, rows, 128), F32),
            pltpu.VMEM((blocks, rows, 128), F32),
            pltpu.VMEM((blocks, rows, 128), F32),
            pltpu.VMEM((2 * rows, chans), F32),
            pltpu.VMEM((tokens, width), BF16),
            pltpu.VMEM((3,) + half, BF16),
            pltpu.VMEM((3,) + half, BF16),
            pltpu.VMEM(half, BF16),
            pltpu.VMEM(half, BF16),
            pltpu.VMEM((4, rows, 128), F32),
            pltpu.VMEM((4, rows, 128), F32),
            pltpu.VMEM((8 * blocks, 128), F32),
            pltpu.VMEM((8 * blocks, 128), F32),
            pltpu.VMEM((8 * blocks, 128), F32),
            pltpu.VMEM((2 * blocks, 128), F32),
            pltpu.VMEM((n_seq, 2 * blocks, 128), F32),
            pltpu.SemaphoreType.DMA((count,)),
            pltpu.SemaphoreType.DMA((count,)),
            exchange,
            exchange,
            pltpu.SemaphoreType.DMA((15 + n_seq // 2,)),
            pltpu.SemaphoreType.DMA((2,)),
        ]
        + line_sems(n_seq, columns, 256),
        compiler_params=params(cid),
        name="pair_sum",
    )(
        lengths,
        *own_rows,
        *gains,
        table,
        scale_g,
        *float_rows,
        pair_part,
        *weights,
        *saved,
        normed_half,
    )


def final_kernel(
    n_seq,
    n_fsdp,
    d_normed,
    d_middle,
    hidden,
    middle,
    norm_gain,
    d_glu_gain,
    d_gain,
    d_bounds,
    table,
    mixer_part,
    act_pair,
    w_down,
    output,
    d_hidden,
    out_grad,
    rest_grad,
    sums,
    d_table,
    out_ref,
    rest_ref,
    part,
    buf,
    act,
    wd,
    rows_part,
    from_x,
    from_y,
    pass_x,
    pass_y,
    norm_sum,
    terms,
    quarters_in,
    terms_q,
    over_seq,
    along_sum,
    over_fsdp,
    send,
    recv,
    local_sems,
    *line,
):
    rows, width = middle.shape
    chans = d_gain.shape[1]
    tokens = 4 * rows
    s, f, fx, fy, fd = plane()
    links, local = Links(send, recv), Locals(local_sems)
    head = chans // 256

    def store(j, value):
        @pl.when(j < head)
        def _():
            out_ref[tile(j, 256)] = value.T

        @pl.when(j >= head)
        def _():
            rest_ref[:, tile(j - head, 256)] = value

    def leave(j, start):
        @pl.when(j < head)
        def _():
            at = tile(j, 256)
            copy = pltpu.make_async_copy(out_ref.at[at], out_grad.at[at], line[4].at[j])
            start_or_wait(copy, start)

        @pl.when(j >= head)
        def _():
            at = tile(j - head, 256)
            copy = pltpu.make_async_copy(rest_ref.at[:, at], rest_grad.at[:, at], line[4].at[j])
            start_or_wait(copy, start)

    z_sum = ZLine(part, buf, line, n_seq, 256, 2, 8, store, leave)
    blocks_in = z_sum.load(local, mixer_part)
    loads = [
        local.start(act_pair.at[pl.ds(0, tokens)], act),
        local.start(w_down, wd),
    ]
    along = seq_peers(n_seq)
    across = [(s, fx), (s, fy), (s, fd)]
    enter(across + along)
    blocks_in[0].wait()
    z_sum.feed_first()
    served = 0

    def serve(number):
        nonlocal served
        z_sum.serve_range(served, served + number)
        served += number

    norm_sum[...] = jnp.zeros_like(norm_sum)

    def hidden_rows(i, _):
        at = pl.ds(pl.multiple_of(i * 16, 16), 16)
        value, came = hidden[at].astype(F32), d_normed[at]
        scale = lax.rsqrt(jnp.mean(value * value, -1, keepdims=True) + epsilon)
        scaled = norm_gain[...] * came
        mean = jnp.mean(scaled * value, -1, keepdims=True)
        d_hidden[at] = (d_middle[at] + scale * scaled - value * (scale**3 * mean)).astype(BF16)
        norm_sum[...] += jnp.sum(came * value * scale, 0, keepdims=True)
        return 0

    wait_all(blocks_in[1:], loads)

    def glu_part(first, slots):
        at = slice(first * rows, (first + slots) * rows)

        def tile_of(n, _):
            cols = tile(n, 512)
            rows_part[at, cols] = mm(act[at], wd[:, cols]).astype(BF16)
            return 0

        lax.fori_loop(0, width // 512, tile_of, 0)

    glu_part(3, 1)
    far = reduce_start_far(links, rows_part, from_x, from_y, rows, s, fx, fy)
    glu_part(1, 2)
    near = reduce_start_near(links, rows_part, from_x, from_y, rows, s, fx, fy)
    glu_part(0, 1)
    serve(2)
    lax.fori_loop(0, rows // 16, hidden_rows, 0)
    terms[...] = jnp.zeros_like(terms)
    for q in range(4):
        terms[q, 0:1] = norm_sum[:, q * chans : (q + 1) * chans]
        terms[q, 1:2] = d_glu_gain[:, q * chans : (q + 1) * chans]
    quarter_copies = [
        links.start(terms.at[peer], quarters_in.at[k], (s, peer))
        for k, peer in enumerate((fx, fy, fd))
    ]
    serve(1)
    passed = reduce_pass(links, far, rows_part, from_x, from_y, pass_x, pass_y, rows, s, fx, fy)
    serve(2)
    quarter = terms[pl.ds(f, 1)][0]
    for k, copy in enumerate(quarter_copies):
        copy.wait_recv()
        quarter = quarter + quarters_in[k]
    half = chans // 2
    for first, cols in ((0, slice(0, half)), (4, slice(half, chans))):
        terms_q[first : first + 2] = quarter[:2, cols]
        terms_q[first + 2 : first + 3] = d_gain[:, cols]
        terms_q[first + 3 : first + 4] = d_bounds[:, cols]
    seq_copies = [links.start(terms_q, over_seq.at[k], peer) for k, peer in enumerate(along)]
    serve(1)
    total = terms_q[...]
    for k, copy in enumerate(seq_copies):
        copy.wait_recv()
        total = total + over_seq[k]
    along_sum[...] = total
    fsdp_copies = [links.start(along_sum, over_fsdp.at[k], peer) for k, peer in enumerate(across)]
    serve(2)
    for copy in near + passed:
        copy.wait_recv()
    middle_half = rows // 2
    for first, one, other in (
        (0, from_x.at[1], from_y.at[2]),
        (middle_half, from_y.at[1], from_x.at[2]),
    ):
        at = slice(first, first + middle_half)
        added = rows_part[at].astype(F32) + one[...].astype(F32) + other[...].astype(F32)
        output[at] = (middle[at] + added).astype(BF16)
    serve(1)
    for copy in fsdp_copies:
        copy.wait_recv()
    for k, group in enumerate((f, fx, fy, fd)):
        total = along_sum[...] if k == 0 else over_fsdp[k - 1]
        for i in range(2):
            at = pl.ds(pl.multiple_of(group * chans + i * half, 128), half)
            sums[:, at] = total[4 * i : 4 * i + 4]
    powers = jnp.exp(table[...] - jnp.max(table[...], 0, keepdims=True))
    soft = powers / jnp.sum(powers, 0, keepdims=True)
    row = lax.broadcasted_iota(jnp.int32, soft.shape, 0)
    chosen = jnp.where((row >= 1) & (row <= LAYER), 1.0, 0.0)
    bound = jnp.sum(soft * chosen, 0, keepdims=True)
    d_table[...] = soft * (chosen - bound) * sums[3:4]
    z_sum.serve_range(served, z_sum.calls, True)
    z_sum.drain()
    sends_done(far, near, passed, quarter_copies, seq_copies, fsdp_copies)


def final_sum(rows_in, gains, table, mixer_part, act_pair, w_down, cid):
    n_seq, n_fsdp = lax.axis_size("seq"), lax.axis_size("fsdp")
    rows, width = rows_in[0].shape
    own, columns = mixer_part.shape
    units = w_down.shape[0]
    chans = columns // 4
    tokens = 4 * rows
    block = width // n_seq
    half = (rows // 2, width)
    terms = (8, chans // 2)
    shape = jax.ShapeDtypeStruct
    count = 6 + n_seq - 1 + 2 * (n_fsdp - 1)
    return pl.pallas_call(
        functools.partial(final_kernel, n_seq, n_fsdp),
        out_shape=(
            shape((rows, width), BF16),
            shape((rows, width), BF16),
            shape((chans, block), F32),
            shape((block, 3 * chans), F32),
            shape((4, width), F32),
            shape(table.shape, F32),
        ),
        in_specs=[VMEM] * 9 + [ANY] * 3,
        out_specs=(VMEM, VMEM, ANY, ANY, VMEM, VMEM),
        scratch_shapes=[
            pltpu.VMEM((chans, block), F32),
            pltpu.VMEM((block, 3 * chans), F32),
            pltpu.VMEM((own, columns), BF16),
            pltpu.VMEM((own + block, columns), BF16),
            pltpu.VMEM((tokens, units), BF16),
            pltpu.VMEM((units, width), BF16),
            pltpu.VMEM((tokens, width), BF16),
            pltpu.VMEM((3,) + half, BF16),
            pltpu.VMEM((3,) + half, BF16),
            pltpu.VMEM(half, BF16),
            pltpu.VMEM(half, BF16),
            pltpu.VMEM((1, width), F32),
            pltpu.VMEM((n_fsdp, 8, chans), F32),
            pltpu.VMEM((n_fsdp - 1, 8, chans), F32),
            pltpu.VMEM(terms, F32),
            pltpu.VMEM((n_seq - 1,) + terms, F32),
            pltpu.VMEM(terms, F32),
            pltpu.VMEM((n_fsdp - 1,) + terms, F32),
            pltpu.SemaphoreType.DMA((count,)),
            pltpu.SemaphoreType.DMA((count,)),
            pltpu.SemaphoreType.DMA((2 + n_seq // 2,)),
        ]
        + line_sems(n_seq, columns, 256),
        compiler_params=params(cid),
        name="final_sum",
    )(*rows_in, *gains, table, mixer_part, act_pair, w_down)


def hand_over_kernel(count, pieces, *refs):
    sources, targets = refs[: len(refs) - 2 * count - 2], refs[len(refs) - 2 * count - 2 :]
    kept, arrived, left = targets[count : 2 * count], targets[2 * count], targets[2 * count + 1]
    loads, stores = [], []
    for n, (i, source, first, rows, column) in enumerate(pieces):
        at = pl.ds(first, rows)
        src = sources[source].at[at, pl.ds(column, kept[i].shape[1])]
        loads.append(copy_in(src, kept[i].at[at], arrived.at[n]))
    for n, (i, source, first, rows, column) in enumerate(pieces):
        at = pl.ds(first, rows)
        loads[n].wait()
        stores.append(copy_in(kept[i].at[at], targets[i].at[at], left.at[n]))
    for store in stores:
        store.wait()


def hand_over(arrays, wanted):
    pieces, shapes = [], []
    for i, (source, column, columns) in enumerate(wanted):
        x = arrays[source]
        height = x.shape[0]
        parts = max(1, height * columns * x.dtype.itemsize >> 18)
        parts = parts if height % (parts * 16) == 0 else 1
        rows = height // parts
        pieces += [(i, source, n * rows, rows, column) for n in range(parts)]
        shapes.append(((height, columns), x.dtype))
    return pl.pallas_call(
        functools.partial(hand_over_kernel, len(wanted), tuple(pieces)),
        out_shape=tuple(jax.ShapeDtypeStruct(*x) for x in shapes),
        in_specs=[ANY] * len(arrays),
        out_specs=(ANY,) * len(wanted),
        scratch_shapes=[pltpu.VMEM(*x) for x in shapes]
        + [pltpu.SemaphoreType.DMA((len(pieces),))] * 2,
        compiler_params=pltpu.CompilerParams(vmem_limit_bytes=56 << 20),
        name="hand_over",
    )(*arrays)


def plane_device(
    hidden,
    lengths,
    w_input,
    w_forget,
    w_gate_out,
    w_output,
    norm_gain,
    gate_gain,
    glu_gain,
    lower_table,
    w_glu_gate,
    w_glu_up,
    w_glu_down,
    cotangent,
):
    hidden, cotangent = hidden[0], cotangent[0]
    tokens = 4 * hidden.shape[0]
    gains = (norm_gain[None], gate_gain[None], glu_gain[None])
    (
        normed_half,
        cot_all,
        in_raw,
        fg_raw,
        gate_raw,
        state_b,
        out_raw,
        before,
        scale_g,
        middle,
        normed_two,
    ) = mixer_forward(
        lengths,
        hidden,
        cotangent,
        gains,
        lower_table,
        (w_input, w_forget, w_gate_out, w_output),
        0,
    )
    two_half, cot_half, act_pair, gate_pair, up_pair = glu(
        normed_two, cot_all, w_glu_gate, w_glu_up, w_glu_down, 1
    )
    d_normed_two, pair_part, down_grad = down_sum(
        *(x.reshape(2 * tokens, -1) for x in (cot_half, act_pair, two_half, gate_pair, up_pair)),
        w_glu_gate,
        w_glu_up,
        2,
    )
    pair_grad, mixer_part, d_normed, d_middle, d_glu_gain, d_gain, d_bounds = pair_sum(
        lengths,
        (hidden, cotangent),
        (gains[2], gains[1]),
        lower_table,
        scale_g,
        (d_normed_two, middle),
        pair_part,
        (w_output, w_input, w_forget, w_gate_out),
        (gate_raw, state_b, out_raw, in_raw, fg_raw, before),
        normed_half.reshape(2 * tokens, -1),
        3,
    )
    output, d_hidden, out_grad, rest_grad, sums, d_table = final_sum(
        (d_normed, d_middle, hidden, middle),
        (gains[0], d_glu_gain, d_gain, d_bounds),
        lower_table,
        mixer_part,
        act_pair.reshape(2 * tokens, -1),
        w_glu_down,
        4,
    )
    width, chans, units = hidden.shape[1], w_input.shape[1], w_glu_gate.shape[1]
    block = down_grad.shape[1]
    (
        down_grad,
        gate_grad,
        up_grad,
        output,
        d_hidden,
        d_table,
        out_grad,
        in_grad,
        fg_grad,
        gt_grad,
    ) = hand_over(
        (down_grad, pair_grad, output, d_hidden, d_table, out_grad, rest_grad),
        (
            (0, 0, block),
            (1, 0, units),
            (1, units, units),
            (2, 0, width),
            (3, 0, width),
            (4, 0, width),
            (5, 0, block),
            (6, 0, chans),
            (6, chans, chans),
            (6, 2 * chans, chans),
        ),
    )
    return (
        output[None],
        d_hidden[None],
        in_grad,
        fg_grad,
        gt_grad,
        out_grad,
        sums[0],
        sums[2],
        sums[1],
        d_table,
        gate_grad,
        up_grad,
        down_grad,
    )


def fits_plane(mesh):
    return mesh.shape["fsdp"] == 4 and mesh.shape["seq"] % 2 == 0


def solution(mesh):
    rows_spec = P("fsdp", "seq", None)
    columns = P(None, "fsdp")
    placed = (
        rows_spec,
        P(),
        columns,
        columns,
        columns,
        P("fsdp", None),
        P(),
        P(),
        P(),
        P(),
        columns,
        columns,
        P("fsdp", None),
        rows_spec,
    )
    by_rows, by_columns = P("seq", "fsdp"), P("fsdp", "seq")
    return jax.shard_map(
        plane_device if fits_plane(mesh) else per_device,
        mesh=mesh,
        in_specs=placed,
        out_specs=(
            rows_spec,
            rows_spec,
            by_rows,
            by_rows,
            by_rows,
            by_columns,
            P(),
            P(),
            P(),
            P(),
            by_rows,
            by_rows,
            by_columns,
        ),
        check_vma=False,
    )
```

```python
import functools

import jax
import jax.numpy as jnp
from jax import lax
from jax.experimental import pallas as pl
from jax.experimental.pallas import tpu as pltpu
from jax.sharding import PartitionSpec as P

LAYER = 12
MESH = pl.DeviceIdType.MESH
F32 = jnp.float32
BF16 = jnp.bfloat16

epsilon = 1e-06

VMEM = pl.BlockSpec(memory_space=pltpu.VMEM)
ANY = pl.BlockSpec(memory_space=pl.ANY)


def lower_bound(table):
    soft = jax.nn.softmax(table, axis=0)
    totals = jnp.cumsum(soft, axis=0)
    return totals[LAYER] - totals[0]


def silu_slope(value, sigma):
    return sigma * (1.0 + value * (1.0 - sigma))


def params(collective_id):
    return pltpu.CompilerParams(
        collective_id=collective_id, has_side_effects=True, vmem_limit_bytes=56 << 20
    )


def round_up(value, unit):
    return -(-value // unit) * unit


def plane():
    s = lax.axis_index("seq")
    f = lax.axis_index("fsdp")
    y, x = f // 2, f % 2
    fx = y * 2 + (1 - x)
    fy = (1 - y) * 2 + x
    fd = (1 - y) * 2 + (1 - x)
    return s, f, fx, fy, fd


def enter(devices):
    barrier = pltpu.get_barrier_semaphore()
    for device in devices:
        pl.semaphore_signal(barrier, inc=1, device_id=device, device_id_type=MESH)
    pl.semaphore_wait(barrier, len(devices))


def remote(src, dst, send, recv, device):
    return pltpu.make_async_remote_copy(
        src_ref=src,
        dst_ref=dst,
        send_sem=send,
        recv_sem=recv,
        device_id=device,
        device_id_type=MESH,
    )


def gather(x, small, collective_id):
    return lax.all_gather(x, "fsdp"), lax.all_gather(small, "fsdp")


def reduce_rows(p, small, collective_id):
    total = lax.psum_scatter(p, "fsdp", scatter_dimension=0, tiled=True)[0]
    return total.astype(F32), lax.psum(small, "fsdp")


def start_exchange(total, gathered, send, recv, n_seq):
    s = lax.axis_index("seq")
    f = lax.axis_index("fsdp")
    copies = []
    for k in range(1, n_seq):
        peer = lax.rem(s + k, n_seq)
        copy = remote(total, gathered.at[s], send.at[k], recv.at[k], (peer, f))
        copy.start()
        copies.append(copy)
    gathered[pl.ds(s, 1)] = total[...][None]
    return copies


def seq_peers(n_seq):
    s = lax.axis_index("seq")
    f = lax.axis_index("fsdp")
    return [(lax.rem(s + k, n_seq), f) for k in range(1, n_seq)]


def lane_blocks(groups, chans):
    return [(g, slice(c, c + 128)) for g in range(groups) for c in range(0, chans, 128)]


def forward_scan_kernel(
    n_seq, in_raw, forget_raw, bounds, keep, state_b, before, a_ref, b_ref, total, gathered, send, recv
):
    groups, rows, chans = in_raw.shape
    part = rows // 8
    blocks = lane_blocks(groups, chans)
    s = lax.axis_index("seq")
    barrier = pltpu.get_barrier_semaphore()
    for peer in seq_peers(n_seq):
        pl.semaphore_signal(barrier, inc=1, device_id=peer, device_id_type=MESH)
    for n, (g, lanes) in enumerate(blocks):
        bound = bounds[:, lanes]
        forget = bound + (1.0 - bound) * jax.nn.sigmoid(forget_raw[g, :, lanes].astype(F32))
        value = in_raw[g, :, lanes].astype(F32)
        a_ref[n] = forget * keep[g]
        b_ref[n] = value * jax.nn.sigmoid(value) * (1.0 - forget)

    def step(i, carry):
        new = []
        at = pl.ds(i, 8, stride=part)
        for n, (product, state) in enumerate(carry):
            a = a_ref[n, at, :]
            state = a * state + b_ref[n, at, :]
            product = product * a
            a_ref[n, at, :] = product
            b_ref[n, at, :] = state
            new.append((product, state))
        return tuple(new)

    start = tuple((jnp.ones((8, 128), F32), jnp.zeros((8, 128), F32)) for _ in blocks)
    ends = lax.fori_loop(0, part, step, start)
    for n, (product, state) in enumerate(ends):
        p_all, s_all = product[0:1], state[0:1]
        for j in range(1, 8):
            p_all, s_all = p_all * product[j : j + 1], state[j : j + 1] + product[j : j + 1] * s_all
        total[2 * n : 2 * n + 1] = p_all
        total[2 * n + 1 : 2 * n + 2] = s_all
    pl.semaphore_wait(barrier, n_seq - 1)
    copies = start_exchange(total, gathered, send, recv, n_seq)
    for copy in copies:
        copy.wait()
    for n, (g, lanes) in enumerate(blocks):
        carry = jnp.zeros((1, 128), F32)
        for j in range(n_seq - 1):
            p_j = gathered[j, 2 * n : 2 * n + 1]
            s_j = gathered[j, 2 * n + 1 : 2 * n + 2]
            carry = jnp.where(j < s, s_j + p_j * carry, carry)
        before[g, 0:1, lanes] = carry
        product, state = ends[n]
        carries = [carry]
        for j in range(7):
            carries.append(state[j : j + 1] + product[j : j + 1] * carries[-1])
        for j in range(8):
            at = slice(j * part, (j + 1) * part)
            b_ref[n, at] = b_ref[n, at] + a_ref[n, at] * carries[j]
        state_b[g, :, lanes] = b_ref[n].astype(BF16)
        before[g, 1:rows, lanes] = b_ref[n, 0 : rows - 1]


def forward_scan(in_raw, forget_raw, bounds, keep, collective_id):
    n_seq = lax.axis_size("seq")
    groups, rows, chans = in_raw.shape
    blocks = groups * chans // 128
    return pl.pallas_call(
        functools.partial(forward_scan_kernel, n_seq),
        out_shape=(
            jax.ShapeDtypeStruct(in_raw.shape, BF16),
            jax.ShapeDtypeStruct(in_raw.shape, F32),
        ),
        in_specs=[VMEM] * 4,
        out_specs=(VMEM, VMEM),
        scratch_shapes=[
            pltpu.VMEM((blocks, rows, 128), F32),
            pltpu.VMEM((blocks, rows, 128), F32),
            pltpu.VMEM((2 * blocks, 128), F32),
            pltpu.VMEM((n_seq, 2 * blocks, 128), F32),
            pltpu.SemaphoreType.DMA((n_seq,)),
            pltpu.SemaphoreType.DMA((n_seq,)),
        ],
        compiler_params=params(collective_id),
        name="forward_scan",
    )(in_raw, forget_raw, bounds, keep)


def backward_scan_kernel(
    n_seq,
    d_state,
    in_raw,
    forget_raw,
    before,
    bounds,
    keep,
    d_in,
    d_forget_raw,
    d_bounds,
    p_ref,
    q_ref,
    total,
    gathered,
    send,
    recv,
):
    groups, rows, chans = in_raw.shape
    part = rows // 8
    blocks = lane_blocks(groups, chans)
    s = lax.axis_index("seq")
    barrier = pltpu.get_barrier_semaphore()
    for peer in seq_peers(n_seq):
        pl.semaphore_signal(barrier, inc=1, device_id=peer, device_id_type=MESH)
    for n, (g, lanes) in enumerate(blocks):
        bound = bounds[:, lanes]
        forget = bound + (1.0 - bound) * jax.nn.sigmoid(forget_raw[g, :, lanes].astype(F32))
        p_ref[n] = forget * keep[g]
        q_ref[n] = d_state[g, :, lanes].astype(F32)

    def step(i, carry):
        new = []
        at = pl.ds(part - 1 - i, 8, stride=part)
        for n, (product, message) in enumerate(carry):
            a = p_ref[n, at, :]
            acc = q_ref[n, at, :] + message
            p_ref[n, at, :] = product
            q_ref[n, at, :] = acc
            new.append((product * a, a * acc))
        return tuple(new)

    start = tuple((jnp.ones((8, 128), F32), jnp.zeros((8, 128), F32)) for _ in blocks)
    ends = lax.fori_loop(0, part, step, start)
    for n, (product, message) in enumerate(ends):
        p_all, m_all = product[7:8], message[7:8]
        for j in range(6, -1, -1):
            p_all, m_all = p_all * product[j : j + 1], message[j : j + 1] + product[j : j + 1] * m_all
        total[2 * n : 2 * n + 1] = p_all
        total[2 * n + 1 : 2 * n + 2] = m_all
    pl.semaphore_wait(barrier, n_seq - 1)
    copies = start_exchange(total, gathered, send, recv, n_seq)
    for copy in copies:
        copy.wait()
    d_bounds[...] = jnp.zeros((1, chans), F32)
    for n, (g, lanes) in enumerate(blocks):
        carry = jnp.zeros((1, 128), F32)
        for j in range(n_seq - 1, 0, -1):
            p_j = gathered[j, 2 * n : 2 * n + 1]
            m_j = gathered[j, 2 * n + 1 : 2 * n + 2]
            carry = jnp.where(j > s, m_j + p_j * carry, carry)
        product, message = ends[n]
        carries = [carry]
        for j in range(7, 0, -1):
            carries.append(message[j : j + 1] + product[j : j + 1] * carries[-1])
        carries = carries[::-1]
        for j in range(8):
            at = slice(j * part, (j + 1) * part)
            q_ref[n, at] = q_ref[n, at] + p_ref[n, at] * carries[j]
        acc = q_ref[n]
        bound = bounds[:, lanes]
        sigma_f = jax.nn.sigmoid(forget_raw[g, :, lanes].astype(F32))
        forget = bound + (1.0 - bound) * sigma_f
        value = in_raw[g, :, lanes].astype(F32)
        sigma_i = jax.nn.sigmoid(value)
        d_forget = acc * (before[g, :, lanes] * keep[g] - value * sigma_i)
        d_in[g, :, lanes] = (acc * (1.0 - forget) * silu_slope(value, sigma_i)).astype(BF16)
        d_sigma = d_forget * (1.0 - sigma_f)
        d_forget_raw[g, :, lanes] = (d_sigma * (1.0 - bound) * sigma_f).astype(BF16)
        d_bounds[:, lanes] += jnp.sum(d_sigma, 0, keepdims=True)


def backward_scan(d_state, in_raw, forget_raw, before, bounds, keep, collective_id):
    n_seq = lax.axis_size("seq")
    groups, rows, chans = in_raw.shape
    blocks = groups * chans // 128
    return pl.pallas_call(
        functools.partial(backward_scan_kernel, n_seq),
        out_shape=(
            jax.ShapeDtypeStruct(in_raw.shape, BF16),
            jax.ShapeDtypeStruct(in_raw.shape, BF16),
            jax.ShapeDtypeStruct((1, chans), F32),
        ),
        in_specs=[VMEM] * 6,
        out_specs=(VMEM, VMEM, VMEM),
        scratch_shapes=[
            pltpu.VMEM((blocks, rows, 128), F32),
            pltpu.VMEM((blocks, rows, 128), F32),
            pltpu.VMEM((2 * blocks, 128), F32),
            pltpu.VMEM((n_seq, 2 * blocks, 128), F32),
            pltpu.SemaphoreType.DMA((n_seq,)),
            pltpu.SemaphoreType.DMA((n_seq,)),
        ],
        compiler_params=params(collective_id),
        name="backward_scan",
    )(d_state, in_raw, forget_raw, before, bounds, keep)


def sum_all_kernel(n_seq, n_fsdp, x, out, middle, over_seq, over_fsdp, send, recv):
    s = lax.axis_index("seq")
    f = lax.axis_index("fsdp")
    along = [(lax.rem(s + k, n_seq), f) for k in range(1, n_seq)]
    across = [(s, lax.rem(f + k, n_fsdp)) for k in range(1, n_fsdp)]
    enter(along + across)
    copies = []
    for k, peer in enumerate(along):
        copy = remote(x, over_seq.at[k], send.at[k], recv.at[k], peer)
        copy.start()
        copies.append(copy)
    total = x[...]
    for k, copy in enumerate(copies):
        copy.wait_recv()
        total = total + over_seq[k]
    middle[...] = total
    later = []
    for k, peer in enumerate(across):
        slot = n_seq - 1 + k
        copy = remote(middle, over_fsdp.at[k], send.at[slot], recv.at[slot], peer)
        copy.start()
        later.append(copy)
    for k, copy in enumerate(later):
        copy.wait_recv()
        total = total + over_fsdp[k]
    out[...] = total
    for copy in copies + later:
        copy.wait_send()


def sum_all(x, collective_id):
    n_seq, n_fsdp = lax.axis_size("seq"), lax.axis_size("fsdp")
    count = n_seq + n_fsdp - 2
    return pl.pallas_call(
        functools.partial(sum_all_kernel, n_seq, n_fsdp),
        out_shape=jax.ShapeDtypeStruct(x.shape, F32),
        in_specs=[VMEM],
        out_specs=VMEM,
        scratch_shapes=[
            pltpu.VMEM(x.shape, F32),
            pltpu.VMEM((n_seq - 1,) + x.shape, F32),
            pltpu.VMEM((n_fsdp - 1,) + x.shape, F32),
            pltpu.SemaphoreType.DMA((count,)),
            pltpu.SemaphoreType.DMA((count,)),
        ],
        compiler_params=params(collective_id),
        name="sum_all",
    )(x)


def sum_over_seq(part):
    return lax.psum_scatter(part.astype(BF16), "seq", scatter_dimension=0, tiled=True).astype(F32)


def per_device(
    hidden,
    lengths,
    w_input,
    w_forget,
    w_gate_out,
    w_output,
    norm_gain,
    gate_gain,
    glu_gain,
    lower_table,
    w_glu_gate,
    w_glu_up,
    w_glu_down,
    cotangent,
):
    seq_index = lax.axis_index("seq")
    fsdp_index = lax.axis_index("fsdp")
    groups = lax.axis_size("fsdp")
    _, rows, width = hidden.shape
    chans = w_input.shape[1]
    units = w_glu_gate.shape[1]
    tokens = groups * rows
    small_shape = (round_up(groups, 8), round_up(rows, 128))

    def to_small(value):
        return jnp.pad(
            value, ((0, small_shape[0] - value.shape[0]), (0, small_shape[1] - value.shape[1]))
        )

    def dot(left, right):
        return jnp.dot(left, right, preferred_element_type=F32)

    def dot_t(left, right):
        return lax.dot_general(left, right, (((1,), (1,)), ((), ())), preferred_element_type=F32)

    def over_tokens(left, right):
        return lax.dot_general(left, right, (((0,), (0,)), ((), ())), preferred_element_type=F32)

    cotangent_all = lax.all_gather(cotangent[0], "fsdp").reshape(tokens, width)

    hidden_f = hidden[0].astype(F32)
    scale_one = lax.rsqrt(jnp.mean(hidden_f * hidden_f, -1, keepdims=True) + epsilon)
    normed = (hidden_f * scale_one * norm_gain).astype(BF16)
    normed_all, _ = gather(normed, jnp.zeros((8, 128), F32), 0)
    normed_all = normed_all.reshape(tokens, width)
    in_raw = dot(normed_all, w_input).astype(BF16).reshape(groups, rows, chans)
    forget_raw = dot(normed_all, w_forget).astype(BF16).reshape(groups, rows, chans)
    gate_raw = dot(normed_all, w_gate_out)

    bounds_full = lower_bound(lower_table)
    bounds = lax.dynamic_slice_in_dim(bounds_full, fsdp_index * chans, chans)[None]
    seq_starts = jnp.cumsum(lengths, axis=1) - lengths
    places = seq_index * rows + jnp.arange(rows, dtype=jnp.int32)
    starts = jnp.any(places[None, :, None] == seq_starts[:, None, :], axis=-1)
    keep = jnp.where(starts, 0.0, 1.0).astype(F32)[:, :, None]
    state_b, before = forward_scan(in_raw, forget_raw, bounds, keep, 1)

    state_f = state_b.astype(F32).reshape(tokens, chans)
    gain_slice = lax.dynamic_slice_in_dim(gate_gain, fsdp_index * chans, chans)
    sigma_g = jax.nn.sigmoid(gate_raw)
    silu_gate = gate_raw * sigma_g
    out_raw = (state_f * gain_slice * silu_gate).astype(BF16)
    squares = jnp.sum(state_f * state_f, -1).reshape(groups, rows)
    mixed_part = dot(out_raw, w_output).astype(BF16).reshape(groups, rows, width)
    mixed_raw, square_sum = reduce_rows(mixed_part, to_small(squares), 2)
    state_scale = lax.rsqrt(square_sum[:groups, :rows] / width + epsilon)
    own_scale = lax.dynamic_slice_in_dim(state_scale, fsdp_index, 1, 0)[0][:, None]
    scale_g = state_scale.reshape(tokens, 1)
    middle = hidden_f + own_scale * mixed_raw
    scale_two = lax.rsqrt(jnp.mean(middle * middle, -1, keepdims=True) + epsilon)
    normed_two = (middle * scale_two * glu_gain).astype(BF16)
    normed_two_all, _ = gather(normed_two, jnp.zeros((8, 128), F32), 3)
    normed_two_all = normed_two_all.reshape(tokens, width)

    gate_val = dot(normed_two_all, w_glu_gate)
    up_val = dot(normed_two_all, w_glu_up)
    sigma_u = jax.nn.sigmoid(gate_val)
    silu_u = gate_val * sigma_u
    activity = (silu_u * up_val).astype(BF16)
    down_grad = sum_over_seq(over_tokens(cotangent_all, activity))
    d_act = dot_t(cotangent_all, w_glu_down)
    d_gate = (d_act * up_val * silu_slope(gate_val, sigma_u)).astype(BF16)
    d_up = (d_act * silu_u).astype(BF16)
    pair_grad = sum_over_seq(
        jnp.concatenate(
            [
                over_tokens(normed_two_all, d_gate).astype(BF16),
                over_tokens(normed_two_all, d_up).astype(BF16),
            ],
            1,
        )
    )
    d_two_part = (dot_t(d_gate, w_glu_gate) + dot_t(d_up, w_glu_up)).astype(BF16)
    no_small = jnp.zeros((8, 128), F32)
    d_normed_two, _ = reduce_rows(d_two_part.reshape(groups, rows, width), no_small, 4)
    glu_part = dot(activity, w_glu_down).astype(BF16).reshape(groups, rows, width)
    glu_result = lax.psum_scatter(glu_part, "fsdp", scatter_dimension=0, tiled=True)[0]
    output = (middle + glu_result.astype(F32)).astype(BF16)[None]

    cotangent_f = cotangent[0].astype(F32)
    scaled_two = glu_gain * d_normed_two
    d_middle = (
        cotangent_f
        + scale_two * scaled_two
        - middle * scale_two**3 * jnp.mean(scaled_two * middle, -1, keepdims=True)
    )
    d_glu_gain = jnp.sum(d_normed_two * middle * scale_two, 0)
    d_mixed = d_middle.astype(BF16)
    own_dot = jnp.sum(d_mixed.astype(F32) * mixed_raw, -1)[None]
    d_mixed_all, dots = gather(d_mixed, to_small(own_dot), 5)
    d_mixed_all = d_mixed_all.reshape(tokens, width)
    dot_rows = dots[:, 0, :rows].reshape(tokens, 1)

    d_out = dot_t(d_mixed_all, w_output)
    scaled_state = state_f * scale_g
    d_gain_slice = jnp.sum(d_out * scaled_state * silu_gate, 0)
    d_scaled = d_out * gain_slice * silu_gate
    d_gate_raw = (d_out * scaled_state * gain_slice * silu_slope(gate_raw, sigma_g)).astype(BF16)
    d_state = scale_g * d_scaled - state_f * (scale_g**3 * (dot_rows / width))
    d_state = d_state.astype(BF16).reshape(groups, rows, chans)
    d_in, d_forget_raw, d_bounds = backward_scan(
        d_state, in_raw, forget_raw, before, bounds, keep, 6
    )
    d_in = d_in.reshape(tokens, chans)
    d_forget_raw = d_forget_raw.reshape(tokens, chans)

    d_normed_part = dot_t(d_in, w_input) + dot_t(d_forget_raw, w_forget)
    d_normed_part = (d_normed_part + dot_t(d_gate_raw, w_gate_out)).astype(BF16)
    out_gate = (out_raw.astype(F32) * scale_g).astype(BF16)
    mixer_grad = sum_over_seq(
        jnp.concatenate(
            [
                over_tokens(d_mixed_all, out_gate).astype(BF16),
                over_tokens(normed_all, d_in).astype(BF16),
                over_tokens(normed_all, d_forget_raw).astype(BF16),
                over_tokens(normed_all, d_gate_raw).astype(BF16),
            ],
            1,
        )
    )
    d_normed, _ = reduce_rows(d_normed_part.reshape(groups, rows, width), no_small, 7)
    scaled_one = norm_gain * d_normed
    d_hidden = (
        d_middle
        + scale_one * scaled_one
        - hidden_f * scale_one**3 * jnp.mean(scaled_one * hidden_f, -1, keepdims=True)
    )
    d_norm_gain = jnp.sum(d_normed * hidden_f * scale_one, 0)
    d_gain_full = lax.dynamic_update_slice(
        jnp.zeros((width,), F32), d_gain_slice, (fsdp_index * chans,)
    )
    d_bounds_full = lax.dynamic_update_slice(
        jnp.zeros((width,), F32), d_bounds[0], (fsdp_index * chans,)
    )
    sums = jnp.stack([d_norm_gain, d_glu_gain, d_gain_full, d_bounds_full])
    totals = sum_all(sums.reshape(8, width // 2), 8).reshape(4, width)
    _, bounds_pull = jax.vjp(lower_bound, lower_table)
    d_table = bounds_pull(totals[3])[0]
    return (
        output,
        d_hidden.astype(BF16)[None],
        mixer_grad[:, chans : 2 * chans],
        mixer_grad[:, 2 * chans : 3 * chans],
        mixer_grad[:, 3 * chans :],
        mixer_grad[:, :chans].T,
        totals[0],
        totals[2],
        totals[1],
        d_table,
        pair_grad[:, :units],
        pair_grad[:, units:],
        down_grad.T,
    )


def copy_in(src, dst, sem):
    copy = pltpu.make_async_copy(src, dst, sem)
    copy.start()
    return copy


class Links:
    def __init__(self, send, recv):
        self.send, self.recv, self.used = send, recv, 0

    def start(self, src, dst, device):
        copy = remote(src, dst, self.send.at[self.used], self.recv.at[self.used], device)
        self.used += 1
        copy.start()
        return copy


class Locals:
    def __init__(self, sems):
        self.sems, self.used = sems, 0

    def start(self, src, dst):
        copy = copy_in(src, dst, self.sems.at[self.used])
        self.used += 1
        return copy


def row_slots(rows):
    half = rows // 2
    top = [pl.ds(k * rows, half) for k in range(4)]
    bottom = [pl.ds(k * rows + half, half) for k in range(4)]
    return top, bottom


def gather_start(links, src, dst, rows, s, fx, fy):
    half = rows // 2
    top, bottom = row_slots(rows)
    here = (pl.ds(0, half), pl.ds(half, half))
    return [
        links.start(src.at[here[0]], dst.at[top[1]], (s, fx)),
        links.start(src.at[here[1]], dst.at[bottom[2]], (s, fy)),
        links.start(src.at[here[1]], dst.at[bottom[1]], (s, fx)),
        links.start(src.at[here[0]], dst.at[top[2]], (s, fy)),
    ]


def gather_forward(links, own, dst, rows, s, fx, fy):
    top, bottom = row_slots(rows)
    own[0].wait_recv()
    on_y = links.start(dst.at[top[1]], dst.at[top[3]], (s, fy))
    own[1].wait_recv()
    on_x = links.start(dst.at[bottom[2]], dst.at[bottom[3]], (s, fx))
    return [on_y, on_x]


def gather_middle(own):
    own[2].wait_recv()
    own[3].wait_recv()


def gather_far(later):
    for copy in later:
        copy.wait_recv()


def sends_done(*lists):
    for copies in lists:
        for copy in copies:
            copy.wait_send()


def wait_all(*lists):
    for copies in lists:
        for copy in copies:
            copy.wait()


def reduce_start_far(links, part, from_x, from_y, rows, s, fx, fy):
    top, bottom = row_slots(rows)
    return [
        links.start(part.at[top[3]], from_x.at[0], (s, fx)),
        links.start(part.at[bottom[3]], from_y.at[0], (s, fy)),
    ]


def reduce_start_near(links, part, from_x, from_y, rows, s, fx, fy):
    top, bottom = row_slots(rows)
    return [
        links.start(part.at[top[1]], from_x.at[1], (s, fx)),
        links.start(part.at[bottom[2]], from_y.at[1], (s, fy)),
    ]


def reduce_pass(links, far, part, from_x, from_y, pass_x, pass_y, rows, s, fx, fy):
    top, bottom = row_slots(rows)
    far[0].wait_recv()
    pass_y[...] = (from_x[0].astype(F32) + part[top[2]].astype(F32)).astype(BF16)
    on_y = links.start(pass_y, from_y.at[2], (s, fy))
    far[1].wait_recv()
    pass_x[...] = (from_y[0].astype(F32) + part[bottom[1]].astype(F32)).astype(BF16)
    on_x = links.start(pass_x, from_x.at[2], (s, fx))
    return [on_y, on_x]


def mm(left, right):
    return jnp.dot(left, right, preferred_element_type=F32)


def mm_t(left, right):
    return lax.dot_general(left, right, (((1,), (1,)), ((), ())), preferred_element_type=F32)


def tile(n, width):
    return pl.ds(pl.multiple_of(n * width, width), width)


def bounds_slice(table, first, count):
    rows = table[:, pl.ds(pl.multiple_of(first, 128), count)]
    powers = jnp.exp(rows - jnp.max(rows, 0, keepdims=True))
    return jnp.sum(powers[1 : LAYER + 1], 0, keepdims=True) / jnp.sum(powers, 0, keepdims=True)


def keep_rows(lengths, group, first, rows):
    places = first + lax.broadcasted_iota(jnp.int32, (rows, 128), 0)
    start = jnp.int32(0)
    keep = jnp.where(places == start, 0.0, 1.0)
    for i in range(lengths.shape[1] - 1):
        start = start + lengths[group, i]
        keep = jnp.where(places == start, 0.0, keep)
    return keep.astype(F32)


def segment_totals(end_p, end_s, blocks, order):
    first, rest = order[0], order[1:]
    p_all = end_p[pl.ds(first, blocks, stride=8), :]
    s_all = end_s[pl.ds(first, blocks, stride=8), :]
    for j in rest:
        p_j = end_p[pl.ds(j, blocks, stride=8), :]
        s_all = end_s[pl.ds(j, blocks, stride=8), :] + p_j * s_all
        p_all = p_all * p_j
    return p_all, s_all


def spread_carry(carry, carr, end_p, end_s, blocks, order):
    for i, j in enumerate(order):
        carr[pl.ds(j, blocks, stride=8), :] = carry
        if i < 7:
            carry = end_s[pl.ds(j, blocks, stride=8), :] + end_p[pl.ds(j, blocks, stride=8), :] * carry


def mixer_kernel(
    n_seq,
    lengths,
    hidden,
    cot,
    norm_gain,
    gate_gain,
    glu_gain,
    table,
    w_in,
    w_fg,
    w_gt,
    w_out,
    normed_half,
    cot_out,
    in_out,
    fg_out,
    gate_out,
    state_out,
    raw_out,
    before_out,
    scale_out,
    middle,
    two,
    wv,
    wo,
    rows_all,
    stage,
    in_ref,
    fg_ref,
    gate_ref,
    a_ref,
    b_ref,
    shifted,
    keep_ref,
    end_p,
    end_s,
    carr,
    total,
    gathered,
    state_ref,
    raw_ref,
    squares,
    squares_t,
    packed,
    squares_in,
    part,
    from_x,
    from_y,
    pass_x,
    pass_y,
    send,
    recv,
    exchange_send,
    exchange_recv,
    local_sems,
):
    rows, width = hidden.shape
    chans = w_in.shape[1]
    lanes_of = [slice(c, c + 128) for c in range(0, chans, 128)]
    count = len(lanes_of)
    blocks = 4 * count
    step_len = rows // 8
    s, f, fx, fy, fd = plane()
    groups = [f, fx, fy, fd]
    links, local = Links(send, recv), Locals(local_sems)

    weights = [
        local.start(w, wv.at[:, pl.ds(i * chans, chans)]) for i, w in enumerate((w_in, w_fg, w_gt))
    ]
    weights.append(local.start(w_out, wo))
    barrier = pltpu.get_barrier_semaphore()
    peers = [(s, fx), (s, fy), (s, fd)] + seq_peers(n_seq)
    for peer in peers:
        pl.semaphore_signal(barrier, inc=1, device_id=peer, device_id_type=MESH)

    def norm_rows(i, _):
        at = pl.ds(pl.multiple_of(i * 16, 16), 16)
        value = hidden[at].astype(F32)
        scale = lax.rsqrt(jnp.mean(value * value, -1, keepdims=True) + epsilon)
        rows_all[at] = (value * scale * norm_gain[...]).astype(BF16)
        return 0

    lax.fori_loop(0, rows // 16, norm_rows, 0)
    pl.semaphore_wait(barrier, len(peers))
    own = gather_start(links, rows_all, rows_all, rows, s, fx, fy)
    bound = bounds_slice(table, f * chans, chans)
    for k in range(4):
        keep_ref[k] = keep_rows(lengths, groups[k], s * rows, rows)
    squares[...] = jnp.zeros_like(squares)
    squares_t[...] = jnp.zeros_like(squares_t)
    for copy in weights[:3]:
        copy.wait()

    def project(first, slots):
        def tile_of(n, _):
            cols = tile(n, 256)
            stage[: slots * rows, cols] = mm(
                rows_all[first * rows : (first + slots) * rows], wv[:, cols]
            )
            return 0

        lax.fori_loop(0, 3 * chans // 256, tile_of, 0)
        for k in range(slots):
            at = slice(k * rows, (k + 1) * rows)
            for c, lanes in enumerate(lanes_of):
                n = (first + k) * count + c
                value = stage[at, lanes].astype(BF16)
                in_ref[first + k, :, lanes] = value
                value = value.astype(F32)
                raw = stage[at, chans + c * 128 : chans + (c + 1) * 128].astype(BF16)
                fg_ref[first + k, :, lanes] = raw
                edge = bound[:, lanes]
                forget = edge + (1.0 - edge) * jax.nn.sigmoid(raw.astype(F32))
                a_ref[n] = forget * keep_ref[first + k]
                b_ref[n] = value * jax.nn.sigmoid(value) * (1.0 - forget)
            gate_ref[first + k] = stage[at, 2 * chans :]

    project(0, 1)
    later = gather_forward(links, own, rows_all, rows, s, fx, fy)
    gather_middle(own)
    project(1, 2)
    gather_far(later)
    cot_own = gather_start(links, cot, cot_out, rows, s, fx, fy)
    core = s % 2
    swaps, outs = swap_columns(
        links, local, rows_all, normed_half, n_seq, core, (s + 1 - 2 * core, f)
    )
    outs.append(local.start(cot, cot_out.at[pl.ds(0, rows)]))
    project(3, 1)
    outs += [
        local.start(in_ref, in_out),
        local.start(fg_ref, fg_out),
        local.start(gate_ref, gate_out),
    ]

    def scan_step(i, carry):
        new = []
        at = pl.ds(i, 8, stride=step_len)
        for n, (product, state) in enumerate(carry):
            a = a_ref[n, at, :]
            state = a * state + b_ref[n, at, :]
            product = product * a
            a_ref[n, at, :] = product
            b_ref[n, at, :] = state
            new.append((product, state))
        return tuple(new)

    start = tuple((jnp.ones((8, 128), F32), jnp.zeros((8, 128), F32)) for _ in range(blocks))
    ends = lax.fori_loop(0, step_len, scan_step, start)
    for n, (product, state) in enumerate(ends):
        end_p[8 * n : 8 * n + 8] = product
        end_s[8 * n : 8 * n + 8] = state
    p_all, s_all = segment_totals(end_p, end_s, blocks, range(8))
    total[:blocks] = p_all
    total[blocks:] = s_all
    copies = start_exchange(total, gathered, exchange_send, exchange_recv, n_seq)
    wait_all(copies)
    carry = jnp.zeros((blocks, 128), F32)
    for j in range(n_seq - 1):
        carry = jnp.where(j < s, gathered[j, blocks:] + gathered[j, :blocks] * carry, carry)
    for n in range(blocks):
        shifted[n, 0:1] = carry[n : n + 1]
    spread_carry(carry, carr, end_p, end_s, blocks, range(8))

    def finish(n, _):
        enter_state = carr[pl.ds(pl.multiple_of(n * 8, 8), 8)]
        for i in range(step_len):
            at = pl.ds(i, 8, stride=step_len)
            state = b_ref[n, at, :] + a_ref[n, at, :] * enter_state
            b_ref[n, at, :] = state
            shifted[n, pl.ds(i + 1, 8, stride=step_len), :] = state
        return 0

    lax.fori_loop(0, blocks, finish, 0)
    outs.append(local.start(shifted.at[:, pl.ds(0, rows)], before_out))

    lane = lax.broadcasted_iota(jnp.int32, (rows, 128), 1)
    for k in (3, 1, 2, 0):
        square = jnp.zeros((rows, 1), F32)
        for c, lanes in enumerate(lanes_of):
            state_b = b_ref[k * count + c].astype(BF16)
            state_ref[k, :, lanes] = state_b
            state = state_b.astype(F32)
            square = square + jnp.sum(state * state, -1, keepdims=True)
            gate = gate_ref[k, :, lanes]
            gain = gate_gain[:, pl.ds(pl.multiple_of(f * chans + c * 128, 128), 128)]
            raw_ref[k * rows : (k + 1) * rows, lanes] = (
                state * gain * gate * jax.nn.sigmoid(gate)
            ).astype(BF16)
        squares[:rows] = jnp.where(lane == groups[k], square, squares[:rows])
    packed[...] = squares[...].T[:8]
    square_copies = [
        links.start(packed, squares_in.at[i], (s, peer)) for i, peer in enumerate((fx, fy, fd))
    ]
    outs += [local.start(state_ref, state_out), local.start(raw_ref, raw_out)]
    cot_later = gather_forward(links, cot_own, cot_out, rows, s, fx, fy)
    weights[3].wait()

    def output_part(first, slots):
        at = slice(first * rows, (first + slots) * rows)

        def tile_of(n, _):
            cols = tile(n, 512)
            part[at, cols] = mm(raw_ref[at], wo[:, cols]).astype(BF16)
            return 0

        lax.fori_loop(0, width // 512, tile_of, 0)

    output_part(3, 1)
    far = reduce_start_far(links, part, from_x, from_y, rows, s, fx, fy)
    output_part(1, 2)
    near = reduce_start_near(links, part, from_x, from_y, rows, s, fx, fy)
    output_part(0, 1)
    passed = reduce_pass(links, far, part, from_x, from_y, pass_x, pass_y, rows, s, fx, fy)
    for copy in square_copies:
        copy.wait_recv()
    all_squares = (packed[...] + squares_in[0]) + (squares_in[1] + squares_in[2])
    squares_t[:8] = lax.rsqrt(all_squares / width + epsilon)
    scales = squares_t[...].T[:rows]
    for k in range(4):
        scale_out[k] = jnp.sum(jnp.where(lane == groups[k], scales, 0.0), -1, keepdims=True)
    for copy in near + passed:
        copy.wait_recv()
    half = rows // 2
    for first, one, other in ((0, from_x.at[1], from_y.at[2]), (half, from_y.at[1], from_x.at[2])):

        def sum_rows(i, _):
            here = pl.ds(pl.multiple_of(i * 16, 16), 16)
            at = pl.ds(pl.multiple_of(first + i * 16, 16), 16)
            mixed = part[at].astype(F32) + one[here].astype(F32) + other[here].astype(F32)
            value = hidden[at].astype(F32) + scale_out[0, at] * mixed
            middle[at] = value
            scale = lax.rsqrt(jnp.mean(value * value, -1, keepdims=True) + epsilon)
            two[at] = (value * scale * glu_gain[...]).astype(BF16)
            return 0

        lax.fori_loop(0, half // 16, sum_rows, 0)
    gather_middle(cot_own)
    gather_far(cot_later)
    sends_done(own, later, cot_own, cot_later, square_copies, far, near, passed)
    wait_all(swaps, outs)


def mixer_forward(lengths, hidden, cot, gains, table, weights, collective_id):
    n_seq = lax.axis_size("seq")
    rows, width = hidden.shape
    chans = weights[0].shape[1]
    blocks = 4 * chans // 128
    tokens = 4 * rows
    half = rows // 2
    shape = jax.ShapeDtypeStruct
    wide = shape((tokens, width), BF16)
    narrow = shape((4, rows, chans), BF16)
    long_rows = round_up(rows, 128)
    return pl.pallas_call(
        functools.partial(mixer_kernel, n_seq),
        out_shape=(
            shape((2, tokens, width // 2), BF16),
            wide,
            narrow,
            narrow,
            shape((4, rows, chans), F32),
            narrow,
            shape((tokens, chans), BF16),
            shape((blocks, rows, 128), F32),
            shape((4, rows, 1), F32),
            shape((rows, width), F32),
            shape((rows, width), BF16),
        ),
        in_specs=[pl.BlockSpec(memory_space=pltpu.SMEM), VMEM, VMEM, VMEM, VMEM, VMEM, VMEM]
        + [ANY] * 4,
        out_specs=(ANY,) * 8 + (VMEM,) * 3,
        scratch_shapes=[
            pltpu.VMEM((width, 3 * chans), BF16),
            pltpu.VMEM((chans, width), BF16),
            pltpu.VMEM((tokens, width), BF16),
            pltpu.VMEM((2 * rows, 3 * chans), F32),
            pltpu.VMEM((4, rows, chans), BF16),
            pltpu.VMEM((4, rows, chans), BF16),
            pltpu.VMEM((4, rows, chans), F32),
            pltpu.VMEM((blocks, rows, 128), F32),
            pltpu.VMEM((blocks, rows, 128), F32),
            pltpu.VMEM((blocks, rows + 8, 128), F32),
            pltpu.VMEM((4, rows, 128), F32),
            pltpu.VMEM((8 * blocks, 128), F32),
            pltpu.VMEM((8 * blocks, 128), F32),
            pltpu.VMEM((8 * blocks, 128), F32),
            pltpu.VMEM((2 * blocks, 128), F32),
            pltpu.VMEM((n_seq, 2 * blocks, 128), F32),
            pltpu.VMEM((4, rows, chans), BF16),
            pltpu.VMEM((tokens, chans), BF16),
            pltpu.VMEM((long_rows, 128), F32),
            pltpu.VMEM((128, long_rows), F32),
            pltpu.VMEM((8, long_rows), F32),
            pltpu.VMEM((3, 8, long_rows), F32),
            pltpu.VMEM((tokens, width), BF16),
            pltpu.VMEM((3, half, width), BF16),
            pltpu.VMEM((3, half, width), BF16),
            pltpu.VMEM((half, width), BF16),
            pltpu.VMEM((half, width), BF16),
            pltpu.SemaphoreType.DMA((21 + n_seq // 2,)),
            pltpu.SemaphoreType.DMA((21 + n_seq // 2,)),
            pltpu.SemaphoreType.DMA((n_seq,)),
            pltpu.SemaphoreType.DMA((n_seq,)),
            pltpu.SemaphoreType.DMA((11 + n_seq // 2,)),
        ],
        compiler_params=params(collective_id),
        name="mixer_forward",
    )(lengths, hidden, cot, *gains, table, *weights)


def swap_columns(links, local, src, dst, n_seq, core, mate):
    part = src.shape[1] // n_seq
    copies, stays = [], []
    for z in range(n_seq // 2):
        to = pl.ds(z * part, part)
        theirs = pl.ds(pl.multiple_of((2 * z + 1 - core) * part, part), part)
        ours = pl.ds(pl.multiple_of((2 * z + core) * part, part), part)
        copies.append(links.start(src.at[:, theirs], dst.at[1, :, to], mate))
        stays.append(local.start(src.at[:, ours], dst.at[0, :, to]))
    return copies, stays


def swap_rows(links, local, src, dst, at, mate):
    copy = links.start(src.at[at], dst.at[1, at], mate)
    return copy, local.start(src.at[at], dst.at[0, at])


def glu_kernel(
    n_seq,
    two,
    cot_all,
    w_gate,
    w_up,
    w_down,
    two_half,
    cot_half,
    act_pair,
    gate_pair,
    up_pair,
    wv,
    wd,
    cot_ref,
    two_ref,
    d_act,
    stage,
    act,
    d_gate,
    d_up,
    send,
    recv,
    local_sems,
):
    rows = two.shape[0]
    units = w_gate.shape[1]
    s, f, fx, fy, fd = plane()
    core = s % 2
    mate = (s + 1 - 2 * core, f)
    links, local = Links(send, recv), Locals(local_sems)
    loads = [local.start(w_down, wd), local.start(cot_all, cot_ref)]
    two_ref[:rows] = two[...]
    enter([(s, fx), (s, fy), mate])
    own = gather_start(links, two_ref, two_ref, rows, s, fx, fy)
    wait_all(loads)
    loads = [
        local.start(w_gate, wv.at[:, pl.ds(0, units)]),
        local.start(w_up, wv.at[:, pl.ds(units, units)]),
    ]
    swaps, stays = swap_columns(links, local, cot_ref, cot_half, n_seq, core, mate)

    def act_tile(n, _):
        cols = tile(n, 256)
        d_act[:, cols] = mm_t(cot_ref[...], wd[cols])
        return 0

    lax.fori_loop(0, units // 256, act_tile, 0)
    if units % 256:
        rest = slice(units // 256 * 256, units)
        d_act[:, rest] = mm_t(cot_ref[...], wd[rest])
    later = gather_forward(links, own, two_ref, rows, s, fx, fy)
    wait_all(loads)

    def slots(first, number):
        nonlocal swaps, stays
        base = first * rows

        def tile_of(n, _):
            cols = tile(n, 256)
            stage[: number * rows, cols] = mm(two_ref[base : base + number * rows], wv[:, cols])
            return 0

        lax.fori_loop(0, 2 * units // 256, tile_of, 0)

        def rows_of(i, _):
            at = pl.ds(pl.multiple_of(i * 16, 16), 16)
            to = pl.ds(pl.multiple_of(base + i * 16, 16), 16)
            gate, up = stage[at, :units], stage[at, units:]
            sigma = jax.nn.sigmoid(gate)
            silu = gate * sigma
            act[to] = (silu * up).astype(BF16)
            d = d_act[to]
            d_gate[to] = (d * up * silu_slope(gate, sigma)).astype(BF16)
            d_up[to] = (d * silu).astype(BF16)
            return 0

        cuts = number * rows // 2
        for first_row in (0, cuts):
            lax.fori_loop(first_row // 16, (first_row + cuts) // 16, rows_of, 0)
            at = pl.ds(base + first_row, cuts)
            for src, dst in ((act, act_pair), (d_gate, gate_pair), (d_up, up_pair)):
                sent, stayed = swap_rows(links, local, src, dst, at, mate)
                swaps, stays = swaps + [sent], stays + [stayed]

    slots(0, 1)
    gather_middle(own)
    slots(1, 2)
    gather_far(later)
    more, keeps = swap_columns(links, local, two_ref, two_half, n_seq, core, mate)
    slots(3, 1)
    sends_done(own, later)
    wait_all(swaps, stays, more, keeps)


def glu(two, cot_all, w_gate, w_up, w_down, collective_id):
    n_seq = lax.axis_size("seq")
    rows, width = two.shape
    units = w_gate.shape[1]
    tokens = 4 * rows
    shape = jax.ShapeDtypeStruct
    half = shape((2, tokens, width // 2), BF16)
    pair = shape((2, tokens, units), BF16)
    remote_count = 6 + n_seq + 18
    return pl.pallas_call(
        functools.partial(glu_kernel, n_seq),
        out_shape=(half, half, pair, pair, pair),
        in_specs=[VMEM] + [ANY] * 4,
        out_specs=(ANY,) * 5,
        scratch_shapes=[
            pltpu.VMEM((width, 2 * units), BF16),
            pltpu.VMEM((units, width), BF16),
            pltpu.VMEM((tokens, width), BF16),
            pltpu.VMEM((tokens, width), BF16),
            pltpu.VMEM((tokens, units), F32),
            pltpu.VMEM((2 * rows, 2 * units), F32),
            pltpu.VMEM((tokens, units), BF16),
            pltpu.VMEM((tokens, units), BF16),
            pltpu.VMEM((tokens, units), BF16),
            pltpu.SemaphoreType.DMA((remote_count,)),
            pltpu.SemaphoreType.DMA((remote_count,)),
            pltpu.SemaphoreType.DMA((4 + n_seq + 18,)),
        ],
        compiler_params=params(collective_id),
        name="glu",
    )(two, cot_all, w_gate, w_up, w_down)


class ZLine:
    def __init__(self, part, buf, sems, n_seq, width, lag, ahead, store=None, leave=None):
        self.part, self.buf, self.width, self.lag, self.ahead = part, buf, width, lag, ahead
        self.send_up, self.recv_up, self.send_down, self.recv_down = sems[:4]
        self.store, self.leave = store, leave
        self.s, self.f = lax.axis_index("seq"), lax.axis_index("fsdp")
        self.n_seq, self.nz = n_seq, n_seq // 2
        self.z = self.s // 2
        self.block = part.shape[0] // self.nz
        self.chunks = part.shape[1] // width
        self.steps = (self.nz - 1) * self.chunks
        self.calls = self.steps + lag * (self.nz - 2)

    def rows(self, t):
        return pl.ds(pl.multiple_of(t * self.block, self.block), self.block)

    def move(self, up, k, j):
        t = self.nz - 1 - k if up else k
        landing = t + 1 if up else t
        cols = tile(j, self.width)
        slot = k * self.chunks + j
        peer = lax.rem(self.s + (2 if up else self.n_seq - 2), self.n_seq)
        send, recv = (
            (self.send_up, self.recv_up) if up else (self.send_down, self.recv_down)
        )
        return remote(
            self.part.at[self.rows(t), cols],
            self.buf.at[self.rows(landing), cols],
            send.at[slot],
            recv.at[slot],
            (peer, self.f),
        )

    def feed(self, q):
        inside = q < self.steps
        q = jnp.minimum(q, self.steps - 1)
        k = q // self.chunks
        j = q - k * self.chunks

        @pl.when(inside & (self.z == 0))
        def _():
            self.move(True, k, j).start()

        @pl.when(inside & (self.z == self.nz - 1))
        def _():
            self.move(False, k, j).start()

    def nth(self, i):
        return jnp.where(self.z < self.nz // 2, self.nz - 1 - i, i)

    def load(self, local, src, first, last):
        order = [self.rows(self.nth(i)) for i in range(first, last)]
        return [local.start(src.at[at], self.part.at[at]) for at in order]

    def feed_first(self):
        def step(q, _):
            self.feed(q)
            return 0

        lax.fori_loop(0, self.ahead, step, 0)

    def serve_one(self, up, q):
        z, nz = self.z, self.nz
        hops = z if up else nz - 1 - z
        q = q - self.lag * (hops - 1)
        inside = (hops >= 1) & (q >= 0) & (q < self.steps)
        q = jnp.clip(q, 0, self.steps - 1)
        k = q // self.chunks
        j = q - k * self.chunks
        left = nz - 1 - k - hops
        cols = tile(j, self.width)

        @pl.when(inside & (left >= 0))
        def _():
            self.move(up, k, j).wait_recv()

        @pl.when(inside & (left > 0))
        def _():
            t = nz - 1 - k if up else k
            landing = t + 1 if up else t
            own = self.part[self.rows(t), cols].astype(F32)
            came = self.buf[self.rows(landing), cols].astype(F32)
            self.part[self.rows(t), cols] = (own + came).astype(BF16)
            self.move(up, k, j).start()

    def serve(self, q, done=False):
        self.serve_one(True, q)
        self.serve_one(False, q)
        if done:
            j = q - (self.nz - 2) * self.chunks

            @pl.when((j >= 0) & (j < self.chunks))
            def _():
                self.finish(j)

    def serve_range(self, first, last, done=False):
        def step(q, _):
            self.feed(q + self.ahead)
            self.serve(q, done)
            return 0

        lax.fori_loop(first, last, step, 0)

    def finish(self, j):
        cols = tile(j, self.width)
        above = self.buf[self.rows(self.z), cols].astype(F32)
        below = self.buf[self.rows(self.z + 1), cols].astype(F32)
        own = self.part[self.rows(self.z), cols].astype(F32)
        own = own + jnp.where(self.z < self.nz - 1, above, 0.0)
        self.store(j, own + jnp.where(self.z > 0, below, 0.0))
        self.leave(j, True)

    def drain(self):
        for k in range(self.nz - 1):
            for up in (True, False):
                hops = self.z if up else self.nz - 1 - self.z

                @pl.when(hops < self.nz - 1 - k)
                def _():
                    def step(j, _):
                        self.move(up, k, j).wait_send()
                        return 0

                    lax.fori_loop(0, self.chunks, step, 0)

        def left(j, _):
            self.leave(j, False)
            return 0

        lax.fori_loop(0, self.chunks, left, 0)


def start_or_wait(copy, start):
    if start:
        copy.start()
    else:
        copy.wait()


def line_sems(n_seq, columns, width):
    count = (n_seq // 2 - 1) * (columns // width)
    leave = pltpu.SemaphoreType.DMA((columns // width,))
    return [pltpu.SemaphoreType.DMA((count,)) for _ in range(4)] + [leave]


def z_peers(n_seq):
    s = lax.axis_index("seq")
    f = lax.axis_index("fsdp")
    return [(lax.rem(s + 2 * k, n_seq), f) for k in range(1, n_seq // 2)]


def mm_tokens(left, right):
    return lax.dot_general(left, right, (((0,), (0,)), ((), ())), preferred_element_type=F32)


def down_kernel(
    n_seq,
    cot_half,
    act_pair,
    two_half,
    gate_pair,
    up_pair,
    w_gate,
    w_up,
    d_two_out,
    pair_part,
    down_out,
    d_two,
    cot_ref,
    act_ref,
    two_ref,
    gate_ref,
    up_ref,
    wg,
    wu,
    part,
    buf,
    rows_part,
    from_x,
    from_y,
    pass_x,
    pass_y,
    pair_ref,
    down_ref,
    send,
    recv,
    local_sems,
    *line,
):
    rows, width = d_two.shape
    units = act_pair.shape[1]
    s, f, fx, fy, fd = plane()
    links, local = Links(send, recv), Locals(local_sems)
    moves = (
        (cot_half, cot_ref),
        (act_pair, act_ref),
        (w_gate, wg),
        (w_up, wu),
        (gate_pair, gate_ref),
        (up_pair, up_ref),
        (two_half, two_ref),
    )
    loads = [local.start(src, dst) for src, dst in moves[:2]]
    enter([(s, fx), (s, fy)] + z_peers(n_seq))

    def store(j, value):
        down_ref[tile(j, 128)] = value.T

    def leave(j, start):
        at = tile(j, 128)
        copy = pltpu.make_async_copy(down_ref.at[at], down_out.at[at], line[4].at[j])
        start_or_wait(copy, start)

    z_sum = ZLine(part, buf, line, n_seq, 128, 3, 11, store, leave)
    block = z_sum.block
    wait_all(loads)
    loads = [local.start(src, dst) for src, dst in moves[2:]]

    def down_tile(i, _):
        t = z_sum.nth(i)
        part[z_sum.rows(t)] = mm_tokens(cot_ref[:, tile(t, block)], act_ref[...]).astype(BF16)
        return 0

    down_tile(jnp.int32(0), 0)
    z_sum.feed_first()
    lax.fori_loop(1, z_sum.nz, down_tile, 0)
    wait_all(loads)

    def two_part(first, slots, base):
        at = slice(first * rows, (first + slots) * rows)

        def tile_of(n, _):
            cols = tile(n, 512)
            total = mm_t(gate_ref[at], wg[cols]) + mm_t(up_ref[at], wu[cols])
            rows_part[at, cols] = total.astype(BF16)
            z_sum.feed(base + n + z_sum.ahead)
            z_sum.serve(base + n)
            return 0

        lax.fori_loop(0, width // 512, tile_of, 0)

    count = width // 512
    two_part(3, 1, 0)
    far = reduce_start_far(links, rows_part, from_x, from_y, rows, s, fx, fy)
    two_part(1, 2, count)
    near = reduce_start_near(links, rows_part, from_x, from_y, rows, s, fx, fy)
    two_part(0, 1, 2 * count)
    served = 3 * count

    def pair_tiles(right, first, base):
        def tile_of(t, _):
            pair_ref[z_sum.rows(t), pl.ds(first, units)] = mm_tokens(
                two_ref[:, tile(t, block)], right[...]
            ).astype(BF16)
            z_sum.serve_range(base + 2 * t, base + 2 * t + 2, True)
            return 0

        lax.fori_loop(0, z_sum.nz, tile_of, 0)

    pair_tiles(gate_ref, 0, served)
    served += 2 * z_sum.nz
    passed = reduce_pass(links, far, rows_part, from_x, from_y, pass_x, pass_y, rows, s, fx, fy)
    pair_tiles(up_ref, units, served)
    served += 2 * z_sum.nz
    stay = local.start(pair_ref, pair_part)
    for copy in near + passed:
        copy.wait_recv()
    half = rows // 2
    d_two[:half] = rows_part[:half].astype(F32) + from_x[1].astype(F32) + from_y[2].astype(F32)
    d_two[half:] = rows_part[half:rows].astype(F32) + from_y[1].astype(F32) + from_x[2].astype(F32)
    early = local.start(d_two, d_two_out)
    z_sum.serve_range(served, z_sum.calls, True)
    z_sum.drain()
    sends_done(far, near, passed)
    wait_all([stay, early])


def down_sum(cot_half, act_pair, two_half, gate_pair, up_pair, w_gate, w_up, collective_id):
    n_seq = lax.axis_size("seq")
    tokens, units = act_pair.shape
    width = w_gate.shape[0]
    rows = tokens // 8
    half = (rows // 2, width)
    own = cot_half.shape[1]
    block = width // n_seq
    shape = jax.ShapeDtypeStruct
    return pl.pallas_call(
        functools.partial(down_kernel, n_seq),
        out_shape=(
            shape((rows, width), F32),
            shape((own, 2 * units), BF16),
            shape((units, block), F32),
        ),
        in_specs=[ANY] * 7,
        out_specs=(ANY, ANY, ANY),
        scratch_shapes=[
            pltpu.VMEM((rows, width), F32),
            pltpu.VMEM((tokens, own), BF16),
            pltpu.VMEM((tokens, units), BF16),
            pltpu.VMEM((tokens, own), BF16),
            pltpu.VMEM((tokens, units), BF16),
            pltpu.VMEM((tokens, units), BF16),
            pltpu.VMEM((width, units), BF16),
            pltpu.VMEM((width, units), BF16),
            pltpu.VMEM((own, units), BF16),
            pltpu.VMEM((own + block, units), BF16),
            pltpu.VMEM((tokens // 2, width), BF16),
            pltpu.VMEM((3,) + half, BF16),
            pltpu.VMEM((3,) + half, BF16),
            pltpu.VMEM(half, BF16),
            pltpu.VMEM(half, BF16),
            pltpu.VMEM((own, 2 * units), BF16),
            pltpu.VMEM((units, block), F32),
            pltpu.SemaphoreType.DMA((6,)),
            pltpu.SemaphoreType.DMA((6,)),
            pltpu.SemaphoreType.DMA((9,)),
        ]
        + line_sems(n_seq, units, 128),
        compiler_params=params(collective_id),
        name="down_sum",
    )(cot_half, act_pair, two_half, gate_pair, up_pair, w_gate, w_up)


def pair_kernel(
    n_seq,
    lengths,
    hidden,
    cot,
    glu_gain,
    gate_gain,
    table,
    scale_g,
    d_two,
    middle,
    pair_part,
    w_out,
    w_in,
    w_fg,
    w_gt,
    gate_raw,
    state_b,
    out_raw,
    in_raw,
    fg_raw,
    before_in,
    normed_half,
    pair_grad,
    mixer_part,
    d_normed_out,
    d_middle_out,
    d_glu_gain,
    d_gain,
    d_bounds,
    d_normed,
    d_middle,
    pair_ref,
    part,
    buf,
    wo,
    wv,
    mixed_all,
    mixed_mate,
    normed_ref,
    d_proj,
    out_gate,
    gate_ref,
    state_ref,
    raw_ref,
    in_ref,
    fg_ref,
    before,
    p_ref,
    q_ref,
    stage,
    rows_part,
    from_x,
    from_y,
    pass_x,
    pass_y,
    dots,
    keep_ref,
    end_p,
    end_s,
    carr,
    total,
    gathered,
    send,
    recv,
    exchange_send,
    exchange_recv,
    local_sems,
    tile_sems,
    *line,
):
    rows, width = hidden.shape
    chans = w_in.shape[1]
    tokens = 4 * rows
    lanes_of = [slice(c, c + 128) for c in range(0, chans, 128)]
    count = len(lanes_of)
    blocks = 4 * count
    step_len = rows // 8
    s, f, fx, fy, fd = plane()
    groups = [f, fx, fy, fd]
    core = s % 2
    mate = (s + 1 - 2 * core, f)
    links, local = Links(send, recv), Locals(local_sems)

    def store(j, value):
        pair_ref[:, tile(j, 256)] = value

    def leave(j, start):
        at = tile(j, 256)
        copy = pltpu.make_async_copy(pair_ref.at[:, at], pair_grad.at[:, at], line[4].at[j])
        start_or_wait(copy, start)

    z_sum = ZLine(part, buf, line, n_seq, 256, 2, 7, store, leave)
    blocks_in = z_sum.load(local, pair_part, 0, 1)
    rows_in = [local.start(d_two, d_middle), local.start(middle, d_normed)]
    enter([(s, fx), (s, fy), (s, fd)] + seq_peers(n_seq))
    blocks_in[0].wait()
    z_sum.feed_first()
    blocks_in = z_sum.load(local, pair_part, 1, z_sum.nz)
    loads = [local.start(w_out, wo)]
    loads += [
        local.start(src, dst)
        for src, dst in (
            (gate_raw, gate_ref),
            (state_b, state_ref),
            (out_raw, raw_ref),
            (in_raw, in_ref),
            (fg_raw, fg_ref),
            (before_in, before),
        )
    ]
    weights = [
        local.start(w, wv.at[:, pl.ds(i * chans, chans)]) for i, w in enumerate((w_in, w_fg, w_gt))
    ]
    weights.append(local.start(normed_half, normed_ref))
    served = 0

    def serve(number):
        nonlocal served
        z_sum.serve_range(served, served + number)
        served += number

    d_glu_gain[...] = jnp.zeros_like(d_glu_gain)
    wait_all(rows_in, blocks_in)

    def middle_rows(i, _):
        at = pl.ds(pl.multiple_of(i * 16, 16), 16)
        value, came = d_normed[at], d_middle[at]
        scale = lax.rsqrt(jnp.mean(value * value, -1, keepdims=True) + epsilon)
        scaled = glu_gain[...] * came
        mean = jnp.mean(scaled * value, -1, keepdims=True)
        grad = cot[at].astype(F32) + scale * scaled - value * (scale**3 * mean)
        d_middle[at] = grad
        grad_b = grad.astype(BF16)
        mixed_all[at] = grad_b
        own_dot = jnp.sum(
            grad_b.astype(F32) * (value - hidden[at].astype(F32)), -1, keepdims=True
        )
        dots[0, at] = jnp.broadcast_to(own_dot, (16, 128))
        d_glu_gain[...] += jnp.sum(came * value * scale, 0, keepdims=True)
        return 0

    lax.fori_loop(0, rows // 16, middle_rows, 0)
    outs = [local.start(d_middle, d_middle_out)]
    own = gather_start(links, mixed_all, mixed_all, rows, s, fx, fy)
    dot_copies = [
        links.start(dots.at[0], dots.at[k], (s, peer)) for k, peer in ((1, fx), (2, fy), (3, fd))
    ]
    bound = bounds_slice(table, f * chans, chans)
    for k in range(4):
        keep_ref[k] = keep_rows(lengths, groups[k], s * rows, rows)
    d_gain[...] = jnp.zeros_like(d_gain)
    serve(1)
    for copy in loads:
        copy.wait()

    def out_rows(first, slots):
        stage[: slots * rows] = mm_t(mixed_all[first * rows : (first + slots) * rows], wo[...])
        for i in range(slots):
            k = first + i
            scale = scale_g[k]
            for c, lanes in enumerate(lanes_of):
                n = k * count + c
                gain = gate_gain[:, pl.ds(pl.multiple_of(f * chans + c * 128, 128), 128)]
                d_out = stage[i * rows : (i + 1) * rows, lanes]
                gate = gate_ref[k, :, lanes]
                sigma = jax.nn.sigmoid(gate)
                silu = gate * sigma
                state = state_ref[k, :, lanes].astype(F32)
                weighed = d_out * (state * scale)
                d_gain[:, lanes] += jnp.sum(weighed * silu, 0, keepdims=True)
                at = slice(k * rows, (k + 1) * rows)
                d_proj[at, 2 * chans + c * 128 : 2 * chans + (c + 1) * 128] = (
                    weighed * gain * silu_slope(gate, sigma)
                ).astype(BF16)
                out_gate[at, lanes] = (raw_ref[at, lanes].astype(F32) * scale).astype(BF16)
                d_state = scale * (d_out * gain * silu) - state * (
                    scale * scale * (dots[k] / width)
                )
                q_ref[n] = d_state.astype(BF16).astype(F32)
                edge = bound[:, lanes]
                forget = edge + (1.0 - edge) * jax.nn.sigmoid(fg_ref[k, :, lanes].astype(F32))
                p_ref[n] = forget * keep_ref[k]

    out_rows(0, 1)
    later = gather_forward(links, own, mixed_all, rows, s, fx, fy)
    serve(2)
    gather_middle(own)
    for copy in dot_copies:
        copy.wait_recv()
    out_rows(1, 2)
    serve(3)
    gather_far(later)
    out_rows(3, 1)
    serve(2)
    own_rows, mate_rows = pl.ds(0, tokens), pl.ds(tokens, tokens)
    last = pl.ds(2 * chans, chans)
    swaps = [
        links.start(out_gate.at[own_rows], out_gate.at[mate_rows], mate),
        links.start(d_proj.at[own_rows, last], d_proj.at[mate_rows, last], mate),
    ]
    wide = z_sum.block
    for t in range(n_seq // 2):
        theirs = pl.ds(pl.multiple_of((2 * t + 1 - core) * wide, wide), wide)
        swaps.append(
            links.start(mixed_all.at[:, theirs], mixed_mate.at[:, pl.ds(t * wide, wide)], mate)
        )

    def scan_step(i, carry):
        new = []
        at = pl.ds(step_len - 1 - i, 8, stride=step_len)
        for n, (product, message) in enumerate(carry):
            a = p_ref[n, at, :]
            acc = q_ref[n, at, :] + message
            p_ref[n, at, :] = product
            q_ref[n, at, :] = acc
            new.append((product * a, a * acc))
        return tuple(new)

    start = tuple((jnp.ones((8, 128), F32), jnp.zeros((8, 128), F32)) for _ in range(blocks))
    ends = lax.fori_loop(0, step_len, scan_step, start)
    for n, (product, message) in enumerate(ends):
        end_p[8 * n : 8 * n + 8] = product
        end_s[8 * n : 8 * n + 8] = message
    p_all, s_all = segment_totals(end_p, end_s, blocks, range(7, -1, -1))
    total[:blocks] = p_all
    total[blocks:] = s_all
    copies = start_exchange(total, gathered, exchange_send, exchange_recv, n_seq)
    serve(2)
    wait_all(copies)
    carry = jnp.zeros((blocks, 128), F32)
    for j in range(n_seq - 1, 0, -1):
        carry = jnp.where(j > s, gathered[j, blocks:] + gathered[j, :blocks] * carry, carry)
    spread_carry(carry, carr, end_p, end_s, blocks, range(7, -1, -1))

    def finish(n, _):
        enter_state = carr[pl.ds(pl.multiple_of(n * 8, 8), 8)]
        for i in range(step_len):
            at = pl.ds(i, 8, stride=step_len)
            q_ref[n, at, :] = q_ref[n, at, :] + p_ref[n, at, :] * enter_state
        return 0

    lax.fori_loop(0, blocks, finish, 0)
    d_bounds[...] = jnp.zeros_like(d_bounds)
    for k in range(4):
        at = slice(k * rows, (k + 1) * rows)
        for c, lanes in enumerate(lanes_of):
            acc = q_ref[k * count + c]
            edge = bound[:, lanes]
            sigma_f = jax.nn.sigmoid(fg_ref[k, :, lanes].astype(F32))
            forget = edge + (1.0 - edge) * sigma_f
            value = in_ref[k, :, lanes].astype(F32)
            sigma_i = jax.nn.sigmoid(value)
            d_forget = acc * (before[k * count + c] * keep_ref[k] - value * sigma_i)
            d_proj[at, lanes] = (acc * (1.0 - forget) * silu_slope(value, sigma_i)).astype(BF16)
            d_sigma = d_forget * (1.0 - sigma_f)
            d_proj[at, chans + c * 128 : chans + (c + 1) * 128] = (
                d_sigma * (1.0 - edge) * sigma_f
            ).astype(BF16)
            d_bounds[:, lanes] += jnp.sum(d_sigma, 0, keepdims=True)
    first = pl.ds(0, 2 * chans)
    swaps.append(links.start(d_proj.at[own_rows, first], d_proj.at[mate_rows, first], mate))
    serve(2)
    for copy in weights:
        copy.wait()

    def normed_part(first_slot, slots):
        at = slice(first_slot * rows, (first_slot + slots) * rows)

        def tile_of(n, _):
            cols = tile(n, 512)
            rows_part[at, cols] = mm_t(d_proj[at], wv[cols]).astype(BF16)
            return 0

        lax.fori_loop(0, width // 512, tile_of, 0)

    normed_part(3, 1)
    far = reduce_start_far(links, rows_part, from_x, from_y, rows, s, fx, fy)
    normed_part(1, 2)
    near = reduce_start_near(links, rows_part, from_x, from_y, rows, s, fx, fy)
    normed_part(0, 1)
    serve(3)
    for copy in swaps:
        copy.wait_recv()

    def tile_out(t):
        slot = lax.rem(t, 2)
        return pltpu.make_async_copy(
            wo.at[tile(slot, wide)], mixer_part.at[z_sum.rows(t)], tile_sems.at[slot]
        )

    def mixer_tile(t, _):
        @pl.when(t >= 2)
        def _():
            tile_out(t - 2).wait()

        at = tile(lax.rem(t, 2), wide)
        ours = mixed_all[:, tile(2 * t + core, wide)]
        out_part = mm_tokens(ours, out_gate[:tokens])
        out_part = out_part + mm_tokens(mixed_mate[:, tile(t, wide)], out_gate[tokens:])
        wo[at, :chans] = out_part.astype(BF16)
        wo[at, chans:] = mm_tokens(normed_ref[:, tile(t, wide)], d_proj[...]).astype(BF16)
        tile_out(t).start()
        return 0

    lax.fori_loop(0, 1, mixer_tile, 0)
    passed = reduce_pass(links, far, rows_part, from_x, from_y, pass_x, pass_y, rows, s, fx, fy)
    serve(1)
    lax.fori_loop(1, z_sum.nz, mixer_tile, 0)
    serve(2)
    for copy in near + passed:
        copy.wait_recv()
    half = rows // 2
    d_normed[:half] = rows_part[:half].astype(F32) + from_x[1].astype(F32) + from_y[2].astype(F32)
    d_normed[half:] = (
        rows_part[half:rows].astype(F32) + from_y[1].astype(F32) + from_x[2].astype(F32)
    )
    outs.append(local.start(d_normed, d_normed_out))
    z_sum.serve_range(served, z_sum.calls, True)
    z_sum.drain()
    sends_done(own, later, dot_copies, swaps, far, near, passed)
    for t in range(z_sum.nz - 2, z_sum.nz):
        tile_out(jnp.int32(t)).wait()
    wait_all(outs)


def pair_sum(
    lengths, own_rows, gains, table, scale_g, float_rows, pair_part, weights, saved, normed_half, cid
):
    n_seq = lax.axis_size("seq")
    rows, width = own_rows[0].shape
    chans = weights[1].shape[1]
    own, columns = pair_part.shape
    tokens = 4 * rows
    blocks = 4 * chans // 128
    block = width // n_seq
    half = (rows // 2, width)
    shape = jax.ShapeDtypeStruct
    exchange = pltpu.SemaphoreType.DMA((n_seq,))
    count = 18 + n_seq // 2
    return pl.pallas_call(
        functools.partial(pair_kernel, n_seq),
        out_shape=(
            shape((block, columns), F32),
            shape((own, 4 * chans), BF16),
            shape((rows, width), F32),
            shape((rows, width), F32),
            shape((1, width), F32),
            shape((1, chans), F32),
            shape((1, chans), F32),
        ),
        in_specs=[pl.BlockSpec(memory_space=pltpu.SMEM)] + [VMEM] * 6 + [ANY] * 14,
        out_specs=(ANY,) * 4 + (VMEM,) * 3,
        scratch_shapes=[
            pltpu.VMEM((rows, width), F32),
            pltpu.VMEM((rows, width), F32),
            pltpu.VMEM((block, columns), F32),
            pltpu.VMEM((own, columns), BF16),
            pltpu.VMEM((own + block, columns), BF16),
            pltpu.VMEM((chans, width), BF16),
            pltpu.VMEM((width, 3 * chans), BF16),
            pltpu.VMEM((tokens, width), BF16),
            pltpu.VMEM((tokens, width // 2), BF16),
            pltpu.VMEM((2 * tokens, width // 2), BF16),
            pltpu.VMEM((2 * tokens, 3 * chans), BF16),
            pltpu.VMEM((2 * tokens, chans), BF16),
            pltpu.VMEM((4, rows, chans), F32),
            pltpu.VMEM((4, rows, chans), BF16),
            pltpu.VMEM((tokens, chans), BF16),
            pltpu.VMEM((4, rows, chans), BF16),
            pltpu.VMEM((4, rows, chans), BF16),
            pltpu.VMEM((blocks, rows, 128), F32),
            pltpu.VMEM((blocks, rows, 128), F32),
            pltpu.VMEM((blocks, rows, 128), F32),
            pltpu.VMEM((2 * rows, chans), F32),
            pltpu.VMEM((tokens, width), BF16),
            pltpu.VMEM((3,) + half, BF16),
            pltpu.VMEM((3,) + half, BF16),
            pltpu.VMEM(half, BF16),
            pltpu.VMEM(half, BF16),
            pltpu.VMEM((4, rows, 128), F32),
            pltpu.VMEM((4, rows, 128), F32),
            pltpu.VMEM((8 * blocks, 128), F32),
            pltpu.VMEM((8 * blocks, 128), F32),
            pltpu.VMEM((8 * blocks, 128), F32),
            pltpu.VMEM((2 * blocks, 128), F32),
            pltpu.VMEM((n_seq, 2 * blocks, 128), F32),
            pltpu.SemaphoreType.DMA((count,)),
            pltpu.SemaphoreType.DMA((count,)),
            exchange,
            exchange,
            pltpu.SemaphoreType.DMA((15 + n_seq // 2,)),
            pltpu.SemaphoreType.DMA((2,)),
        ]
        + line_sems(n_seq, columns, 256),
        compiler_params=params(cid),
        name="pair_sum",
    )(
        lengths,
        *own_rows,
        *gains,
        table,
        scale_g,
        *float_rows,
        pair_part,
        *weights,
        *saved,
        normed_half,
    )


def final_kernel(
    n_seq,
    n_fsdp,
    hidden,
    norm_gain,
    d_glu_gain,
    d_gain,
    d_bounds,
    table,
    d_normed_in,
    d_middle_in,
    middle_in,
    mixer_part,
    act_pair,
    w_down,
    output_out,
    d_hidden_out,
    out_grad,
    rest_grad,
    sums,
    d_table,
    d_normed,
    d_middle,
    middle,
    output,
    d_hidden,
    out_ref,
    rest_ref,
    part,
    buf,
    act,
    wd,
    rows_part,
    from_x,
    from_y,
    pass_x,
    pass_y,
    norm_sum,
    terms,
    quarters_in,
    terms_q,
    over_seq,
    along_sum,
    over_fsdp,
    send,
    recv,
    local_sems,
    *line,
):
    rows, width = hidden.shape
    chans = d_gain.shape[1]
    tokens = 4 * rows
    s, f, fx, fy, fd = plane()
    links, local = Links(send, recv), Locals(local_sems)
    head = chans // 256

    def store(j, value):
        @pl.when(j < head)
        def _():
            out_ref[tile(j, 256)] = value.T

        @pl.when(j >= head)
        def _():
            rest_ref[:, tile(j - head, 256)] = value

    def leave(j, start):
        @pl.when(j < head)
        def _():
            at = tile(j, 256)
            copy = pltpu.make_async_copy(out_ref.at[at], out_grad.at[at], line[4].at[j])
            start_or_wait(copy, start)

        @pl.when(j >= head)
        def _():
            at = tile(j - head, 256)
            copy = pltpu.make_async_copy(rest_ref.at[:, at], rest_grad.at[:, at], line[4].at[j])
            start_or_wait(copy, start)

    z_sum = ZLine(part, buf, line, n_seq, 256, 2, 6, store, leave)
    blocks_in = z_sum.load(local, mixer_part, 0, 1)
    along = seq_peers(n_seq)
    across = [(s, fx), (s, fy), (s, fd)]
    enter(across + along)
    blocks_in[0].wait()
    z_sum.feed_first()
    loads = [local.start(act_pair.at[pl.ds(0, tokens)], act), local.start(w_down, wd)]
    blocks_in = z_sum.load(local, mixer_part, 1, z_sum.nz)
    rows_in = [
        local.start(src, dst)
        for src, dst in ((d_normed_in, d_normed), (d_middle_in, d_middle), (middle_in, middle))
    ]
    served = 0

    def serve(number):
        nonlocal served
        z_sum.serve_range(served, served + number)
        served += number

    norm_sum[...] = jnp.zeros_like(norm_sum)

    def hidden_rows(i, _):
        at = pl.ds(pl.multiple_of(i * 16, 16), 16)
        value, came = hidden[at].astype(F32), d_normed[at]
        scale = lax.rsqrt(jnp.mean(value * value, -1, keepdims=True) + epsilon)
        scaled = norm_gain[...] * came
        mean = jnp.mean(scaled * value, -1, keepdims=True)
        d_hidden[at] = (d_middle[at] + scale * scaled - value * (scale**3 * mean)).astype(BF16)
        norm_sum[...] += jnp.sum(came * value * scale, 0, keepdims=True)
        return 0

    wait_all(loads)

    def glu_part(first, slots):
        at = slice(first * rows, (first + slots) * rows)

        def tile_of(n, _):
            cols = tile(n, 512)
            rows_part[at, cols] = mm(act[at], wd[:, cols]).astype(BF16)
            return 0

        lax.fori_loop(0, width // 512, tile_of, 0)

    glu_part(3, 1)
    far = reduce_start_far(links, rows_part, from_x, from_y, rows, s, fx, fy)
    glu_part(1, 2)
    near = reduce_start_near(links, rows_part, from_x, from_y, rows, s, fx, fy)
    glu_part(0, 1)
    wait_all(blocks_in, rows_in)
    serve(2)
    lax.fori_loop(0, rows // 16, hidden_rows, 0)
    terms[...] = jnp.zeros_like(terms)
    for q in range(4):
        terms[q, 0:1] = norm_sum[:, q * chans : (q + 1) * chans]
        terms[q, 1:2] = d_glu_gain[:, q * chans : (q + 1) * chans]
    quarter_copies = [
        links.start(terms.at[peer], quarters_in.at[k], (s, peer))
        for k, peer in enumerate((fx, fy, fd))
    ]
    serve(1)
    passed = reduce_pass(links, far, rows_part, from_x, from_y, pass_x, pass_y, rows, s, fx, fy)
    serve(2)
    quarter = terms[pl.ds(f, 1)][0]
    for k, copy in enumerate(quarter_copies):
        copy.wait_recv()
        quarter = quarter + quarters_in[k]
    half = chans // 2
    for first, cols in ((0, slice(0, half)), (4, slice(half, chans))):
        terms_q[first : first + 2] = quarter[:2, cols]
        terms_q[first + 2 : first + 3] = d_gain[:, cols]
        terms_q[first + 3 : first + 4] = d_bounds[:, cols]
    seq_copies = [links.start(terms_q, over_seq.at[k], peer) for k, peer in enumerate(along)]
    serve(1)
    serve(2)
    for copy in near + passed:
        copy.wait_recv()
    middle_half = rows // 2
    for first, one, other in (
        (0, from_x.at[1], from_y.at[2]),
        (middle_half, from_y.at[1], from_x.at[2]),
    ):
        at = slice(first, first + middle_half)
        added = rows_part[at].astype(F32) + one[...].astype(F32) + other[...].astype(F32)
        output[at] = (middle[at] + added).astype(BF16)
    total = terms_q[...]
    for k, copy in enumerate(seq_copies):
        copy.wait_recv()
        total = total + over_seq[k]
    along_sum[...] = total
    fsdp_copies = [links.start(along_sum, over_fsdp.at[k], peer) for k, peer in enumerate(across)]
    serve(2)
    for copy in fsdp_copies:
        copy.wait_recv()
    for k, group in enumerate((f, fx, fy, fd)):
        total = along_sum[...] if k == 0 else over_fsdp[k - 1]
        for i in range(2):
            at = pl.ds(pl.multiple_of(group * chans + i * half, 128), half)
            sums[:, at] = total[4 * i : 4 * i + 4]
    powers = jnp.exp(table[...] - jnp.max(table[...], 0, keepdims=True))
    soft = powers / jnp.sum(powers, 0, keepdims=True)
    row = lax.broadcasted_iota(jnp.int32, soft.shape, 0)
    chosen = jnp.where((row >= 1) & (row <= LAYER), 1.0, 0.0)
    bound = jnp.sum(soft * chosen, 0, keepdims=True)
    d_table[...] = soft * (chosen - bound) * sums[3:4]
    outs = [local.start(output, output_out), local.start(d_hidden, d_hidden_out)]
    z_sum.serve_range(served, z_sum.calls, True)
    z_sum.drain()
    wait_all(outs)
    sends_done(far, near, passed, quarter_copies, seq_copies, fsdp_copies)


def final_sum(hidden, rows_in, gains, table, mixer_part, act_pair, w_down, cid):
    n_seq, n_fsdp = lax.axis_size("seq"), lax.axis_size("fsdp")
    rows, width = hidden.shape
    own, columns = mixer_part.shape
    units = w_down.shape[0]
    chans = columns // 4
    tokens = 4 * rows
    block = width // n_seq
    half = (rows // 2, width)
    terms = (8, chans // 2)
    shape = jax.ShapeDtypeStruct
    count = 6 + n_seq - 1 + 2 * (n_fsdp - 1)
    return pl.pallas_call(
        functools.partial(final_kernel, n_seq, n_fsdp),
        out_shape=(
            shape((rows, width), BF16),
            shape((rows, width), BF16),
            shape((chans, block), F32),
            shape((block, 3 * chans), F32),
            shape((4, width), F32),
            shape(table.shape, F32),
        ),
        in_specs=[VMEM] * 6 + [ANY] * 6,
        out_specs=(ANY,) * 4 + (VMEM,) * 2,
        scratch_shapes=[
            pltpu.VMEM((rows, width), F32),
            pltpu.VMEM((rows, width), F32),
            pltpu.VMEM((rows, width), F32),
            pltpu.VMEM((rows, width), BF16),
            pltpu.VMEM((rows, width), BF16),
            pltpu.VMEM((chans, block), F32),
            pltpu.VMEM((block, 3 * chans), F32),
            pltpu.VMEM((own, columns), BF16),
            pltpu.VMEM((own + block, columns), BF16),
            pltpu.VMEM((tokens, units), BF16),
            pltpu.VMEM((units, width), BF16),
            pltpu.VMEM((tokens, width), BF16),
            pltpu.VMEM((3,) + half, BF16),
            pltpu.VMEM((3,) + half, BF16),
            pltpu.VMEM(half, BF16),
            pltpu.VMEM(half, BF16),
            pltpu.VMEM((1, width), F32),
            pltpu.VMEM((n_fsdp, 8, chans), F32),
            pltpu.VMEM((n_fsdp - 1, 8, chans), F32),
            pltpu.VMEM(terms, F32),
            pltpu.VMEM((n_seq - 1,) + terms, F32),
            pltpu.VMEM(terms, F32),
            pltpu.VMEM((n_fsdp - 1,) + terms, F32),
            pltpu.SemaphoreType.DMA((count,)),
            pltpu.SemaphoreType.DMA((count,)),
            pltpu.SemaphoreType.DMA((7 + n_seq // 2,)),
        ]
        + line_sems(n_seq, columns, 256),
        compiler_params=params(cid),
        name="final_sum",
    )(hidden, *gains, table, *rows_in, mixer_part, act_pair, w_down)


def hand_over_kernel(count, pieces, *refs):
    sources, targets = refs[: len(refs) - 2 * count - 2], refs[len(refs) - 2 * count - 2 :]
    kept, arrived, left = targets[count : 2 * count], targets[2 * count], targets[2 * count + 1]
    loads, stores = [], []
    for n, (i, source, first, rows, column) in enumerate(pieces):
        at = pl.ds(first, rows)
        src = sources[source].at[at, pl.ds(column, kept[i].shape[1])]
        loads.append(copy_in(src, kept[i].at[at], arrived.at[n]))
    for n, (i, source, first, rows, column) in enumerate(pieces):
        at = pl.ds(first, rows)
        loads[n].wait()
        stores.append(copy_in(kept[i].at[at], targets[i].at[at], left.at[n]))
    for store in stores:
        store.wait()


def hand_over(arrays, wanted):
    pieces, shapes = [], []
    for i, (source, column, columns) in enumerate(wanted):
        x = arrays[source]
        height = x.shape[0]
        parts = max(1, height * columns * x.dtype.itemsize >> 18)
        parts = parts if height % (parts * 16) == 0 else 1
        rows = height // parts
        pieces += [(i, source, n * rows, rows, column) for n in range(parts)]
        shapes.append(((height, columns), x.dtype))
    return pl.pallas_call(
        functools.partial(hand_over_kernel, len(wanted), tuple(pieces)),
        out_shape=tuple(jax.ShapeDtypeStruct(*x) for x in shapes),
        in_specs=[ANY] * len(arrays),
        out_specs=(ANY,) * len(wanted),
        scratch_shapes=[pltpu.VMEM(*x) for x in shapes]
        + [pltpu.SemaphoreType.DMA((len(pieces),))] * 2,
        compiler_params=pltpu.CompilerParams(vmem_limit_bytes=56 << 20),
        name="hand_over",
    )(*arrays)


def plane_device(
    hidden,
    lengths,
    w_input,
    w_forget,
    w_gate_out,
    w_output,
    norm_gain,
    gate_gain,
    glu_gain,
    lower_table,
    w_glu_gate,
    w_glu_up,
    w_glu_down,
    cotangent,
):
    hidden, cotangent = hidden[0], cotangent[0]
    tokens = 4 * hidden.shape[0]
    gains = (norm_gain[None], gate_gain[None], glu_gain[None])
    (
        normed_half,
        cot_all,
        in_raw,
        fg_raw,
        gate_raw,
        state_b,
        out_raw,
        before,
        scale_g,
        middle,
        normed_two,
    ) = mixer_forward(
        lengths,
        hidden,
        cotangent,
        gains,
        lower_table,
        (w_input, w_forget, w_gate_out, w_output),
        0,
    )
    two_half, cot_half, act_pair, gate_pair, up_pair = glu(
        normed_two, cot_all, w_glu_gate, w_glu_up, w_glu_down, 1
    )
    d_normed_two, pair_part, down_grad = down_sum(
        *(x.reshape(2 * tokens, -1) for x in (cot_half, act_pair, two_half, gate_pair, up_pair)),
        w_glu_gate,
        w_glu_up,
        2,
    )
    pair_grad, mixer_part, d_normed, d_middle, d_glu_gain, d_gain, d_bounds = pair_sum(
        lengths,
        (hidden, cotangent),
        (gains[2], gains[1]),
        lower_table,
        scale_g,
        (d_normed_two, middle),
        pair_part,
        (w_output, w_input, w_forget, w_gate_out),
        (gate_raw, state_b, out_raw, in_raw, fg_raw, before),
        normed_half.reshape(2 * tokens, -1),
        3,
    )
    output, d_hidden, out_grad, rest_grad, sums, d_table = final_sum(
        hidden,
        (d_normed, d_middle, middle),
        (gains[0], d_glu_gain, d_gain, d_bounds),
        lower_table,
        mixer_part,
        act_pair.reshape(2 * tokens, -1),
        w_glu_down,
        4,
    )
    width, chans, units = hidden.shape[1], w_input.shape[1], w_glu_gate.shape[1]
    block = down_grad.shape[1]
    (
        down_grad,
        gate_grad,
        up_grad,
        output,
        d_hidden,
        d_table,
        out_grad,
        in_grad,
        fg_grad,
        gt_grad,
    ) = hand_over(
        (down_grad, pair_grad, output, d_hidden, d_table, out_grad, rest_grad),
        (
            (0, 0, block),
            (1, 0, units),
            (1, units, units),
            (2, 0, width),
            (3, 0, width),
            (4, 0, width),
            (5, 0, block),
            (6, 0, chans),
            (6, chans, chans),
            (6, 2 * chans, chans),
        ),
    )
    return (
        output[None],
        d_hidden[None],
        in_grad,
        fg_grad,
        gt_grad,
        out_grad,
        sums[0],
        sums[2],
        sums[1],
        d_table,
        gate_grad,
        up_grad,
        down_grad,
    )


def fits_plane(mesh):
    return mesh.shape["fsdp"] == 4 and mesh.shape["seq"] % 2 == 0


def solution(mesh):
    rows_spec = P("fsdp", "seq", None)
    columns = P(None, "fsdp")
    placed = (
        rows_spec,
        P(),
        columns,
        columns,
        columns,
        P("fsdp", None),
        P(),
        P(),
        P(),
        P(),
        columns,
        columns,
        P("fsdp", None),
        rows_spec,
    )
    by_rows, by_columns = P("seq", "fsdp"), P("fsdp", "seq")
    return jax.shard_map(
        plane_device if fits_plane(mesh) else per_device,
        mesh=mesh,
        in_specs=placed,
        out_specs=(
            rows_spec,
            rows_spec,
            by_rows,
            by_rows,
            by_rows,
            by_columns,
            P(),
            P(),
            P(),
            P(),
            by_rows,
            by_rows,
            by_columns,
        ),
        check_vma=False,
    )
```

```python
import functools

import jax
import jax.numpy as jnp
from jax import lax
from jax.experimental import pallas as pl
from jax.experimental.pallas import tpu as pltpu
from jax.sharding import PartitionSpec as P

LAYER = 12
MESH = pl.DeviceIdType.MESH
F32 = jnp.float32
BF16 = jnp.bfloat16

epsilon = 1e-06

VMEM = pl.BlockSpec(memory_space=pltpu.VMEM)
ANY = pl.BlockSpec(memory_space=pl.ANY)


def lower_bound(table):
    soft = jax.nn.softmax(table, axis=0)
    totals = jnp.cumsum(soft, axis=0)
    return totals[LAYER] - totals[0]


def silu_slope(value, sigma):
    return sigma * (1.0 + value * (1.0 - sigma))


def params(collective_id):
    return pltpu.CompilerParams(
        collective_id=collective_id, has_side_effects=True, vmem_limit_bytes=56 << 20
    )


def round_up(value, unit):
    return -(-value // unit) * unit


def plane():
    s = lax.axis_index("seq")
    f = lax.axis_index("fsdp")
    y, x = f // 2, f % 2
    fx = y * 2 + (1 - x)
    fy = (1 - y) * 2 + x
    fd = (1 - y) * 2 + (1 - x)
    return s, f, fx, fy, fd


def enter(devices):
    barrier = pltpu.get_barrier_semaphore()
    for device in devices:
        pl.semaphore_signal(barrier, inc=1, device_id=device, device_id_type=MESH)
    pl.semaphore_wait(barrier, len(devices))


def remote(src, dst, send, recv, device):
    return pltpu.make_async_remote_copy(
        src_ref=src,
        dst_ref=dst,
        send_sem=send,
        recv_sem=recv,
        device_id=device,
        device_id_type=MESH,
    )


def gather(x, small, collective_id):
    return lax.all_gather(x, "fsdp"), lax.all_gather(small, "fsdp")


def reduce_rows(p, small, collective_id):
    total = lax.psum_scatter(p, "fsdp", scatter_dimension=0, tiled=True)[0]
    return total.astype(F32), lax.psum(small, "fsdp")


def start_exchange(total, gathered, send, recv, n_seq):
    s = lax.axis_index("seq")
    f = lax.axis_index("fsdp")
    copies = []
    for k in range(1, n_seq):
        peer = lax.rem(s + k, n_seq)
        copy = remote(total, gathered.at[s], send.at[k], recv.at[k], (peer, f))
        copy.start()
        copies.append(copy)
    gathered[pl.ds(s, 1)] = total[...][None]
    return copies


def seq_peers(n_seq):
    s = lax.axis_index("seq")
    f = lax.axis_index("fsdp")
    return [(lax.rem(s + k, n_seq), f) for k in range(1, n_seq)]


def lane_blocks(groups, chans):
    return [(g, slice(c, c + 128)) for g in range(groups) for c in range(0, chans, 128)]


def forward_scan_kernel(
    n_seq, in_raw, forget_raw, bounds, keep, state_b, before, a_ref, b_ref, total, gathered, send, recv
):
    groups, rows, chans = in_raw.shape
    part = rows // 8
    blocks = lane_blocks(groups, chans)
    s = lax.axis_index("seq")
    barrier = pltpu.get_barrier_semaphore()
    for peer in seq_peers(n_seq):
        pl.semaphore_signal(barrier, inc=1, device_id=peer, device_id_type=MESH)
    for n, (g, lanes) in enumerate(blocks):
        bound = bounds[:, lanes]
        forget = bound + (1.0 - bound) * jax.nn.sigmoid(forget_raw[g, :, lanes].astype(F32))
        value = in_raw[g, :, lanes].astype(F32)
        a_ref[n] = forget * keep[g]
        b_ref[n] = value * jax.nn.sigmoid(value) * (1.0 - forget)

    def step(i, carry):
        new = []
        at = pl.ds(i, 8, stride=part)
        for n, (product, state) in enumerate(carry):
            a = a_ref[n, at, :]
            state = a * state + b_ref[n, at, :]
            product = product * a
            a_ref[n, at, :] = product
            b_ref[n, at, :] = state
            new.append((product, state))
        return tuple(new)

    start = tuple((jnp.ones((8, 128), F32), jnp.zeros((8, 128), F32)) for _ in blocks)
    ends = lax.fori_loop(0, part, step, start)
    for n, (product, state) in enumerate(ends):
        p_all, s_all = product[0:1], state[0:1]
        for j in range(1, 8):
            p_all, s_all = p_all * product[j : j + 1], state[j : j + 1] + product[j : j + 1] * s_all
        total[2 * n : 2 * n + 1] = p_all
        total[2 * n + 1 : 2 * n + 2] = s_all
    pl.semaphore_wait(barrier, n_seq - 1)
    copies = start_exchange(total, gathered, send, recv, n_seq)
    for copy in copies:
        copy.wait()
    for n, (g, lanes) in enumerate(blocks):
        carry = jnp.zeros((1, 128), F32)
        for j in range(n_seq - 1):
            p_j = gathered[j, 2 * n : 2 * n + 1]
            s_j = gathered[j, 2 * n + 1 : 2 * n + 2]
            carry = jnp.where(j < s, s_j + p_j * carry, carry)
        before[g, 0:1, lanes] = carry
        product, state = ends[n]
        carries = [carry]
        for j in range(7):
            carries.append(state[j : j + 1] + product[j : j + 1] * carries[-1])
        for j in range(8):
            at = slice(j * part, (j + 1) * part)
            b_ref[n, at] = b_ref[n, at] + a_ref[n, at] * carries[j]
        state_b[g, :, lanes] = b_ref[n].astype(BF16)
        before[g, 1:rows, lanes] = b_ref[n, 0 : rows - 1]


def forward_scan(in_raw, forget_raw, bounds, keep, collective_id):
    n_seq = lax.axis_size("seq")
    groups, rows, chans = in_raw.shape
    blocks = groups * chans // 128
    return pl.pallas_call(
        functools.partial(forward_scan_kernel, n_seq),
        out_shape=(
            jax.ShapeDtypeStruct(in_raw.shape, BF16),
            jax.ShapeDtypeStruct(in_raw.shape, F32),
        ),
        in_specs=[VMEM] * 4,
        out_specs=(VMEM, VMEM),
        scratch_shapes=[
            pltpu.VMEM((blocks, rows, 128), F32),
            pltpu.VMEM((blocks, rows, 128), F32),
            pltpu.VMEM((2 * blocks, 128), F32),
            pltpu.VMEM((n_seq, 2 * blocks, 128), F32),
            pltpu.SemaphoreType.DMA((n_seq,)),
            pltpu.SemaphoreType.DMA((n_seq,)),
        ],
        compiler_params=params(collective_id),
        name="forward_scan",
    )(in_raw, forget_raw, bounds, keep)


def backward_scan_kernel(
    n_seq,
    d_state,
    in_raw,
    forget_raw,
    before,
    bounds,
    keep,
    d_in,
    d_forget_raw,
    d_bounds,
    p_ref,
    q_ref,
    total,
    gathered,
    send,
    recv,
):
    groups, rows, chans = in_raw.shape
    part = rows // 8
    blocks = lane_blocks(groups, chans)
    s = lax.axis_index("seq")
    barrier = pltpu.get_barrier_semaphore()
    for peer in seq_peers(n_seq):
        pl.semaphore_signal(barrier, inc=1, device_id=peer, device_id_type=MESH)
    for n, (g, lanes) in enumerate(blocks):
        bound = bounds[:, lanes]
        forget = bound + (1.0 - bound) * jax.nn.sigmoid(forget_raw[g, :, lanes].astype(F32))
        p_ref[n] = forget * keep[g]
        q_ref[n] = d_state[g, :, lanes].astype(F32)

    def step(i, carry):
        new = []
        at = pl.ds(part - 1 - i, 8, stride=part)
        for n, (product, message) in enumerate(carry):
            a = p_ref[n, at, :]
            acc = q_ref[n, at, :] + message
            p_ref[n, at, :] = product
            q_ref[n, at, :] = acc
            new.append((product * a, a * acc))
        return tuple(new)

    start = tuple((jnp.ones((8, 128), F32), jnp.zeros((8, 128), F32)) for _ in blocks)
    ends = lax.fori_loop(0, part, step, start)
    for n, (product, message) in enumerate(ends):
        p_all, m_all = product[7:8], message[7:8]
        for j in range(6, -1, -1):
            p_all, m_all = p_all * product[j : j + 1], message[j : j + 1] + product[j : j + 1] * m_all
        total[2 * n : 2 * n + 1] = p_all
        total[2 * n + 1 : 2 * n + 2] = m_all
    pl.semaphore_wait(barrier, n_seq - 1)
    copies = start_exchange(total, gathered, send, recv, n_seq)
    for copy in copies:
        copy.wait()
    d_bounds[...] = jnp.zeros((1, chans), F32)
    for n, (g, lanes) in enumerate(blocks):
        carry = jnp.zeros((1, 128), F32)
        for j in range(n_seq - 1, 0, -1):
            p_j = gathered[j, 2 * n : 2 * n + 1]
            m_j = gathered[j, 2 * n + 1 : 2 * n + 2]
            carry = jnp.where(j > s, m_j + p_j * carry, carry)
        product, message = ends[n]
        carries = [carry]
        for j in range(7, 0, -1):
            carries.append(message[j : j + 1] + product[j : j + 1] * carries[-1])
        carries = carries[::-1]
        for j in range(8):
            at = slice(j * part, (j + 1) * part)
            q_ref[n, at] = q_ref[n, at] + p_ref[n, at] * carries[j]
        acc = q_ref[n]
        bound = bounds[:, lanes]
        sigma_f = jax.nn.sigmoid(forget_raw[g, :, lanes].astype(F32))
        forget = bound + (1.0 - bound) * sigma_f
        value = in_raw[g, :, lanes].astype(F32)
        sigma_i = jax.nn.sigmoid(value)
        d_forget = acc * (before[g, :, lanes] * keep[g] - value * sigma_i)
        d_in[g, :, lanes] = (acc * (1.0 - forget) * silu_slope(value, sigma_i)).astype(BF16)
        d_sigma = d_forget * (1.0 - sigma_f)
        d_forget_raw[g, :, lanes] = (d_sigma * (1.0 - bound) * sigma_f).astype(BF16)
        d_bounds[:, lanes] += jnp.sum(d_sigma, 0, keepdims=True)


def backward_scan(d_state, in_raw, forget_raw, before, bounds, keep, collective_id):
    n_seq = lax.axis_size("seq")
    groups, rows, chans = in_raw.shape
    blocks = groups * chans // 128
    return pl.pallas_call(
        functools.partial(backward_scan_kernel, n_seq),
        out_shape=(
            jax.ShapeDtypeStruct(in_raw.shape, BF16),
            jax.ShapeDtypeStruct(in_raw.shape, BF16),
            jax.ShapeDtypeStruct((1, chans), F32),
        ),
        in_specs=[VMEM] * 6,
        out_specs=(VMEM, VMEM, VMEM),
        scratch_shapes=[
            pltpu.VMEM((blocks, rows, 128), F32),
            pltpu.VMEM((blocks, rows, 128), F32),
            pltpu.VMEM((2 * blocks, 128), F32),
            pltpu.VMEM((n_seq, 2 * blocks, 128), F32),
            pltpu.SemaphoreType.DMA((n_seq,)),
            pltpu.SemaphoreType.DMA((n_seq,)),
        ],
        compiler_params=params(collective_id),
        name="backward_scan",
    )(d_state, in_raw, forget_raw, before, bounds, keep)


def sum_all_kernel(n_seq, n_fsdp, x, out, middle, over_seq, over_fsdp, send, recv):
    s = lax.axis_index("seq")
    f = lax.axis_index("fsdp")
    along = [(lax.rem(s + k, n_seq), f) for k in range(1, n_seq)]
    across = [(s, lax.rem(f + k, n_fsdp)) for k in range(1, n_fsdp)]
    enter(along + across)
    copies = []
    for k, peer in enumerate(along):
        copy = remote(x, over_seq.at[k], send.at[k], recv.at[k], peer)
        copy.start()
        copies.append(copy)
    total = x[...]
    for k, copy in enumerate(copies):
        copy.wait_recv()
        total = total + over_seq[k]
    middle[...] = total
    later = []
    for k, peer in enumerate(across):
        slot = n_seq - 1 + k
        copy = remote(middle, over_fsdp.at[k], send.at[slot], recv.at[slot], peer)
        copy.start()
        later.append(copy)
    for k, copy in enumerate(later):
        copy.wait_recv()
        total = total + over_fsdp[k]
    out[...] = total
    for copy in copies + later:
        copy.wait_send()


def sum_all(x, collective_id):
    n_seq, n_fsdp = lax.axis_size("seq"), lax.axis_size("fsdp")
    count = n_seq + n_fsdp - 2
    return pl.pallas_call(
        functools.partial(sum_all_kernel, n_seq, n_fsdp),
        out_shape=jax.ShapeDtypeStruct(x.shape, F32),
        in_specs=[VMEM],
        out_specs=VMEM,
        scratch_shapes=[
            pltpu.VMEM(x.shape, F32),
            pltpu.VMEM((n_seq - 1,) + x.shape, F32),
            pltpu.VMEM((n_fsdp - 1,) + x.shape, F32),
            pltpu.SemaphoreType.DMA((count,)),
            pltpu.SemaphoreType.DMA((count,)),
        ],
        compiler_params=params(collective_id),
        name="sum_all",
    )(x)


def sum_over_seq(part):
    return lax.psum_scatter(part.astype(BF16), "seq", scatter_dimension=0, tiled=True).astype(F32)


def per_device(
    hidden,
    lengths,
    w_input,
    w_forget,
    w_gate_out,
    w_output,
    norm_gain,
    gate_gain,
    glu_gain,
    lower_table,
    w_glu_gate,
    w_glu_up,
    w_glu_down,
    cotangent,
):
    seq_index = lax.axis_index("seq")
    fsdp_index = lax.axis_index("fsdp")
    groups = lax.axis_size("fsdp")
    _, rows, width = hidden.shape
    chans = w_input.shape[1]
    units = w_glu_gate.shape[1]
    tokens = groups * rows
    small_shape = (round_up(groups, 8), round_up(rows, 128))

    def to_small(value):
        return jnp.pad(
            value, ((0, small_shape[0] - value.shape[0]), (0, small_shape[1] - value.shape[1]))
        )

    def dot(left, right):
        return jnp.dot(left, right, preferred_element_type=F32)

    def dot_t(left, right):
        return lax.dot_general(left, right, (((1,), (1,)), ((), ())), preferred_element_type=F32)

    def over_tokens(left, right):
        return lax.dot_general(left, right, (((0,), (0,)), ((), ())), preferred_element_type=F32)

    cotangent_all = lax.all_gather(cotangent[0], "fsdp").reshape(tokens, width)

    hidden_f = hidden[0].astype(F32)
    scale_one = lax.rsqrt(jnp.mean(hidden_f * hidden_f, -1, keepdims=True) + epsilon)
    normed = (hidden_f * scale_one * norm_gain).astype(BF16)
    normed_all, _ = gather(normed, jnp.zeros((8, 128), F32), 0)
    normed_all = normed_all.reshape(tokens, width)
    in_raw = dot(normed_all, w_input).astype(BF16).reshape(groups, rows, chans)
    forget_raw = dot(normed_all, w_forget).astype(BF16).reshape(groups, rows, chans)
    gate_raw = dot(normed_all, w_gate_out)

    bounds_full = lower_bound(lower_table)
    bounds = lax.dynamic_slice_in_dim(bounds_full, fsdp_index * chans, chans)[None]
    seq_starts = jnp.cumsum(lengths, axis=1) - lengths
    places = seq_index * rows + jnp.arange(rows, dtype=jnp.int32)
    starts = jnp.any(places[None, :, None] == seq_starts[:, None, :], axis=-1)
    keep = jnp.where(starts, 0.0, 1.0).astype(F32)[:, :, None]
    state_b, before = forward_scan(in_raw, forget_raw, bounds, keep, 1)

    state_f = state_b.astype(F32).reshape(tokens, chans)
    gain_slice = lax.dynamic_slice_in_dim(gate_gain, fsdp_index * chans, chans)
    sigma_g = jax.nn.sigmoid(gate_raw)
    silu_gate = gate_raw * sigma_g
    out_raw = (state_f * gain_slice * silu_gate).astype(BF16)
    squares = jnp.sum(state_f * state_f, -1).reshape(groups, rows)
    mixed_part = dot(out_raw, w_output).astype(BF16).reshape(groups, rows, width)
    mixed_raw, square_sum = reduce_rows(mixed_part, to_small(squares), 2)
    state_scale = lax.rsqrt(square_sum[:groups, :rows] / width + epsilon)
    own_scale = lax.dynamic_slice_in_dim(state_scale, fsdp_index, 1, 0)[0][:, None]
    scale_g = state_scale.reshape(tokens, 1)
    middle = hidden_f + own_scale * mixed_raw
    scale_two = lax.rsqrt(jnp.mean(middle * middle, -1, keepdims=True) + epsilon)
    normed_two = (middle * scale_two * glu_gain).astype(BF16)
    normed_two_all, _ = gather(normed_two, jnp.zeros((8, 128), F32), 3)
    normed_two_all = normed_two_all.reshape(tokens, width)

    gate_val = dot(normed_two_all, w_glu_gate)
    up_val = dot(normed_two_all, w_glu_up)
    sigma_u = jax.nn.sigmoid(gate_val)
    silu_u = gate_val * sigma_u
    activity = (silu_u * up_val).astype(BF16)
    down_grad = sum_over_seq(over_tokens(cotangent_all, activity))
    d_act = dot_t(cotangent_all, w_glu_down)
    d_gate = (d_act * up_val * silu_slope(gate_val, sigma_u)).astype(BF16)
    d_up = (d_act * silu_u).astype(BF16)
    pair_grad = sum_over_seq(
        jnp.concatenate(
            [
                over_tokens(normed_two_all, d_gate).astype(BF16),
                over_tokens(normed_two_all, d_up).astype(BF16),
            ],
            1,
        )
    )
    d_two_part = (dot_t(d_gate, w_glu_gate) + dot_t(d_up, w_glu_up)).astype(BF16)
    no_small = jnp.zeros((8, 128), F32)
    d_normed_two, _ = reduce_rows(d_two_part.reshape(groups, rows, width), no_small, 4)
    glu_part = dot(activity, w_glu_down).astype(BF16).reshape(groups, rows, width)
    glu_result = lax.psum_scatter(glu_part, "fsdp", scatter_dimension=0, tiled=True)[0]
    output = (middle + glu_result.astype(F32)).astype(BF16)[None]

    cotangent_f = cotangent[0].astype(F32)
    scaled_two = glu_gain * d_normed_two
    d_middle = (
        cotangent_f
        + scale_two * scaled_two
        - middle * scale_two**3 * jnp.mean(scaled_two * middle, -1, keepdims=True)
    )
    d_glu_gain = jnp.sum(d_normed_two * middle * scale_two, 0)
    d_mixed = d_middle.astype(BF16)
    own_dot = jnp.sum(d_mixed.astype(F32) * mixed_raw, -1)[None]
    d_mixed_all, dots = gather(d_mixed, to_small(own_dot), 5)
    d_mixed_all = d_mixed_all.reshape(tokens, width)
    dot_rows = dots[:, 0, :rows].reshape(tokens, 1)

    d_out = dot_t(d_mixed_all, w_output)
    scaled_state = state_f * scale_g
    d_gain_slice = jnp.sum(d_out * scaled_state * silu_gate, 0)
    d_scaled = d_out * gain_slice * silu_gate
    d_gate_raw = (d_out * scaled_state * gain_slice * silu_slope(gate_raw, sigma_g)).astype(BF16)
    d_state = scale_g * d_scaled - state_f * (scale_g**3 * (dot_rows / width))
    d_state = d_state.astype(BF16).reshape(groups, rows, chans)
    d_in, d_forget_raw, d_bounds = backward_scan(
        d_state, in_raw, forget_raw, before, bounds, keep, 6
    )
    d_in = d_in.reshape(tokens, chans)
    d_forget_raw = d_forget_raw.reshape(tokens, chans)

    d_normed_part = dot_t(d_in, w_input) + dot_t(d_forget_raw, w_forget)
    d_normed_part = (d_normed_part + dot_t(d_gate_raw, w_gate_out)).astype(BF16)
    out_gate = (out_raw.astype(F32) * scale_g).astype(BF16)
    mixer_grad = sum_over_seq(
        jnp.concatenate(
            [
                over_tokens(d_mixed_all, out_gate).astype(BF16),
                over_tokens(normed_all, d_in).astype(BF16),
                over_tokens(normed_all, d_forget_raw).astype(BF16),
                over_tokens(normed_all, d_gate_raw).astype(BF16),
            ],
            1,
        )
    )
    d_normed, _ = reduce_rows(d_normed_part.reshape(groups, rows, width), no_small, 7)
    scaled_one = norm_gain * d_normed
    d_hidden = (
        d_middle
        + scale_one * scaled_one
        - hidden_f * scale_one**3 * jnp.mean(scaled_one * hidden_f, -1, keepdims=True)
    )
    d_norm_gain = jnp.sum(d_normed * hidden_f * scale_one, 0)
    d_gain_full = lax.dynamic_update_slice(
        jnp.zeros((width,), F32), d_gain_slice, (fsdp_index * chans,)
    )
    d_bounds_full = lax.dynamic_update_slice(
        jnp.zeros((width,), F32), d_bounds[0], (fsdp_index * chans,)
    )
    sums = jnp.stack([d_norm_gain, d_glu_gain, d_gain_full, d_bounds_full])
    totals = sum_all(sums.reshape(8, width // 2), 8).reshape(4, width)
    _, bounds_pull = jax.vjp(lower_bound, lower_table)
    d_table = bounds_pull(totals[3])[0]
    return (
        output,
        d_hidden.astype(BF16)[None],
        mixer_grad[:, chans : 2 * chans],
        mixer_grad[:, 2 * chans : 3 * chans],
        mixer_grad[:, 3 * chans :],
        mixer_grad[:, :chans].T,
        totals[0],
        totals[2],
        totals[1],
        d_table,
        pair_grad[:, :units],
        pair_grad[:, units:],
        down_grad.T,
    )


def copy_in(src, dst, sem):
    copy = pltpu.make_async_copy(src, dst, sem)
    copy.start()
    return copy


class Links:
    def __init__(self, send, recv):
        self.send, self.recv, self.used = send, recv, 0

    def start(self, src, dst, device):
        copy = remote(src, dst, self.send.at[self.used], self.recv.at[self.used], device)
        self.used += 1
        copy.start()
        return copy


class Locals:
    def __init__(self, sems):
        self.sems, self.used = sems, 0

    def start(self, src, dst):
        copy = copy_in(src, dst, self.sems.at[self.used])
        self.used += 1
        return copy


def row_slots(rows):
    half = rows // 2
    top = [pl.ds(k * rows, half) for k in range(4)]
    bottom = [pl.ds(k * rows + half, half) for k in range(4)]
    return top, bottom


def gather_start(links, src, dst, rows, s, fx, fy):
    half = rows // 2
    top, bottom = row_slots(rows)
    here = (pl.ds(0, half), pl.ds(half, half))
    return [
        links.start(src.at[here[0]], dst.at[top[1]], (s, fx)),
        links.start(src.at[here[1]], dst.at[bottom[2]], (s, fy)),
        links.start(src.at[here[1]], dst.at[bottom[1]], (s, fx)),
        links.start(src.at[here[0]], dst.at[top[2]], (s, fy)),
    ]


def gather_forward(links, own, dst, rows, s, fx, fy):
    top, bottom = row_slots(rows)
    own[0].wait_recv()
    on_y = links.start(dst.at[top[1]], dst.at[top[3]], (s, fy))
    own[1].wait_recv()
    on_x = links.start(dst.at[bottom[2]], dst.at[bottom[3]], (s, fx))
    return [on_y, on_x]


def gather_middle(own):
    own[2].wait_recv()
    own[3].wait_recv()


def gather_far(later):
    for copy in later:
        copy.wait_recv()


def sends_done(*lists):
    for copies in lists:
        for copy in copies:
            copy.wait_send()


def wait_all(*lists):
    for copies in lists:
        for copy in copies:
            copy.wait()


def reduce_start_far(links, part, from_x, from_y, rows, s, fx, fy):
    top, bottom = row_slots(rows)
    return [
        links.start(part.at[top[3]], from_x.at[0], (s, fx)),
        links.start(part.at[bottom[3]], from_y.at[0], (s, fy)),
    ]


def reduce_start_near(links, part, from_x, from_y, rows, s, fx, fy):
    top, bottom = row_slots(rows)
    return [
        links.start(part.at[top[1]], from_x.at[1], (s, fx)),
        links.start(part.at[bottom[2]], from_y.at[1], (s, fy)),
    ]


def reduce_pass(links, far, part, from_x, from_y, pass_x, pass_y, rows, s, fx, fy):
    top, bottom = row_slots(rows)
    far[0].wait_recv()
    pass_y[...] = (from_x[0].astype(F32) + part[top[2]].astype(F32)).astype(BF16)
    on_y = links.start(pass_y, from_y.at[2], (s, fy))
    far[1].wait_recv()
    pass_x[...] = (from_y[0].astype(F32) + part[bottom[1]].astype(F32)).astype(BF16)
    on_x = links.start(pass_x, from_x.at[2], (s, fx))
    return [on_y, on_x]


def mm(left, right):
    return jnp.dot(left, right, preferred_element_type=F32)


def mm_t(left, right):
    return lax.dot_general(left, right, (((1,), (1,)), ((), ())), preferred_element_type=F32)


def tile(n, width):
    return pl.ds(pl.multiple_of(n * width, width), width)


def bounds_slice(table, first, count):
    rows = table[:, pl.ds(pl.multiple_of(first, 128), count)]
    powers = jnp.exp(rows - jnp.max(rows, 0, keepdims=True))
    return jnp.sum(powers[1 : LAYER + 1], 0, keepdims=True) / jnp.sum(powers, 0, keepdims=True)


def keep_rows(lengths, group, first, rows):
    places = first + lax.broadcasted_iota(jnp.int32, (rows, 128), 0)
    start = jnp.int32(0)
    keep = jnp.where(places == start, 0.0, 1.0)
    for i in range(lengths.shape[1] - 1):
        start = start + lengths[group, i]
        keep = jnp.where(places == start, 0.0, keep)
    return keep.astype(F32)


def segment_totals(end_p, end_s, blocks, order):
    first, rest = order[0], order[1:]
    p_all = end_p[pl.ds(first, blocks, stride=8), :]
    s_all = end_s[pl.ds(first, blocks, stride=8), :]
    for j in rest:
        p_j = end_p[pl.ds(j, blocks, stride=8), :]
        s_all = end_s[pl.ds(j, blocks, stride=8), :] + p_j * s_all
        p_all = p_all * p_j
    return p_all, s_all


def spread_carry(carry, carr, end_p, end_s, blocks, order):
    for i, j in enumerate(order):
        carr[pl.ds(j, blocks, stride=8), :] = carry
        if i < 7:
            carry = end_s[pl.ds(j, blocks, stride=8), :] + end_p[pl.ds(j, blocks, stride=8), :] * carry


def mixer_kernel(
    n_seq,
    lengths,
    hidden,
    cot,
    norm_gain,
    gate_gain,
    glu_gain,
    table,
    w_in,
    w_fg,
    w_gt,
    w_out,
    normed_half,
    cot_out,
    in_out,
    fg_out,
    gate_out,
    state_out,
    raw_out,
    before_out,
    scale_out,
    middle,
    two,
    wv,
    wo,
    rows_all,
    stage,
    in_ref,
    fg_ref,
    gate_ref,
    a_ref,
    b_ref,
    shifted,
    keep_ref,
    end_p,
    end_s,
    carr,
    total,
    gathered,
    state_ref,
    raw_ref,
    squares,
    squares_t,
    packed,
    squares_in,
    part,
    from_x,
    from_y,
    pass_x,
    pass_y,
    send,
    recv,
    exchange_send,
    exchange_recv,
    local_sems,
):
    rows, width = hidden.shape
    chans = w_in.shape[1]
    lanes_of = [slice(c, c + 128) for c in range(0, chans, 128)]
    count = len(lanes_of)
    blocks = 4 * count
    step_len = rows // 8
    s, f, fx, fy, fd = plane()
    groups = [f, fx, fy, fd]
    links, local = Links(send, recv), Locals(local_sems)

    weights = [
        local.start(w, wv.at[:, pl.ds(i * chans, chans)]) for i, w in enumerate((w_in, w_fg, w_gt))
    ]
    weights.append(local.start(w_out, wo))
    barrier = pltpu.get_barrier_semaphore()
    peers = [(s, fx), (s, fy), (s, fd)] + seq_peers(n_seq)
    for peer in peers:
        pl.semaphore_signal(barrier, inc=1, device_id=peer, device_id_type=MESH)

    def norm_rows(i, _):
        at = pl.ds(pl.multiple_of(i * 16, 16), 16)
        value = hidden[at].astype(F32)
        scale = lax.rsqrt(jnp.mean(value * value, -1, keepdims=True) + epsilon)
        rows_all[at] = (value * scale * norm_gain[...]).astype(BF16)
        return 0

    lax.fori_loop(0, rows // 16, norm_rows, 0)
    pl.semaphore_wait(barrier, len(peers))
    own = gather_start(links, rows_all, rows_all, rows, s, fx, fy)
    bound = bounds_slice(table, f * chans, chans)
    for k in range(4):
        keep_ref[k] = keep_rows(lengths, groups[k], s * rows, rows)
    squares[...] = jnp.zeros_like(squares)
    squares_t[...] = jnp.zeros_like(squares_t)
    for copy in weights[:3]:
        copy.wait()

    def project(first, slots):
        def tile_of(n, _):
            cols = tile(n, 256)
            stage[: slots * rows, cols] = mm(
                rows_all[first * rows : (first + slots) * rows], wv[:, cols]
            )
            return 0

        lax.fori_loop(0, 3 * chans // 256, tile_of, 0)
        for k in range(slots):
            at = slice(k * rows, (k + 1) * rows)
            for c, lanes in enumerate(lanes_of):
                n = (first + k) * count + c
                value = stage[at, lanes].astype(BF16)
                in_ref[first + k, :, lanes] = value
                value = value.astype(F32)
                raw = stage[at, chans + c * 128 : chans + (c + 1) * 128].astype(BF16)
                fg_ref[first + k, :, lanes] = raw
                edge = bound[:, lanes]
                forget = edge + (1.0 - edge) * jax.nn.sigmoid(raw.astype(F32))
                a_ref[n] = forget * keep_ref[first + k]
                b_ref[n] = value * jax.nn.sigmoid(value) * (1.0 - forget)
            gate_ref[first + k] = stage[at, 2 * chans :]

    project(0, 1)
    later = gather_forward(links, own, rows_all, rows, s, fx, fy)
    gather_middle(own)
    project(1, 2)
    gather_far(later)
    cot_own = gather_start(links, cot, cot_out, rows, s, fx, fy)
    core = s % 2
    swaps, outs = swap_columns(
        links, local, rows_all, normed_half, n_seq, core, (s + 1 - 2 * core, f)
    )
    outs.append(local.start(cot, cot_out.at[pl.ds(0, rows)]))
    project(3, 1)
    outs += [
        local.start(in_ref, in_out),
        local.start(fg_ref, fg_out),
        local.start(gate_ref, gate_out),
    ]

    def scan_step(i, carry):
        new = []
        at = pl.ds(i, 8, stride=step_len)
        for n, (product, state) in enumerate(carry):
            a = a_ref[n, at, :]
            state = a * state + b_ref[n, at, :]
            product = product * a
            a_ref[n, at, :] = product
            b_ref[n, at, :] = state
            new.append((product, state))
        return tuple(new)

    start = tuple((jnp.ones((8, 128), F32), jnp.zeros((8, 128), F32)) for _ in range(blocks))
    ends = lax.fori_loop(0, step_len, scan_step, start)
    for n, (product, state) in enumerate(ends):
        end_p[8 * n : 8 * n + 8] = product
        end_s[8 * n : 8 * n + 8] = state
    p_all, s_all = segment_totals(end_p, end_s, blocks, range(8))
    total[:blocks] = p_all
    total[blocks:] = s_all
    copies = start_exchange(total, gathered, exchange_send, exchange_recv, n_seq)
    wait_all(copies)
    carry = jnp.zeros((blocks, 128), F32)
    for j in range(n_seq - 1):
        carry = jnp.where(j < s, gathered[j, blocks:] + gathered[j, :blocks] * carry, carry)
    for n in range(blocks):
        shifted[n, 0:1] = carry[n : n + 1]
    spread_carry(carry, carr, end_p, end_s, blocks, range(8))

    def finish(n, _):
        enter_state = carr[pl.ds(pl.multiple_of(n * 8, 8), 8)]
        for i in range(step_len):
            at = pl.ds(i, 8, stride=step_len)
            state = b_ref[n, at, :] + a_ref[n, at, :] * enter_state
            b_ref[n, at, :] = state
            shifted[n, pl.ds(i + 1, 8, stride=step_len), :] = state
        return 0

    lax.fori_loop(0, blocks, finish, 0)
    outs.append(local.start(shifted.at[:, pl.ds(0, rows)], before_out))

    lane = lax.broadcasted_iota(jnp.int32, (rows, 128), 1)
    for k in (3, 1, 2, 0):
        square = jnp.zeros((rows, 1), F32)
        for c, lanes in enumerate(lanes_of):
            state_b = b_ref[k * count + c].astype(BF16)
            state_ref[k, :, lanes] = state_b
            state = state_b.astype(F32)
            square = square + jnp.sum(state * state, -1, keepdims=True)
            gate = gate_ref[k, :, lanes]
            gain = gate_gain[:, pl.ds(pl.multiple_of(f * chans + c * 128, 128), 128)]
            raw_ref[k * rows : (k + 1) * rows, lanes] = (
                state * gain * gate * jax.nn.sigmoid(gate)
            ).astype(BF16)
        squares[:rows] = jnp.where(lane == groups[k], square, squares[:rows])
    packed[...] = squares[...].T[:8]
    square_copies = [
        links.start(packed, squares_in.at[i], (s, peer)) for i, peer in enumerate((fx, fy, fd))
    ]
    outs += [local.start(state_ref, state_out), local.start(raw_ref, raw_out)]
    cot_later = gather_forward(links, cot_own, cot_out, rows, s, fx, fy)
    weights[3].wait()

    def output_part(first, slots):
        at = slice(first * rows, (first + slots) * rows)

        def tile_of(n, _):
            cols = tile(n, 512)
            part[at, cols] = mm(raw_ref[at], wo[:, cols]).astype(BF16)
            return 0

        lax.fori_loop(0, width // 512, tile_of, 0)

    output_part(3, 1)
    far = reduce_start_far(links, part, from_x, from_y, rows, s, fx, fy)
    output_part(1, 2)
    near = reduce_start_near(links, part, from_x, from_y, rows, s, fx, fy)
    output_part(0, 1)
    passed = reduce_pass(links, far, part, from_x, from_y, pass_x, pass_y, rows, s, fx, fy)
    for copy in square_copies:
        copy.wait_recv()
    all_squares = (packed[...] + squares_in[0]) + (squares_in[1] + squares_in[2])
    squares_t[:8] = lax.rsqrt(all_squares / width + epsilon)
    scales = squares_t[...].T[:rows]
    for k in range(4):
        scale_out[k] = jnp.sum(jnp.where(lane == groups[k], scales, 0.0), -1, keepdims=True)
    for copy in near + passed:
        copy.wait_recv()
    half = rows // 2
    for first, one, other in ((0, from_x.at[1], from_y.at[2]), (half, from_y.at[1], from_x.at[2])):

        def sum_rows(i, _):
            here = pl.ds(pl.multiple_of(i * 16, 16), 16)
            at = pl.ds(pl.multiple_of(first + i * 16, 16), 16)
            mixed = part[at].astype(F32) + one[here].astype(F32) + other[here].astype(F32)
            value = hidden[at].astype(F32) + scale_out[0, at] * mixed
            middle[at] = value
            scale = lax.rsqrt(jnp.mean(value * value, -1, keepdims=True) + epsilon)
            two[at] = (value * scale * glu_gain[...]).astype(BF16)
            return 0

        lax.fori_loop(0, half // 16, sum_rows, 0)
    gather_middle(cot_own)
    gather_far(cot_later)
    sends_done(own, later, cot_own, cot_later, square_copies, far, near, passed)
    wait_all(swaps, outs)


def mixer_forward(lengths, hidden, cot, gains, table, weights, collective_id):
    n_seq = lax.axis_size("seq")
    rows, width = hidden.shape
    chans = weights[0].shape[1]
    blocks = 4 * chans // 128
    tokens = 4 * rows
    half = rows // 2
    shape = jax.ShapeDtypeStruct
    wide = shape((tokens, width), BF16)
    narrow = shape((4, rows, chans), BF16)
    long_rows = round_up(rows, 128)
    return pl.pallas_call(
        functools.partial(mixer_kernel, n_seq),
        out_shape=(
            shape((2, tokens, width // 2), BF16),
            wide,
            narrow,
            narrow,
            shape((4, rows, chans), F32),
            narrow,
            shape((tokens, chans), BF16),
            shape((blocks, rows, 128), F32),
            shape((4, rows, 1), F32),
            shape((rows, width), F32),
            shape((rows, width), BF16),
        ),
        in_specs=[pl.BlockSpec(memory_space=pltpu.SMEM), VMEM, VMEM, VMEM, VMEM, VMEM, VMEM]
        + [ANY] * 4,
        out_specs=(ANY,) * 8 + (VMEM,) * 3,
        scratch_shapes=[
            pltpu.VMEM((width, 3 * chans), BF16),
            pltpu.VMEM((chans, width), BF16),
            pltpu.VMEM((tokens, width), BF16),
            pltpu.VMEM((2 * rows, 3 * chans), F32),
            pltpu.VMEM((4, rows, chans), BF16),
            pltpu.VMEM((4, rows, chans), BF16),
            pltpu.VMEM((4, rows, chans), F32),
            pltpu.VMEM((blocks, rows, 128), F32),
            pltpu.VMEM((blocks, rows, 128), F32),
            pltpu.VMEM((blocks, rows + 8, 128), F32),
            pltpu.VMEM((4, rows, 128), F32),
            pltpu.VMEM((8 * blocks, 128), F32),
            pltpu.VMEM((8 * blocks, 128), F32),
            pltpu.VMEM((8 * blocks, 128), F32),
            pltpu.VMEM((2 * blocks, 128), F32),
            pltpu.VMEM((n_seq, 2 * blocks, 128), F32),
            pltpu.VMEM((4, rows, chans), BF16),
            pltpu.VMEM((tokens, chans), BF16),
            pltpu.VMEM((long_rows, 128), F32),
            pltpu.VMEM((128, long_rows), F32),
            pltpu.VMEM((8, long_rows), F32),
            pltpu.VMEM((3, 8, long_rows), F32),
            pltpu.VMEM((tokens, width), BF16),
            pltpu.VMEM((3, half, width), BF16),
            pltpu.VMEM((3, half, width), BF16),
            pltpu.VMEM((half, width), BF16),
            pltpu.VMEM((half, width), BF16),
            pltpu.SemaphoreType.DMA((21 + n_seq // 2,)),
            pltpu.SemaphoreType.DMA((21 + n_seq // 2,)),
            pltpu.SemaphoreType.DMA((n_seq,)),
            pltpu.SemaphoreType.DMA((n_seq,)),
            pltpu.SemaphoreType.DMA((11 + n_seq // 2,)),
        ],
        compiler_params=params(collective_id),
        name="mixer_forward",
    )(lengths, hidden, cot, *gains, table, *weights)


def swap_columns(links, local, src, dst, n_seq, core, mate):
    part = src.shape[1] // n_seq
    copies, stays = [], []
    for z in range(n_seq // 2):
        to = pl.ds(z * part, part)
        theirs = pl.ds(pl.multiple_of((2 * z + 1 - core) * part, part), part)
        ours = pl.ds(pl.multiple_of((2 * z + core) * part, part), part)
        copies.append(links.start(src.at[:, theirs], dst.at[1, :, to], mate))
        stays.append(local.start(src.at[:, ours], dst.at[0, :, to]))
    return copies, stays


def glu_kernel(
    n_seq,
    two,
    cot_all,
    w_gate,
    w_up,
    w_down,
    two_half,
    cot_half,
    act_pair,
    gate_pair,
    up_pair,
    wv,
    wd,
    cot_ref,
    two_ref,
    d_act,
    stage,
    act,
    d_gate,
    d_up,
    send,
    recv,
    local_sems,
):
    rows = two.shape[0]
    units = w_gate.shape[1]
    s, f, fx, fy, fd = plane()
    core = s % 2
    mate = (s + 1 - 2 * core, f)
    links, local = Links(send, recv), Locals(local_sems)
    loads = [local.start(w_down, wd), local.start(cot_all, cot_ref)]
    two_ref[:rows] = two[...]
    enter([(s, fx), (s, fy), mate])
    own = gather_start(links, two_ref, two_ref, rows, s, fx, fy)
    wait_all(loads)
    loads = [
        local.start(w_gate, wv.at[:, pl.ds(0, units)]),
        local.start(w_up, wv.at[:, pl.ds(units, units)]),
    ]
    swaps, stays = swap_columns(links, local, cot_ref, cot_half, n_seq, core, mate)

    def act_tile(n, _):
        cols = tile(n, 256)
        d_act[:, cols] = mm_t(cot_ref[...], wd[cols])
        return 0

    lax.fori_loop(0, units // 256, act_tile, 0)
    if units % 256:
        rest = slice(units // 256 * 256, units)
        d_act[:, rest] = mm_t(cot_ref[...], wd[rest])
    later = gather_forward(links, own, two_ref, rows, s, fx, fy)
    wait_all(loads)

    def slots(first, number, swap=True):
        nonlocal swaps, stays
        base = first * rows

        def tile_of(n, _):
            cols = tile(n, 256)
            stage[: number * rows, cols] = mm(two_ref[base : base + number * rows], wv[:, cols])
            return 0

        lax.fori_loop(0, 2 * units // 256, tile_of, 0)

        def rows_of(i, _):
            at = pl.ds(pl.multiple_of(i * 16, 16), 16)
            to = pl.ds(pl.multiple_of(base + i * 16, 16), 16)
            gate, up = stage[at, :units], stage[at, units:]
            sigma = jax.nn.sigmoid(gate)
            silu = gate * sigma
            act[to] = (silu * up).astype(BF16)
            d = d_act[to]
            d_gate[to] = (d * up * silu_slope(gate, sigma)).astype(BF16)
            d_up[to] = (d * silu).astype(BF16)
            return 0

        cuts = number * rows // 2
        for first_row in (0, cuts):
            lax.fori_loop(first_row // 16, (first_row + cuts) // 16, rows_of, 0)
            at = pl.ds(base + first_row, cuts)
            for src, dst in ((act, act_pair), (d_gate, gate_pair), (d_up, up_pair)):
                stays = stays + [local.start(src.at[at], dst.at[0, at])]
                if swap:
                    swaps = swaps + [links.start(src.at[at], dst.at[1, at], mate)]

    slots(0, 1)
    gather_middle(own)
    slots(1, 2)
    gather_far(later)
    more, keeps = swap_columns(links, local, two_ref, two_half, n_seq, core, mate)
    slots(3, 1, False)
    sends_done(own, later)
    wait_all(swaps, stays, more, keeps)


def glu(two, cot_all, w_gate, w_up, w_down, collective_id):
    n_seq = lax.axis_size("seq")
    rows, width = two.shape
    units = w_gate.shape[1]
    tokens = 4 * rows
    shape = jax.ShapeDtypeStruct
    half = shape((2, tokens, width // 2), BF16)
    pair = shape((2, tokens, units), BF16)
    remote_count = 6 + n_seq + 12
    return pl.pallas_call(
        functools.partial(glu_kernel, n_seq),
        out_shape=(half, half, pair, pair, pair),
        in_specs=[VMEM] + [ANY] * 4,
        out_specs=(ANY,) * 5,
        scratch_shapes=[
            pltpu.VMEM((width, 2 * units), BF16),
            pltpu.VMEM((units, width), BF16),
            pltpu.VMEM((tokens, width), BF16),
            pltpu.VMEM((tokens, width), BF16),
            pltpu.VMEM((tokens, units), F32),
            pltpu.VMEM((2 * rows, 2 * units), F32),
            pltpu.VMEM((tokens, units), BF16),
            pltpu.VMEM((tokens, units), BF16),
            pltpu.VMEM((tokens, units), BF16),
            pltpu.SemaphoreType.DMA((remote_count,)),
            pltpu.SemaphoreType.DMA((remote_count,)),
            pltpu.SemaphoreType.DMA((4 + n_seq + 18,)),
        ],
        compiler_params=params(collective_id),
        name="glu",
    )(two, cot_all, w_gate, w_up, w_down)


class ZLine:
    def __init__(self, part, buf, sems, n_seq, width, lag, ahead, store=None, leave=None):
        self.part, self.buf, self.width, self.lag, self.ahead = part, buf, width, lag, ahead
        self.send_up, self.recv_up, self.send_down, self.recv_down = sems[:4]
        self.store, self.leave = store, leave
        self.s, self.f = lax.axis_index("seq"), lax.axis_index("fsdp")
        self.n_seq, self.nz = n_seq, n_seq // 2
        self.z = self.s // 2
        self.block = part.shape[0] // self.nz
        self.chunks = part.shape[1] // width
        self.steps = (self.nz - 1) * self.chunks
        self.calls = self.steps + lag * (self.nz - 2)

    def rows(self, t):
        return pl.ds(pl.multiple_of(t * self.block, self.block), self.block)

    def move(self, up, k, j):
        t = self.nz - 1 - k if up else k
        landing = t + 1 if up else t
        cols = tile(j, self.width)
        slot = k * self.chunks + j
        peer = lax.rem(self.s + (2 if up else self.n_seq - 2), self.n_seq)
        send, recv = (
            (self.send_up, self.recv_up) if up else (self.send_down, self.recv_down)
        )
        return remote(
            self.part.at[self.rows(t), cols],
            self.buf.at[self.rows(landing), cols],
            send.at[slot],
            recv.at[slot],
            (peer, self.f),
        )

    def feed(self, q):
        inside = q < self.steps
        q = jnp.minimum(q, self.steps - 1)
        k = q // self.chunks
        j = q - k * self.chunks

        @pl.when(inside & (self.z == 0))
        def _():
            self.move(True, k, j).start()

        @pl.when(inside & (self.z == self.nz - 1))
        def _():
            self.move(False, k, j).start()

    def nth(self, i):
        return jnp.where(self.z < self.nz // 2, self.nz - 1 - i, i)

    def load(self, local, src, first, last):
        order = [self.rows(self.nth(i)) for i in range(first, last)]
        return [local.start(src.at[at], self.part.at[at]) for at in order]

    def feed_first(self):
        def step(q, _):
            self.feed(q)
            return 0

        lax.fori_loop(0, self.ahead, step, 0)

    def serve_one(self, up, q):
        z, nz = self.z, self.nz
        hops = z if up else nz - 1 - z
        q = q - self.lag * (hops - 1)
        inside = (hops >= 1) & (q >= 0) & (q < self.steps)
        q = jnp.clip(q, 0, self.steps - 1)
        k = q // self.chunks
        j = q - k * self.chunks
        left = nz - 1 - k - hops
        cols = tile(j, self.width)

        @pl.when(inside & (left >= 0))
        def _():
            self.move(up, k, j).wait_recv()

        @pl.when(inside & (left > 0))
        def _():
            t = nz - 1 - k if up else k
            landing = t + 1 if up else t
            own = self.part[self.rows(t), cols].astype(F32)
            came = self.buf[self.rows(landing), cols].astype(F32)
            self.part[self.rows(t), cols] = (own + came).astype(BF16)
            self.move(up, k, j).start()

    def serve(self, q, done=False):
        self.serve_one(True, q)
        self.serve_one(False, q)
        if done:
            j = q - (self.nz - 2) * self.chunks

            @pl.when((j >= 0) & (j < self.chunks))
            def _():
                self.finish(j)

    def serve_range(self, first, last, done=False):
        def step(q, _):
            self.feed(q + self.ahead)
            self.serve(q, done)
            return 0

        lax.fori_loop(first, last, step, 0)

    def finish(self, j):
        cols = tile(j, self.width)
        above = self.buf[self.rows(self.z), cols].astype(F32)
        below = self.buf[self.rows(self.z + 1), cols].astype(F32)
        own = self.part[self.rows(self.z), cols].astype(F32)
        own = own + jnp.where(self.z < self.nz - 1, above, 0.0)
        self.store(j, own + jnp.where(self.z > 0, below, 0.0))
        self.leave(j, True)

    def drain(self):
        for k in range(self.nz - 1):
            for up in (True, False):
                hops = self.z if up else self.nz - 1 - self.z

                @pl.when(hops < self.nz - 1 - k)
                def _():
                    def step(j, _):
                        self.move(up, k, j).wait_send()
                        return 0

                    lax.fori_loop(0, self.chunks, step, 0)

        def left(j, _):
            self.leave(j, False)
            return 0

        lax.fori_loop(0, self.chunks, left, 0)


def start_or_wait(copy, start):
    if start:
        copy.start()
    else:
        copy.wait()


def line_sems(n_seq, columns, width):
    count = (n_seq // 2 - 1) * (columns // width)
    leave = pltpu.SemaphoreType.DMA((columns // width,))
    return [pltpu.SemaphoreType.DMA((count,)) for _ in range(4)] + [leave]


def z_peers(n_seq):
    s = lax.axis_index("seq")
    f = lax.axis_index("fsdp")
    return [(lax.rem(s + 2 * k, n_seq), f) for k in range(1, n_seq // 2)]


def mm_tokens(left, right):
    return lax.dot_general(left, right, (((0,), (0,)), ((), ())), preferred_element_type=F32)


def down_kernel(
    n_seq,
    cot_half,
    act_pair,
    two_half,
    gate_pair,
    up_pair,
    w_gate,
    w_up,
    d_two_out,
    pair_part,
    down_out,
    d_two,
    cot_ref,
    act_ref,
    two_ref,
    gate_ref,
    up_ref,
    wg,
    wu,
    part,
    buf,
    rows_part,
    from_x,
    from_y,
    pass_x,
    pass_y,
    pair_ref,
    down_ref,
    send,
    recv,
    local_sems,
    *line,
):
    rows, width = d_two.shape
    units = act_pair.shape[1]
    s, f, fx, fy, fd = plane()
    links, local = Links(send, recv), Locals(local_sems)
    core = s % 2
    mate = (s + 1 - 2 * core, f)
    tokens = 4 * rows
    near_rows, far_own = pl.ds(0, 2 * tokens - rows), pl.ds(3 * rows, rows)
    far_mate = pl.ds(2 * tokens - rows, rows)
    loads = [local.start(act_pair.at[near_rows], act_ref.at[near_rows])]
    enter([(s, fx), (s, fy), mate] + z_peers(n_seq))
    swaps = [links.start(act_pair.at[far_own], act_ref.at[far_mate], mate)]

    def store(j, value):
        down_ref[tile(j, 128)] = value.T

    def leave(j, start):
        at = tile(j, 128)
        copy = pltpu.make_async_copy(down_ref.at[at], down_out.at[at], line[4].at[j])
        start_or_wait(copy, start)

    z_sum = ZLine(part, buf, line, n_seq, 128, 3, 11, store, leave)
    block = z_sum.block
    tiles_in = [
        local.start(cot_half.at[:, at], cot_ref.at[:, at])
        for at in (tile(z_sum.nth(i), block) for i in range(z_sum.nz))
    ]
    wait_all(loads, tiles_in[:1])
    swaps[0].wait_recv()
    swaps += [
        links.start(src.at[far_own], dst.at[far_mate], mate)
        for src, dst in ((gate_pair, gate_ref), (up_pair, up_ref))
    ]
    loads = [
        local.start(src, dst)
        for src, dst in (
            (w_gate, wg),
            (w_up, wu),
            (gate_pair.at[near_rows], gate_ref.at[near_rows]),
            (up_pair.at[near_rows], up_ref.at[near_rows]),
            (two_half, two_ref),
        )
    ]

    def down_tile(i, _):
        t = z_sum.nth(i)
        part[z_sum.rows(t)] = mm_tokens(cot_ref[:, tile(t, block)], act_ref[...]).astype(BF16)
        return 0

    down_tile(jnp.int32(0), 0)
    z_sum.feed_first()
    wait_all(tiles_in[1:])
    lax.fori_loop(1, z_sum.nz, down_tile, 0)
    wait_all(loads)
    for copy in swaps[1:]:
        copy.wait_recv()

    def two_part(first, slots, base):
        at = slice(first * rows, (first + slots) * rows)

        def tile_of(n, _):
            cols = tile(n, 512)
            total = mm_t(gate_ref[at], wg[cols]) + mm_t(up_ref[at], wu[cols])
            rows_part[at, cols] = total.astype(BF16)
            z_sum.feed(base + n + z_sum.ahead)
            z_sum.serve(base + n)
            return 0

        lax.fori_loop(0, width // 512, tile_of, 0)

    count = width // 512
    two_part(3, 1, 0)
    far = reduce_start_far(links, rows_part, from_x, from_y, rows, s, fx, fy)
    two_part(1, 2, count)
    near = reduce_start_near(links, rows_part, from_x, from_y, rows, s, fx, fy)
    two_part(0, 1, 2 * count)
    served = 3 * count

    def pair_tiles(right, first, base):
        def tile_of(t, _):
            pair_ref[z_sum.rows(t), pl.ds(first, units)] = mm_tokens(
                two_ref[:, tile(t, block)], right[...]
            ).astype(BF16)
            z_sum.serve_range(base + 2 * t, base + 2 * t + 2, True)
            return 0

        lax.fori_loop(0, z_sum.nz, tile_of, 0)

    pair_tiles(gate_ref, 0, served)
    served += 2 * z_sum.nz
    passed = reduce_pass(links, far, rows_part, from_x, from_y, pass_x, pass_y, rows, s, fx, fy)
    pair_tiles(up_ref, units, served)
    served += 2 * z_sum.nz
    stay = local.start(pair_ref, pair_part)
    for copy in near + passed:
        copy.wait_recv()
    half = rows // 2
    d_two[:half] = rows_part[:half].astype(F32) + from_x[1].astype(F32) + from_y[2].astype(F32)
    d_two[half:] = rows_part[half:rows].astype(F32) + from_y[1].astype(F32) + from_x[2].astype(F32)
    early = local.start(d_two, d_two_out)
    z_sum.serve_range(served, z_sum.calls, True)
    z_sum.drain()
    sends_done(swaps, far, near, passed)
    wait_all([stay, early])


def down_sum(cot_half, act_pair, two_half, gate_pair, up_pair, w_gate, w_up, collective_id):
    n_seq = lax.axis_size("seq")
    tokens, units = act_pair.shape
    width = w_gate.shape[0]
    rows = tokens // 8
    half = (rows // 2, width)
    own = cot_half.shape[1]
    block = width // n_seq
    shape = jax.ShapeDtypeStruct
    return pl.pallas_call(
        functools.partial(down_kernel, n_seq),
        out_shape=(
            shape((rows, width), F32),
            shape((own, 2 * units), BF16),
            shape((units, block), F32),
        ),
        in_specs=[ANY] * 7,
        out_specs=(ANY, ANY, ANY),
        scratch_shapes=[
            pltpu.VMEM((rows, width), F32),
            pltpu.VMEM((tokens, own), BF16),
            pltpu.VMEM((tokens, units), BF16),
            pltpu.VMEM((tokens, own), BF16),
            pltpu.VMEM((tokens, units), BF16),
            pltpu.VMEM((tokens, units), BF16),
            pltpu.VMEM((width, units), BF16),
            pltpu.VMEM((width, units), BF16),
            pltpu.VMEM((own, units), BF16),
            pltpu.VMEM((own + block, units), BF16),
            pltpu.VMEM((tokens // 2, width), BF16),
            pltpu.VMEM((3,) + half, BF16),
            pltpu.VMEM((3,) + half, BF16),
            pltpu.VMEM(half, BF16),
            pltpu.VMEM(half, BF16),
            pltpu.VMEM((own, 2 * units), BF16),
            pltpu.VMEM((units, block), F32),
            pltpu.SemaphoreType.DMA((9,)),
            pltpu.SemaphoreType.DMA((9,)),
            pltpu.SemaphoreType.DMA((8 + n_seq // 2,)),
        ]
        + line_sems(n_seq, units, 128),
        compiler_params=params(collective_id),
        name="down_sum",
    )(cot_half, act_pair, two_half, gate_pair, up_pair, w_gate, w_up)


class TotalsFromAbove:
    def __init__(self, total, gathered, send, recv, n_seq):
        self.total, self.gathered, self.send, self.recv = total, gathered, send, recv
        self.s, self.f = lax.axis_index("seq"), lax.axis_index("fsdp")
        self.nz = n_seq // 2
        self.z, self.core = self.s // 2, self.s % 2
        self.mate = (2 * self.z + 1 - self.core, self.f)

    def down(self, sender, target):
        return remote(
            self.total,
            self.gathered.at[2 * sender + self.core],
            self.send.at[target],
            self.recv.at[2 * sender + self.core],
            (2 * target + self.core, self.f),
        )

    def across(self, sender, core):
        slot = 2 * sender + core
        return remote(
            self.gathered.at[slot],
            self.gathered.at[slot],
            self.send.at[self.nz + sender],
            self.recv.at[slot],
            self.mate,
        )

    def to_mate(self, core):
        slot = 2 * self.z + core
        return remote(
            self.total,
            self.gathered.at[slot],
            self.send.at[2 * self.nz],
            self.recv.at[slot],
            self.mate,
        )

    def start(self):
        self.to_mate(self.core).start()
        for target in range(self.nz - 1):

            @pl.when(target < self.z)
            def _():
                self.down(self.z, target).start()

    def relay(self):
        for sender in range(1, self.nz):

            @pl.when(sender > self.z)
            def _():
                self.down(sender, self.z).wait_recv()
                self.across(sender, self.core).start()

    def wait(self):
        self.to_mate(1 - self.core).wait_recv()
        for sender in range(1, self.nz):

            @pl.when(sender > self.z)
            def _():
                self.across(sender, 1 - self.core).wait_recv()

    def drain(self):
        self.to_mate(self.core).wait_send()
        for z in range(self.nz):

            @pl.when(z < self.z)
            def _():
                self.down(self.z, z).wait_send()

            @pl.when(z > self.z)
            def _():
                self.across(z, self.core).wait_send()


def pair_kernel(
    n_seq,
    lengths,
    hidden,
    cot,
    glu_gain,
    gate_gain,
    table,
    scale_g,
    d_two,
    middle,
    pair_part,
    w_out,
    w_in,
    w_fg,
    w_gt,
    gate_raw,
    state_b,
    out_raw,
    in_raw,
    fg_raw,
    before_in,
    normed_half,
    pair_grad,
    mixer_part,
    d_normed_out,
    d_middle_out,
    d_glu_gain,
    d_gain,
    d_bounds,
    d_normed,
    d_middle,
    pair_ref,
    part,
    buf,
    wo,
    wv,
    mixed_all,
    mixed_mate,
    normed_ref,
    d_proj,
    out_gate,
    gate_ref,
    state_ref,
    raw_ref,
    in_ref,
    fg_ref,
    before,
    p_ref,
    q_ref,
    stage,
    rows_part,
    from_x,
    from_y,
    pass_x,
    pass_y,
    dots,
    keep_ref,
    end_p,
    end_s,
    carr,
    total,
    gathered,
    send,
    recv,
    exchange_send,
    exchange_recv,
    local_sems,
    tile_sems,
    *line,
):
    rows, width = hidden.shape
    chans = w_in.shape[1]
    tokens = 4 * rows
    lanes_of = [slice(c, c + 128) for c in range(0, chans, 128)]
    count = len(lanes_of)
    blocks = 4 * count
    step_len = rows // 8
    s, f, fx, fy, fd = plane()
    groups = [f, fx, fy, fd]
    core = s % 2
    mate = (s + 1 - 2 * core, f)
    links, local = Links(send, recv), Locals(local_sems)

    def store(j, value):
        pair_ref[:, tile(j, 256)] = value

    def leave(j, start):
        at = tile(j, 256)
        copy = pltpu.make_async_copy(pair_ref.at[:, at], pair_grad.at[:, at], line[4].at[j])
        start_or_wait(copy, start)

    z_sum = ZLine(part, buf, line, n_seq, 256, 2, 7, store, leave)
    blocks_in = z_sum.load(local, pair_part, 0, 1)
    rows_in = [local.start(d_two, d_middle), local.start(middle, d_normed)]
    enter([(s, fx), (s, fy), (s, fd)] + seq_peers(n_seq))
    blocks_in[0].wait()
    z_sum.feed_first()
    blocks_in = z_sum.load(local, pair_part, 1, z_sum.nz)
    loads = [local.start(w_out, wo)]
    loads += [
        local.start(src, dst)
        for src, dst in (
            (gate_raw, gate_ref),
            (state_b, state_ref),
            (out_raw, raw_ref),
            (in_raw, in_ref),
            (fg_raw, fg_ref),
            (before_in, before),
        )
    ]
    weights = [
        local.start(w, wv.at[:, pl.ds(i * chans, chans)]) for i, w in enumerate((w_in, w_fg, w_gt))
    ]
    weights.append(local.start(normed_half, normed_ref))
    served = 0

    def serve(number):
        nonlocal served
        z_sum.serve_range(served, served + number)
        served += number

    d_glu_gain[...] = jnp.zeros_like(d_glu_gain)
    wait_all(rows_in, blocks_in)

    def middle_rows(i, _):
        at = pl.ds(pl.multiple_of(i * 16, 16), 16)
        value, came = d_normed[at], d_middle[at]
        scale = lax.rsqrt(jnp.mean(value * value, -1, keepdims=True) + epsilon)
        scaled = glu_gain[...] * came
        mean = jnp.mean(scaled * value, -1, keepdims=True)
        grad = cot[at].astype(F32) + scale * scaled - value * (scale**3 * mean)
        d_middle[at] = grad
        grad_b = grad.astype(BF16)
        mixed_all[at] = grad_b
        own_dot = jnp.sum(
            grad_b.astype(F32) * (value - hidden[at].astype(F32)), -1, keepdims=True
        )
        dots[0, at] = jnp.broadcast_to(own_dot, (16, 128))
        d_glu_gain[...] += jnp.sum(came * value * scale, 0, keepdims=True)
        return 0

    lax.fori_loop(0, rows // 16, middle_rows, 0)
    outs = [local.start(d_middle, d_middle_out)]
    own = gather_start(links, mixed_all, mixed_all, rows, s, fx, fy)
    dot_copies = [
        links.start(dots.at[0], dots.at[k], (s, peer)) for k, peer in ((1, fx), (2, fy), (3, fd))
    ]
    bound = bounds_slice(table, f * chans, chans)
    for k in range(4):
        keep_ref[k] = keep_rows(lengths, groups[k], s * rows, rows)
    d_gain[...] = jnp.zeros_like(d_gain)
    serve(1)
    for copy in loads:
        copy.wait()

    def out_rows(first, slots):
        stage[: slots * rows] = mm_t(mixed_all[first * rows : (first + slots) * rows], wo[...])
        for i in range(slots):
            k = first + i
            scale = scale_g[k]
            for c, lanes in enumerate(lanes_of):
                n = k * count + c
                gain = gate_gain[:, pl.ds(pl.multiple_of(f * chans + c * 128, 128), 128)]
                d_out = stage[i * rows : (i + 1) * rows, lanes]
                gate = gate_ref[k, :, lanes]
                sigma = jax.nn.sigmoid(gate)
                silu = gate * sigma
                state = state_ref[k, :, lanes].astype(F32)
                weighed = d_out * (state * scale)
                d_gain[:, lanes] += jnp.sum(weighed * silu, 0, keepdims=True)
                at = slice(k * rows, (k + 1) * rows)
                d_proj[at, 2 * chans + c * 128 : 2 * chans + (c + 1) * 128] = (
                    weighed * gain * silu_slope(gate, sigma)
                ).astype(BF16)
                out_gate[at, lanes] = (raw_ref[at, lanes].astype(F32) * scale).astype(BF16)
                d_state = scale * (d_out * gain * silu) - state * (
                    scale * scale * (dots[k] / width)
                )
                q_ref[n] = d_state.astype(BF16).astype(F32)
                edge = bound[:, lanes]
                forget = edge + (1.0 - edge) * jax.nn.sigmoid(fg_ref[k, :, lanes].astype(F32))
                p_ref[n] = forget * keep_ref[k]

    out_rows(0, 1)
    later = gather_forward(links, own, mixed_all, rows, s, fx, fy)
    serve(2)
    gather_middle(own)
    for copy in dot_copies:
        copy.wait_recv()
    out_rows(1, 2)
    serve(3)
    gather_far(later)
    out_rows(3, 1)
    serve(2)
    own_rows, mate_rows = pl.ds(0, tokens), pl.ds(tokens, tokens)
    last = pl.ds(2 * chans, chans)
    swaps = [
        links.start(out_gate.at[own_rows], out_gate.at[mate_rows], mate),
        links.start(d_proj.at[own_rows, last], d_proj.at[mate_rows, last], mate),
    ]
    wide = z_sum.block
    for t in range(n_seq // 2):
        theirs = pl.ds(pl.multiple_of((2 * t + 1 - core) * wide, wide), wide)
        swaps.append(
            links.start(mixed_all.at[:, theirs], mixed_mate.at[:, pl.ds(t * wide, wide)], mate)
        )

    def scan_step(i, carry):
        new = []
        at = pl.ds(step_len - 1 - i, 8, stride=step_len)
        for n, (product, message) in enumerate(carry):
            a = p_ref[n, at, :]
            acc = q_ref[n, at, :] + message
            p_ref[n, at, :] = product
            q_ref[n, at, :] = acc
            new.append((product * a, a * acc))
        return tuple(new)

    start = tuple((jnp.ones((8, 128), F32), jnp.zeros((8, 128), F32)) for _ in range(blocks))
    ends = lax.fori_loop(0, step_len, scan_step, start)
    for n, (product, message) in enumerate(ends):
        end_p[8 * n : 8 * n + 8] = product
        end_s[8 * n : 8 * n + 8] = message
    p_all, s_all = segment_totals(end_p, end_s, blocks, range(7, -1, -1))
    total[:blocks] = p_all
    total[blocks:] = s_all
    above = TotalsFromAbove(total, gathered, exchange_send, exchange_recv, n_seq)
    above.start()
    serve(1)
    above.relay()
    serve(1)
    above.wait()
    carry = jnp.zeros((blocks, 128), F32)
    for j in range(n_seq - 1, 0, -1):
        carry = jnp.where(j > s, gathered[j, blocks:] + gathered[j, :blocks] * carry, carry)
    spread_carry(carry, carr, end_p, end_s, blocks, range(7, -1, -1))

    def finish(n, _):
        enter_state = carr[pl.ds(pl.multiple_of(n * 8, 8), 8)]
        for i in range(step_len):
            at = pl.ds(i, 8, stride=step_len)
            q_ref[n, at, :] = q_ref[n, at, :] + p_ref[n, at, :] * enter_state
        return 0

    lax.fori_loop(0, blocks, finish, 0)
    d_bounds[...] = jnp.zeros_like(d_bounds)
    for k in range(4):
        at = slice(k * rows, (k + 1) * rows)
        for c, lanes in enumerate(lanes_of):
            acc = q_ref[k * count + c]
            edge = bound[:, lanes]
            sigma_f = jax.nn.sigmoid(fg_ref[k, :, lanes].astype(F32))
            forget = edge + (1.0 - edge) * sigma_f
            value = in_ref[k, :, lanes].astype(F32)
            sigma_i = jax.nn.sigmoid(value)
            d_forget = acc * (before[k * count + c] * keep_ref[k] - value * sigma_i)
            d_proj[at, lanes] = (acc * (1.0 - forget) * silu_slope(value, sigma_i)).astype(BF16)
            d_sigma = d_forget * (1.0 - sigma_f)
            d_proj[at, chans + c * 128 : chans + (c + 1) * 128] = (
                d_sigma * (1.0 - edge) * sigma_f
            ).astype(BF16)
            d_bounds[:, lanes] += jnp.sum(d_sigma, 0, keepdims=True)
    first = pl.ds(0, 2 * chans)
    swaps.append(links.start(d_proj.at[own_rows, first], d_proj.at[mate_rows, first], mate))
    serve(2)
    for copy in weights:
        copy.wait()

    def normed_part(first_slot, slots):
        at = slice(first_slot * rows, (first_slot + slots) * rows)

        def tile_of(n, _):
            cols = tile(n, 512)
            rows_part[at, cols] = mm_t(d_proj[at], wv[cols]).astype(BF16)
            return 0

        lax.fori_loop(0, width // 512, tile_of, 0)

    normed_part(3, 1)
    far = reduce_start_far(links, rows_part, from_x, from_y, rows, s, fx, fy)
    normed_part(1, 2)
    near = reduce_start_near(links, rows_part, from_x, from_y, rows, s, fx, fy)
    normed_part(0, 1)
    serve(3)
    for copy in swaps:
        copy.wait_recv()

    def tile_out(t):
        slot = lax.rem(t, 2)
        return pltpu.make_async_copy(
            wo.at[tile(slot, wide)], mixer_part.at[z_sum.rows(t)], tile_sems.at[slot]
        )

    def mixer_tile(t, _):
        @pl.when(t >= 2)
        def _():
            tile_out(t - 2).wait()

        at = tile(lax.rem(t, 2), wide)
        ours = mixed_all[:, tile(2 * t + core, wide)]
        out_part = mm_tokens(ours, out_gate[:tokens])
        out_part = out_part + mm_tokens(mixed_mate[:, tile(t, wide)], out_gate[tokens:])
        wo[at, :chans] = out_part.astype(BF16)
        wo[at, chans:] = mm_tokens(normed_ref[:, tile(t, wide)], d_proj[...]).astype(BF16)
        tile_out(t).start()
        return 0

    lax.fori_loop(0, 1, mixer_tile, 0)
    passed = reduce_pass(links, far, rows_part, from_x, from_y, pass_x, pass_y, rows, s, fx, fy)
    serve(1)
    lax.fori_loop(1, z_sum.nz, mixer_tile, 0)
    serve(2)
    for copy in near + passed:
        copy.wait_recv()
    half = rows // 2
    d_normed[:half] = rows_part[:half].astype(F32) + from_x[1].astype(F32) + from_y[2].astype(F32)
    d_normed[half:] = (
        rows_part[half:rows].astype(F32) + from_y[1].astype(F32) + from_x[2].astype(F32)
    )
    outs.append(local.start(d_normed, d_normed_out))
    z_sum.serve_range(served, z_sum.calls, True)
    z_sum.drain()
    above.drain()
    sends_done(own, later, dot_copies, swaps, far, near, passed)
    for t in range(z_sum.nz - 2, z_sum.nz):
        tile_out(jnp.int32(t)).wait()
    wait_all(outs)


def pair_sum(
    lengths, own_rows, gains, table, scale_g, float_rows, pair_part, weights, saved, normed_half, cid
):
    n_seq = lax.axis_size("seq")
    rows, width = own_rows[0].shape
    chans = weights[1].shape[1]
    own, columns = pair_part.shape
    tokens = 4 * rows
    blocks = 4 * chans // 128
    block = width // n_seq
    half = (rows // 2, width)
    shape = jax.ShapeDtypeStruct
    count = 18 + n_seq // 2
    return pl.pallas_call(
        functools.partial(pair_kernel, n_seq),
        out_shape=(
            shape((block, columns), F32),
            shape((own, 4 * chans), BF16),
            shape((rows, width), F32),
            shape((rows, width), F32),
            shape((1, width), F32),
            shape((1, chans), F32),
            shape((1, chans), F32),
        ),
        in_specs=[pl.BlockSpec(memory_space=pltpu.SMEM)] + [VMEM] * 6 + [ANY] * 14,
        out_specs=(ANY,) * 4 + (VMEM,) * 3,
        scratch_shapes=[
            pltpu.VMEM((rows, width), F32),
            pltpu.VMEM((rows, width), F32),
            pltpu.VMEM((block, columns), F32),
            pltpu.VMEM((own, columns), BF16),
            pltpu.VMEM((own + block, columns), BF16),
            pltpu.VMEM((chans, width), BF16),
            pltpu.VMEM((width, 3 * chans), BF16),
            pltpu.VMEM((tokens, width), BF16),
            pltpu.VMEM((tokens, width // 2), BF16),
            pltpu.VMEM((2 * tokens, width // 2), BF16),
            pltpu.VMEM((2 * tokens, 3 * chans), BF16),
            pltpu.VMEM((2 * tokens, chans), BF16),
            pltpu.VMEM((4, rows, chans), F32),
            pltpu.VMEM((4, rows, chans), BF16),
            pltpu.VMEM((tokens, chans), BF16),
            pltpu.VMEM((4, rows, chans), BF16),
            pltpu.VMEM((4, rows, chans), BF16),
            pltpu.VMEM((blocks, rows, 128), F32),
            pltpu.VMEM((blocks, rows, 128), F32),
            pltpu.VMEM((blocks, rows, 128), F32),
            pltpu.VMEM((2 * rows, chans), F32),
            pltpu.VMEM((tokens, width), BF16),
            pltpu.VMEM((3,) + half, BF16),
            pltpu.VMEM((3,) + half, BF16),
            pltpu.VMEM(half, BF16),
            pltpu.VMEM(half, BF16),
            pltpu.VMEM((4, rows, 128), F32),
            pltpu.VMEM((4, rows, 128), F32),
            pltpu.VMEM((8 * blocks, 128), F32),
            pltpu.VMEM((8 * blocks, 128), F32),
            pltpu.VMEM((8 * blocks, 128), F32),
            pltpu.VMEM((2 * blocks, 128), F32),
            pltpu.VMEM((n_seq, 2 * blocks, 128), F32),
            pltpu.SemaphoreType.DMA((count,)),
            pltpu.SemaphoreType.DMA((count,)),
            pltpu.SemaphoreType.DMA((n_seq + 1,)),
            pltpu.SemaphoreType.DMA((n_seq,)),
            pltpu.SemaphoreType.DMA((15 + n_seq // 2,)),
            pltpu.SemaphoreType.DMA((2,)),
        ]
        + line_sems(n_seq, columns, 256),
        compiler_params=params(cid),
        name="pair_sum",
    )(
        lengths,
        *own_rows,
        *gains,
        table,
        scale_g,
        *float_rows,
        pair_part,
        *weights,
        *saved,
        normed_half,
    )


def final_kernel(
    n_seq,
    n_fsdp,
    hidden,
    norm_gain,
    d_glu_gain,
    d_gain,
    d_bounds,
    table,
    d_normed_in,
    d_middle_in,
    middle_in,
    mixer_part,
    act_pair,
    w_down,
    output_out,
    d_hidden_out,
    out_grad,
    rest_grad,
    norm_out,
    glu_out,
    gate_out,
    d_table,
    d_normed,
    d_middle,
    middle,
    output,
    d_hidden,
    out_ref,
    rest_ref,
    part,
    buf,
    act,
    wd,
    rows_part,
    from_x,
    from_y,
    pass_x,
    pass_y,
    norm_sum,
    bounds_out,
    terms,
    quarters_in,
    terms_q,
    from_mate,
    terms_chip,
    over_seq,
    along_sum,
    over_fsdp,
    send,
    recv,
    local_sems,
    *line,
):
    rows, width = hidden.shape
    chans = d_gain.shape[1]
    tokens = 4 * rows
    s, f, fx, fy, fd = plane()
    links, local = Links(send, recv), Locals(local_sems)
    head = chans // 256

    def store(j, value):
        @pl.when(j < head)
        def _():
            out_ref[tile(j, 256)] = value.T

        @pl.when(j >= head)
        def _():
            rest_ref[:, tile(j - head, 256)] = value

    def leave(j, start):
        @pl.when(j < head)
        def _():
            at = tile(j, 256)
            copy = pltpu.make_async_copy(out_ref.at[at], out_grad.at[at], line[4].at[j])
            start_or_wait(copy, start)

        @pl.when(j >= head)
        def _():
            at = tile(j - head, 256)
            copy = pltpu.make_async_copy(rest_ref.at[:, at], rest_grad.at[:, at], line[4].at[j])
            start_or_wait(copy, start)

    z_sum = ZLine(part, buf, line, n_seq, 256, 2, 6, store, leave)
    blocks_in = z_sum.load(local, mixer_part, 0, 1)
    along = seq_peers(n_seq)
    across = [(s, fx), (s, fy), (s, fd)]
    enter(across + along)
    blocks_in[0].wait()
    z_sum.feed_first()
    loads = [local.start(act_pair.at[pl.ds(0, tokens)], act), local.start(w_down, wd)]
    blocks_in = z_sum.load(local, mixer_part, 1, z_sum.nz)
    rows_in = [
        local.start(src, dst)
        for src, dst in ((d_normed_in, d_normed), (d_middle_in, d_middle), (middle_in, middle))
    ]
    served = 0

    def serve(number):
        nonlocal served
        z_sum.serve_range(served, served + number)
        served += number

    norm_sum[...] = jnp.zeros_like(norm_sum)

    def hidden_rows(i, _):
        at = pl.ds(pl.multiple_of(i * 16, 16), 16)
        value, came = hidden[at].astype(F32), d_normed[at]
        scale = lax.rsqrt(jnp.mean(value * value, -1, keepdims=True) + epsilon)
        scaled = norm_gain[...] * came
        mean = jnp.mean(scaled * value, -1, keepdims=True)
        d_hidden[at] = (d_middle[at] + scale * scaled - value * (scale**3 * mean)).astype(BF16)
        norm_sum[...] += jnp.sum(came * value * scale, 0, keepdims=True)
        return 0

    wait_all(loads)

    def glu_part(first, slots):
        at = slice(first * rows, (first + slots) * rows)

        def tile_of(n, _):
            cols = tile(n, 512)
            rows_part[at, cols] = mm(act[at], wd[:, cols]).astype(BF16)
            return 0

        lax.fori_loop(0, width // 512, tile_of, 0)

    glu_part(3, 1)
    far = reduce_start_far(links, rows_part, from_x, from_y, rows, s, fx, fy)
    glu_part(1, 2)
    near = reduce_start_near(links, rows_part, from_x, from_y, rows, s, fx, fy)
    glu_part(0, 1)
    wait_all(blocks_in, rows_in)
    serve(2)
    lax.fori_loop(0, rows // 16, hidden_rows, 0)
    terms[...] = jnp.zeros_like(terms)
    for q in range(4):
        terms[q, 0:1] = norm_sum[:, q * chans : (q + 1) * chans]
        terms[q, 1:2] = d_glu_gain[:, q * chans : (q + 1) * chans]
    quarter_copies = [
        links.start(terms.at[peer], quarters_in.at[k], (s, peer))
        for k, peer in enumerate((fx, fy, fd))
    ]
    serve(1)
    passed = reduce_pass(links, far, rows_part, from_x, from_y, pass_x, pass_y, rows, s, fx, fy)
    serve(2)
    quarter = terms[pl.ds(f, 1)][0]
    for k, copy in enumerate(quarter_copies):
        copy.wait_recv()
        quarter = quarter + quarters_in[k]
    half = chans // 2
    for first, cols in ((0, slice(0, half)), (4, slice(half, chans))):
        terms_q[first : first + 2] = quarter[:2, cols]
        terms_q[first + 2 : first + 3] = d_gain[:, cols]
        terms_q[first + 3 : first + 4] = d_bounds[:, cols]
    mate_copy = links.start(terms_q, from_mate, (s + 1 - 2 * (s % 2), f))
    serve(1)
    serve(2)
    for copy in near + passed:
        copy.wait_recv()
    middle_half = rows // 2
    for first, one, other in (
        (0, from_x.at[1], from_y.at[2]),
        (middle_half, from_y.at[1], from_x.at[2]),
    ):
        at = slice(first, first + middle_half)
        added = rows_part[at].astype(F32) + one[...].astype(F32) + other[...].astype(F32)
        output[at] = (middle[at] + added).astype(BF16)
    mate_copy.wait_recv()
    terms_chip[...] = terms_q[...] + from_mate[...]
    seq_copies = [
        links.start(terms_chip, over_seq.at[k], peer) for k, peer in enumerate(z_peers(n_seq))
    ]
    serve(2)
    total = terms_chip[...]
    for k, copy in enumerate(seq_copies):
        copy.wait_recv()
        total = total + over_seq[k]
    along_sum[...] = total
    fsdp_copies = [links.start(along_sum, over_fsdp.at[k], peer) for k, peer in enumerate(across)]
    serve(2)
    for copy in fsdp_copies:
        copy.wait_recv()
    for k, group in enumerate((f, fx, fy, fd)):
        total = along_sum[...] if k == 0 else over_fsdp[k - 1]
        for i in range(2):
            at = pl.ds(pl.multiple_of(group * chans + i * half, 128), half)
            for r, out in enumerate((norm_out, glu_out, gate_out, bounds_out)):
                out[:, at] = total[4 * i + r : 4 * i + r + 1]
    powers = jnp.exp(table[...] - jnp.max(table[...], 0, keepdims=True))
    soft = powers / jnp.sum(powers, 0, keepdims=True)
    row = lax.broadcasted_iota(jnp.int32, soft.shape, 0)
    chosen = jnp.where((row >= 1) & (row <= LAYER), 1.0, 0.0)
    bound = jnp.sum(soft * chosen, 0, keepdims=True)
    d_table[...] = soft * (chosen - bound) * bounds_out[...]
    outs = [local.start(output, output_out), local.start(d_hidden, d_hidden_out)]
    z_sum.serve_range(served, z_sum.calls, True)
    z_sum.drain()
    wait_all(outs)
    sends_done(far, near, passed, quarter_copies, [mate_copy], seq_copies, fsdp_copies)


def final_sum(hidden, rows_in, gains, table, mixer_part, act_pair, w_down, cid):
    n_seq, n_fsdp = lax.axis_size("seq"), lax.axis_size("fsdp")
    rows, width = hidden.shape
    own, columns = mixer_part.shape
    units = w_down.shape[0]
    chans = columns // 4
    tokens = 4 * rows
    block = width // n_seq
    half = (rows // 2, width)
    terms = (8, chans // 2)
    shape = jax.ShapeDtypeStruct
    count = 6 + n_seq // 2 + 2 * (n_fsdp - 1)
    return pl.pallas_call(
        functools.partial(final_kernel, n_seq, n_fsdp),
        out_shape=(
            shape((rows, width), BF16),
            shape((rows, width), BF16),
            shape((chans, block), F32),
            shape((block, 3 * chans), F32),
            shape((1, width), F32),
            shape((1, width), F32),
            shape((1, width), F32),
            shape(table.shape, F32),
        ),
        in_specs=[VMEM] * 6 + [ANY] * 6,
        out_specs=(ANY,) * 4 + (VMEM,) * 4,
        scratch_shapes=[
            pltpu.VMEM((rows, width), F32),
            pltpu.VMEM((rows, width), F32),
            pltpu.VMEM((rows, width), F32),
            pltpu.VMEM((rows, width), BF16),
            pltpu.VMEM((rows, width), BF16),
            pltpu.VMEM((chans, block), F32),
            pltpu.VMEM((block, 3 * chans), F32),
            pltpu.VMEM((own, columns), BF16),
            pltpu.VMEM((own + block, columns), BF16),
            pltpu.VMEM((tokens, units), BF16),
            pltpu.VMEM((units, width), BF16),
            pltpu.VMEM((tokens, width), BF16),
            pltpu.VMEM((3,) + half, BF16),
            pltpu.VMEM((3,) + half, BF16),
            pltpu.VMEM(half, BF16),
            pltpu.VMEM(half, BF16),
            pltpu.VMEM((1, width), F32),
            pltpu.VMEM((1, width), F32),
            pltpu.VMEM((n_fsdp, 8, chans), F32),
            pltpu.VMEM((n_fsdp - 1, 8, chans), F32),
            pltpu.VMEM(terms, F32),
            pltpu.VMEM(terms, F32),
            pltpu.VMEM(terms, F32),
            pltpu.VMEM((n_seq // 2 - 1,) + terms, F32),
            pltpu.VMEM(terms, F32),
            pltpu.VMEM((n_fsdp - 1,) + terms, F32),
            pltpu.SemaphoreType.DMA((count,)),
            pltpu.SemaphoreType.DMA((count,)),
            pltpu.SemaphoreType.DMA((7 + n_seq // 2,)),
        ]
        + line_sems(n_seq, columns, 256),
        compiler_params=params(cid),
        name="final_sum",
    )(hidden, *gains, table, *rows_in, mixer_part, act_pair, w_down)


def hand_over_kernel(count, pieces, *refs):
    sources, targets = refs[: len(refs) - 2 * count - 2], refs[len(refs) - 2 * count - 2 :]
    kept, arrived, left = targets[count : 2 * count], targets[2 * count], targets[2 * count + 1]
    loads, stores = [], []
    for n, (i, source, first, rows, column) in enumerate(pieces):
        at = pl.ds(first, rows)
        src = sources[source].at[at, pl.ds(column, kept[i].shape[1])]
        loads.append(copy_in(src, kept[i].at[at], arrived.at[n]))
    for n, (i, source, first, rows, column) in enumerate(pieces):
        at = pl.ds(first, rows)
        loads[n].wait()
        stores.append(copy_in(kept[i].at[at], targets[i].at[at], left.at[n]))
    for store in stores:
        store.wait()


def hand_over(arrays, wanted):
    pieces, shapes = [], []
    for i, (source, column, columns) in enumerate(wanted):
        x = arrays[source]
        height = x.shape[0]
        parts = max(1, height * columns * x.dtype.itemsize >> 18)
        parts = parts if height % (parts * 16) == 0 else 1
        rows = height // parts
        pieces += [(i, source, n * rows, rows, column) for n in range(parts)]
        shapes.append(((height, columns), x.dtype))
    return pl.pallas_call(
        functools.partial(hand_over_kernel, len(wanted), tuple(pieces)),
        out_shape=tuple(jax.ShapeDtypeStruct(*x) for x in shapes),
        in_specs=[ANY] * len(arrays),
        out_specs=(ANY,) * len(wanted),
        scratch_shapes=[pltpu.VMEM(*x) for x in shapes]
        + [pltpu.SemaphoreType.DMA((len(pieces),))] * 2,
        compiler_params=pltpu.CompilerParams(vmem_limit_bytes=56 << 20),
        name="hand_over",
    )(*arrays)


def plane_device(
    hidden,
    lengths,
    w_input,
    w_forget,
    w_gate_out,
    w_output,
    norm_gain,
    gate_gain,
    glu_gain,
    lower_table,
    w_glu_gate,
    w_glu_up,
    w_glu_down,
    cotangent,
):
    hidden, cotangent = hidden[0], cotangent[0]
    tokens = 4 * hidden.shape[0]
    gains = (norm_gain[None], gate_gain[None], glu_gain[None])
    (
        normed_half,
        cot_all,
        in_raw,
        fg_raw,
        gate_raw,
        state_b,
        out_raw,
        before,
        scale_g,
        middle,
        normed_two,
    ) = mixer_forward(
        lengths,
        hidden,
        cotangent,
        gains,
        lower_table,
        (w_input, w_forget, w_gate_out, w_output),
        0,
    )
    two_half, cot_half, act_pair, gate_pair, up_pair = glu(
        normed_two, cot_all, w_glu_gate, w_glu_up, w_glu_down, 1
    )
    d_normed_two, pair_part, down_grad = down_sum(
        *(x.reshape(2 * tokens, -1) for x in (cot_half, act_pair, two_half, gate_pair, up_pair)),
        w_glu_gate,
        w_glu_up,
        2,
    )
    pair_grad, mixer_part, d_normed, d_middle, d_glu_gain, d_gain, d_bounds = pair_sum(
        lengths,
        (hidden, cotangent),
        (gains[2], gains[1]),
        lower_table,
        scale_g,
        (d_normed_two, middle),
        pair_part,
        (w_output, w_input, w_forget, w_gate_out),
        (gate_raw, state_b, out_raw, in_raw, fg_raw, before),
        normed_half.reshape(2 * tokens, -1),
        3,
    )
    output, d_hidden, out_grad, rest_grad, *sums, d_table = final_sum(
        hidden,
        (d_normed, d_middle, middle),
        (gains[0], d_glu_gain, d_gain, d_bounds),
        lower_table,
        mixer_part,
        act_pair.reshape(2 * tokens, -1),
        w_glu_down,
        4,
    )
    width, chans, units = hidden.shape[1], w_input.shape[1], w_glu_gate.shape[1]
    block = down_grad.shape[1]
    (
        down_grad,
        gate_grad,
        up_grad,
        output,
        d_hidden,
        d_table,
        out_grad,
        in_grad,
        fg_grad,
        gt_grad,
        *sums,
    ) = hand_over(
        (down_grad, pair_grad, output, d_hidden, d_table, out_grad, rest_grad, *sums),
        (
            (0, 0, block),
            (1, 0, units),
            (1, units, units),
            (2, 0, width),
            (3, 0, width),
            (4, 0, width),
            (5, 0, block),
            (6, 0, chans),
            (6, chans, chans),
            (6, 2 * chans, chans),
            (7, 0, width),
            (8, 0, width),
            (9, 0, width),
        ),
    )
    return (
        output[None],
        d_hidden[None],
        in_grad,
        fg_grad,
        gt_grad,
        out_grad,
        sums[0][0],
        sums[2][0],
        sums[1][0],
        d_table,
        gate_grad,
        up_grad,
        down_grad,
    )


def fits_plane(mesh):
    return mesh.shape["fsdp"] == 4 and mesh.shape["seq"] % 2 == 0


def solution(mesh):
    rows_spec = P("fsdp", "seq", None)
    columns = P(None, "fsdp")
    placed = (
        rows_spec,
        P(),
        columns,
        columns,
        columns,
        P("fsdp", None),
        P(),
        P(),
        P(),
        P(),
        columns,
        columns,
        P("fsdp", None),
        rows_spec,
    )
    by_rows, by_columns = P("seq", "fsdp"), P("fsdp", "seq")
    return jax.shard_map(
        plane_device if fits_plane(mesh) else per_device,
        mesh=mesh,
        in_specs=placed,
        out_specs=(
            rows_spec,
            rows_spec,
            by_rows,
            by_rows,
            by_rows,
            by_columns,
            P(),
            P(),
            P(),
            P(),
            by_rows,
            by_rows,
            by_columns,
        ),
        check_vma=False,
    )
```

```python
import functools

import jax
import jax.numpy as jnp
from jax import lax
from jax.experimental import pallas as pl
from jax.experimental.pallas import tpu as pltpu
from jax.sharding import PartitionSpec as P

LAYER = 12
MESH = pl.DeviceIdType.MESH
F32 = jnp.float32
BF16 = jnp.bfloat16

epsilon = 1e-06

VMEM = pl.BlockSpec(memory_space=pltpu.VMEM)
ANY = pl.BlockSpec(memory_space=pl.ANY)


def lower_bound(table):
    soft = jax.nn.softmax(table, axis=0)
    totals = jnp.cumsum(soft, axis=0)
    return totals[LAYER] - totals[0]


def silu_slope(value, sigma):
    return sigma * (1.0 + value * (1.0 - sigma))


def params(collective_id, limit=56):
    return pltpu.CompilerParams(
        collective_id=collective_id, has_side_effects=True, vmem_limit_bytes=limit << 20
    )


def round_up(value, unit):
    return -(-value // unit) * unit


def plane():
    s = lax.axis_index("seq")
    f = lax.axis_index("fsdp")
    y, x = f // 2, f % 2
    fx = y * 2 + (1 - x)
    fy = (1 - y) * 2 + x
    fd = (1 - y) * 2 + (1 - x)
    return s, f, fx, fy, fd


def enter(devices):
    barrier = pltpu.get_barrier_semaphore()
    for device in devices:
        pl.semaphore_signal(barrier, inc=1, device_id=device, device_id_type=MESH)
    pl.semaphore_wait(barrier, len(devices))


def remote(src, dst, send, recv, device):
    return pltpu.make_async_remote_copy(
        src_ref=src,
        dst_ref=dst,
        send_sem=send,
        recv_sem=recv,
        device_id=device,
        device_id_type=MESH,
    )


def gather(x, small, collective_id):
    return lax.all_gather(x, "fsdp"), lax.all_gather(small, "fsdp")


def reduce_rows(p, small, collective_id):
    total = lax.psum_scatter(p, "fsdp", scatter_dimension=0, tiled=True)[0]
    return total.astype(F32), lax.psum(small, "fsdp")


def start_exchange(total, gathered, send, recv, n_seq):
    s = lax.axis_index("seq")
    f = lax.axis_index("fsdp")
    copies = []
    for k in range(1, n_seq):
        peer = lax.rem(s + k, n_seq)
        copy = remote(total, gathered.at[s], send.at[k], recv.at[k], (peer, f))
        copy.start()
        copies.append(copy)
    gathered[pl.ds(s, 1)] = total[...][None]
    return copies


def seq_peers(n_seq):
    s = lax.axis_index("seq")
    f = lax.axis_index("fsdp")
    return [(lax.rem(s + k, n_seq), f) for k in range(1, n_seq)]


def lane_blocks(groups, chans):
    return [(g, slice(c, c + 128)) for g in range(groups) for c in range(0, chans, 128)]


def forward_scan_kernel(
    n_seq, in_raw, forget_raw, bounds, keep, state_b, before, a_ref, b_ref, total, gathered, send, recv
):
    groups, rows, chans = in_raw.shape
    part = rows // 8
    blocks = lane_blocks(groups, chans)
    s = lax.axis_index("seq")
    barrier = pltpu.get_barrier_semaphore()
    for peer in seq_peers(n_seq):
        pl.semaphore_signal(barrier, inc=1, device_id=peer, device_id_type=MESH)
    for n, (g, lanes) in enumerate(blocks):
        bound = bounds[:, lanes]
        forget = bound + (1.0 - bound) * jax.nn.sigmoid(forget_raw[g, :, lanes].astype(F32))
        value = in_raw[g, :, lanes].astype(F32)
        a_ref[n] = forget * keep[g]
        b_ref[n] = value * jax.nn.sigmoid(value) * (1.0 - forget)

    def step(i, carry):
        new = []
        at = pl.ds(i, 8, stride=part)
        for n, (product, state) in enumerate(carry):
            a = a_ref[n, at, :]
            state = a * state + b_ref[n, at, :]
            product = product * a
            a_ref[n, at, :] = product
            b_ref[n, at, :] = state
            new.append((product, state))
        return tuple(new)

    start = tuple((jnp.ones((8, 128), F32), jnp.zeros((8, 128), F32)) for _ in blocks)
    ends = lax.fori_loop(0, part, step, start)
    for n, (product, state) in enumerate(ends):
        p_all, s_all = product[0:1], state[0:1]
        for j in range(1, 8):
            p_all, s_all = p_all * product[j : j + 1], state[j : j + 1] + product[j : j + 1] * s_all
        total[2 * n : 2 * n + 1] = p_all
        total[2 * n + 1 : 2 * n + 2] = s_all
    pl.semaphore_wait(barrier, n_seq - 1)
    copies = start_exchange(total, gathered, send, recv, n_seq)
    for copy in copies:
        copy.wait()
    for n, (g, lanes) in enumerate(blocks):
        carry = jnp.zeros((1, 128), F32)
        for j in range(n_seq - 1):
            p_j = gathered[j, 2 * n : 2 * n + 1]
            s_j = gathered[j, 2 * n + 1 : 2 * n + 2]
            carry = jnp.where(j < s, s_j + p_j * carry, carry)
        before[g, 0:1, lanes] = carry
        product, state = ends[n]
        carries = [carry]
        for j in range(7):
            carries.append(state[j : j + 1] + product[j : j + 1] * carries[-1])
        for j in range(8):
            at = slice(j * part, (j + 1) * part)
            b_ref[n, at] = b_ref[n, at] + a_ref[n, at] * carries[j]
        state_b[g, :, lanes] = b_ref[n].astype(BF16)
        before[g, 1:rows, lanes] = b_ref[n, 0 : rows - 1]


def forward_scan(in_raw, forget_raw, bounds, keep, collective_id):
    n_seq = lax.axis_size("seq")
    groups, rows, chans = in_raw.shape
    blocks = groups * chans // 128
    return pl.pallas_call(
        functools.partial(forward_scan_kernel, n_seq),
        out_shape=(
            jax.ShapeDtypeStruct(in_raw.shape, BF16),
            jax.ShapeDtypeStruct(in_raw.shape, F32),
        ),
        in_specs=[VMEM] * 4,
        out_specs=(VMEM, VMEM),
        scratch_shapes=[
            pltpu.VMEM((blocks, rows, 128), F32),
            pltpu.VMEM((blocks, rows, 128), F32),
            pltpu.VMEM((2 * blocks, 128), F32),
            pltpu.VMEM((n_seq, 2 * blocks, 128), F32),
            pltpu.SemaphoreType.DMA((n_seq,)),
            pltpu.SemaphoreType.DMA((n_seq,)),
        ],
        compiler_params=params(collective_id),
        name="forward_scan",
    )(in_raw, forget_raw, bounds, keep)


def backward_scan_kernel(
    n_seq,
    d_state,
    in_raw,
    forget_raw,
    before,
    bounds,
    keep,
    d_in,
    d_forget_raw,
    d_bounds,
    p_ref,
    q_ref,
    total,
    gathered,
    send,
    recv,
):
    groups, rows, chans = in_raw.shape
    part = rows // 8
    blocks = lane_blocks(groups, chans)
    s = lax.axis_index("seq")
    barrier = pltpu.get_barrier_semaphore()
    for peer in seq_peers(n_seq):
        pl.semaphore_signal(barrier, inc=1, device_id=peer, device_id_type=MESH)
    for n, (g, lanes) in enumerate(blocks):
        bound = bounds[:, lanes]
        forget = bound + (1.0 - bound) * jax.nn.sigmoid(forget_raw[g, :, lanes].astype(F32))
        p_ref[n] = forget * keep[g]
        q_ref[n] = d_state[g, :, lanes].astype(F32)

    def step(i, carry):
        new = []
        at = pl.ds(part - 1 - i, 8, stride=part)
        for n, (product, message) in enumerate(carry):
            a = p_ref[n, at, :]
            acc = q_ref[n, at, :] + message
            p_ref[n, at, :] = product
            q_ref[n, at, :] = acc
            new.append((product * a, a * acc))
        return tuple(new)

    start = tuple((jnp.ones((8, 128), F32), jnp.zeros((8, 128), F32)) for _ in blocks)
    ends = lax.fori_loop(0, part, step, start)
    for n, (product, message) in enumerate(ends):
        p_all, m_all = product[7:8], message[7:8]
        for j in range(6, -1, -1):
            p_all, m_all = p_all * product[j : j + 1], message[j : j + 1] + product[j : j + 1] * m_all
        total[2 * n : 2 * n + 1] = p_all
        total[2 * n + 1 : 2 * n + 2] = m_all
    pl.semaphore_wait(barrier, n_seq - 1)
    copies = start_exchange(total, gathered, send, recv, n_seq)
    for copy in copies:
        copy.wait()
    d_bounds[...] = jnp.zeros((1, chans), F32)
    for n, (g, lanes) in enumerate(blocks):
        carry = jnp.zeros((1, 128), F32)
        for j in range(n_seq - 1, 0, -1):
            p_j = gathered[j, 2 * n : 2 * n + 1]
            m_j = gathered[j, 2 * n + 1 : 2 * n + 2]
            carry = jnp.where(j > s, m_j + p_j * carry, carry)
        product, message = ends[n]
        carries = [carry]
        for j in range(7, 0, -1):
            carries.append(message[j : j + 1] + product[j : j + 1] * carries[-1])
        carries = carries[::-1]
        for j in range(8):
            at = slice(j * part, (j + 1) * part)
            q_ref[n, at] = q_ref[n, at] + p_ref[n, at] * carries[j]
        acc = q_ref[n]
        bound = bounds[:, lanes]
        sigma_f = jax.nn.sigmoid(forget_raw[g, :, lanes].astype(F32))
        forget = bound + (1.0 - bound) * sigma_f
        value = in_raw[g, :, lanes].astype(F32)
        sigma_i = jax.nn.sigmoid(value)
        d_forget = acc * (before[g, :, lanes] * keep[g] - value * sigma_i)
        d_in[g, :, lanes] = (acc * (1.0 - forget) * silu_slope(value, sigma_i)).astype(BF16)
        d_sigma = d_forget * (1.0 - sigma_f)
        d_forget_raw[g, :, lanes] = (d_sigma * (1.0 - bound) * sigma_f).astype(BF16)
        d_bounds[:, lanes] += jnp.sum(d_sigma, 0, keepdims=True)


def backward_scan(d_state, in_raw, forget_raw, before, bounds, keep, collective_id):
    n_seq = lax.axis_size("seq")
    groups, rows, chans = in_raw.shape
    blocks = groups * chans // 128
    return pl.pallas_call(
        functools.partial(backward_scan_kernel, n_seq),
        out_shape=(
            jax.ShapeDtypeStruct(in_raw.shape, BF16),
            jax.ShapeDtypeStruct(in_raw.shape, BF16),
            jax.ShapeDtypeStruct((1, chans), F32),
        ),
        in_specs=[VMEM] * 6,
        out_specs=(VMEM, VMEM, VMEM),
        scratch_shapes=[
            pltpu.VMEM((blocks, rows, 128), F32),
            pltpu.VMEM((blocks, rows, 128), F32),
            pltpu.VMEM((2 * blocks, 128), F32),
            pltpu.VMEM((n_seq, 2 * blocks, 128), F32),
            pltpu.SemaphoreType.DMA((n_seq,)),
            pltpu.SemaphoreType.DMA((n_seq,)),
        ],
        compiler_params=params(collective_id),
        name="backward_scan",
    )(d_state, in_raw, forget_raw, before, bounds, keep)


def sum_all_kernel(n_seq, n_fsdp, x, out, middle, over_seq, over_fsdp, send, recv):
    s = lax.axis_index("seq")
    f = lax.axis_index("fsdp")
    along = [(lax.rem(s + k, n_seq), f) for k in range(1, n_seq)]
    across = [(s, lax.rem(f + k, n_fsdp)) for k in range(1, n_fsdp)]
    enter(along + across)
    copies = []
    for k, peer in enumerate(along):
        copy = remote(x, over_seq.at[k], send.at[k], recv.at[k], peer)
        copy.start()
        copies.append(copy)
    total = x[...]
    for k, copy in enumerate(copies):
        copy.wait_recv()
        total = total + over_seq[k]
    middle[...] = total
    later = []
    for k, peer in enumerate(across):
        slot = n_seq - 1 + k
        copy = remote(middle, over_fsdp.at[k], send.at[slot], recv.at[slot], peer)
        copy.start()
        later.append(copy)
    for k, copy in enumerate(later):
        copy.wait_recv()
        total = total + over_fsdp[k]
    out[...] = total
    for copy in copies + later:
        copy.wait_send()


def sum_all(x, collective_id):
    n_seq, n_fsdp = lax.axis_size("seq"), lax.axis_size("fsdp")
    count = n_seq + n_fsdp - 2
    return pl.pallas_call(
        functools.partial(sum_all_kernel, n_seq, n_fsdp),
        out_shape=jax.ShapeDtypeStruct(x.shape, F32),
        in_specs=[VMEM],
        out_specs=VMEM,
        scratch_shapes=[
            pltpu.VMEM(x.shape, F32),
            pltpu.VMEM((n_seq - 1,) + x.shape, F32),
            pltpu.VMEM((n_fsdp - 1,) + x.shape, F32),
            pltpu.SemaphoreType.DMA((count,)),
            pltpu.SemaphoreType.DMA((count,)),
        ],
        compiler_params=params(collective_id),
        name="sum_all",
    )(x)


def sum_over_seq(part):
    return lax.psum_scatter(part.astype(BF16), "seq", scatter_dimension=0, tiled=True).astype(F32)


def per_device(
    hidden,
    lengths,
    w_input,
    w_forget,
    w_gate_out,
    w_output,
    norm_gain,
    gate_gain,
    glu_gain,
    lower_table,
    w_glu_gate,
    w_glu_up,
    w_glu_down,
    cotangent,
):
    seq_index = lax.axis_index("seq")
    fsdp_index = lax.axis_index("fsdp")
    groups = lax.axis_size("fsdp")
    _, rows, width = hidden.shape
    chans = w_input.shape[1]
    units = w_glu_gate.shape[1]
    tokens = groups * rows
    small_shape = (round_up(groups, 8), round_up(rows, 128))

    def to_small(value):
        return jnp.pad(
            value, ((0, small_shape[0] - value.shape[0]), (0, small_shape[1] - value.shape[1]))
        )

    def dot(left, right):
        return jnp.dot(left, right, preferred_element_type=F32)

    def dot_t(left, right):
        return lax.dot_general(left, right, (((1,), (1,)), ((), ())), preferred_element_type=F32)

    def over_tokens(left, right):
        return lax.dot_general(left, right, (((0,), (0,)), ((), ())), preferred_element_type=F32)

    cotangent_all = lax.all_gather(cotangent[0], "fsdp").reshape(tokens, width)

    hidden_f = hidden[0].astype(F32)
    scale_one = lax.rsqrt(jnp.mean(hidden_f * hidden_f, -1, keepdims=True) + epsilon)
    normed = (hidden_f * scale_one * norm_gain).astype(BF16)
    normed_all, _ = gather(normed, jnp.zeros((8, 128), F32), 0)
    normed_all = normed_all.reshape(tokens, width)
    in_raw = dot(normed_all, w_input).astype(BF16).reshape(groups, rows, chans)
    forget_raw = dot(normed_all, w_forget).astype(BF16).reshape(groups, rows, chans)
    gate_raw = dot(normed_all, w_gate_out)

    bounds_full = lower_bound(lower_table)
    bounds = lax.dynamic_slice_in_dim(bounds_full, fsdp_index * chans, chans)[None]
    seq_starts = jnp.cumsum(lengths, axis=1) - lengths
    places = seq_index * rows + jnp.arange(rows, dtype=jnp.int32)
    starts = jnp.any(places[None, :, None] == seq_starts[:, None, :], axis=-1)
    keep = jnp.where(starts, 0.0, 1.0).astype(F32)[:, :, None]
    state_b, before = forward_scan(in_raw, forget_raw, bounds, keep, 1)

    state_f = state_b.astype(F32).reshape(tokens, chans)
    gain_slice = lax.dynamic_slice_in_dim(gate_gain, fsdp_index * chans, chans)
    sigma_g = jax.nn.sigmoid(gate_raw)
    silu_gate = gate_raw * sigma_g
    out_raw = (state_f * gain_slice * silu_gate).astype(BF16)
    squares = jnp.sum(state_f * state_f, -1).reshape(groups, rows)
    mixed_part = dot(out_raw, w_output).astype(BF16).reshape(groups, rows, width)
    mixed_raw, square_sum = reduce_rows(mixed_part, to_small(squares), 2)
    state_scale = lax.rsqrt(square_sum[:groups, :rows] / width + epsilon)
    own_scale = lax.dynamic_slice_in_dim(state_scale, fsdp_index, 1, 0)[0][:, None]
    scale_g = state_scale.reshape(tokens, 1)
    middle = hidden_f + own_scale * mixed_raw
    scale_two = lax.rsqrt(jnp.mean(middle * middle, -1, keepdims=True) + epsilon)
    normed_two = (middle * scale_two * glu_gain).astype(BF16)
    normed_two_all, _ = gather(normed_two, jnp.zeros((8, 128), F32), 3)
    normed_two_all = normed_two_all.reshape(tokens, width)

    gate_val = dot(normed_two_all, w_glu_gate)
    up_val = dot(normed_two_all, w_glu_up)
    sigma_u = jax.nn.sigmoid(gate_val)
    silu_u = gate_val * sigma_u
    activity = (silu_u * up_val).astype(BF16)
    down_grad = sum_over_seq(over_tokens(cotangent_all, activity))
    d_act = dot_t(cotangent_all, w_glu_down)
    d_gate = (d_act * up_val * silu_slope(gate_val, sigma_u)).astype(BF16)
    d_up = (d_act * silu_u).astype(BF16)
    pair_grad = sum_over_seq(
        jnp.concatenate(
            [
                over_tokens(normed_two_all, d_gate).astype(BF16),
                over_tokens(normed_two_all, d_up).astype(BF16),
            ],
            1,
        )
    )
    d_two_part = (dot_t(d_gate, w_glu_gate) + dot_t(d_up, w_glu_up)).astype(BF16)
    no_small = jnp.zeros((8, 128), F32)
    d_normed_two, _ = reduce_rows(d_two_part.reshape(groups, rows, width), no_small, 4)
    glu_part = dot(activity, w_glu_down).astype(BF16).reshape(groups, rows, width)
    glu_result = lax.psum_scatter(glu_part, "fsdp", scatter_dimension=0, tiled=True)[0]
    output = (middle + glu_result.astype(F32)).astype(BF16)[None]

    cotangent_f = cotangent[0].astype(F32)
    scaled_two = glu_gain * d_normed_two
    d_middle = (
        cotangent_f
        + scale_two * scaled_two
        - middle * scale_two**3 * jnp.mean(scaled_two * middle, -1, keepdims=True)
    )
    d_glu_gain = jnp.sum(d_normed_two * middle * scale_two, 0)
    d_mixed = d_middle.astype(BF16)
    own_dot = jnp.sum(d_mixed.astype(F32) * mixed_raw, -1)[None]
    d_mixed_all, dots = gather(d_mixed, to_small(own_dot), 5)
    d_mixed_all = d_mixed_all.reshape(tokens, width)
    dot_rows = dots[:, 0, :rows].reshape(tokens, 1)

    d_out = dot_t(d_mixed_all, w_output)
    scaled_state = state_f * scale_g
    d_gain_slice = jnp.sum(d_out * scaled_state * silu_gate, 0)
    d_scaled = d_out * gain_slice * silu_gate
    d_gate_raw = (d_out * scaled_state * gain_slice * silu_slope(gate_raw, sigma_g)).astype(BF16)
    d_state = scale_g * d_scaled - state_f * (scale_g**3 * (dot_rows / width))
    d_state = d_state.astype(BF16).reshape(groups, rows, chans)
    d_in, d_forget_raw, d_bounds = backward_scan(
        d_state, in_raw, forget_raw, before, bounds, keep, 6
    )
    d_in = d_in.reshape(tokens, chans)
    d_forget_raw = d_forget_raw.reshape(tokens, chans)

    d_normed_part = dot_t(d_in, w_input) + dot_t(d_forget_raw, w_forget)
    d_normed_part = (d_normed_part + dot_t(d_gate_raw, w_gate_out)).astype(BF16)
    out_gate = (out_raw.astype(F32) * scale_g).astype(BF16)
    mixer_grad = sum_over_seq(
        jnp.concatenate(
            [
                over_tokens(d_mixed_all, out_gate).astype(BF16),
                over_tokens(normed_all, d_in).astype(BF16),
                over_tokens(normed_all, d_forget_raw).astype(BF16),
                over_tokens(normed_all, d_gate_raw).astype(BF16),
            ],
            1,
        )
    )
    d_normed, _ = reduce_rows(d_normed_part.reshape(groups, rows, width), no_small, 7)
    scaled_one = norm_gain * d_normed
    d_hidden = (
        d_middle
        + scale_one * scaled_one
        - hidden_f * scale_one**3 * jnp.mean(scaled_one * hidden_f, -1, keepdims=True)
    )
    d_norm_gain = jnp.sum(d_normed * hidden_f * scale_one, 0)
    d_gain_full = lax.dynamic_update_slice(
        jnp.zeros((width,), F32), d_gain_slice, (fsdp_index * chans,)
    )
    d_bounds_full = lax.dynamic_update_slice(
        jnp.zeros((width,), F32), d_bounds[0], (fsdp_index * chans,)
    )
    sums = jnp.stack([d_norm_gain, d_glu_gain, d_gain_full, d_bounds_full])
    totals = sum_all(sums.reshape(8, width // 2), 8).reshape(4, width)
    _, bounds_pull = jax.vjp(lower_bound, lower_table)
    d_table = bounds_pull(totals[3])[0]
    return (
        output,
        d_hidden.astype(BF16)[None],
        mixer_grad[:, chans : 2 * chans],
        mixer_grad[:, 2 * chans : 3 * chans],
        mixer_grad[:, 3 * chans :],
        mixer_grad[:, :chans].T,
        totals[0],
        totals[2],
        totals[1],
        d_table,
        pair_grad[:, :units],
        pair_grad[:, units:],
        down_grad.T,
    )


def copy_in(src, dst, sem):
    copy = pltpu.make_async_copy(src, dst, sem)
    copy.start()
    return copy


class Links:
    def __init__(self, send, recv):
        self.send, self.recv, self.used = send, recv, 0

    def start(self, src, dst, device):
        copy = remote(src, dst, self.send.at[self.used], self.recv.at[self.used], device)
        self.used += 1
        copy.start()
        return copy


class Locals:
    def __init__(self, sems):
        self.sems, self.used = sems, 0

    def start(self, src, dst):
        copy = copy_in(src, dst, self.sems.at[self.used])
        self.used += 1
        return copy


def row_slots(rows):
    half = rows // 2
    top = [pl.ds(k * rows, half) for k in range(4)]
    bottom = [pl.ds(k * rows + half, half) for k in range(4)]
    return top, bottom


def gather_start(links, src, dst, rows, s, fx, fy):
    half = rows // 2
    top, bottom = row_slots(rows)
    here = (pl.ds(0, half), pl.ds(half, half))
    return [
        links.start(src.at[here[0]], dst.at[top[1]], (s, fx)),
        links.start(src.at[here[1]], dst.at[bottom[2]], (s, fy)),
        links.start(src.at[here[1]], dst.at[bottom[1]], (s, fx)),
        links.start(src.at[here[0]], dst.at[top[2]], (s, fy)),
    ]


def gather_forward(links, own, dst, rows, s, fx, fy):
    top, bottom = row_slots(rows)
    own[0].wait_recv()
    on_y = links.start(dst.at[top[1]], dst.at[top[3]], (s, fy))
    own[1].wait_recv()
    on_x = links.start(dst.at[bottom[2]], dst.at[bottom[3]], (s, fx))
    return [on_y, on_x]


def gather_middle(own):
    own[2].wait_recv()
    own[3].wait_recv()


def gather_far(later):
    for copy in later:
        copy.wait_recv()


def sends_done(*lists):
    for copies in lists:
        for copy in copies:
            copy.wait_send()


def wait_all(*lists):
    for copies in lists:
        for copy in copies:
            copy.wait()


def reduce_start_far(links, part, from_x, from_y, rows, s, fx, fy):
    top, bottom = row_slots(rows)
    return [
        links.start(part.at[top[3]], from_x.at[0], (s, fx)),
        links.start(part.at[bottom[3]], from_y.at[0], (s, fy)),
    ]


def reduce_start_near(links, part, from_x, from_y, rows, s, fx, fy):
    top, bottom = row_slots(rows)
    return [
        links.start(part.at[top[1]], from_x.at[1], (s, fx)),
        links.start(part.at[bottom[2]], from_y.at[1], (s, fy)),
    ]


def reduce_pass(links, far, part, from_x, from_y, pass_x, pass_y, rows, s, fx, fy):
    top, bottom = row_slots(rows)
    far[0].wait_recv()
    pass_y[...] = (from_x[0].astype(F32) + part[top[2]].astype(F32)).astype(BF16)
    on_y = links.start(pass_y, from_y.at[2], (s, fy))
    far[1].wait_recv()
    pass_x[...] = (from_y[0].astype(F32) + part[bottom[1]].astype(F32)).astype(BF16)
    on_x = links.start(pass_x, from_x.at[2], (s, fx))
    return [on_y, on_x]


def mm(left, right):
    return jnp.dot(left, right, preferred_element_type=F32)


def mm_t(left, right):
    return lax.dot_general(left, right, (((1,), (1,)), ((), ())), preferred_element_type=F32)


def tile(n, width):
    return pl.ds(pl.multiple_of(n * width, width), width)


def bounds_slice(table, first, count):
    rows = table[:, pl.ds(pl.multiple_of(first, 128), count)]
    powers = jnp.exp(rows - jnp.max(rows, 0, keepdims=True))
    return jnp.sum(powers[1 : LAYER + 1], 0, keepdims=True) / jnp.sum(powers, 0, keepdims=True)


def keep_rows(lengths, group, first, rows):
    places = first + lax.broadcasted_iota(jnp.int32, (rows, 128), 0)
    start = jnp.int32(0)
    keep = jnp.where(places == start, 0.0, 1.0)
    for i in range(lengths.shape[1] - 1):
        start = start + lengths[group, i]
        keep = jnp.where(places == start, 0.0, keep)
    return keep.astype(F32)


def segment_totals(end_p, end_s, blocks, order):
    first, rest = order[0], order[1:]
    p_all = end_p[pl.ds(first, blocks, stride=8), :]
    s_all = end_s[pl.ds(first, blocks, stride=8), :]
    for j in rest:
        p_j = end_p[pl.ds(j, blocks, stride=8), :]
        s_all = end_s[pl.ds(j, blocks, stride=8), :] + p_j * s_all
        p_all = p_all * p_j
    return p_all, s_all


def spread_carry(carry, carr, end_p, end_s, blocks, order):
    for i, j in enumerate(order):
        carr[pl.ds(j, blocks, stride=8), :] = carry
        if i < 7:
            carry = end_s[pl.ds(j, blocks, stride=8), :] + end_p[pl.ds(j, blocks, stride=8), :] * carry


def mixer_kernel(
    n_seq,
    lengths,
    hidden,
    cot,
    norm_gain,
    gate_gain,
    glu_gain,
    table,
    w_in,
    w_fg,
    w_gt,
    w_out,
    normed_half,
    cot_out,
    in_out,
    fg_out,
    gate_out,
    state_out,
    raw_out,
    before_out,
    scale_out,
    middle,
    two,
    wv,
    wo,
    rows_all,
    stage,
    in_ref,
    fg_ref,
    gate_ref,
    a_ref,
    b_ref,
    shifted,
    keep_ref,
    end_p,
    end_s,
    carr,
    total,
    gathered,
    state_ref,
    raw_ref,
    squares,
    squares_t,
    packed,
    squares_in,
    part,
    from_x,
    from_y,
    pass_x,
    pass_y,
    send,
    recv,
    exchange_send,
    exchange_recv,
    local_sems,
):
    rows, width = hidden.shape
    chans = w_in.shape[1]
    lanes_of = [slice(c, c + 128) for c in range(0, chans, 128)]
    count = len(lanes_of)
    blocks = 4 * count
    step_len = rows // 8
    s, f, fx, fy, fd = plane()
    groups = [f, fx, fy, fd]
    links, local = Links(send, recv), Locals(local_sems)

    weights = [
        local.start(w, wv.at[:, pl.ds(i * chans, chans)]) for i, w in enumerate((w_in, w_fg, w_gt))
    ]
    weights.append(local.start(w_out, wo))
    barrier = pltpu.get_barrier_semaphore()
    peers = [(s, fx), (s, fy), (s, fd)] + seq_peers(n_seq)
    for peer in peers:
        pl.semaphore_signal(barrier, inc=1, device_id=peer, device_id_type=MESH)

    def norm_rows(i, _):
        at = pl.ds(pl.multiple_of(i * 16, 16), 16)
        value = hidden[at].astype(F32)
        scale = lax.rsqrt(jnp.mean(value * value, -1, keepdims=True) + epsilon)
        rows_all[at] = (value * scale * norm_gain[...]).astype(BF16)
        return 0

    lax.fori_loop(0, rows // 16, norm_rows, 0)
    pl.semaphore_wait(barrier, len(peers))
    own = gather_start(links, rows_all, rows_all, rows, s, fx, fy)
    bound = bounds_slice(table, f * chans, chans)
    for k in range(4):
        keep_ref[k] = keep_rows(lengths, groups[k], s * rows, rows)
    squares[...] = jnp.zeros_like(squares)
    squares_t[...] = jnp.zeros_like(squares_t)
    for copy in weights[:3]:
        copy.wait()

    def project(first, slots):
        def tile_of(n, _):
            cols = tile(n, 256)
            stage[: slots * rows, cols] = mm(
                rows_all[first * rows : (first + slots) * rows], wv[:, cols]
            )
            return 0

        lax.fori_loop(0, 3 * chans // 256, tile_of, 0)
        for k in range(slots):
            at = slice(k * rows, (k + 1) * rows)
            for c, lanes in enumerate(lanes_of):
                n = (first + k) * count + c
                value = stage[at, lanes].astype(BF16)
                in_ref[first + k, :, lanes] = value
                value = value.astype(F32)
                raw = stage[at, chans + c * 128 : chans + (c + 1) * 128].astype(BF16)
                fg_ref[first + k, :, lanes] = raw
                edge = bound[:, lanes]
                forget = edge + (1.0 - edge) * jax.nn.sigmoid(raw.astype(F32))
                a_ref[n] = forget * keep_ref[first + k]
                b_ref[n] = value * jax.nn.sigmoid(value) * (1.0 - forget)
            gate_ref[first + k] = stage[at, 2 * chans :]

    project(0, 1)
    later = gather_forward(links, own, rows_all, rows, s, fx, fy)
    gather_middle(own)
    project(1, 2)
    gather_far(later)
    cot_own = gather_start(links, cot, cot_out, rows, s, fx, fy)
    core = s % 2
    swaps, outs = swap_columns(
        links, local, rows_all, normed_half, n_seq, core, (s + 1 - 2 * core, f)
    )
    outs.append(local.start(cot, cot_out.at[pl.ds(0, rows)]))
    project(3, 1)
    outs += [
        local.start(in_ref, in_out),
        local.start(fg_ref, fg_out),
        local.start(gate_ref, gate_out),
    ]

    def scan_step(i, carry):
        new = []
        at = pl.ds(i, 8, stride=step_len)
        for n, (product, state) in enumerate(carry):
            a = a_ref[n, at, :]
            state = a * state + b_ref[n, at, :]
            product = product * a
            a_ref[n, at, :] = product
            b_ref[n, at, :] = state
            new.append((product, state))
        return tuple(new)

    start = tuple((jnp.ones((8, 128), F32), jnp.zeros((8, 128), F32)) for _ in range(blocks))
    ends = lax.fori_loop(0, step_len, scan_step, start)
    for n, (product, state) in enumerate(ends):
        end_p[8 * n : 8 * n + 8] = product
        end_s[8 * n : 8 * n + 8] = state
    p_all, s_all = segment_totals(end_p, end_s, blocks, range(8))
    total[:blocks] = p_all
    total[blocks:] = s_all
    copies = start_exchange(total, gathered, exchange_send, exchange_recv, n_seq)
    wait_all(copies)
    carry = jnp.zeros((blocks, 128), F32)
    for j in range(n_seq - 1):
        carry = jnp.where(j < s, gathered[j, blocks:] + gathered[j, :blocks] * carry, carry)
    for n in range(blocks):
        shifted[n, 0:1] = carry[n : n + 1]
    spread_carry(carry, carr, end_p, end_s, blocks, range(8))

    def finish(n, _):
        enter_state = carr[pl.ds(pl.multiple_of(n * 8, 8), 8)]
        for i in range(step_len):
            at = pl.ds(i, 8, stride=step_len)
            state = b_ref[n, at, :] + a_ref[n, at, :] * enter_state
            b_ref[n, at, :] = state
            shifted[n, pl.ds(i + 1, 8, stride=step_len), :] = state
        return 0

    lax.fori_loop(0, blocks, finish, 0)
    outs.append(local.start(shifted.at[:, pl.ds(0, rows)], before_out))

    lane = lax.broadcasted_iota(jnp.int32, (rows, 128), 1)
    for k in (3, 1, 2, 0):
        square = jnp.zeros((rows, 1), F32)
        for c, lanes in enumerate(lanes_of):
            state_b = b_ref[k * count + c].astype(BF16)
            state_ref[k, :, lanes] = state_b
            state = state_b.astype(F32)
            square = square + jnp.sum(state * state, -1, keepdims=True)
            gate = gate_ref[k, :, lanes]
            gain = gate_gain[:, pl.ds(pl.multiple_of(f * chans + c * 128, 128), 128)]
            raw_ref[k * rows : (k + 1) * rows, lanes] = (
                state * gain * gate * jax.nn.sigmoid(gate)
            ).astype(BF16)
        squares[:rows] = jnp.where(lane == groups[k], square, squares[:rows])
    packed[...] = squares[...].T[:8]
    square_copies = [
        links.start(packed, squares_in.at[i], (s, peer)) for i, peer in enumerate((fx, fy, fd))
    ]
    outs += [local.start(state_ref, state_out), local.start(raw_ref, raw_out)]
    cot_later = gather_forward(links, cot_own, cot_out, rows, s, fx, fy)
    weights[3].wait()

    def output_part(first, slots):
        at = slice(first * rows, (first + slots) * rows)

        def tile_of(n, _):
            cols = tile(n, 512)
            part[at, cols] = mm(raw_ref[at], wo[:, cols]).astype(BF16)
            return 0

        lax.fori_loop(0, width // 512, tile_of, 0)

    output_part(3, 1)
    far = reduce_start_far(links, part, from_x, from_y, rows, s, fx, fy)
    output_part(1, 2)
    near = reduce_start_near(links, part, from_x, from_y, rows, s, fx, fy)
    output_part(0, 1)
    passed = reduce_pass(links, far, part, from_x, from_y, pass_x, pass_y, rows, s, fx, fy)
    for copy in square_copies:
        copy.wait_recv()
    all_squares = (packed[...] + squares_in[0]) + (squares_in[1] + squares_in[2])
    squares_t[:8] = lax.rsqrt(all_squares / width + epsilon)
    scales = squares_t[...].T[:rows]
    for k in range(4):
        scale_out[k] = jnp.sum(jnp.where(lane == groups[k], scales, 0.0), -1, keepdims=True)
    for copy in near + passed:
        copy.wait_recv()
    half = rows // 2
    for first, one, other in ((0, from_x.at[1], from_y.at[2]), (half, from_y.at[1], from_x.at[2])):

        def sum_rows(i, _):
            here = pl.ds(pl.multiple_of(i * 16, 16), 16)
            at = pl.ds(pl.multiple_of(first + i * 16, 16), 16)
            mixed = part[at].astype(F32) + one[here].astype(F32) + other[here].astype(F32)
            value = hidden[at].astype(F32) + scale_out[0, at] * mixed
            middle[at] = value
            scale = lax.rsqrt(jnp.mean(value * value, -1, keepdims=True) + epsilon)
            two[at] = (value * scale * glu_gain[...]).astype(BF16)
            return 0

        lax.fori_loop(0, half // 16, sum_rows, 0)
    gather_middle(cot_own)
    gather_far(cot_later)
    sends_done(own, later, cot_own, cot_later, square_copies, far, near, passed)
    wait_all(swaps, outs)


def mixer_forward(lengths, hidden, cot, gains, table, weights, collective_id):
    n_seq = lax.axis_size("seq")
    rows, width = hidden.shape
    chans = weights[0].shape[1]
    blocks = 4 * chans // 128
    tokens = 4 * rows
    half = rows // 2
    shape = jax.ShapeDtypeStruct
    wide = shape((tokens, width), BF16)
    narrow = shape((4, rows, chans), BF16)
    long_rows = round_up(rows, 128)
    return pl.pallas_call(
        functools.partial(mixer_kernel, n_seq),
        out_shape=(
            shape((2, tokens, width // 2), BF16),
            wide,
            narrow,
            narrow,
            shape((4, rows, chans), F32),
            narrow,
            shape((tokens, chans), BF16),
            shape((blocks, rows, 128), F32),
            shape((4, rows, 1), F32),
            shape((rows, width), F32),
            shape((rows, width), BF16),
        ),
        in_specs=[pl.BlockSpec(memory_space=pltpu.SMEM), VMEM, VMEM, VMEM, VMEM, VMEM, VMEM]
        + [ANY] * 4,
        out_specs=(ANY,) * 8 + (VMEM,) * 3,
        scratch_shapes=[
            pltpu.VMEM((width, 3 * chans), BF16),
            pltpu.VMEM((chans, width), BF16),
            pltpu.VMEM((tokens, width), BF16),
            pltpu.VMEM((2 * rows, 3 * chans), F32),
            pltpu.VMEM((4, rows, chans), BF16),
            pltpu.VMEM((4, rows, chans), BF16),
            pltpu.VMEM((4, rows, chans), F32),
            pltpu.VMEM((blocks, rows, 128), F32),
            pltpu.VMEM((blocks, rows, 128), F32),
            pltpu.VMEM((blocks, rows + 8, 128), F32),
            pltpu.VMEM((4, rows, 128), F32),
            pltpu.VMEM((8 * blocks, 128), F32),
            pltpu.VMEM((8 * blocks, 128), F32),
            pltpu.VMEM((8 * blocks, 128), F32),
            pltpu.VMEM((2 * blocks, 128), F32),
            pltpu.VMEM((n_seq, 2 * blocks, 128), F32),
            pltpu.VMEM((4, rows, chans), BF16),
            pltpu.VMEM((tokens, chans), BF16),
            pltpu.VMEM((long_rows, 128), F32),
            pltpu.VMEM((128, long_rows), F32),
            pltpu.VMEM((8, long_rows), F32),
            pltpu.VMEM((3, 8, long_rows), F32),
            pltpu.VMEM((tokens, width), BF16),
            pltpu.VMEM((3, half, width), BF16),
            pltpu.VMEM((3, half, width), BF16),
            pltpu.VMEM((half, width), BF16),
            pltpu.VMEM((half, width), BF16),
            pltpu.SemaphoreType.DMA((21 + n_seq // 2,)),
            pltpu.SemaphoreType.DMA((21 + n_seq // 2,)),
            pltpu.SemaphoreType.DMA((n_seq,)),
            pltpu.SemaphoreType.DMA((n_seq,)),
            pltpu.SemaphoreType.DMA((11 + n_seq // 2,)),
        ],
        compiler_params=params(collective_id),
        name="mixer_forward",
    )(lengths, hidden, cot, *gains, table, *weights)


def swap_columns(links, local, src, dst, n_seq, core, mate):
    part = src.shape[1] // n_seq
    copies, stays = [], []
    for z in range(n_seq // 2):
        to = pl.ds(z * part, part)
        theirs = pl.ds(pl.multiple_of((2 * z + 1 - core) * part, part), part)
        ours = pl.ds(pl.multiple_of((2 * z + core) * part, part), part)
        copies.append(links.start(src.at[:, theirs], dst.at[1, :, to], mate))
        stays.append(local.start(src.at[:, ours], dst.at[0, :, to]))
    return copies, stays


def glu_kernel(
    n_seq,
    two,
    cot_all,
    w_gate,
    w_up,
    w_down,
    two_half,
    cot_half,
    act_pair,
    gate_pair,
    up_pair,
    wv,
    wd,
    cot_ref,
    two_ref,
    d_act,
    stage,
    act,
    d_gate,
    d_up,
    send,
    recv,
    local_sems,
):
    rows = two.shape[0]
    units = w_gate.shape[1]
    s, f, fx, fy, fd = plane()
    core = s % 2
    mate = (s + 1 - 2 * core, f)
    links, local = Links(send, recv), Locals(local_sems)
    loads = [local.start(w_down, wd), local.start(cot_all, cot_ref)]
    two_ref[:rows] = two[...]
    enter([(s, fx), (s, fy), mate])
    own = gather_start(links, two_ref, two_ref, rows, s, fx, fy)
    wait_all(loads)
    loads = [
        local.start(w_gate, wv.at[:, pl.ds(0, units)]),
        local.start(w_up, wv.at[:, pl.ds(units, units)]),
    ]
    swaps, stays = swap_columns(links, local, cot_ref, cot_half, n_seq, core, mate)

    def act_tile(n, _):
        cols = tile(n, 256)
        d_act[:, cols] = mm_t(cot_ref[...], wd[cols])
        return 0

    lax.fori_loop(0, units // 256, act_tile, 0)
    if units % 256:
        rest = slice(units // 256 * 256, units)
        d_act[:, rest] = mm_t(cot_ref[...], wd[rest])
    later = gather_forward(links, own, two_ref, rows, s, fx, fy)
    wait_all(loads)

    def slots(first, number, swap=True):
        nonlocal swaps, stays
        base = first * rows

        def tile_of(n, _):
            cols = tile(n, 256)
            stage[: number * rows, cols] = mm(two_ref[base : base + number * rows], wv[:, cols])
            return 0

        lax.fori_loop(0, 2 * units // 256, tile_of, 0)

        def rows_of(i, _):
            at = pl.ds(pl.multiple_of(i * 16, 16), 16)
            to = pl.ds(pl.multiple_of(base + i * 16, 16), 16)
            gate, up = stage[at, :units], stage[at, units:]
            sigma = jax.nn.sigmoid(gate)
            silu = gate * sigma
            act[to] = (silu * up).astype(BF16)
            d = d_act[to]
            d_gate[to] = (d * up * silu_slope(gate, sigma)).astype(BF16)
            d_up[to] = (d * silu).astype(BF16)
            return 0

        cuts = number * rows // 2
        for first_row in (0, cuts):
            lax.fori_loop(first_row // 16, (first_row + cuts) // 16, rows_of, 0)
            at = pl.ds(base + first_row, cuts)
            for src, dst in ((act, act_pair), (d_gate, gate_pair), (d_up, up_pair)):
                stays = stays + [local.start(src.at[at], dst.at[0, at])]
                if swap:
                    swaps = swaps + [links.start(src.at[at], dst.at[1, at], mate)]

    slots(0, 1)
    gather_middle(own)
    slots(1, 2)
    gather_far(later)
    more, keeps = swap_columns(links, local, two_ref, two_half, n_seq, core, mate)
    slots(3, 1, False)
    sends_done(own, later)
    wait_all(swaps, stays, more, keeps)


def glu(two, cot_all, w_gate, w_up, w_down, collective_id):
    n_seq = lax.axis_size("seq")
    rows, width = two.shape
    units = w_gate.shape[1]
    tokens = 4 * rows
    shape = jax.ShapeDtypeStruct
    half = shape((2, tokens, width // 2), BF16)
    pair = shape((2, tokens, units), BF16)
    remote_count = 6 + n_seq + 12
    return pl.pallas_call(
        functools.partial(glu_kernel, n_seq),
        out_shape=(half, half, pair, pair, pair),
        in_specs=[VMEM] + [ANY] * 4,
        out_specs=(ANY,) * 5,
        scratch_shapes=[
            pltpu.VMEM((width, 2 * units), BF16),
            pltpu.VMEM((units, width), BF16),
            pltpu.VMEM((tokens, width), BF16),
            pltpu.VMEM((tokens, width), BF16),
            pltpu.VMEM((tokens, units), F32),
            pltpu.VMEM((2 * rows, 2 * units), F32),
            pltpu.VMEM((tokens, units), BF16),
            pltpu.VMEM((tokens, units), BF16),
            pltpu.VMEM((tokens, units), BF16),
            pltpu.SemaphoreType.DMA((remote_count,)),
            pltpu.SemaphoreType.DMA((remote_count,)),
            pltpu.SemaphoreType.DMA((4 + n_seq + 18,)),
        ],
        compiler_params=params(collective_id),
        name="glu",
    )(two, cot_all, w_gate, w_up, w_down)


class ZLine:
    def __init__(self, part, buf, sems, n_seq, width, lag, ahead, store=None, leave=None):
        self.part, self.buf, self.width, self.lag, self.ahead = part, buf, width, lag, ahead
        self.send_up, self.recv_up, self.send_down, self.recv_down = sems[:4]
        self.store, self.leave = store, leave
        self.s, self.f = lax.axis_index("seq"), lax.axis_index("fsdp")
        self.n_seq, self.nz = n_seq, n_seq // 2
        self.z = self.s // 2
        self.block = part.shape[0] // self.nz
        self.chunks = part.shape[1] // width
        self.steps = (self.nz - 1) * self.chunks
        self.calls = self.steps + lag * (self.nz - 2)

    def rows(self, t):
        return pl.ds(pl.multiple_of(t * self.block, self.block), self.block)

    def move(self, up, k, j):
        t = self.nz - 1 - k if up else k
        landing = t + 1 if up else t
        cols = tile(j, self.width)
        slot = k * self.chunks + j
        peer = lax.rem(self.s + (2 if up else self.n_seq - 2), self.n_seq)
        send, recv = (
            (self.send_up, self.recv_up) if up else (self.send_down, self.recv_down)
        )
        return remote(
            self.part.at[self.rows(t), cols],
            self.buf.at[self.rows(landing), cols],
            send.at[slot],
            recv.at[slot],
            (peer, self.f),
        )

    def feed(self, q):
        inside = q < self.steps
        q = jnp.minimum(q, self.steps - 1)
        k = q // self.chunks
        j = q - k * self.chunks

        @pl.when(inside & (self.z == 0))
        def _():
            self.move(True, k, j).start()

        @pl.when(inside & (self.z == self.nz - 1))
        def _():
            self.move(False, k, j).start()

    def nth(self, i):
        return jnp.where(self.z < self.nz // 2, self.nz - 1 - i, i)

    def load(self, local, src, first, last):
        order = [self.rows(self.nth(i)) for i in range(first, last)]
        return [local.start(src.at[at], self.part.at[at]) for at in order]

    def feed_first(self):
        def step(q, _):
            self.feed(q)
            return 0

        lax.fori_loop(0, self.ahead, step, 0)

    def serve_one(self, up, q):
        z, nz = self.z, self.nz
        hops = z if up else nz - 1 - z
        q = q - self.lag * (hops - 1)
        inside = (hops >= 1) & (q >= 0) & (q < self.steps)
        q = jnp.clip(q, 0, self.steps - 1)
        k = q // self.chunks
        j = q - k * self.chunks
        left = nz - 1 - k - hops
        cols = tile(j, self.width)

        @pl.when(inside & (left >= 0))
        def _():
            self.move(up, k, j).wait_recv()

        @pl.when(inside & (left > 0))
        def _():
            t = nz - 1 - k if up else k
            landing = t + 1 if up else t
            own = self.part[self.rows(t), cols].astype(F32)
            came = self.buf[self.rows(landing), cols].astype(F32)
            self.part[self.rows(t), cols] = (own + came).astype(BF16)
            self.move(up, k, j).start()

    def serve(self, q, done=False):
        self.serve_one(True, q)
        self.serve_one(False, q)
        if done:
            j = q - (self.nz - 2) * self.chunks

            @pl.when((j >= 0) & (j < self.chunks))
            def _():
                self.finish(j)

    def serve_range(self, first, last, done=False):
        def step(q, _):
            self.feed(q + self.ahead)
            self.serve(q, done)
            return 0

        lax.fori_loop(first, last, step, 0)

    def finish(self, j):
        cols = tile(j, self.width)
        above = self.buf[self.rows(self.z), cols].astype(F32)
        below = self.buf[self.rows(self.z + 1), cols].astype(F32)
        own = self.part[self.rows(self.z), cols].astype(F32)
        own = own + jnp.where(self.z < self.nz - 1, above, 0.0)
        self.store(j, own + jnp.where(self.z > 0, below, 0.0))
        self.leave(j, True)

    def drain(self):
        for k in range(self.nz - 1):
            for up in (True, False):
                hops = self.z if up else self.nz - 1 - self.z

                @pl.when(hops < self.nz - 1 - k)
                def _():
                    def step(j, _):
                        self.move(up, k, j).wait_send()
                        return 0

                    lax.fori_loop(0, self.chunks, step, 0)

        def left(j, _):
            self.leave(j, False)
            return 0

        lax.fori_loop(0, self.chunks, left, 0)


def start_or_wait(copy, start):
    if start:
        copy.start()
    else:
        copy.wait()


def line_sems(n_seq, columns, width):
    count = (n_seq // 2 - 1) * (columns // width)
    leave = pltpu.SemaphoreType.DMA((columns // width,))
    return [pltpu.SemaphoreType.DMA((count,)) for _ in range(4)] + [leave]


def z_peers(n_seq):
    s = lax.axis_index("seq")
    f = lax.axis_index("fsdp")
    return [(lax.rem(s + 2 * k, n_seq), f) for k in range(1, n_seq // 2)]


def mm_tokens(left, right):
    return lax.dot_general(left, right, (((0,), (0,)), ((), ())), preferred_element_type=F32)


def down_kernel(
    n_seq,
    cot_half,
    act_pair,
    two_half,
    gate_pair,
    up_pair,
    w_gate,
    w_up,
    d_two_out,
    pair_part,
    down_out,
    d_two,
    cot_ref,
    act_ref,
    two_ref,
    gate_ref,
    up_ref,
    wg,
    wu,
    part,
    buf,
    rows_part,
    from_x,
    from_y,
    pass_x,
    pass_y,
    pair_ref,
    down_ref,
    send,
    recv,
    local_sems,
    *line,
):
    rows, width = d_two.shape
    units = act_pair.shape[1]
    s, f, fx, fy, fd = plane()
    links, local = Links(send, recv), Locals(local_sems)
    core = s % 2
    mate = (s + 1 - 2 * core, f)
    tokens = 4 * rows
    near_rows, far_own = pl.ds(0, 2 * tokens - rows), pl.ds(3 * rows, rows)
    far_mate = pl.ds(2 * tokens - rows, rows)
    loads = [local.start(act_pair.at[near_rows], act_ref.at[near_rows])]
    enter([(s, fx), (s, fy), mate] + z_peers(n_seq))
    swaps = [links.start(act_pair.at[far_own], act_ref.at[far_mate], mate)]

    def store(j, value):
        down_ref[tile(j, 128)] = value.T

    def leave(j, start):
        at = tile(j, 128)
        copy = pltpu.make_async_copy(down_ref.at[at], down_out.at[at], line[4].at[j])
        start_or_wait(copy, start)

    z_sum = ZLine(part, buf, line, n_seq, 128, 3, 11, store, leave)
    block = z_sum.block
    tiles_in = [
        local.start(cot_half.at[:, at], cot_ref.at[:, at])
        for at in (tile(z_sum.nth(i), block) for i in range(z_sum.nz))
    ]
    wait_all(loads, tiles_in[:1])
    swaps[0].wait_recv()
    swaps += [
        links.start(src.at[far_own], dst.at[far_mate], mate)
        for src, dst in ((gate_pair, gate_ref), (up_pair, up_ref))
    ]
    loads = [
        local.start(src, dst)
        for src, dst in (
            (w_gate, wg),
            (w_up, wu),
            (gate_pair.at[near_rows], gate_ref.at[near_rows]),
            (up_pair.at[near_rows], up_ref.at[near_rows]),
            (two_half, two_ref),
        )
    ]

    def down_tile(i, _):
        t = z_sum.nth(i)
        part[z_sum.rows(t)] = mm_tokens(cot_ref[:, tile(t, block)], act_ref[...]).astype(BF16)
        return 0

    down_tile(jnp.int32(0), 0)
    z_sum.feed_first()
    wait_all(tiles_in[1:])
    lax.fori_loop(1, z_sum.nz, down_tile, 0)
    wait_all(loads)
    for copy in swaps[1:]:
        copy.wait_recv()

    def two_part(first, slots, base):
        at = slice(first * rows, (first + slots) * rows)

        def tile_of(n, _):
            cols = tile(n, 512)
            total = mm_t(gate_ref[at], wg[cols]) + mm_t(up_ref[at], wu[cols])
            rows_part[at, cols] = total.astype(BF16)
            z_sum.feed(base + n + z_sum.ahead)
            z_sum.serve(base + n)
            return 0

        lax.fori_loop(0, width // 512, tile_of, 0)

    count = width // 512
    two_part(3, 1, 0)
    far = reduce_start_far(links, rows_part, from_x, from_y, rows, s, fx, fy)
    two_part(1, 2, count)
    near = reduce_start_near(links, rows_part, from_x, from_y, rows, s, fx, fy)
    two_part(0, 1, 2 * count)
    served = 3 * count

    def pair_tiles(right, first, base):
        def tile_of(t, _):
            pair_ref[z_sum.rows(t), pl.ds(first, units)] = mm_tokens(
                two_ref[:, tile(t, block)], right[...]
            ).astype(BF16)
            z_sum.serve_range(base + 2 * t, base + 2 * t + 2, True)
            return 0

        lax.fori_loop(0, z_sum.nz, tile_of, 0)

    pair_tiles(gate_ref, 0, served)
    served += 2 * z_sum.nz
    passed = reduce_pass(links, far, rows_part, from_x, from_y, pass_x, pass_y, rows, s, fx, fy)
    pair_tiles(up_ref, units, served)
    served += 2 * z_sum.nz
    stay = local.start(pair_ref, pair_part)
    for copy in near + passed:
        copy.wait_recv()
    half = rows // 2
    d_two[:half] = rows_part[:half].astype(F32) + from_x[1].astype(F32) + from_y[2].astype(F32)
    d_two[half:] = rows_part[half:rows].astype(F32) + from_y[1].astype(F32) + from_x[2].astype(F32)
    early = local.start(d_two, d_two_out)
    z_sum.serve_range(served, z_sum.calls, True)
    z_sum.drain()
    sends_done(swaps, far, near, passed)
    wait_all([stay, early])


def down_sum(cot_half, act_pair, two_half, gate_pair, up_pair, w_gate, w_up, collective_id):
    n_seq = lax.axis_size("seq")
    tokens, units = act_pair.shape
    width = w_gate.shape[0]
    rows = tokens // 8
    half = (rows // 2, width)
    own = cot_half.shape[1]
    block = width // n_seq
    shape = jax.ShapeDtypeStruct
    return pl.pallas_call(
        functools.partial(down_kernel, n_seq),
        out_shape=(
            shape((rows, width), F32),
            shape((own, 2 * units), BF16),
            shape((units, block), F32),
        ),
        in_specs=[ANY] * 7,
        out_specs=(ANY, ANY, ANY),
        scratch_shapes=[
            pltpu.VMEM((rows, width), F32),
            pltpu.VMEM((tokens, own), BF16),
            pltpu.VMEM((tokens, units), BF16),
            pltpu.VMEM((tokens, own), BF16),
            pltpu.VMEM((tokens, units), BF16),
            pltpu.VMEM((tokens, units), BF16),
            pltpu.VMEM((width, units), BF16),
            pltpu.VMEM((width, units), BF16),
            pltpu.VMEM((own, units), BF16),
            pltpu.VMEM((own + block, units), BF16),
            pltpu.VMEM((tokens // 2, width), BF16),
            pltpu.VMEM((3,) + half, BF16),
            pltpu.VMEM((3,) + half, BF16),
            pltpu.VMEM(half, BF16),
            pltpu.VMEM(half, BF16),
            pltpu.VMEM((own, 2 * units), BF16),
            pltpu.VMEM((units, block), F32),
            pltpu.SemaphoreType.DMA((9,)),
            pltpu.SemaphoreType.DMA((9,)),
            pltpu.SemaphoreType.DMA((8 + n_seq // 2,)),
        ]
        + line_sems(n_seq, units, 128),
        compiler_params=params(collective_id),
        name="down_sum",
    )(cot_half, act_pair, two_half, gate_pair, up_pair, w_gate, w_up)


class TotalsFromAbove:
    def __init__(self, total, gathered, send, recv, n_seq):
        self.total, self.gathered, self.send, self.recv = total, gathered, send, recv
        self.s, self.f = lax.axis_index("seq"), lax.axis_index("fsdp")
        self.nz = n_seq // 2
        self.z, self.core = self.s // 2, self.s % 2
        self.mate = (2 * self.z + 1 - self.core, self.f)

    def down(self, sender, target):
        return remote(
            self.total,
            self.gathered.at[2 * sender + self.core],
            self.send.at[target],
            self.recv.at[2 * sender + self.core],
            (2 * target + self.core, self.f),
        )

    def across(self, sender, core):
        slot = 2 * sender + core
        return remote(
            self.gathered.at[slot],
            self.gathered.at[slot],
            self.send.at[self.nz + sender],
            self.recv.at[slot],
            self.mate,
        )

    def to_mate(self, core):
        slot = 2 * self.z + core
        return remote(
            self.total,
            self.gathered.at[slot],
            self.send.at[2 * self.nz],
            self.recv.at[slot],
            self.mate,
        )

    def start(self):
        self.to_mate(self.core).start()
        for target in range(self.nz - 1):

            @pl.when(target < self.z)
            def _():
                self.down(self.z, target).start()

    def relay(self):
        for sender in range(1, self.nz):

            @pl.when(sender > self.z)
            def _():
                self.down(sender, self.z).wait_recv()
                self.across(sender, self.core).start()

    def wait(self):
        self.to_mate(1 - self.core).wait_recv()
        for sender in range(1, self.nz):

            @pl.when(sender > self.z)
            def _():
                self.across(sender, 1 - self.core).wait_recv()

    def drain(self):
        self.to_mate(self.core).wait_send()
        for z in range(self.nz):

            @pl.when(z < self.z)
            def _():
                self.down(self.z, z).wait_send()

            @pl.when(z > self.z)
            def _():
                self.across(z, self.core).wait_send()


def pair_kernel(
    n_seq,
    lengths,
    hidden,
    cot,
    glu_gain,
    gate_gain,
    table,
    scale_g,
    d_two,
    middle,
    pair_part,
    w_out,
    w_in,
    w_fg,
    w_gt,
    gate_raw,
    state_b,
    out_raw,
    in_raw,
    fg_raw,
    before_in,
    normed_half,
    pair_grad,
    mixer_part,
    rows_out,
    sums_ref,
    d_glu_gain,
    d_gain,
    d_bounds,
    d_normed,
    d_middle,
    pair_ref,
    part,
    buf,
    wo,
    wv,
    mixed_all,
    mixed_mate,
    normed_ref,
    d_proj,
    out_gate,
    gate_ref,
    state_ref,
    raw_ref,
    in_ref,
    fg_ref,
    before,
    p_ref,
    q_ref,
    stage,
    rows_part,
    from_x,
    from_y,
    pass_x,
    pass_y,
    dots,
    keep_ref,
    end_p,
    end_s,
    carr,
    total,
    gathered,
    send,
    recv,
    exchange_send,
    exchange_recv,
    local_sems,
    tile_sems,
    *line,
):
    rows, width = hidden.shape
    chans = w_in.shape[1]
    tokens = 4 * rows
    lanes_of = [slice(c, c + 128) for c in range(0, chans, 128)]
    count = len(lanes_of)
    blocks = 4 * count
    step_len = rows // 8
    s, f, fx, fy, fd = plane()
    groups = [f, fx, fy, fd]
    core = s % 2
    mate = (s + 1 - 2 * core, f)
    links, local = Links(send, recv), Locals(local_sems)

    def store(j, value):
        pair_ref[:, tile(j, 256)] = value

    def leave(j, start):
        at = tile(j, 256)
        copy = pltpu.make_async_copy(pair_ref.at[:, at], pair_grad.at[:, at], line[4].at[j])
        start_or_wait(copy, start)

    z_sum = ZLine(part, buf, line, n_seq, 256, 2, 7, store, leave)
    blocks_in = z_sum.load(local, pair_part, 0, 1)
    rows_in = [local.start(d_two, d_middle), local.start(middle, d_normed)]
    enter([(s, fx), (s, fy), (s, fd)] + seq_peers(n_seq))
    blocks_in[0].wait()
    z_sum.feed_first()
    blocks_in = z_sum.load(local, pair_part, 1, z_sum.nz)
    loads = [local.start(w_out, wo)]
    loads += [
        local.start(src, dst)
        for src, dst in (
            (gate_raw, gate_ref),
            (state_b, state_ref),
            (out_raw, raw_ref),
            (in_raw, in_ref),
            (fg_raw, fg_ref),
            (before_in, before),
        )
    ]
    weights = [
        local.start(w, wv.at[:, pl.ds(i * chans, chans)]) for i, w in enumerate((w_in, w_fg, w_gt))
    ]
    weights.append(local.start(normed_half, normed_ref))
    served = 0

    def serve(number):
        nonlocal served
        z_sum.serve_range(served, served + number)
        served += number

    d_glu_gain[...] = jnp.zeros_like(d_glu_gain)
    wait_all(rows_in, blocks_in)

    def middle_rows(i, _):
        at = pl.ds(pl.multiple_of(i * 16, 16), 16)
        value, came = d_normed[at], d_middle[at]
        scale = lax.rsqrt(jnp.mean(value * value, -1, keepdims=True) + epsilon)
        scaled = glu_gain[...] * came
        mean = jnp.mean(scaled * value, -1, keepdims=True)
        grad = cot[at].astype(F32) + scale * scaled - value * (scale**3 * mean)
        d_middle[at] = grad
        grad_b = grad.astype(BF16)
        mixed_all[at] = grad_b
        own_dot = jnp.sum(
            grad_b.astype(F32) * (value - hidden[at].astype(F32)), -1, keepdims=True
        )
        dots[0, at] = jnp.broadcast_to(own_dot, (16, 128))
        d_glu_gain[...] += jnp.sum(came * value * scale, 0, keepdims=True)
        return 0

    lax.fori_loop(0, rows // 16, middle_rows, 0)
    outs = [local.start(d_middle, rows_out.at[pl.ds(rows, rows)])]
    own = gather_start(links, mixed_all, mixed_all, rows, s, fx, fy)
    dot_copies = [
        links.start(dots.at[0], dots.at[k], (s, peer)) for k, peer in ((1, fx), (2, fy), (3, fd))
    ]
    bound = bounds_slice(table, f * chans, chans)
    for k in range(4):
        keep_ref[k] = keep_rows(lengths, groups[k], s * rows, rows)
    d_gain[...] = jnp.zeros_like(d_gain)
    serve(1)
    for copy in loads:
        copy.wait()

    def out_rows(first, slots):
        stage[: slots * rows] = mm_t(mixed_all[first * rows : (first + slots) * rows], wo[...])
        for i in range(slots):
            k = first + i
            scale = scale_g[k]
            for c, lanes in enumerate(lanes_of):
                n = k * count + c
                gain = gate_gain[:, pl.ds(pl.multiple_of(f * chans + c * 128, 128), 128)]
                d_out = stage[i * rows : (i + 1) * rows, lanes]
                gate = gate_ref[k, :, lanes]
                sigma = jax.nn.sigmoid(gate)
                silu = gate * sigma
                state = state_ref[k, :, lanes].astype(F32)
                weighed = d_out * (state * scale)
                d_gain[:, lanes] += jnp.sum(weighed * silu, 0, keepdims=True)
                at = slice(k * rows, (k + 1) * rows)
                d_proj[at, 2 * chans + c * 128 : 2 * chans + (c + 1) * 128] = (
                    weighed * gain * silu_slope(gate, sigma)
                ).astype(BF16)
                out_gate[at, lanes] = (raw_ref[at, lanes].astype(F32) * scale).astype(BF16)
                d_state = scale * (d_out * gain * silu) - state * (
                    scale * scale * (dots[k] / width)
                )
                q_ref[n] = d_state.astype(BF16).astype(F32)
                edge = bound[:, lanes]
                forget = edge + (1.0 - edge) * jax.nn.sigmoid(fg_ref[k, :, lanes].astype(F32))
                p_ref[n] = forget * keep_ref[k]

    out_rows(0, 1)
    later = gather_forward(links, own, mixed_all, rows, s, fx, fy)
    serve(2)
    gather_middle(own)
    for copy in dot_copies:
        copy.wait_recv()
    out_rows(1, 2)
    serve(3)
    gather_far(later)
    out_rows(3, 1)
    serve(2)
    own_rows, mate_rows = pl.ds(0, tokens), pl.ds(tokens, tokens)
    last = pl.ds(2 * chans, chans)
    swaps = [
        links.start(out_gate.at[own_rows], out_gate.at[mate_rows], mate),
        links.start(d_proj.at[own_rows, last], d_proj.at[mate_rows, last], mate),
    ]
    wide = z_sum.block
    for t in range(n_seq // 2):
        theirs = pl.ds(pl.multiple_of((2 * t + 1 - core) * wide, wide), wide)
        swaps.append(
            links.start(mixed_all.at[:, theirs], mixed_mate.at[:, pl.ds(t * wide, wide)], mate)
        )

    def scan_step(i, carry):
        new = []
        at = pl.ds(step_len - 1 - i, 8, stride=step_len)
        for n, (product, message) in enumerate(carry):
            a = p_ref[n, at, :]
            acc = q_ref[n, at, :] + message
            p_ref[n, at, :] = product
            q_ref[n, at, :] = acc
            new.append((product * a, a * acc))
        return tuple(new)

    start = tuple((jnp.ones((8, 128), F32), jnp.zeros((8, 128), F32)) for _ in range(blocks))
    ends = lax.fori_loop(0, step_len, scan_step, start)
    for n, (product, message) in enumerate(ends):
        end_p[8 * n : 8 * n + 8] = product
        end_s[8 * n : 8 * n + 8] = message
    p_all, s_all = segment_totals(end_p, end_s, blocks, range(7, -1, -1))
    total[:blocks] = p_all
    total[blocks:] = s_all
    above = TotalsFromAbove(total, gathered, exchange_send, exchange_recv, n_seq)
    above.start()
    serve(1)
    above.relay()
    serve(1)
    above.wait()
    carry = jnp.zeros((blocks, 128), F32)
    for j in range(n_seq - 1, 0, -1):
        carry = jnp.where(j > s, gathered[j, blocks:] + gathered[j, :blocks] * carry, carry)
    spread_carry(carry, carr, end_p, end_s, blocks, range(7, -1, -1))

    def finish(n, _):
        enter_state = carr[pl.ds(pl.multiple_of(n * 8, 8), 8)]
        for i in range(step_len):
            at = pl.ds(i, 8, stride=step_len)
            q_ref[n, at, :] = q_ref[n, at, :] + p_ref[n, at, :] * enter_state
        return 0

    lax.fori_loop(0, blocks, finish, 0)
    d_bounds[...] = jnp.zeros_like(d_bounds)
    for k in range(4):
        at = slice(k * rows, (k + 1) * rows)
        for c, lanes in enumerate(lanes_of):
            acc = q_ref[k * count + c]
            edge = bound[:, lanes]
            sigma_f = jax.nn.sigmoid(fg_ref[k, :, lanes].astype(F32))
            forget = edge + (1.0 - edge) * sigma_f
            value = in_ref[k, :, lanes].astype(F32)
            sigma_i = jax.nn.sigmoid(value)
            d_forget = acc * (before[k * count + c] * keep_ref[k] - value * sigma_i)
            d_proj[at, lanes] = (acc * (1.0 - forget) * silu_slope(value, sigma_i)).astype(BF16)
            d_sigma = d_forget * (1.0 - sigma_f)
            d_proj[at, chans + c * 128 : chans + (c + 1) * 128] = (
                d_sigma * (1.0 - edge) * sigma_f
            ).astype(BF16)
            d_bounds[:, lanes] += jnp.sum(d_sigma, 0, keepdims=True)
    first = pl.ds(0, 2 * chans)
    swaps.append(links.start(d_proj.at[own_rows, first], d_proj.at[mate_rows, first], mate))
    serve(2)
    for copy in weights:
        copy.wait()

    def normed_part(first_slot, slots):
        at = slice(first_slot * rows, (first_slot + slots) * rows)

        def tile_of(n, _):
            cols = tile(n, 512)
            rows_part[at, cols] = mm_t(d_proj[at], wv[cols]).astype(BF16)
            return 0

        lax.fori_loop(0, width // 512, tile_of, 0)

    normed_part(3, 1)
    far = reduce_start_far(links, rows_part, from_x, from_y, rows, s, fx, fy)
    normed_part(1, 2)
    near = reduce_start_near(links, rows_part, from_x, from_y, rows, s, fx, fy)
    normed_part(0, 1)
    serve(3)
    for copy in swaps:
        copy.wait_recv()

    def tile_out(t):
        slot = lax.rem(t, 2)
        return pltpu.make_async_copy(
            wo.at[tile(slot, wide)], mixer_part.at[z_sum.rows(t)], tile_sems.at[slot]
        )

    def mixer_tile(t, _):
        @pl.when(t >= 2)
        def _():
            tile_out(t - 2).wait()

        at = tile(lax.rem(t, 2), wide)
        ours = mixed_all[:, tile(2 * t + core, wide)]
        out_part = mm_tokens(ours, out_gate[:tokens])
        out_part = out_part + mm_tokens(mixed_mate[:, tile(t, wide)], out_gate[tokens:])
        wo[at, :chans] = out_part.astype(BF16)
        wo[at, chans:] = mm_tokens(normed_ref[:, tile(t, wide)], d_proj[...]).astype(BF16)
        tile_out(t).start()
        return 0

    lax.fori_loop(0, 1, mixer_tile, 0)
    passed = reduce_pass(links, far, rows_part, from_x, from_y, pass_x, pass_y, rows, s, fx, fy)
    serve(1)
    lax.fori_loop(1, z_sum.nz, mixer_tile, 0)
    serve(2)
    for copy in near + passed:
        copy.wait_recv()
    half = rows // 2
    d_normed[:half] = rows_part[:half].astype(F32) + from_x[1].astype(F32) + from_y[2].astype(F32)
    d_normed[half:] = (
        rows_part[half:rows].astype(F32) + from_y[1].astype(F32) + from_x[2].astype(F32)
    )
    outs.append(local.start(d_normed, rows_out.at[pl.ds(0, rows)]))
    sums_ref[...] = jnp.zeros_like(sums_ref)
    sums_ref[0:1] = d_glu_gain[...]
    sums_ref[1:2, :chans] = d_gain[...]
    sums_ref[2:3, :chans] = d_bounds[...]
    outs.append(local.start(sums_ref, rows_out.at[pl.ds(2 * rows, 8)]))
    z_sum.serve_range(served, z_sum.calls, True)
    z_sum.drain()
    above.drain()
    sends_done(own, later, dot_copies, swaps, far, near, passed)
    for t in range(z_sum.nz - 2, z_sum.nz):
        tile_out(jnp.int32(t)).wait()
    wait_all(outs)


def pair_sum(
    lengths, own_rows, gains, table, scale_g, float_rows, pair_part, weights, saved, normed_half, cid
):
    n_seq = lax.axis_size("seq")
    rows, width = own_rows[0].shape
    chans = weights[1].shape[1]
    own, columns = pair_part.shape
    tokens = 4 * rows
    blocks = 4 * chans // 128
    block = width // n_seq
    half = (rows // 2, width)
    shape = jax.ShapeDtypeStruct
    count = 18 + n_seq // 2
    return pl.pallas_call(
        functools.partial(pair_kernel, n_seq),
        out_shape=(
            shape((block, columns), F32),
            shape((own, 4 * chans), BF16),
            shape((2 * rows + 8, width), F32),
        ),
        in_specs=[pl.BlockSpec(memory_space=pltpu.SMEM)] + [VMEM] * 6 + [ANY] * 14,
        out_specs=(ANY,) * 3,
        scratch_shapes=[
            pltpu.VMEM((8, width), F32),
            pltpu.VMEM((1, width), F32),
            pltpu.VMEM((1, chans), F32),
            pltpu.VMEM((1, chans), F32),
            pltpu.VMEM((rows, width), F32),
            pltpu.VMEM((rows, width), F32),
            pltpu.VMEM((block, columns), F32),
            pltpu.VMEM((own, columns), BF16),
            pltpu.VMEM((own + block, columns), BF16),
            pltpu.VMEM((chans, width), BF16),
            pltpu.VMEM((width, 3 * chans), BF16),
            pltpu.VMEM((tokens, width), BF16),
            pltpu.VMEM((tokens, width // 2), BF16),
            pltpu.VMEM((2 * tokens, width // 2), BF16),
            pltpu.VMEM((2 * tokens, 3 * chans), BF16),
            pltpu.VMEM((2 * tokens, chans), BF16),
            pltpu.VMEM((4, rows, chans), F32),
            pltpu.VMEM((4, rows, chans), BF16),
            pltpu.VMEM((tokens, chans), BF16),
            pltpu.VMEM((4, rows, chans), BF16),
            pltpu.VMEM((4, rows, chans), BF16),
            pltpu.VMEM((blocks, rows, 128), F32),
            pltpu.VMEM((blocks, rows, 128), F32),
            pltpu.VMEM((blocks, rows, 128), F32),
            pltpu.VMEM((2 * rows, chans), F32),
            pltpu.VMEM((tokens, width), BF16),
            pltpu.VMEM((3,) + half, BF16),
            pltpu.VMEM((3,) + half, BF16),
            pltpu.VMEM(half, BF16),
            pltpu.VMEM(half, BF16),
            pltpu.VMEM((4, rows, 128), F32),
            pltpu.VMEM((4, rows, 128), F32),
            pltpu.VMEM((8 * blocks, 128), F32),
            pltpu.VMEM((8 * blocks, 128), F32),
            pltpu.VMEM((8 * blocks, 128), F32),
            pltpu.VMEM((2 * blocks, 128), F32),
            pltpu.VMEM((n_seq, 2 * blocks, 128), F32),
            pltpu.SemaphoreType.DMA((count,)),
            pltpu.SemaphoreType.DMA((count,)),
            pltpu.SemaphoreType.DMA((n_seq + 1,)),
            pltpu.SemaphoreType.DMA((n_seq,)),
            pltpu.SemaphoreType.DMA((16 + n_seq // 2,)),
            pltpu.SemaphoreType.DMA((2,)),
        ]
        + line_sems(n_seq, columns, 256),
        compiler_params=params(cid),
        name="pair_sum",
    )(
        lengths,
        *own_rows,
        *gains,
        table,
        scale_g,
        *float_rows,
        pair_part,
        *weights,
        *saved,
        normed_half,
    )


def final_kernel(
    n_seq,
    n_fsdp,
    hidden,
    norm_gain,
    table,
    float_rows,
    middle_in,
    mixer_part,
    act_pair,
    w_down,
    output_out,
    d_hidden_out,
    out_grad,
    rest_grad,
    norm_out,
    glu_out,
    gate_out,
    d_table,
    sums_ref,
    d_normed,
    d_middle,
    middle,
    output,
    d_hidden,
    out_ref,
    rest_ref,
    part,
    buf,
    act,
    wd,
    rows_part,
    from_x,
    from_y,
    pass_x,
    pass_y,
    norm_sum,
    bounds_out,
    terms,
    quarters_in,
    terms_q,
    from_mate,
    terms_chip,
    over_seq,
    along_sum,
    over_fsdp,
    send,
    recv,
    local_sems,
    *line,
):
    rows, width = hidden.shape
    chans = out_grad.shape[0]
    tokens = 4 * rows
    s, f, fx, fy, fd = plane()
    links, local = Links(send, recv), Locals(local_sems)
    head = chans // 256

    def store(j, value):
        @pl.when(j < head)
        def _():
            out_ref[tile(j, 256)] = value.T

        @pl.when(j >= head)
        def _():
            rest_ref[:, tile(j - head, 256)] = value

    def leave(j, start):
        @pl.when(j < head)
        def _():
            at = tile(j, 256)
            copy = pltpu.make_async_copy(out_ref.at[at], out_grad.at[at], line[4].at[j])
            start_or_wait(copy, start)

        @pl.when(j >= head)
        def _():
            at = tile(j - head, 256)
            copy = pltpu.make_async_copy(rest_ref.at[:, at], rest_grad.at[:, at], line[4].at[j])
            start_or_wait(copy, start)

    z_sum = ZLine(part, buf, line, n_seq, 256, 2, 6, store, leave)
    blocks_in = z_sum.load(local, mixer_part, 0, 1)
    along = seq_peers(n_seq)
    across = [(s, fx), (s, fy), (s, fd)]
    enter(across + along)
    blocks_in[0].wait()
    z_sum.feed_first()
    loads = [local.start(act_pair.at[pl.ds(0, tokens)], act), local.start(w_down, wd)]
    blocks_in = z_sum.load(local, mixer_part, 1, z_sum.nz)
    rows_in = [
        local.start(src, dst)
        for src, dst in (
            (float_rows.at[pl.ds(0, rows)], d_normed),
            (float_rows.at[pl.ds(rows, rows)], d_middle),
            (float_rows.at[pl.ds(2 * rows, 8)], sums_ref),
            (middle_in, middle),
        )
    ]
    served = 0

    def serve(number):
        nonlocal served
        z_sum.serve_range(served, served + number)
        served += number

    norm_sum[...] = jnp.zeros_like(norm_sum)

    def hidden_rows(i, _):
        at = pl.ds(pl.multiple_of(i * 16, 16), 16)
        value, came = hidden[at].astype(F32), d_normed[at]
        scale = lax.rsqrt(jnp.mean(value * value, -1, keepdims=True) + epsilon)
        scaled = norm_gain[...] * came
        mean = jnp.mean(scaled * value, -1, keepdims=True)
        d_hidden[at] = (d_middle[at] + scale * scaled - value * (scale**3 * mean)).astype(BF16)
        norm_sum[...] += jnp.sum(came * value * scale, 0, keepdims=True)
        return 0

    wait_all(loads)

    def glu_part(first, slots):
        at = slice(first * rows, (first + slots) * rows)

        def tile_of(n, _):
            cols = tile(n, 512)
            rows_part[at, cols] = mm(act[at], wd[:, cols]).astype(BF16)
            return 0

        lax.fori_loop(0, width // 512, tile_of, 0)

    glu_part(3, 1)
    far = reduce_start_far(links, rows_part, from_x, from_y, rows, s, fx, fy)
    glu_part(1, 2)
    near = reduce_start_near(links, rows_part, from_x, from_y, rows, s, fx, fy)
    glu_part(0, 1)
    wait_all(blocks_in, rows_in)
    serve(2)
    lax.fori_loop(0, rows // 16, hidden_rows, 0)
    terms[...] = jnp.zeros_like(terms)
    for q in range(4):
        terms[q, 0:1] = norm_sum[:, q * chans : (q + 1) * chans]
        terms[q, 1:2] = sums_ref[0:1, q * chans : (q + 1) * chans]
    quarter_copies = [
        links.start(terms.at[peer], quarters_in.at[k], (s, peer))
        for k, peer in enumerate((fx, fy, fd))
    ]
    serve(1)
    passed = reduce_pass(links, far, rows_part, from_x, from_y, pass_x, pass_y, rows, s, fx, fy)
    serve(2)
    quarter = terms[pl.ds(f, 1)][0]
    for k, copy in enumerate(quarter_copies):
        copy.wait_recv()
        quarter = quarter + quarters_in[k]
    half = chans // 2
    for first, cols in ((0, slice(0, half)), (4, slice(half, chans))):
        terms_q[first : first + 2] = quarter[:2, cols]
        terms_q[first + 2 : first + 3] = sums_ref[1:2, cols]
        terms_q[first + 3 : first + 4] = sums_ref[2:3, cols]
    mate_copy = links.start(terms_q, from_mate, (s + 1 - 2 * (s % 2), f))
    serve(1)
    serve(2)
    for copy in near + passed:
        copy.wait_recv()
    middle_half = rows // 2
    for first, one, other in (
        (0, from_x.at[1], from_y.at[2]),
        (middle_half, from_y.at[1], from_x.at[2]),
    ):
        at = slice(first, first + middle_half)
        added = rows_part[at].astype(F32) + one[...].astype(F32) + other[...].astype(F32)
        output[at] = (middle[at] + added).astype(BF16)
    mate_copy.wait_recv()
    terms_chip[...] = terms_q[...] + from_mate[...]
    seq_copies = [
        links.start(terms_chip, over_seq.at[k], peer) for k, peer in enumerate(z_peers(n_seq))
    ]
    serve(2)
    total = terms_chip[...]
    for k, copy in enumerate(seq_copies):
        copy.wait_recv()
        total = total + over_seq[k]
    along_sum[...] = total
    fsdp_copies = [links.start(along_sum, over_fsdp.at[k], peer) for k, peer in enumerate(across)]
    serve(2)
    for copy in fsdp_copies:
        copy.wait_recv()
    for k, group in enumerate((f, fx, fy, fd)):
        total = along_sum[...] if k == 0 else over_fsdp[k - 1]
        for i in range(2):
            at = pl.ds(pl.multiple_of(group * chans + i * half, 128), half)
            for r, out in enumerate((norm_out, glu_out, gate_out, bounds_out)):
                out[:, at] = total[4 * i + r : 4 * i + r + 1]
    powers = jnp.exp(table[...] - jnp.max(table[...], 0, keepdims=True))
    soft = powers / jnp.sum(powers, 0, keepdims=True)
    row = lax.broadcasted_iota(jnp.int32, soft.shape, 0)
    chosen = jnp.where((row >= 1) & (row <= LAYER), 1.0, 0.0)
    bound = jnp.sum(soft * chosen, 0, keepdims=True)
    d_table[...] = soft * (chosen - bound) * bounds_out[...]
    outs = [local.start(output, output_out), local.start(d_hidden, d_hidden_out)]
    z_sum.serve_range(served, z_sum.calls, True)
    z_sum.drain()
    wait_all(outs)
    sends_done(far, near, passed, quarter_copies, [mate_copy], seq_copies, fsdp_copies)


def final_sum(hidden, norm_gain, table, float_rows, middle, mixer_part, act_pair, w_down, cid):
    n_seq, n_fsdp = lax.axis_size("seq"), lax.axis_size("fsdp")
    rows, width = hidden.shape
    own, columns = mixer_part.shape
    units = w_down.shape[0]
    chans = columns // 4
    tokens = 4 * rows
    block = width // n_seq
    half = (rows // 2, width)
    terms = (8, chans // 2)
    shape = jax.ShapeDtypeStruct
    count = 6 + n_seq // 2 + 2 * (n_fsdp - 1)
    return pl.pallas_call(
        functools.partial(final_kernel, n_seq, n_fsdp),
        out_shape=(
            shape((rows, width), BF16),
            shape((rows, width), BF16),
            shape((chans, block), F32),
            shape((block, 3 * chans), F32),
            shape((1, width), F32),
            shape((1, width), F32),
            shape((1, width), F32),
            shape(table.shape, F32),
        ),
        in_specs=[VMEM] * 3 + [ANY] * 5,
        out_specs=(ANY,) * 4 + (VMEM,) * 4,
        scratch_shapes=[
            pltpu.VMEM((8, width), F32),
            pltpu.VMEM((rows, width), F32),
            pltpu.VMEM((rows, width), F32),
            pltpu.VMEM((rows, width), F32),
            pltpu.VMEM((rows, width), BF16),
            pltpu.VMEM((rows, width), BF16),
            pltpu.VMEM((chans, block), F32),
            pltpu.VMEM((block, 3 * chans), F32),
            pltpu.VMEM((own, columns), BF16),
            pltpu.VMEM((own + block, columns), BF16),
            pltpu.VMEM((tokens, units), BF16),
            pltpu.VMEM((units, width), BF16),
            pltpu.VMEM((tokens, width), BF16),
            pltpu.VMEM((3,) + half, BF16),
            pltpu.VMEM((3,) + half, BF16),
            pltpu.VMEM(half, BF16),
            pltpu.VMEM(half, BF16),
            pltpu.VMEM((1, width), F32),
            pltpu.VMEM((1, width), F32),
            pltpu.VMEM((n_fsdp, 8, chans), F32),
            pltpu.VMEM((n_fsdp - 1, 8, chans), F32),
            pltpu.VMEM(terms, F32),
            pltpu.VMEM(terms, F32),
            pltpu.VMEM(terms, F32),
            pltpu.VMEM((n_seq // 2 - 1,) + terms, F32),
            pltpu.VMEM(terms, F32),
            pltpu.VMEM((n_fsdp - 1,) + terms, F32),
            pltpu.SemaphoreType.DMA((count,)),
            pltpu.SemaphoreType.DMA((count,)),
            pltpu.SemaphoreType.DMA((8 + n_seq // 2,)),
        ]
        + line_sems(n_seq, columns, 256),
        compiler_params=params(cid, 48),
        name="final_sum",
    )(hidden, norm_gain, table, float_rows, middle, mixer_part, act_pair, w_down)


def hand_over_kernel(count, pieces, *refs):
    sources, targets = refs[: len(refs) - 2 * count - 2], refs[len(refs) - 2 * count - 2 :]
    kept, arrived, left = targets[count : 2 * count], targets[2 * count], targets[2 * count + 1]
    loads, stores = [], []
    for n, (i, source, first, rows, column) in enumerate(pieces):
        at = pl.ds(first, rows)
        src = sources[source].at[at, pl.ds(column, kept[i].shape[1])]
        loads.append(copy_in(src, kept[i].at[at], arrived.at[n]))
    for n, (i, source, first, rows, column) in enumerate(pieces):
        at = pl.ds(first, rows)
        loads[n].wait()
        stores.append(copy_in(kept[i].at[at], targets[i].at[at], left.at[n]))
    for store in stores:
        store.wait()


def hand_over(arrays, wanted):
    pieces, shapes = [], []
    for i, (source, column, columns) in enumerate(wanted):
        x = arrays[source]
        height = x.shape[0]
        parts = max(1, height * columns * x.dtype.itemsize >> 18)
        parts = parts if height % (parts * 16) == 0 else 1
        rows = height // parts
        pieces += [(i, source, n * rows, rows, column) for n in range(parts)]
        shapes.append(((height, columns), x.dtype))
    return pl.pallas_call(
        functools.partial(hand_over_kernel, len(wanted), tuple(pieces)),
        out_shape=tuple(jax.ShapeDtypeStruct(*x) for x in shapes),
        in_specs=[ANY] * len(arrays),
        out_specs=(ANY,) * len(wanted),
        scratch_shapes=[pltpu.VMEM(*x) for x in shapes]
        + [pltpu.SemaphoreType.DMA((len(pieces),))] * 2,
        compiler_params=pltpu.CompilerParams(vmem_limit_bytes=16 << 20),
        name="hand_over",
    )(*arrays)


def plane_device(
    hidden,
    lengths,
    w_input,
    w_forget,
    w_gate_out,
    w_output,
    norm_gain,
    gate_gain,
    glu_gain,
    lower_table,
    w_glu_gate,
    w_glu_up,
    w_glu_down,
    cotangent,
):
    hidden, cotangent = hidden[0], cotangent[0]
    tokens = 4 * hidden.shape[0]
    gains = (norm_gain[None], gate_gain[None], glu_gain[None])
    (
        normed_half,
        cot_all,
        in_raw,
        fg_raw,
        gate_raw,
        state_b,
        out_raw,
        before,
        scale_g,
        middle,
        normed_two,
    ) = mixer_forward(
        lengths,
        hidden,
        cotangent,
        gains,
        lower_table,
        (w_input, w_forget, w_gate_out, w_output),
        0,
    )
    two_half, cot_half, act_pair, gate_pair, up_pair = glu(
        normed_two, cot_all, w_glu_gate, w_glu_up, w_glu_down, 1
    )
    d_normed_two, pair_part, down_grad = down_sum(
        *(x.reshape(2 * tokens, -1) for x in (cot_half, act_pair, two_half, gate_pair, up_pair)),
        w_glu_gate,
        w_glu_up,
        2,
    )
    pair_grad, mixer_part, float_rows = pair_sum(
        lengths,
        (hidden, cotangent),
        (gains[2], gains[1]),
        lower_table,
        scale_g,
        (d_normed_two, middle),
        pair_part,
        (w_output, w_input, w_forget, w_gate_out),
        (gate_raw, state_b, out_raw, in_raw, fg_raw, before),
        normed_half.reshape(2 * tokens, -1),
        3,
    )
    output, d_hidden, out_grad, rest_grad, *sums, d_table = final_sum(
        hidden,
        gains[0],
        lower_table,
        float_rows,
        middle,
        mixer_part,
        act_pair.reshape(2 * tokens, -1),
        w_glu_down,
        4,
    )
    width, chans, units = hidden.shape[1], w_input.shape[1], w_glu_gate.shape[1]
    block = down_grad.shape[1]
    (
        down_grad,
        gate_grad,
        up_grad,
        output,
        d_hidden,
        d_table,
        out_grad,
        in_grad,
        fg_grad,
        gt_grad,
        *sums,
    ) = hand_over(
        (down_grad, pair_grad, output, d_hidden, d_table, out_grad, rest_grad, *sums),
        (
            (0, 0, block),
            (1, 0, units),
            (1, units, units),
            (2, 0, width),
            (3, 0, width),
            (4, 0, width),
            (5, 0, block),
            (6, 0, chans),
            (6, chans, chans),
            (6, 2 * chans, chans),
            (7, 0, width),
            (8, 0, width),
            (9, 0, width),
        ),
    )
    return (
        output[None],
        d_hidden[None],
        in_grad,
        fg_grad,
        gt_grad,
        out_grad,
        sums[0][0],
        sums[2][0],
        sums[1][0],
        d_table,
        gate_grad,
        up_grad,
        down_grad,
    )


def fits_plane(mesh):
    return mesh.shape["fsdp"] == 4 and mesh.shape["seq"] % 2 == 0


def solution(mesh):
    rows_spec = P("fsdp", "seq", None)
    columns = P(None, "fsdp")
    placed = (
        rows_spec,
        P(),
        columns,
        columns,
        columns,
        P("fsdp", None),
        P(),
        P(),
        P(),
        P(),
        columns,
        columns,
        P("fsdp", None),
        rows_spec,
    )
    by_rows, by_columns = P("seq", "fsdp"), P("fsdp", "seq")
    return jax.shard_map(
        plane_device if fits_plane(mesh) else per_device,
        mesh=mesh,
        in_specs=placed,
        out_specs=(
            rows_spec,
            rows_spec,
            by_rows,
            by_rows,
            by_rows,
            by_columns,
            P(),
            P(),
            P(),
            P(),
            by_rows,
            by_rows,
            by_columns,
        ),
        check_vma=False,
    )
```

```python
import functools

import jax
import jax.numpy as jnp
from jax import lax
from jax.experimental import pallas as pl
from jax.experimental.pallas import tpu as pltpu
from jax.sharding import PartitionSpec as P

LAYER = 12
MESH = pl.DeviceIdType.MESH
F32 = jnp.float32
BF16 = jnp.bfloat16

epsilon = 1e-06

VMEM = pl.BlockSpec(memory_space=pltpu.VMEM)
ANY = pl.BlockSpec(memory_space=pl.ANY)


def lower_bound(table):
    soft = jax.nn.softmax(table, axis=0)
    totals = jnp.cumsum(soft, axis=0)
    return totals[LAYER] - totals[0]


def silu_slope(value, sigma):
    return sigma * (1.0 + value * (1.0 - sigma))


def params(collective_id, limit=56):
    return pltpu.CompilerParams(
        collective_id=collective_id, has_side_effects=True, vmem_limit_bytes=limit << 20
    )


def round_up(value, unit):
    return -(-value // unit) * unit


def plane():
    s = lax.axis_index("seq")
    f = lax.axis_index("fsdp")
    y, x = f // 2, f % 2
    fx = y * 2 + (1 - x)
    fy = (1 - y) * 2 + x
    fd = (1 - y) * 2 + (1 - x)
    return s, f, fx, fy, fd


def enter(devices):
    barrier = pltpu.get_barrier_semaphore()
    for device in devices:
        pl.semaphore_signal(barrier, inc=1, device_id=device, device_id_type=MESH)
    pl.semaphore_wait(barrier, len(devices))


def remote(src, dst, send, recv, device):
    return pltpu.make_async_remote_copy(
        src_ref=src,
        dst_ref=dst,
        send_sem=send,
        recv_sem=recv,
        device_id=device,
        device_id_type=MESH,
    )


def gather(x, small, collective_id):
    return lax.all_gather(x, "fsdp"), lax.all_gather(small, "fsdp")


def reduce_rows(p, small, collective_id):
    total = lax.psum_scatter(p, "fsdp", scatter_dimension=0, tiled=True)[0]
    return total.astype(F32), lax.psum(small, "fsdp")


def start_exchange(total, gathered, send, recv, n_seq):
    s = lax.axis_index("seq")
    f = lax.axis_index("fsdp")
    copies = []
    for k in range(1, n_seq):
        peer = lax.rem(s + k, n_seq)
        copy = remote(total, gathered.at[s], send.at[k], recv.at[k], (peer, f))
        copy.start()
        copies.append(copy)
    gathered[pl.ds(s, 1)] = total[...][None]
    return copies


def seq_peers(n_seq):
    s = lax.axis_index("seq")
    f = lax.axis_index("fsdp")
    return [(lax.rem(s + k, n_seq), f) for k in range(1, n_seq)]


def lane_blocks(groups, chans):
    return [(g, slice(c, c + 128)) for g in range(groups) for c in range(0, chans, 128)]


def forward_scan_kernel(
    n_seq, in_raw, forget_raw, bounds, keep, state_b, before, a_ref, b_ref, total, gathered, send, recv
):
    groups, rows, chans = in_raw.shape
    part = rows // 8
    blocks = lane_blocks(groups, chans)
    s = lax.axis_index("seq")
    barrier = pltpu.get_barrier_semaphore()
    for peer in seq_peers(n_seq):
        pl.semaphore_signal(barrier, inc=1, device_id=peer, device_id_type=MESH)
    for n, (g, lanes) in enumerate(blocks):
        bound = bounds[:, lanes]
        forget = bound + (1.0 - bound) * jax.nn.sigmoid(forget_raw[g, :, lanes].astype(F32))
        value = in_raw[g, :, lanes].astype(F32)
        a_ref[n] = forget * keep[g]
        b_ref[n] = value * jax.nn.sigmoid(value) * (1.0 - forget)

    def step(i, carry):
        new = []
        at = pl.ds(i, 8, stride=part)
        for n, (product, state) in enumerate(carry):
            a = a_ref[n, at, :]
            state = a * state + b_ref[n, at, :]
            product = product * a
            a_ref[n, at, :] = product
            b_ref[n, at, :] = state
            new.append((product, state))
        return tuple(new)

    start = tuple((jnp.ones((8, 128), F32), jnp.zeros((8, 128), F32)) for _ in blocks)
    ends = lax.fori_loop(0, part, step, start)
    for n, (product, state) in enumerate(ends):
        p_all, s_all = product[0:1], state[0:1]
        for j in range(1, 8):
            p_all, s_all = p_all * product[j : j + 1], state[j : j + 1] + product[j : j + 1] * s_all
        total[2 * n : 2 * n + 1] = p_all
        total[2 * n + 1 : 2 * n + 2] = s_all
    pl.semaphore_wait(barrier, n_seq - 1)
    copies = start_exchange(total, gathered, send, recv, n_seq)
    for copy in copies:
        copy.wait()
    for n, (g, lanes) in enumerate(blocks):
        carry = jnp.zeros((1, 128), F32)
        for j in range(n_seq - 1):
            p_j = gathered[j, 2 * n : 2 * n + 1]
            s_j = gathered[j, 2 * n + 1 : 2 * n + 2]
            carry = jnp.where(j < s, s_j + p_j * carry, carry)
        before[g, 0:1, lanes] = carry
        product, state = ends[n]
        carries = [carry]
        for j in range(7):
            carries.append(state[j : j + 1] + product[j : j + 1] * carries[-1])
        for j in range(8):
            at = slice(j * part, (j + 1) * part)
            b_ref[n, at] = b_ref[n, at] + a_ref[n, at] * carries[j]
        state_b[g, :, lanes] = b_ref[n].astype(BF16)
        before[g, 1:rows, lanes] = b_ref[n, 0 : rows - 1]


def forward_scan(in_raw, forget_raw, bounds, keep, collective_id):
    n_seq = lax.axis_size("seq")
    groups, rows, chans = in_raw.shape
    blocks = groups * chans // 128
    return pl.pallas_call(
        functools.partial(forward_scan_kernel, n_seq),
        out_shape=(
            jax.ShapeDtypeStruct(in_raw.shape, BF16),
            jax.ShapeDtypeStruct(in_raw.shape, F32),
        ),
        in_specs=[VMEM] * 4,
        out_specs=(VMEM, VMEM),
        scratch_shapes=[
            pltpu.VMEM((blocks, rows, 128), F32),
            pltpu.VMEM((blocks, rows, 128), F32),
            pltpu.VMEM((2 * blocks, 128), F32),
            pltpu.VMEM((n_seq, 2 * blocks, 128), F32),
            pltpu.SemaphoreType.DMA((n_seq,)),
            pltpu.SemaphoreType.DMA((n_seq,)),
        ],
        compiler_params=params(collective_id),
        name="forward_scan",
    )(in_raw, forget_raw, bounds, keep)


def backward_scan_kernel(
    n_seq,
    d_state,
    in_raw,
    forget_raw,
    before,
    bounds,
    keep,
    d_in,
    d_forget_raw,
    d_bounds,
    p_ref,
    q_ref,
    total,
    gathered,
    send,
    recv,
):
    groups, rows, chans = in_raw.shape
    part = rows // 8
    blocks = lane_blocks(groups, chans)
    s = lax.axis_index("seq")
    barrier = pltpu.get_barrier_semaphore()
    for peer in seq_peers(n_seq):
        pl.semaphore_signal(barrier, inc=1, device_id=peer, device_id_type=MESH)
    for n, (g, lanes) in enumerate(blocks):
        bound = bounds[:, lanes]
        forget = bound + (1.0 - bound) * jax.nn.sigmoid(forget_raw[g, :, lanes].astype(F32))
        p_ref[n] = forget * keep[g]
        q_ref[n] = d_state[g, :, lanes].astype(F32)

    def step(i, carry):
        new = []
        at = pl.ds(part - 1 - i, 8, stride=part)
        for n, (product, message) in enumerate(carry):
            a = p_ref[n, at, :]
            acc = q_ref[n, at, :] + message
            p_ref[n, at, :] = product
            q_ref[n, at, :] = acc
            new.append((product * a, a * acc))
        return tuple(new)

    start = tuple((jnp.ones((8, 128), F32), jnp.zeros((8, 128), F32)) for _ in blocks)
    ends = lax.fori_loop(0, part, step, start)
    for n, (product, message) in enumerate(ends):
        p_all, m_all = product[7:8], message[7:8]
        for j in range(6, -1, -1):
            p_all, m_all = p_all * product[j : j + 1], message[j : j + 1] + product[j : j + 1] * m_all
        total[2 * n : 2 * n + 1] = p_all
        total[2 * n + 1 : 2 * n + 2] = m_all
    pl.semaphore_wait(barrier, n_seq - 1)
    copies = start_exchange(total, gathered, send, recv, n_seq)
    for copy in copies:
        copy.wait()
    d_bounds[...] = jnp.zeros((1, chans), F32)
    for n, (g, lanes) in enumerate(blocks):
        carry = jnp.zeros((1, 128), F32)
        for j in range(n_seq - 1, 0, -1):
            p_j = gathered[j, 2 * n : 2 * n + 1]
            m_j = gathered[j, 2 * n + 1 : 2 * n + 2]
            carry = jnp.where(j > s, m_j + p_j * carry, carry)
        product, message = ends[n]
        carries = [carry]
        for j in range(7, 0, -1):
            carries.append(message[j : j + 1] + product[j : j + 1] * carries[-1])
        carries = carries[::-1]
        for j in range(8):
            at = slice(j * part, (j + 1) * part)
            q_ref[n, at] = q_ref[n, at] + p_ref[n, at] * carries[j]
        acc = q_ref[n]
        bound = bounds[:, lanes]
        sigma_f = jax.nn.sigmoid(forget_raw[g, :, lanes].astype(F32))
        forget = bound + (1.0 - bound) * sigma_f
        value = in_raw[g, :, lanes].astype(F32)
        sigma_i = jax.nn.sigmoid(value)
        d_forget = acc * (before[g, :, lanes] * keep[g] - value * sigma_i)
        d_in[g, :, lanes] = (acc * (1.0 - forget) * silu_slope(value, sigma_i)).astype(BF16)
        d_sigma = d_forget * (1.0 - sigma_f)
        d_forget_raw[g, :, lanes] = (d_sigma * (1.0 - bound) * sigma_f).astype(BF16)
        d_bounds[:, lanes] += jnp.sum(d_sigma, 0, keepdims=True)


def backward_scan(d_state, in_raw, forget_raw, before, bounds, keep, collective_id):
    n_seq = lax.axis_size("seq")
    groups, rows, chans = in_raw.shape
    blocks = groups * chans // 128
    return pl.pallas_call(
        functools.partial(backward_scan_kernel, n_seq),
        out_shape=(
            jax.ShapeDtypeStruct(in_raw.shape, BF16),
            jax.ShapeDtypeStruct(in_raw.shape, BF16),
            jax.ShapeDtypeStruct((1, chans), F32),
        ),
        in_specs=[VMEM] * 6,
        out_specs=(VMEM, VMEM, VMEM),
        scratch_shapes=[
            pltpu.VMEM((blocks, rows, 128), F32),
            pltpu.VMEM((blocks, rows, 128), F32),
            pltpu.VMEM((2 * blocks, 128), F32),
            pltpu.VMEM((n_seq, 2 * blocks, 128), F32),
            pltpu.SemaphoreType.DMA((n_seq,)),
            pltpu.SemaphoreType.DMA((n_seq,)),
        ],
        compiler_params=params(collective_id),
        name="backward_scan",
    )(d_state, in_raw, forget_raw, before, bounds, keep)


def sum_all_kernel(n_seq, n_fsdp, x, out, middle, over_seq, over_fsdp, send, recv):
    s = lax.axis_index("seq")
    f = lax.axis_index("fsdp")
    along = [(lax.rem(s + k, n_seq), f) for k in range(1, n_seq)]
    across = [(s, lax.rem(f + k, n_fsdp)) for k in range(1, n_fsdp)]
    enter(along + across)
    copies = []
    for k, peer in enumerate(along):
        copy = remote(x, over_seq.at[k], send.at[k], recv.at[k], peer)
        copy.start()
        copies.append(copy)
    total = x[...]
    for k, copy in enumerate(copies):
        copy.wait_recv()
        total = total + over_seq[k]
    middle[...] = total
    later = []
    for k, peer in enumerate(across):
        slot = n_seq - 1 + k
        copy = remote(middle, over_fsdp.at[k], send.at[slot], recv.at[slot], peer)
        copy.start()
        later.append(copy)
    for k, copy in enumerate(later):
        copy.wait_recv()
        total = total + over_fsdp[k]
    out[...] = total
    for copy in copies + later:
        copy.wait_send()


def sum_all(x, collective_id):
    n_seq, n_fsdp = lax.axis_size("seq"), lax.axis_size("fsdp")
    count = n_seq + n_fsdp - 2
    return pl.pallas_call(
        functools.partial(sum_all_kernel, n_seq, n_fsdp),
        out_shape=jax.ShapeDtypeStruct(x.shape, F32),
        in_specs=[VMEM],
        out_specs=VMEM,
        scratch_shapes=[
            pltpu.VMEM(x.shape, F32),
            pltpu.VMEM((n_seq - 1,) + x.shape, F32),
            pltpu.VMEM((n_fsdp - 1,) + x.shape, F32),
            pltpu.SemaphoreType.DMA((count,)),
            pltpu.SemaphoreType.DMA((count,)),
        ],
        compiler_params=params(collective_id),
        name="sum_all",
    )(x)


def sum_over_seq(part):
    return lax.psum_scatter(part.astype(BF16), "seq", scatter_dimension=0, tiled=True).astype(F32)


def per_device(
    hidden,
    lengths,
    w_input,
    w_forget,
    w_gate_out,
    w_output,
    norm_gain,
    gate_gain,
    glu_gain,
    lower_table,
    w_glu_gate,
    w_glu_up,
    w_glu_down,
    cotangent,
):
    seq_index = lax.axis_index("seq")
    fsdp_index = lax.axis_index("fsdp")
    groups = lax.axis_size("fsdp")
    _, rows, width = hidden.shape
    chans = w_input.shape[1]
    units = w_glu_gate.shape[1]
    tokens = groups * rows
    small_shape = (round_up(groups, 8), round_up(rows, 128))

    def to_small(value):
        return jnp.pad(
            value, ((0, small_shape[0] - value.shape[0]), (0, small_shape[1] - value.shape[1]))
        )

    def dot(left, right):
        return jnp.dot(left, right, preferred_element_type=F32)

    def dot_t(left, right):
        return lax.dot_general(left, right, (((1,), (1,)), ((), ())), preferred_element_type=F32)

    def over_tokens(left, right):
        return lax.dot_general(left, right, (((0,), (0,)), ((), ())), preferred_element_type=F32)

    cotangent_all = lax.all_gather(cotangent[0], "fsdp").reshape(tokens, width)

    hidden_f = hidden[0].astype(F32)
    scale_one = lax.rsqrt(jnp.mean(hidden_f * hidden_f, -1, keepdims=True) + epsilon)
    normed = (hidden_f * scale_one * norm_gain).astype(BF16)
    normed_all, _ = gather(normed, jnp.zeros((8, 128), F32), 0)
    normed_all = normed_all.reshape(tokens, width)
    in_raw = dot(normed_all, w_input).astype(BF16).reshape(groups, rows, chans)
    forget_raw = dot(normed_all, w_forget).astype(BF16).reshape(groups, rows, chans)
    gate_raw = dot(normed_all, w_gate_out)

    bounds_full = lower_bound(lower_table)
    bounds = lax.dynamic_slice_in_dim(bounds_full, fsdp_index * chans, chans)[None]
    seq_starts = jnp.cumsum(lengths, axis=1) - lengths
    places = seq_index * rows + jnp.arange(rows, dtype=jnp.int32)
    starts = jnp.any(places[None, :, None] == seq_starts[:, None, :], axis=-1)
    keep = jnp.where(starts, 0.0, 1.0).astype(F32)[:, :, None]
    state_b, before = forward_scan(in_raw, forget_raw, bounds, keep, 1)

    state_f = state_b.astype(F32).reshape(tokens, chans)
    gain_slice = lax.dynamic_slice_in_dim(gate_gain, fsdp_index * chans, chans)
    sigma_g = jax.nn.sigmoid(gate_raw)
    silu_gate = gate_raw * sigma_g
    out_raw = (state_f * gain_slice * silu_gate).astype(BF16)
    squares = jnp.sum(state_f * state_f, -1).reshape(groups, rows)
    mixed_part = dot(out_raw, w_output).astype(BF16).reshape(groups, rows, width)
    mixed_raw, square_sum = reduce_rows(mixed_part, to_small(squares), 2)
    state_scale = lax.rsqrt(square_sum[:groups, :rows] / width + epsilon)
    own_scale = lax.dynamic_slice_in_dim(state_scale, fsdp_index, 1, 0)[0][:, None]
    scale_g = state_scale.reshape(tokens, 1)
    middle = hidden_f + own_scale * mixed_raw
    scale_two = lax.rsqrt(jnp.mean(middle * middle, -1, keepdims=True) + epsilon)
    normed_two = (middle * scale_two * glu_gain).astype(BF16)
    normed_two_all, _ = gather(normed_two, jnp.zeros((8, 128), F32), 3)
    normed_two_all = normed_two_all.reshape(tokens, width)

    gate_val = dot(normed_two_all, w_glu_gate)
    up_val = dot(normed_two_all, w_glu_up)
    sigma_u = jax.nn.sigmoid(gate_val)
    silu_u = gate_val * sigma_u
    activity = (silu_u * up_val).astype(BF16)
    down_grad = sum_over_seq(over_tokens(cotangent_all, activity))
    d_act = dot_t(cotangent_all, w_glu_down)
    d_gate = (d_act * up_val * silu_slope(gate_val, sigma_u)).astype(BF16)
    d_up = (d_act * silu_u).astype(BF16)
    pair_grad = sum_over_seq(
        jnp.concatenate(
            [
                over_tokens(normed_two_all, d_gate).astype(BF16),
                over_tokens(normed_two_all, d_up).astype(BF16),
            ],
            1,
        )
    )
    d_two_part = (dot_t(d_gate, w_glu_gate) + dot_t(d_up, w_glu_up)).astype(BF16)
    no_small = jnp.zeros((8, 128), F32)
    d_normed_two, _ = reduce_rows(d_two_part.reshape(groups, rows, width), no_small, 4)
    glu_part = dot(activity, w_glu_down).astype(BF16).reshape(groups, rows, width)
    glu_result = lax.psum_scatter(glu_part, "fsdp", scatter_dimension=0, tiled=True)[0]
    output = (middle + glu_result.astype(F32)).astype(BF16)[None]

    cotangent_f = cotangent[0].astype(F32)
    scaled_two = glu_gain * d_normed_two
    d_middle = (
        cotangent_f
        + scale_two * scaled_two
        - middle * scale_two**3 * jnp.mean(scaled_two * middle, -1, keepdims=True)
    )
    d_glu_gain = jnp.sum(d_normed_two * middle * scale_two, 0)
    d_mixed = d_middle.astype(BF16)
    own_dot = jnp.sum(d_mixed.astype(F32) * mixed_raw, -1)[None]
    d_mixed_all, dots = gather(d_mixed, to_small(own_dot), 5)
    d_mixed_all = d_mixed_all.reshape(tokens, width)
    dot_rows = dots[:, 0, :rows].reshape(tokens, 1)

    d_out = dot_t(d_mixed_all, w_output)
    scaled_state = state_f * scale_g
    d_gain_slice = jnp.sum(d_out * scaled_state * silu_gate, 0)
    d_scaled = d_out * gain_slice * silu_gate
    d_gate_raw = (d_out * scaled_state * gain_slice * silu_slope(gate_raw, sigma_g)).astype(BF16)
    d_state = scale_g * d_scaled - state_f * (scale_g**3 * (dot_rows / width))
    d_state = d_state.astype(BF16).reshape(groups, rows, chans)
    d_in, d_forget_raw, d_bounds = backward_scan(
        d_state, in_raw, forget_raw, before, bounds, keep, 6
    )
    d_in = d_in.reshape(tokens, chans)
    d_forget_raw = d_forget_raw.reshape(tokens, chans)

    d_normed_part = dot_t(d_in, w_input) + dot_t(d_forget_raw, w_forget)
    d_normed_part = (d_normed_part + dot_t(d_gate_raw, w_gate_out)).astype(BF16)
    out_gate = (out_raw.astype(F32) * scale_g).astype(BF16)
    mixer_grad = sum_over_seq(
        jnp.concatenate(
            [
                over_tokens(d_mixed_all, out_gate).astype(BF16),
                over_tokens(normed_all, d_in).astype(BF16),
                over_tokens(normed_all, d_forget_raw).astype(BF16),
                over_tokens(normed_all, d_gate_raw).astype(BF16),
            ],
            1,
        )
    )
    d_normed, _ = reduce_rows(d_normed_part.reshape(groups, rows, width), no_small, 7)
    scaled_one = norm_gain * d_normed
    d_hidden = (
        d_middle
        + scale_one * scaled_one
        - hidden_f * scale_one**3 * jnp.mean(scaled_one * hidden_f, -1, keepdims=True)
    )
    d_norm_gain = jnp.sum(d_normed * hidden_f * scale_one, 0)
    d_gain_full = lax.dynamic_update_slice(
        jnp.zeros((width,), F32), d_gain_slice, (fsdp_index * chans,)
    )
    d_bounds_full = lax.dynamic_update_slice(
        jnp.zeros((width,), F32), d_bounds[0], (fsdp_index * chans,)
    )
    sums = jnp.stack([d_norm_gain, d_glu_gain, d_gain_full, d_bounds_full])
    totals = sum_all(sums.reshape(8, width // 2), 8).reshape(4, width)
    _, bounds_pull = jax.vjp(lower_bound, lower_table)
    d_table = bounds_pull(totals[3])[0]
    return (
        output,
        d_hidden.astype(BF16)[None],
        mixer_grad[:, chans : 2 * chans],
        mixer_grad[:, 2 * chans : 3 * chans],
        mixer_grad[:, 3 * chans :],
        mixer_grad[:, :chans].T,
        totals[0],
        totals[2],
        totals[1],
        d_table,
        pair_grad[:, :units],
        pair_grad[:, units:],
        down_grad.T,
    )


def copy_in(src, dst, sem):
    copy = pltpu.make_async_copy(src, dst, sem)
    copy.start()
    return copy


class Links:
    def __init__(self, send, recv):
        self.send, self.recv, self.used = send, recv, 0

    def start(self, src, dst, device):
        copy = remote(src, dst, self.send.at[self.used], self.recv.at[self.used], device)
        self.used += 1
        copy.start()
        return copy


class Locals:
    def __init__(self, sems):
        self.sems, self.used = sems, 0

    def start(self, src, dst):
        copy = copy_in(src, dst, self.sems.at[self.used])
        self.used += 1
        return copy


def row_slots(rows):
    half = rows // 2
    top = [pl.ds(k * rows, half) for k in range(4)]
    bottom = [pl.ds(k * rows + half, half) for k in range(4)]
    return top, bottom


def gather_start(links, src, dst, rows, s, fx, fy):
    half = rows // 2
    top, bottom = row_slots(rows)
    here = (pl.ds(0, half), pl.ds(half, half))
    return [
        links.start(src.at[here[0]], dst.at[top[1]], (s, fx)),
        links.start(src.at[here[1]], dst.at[bottom[2]], (s, fy)),
        links.start(src.at[here[1]], dst.at[bottom[1]], (s, fx)),
        links.start(src.at[here[0]], dst.at[top[2]], (s, fy)),
    ]


def gather_forward(links, own, dst, rows, s, fx, fy):
    top, bottom = row_slots(rows)
    own[0].wait_recv()
    on_y = links.start(dst.at[top[1]], dst.at[top[3]], (s, fy))
    own[1].wait_recv()
    on_x = links.start(dst.at[bottom[2]], dst.at[bottom[3]], (s, fx))
    return [on_y, on_x]


def gather_middle(own):
    own[2].wait_recv()
    own[3].wait_recv()


def gather_far(later):
    for copy in later:
        copy.wait_recv()


def sends_done(*lists):
    for copies in lists:
        for copy in copies:
            copy.wait_send()


def wait_all(*lists):
    for copies in lists:
        for copy in copies:
            copy.wait()


def reduce_start_far(links, part, from_x, from_y, rows, s, fx, fy):
    top, bottom = row_slots(rows)
    return [
        links.start(part.at[top[3]], from_x.at[0], (s, fx)),
        links.start(part.at[bottom[3]], from_y.at[0], (s, fy)),
    ]


def reduce_start_near(links, part, from_x, from_y, rows, s, fx, fy):
    top, bottom = row_slots(rows)
    return [
        links.start(part.at[top[1]], from_x.at[1], (s, fx)),
        links.start(part.at[bottom[2]], from_y.at[1], (s, fy)),
    ]


def reduce_pass(links, far, part, from_x, from_y, pass_x, pass_y, rows, s, fx, fy):
    top, bottom = row_slots(rows)
    far[0].wait_recv()
    pass_y[...] = (from_x[0].astype(F32) + part[top[2]].astype(F32)).astype(BF16)
    on_y = links.start(pass_y, from_y.at[2], (s, fy))
    far[1].wait_recv()
    pass_x[...] = (from_y[0].astype(F32) + part[bottom[1]].astype(F32)).astype(BF16)
    on_x = links.start(pass_x, from_x.at[2], (s, fx))
    return [on_y, on_x]


def mm(left, right):
    return jnp.dot(left, right, preferred_element_type=F32)


def mm_t(left, right):
    return lax.dot_general(left, right, (((1,), (1,)), ((), ())), preferred_element_type=F32)


def tile(n, width):
    return pl.ds(pl.multiple_of(n * width, width), width)


def bounds_slice(table, first, count):
    rows = table[:, pl.ds(pl.multiple_of(first, 128), count)]
    powers = jnp.exp(rows - jnp.max(rows, 0, keepdims=True))
    return jnp.sum(powers[1 : LAYER + 1], 0, keepdims=True) / jnp.sum(powers, 0, keepdims=True)


def keep_rows(lengths, group, first, rows):
    places = first + lax.broadcasted_iota(jnp.int32, (rows, 128), 0)
    start = jnp.int32(0)
    keep = jnp.where(places == start, 0.0, 1.0)
    for i in range(lengths.shape[1] - 1):
        start = start + lengths[group, i]
        keep = jnp.where(places == start, 0.0, keep)
    return keep.astype(F32)


def segment_totals(end_p, end_s, blocks, order):
    first, rest = order[0], order[1:]
    p_all = end_p[pl.ds(first, blocks, stride=8), :]
    s_all = end_s[pl.ds(first, blocks, stride=8), :]
    for j in rest:
        p_j = end_p[pl.ds(j, blocks, stride=8), :]
        s_all = end_s[pl.ds(j, blocks, stride=8), :] + p_j * s_all
        p_all = p_all * p_j
    return p_all, s_all


def spread_carry(carry, carr, end_p, end_s, blocks, order):
    for i, j in enumerate(order):
        carr[pl.ds(j, blocks, stride=8), :] = carry
        if i < 7:
            carry = end_s[pl.ds(j, blocks, stride=8), :] + end_p[pl.ds(j, blocks, stride=8), :] * carry


def mixer_kernel(
    n_seq,
    lengths,
    hidden,
    cot,
    norm_gain,
    gate_gain,
    glu_gain,
    table,
    w_in,
    w_fg,
    w_gt,
    w_out,
    normed_half,
    cot_out,
    in_out,
    fg_out,
    gate_out,
    state_out,
    raw_out,
    before_out,
    scale_out,
    middle,
    two,
    wv,
    wo,
    rows_all,
    stage,
    in_ref,
    fg_ref,
    gate_ref,
    a_ref,
    b_ref,
    shifted,
    keep_ref,
    end_p,
    end_s,
    carr,
    total,
    gathered,
    state_ref,
    raw_ref,
    squares,
    squares_t,
    packed,
    squares_in,
    part,
    from_x,
    from_y,
    pass_x,
    pass_y,
    send,
    recv,
    exchange_send,
    exchange_recv,
    local_sems,
):
    rows, width = hidden.shape
    chans = w_in.shape[1]
    lanes_of = [slice(c, c + 128) for c in range(0, chans, 128)]
    count = len(lanes_of)
    blocks = 4 * count
    step_len = rows // 8
    s, f, fx, fy, fd = plane()
    groups = [f, fx, fy, fd]
    links, local = Links(send, recv), Locals(local_sems)

    weights = [
        local.start(w, wv.at[:, pl.ds(i * chans, chans)]) for i, w in enumerate((w_in, w_fg, w_gt))
    ]
    weights.append(local.start(w_out, wo))
    barrier = pltpu.get_barrier_semaphore()
    peers = [(s, fx), (s, fy), (s, fd)] + seq_peers(n_seq)
    for peer in peers:
        pl.semaphore_signal(barrier, inc=1, device_id=peer, device_id_type=MESH)

    def norm_rows(i, _):
        at = pl.ds(pl.multiple_of(i * 16, 16), 16)
        value = hidden[at].astype(F32)
        scale = lax.rsqrt(jnp.mean(value * value, -1, keepdims=True) + epsilon)
        rows_all[at] = (value * scale * norm_gain[...]).astype(BF16)
        return 0

    lax.fori_loop(0, rows // 16, norm_rows, 0)
    pl.semaphore_wait(barrier, len(peers))
    own = gather_start(links, rows_all, rows_all, rows, s, fx, fy)
    bound = bounds_slice(table, f * chans, chans)
    for k in range(4):
        keep_ref[k] = keep_rows(lengths, groups[k], s * rows, rows)
    squares[...] = jnp.zeros_like(squares)
    squares_t[...] = jnp.zeros_like(squares_t)
    for copy in weights[:3]:
        copy.wait()

    def project(first, slots):
        def tile_of(n, _):
            cols = tile(n, 256)
            stage[: slots * rows, cols] = mm(
                rows_all[first * rows : (first + slots) * rows], wv[:, cols]
            )
            return 0

        lax.fori_loop(0, 3 * chans // 256, tile_of, 0)
        for k in range(slots):
            at = slice(k * rows, (k + 1) * rows)
            for c, lanes in enumerate(lanes_of):
                n = (first + k) * count + c
                value = stage[at, lanes].astype(BF16)
                in_ref[first + k, :, lanes] = value
                value = value.astype(F32)
                raw = stage[at, chans + c * 128 : chans + (c + 1) * 128].astype(BF16)
                fg_ref[first + k, :, lanes] = raw
                edge = bound[:, lanes]
                forget = edge + (1.0 - edge) * jax.nn.sigmoid(raw.astype(F32))
                a_ref[n] = forget * keep_ref[first + k]
                b_ref[n] = value * jax.nn.sigmoid(value) * (1.0 - forget)
            gate_ref[first + k] = stage[at, 2 * chans :]

    project(0, 1)
    later = gather_forward(links, own, rows_all, rows, s, fx, fy)
    gather_middle(own)
    project(1, 2)
    gather_far(later)
    cot_own = gather_start(links, cot, cot_out, rows, s, fx, fy)
    core = s % 2
    swaps, outs = swap_columns(
        links, local, rows_all, normed_half, n_seq, core, (s + 1 - 2 * core, f)
    )
    outs.append(local.start(cot, cot_out.at[pl.ds(0, rows)]))
    project(3, 1)
    outs += [
        local.start(in_ref, in_out),
        local.start(fg_ref, fg_out),
        local.start(gate_ref, gate_out),
    ]

    def scan_step(i, carry):
        new = []
        at = pl.ds(i, 8, stride=step_len)
        for n, (product, state) in enumerate(carry):
            a = a_ref[n, at, :]
            state = a * state + b_ref[n, at, :]
            product = product * a
            a_ref[n, at, :] = product
            b_ref[n, at, :] = state
            new.append((product, state))
        return tuple(new)

    start = tuple((jnp.ones((8, 128), F32), jnp.zeros((8, 128), F32)) for _ in range(blocks))
    ends = lax.fori_loop(0, step_len, scan_step, start)
    for n, (product, state) in enumerate(ends):
        end_p[8 * n : 8 * n + 8] = product
        end_s[8 * n : 8 * n + 8] = state
    p_all, s_all = segment_totals(end_p, end_s, blocks, range(8))
    total[:blocks] = p_all
    total[blocks:] = s_all
    copies = start_exchange(total, gathered, exchange_send, exchange_recv, n_seq)
    wait_all(copies)
    carry = jnp.zeros((blocks, 128), F32)
    for j in range(n_seq - 1):
        carry = jnp.where(j < s, gathered[j, blocks:] + gathered[j, :blocks] * carry, carry)
    for n in range(blocks):
        shifted[n, 0:1] = carry[n : n + 1]
    spread_carry(carry, carr, end_p, end_s, blocks, range(8))

    def finish(n, _):
        enter_state = carr[pl.ds(pl.multiple_of(n * 8, 8), 8)]
        for i in range(step_len):
            at = pl.ds(i, 8, stride=step_len)
            state = b_ref[n, at, :] + a_ref[n, at, :] * enter_state
            b_ref[n, at, :] = state
            shifted[n, pl.ds(i + 1, 8, stride=step_len), :] = state
        return 0

    lax.fori_loop(0, blocks, finish, 0)
    outs.append(local.start(shifted.at[:, pl.ds(0, rows)], before_out))

    lane = lax.broadcasted_iota(jnp.int32, (rows, 128), 1)
    for k in (3, 1, 2, 0):
        square = jnp.zeros((rows, 1), F32)
        for c, lanes in enumerate(lanes_of):
            state_b = b_ref[k * count + c].astype(BF16)
            state_ref[k, :, lanes] = state_b
            state = state_b.astype(F32)
            square = square + jnp.sum(state * state, -1, keepdims=True)
            gate = gate_ref[k, :, lanes]
            gain = gate_gain[:, pl.ds(pl.multiple_of(f * chans + c * 128, 128), 128)]
            raw_ref[k * rows : (k + 1) * rows, lanes] = (
                state * gain * gate * jax.nn.sigmoid(gate)
            ).astype(BF16)
        squares[:rows] = jnp.where(lane == groups[k], square, squares[:rows])
    packed[...] = squares[...].T[:8]
    square_copies = [
        links.start(packed, squares_in.at[i], (s, peer)) for i, peer in enumerate((fx, fy, fd))
    ]
    outs += [local.start(state_ref, state_out), local.start(raw_ref, raw_out)]
    cot_later = gather_forward(links, cot_own, cot_out, rows, s, fx, fy)
    weights[3].wait()

    def output_part(first, slots):
        at = slice(first * rows, (first + slots) * rows)

        def tile_of(n, _):
            cols = tile(n, 512)
            part[at, cols] = mm(raw_ref[at], wo[:, cols]).astype(BF16)
            return 0

        lax.fori_loop(0, width // 512, tile_of, 0)

    output_part(3, 1)
    far = reduce_start_far(links, part, from_x, from_y, rows, s, fx, fy)
    output_part(1, 2)
    near = reduce_start_near(links, part, from_x, from_y, rows, s, fx, fy)
    output_part(0, 1)
    passed = reduce_pass(links, far, part, from_x, from_y, pass_x, pass_y, rows, s, fx, fy)
    for copy in square_copies:
        copy.wait_recv()
    all_squares = (packed[...] + squares_in[0]) + (squares_in[1] + squares_in[2])
    squares_t[:8] = lax.rsqrt(all_squares / width + epsilon)
    scales = squares_t[...].T[:rows]
    for k in range(4):
        scale_out[k] = jnp.sum(jnp.where(lane == groups[k], scales, 0.0), -1, keepdims=True)
    for copy in near + passed:
        copy.wait_recv()
    half = rows // 2
    for first, one, other in ((0, from_x.at[1], from_y.at[2]), (half, from_y.at[1], from_x.at[2])):

        def sum_rows(i, _):
            here = pl.ds(pl.multiple_of(i * 16, 16), 16)
            at = pl.ds(pl.multiple_of(first + i * 16, 16), 16)
            mixed = part[at].astype(F32) + one[here].astype(F32) + other[here].astype(F32)
            value = hidden[at].astype(F32) + scale_out[0, at] * mixed
            middle[at] = value
            scale = lax.rsqrt(jnp.mean(value * value, -1, keepdims=True) + epsilon)
            two[at] = (value * scale * glu_gain[...]).astype(BF16)
            return 0

        lax.fori_loop(0, half // 16, sum_rows, 0)
    gather_middle(cot_own)
    gather_far(cot_later)
    sends_done(own, later, cot_own, cot_later, square_copies, far, near, passed)
    wait_all(swaps, outs)


def mixer_forward(lengths, hidden, cot, gains, table, weights, collective_id):
    n_seq = lax.axis_size("seq")
    rows, width = hidden.shape
    chans = weights[0].shape[1]
    blocks = 4 * chans // 128
    tokens = 4 * rows
    half = rows // 2
    shape = jax.ShapeDtypeStruct
    wide = shape((tokens, width), BF16)
    narrow = shape((4, rows, chans), BF16)
    long_rows = round_up(rows, 128)
    return pl.pallas_call(
        functools.partial(mixer_kernel, n_seq),
        out_shape=(
            shape((2, tokens, width // 2), BF16),
            wide,
            narrow,
            narrow,
            shape((4, rows, chans), F32),
            narrow,
            shape((tokens, chans), BF16),
            shape((blocks, rows, 128), F32),
            shape((4, rows, 1), F32),
            shape((rows, width), F32),
            shape((rows, width), BF16),
        ),
        in_specs=[pl.BlockSpec(memory_space=pltpu.SMEM), VMEM, VMEM, VMEM, VMEM, VMEM, VMEM]
        + [ANY] * 4,
        out_specs=(ANY,) * 8 + (VMEM,) * 3,
        scratch_shapes=[
            pltpu.VMEM((width, 3 * chans), BF16),
            pltpu.VMEM((chans, width), BF16),
            pltpu.VMEM((tokens, width), BF16),
            pltpu.VMEM((2 * rows, 3 * chans), F32),
            pltpu.VMEM((4, rows, chans), BF16),
            pltpu.VMEM((4, rows, chans), BF16),
            pltpu.VMEM((4, rows, chans), F32),
            pltpu.VMEM((blocks, rows, 128), F32),
            pltpu.VMEM((blocks, rows, 128), F32),
            pltpu.VMEM((blocks, rows + 8, 128), F32),
            pltpu.VMEM((4, rows, 128), F32),
            pltpu.VMEM((8 * blocks, 128), F32),
            pltpu.VMEM((8 * blocks, 128), F32),
            pltpu.VMEM((8 * blocks, 128), F32),
            pltpu.VMEM((2 * blocks, 128), F32),
            pltpu.VMEM((n_seq, 2 * blocks, 128), F32),
            pltpu.VMEM((4, rows, chans), BF16),
            pltpu.VMEM((tokens, chans), BF16),
            pltpu.VMEM((long_rows, 128), F32),
            pltpu.VMEM((128, long_rows), F32),
            pltpu.VMEM((8, long_rows), F32),
            pltpu.VMEM((3, 8, long_rows), F32),
            pltpu.VMEM((tokens, width), BF16),
            pltpu.VMEM((3, half, width), BF16),
            pltpu.VMEM((3, half, width), BF16),
            pltpu.VMEM((half, width), BF16),
            pltpu.VMEM((half, width), BF16),
            pltpu.SemaphoreType.DMA((21 + n_seq // 2,)),
            pltpu.SemaphoreType.DMA((21 + n_seq // 2,)),
            pltpu.SemaphoreType.DMA((n_seq,)),
            pltpu.SemaphoreType.DMA((n_seq,)),
            pltpu.SemaphoreType.DMA((11 + n_seq // 2,)),
        ],
        compiler_params=params(collective_id),
        name="mixer_forward",
    )(lengths, hidden, cot, *gains, table, *weights)


def swap_columns(links, local, src, dst, n_seq, core, mate):
    part = src.shape[1] // n_seq
    copies, stays = [], []
    for z in range(n_seq // 2):
        to = pl.ds(z * part, part)
        theirs = pl.ds(pl.multiple_of((2 * z + 1 - core) * part, part), part)
        ours = pl.ds(pl.multiple_of((2 * z + core) * part, part), part)
        copies.append(links.start(src.at[:, theirs], dst.at[1, :, to], mate))
        stays.append(local.start(src.at[:, ours], dst.at[0, :, to]))
    return copies, stays


def glu_kernel(
    n_seq,
    two,
    cot_all,
    w_gate,
    w_up,
    w_down,
    two_half,
    cot_half,
    act_pair,
    gate_pair,
    up_pair,
    wv,
    wd,
    cot_ref,
    two_ref,
    d_act,
    stage,
    act,
    d_gate,
    d_up,
    send,
    recv,
    local_sems,
):
    rows = two.shape[0]
    units = w_gate.shape[1]
    s, f, fx, fy, fd = plane()
    core = s % 2
    mate = (s + 1 - 2 * core, f)
    links, local = Links(send, recv), Locals(local_sems)
    loads = [local.start(w_down, wd), local.start(cot_all, cot_ref)]
    two_ref[:rows] = two[...]
    enter([(s, fx), (s, fy), mate])
    own = gather_start(links, two_ref, two_ref, rows, s, fx, fy)
    wait_all(loads)
    loads = [
        local.start(w_gate, wv.at[:, pl.ds(0, units)]),
        local.start(w_up, wv.at[:, pl.ds(units, units)]),
    ]
    swaps, stays = swap_columns(links, local, cot_ref, cot_half, n_seq, core, mate)

    def act_tile(n, _):
        cols = tile(n, 256)
        d_act[:, cols] = mm_t(cot_ref[...], wd[cols])
        return 0

    lax.fori_loop(0, units // 256, act_tile, 0)
    if units % 256:
        rest = slice(units // 256 * 256, units)
        d_act[:, rest] = mm_t(cot_ref[...], wd[rest])
    later = gather_forward(links, own, two_ref, rows, s, fx, fy)
    wait_all(loads)

    def slots(first, number, swap=True):
        nonlocal swaps, stays
        base = first * rows

        def tile_of(n, _):
            cols = tile(n, 256)
            stage[: number * rows, cols] = mm(two_ref[base : base + number * rows], wv[:, cols])
            return 0

        lax.fori_loop(0, 2 * units // 256, tile_of, 0)

        def rows_of(i, _):
            at = pl.ds(pl.multiple_of(i * 16, 16), 16)
            to = pl.ds(pl.multiple_of(base + i * 16, 16), 16)
            gate, up = stage[at, :units], stage[at, units:]
            sigma = jax.nn.sigmoid(gate)
            silu = gate * sigma
            act[to] = (silu * up).astype(BF16)
            d = d_act[to]
            d_gate[to] = (d * up * silu_slope(gate, sigma)).astype(BF16)
            d_up[to] = (d * silu).astype(BF16)
            return 0

        cuts = number * rows // 2
        for first_row in (0, cuts):
            lax.fori_loop(first_row // 16, (first_row + cuts) // 16, rows_of, 0)
            at = pl.ds(base + first_row, cuts)
            for src, dst in ((act, act_pair), (d_gate, gate_pair), (d_up, up_pair)):
                stays = stays + [local.start(src.at[at], dst.at[0, at])]
                if swap:
                    swaps = swaps + [links.start(src.at[at], dst.at[1, at], mate)]

    slots(0, 1)
    gather_middle(own)
    slots(1, 2)
    gather_far(later)
    more, keeps = swap_columns(links, local, two_ref, two_half, n_seq, core, mate)
    slots(3, 1, False)
    sends_done(own, later)
    wait_all(swaps, stays, more, keeps)


def glu(two, cot_all, w_gate, w_up, w_down, collective_id):
    n_seq = lax.axis_size("seq")
    rows, width = two.shape
    units = w_gate.shape[1]
    tokens = 4 * rows
    shape = jax.ShapeDtypeStruct
    half = shape((2, tokens, width // 2), BF16)
    pair = shape((2, tokens, units), BF16)
    remote_count = 6 + n_seq + 12
    return pl.pallas_call(
        functools.partial(glu_kernel, n_seq),
        out_shape=(half, half, pair, pair, pair),
        in_specs=[VMEM] + [ANY] * 4,
        out_specs=(ANY,) * 5,
        scratch_shapes=[
            pltpu.VMEM((width, 2 * units), BF16),
            pltpu.VMEM((units, width), BF16),
            pltpu.VMEM((tokens, width), BF16),
            pltpu.VMEM((tokens, width), BF16),
            pltpu.VMEM((tokens, units), F32),
            pltpu.VMEM((2 * rows, 2 * units), F32),
            pltpu.VMEM((tokens, units), BF16),
            pltpu.VMEM((tokens, units), BF16),
            pltpu.VMEM((tokens, units), BF16),
            pltpu.SemaphoreType.DMA((remote_count,)),
            pltpu.SemaphoreType.DMA((remote_count,)),
            pltpu.SemaphoreType.DMA((4 + n_seq + 18,)),
        ],
        compiler_params=params(collective_id),
        name="glu",
    )(two, cot_all, w_gate, w_up, w_down)


class ZLine:
    def __init__(self, part, buf, sems, n_seq, width, lag, ahead, store=None, leave=None):
        self.part, self.buf, self.width, self.lag, self.ahead = part, buf, width, lag, ahead
        self.send_up, self.recv_up, self.send_down, self.recv_down = sems[:4]
        self.store, self.leave = store, leave
        self.s, self.f = lax.axis_index("seq"), lax.axis_index("fsdp")
        self.n_seq, self.nz = n_seq, n_seq // 2
        self.z = self.s // 2
        self.block = part.shape[0] // self.nz
        self.chunks = part.shape[1] // width
        self.steps = (self.nz - 1) * self.chunks
        self.calls = self.steps + lag * (self.nz - 2)

    def rows(self, t):
        return pl.ds(pl.multiple_of(t * self.block, self.block), self.block)

    def move(self, up, k, j):
        t = self.nz - 1 - k if up else k
        landing = t + 1 if up else t
        cols = tile(j, self.width)
        slot = k * self.chunks + j
        peer = lax.rem(self.s + (2 if up else self.n_seq - 2), self.n_seq)
        send, recv = (
            (self.send_up, self.recv_up) if up else (self.send_down, self.recv_down)
        )
        return remote(
            self.part.at[self.rows(t), cols],
            self.buf.at[self.rows(landing), cols],
            send.at[slot],
            recv.at[slot],
            (peer, self.f),
        )

    def feed(self, q):
        inside = q < self.steps
        q = jnp.minimum(q, self.steps - 1)
        k = q // self.chunks
        j = q - k * self.chunks

        @pl.when(inside & (self.z == 0))
        def _():
            self.move(True, k, j).start()

        @pl.when(inside & (self.z == self.nz - 1))
        def _():
            self.move(False, k, j).start()

    def nth(self, i):
        return jnp.where(self.z < self.nz // 2, self.nz - 1 - i, i)

    def load(self, local, src, first, last):
        order = [self.rows(self.nth(i)) for i in range(first, last)]
        return [local.start(src.at[at], self.part.at[at]) for at in order]

    def feed_first(self):
        def step(q, _):
            self.feed(q)
            return 0

        lax.fori_loop(0, self.ahead, step, 0)

    def serve_one(self, up, q):
        z, nz = self.z, self.nz
        hops = z if up else nz - 1 - z
        q = q - self.lag * (hops - 1)
        inside = (hops >= 1) & (q >= 0) & (q < self.steps)
        q = jnp.clip(q, 0, self.steps - 1)
        k = q // self.chunks
        j = q - k * self.chunks
        left = nz - 1 - k - hops
        cols = tile(j, self.width)

        @pl.when(inside & (left >= 0))
        def _():
            self.move(up, k, j).wait_recv()

        @pl.when(inside & (left > 0))
        def _():
            t = nz - 1 - k if up else k
            landing = t + 1 if up else t
            own = self.part[self.rows(t), cols].astype(F32)
            came = self.buf[self.rows(landing), cols].astype(F32)
            self.part[self.rows(t), cols] = (own + came).astype(BF16)
            self.move(up, k, j).start()

    def serve(self, q, done=False):
        self.serve_one(True, q)
        self.serve_one(False, q)
        if done:
            j = q - (self.nz - 2) * self.chunks

            @pl.when((j >= 0) & (j < self.chunks))
            def _():
                self.finish(j)

    def serve_range(self, first, last, done=False):
        def step(q, _):
            self.feed(q + self.ahead)
            self.serve(q, done)
            return 0

        lax.fori_loop(first, last, step, 0)

    def finish(self, j):
        cols = tile(j, self.width)
        above = self.buf[self.rows(self.z), cols].astype(F32)
        below = self.buf[self.rows(self.z + 1), cols].astype(F32)
        own = self.part[self.rows(self.z), cols].astype(F32)
        own = own + jnp.where(self.z < self.nz - 1, above, 0.0)
        self.store(j, own + jnp.where(self.z > 0, below, 0.0))
        self.leave(j, True)

    def drain(self):
        for k in range(self.nz - 1):
            for up in (True, False):
                hops = self.z if up else self.nz - 1 - self.z

                @pl.when(hops < self.nz - 1 - k)
                def _():
                    def step(j, _):
                        self.move(up, k, j).wait_send()
                        return 0

                    lax.fori_loop(0, self.chunks, step, 0)

        def left(j, _):
            self.leave(j, False)
            return 0

        lax.fori_loop(0, self.chunks, left, 0)


def start_or_wait(copy, start):
    if start:
        copy.start()
    else:
        copy.wait()


def line_sems(n_seq, columns, width):
    count = (n_seq // 2 - 1) * (columns // width)
    leave = pltpu.SemaphoreType.DMA((columns // width,))
    return [pltpu.SemaphoreType.DMA((count,)) for _ in range(4)] + [leave]


def z_peers(n_seq):
    s = lax.axis_index("seq")
    f = lax.axis_index("fsdp")
    return [(lax.rem(s + 2 * k, n_seq), f) for k in range(1, n_seq // 2)]


def mm_tokens(left, right):
    return lax.dot_general(left, right, (((0,), (0,)), ((), ())), preferred_element_type=F32)


def down_kernel(
    n_seq,
    cot_half,
    act_pair,
    two_half,
    gate_pair,
    up_pair,
    w_gate,
    w_up,
    d_two_out,
    pair_part,
    down_out,
    d_two,
    cot_ref,
    act_ref,
    two_ref,
    gate_ref,
    up_ref,
    wg,
    wu,
    part,
    buf,
    rows_part,
    from_x,
    from_y,
    pass_x,
    pass_y,
    pair_ref,
    down_ref,
    send,
    recv,
    local_sems,
    *line,
):
    rows, width = d_two.shape
    units = act_pair.shape[1]
    s, f, fx, fy, fd = plane()
    links, local = Links(send, recv), Locals(local_sems)
    core = s % 2
    mate = (s + 1 - 2 * core, f)
    tokens = 4 * rows
    near_rows, far_own = pl.ds(0, 2 * tokens - rows), pl.ds(3 * rows, rows)
    far_mate = pl.ds(2 * tokens - rows, rows)
    loads = [local.start(act_pair.at[near_rows], act_ref.at[near_rows])]
    enter([(s, fx), (s, fy), mate] + z_peers(n_seq))
    swaps = [links.start(act_pair.at[far_own], act_ref.at[far_mate], mate)]

    def store(j, value):
        down_ref[tile(j, 128)] = value.T

    def leave(j, start):
        at = tile(j, 128)
        copy = pltpu.make_async_copy(down_ref.at[at], down_out.at[at], line[4].at[j])
        start_or_wait(copy, start)

    z_sum = ZLine(part, buf, line, n_seq, 128, 3, 11, store, leave)
    block = z_sum.block
    tiles_in = [
        local.start(cot_half.at[:, at], cot_ref.at[:, at])
        for at in (tile(z_sum.nth(i), block) for i in range(z_sum.nz))
    ]
    wait_all(loads, tiles_in[:1])
    swaps[0].wait_recv()
    swaps += [
        links.start(src.at[far_own], dst.at[far_mate], mate)
        for src, dst in ((gate_pair, gate_ref), (up_pair, up_ref))
    ]
    loads = [
        local.start(src, dst)
        for src, dst in (
            (w_gate, wg),
            (w_up, wu),
            (gate_pair.at[near_rows], gate_ref.at[near_rows]),
            (up_pair.at[near_rows], up_ref.at[near_rows]),
            (two_half, two_ref),
        )
    ]

    def down_tile(i, _):
        t = z_sum.nth(i)
        part[z_sum.rows(t)] = mm_tokens(cot_ref[:, tile(t, block)], act_ref[...]).astype(BF16)
        return 0

    down_tile(jnp.int32(0), 0)
    z_sum.feed_first()
    wait_all(tiles_in[1:])
    lax.fori_loop(1, z_sum.nz, down_tile, 0)
    wait_all(loads)
    for copy in swaps[1:]:
        copy.wait_recv()

    def two_part(first, slots, base):
        at = slice(first * rows, (first + slots) * rows)

        def tile_of(n, _):
            cols = tile(n, 512)
            total = mm_t(gate_ref[at], wg[cols]) + mm_t(up_ref[at], wu[cols])
            rows_part[at, cols] = total.astype(BF16)
            z_sum.feed(base + n + z_sum.ahead)
            z_sum.serve(base + n)
            return 0

        lax.fori_loop(0, width // 512, tile_of, 0)

    count = width // 512
    two_part(3, 1, 0)
    far = reduce_start_far(links, rows_part, from_x, from_y, rows, s, fx, fy)
    two_part(1, 2, count)
    near = reduce_start_near(links, rows_part, from_x, from_y, rows, s, fx, fy)
    two_part(0, 1, 2 * count)
    served = 3 * count

    def pair_tiles(right, first, base):
        def tile_of(t, _):
            pair_ref[z_sum.rows(t), pl.ds(first, units)] = mm_tokens(
                two_ref[:, tile(t, block)], right[...]
            ).astype(BF16)
            z_sum.serve_range(base + 2 * t, base + 2 * t + 2, True)
            return 0

        lax.fori_loop(0, z_sum.nz, tile_of, 0)

    pair_tiles(gate_ref, 0, served)
    served += 2 * z_sum.nz
    passed = reduce_pass(links, far, rows_part, from_x, from_y, pass_x, pass_y, rows, s, fx, fy)
    pair_tiles(up_ref, units, served)
    served += 2 * z_sum.nz
    stay = local.start(pair_ref, pair_part)
    for copy in near + passed:
        copy.wait_recv()
    half = rows // 2
    d_two[:half] = rows_part[:half].astype(F32) + from_x[1].astype(F32) + from_y[2].astype(F32)
    d_two[half:] = rows_part[half:rows].astype(F32) + from_y[1].astype(F32) + from_x[2].astype(F32)
    early = local.start(d_two, d_two_out)
    z_sum.serve_range(served, z_sum.calls, True)
    z_sum.drain()
    sends_done(swaps, far, near, passed)
    wait_all([stay, early])


def down_sum(cot_half, act_pair, two_half, gate_pair, up_pair, w_gate, w_up, collective_id):
    n_seq = lax.axis_size("seq")
    tokens, units = act_pair.shape
    width = w_gate.shape[0]
    rows = tokens // 8
    half = (rows // 2, width)
    own = cot_half.shape[1]
    block = width // n_seq
    shape = jax.ShapeDtypeStruct
    return pl.pallas_call(
        functools.partial(down_kernel, n_seq),
        out_shape=(
            shape((rows, width), F32),
            shape((own, 2 * units), BF16),
            shape((units, block), F32),
        ),
        in_specs=[ANY] * 7,
        out_specs=(ANY, ANY, ANY),
        scratch_shapes=[
            pltpu.VMEM((rows, width), F32),
            pltpu.VMEM((tokens, own), BF16),
            pltpu.VMEM((tokens, units), BF16),
            pltpu.VMEM((tokens, own), BF16),
            pltpu.VMEM((tokens, units), BF16),
            pltpu.VMEM((tokens, units), BF16),
            pltpu.VMEM((width, units), BF16),
            pltpu.VMEM((width, units), BF16),
            pltpu.VMEM((own, units), BF16),
            pltpu.VMEM((own + block, units), BF16),
            pltpu.VMEM((tokens // 2, width), BF16),
            pltpu.VMEM((3,) + half, BF16),
            pltpu.VMEM((3,) + half, BF16),
            pltpu.VMEM(half, BF16),
            pltpu.VMEM(half, BF16),
            pltpu.VMEM((own, 2 * units), BF16),
            pltpu.VMEM((units, block), F32),
            pltpu.SemaphoreType.DMA((9,)),
            pltpu.SemaphoreType.DMA((9,)),
            pltpu.SemaphoreType.DMA((8 + n_seq // 2,)),
        ]
        + line_sems(n_seq, units, 128),
        compiler_params=params(collective_id),
        name="down_sum",
    )(cot_half, act_pair, two_half, gate_pair, up_pair, w_gate, w_up)


class TotalsFromAbove:
    def __init__(self, total, gathered, send, recv, n_seq):
        self.total, self.gathered, self.send, self.recv = total, gathered, send, recv
        self.s, self.f = lax.axis_index("seq"), lax.axis_index("fsdp")
        self.nz = n_seq // 2
        self.z, self.core = self.s // 2, self.s % 2
        self.mate = (2 * self.z + 1 - self.core, self.f)

    def down(self, sender, target):
        return remote(
            self.total,
            self.gathered.at[2 * sender + self.core],
            self.send.at[target],
            self.recv.at[2 * sender + self.core],
            (2 * target + self.core, self.f),
        )

    def across(self, sender, core):
        slot = 2 * sender + core
        return remote(
            self.gathered.at[slot],
            self.gathered.at[slot],
            self.send.at[self.nz + sender],
            self.recv.at[slot],
            self.mate,
        )

    def to_mate(self, core):
        slot = 2 * self.z + core
        return remote(
            self.total,
            self.gathered.at[slot],
            self.send.at[2 * self.nz],
            self.recv.at[slot],
            self.mate,
        )

    def start(self):
        self.to_mate(self.core).start()
        for target in range(self.nz - 1):

            @pl.when(target < self.z)
            def _():
                self.down(self.z, target).start()

    def relay(self):
        for sender in range(1, self.nz):

            @pl.when(sender > self.z)
            def _():
                self.down(sender, self.z).wait_recv()
                self.across(sender, self.core).start()

    def wait(self):
        self.to_mate(1 - self.core).wait_recv()
        for sender in range(1, self.nz):

            @pl.when(sender > self.z)
            def _():
                self.across(sender, 1 - self.core).wait_recv()

    def drain(self):
        self.to_mate(self.core).wait_send()
        for z in range(self.nz):

            @pl.when(z < self.z)
            def _():
                self.down(self.z, z).wait_send()

            @pl.when(z > self.z)
            def _():
                self.across(z, self.core).wait_send()


def pair_kernel(
    n_seq,
    lengths,
    hidden,
    cot,
    glu_gain,
    gate_gain,
    table,
    scale_g,
    d_two,
    middle,
    pair_part,
    w_out,
    w_in,
    w_fg,
    w_gt,
    gate_raw,
    state_b,
    out_raw,
    in_raw,
    fg_raw,
    before_in,
    normed_half,
    pair_grad,
    mixer_part,
    rows_out,
    sums_ref,
    d_glu_gain,
    d_gain,
    d_bounds,
    d_normed,
    d_middle,
    pair_ref,
    part,
    buf,
    wo,
    wv,
    mixed_all,
    mixed_mate,
    normed_ref,
    d_proj,
    out_gate,
    gate_ref,
    state_ref,
    raw_ref,
    in_ref,
    fg_ref,
    before,
    p_ref,
    q_ref,
    stage,
    rows_part,
    from_x,
    from_y,
    pass_x,
    pass_y,
    dots,
    keep_ref,
    end_p,
    end_s,
    carr,
    total,
    gathered,
    send,
    recv,
    exchange_send,
    exchange_recv,
    local_sems,
    tile_sems,
    *line,
):
    rows, width = hidden.shape
    chans = w_in.shape[1]
    tokens = 4 * rows
    lanes_of = [slice(c, c + 128) for c in range(0, chans, 128)]
    count = len(lanes_of)
    blocks = 4 * count
    step_len = rows // 8
    s, f, fx, fy, fd = plane()
    groups = [f, fx, fy, fd]
    core = s % 2
    mate = (s + 1 - 2 * core, f)
    links, local = Links(send, recv), Locals(local_sems)

    def store(j, value):
        pair_ref[:, tile(j, 256)] = value

    def leave(j, start):
        at = tile(j, 256)
        copy = pltpu.make_async_copy(pair_ref.at[:, at], pair_grad.at[:, at], line[4].at[j])
        start_or_wait(copy, start)

    z_sum = ZLine(part, buf, line, n_seq, 256, 2, 7, store, leave)
    blocks_in = z_sum.load(local, pair_part, 0, 1)
    rows_in = [local.start(d_two, d_middle), local.start(middle, d_normed)]
    enter([(s, fx), (s, fy), (s, fd)] + seq_peers(n_seq))
    blocks_in[0].wait()
    z_sum.feed_first()
    blocks_in = z_sum.load(local, pair_part, 1, z_sum.nz)
    loads = [local.start(w_out, wo)]
    loads += [
        local.start(src, dst)
        for src, dst in (
            (gate_raw, gate_ref),
            (state_b, state_ref),
            (out_raw, raw_ref),
            (in_raw, in_ref),
            (fg_raw, fg_ref),
            (before_in, before),
        )
    ]
    weights = [
        local.start(w, wv.at[:, pl.ds(i * chans, chans)]) for i, w in enumerate((w_in, w_fg, w_gt))
    ]
    weights.append(local.start(normed_half, normed_ref))
    served = 0

    def serve(number):
        nonlocal served
        z_sum.serve_range(served, served + number)
        served += number

    d_glu_gain[...] = jnp.zeros_like(d_glu_gain)
    wait_all(rows_in, blocks_in)

    def middle_rows(i, _):
        at = pl.ds(pl.multiple_of(i * 16, 16), 16)
        value, came = d_normed[at], d_middle[at]
        scale = lax.rsqrt(jnp.mean(value * value, -1, keepdims=True) + epsilon)
        scaled = glu_gain[...] * came
        mean = jnp.mean(scaled * value, -1, keepdims=True)
        grad = cot[at].astype(F32) + scale * scaled - value * (scale**3 * mean)
        d_middle[at] = grad
        grad_b = grad.astype(BF16)
        mixed_all[at] = grad_b
        own_dot = jnp.sum(
            grad_b.astype(F32) * (value - hidden[at].astype(F32)), -1, keepdims=True
        )
        dots[0, at] = jnp.broadcast_to(own_dot, (16, 128))
        d_glu_gain[...] += jnp.sum(came * value * scale, 0, keepdims=True)
        return 0

    lax.fori_loop(0, rows // 16, middle_rows, 0)
    outs = [local.start(d_middle, rows_out.at[pl.ds(rows, rows)])]
    own = gather_start(links, mixed_all, mixed_all, rows, s, fx, fy)
    dot_copies = [
        links.start(dots.at[0], dots.at[k], (s, peer)) for k, peer in ((1, fx), (2, fy), (3, fd))
    ]
    bound = bounds_slice(table, f * chans, chans)
    for k in range(4):
        keep_ref[k] = keep_rows(lengths, groups[k], s * rows, rows)
    d_gain[...] = jnp.zeros_like(d_gain)
    serve(1)
    for copy in loads:
        copy.wait()

    def out_rows(first, slots):
        stage[: slots * rows] = mm_t(mixed_all[first * rows : (first + slots) * rows], wo[...])
        for i in range(slots):
            k = first + i
            scale = scale_g[k]
            for c, lanes in enumerate(lanes_of):
                n = k * count + c
                gain = gate_gain[:, pl.ds(pl.multiple_of(f * chans + c * 128, 128), 128)]
                d_out = stage[i * rows : (i + 1) * rows, lanes]
                gate = gate_ref[k, :, lanes]
                sigma = jax.nn.sigmoid(gate)
                silu = gate * sigma
                state = state_ref[k, :, lanes].astype(F32)
                weighed = d_out * (state * scale)
                d_gain[:, lanes] += jnp.sum(weighed * silu, 0, keepdims=True)
                at = slice(k * rows, (k + 1) * rows)
                d_proj[at, 2 * chans + c * 128 : 2 * chans + (c + 1) * 128] = (
                    weighed * gain * silu_slope(gate, sigma)
                ).astype(BF16)
                out_gate[at, lanes] = (raw_ref[at, lanes].astype(F32) * scale).astype(BF16)
                d_state = scale * (d_out * gain * silu) - state * (
                    scale * scale * (dots[k] / width)
                )
                q_ref[n] = d_state.astype(BF16).astype(F32)
                edge = bound[:, lanes]
                forget = edge + (1.0 - edge) * jax.nn.sigmoid(fg_ref[k, :, lanes].astype(F32))
                p_ref[n] = forget * keep_ref[k]

    out_rows(0, 1)
    later = gather_forward(links, own, mixed_all, rows, s, fx, fy)
    serve(2)
    gather_middle(own)
    for copy in dot_copies:
        copy.wait_recv()
    out_rows(1, 2)
    serve(3)
    gather_far(later)
    out_rows(3, 1)
    serve(2)
    own_rows, mate_rows = pl.ds(0, tokens), pl.ds(tokens, tokens)
    last = pl.ds(2 * chans, chans)
    swaps = [
        links.start(out_gate.at[own_rows], out_gate.at[mate_rows], mate),
        links.start(d_proj.at[own_rows, last], d_proj.at[mate_rows, last], mate),
    ]
    wide = z_sum.block
    for t in range(n_seq // 2):
        theirs = pl.ds(pl.multiple_of((2 * t + 1 - core) * wide, wide), wide)
        swaps.append(
            links.start(mixed_all.at[:, theirs], mixed_mate.at[:, pl.ds(t * wide, wide)], mate)
        )

    def scan_step(i, carry):
        new = []
        at = pl.ds(step_len - 1 - i, 8, stride=step_len)
        for n, (product, message) in enumerate(carry):
            a = p_ref[n, at, :]
            acc = q_ref[n, at, :] + message
            p_ref[n, at, :] = product
            q_ref[n, at, :] = acc
            new.append((product * a, a * acc))
        return tuple(new)

    start = tuple((jnp.ones((8, 128), F32), jnp.zeros((8, 128), F32)) for _ in range(blocks))
    ends = lax.fori_loop(0, step_len, scan_step, start)
    for n, (product, message) in enumerate(ends):
        end_p[8 * n : 8 * n + 8] = product
        end_s[8 * n : 8 * n + 8] = message
    p_all, s_all = segment_totals(end_p, end_s, blocks, range(7, -1, -1))
    total[:blocks] = p_all
    total[blocks:] = s_all
    above = TotalsFromAbove(total, gathered, exchange_send, exchange_recv, n_seq)
    above.start()
    serve(2)
    above.relay()
    serve(2)
    above.wait()
    carry = jnp.zeros((blocks, 128), F32)
    for j in range(n_seq - 1, 0, -1):
        carry = jnp.where(j > s, gathered[j, blocks:] + gathered[j, :blocks] * carry, carry)
    spread_carry(carry, carr, end_p, end_s, blocks, range(7, -1, -1))

    def finish(n, _):
        enter_state = carr[pl.ds(pl.multiple_of(n * 8, 8), 8)]
        for i in range(step_len):
            at = pl.ds(i, 8, stride=step_len)
            q_ref[n, at, :] = q_ref[n, at, :] + p_ref[n, at, :] * enter_state
        return 0

    lax.fori_loop(0, blocks, finish, 0)
    d_bounds[...] = jnp.zeros_like(d_bounds)
    for k in range(4):
        at = slice(k * rows, (k + 1) * rows)
        for c, lanes in enumerate(lanes_of):
            acc = q_ref[k * count + c]
            edge = bound[:, lanes]
            sigma_f = jax.nn.sigmoid(fg_ref[k, :, lanes].astype(F32))
            forget = edge + (1.0 - edge) * sigma_f
            value = in_ref[k, :, lanes].astype(F32)
            sigma_i = jax.nn.sigmoid(value)
            d_forget = acc * (before[k * count + c] * keep_ref[k] - value * sigma_i)
            d_proj[at, lanes] = (acc * (1.0 - forget) * silu_slope(value, sigma_i)).astype(BF16)
            d_sigma = d_forget * (1.0 - sigma_f)
            d_proj[at, chans + c * 128 : chans + (c + 1) * 128] = (
                d_sigma * (1.0 - edge) * sigma_f
            ).astype(BF16)
            d_bounds[:, lanes] += jnp.sum(d_sigma, 0, keepdims=True)
    first = pl.ds(0, 2 * chans)
    swaps.append(links.start(d_proj.at[own_rows, first], d_proj.at[mate_rows, first], mate))
    serve(2)
    for copy in weights:
        copy.wait()

    def normed_part(first_slot, slots):
        at = slice(first_slot * rows, (first_slot + slots) * rows)

        def tile_of(n, _):
            cols = tile(n, 512)
            rows_part[at, cols] = mm_t(d_proj[at], wv[cols]).astype(BF16)
            return 0

        lax.fori_loop(0, width // 512, tile_of, 0)

    normed_part(3, 1)
    far = reduce_start_far(links, rows_part, from_x, from_y, rows, s, fx, fy)
    normed_part(1, 2)
    near = reduce_start_near(links, rows_part, from_x, from_y, rows, s, fx, fy)
    normed_part(0, 1)
    serve(3)
    for copy in swaps:
        copy.wait_recv()

    def tile_out(t):
        slot = lax.rem(t, 2)
        return pltpu.make_async_copy(
            wo.at[tile(slot, wide)], mixer_part.at[z_sum.rows(t)], tile_sems.at[slot]
        )

    def mixer_tile(t, _):
        @pl.when(t >= 2)
        def _():
            tile_out(t - 2).wait()

        at = tile(lax.rem(t, 2), wide)
        ours = mixed_all[:, tile(2 * t + core, wide)]
        out_part = mm_tokens(ours, out_gate[:tokens])
        out_part = out_part + mm_tokens(mixed_mate[:, tile(t, wide)], out_gate[tokens:])
        wo[at, :chans] = out_part.astype(BF16)
        wo[at, chans:] = mm_tokens(normed_ref[:, tile(t, wide)], d_proj[...]).astype(BF16)
        tile_out(t).start()
        return 0

    lax.fori_loop(0, 1, mixer_tile, 0)
    passed = reduce_pass(links, far, rows_part, from_x, from_y, pass_x, pass_y, rows, s, fx, fy)
    serve(2)
    lax.fori_loop(1, z_sum.nz, mixer_tile, 0)
    serve(3)
    for copy in near + passed:
        copy.wait_recv()
    half = rows // 2
    d_normed[:half] = rows_part[:half].astype(F32) + from_x[1].astype(F32) + from_y[2].astype(F32)
    d_normed[half:] = (
        rows_part[half:rows].astype(F32) + from_y[1].astype(F32) + from_x[2].astype(F32)
    )
    outs.append(local.start(d_normed, rows_out.at[pl.ds(0, rows)]))
    sums_ref[...] = jnp.zeros_like(sums_ref)
    sums_ref[0:1] = d_glu_gain[...]
    sums_ref[1:2, :chans] = d_gain[...]
    sums_ref[2:3, :chans] = d_bounds[...]
    outs.append(local.start(sums_ref, rows_out.at[pl.ds(2 * rows, 8)]))
    z_sum.serve_range(served, z_sum.calls, True)
    z_sum.drain()
    above.drain()
    sends_done(own, later, dot_copies, swaps, far, near, passed)
    for t in range(z_sum.nz - 2, z_sum.nz):
        tile_out(jnp.int32(t)).wait()
    wait_all(outs)


def pair_sum(
    lengths, own_rows, gains, table, scale_g, float_rows, pair_part, weights, saved, normed_half, cid
):
    n_seq = lax.axis_size("seq")
    rows, width = own_rows[0].shape
    chans = weights[1].shape[1]
    own, columns = pair_part.shape
    tokens = 4 * rows
    blocks = 4 * chans // 128
    block = width // n_seq
    half = (rows // 2, width)
    shape = jax.ShapeDtypeStruct
    count = 18 + n_seq // 2
    return pl.pallas_call(
        functools.partial(pair_kernel, n_seq),
        out_shape=(
            shape((block, columns), F32),
            shape((own, 4 * chans), BF16),
            shape((2 * rows + 8, width), F32),
        ),
        in_specs=[pl.BlockSpec(memory_space=pltpu.SMEM)] + [VMEM] * 6 + [ANY] * 14,
        out_specs=(ANY,) * 3,
        scratch_shapes=[
            pltpu.VMEM((8, width), F32),
            pltpu.VMEM((1, width), F32),
            pltpu.VMEM((1, chans), F32),
            pltpu.VMEM((1, chans), F32),
            pltpu.VMEM((rows, width), F32),
            pltpu.VMEM((rows, width), F32),
            pltpu.VMEM((block, columns), F32),
            pltpu.VMEM((own, columns), BF16),
            pltpu.VMEM((own + block, columns), BF16),
            pltpu.VMEM((chans, width), BF16),
            pltpu.VMEM((width, 3 * chans), BF16),
            pltpu.VMEM((tokens, width), BF16),
            pltpu.VMEM((tokens, width // 2), BF16),
            pltpu.VMEM((2 * tokens, width // 2), BF16),
            pltpu.VMEM((2 * tokens, 3 * chans), BF16),
            pltpu.VMEM((2 * tokens, chans), BF16),
            pltpu.VMEM((4, rows, chans), F32),
            pltpu.VMEM((4, rows, chans), BF16),
            pltpu.VMEM((tokens, chans), BF16),
            pltpu.VMEM((4, rows, chans), BF16),
            pltpu.VMEM((4, rows, chans), BF16),
            pltpu.VMEM((blocks, rows, 128), F32),
            pltpu.VMEM((blocks, rows, 128), F32),
            pltpu.VMEM((blocks, rows, 128), F32),
            pltpu.VMEM((2 * rows, chans), F32),
            pltpu.VMEM((tokens, width), BF16),
            pltpu.VMEM((3,) + half, BF16),
            pltpu.VMEM((3,) + half, BF16),
            pltpu.VMEM(half, BF16),
            pltpu.VMEM(half, BF16),
            pltpu.VMEM((4, rows, 128), F32),
            pltpu.VMEM((4, rows, 128), F32),
            pltpu.VMEM((8 * blocks, 128), F32),
            pltpu.VMEM((8 * blocks, 128), F32),
            pltpu.VMEM((8 * blocks, 128), F32),
            pltpu.VMEM((2 * blocks, 128), F32),
            pltpu.VMEM((n_seq, 2 * blocks, 128), F32),
            pltpu.SemaphoreType.DMA((count,)),
            pltpu.SemaphoreType.DMA((count,)),
            pltpu.SemaphoreType.DMA((n_seq + 1,)),
            pltpu.SemaphoreType.DMA((n_seq,)),
            pltpu.SemaphoreType.DMA((16 + n_seq // 2,)),
            pltpu.SemaphoreType.DMA((2,)),
        ]
        + line_sems(n_seq, columns, 256),
        compiler_params=params(cid),
        name="pair_sum",
    )(
        lengths,
        *own_rows,
        *gains,
        table,
        scale_g,
        *float_rows,
        pair_part,
        *weights,
        *saved,
        normed_half,
    )


def final_kernel(
    n_seq,
    n_fsdp,
    hidden,
    norm_gain,
    table,
    float_rows,
    middle_in,
    mixer_part,
    act_pair,
    w_down,
    output_out,
    d_hidden_out,
    out_grad,
    rest_grad,
    norm_out,
    glu_out,
    gate_out,
    d_table,
    sums_ref,
    d_normed,
    d_middle,
    middle,
    output,
    d_hidden,
    out_ref,
    rest_ref,
    part,
    buf,
    act,
    wd,
    rows_part,
    from_x,
    from_y,
    pass_x,
    pass_y,
    norm_sum,
    bounds_out,
    terms,
    quarters_in,
    terms_q,
    from_mate,
    terms_chip,
    over_seq,
    along_sum,
    over_fsdp,
    send,
    recv,
    local_sems,
    *line,
):
    rows, width = hidden.shape
    chans = out_grad.shape[0]
    tokens = 4 * rows
    s, f, fx, fy, fd = plane()
    links, local = Links(send, recv), Locals(local_sems)
    head = chans // 256

    def store(j, value):
        @pl.when(j < head)
        def _():
            out_ref[tile(j, 256)] = value.T

        @pl.when(j >= head)
        def _():
            rest_ref[:, tile(j - head, 256)] = value

    def leave(j, start):
        @pl.when(j < head)
        def _():
            at = tile(j, 256)
            copy = pltpu.make_async_copy(out_ref.at[at], out_grad.at[at], line[4].at[j])
            start_or_wait(copy, start)

        @pl.when(j >= head)
        def _():
            at = tile(j - head, 256)
            copy = pltpu.make_async_copy(rest_ref.at[:, at], rest_grad.at[:, at], line[4].at[j])
            start_or_wait(copy, start)

    z_sum = ZLine(part, buf, line, n_seq, 256, 2, 6, store, leave)
    blocks_in = z_sum.load(local, mixer_part, 0, 1)
    along = seq_peers(n_seq)
    across = [(s, fx), (s, fy), (s, fd)]
    enter(across + along)
    blocks_in[0].wait()
    z_sum.feed_first()
    loads = [local.start(act_pair.at[pl.ds(0, tokens)], act), local.start(w_down, wd)]
    blocks_in = z_sum.load(local, mixer_part, 1, z_sum.nz)
    rows_in = [
        local.start(src, dst)
        for src, dst in (
            (float_rows.at[pl.ds(0, rows)], d_normed),
            (float_rows.at[pl.ds(rows, rows)], d_middle),
            (float_rows.at[pl.ds(2 * rows, 8)], sums_ref),
            (middle_in, middle),
        )
    ]
    served = 0

    def serve(number):
        nonlocal served
        z_sum.serve_range(served, served + number)
        served += number

    norm_sum[...] = jnp.zeros_like(norm_sum)

    def hidden_rows(i, _):
        at = pl.ds(pl.multiple_of(i * 16, 16), 16)
        value, came = hidden[at].astype(F32), d_normed[at]
        scale = lax.rsqrt(jnp.mean(value * value, -1, keepdims=True) + epsilon)
        scaled = norm_gain[...] * came
        mean = jnp.mean(scaled * value, -1, keepdims=True)
        d_hidden[at] = (d_middle[at] + scale * scaled - value * (scale**3 * mean)).astype(BF16)
        norm_sum[...] += jnp.sum(came * value * scale, 0, keepdims=True)
        return 0

    wait_all(loads)

    def glu_part(first, slots):
        at = slice(first * rows, (first + slots) * rows)

        def tile_of(n, _):
            cols = tile(n, 512)
            rows_part[at, cols] = mm(act[at], wd[:, cols]).astype(BF16)
            return 0

        lax.fori_loop(0, width // 512, tile_of, 0)

    glu_part(3, 1)
    far = reduce_start_far(links, rows_part, from_x, from_y, rows, s, fx, fy)
    glu_part(1, 2)
    near = reduce_start_near(links, rows_part, from_x, from_y, rows, s, fx, fy)
    glu_part(0, 1)
    wait_all(blocks_in, rows_in)
    serve(2)
    lax.fori_loop(0, rows // 16, hidden_rows, 0)
    terms[...] = jnp.zeros_like(terms)
    for q in range(4):
        terms[q, 0:1] = norm_sum[:, q * chans : (q + 1) * chans]
        terms[q, 1:2] = sums_ref[0:1, q * chans : (q + 1) * chans]
    quarter_copies = [
        links.start(terms.at[peer], quarters_in.at[k], (s, peer))
        for k, peer in enumerate((fx, fy, fd))
    ]
    serve(1)
    passed = reduce_pass(links, far, rows_part, from_x, from_y, pass_x, pass_y, rows, s, fx, fy)
    serve(2)
    quarter = terms[pl.ds(f, 1)][0]
    for k, copy in enumerate(quarter_copies):
        copy.wait_recv()
        quarter = quarter + quarters_in[k]
    half = chans // 2
    for first, cols in ((0, slice(0, half)), (4, slice(half, chans))):
        terms_q[first : first + 2] = quarter[:2, cols]
        terms_q[first + 2 : first + 3] = sums_ref[1:2, cols]
        terms_q[first + 3 : first + 4] = sums_ref[2:3, cols]
    mate_copy = links.start(terms_q, from_mate, (s + 1 - 2 * (s % 2), f))
    serve(1)
    serve(2)
    for copy in near + passed:
        copy.wait_recv()
    middle_half = rows // 2
    for first, one, other in (
        (0, from_x.at[1], from_y.at[2]),
        (middle_half, from_y.at[1], from_x.at[2]),
    ):
        at = slice(first, first + middle_half)
        added = rows_part[at].astype(F32) + one[...].astype(F32) + other[...].astype(F32)
        output[at] = (middle[at] + added).astype(BF16)
    mate_copy.wait_recv()
    terms_chip[...] = terms_q[...] + from_mate[...]
    seq_copies = [
        links.start(terms_chip, over_seq.at[k], peer) for k, peer in enumerate(z_peers(n_seq))
    ]
    serve(2)
    total = terms_chip[...]
    for k, copy in enumerate(seq_copies):
        copy.wait_recv()
        total = total + over_seq[k]
    along_sum[...] = total
    fsdp_copies = [links.start(along_sum, over_fsdp.at[k], peer) for k, peer in enumerate(across)]
    serve(2)
    for copy in fsdp_copies:
        copy.wait_recv()
    for k, group in enumerate((f, fx, fy, fd)):
        total = along_sum[...] if k == 0 else over_fsdp[k - 1]
        for i in range(2):
            at = pl.ds(pl.multiple_of(group * chans + i * half, 128), half)
            for r, out in enumerate((norm_out, glu_out, gate_out, bounds_out)):
                out[:, at] = total[4 * i + r : 4 * i + r + 1]
    powers = jnp.exp(table[...] - jnp.max(table[...], 0, keepdims=True))
    soft = powers / jnp.sum(powers, 0, keepdims=True)
    row = lax.broadcasted_iota(jnp.int32, soft.shape, 0)
    chosen = jnp.where((row >= 1) & (row <= LAYER), 1.0, 0.0)
    bound = jnp.sum(soft * chosen, 0, keepdims=True)
    d_table[...] = soft * (chosen - bound) * bounds_out[...]
    outs = [local.start(output, output_out), local.start(d_hidden, d_hidden_out)]
    z_sum.serve_range(served, z_sum.calls, True)
    z_sum.drain()
    wait_all(outs)
    sends_done(far, near, passed, quarter_copies, [mate_copy], seq_copies, fsdp_copies)


def final_sum(hidden, norm_gain, table, float_rows, middle, mixer_part, act_pair, w_down, cid):
    n_seq, n_fsdp = lax.axis_size("seq"), lax.axis_size("fsdp")
    rows, width = hidden.shape
    own, columns = mixer_part.shape
    units = w_down.shape[0]
    chans = columns // 4
    tokens = 4 * rows
    block = width // n_seq
    half = (rows // 2, width)
    terms = (8, chans // 2)
    shape = jax.ShapeDtypeStruct
    count = 6 + n_seq // 2 + 2 * (n_fsdp - 1)
    return pl.pallas_call(
        functools.partial(final_kernel, n_seq, n_fsdp),
        out_shape=(
            shape((rows, width), BF16),
            shape((rows, width), BF16),
            shape((chans, block), F32),
            shape((block, 3 * chans), F32),
            shape((1, width), F32),
            shape((1, width), F32),
            shape((1, width), F32),
            shape(table.shape, F32),
        ),
        in_specs=[VMEM] * 3 + [ANY] * 5,
        out_specs=(ANY,) * 4 + (VMEM,) * 4,
        scratch_shapes=[
            pltpu.VMEM((8, width), F32),
            pltpu.VMEM((rows, width), F32),
            pltpu.VMEM((rows, width), F32),
            pltpu.VMEM((rows, width), F32),
            pltpu.VMEM((rows, width), BF16),
            pltpu.VMEM((rows, width), BF16),
            pltpu.VMEM((chans, block), F32),
            pltpu.VMEM((block, 3 * chans), F32),
            pltpu.VMEM((own, columns), BF16),
            pltpu.VMEM((own + block, columns), BF16),
            pltpu.VMEM((tokens, units), BF16),
            pltpu.VMEM((units, width), BF16),
            pltpu.VMEM((tokens, width), BF16),
            pltpu.VMEM((3,) + half, BF16),
            pltpu.VMEM((3,) + half, BF16),
            pltpu.VMEM(half, BF16),
            pltpu.VMEM(half, BF16),
            pltpu.VMEM((1, width), F32),
            pltpu.VMEM((1, width), F32),
            pltpu.VMEM((n_fsdp, 8, chans), F32),
            pltpu.VMEM((n_fsdp - 1, 8, chans), F32),
            pltpu.VMEM(terms, F32),
            pltpu.VMEM(terms, F32),
            pltpu.VMEM(terms, F32),
            pltpu.VMEM((n_seq // 2 - 1,) + terms, F32),
            pltpu.VMEM(terms, F32),
            pltpu.VMEM((n_fsdp - 1,) + terms, F32),
            pltpu.SemaphoreType.DMA((count,)),
            pltpu.SemaphoreType.DMA((count,)),
            pltpu.SemaphoreType.DMA((8 + n_seq // 2,)),
        ]
        + line_sems(n_seq, columns, 256),
        compiler_params=params(cid, 48),
        name="final_sum",
    )(hidden, norm_gain, table, float_rows, middle, mixer_part, act_pair, w_down)


def hand_over_kernel(count, pieces, *refs):
    sources, targets = refs[: len(refs) - 2 * count - 2], refs[len(refs) - 2 * count - 2 :]
    kept, arrived, left = targets[count : 2 * count], targets[2 * count], targets[2 * count + 1]
    loads, stores = [], []
    for n, (i, source, first, rows, column) in enumerate(pieces):
        at = pl.ds(first, rows)
        src = sources[source].at[at, pl.ds(column, kept[i].shape[1])]
        loads.append(copy_in(src, kept[i].at[at], arrived.at[n]))
    for n, (i, source, first, rows, column) in enumerate(pieces):
        at = pl.ds(first, rows)
        loads[n].wait()
        stores.append(copy_in(kept[i].at[at], targets[i].at[at], left.at[n]))
    for store in stores:
        store.wait()


def hand_over(arrays, wanted):
    pieces, shapes = [], []
    for i, (source, column, columns) in enumerate(wanted):
        x = arrays[source]
        height = x.shape[0]
        parts = max(1, height * columns * x.dtype.itemsize >> 18)
        parts = parts if height % (parts * 16) == 0 else 1
        rows = height // parts
        pieces += [(i, source, n * rows, rows, column) for n in range(parts)]
        shapes.append(((height, columns), x.dtype))
    return pl.pallas_call(
        functools.partial(hand_over_kernel, len(wanted), tuple(pieces)),
        out_shape=tuple(jax.ShapeDtypeStruct(*x) for x in shapes),
        in_specs=[ANY] * len(arrays),
        out_specs=(ANY,) * len(wanted),
        scratch_shapes=[pltpu.VMEM(*x) for x in shapes]
        + [pltpu.SemaphoreType.DMA((len(pieces),))] * 2,
        compiler_params=pltpu.CompilerParams(vmem_limit_bytes=16 << 20),
        name="hand_over",
    )(*arrays)


def plane_device(
    hidden,
    lengths,
    w_input,
    w_forget,
    w_gate_out,
    w_output,
    norm_gain,
    gate_gain,
    glu_gain,
    lower_table,
    w_glu_gate,
    w_glu_up,
    w_glu_down,
    cotangent,
):
    hidden, cotangent = hidden[0], cotangent[0]
    tokens = 4 * hidden.shape[0]
    gains = (norm_gain[None], gate_gain[None], glu_gain[None])
    (
        normed_half,
        cot_all,
        in_raw,
        fg_raw,
        gate_raw,
        state_b,
        out_raw,
        before,
        scale_g,
        middle,
        normed_two,
    ) = mixer_forward(
        lengths,
        hidden,
        cotangent,
        gains,
        lower_table,
        (w_input, w_forget, w_gate_out, w_output),
        0,
    )
    two_half, cot_half, act_pair, gate_pair, up_pair = glu(
        normed_two, cot_all, w_glu_gate, w_glu_up, w_glu_down, 1
    )
    d_normed_two, pair_part, down_grad = down_sum(
        *(x.reshape(2 * tokens, -1) for x in (cot_half, act_pair, two_half, gate_pair, up_pair)),
        w_glu_gate,
        w_glu_up,
        2,
    )
    pair_grad, mixer_part, float_rows = pair_sum(
        lengths,
        (hidden, cotangent),
        (gains[2], gains[1]),
        lower_table,
        scale_g,
        (d_normed_two, middle),
        pair_part,
        (w_output, w_input, w_forget, w_gate_out),
        (gate_raw, state_b, out_raw, in_raw, fg_raw, before),
        normed_half.reshape(2 * tokens, -1),
        3,
    )
    output, d_hidden, out_grad, rest_grad, *sums, d_table = final_sum(
        hidden,
        gains[0],
        lower_table,
        float_rows,
        middle,
        mixer_part,
        act_pair.reshape(2 * tokens, -1),
        w_glu_down,
        4,
    )
    width, chans, units = hidden.shape[1], w_input.shape[1], w_glu_gate.shape[1]
    block = down_grad.shape[1]
    (
        down_grad,
        gate_grad,
        up_grad,
        output,
        d_hidden,
        d_table,
        out_grad,
        in_grad,
        fg_grad,
        gt_grad,
        *sums,
    ) = hand_over(
        (down_grad, pair_grad, output, d_hidden, d_table, out_grad, rest_grad, *sums),
        (
            (0, 0, block),
            (1, 0, units),
            (1, units, units),
            (2, 0, width),
            (3, 0, width),
            (4, 0, width),
            (5, 0, block),
            (6, 0, chans),
            (6, chans, chans),
            (6, 2 * chans, chans),
            (7, 0, width),
            (8, 0, width),
            (9, 0, width),
        ),
    )
    return (
        output[None],
        d_hidden[None],
        in_grad,
        fg_grad,
        gt_grad,
        out_grad,
        sums[0][0],
        sums[2][0],
        sums[1][0],
        d_table,
        gate_grad,
        up_grad,
        down_grad,
    )


def fits_plane(mesh):
    return mesh.shape["fsdp"] == 4 and mesh.shape["seq"] % 2 == 0


def solution(mesh):
    rows_spec = P("fsdp", "seq", None)
    columns = P(None, "fsdp")
    placed = (
        rows_spec,
        P(),
        columns,
        columns,
        columns,
        P("fsdp", None),
        P(),
        P(),
        P(),
        P(),
        columns,
        columns,
        P("fsdp", None),
        rows_spec,
    )
    by_rows, by_columns = P("seq", "fsdp"), P("fsdp", "seq")
    return jax.shard_map(
        plane_device if fits_plane(mesh) else per_device,
        mesh=mesh,
        in_specs=placed,
        out_specs=(
            rows_spec,
            rows_spec,
            by_rows,
            by_rows,
            by_rows,
            by_columns,
            P(),
            P(),
            P(),
            P(),
            by_rows,
            by_rows,
            by_columns,
        ),
        check_vma=False,
    )
```

```python
import functools

import jax
import jax.numpy as jnp
from jax import lax
from jax.experimental import pallas as pl
from jax.experimental.pallas import tpu as pltpu
from jax.sharding import PartitionSpec as P

LAYER = 12
MESH = pl.DeviceIdType.MESH
F32 = jnp.float32
BF16 = jnp.bfloat16

epsilon = 1e-06

VMEM = pl.BlockSpec(memory_space=pltpu.VMEM)
ANY = pl.BlockSpec(memory_space=pl.ANY)


def lower_bound(table):
    soft = jax.nn.softmax(table, axis=0)
    totals = jnp.cumsum(soft, axis=0)
    return totals[LAYER] - totals[0]


def silu_slope(value, sigma):
    return sigma * (1.0 + value * (1.0 - sigma))


def params(collective_id, limit=56):
    return pltpu.CompilerParams(
        collective_id=collective_id, has_side_effects=True, vmem_limit_bytes=limit << 20
    )


def round_up(value, unit):
    return -(-value // unit) * unit


def plane():
    s = lax.axis_index("seq")
    f = lax.axis_index("fsdp")
    y, x = f // 2, f % 2
    fx = y * 2 + (1 - x)
    fy = (1 - y) * 2 + x
    fd = (1 - y) * 2 + (1 - x)
    return s, f, fx, fy, fd


def enter(devices):
    barrier = pltpu.get_barrier_semaphore()
    for device in devices:
        pl.semaphore_signal(barrier, inc=1, device_id=device, device_id_type=MESH)
    pl.semaphore_wait(barrier, len(devices))


def remote(src, dst, send, recv, device):
    return pltpu.make_async_remote_copy(
        src_ref=src,
        dst_ref=dst,
        send_sem=send,
        recv_sem=recv,
        device_id=device,
        device_id_type=MESH,
    )


def gather(x, small, collective_id):
    return lax.all_gather(x, "fsdp"), lax.all_gather(small, "fsdp")


def reduce_rows(p, small, collective_id):
    total = lax.psum_scatter(p, "fsdp", scatter_dimension=0, tiled=True)[0]
    return total.astype(F32), lax.psum(small, "fsdp")


def start_exchange(total, gathered, send, recv, n_seq):
    s = lax.axis_index("seq")
    f = lax.axis_index("fsdp")
    copies = []
    for k in range(1, n_seq):
        peer = lax.rem(s + k, n_seq)
        copy = remote(total, gathered.at[s], send.at[k], recv.at[k], (peer, f))
        copy.start()
        copies.append(copy)
    gathered[pl.ds(s, 1)] = total[...][None]
    return copies


def seq_peers(n_seq):
    s = lax.axis_index("seq")
    f = lax.axis_index("fsdp")
    return [(lax.rem(s + k, n_seq), f) for k in range(1, n_seq)]


def lane_blocks(groups, chans):
    return [(g, slice(c, c + 128)) for g in range(groups) for c in range(0, chans, 128)]


def forward_scan_kernel(
    n_seq, in_raw, forget_raw, bounds, keep, state_b, before, a_ref, b_ref, total, gathered, send, recv
):
    groups, rows, chans = in_raw.shape
    part = rows // 8
    blocks = lane_blocks(groups, chans)
    s = lax.axis_index("seq")
    barrier = pltpu.get_barrier_semaphore()
    for peer in seq_peers(n_seq):
        pl.semaphore_signal(barrier, inc=1, device_id=peer, device_id_type=MESH)
    for n, (g, lanes) in enumerate(blocks):
        bound = bounds[:, lanes]
        forget = bound + (1.0 - bound) * jax.nn.sigmoid(forget_raw[g, :, lanes].astype(F32))
        value = in_raw[g, :, lanes].astype(F32)
        a_ref[n] = forget * keep[g]
        b_ref[n] = value * jax.nn.sigmoid(value) * (1.0 - forget)

    def step(i, carry):
        new = []
        at = pl.ds(i, 8, stride=part)
        for n, (product, state) in enumerate(carry):
            a = a_ref[n, at, :]
            state = a * state + b_ref[n, at, :]
            product = product * a
            a_ref[n, at, :] = product
            b_ref[n, at, :] = state
            new.append((product, state))
        return tuple(new)

    start = tuple((jnp.ones((8, 128), F32), jnp.zeros((8, 128), F32)) for _ in blocks)
    ends = lax.fori_loop(0, part, step, start)
    for n, (product, state) in enumerate(ends):
        p_all, s_all = product[0:1], state[0:1]
        for j in range(1, 8):
            p_all, s_all = p_all * product[j : j + 1], state[j : j + 1] + product[j : j + 1] * s_all
        total[2 * n : 2 * n + 1] = p_all
        total[2 * n + 1 : 2 * n + 2] = s_all
    pl.semaphore_wait(barrier, n_seq - 1)
    copies = start_exchange(total, gathered, send, recv, n_seq)
    for copy in copies:
        copy.wait()
    for n, (g, lanes) in enumerate(blocks):
        carry = jnp.zeros((1, 128), F32)
        for j in range(n_seq - 1):
            p_j = gathered[j, 2 * n : 2 * n + 1]
            s_j = gathered[j, 2 * n + 1 : 2 * n + 2]
            carry = jnp.where(j < s, s_j + p_j * carry, carry)
        before[g, 0:1, lanes] = carry
        product, state = ends[n]
        carries = [carry]
        for j in range(7):
            carries.append(state[j : j + 1] + product[j : j + 1] * carries[-1])
        for j in range(8):
            at = slice(j * part, (j + 1) * part)
            b_ref[n, at] = b_ref[n, at] + a_ref[n, at] * carries[j]
        state_b[g, :, lanes] = b_ref[n].astype(BF16)
        before[g, 1:rows, lanes] = b_ref[n, 0 : rows - 1]


def forward_scan(in_raw, forget_raw, bounds, keep, collective_id):
    n_seq = lax.axis_size("seq")
    groups, rows, chans = in_raw.shape
    blocks = groups * chans // 128
    return pl.pallas_call(
        functools.partial(forward_scan_kernel, n_seq),
        out_shape=(
            jax.ShapeDtypeStruct(in_raw.shape, BF16),
            jax.ShapeDtypeStruct(in_raw.shape, F32),
        ),
        in_specs=[VMEM] * 4,
        out_specs=(VMEM, VMEM),
        scratch_shapes=[
            pltpu.VMEM((blocks, rows, 128), F32),
            pltpu.VMEM((blocks, rows, 128), F32),
            pltpu.VMEM((2 * blocks, 128), F32),
            pltpu.VMEM((n_seq, 2 * blocks, 128), F32),
            pltpu.SemaphoreType.DMA((n_seq,)),
            pltpu.SemaphoreType.DMA((n_seq,)),
        ],
        compiler_params=params(collective_id),
        name="forward_scan",
    )(in_raw, forget_raw, bounds, keep)


def backward_scan_kernel(
    n_seq,
    d_state,
    in_raw,
    forget_raw,
    before,
    bounds,
    keep,
    d_in,
    d_forget_raw,
    d_bounds,
    p_ref,
    q_ref,
    total,
    gathered,
    send,
    recv,
):
    groups, rows, chans = in_raw.shape
    part = rows // 8
    blocks = lane_blocks(groups, chans)
    s = lax.axis_index("seq")
    barrier = pltpu.get_barrier_semaphore()
    for peer in seq_peers(n_seq):
        pl.semaphore_signal(barrier, inc=1, device_id=peer, device_id_type=MESH)
    for n, (g, lanes) in enumerate(blocks):
        bound = bounds[:, lanes]
        forget = bound + (1.0 - bound) * jax.nn.sigmoid(forget_raw[g, :, lanes].astype(F32))
        p_ref[n] = forget * keep[g]
        q_ref[n] = d_state[g, :, lanes].astype(F32)

    def step(i, carry):
        new = []
        at = pl.ds(part - 1 - i, 8, stride=part)
        for n, (product, message) in enumerate(carry):
            a = p_ref[n, at, :]
            acc = q_ref[n, at, :] + message
            p_ref[n, at, :] = product
            q_ref[n, at, :] = acc
            new.append((product * a, a * acc))
        return tuple(new)

    start = tuple((jnp.ones((8, 128), F32), jnp.zeros((8, 128), F32)) for _ in blocks)
    ends = lax.fori_loop(0, part, step, start)
    for n, (product, message) in enumerate(ends):
        p_all, m_all = product[7:8], message[7:8]
        for j in range(6, -1, -1):
            p_all, m_all = p_all * product[j : j + 1], message[j : j + 1] + product[j : j + 1] * m_all
        total[2 * n : 2 * n + 1] = p_all
        total[2 * n + 1 : 2 * n + 2] = m_all
    pl.semaphore_wait(barrier, n_seq - 1)
    copies = start_exchange(total, gathered, send, recv, n_seq)
    for copy in copies:
        copy.wait()
    d_bounds[...] = jnp.zeros((1, chans), F32)
    for n, (g, lanes) in enumerate(blocks):
        carry = jnp.zeros((1, 128), F32)
        for j in range(n_seq - 1, 0, -1):
            p_j = gathered[j, 2 * n : 2 * n + 1]
            m_j = gathered[j, 2 * n + 1 : 2 * n + 2]
            carry = jnp.where(j > s, m_j + p_j * carry, carry)
        product, message = ends[n]
        carries = [carry]
        for j in range(7, 0, -1):
            carries.append(message[j : j + 1] + product[j : j + 1] * carries[-1])
        carries = carries[::-1]
        for j in range(8):
            at = slice(j * part, (j + 1) * part)
            q_ref[n, at] = q_ref[n, at] + p_ref[n, at] * carries[j]
        acc = q_ref[n]
        bound = bounds[:, lanes]
        sigma_f = jax.nn.sigmoid(forget_raw[g, :, lanes].astype(F32))
        forget = bound + (1.0 - bound) * sigma_f
        value = in_raw[g, :, lanes].astype(F32)
        sigma_i = jax.nn.sigmoid(value)
        d_forget = acc * (before[g, :, lanes] * keep[g] - value * sigma_i)
        d_in[g, :, lanes] = (acc * (1.0 - forget) * silu_slope(value, sigma_i)).astype(BF16)
        d_sigma = d_forget * (1.0 - sigma_f)
        d_forget_raw[g, :, lanes] = (d_sigma * (1.0 - bound) * sigma_f).astype(BF16)
        d_bounds[:, lanes] += jnp.sum(d_sigma, 0, keepdims=True)


def backward_scan(d_state, in_raw, forget_raw, before, bounds, keep, collective_id):
    n_seq = lax.axis_size("seq")
    groups, rows, chans = in_raw.shape
    blocks = groups * chans // 128
    return pl.pallas_call(
        functools.partial(backward_scan_kernel, n_seq),
        out_shape=(
            jax.ShapeDtypeStruct(in_raw.shape, BF16),
            jax.ShapeDtypeStruct(in_raw.shape, BF16),
            jax.ShapeDtypeStruct((1, chans), F32),
        ),
        in_specs=[VMEM] * 6,
        out_specs=(VMEM, VMEM, VMEM),
        scratch_shapes=[
            pltpu.VMEM((blocks, rows, 128), F32),
            pltpu.VMEM((blocks, rows, 128), F32),
            pltpu.VMEM((2 * blocks, 128), F32),
            pltpu.VMEM((n_seq, 2 * blocks, 128), F32),
            pltpu.SemaphoreType.DMA((n_seq,)),
            pltpu.SemaphoreType.DMA((n_seq,)),
        ],
        compiler_params=params(collective_id),
        name="backward_scan",
    )(d_state, in_raw, forget_raw, before, bounds, keep)


def sum_all_kernel(n_seq, n_fsdp, x, out, middle, over_seq, over_fsdp, send, recv):
    s = lax.axis_index("seq")
    f = lax.axis_index("fsdp")
    along = [(lax.rem(s + k, n_seq), f) for k in range(1, n_seq)]
    across = [(s, lax.rem(f + k, n_fsdp)) for k in range(1, n_fsdp)]
    enter(along + across)
    copies = []
    for k, peer in enumerate(along):
        copy = remote(x, over_seq.at[k], send.at[k], recv.at[k], peer)
        copy.start()
        copies.append(copy)
    total = x[...]
    for k, copy in enumerate(copies):
        copy.wait_recv()
        total = total + over_seq[k]
    middle[...] = total
    later = []
    for k, peer in enumerate(across):
        slot = n_seq - 1 + k
        copy = remote(middle, over_fsdp.at[k], send.at[slot], recv.at[slot], peer)
        copy.start()
        later.append(copy)
    for k, copy in enumerate(later):
        copy.wait_recv()
        total = total + over_fsdp[k]
    out[...] = total
    for copy in copies + later:
        copy.wait_send()


def sum_all(x, collective_id):
    n_seq, n_fsdp = lax.axis_size("seq"), lax.axis_size("fsdp")
    count = n_seq + n_fsdp - 2
    return pl.pallas_call(
        functools.partial(sum_all_kernel, n_seq, n_fsdp),
        out_shape=jax.ShapeDtypeStruct(x.shape, F32),
        in_specs=[VMEM],
        out_specs=VMEM,
        scratch_shapes=[
            pltpu.VMEM(x.shape, F32),
            pltpu.VMEM((n_seq - 1,) + x.shape, F32),
            pltpu.VMEM((n_fsdp - 1,) + x.shape, F32),
            pltpu.SemaphoreType.DMA((count,)),
            pltpu.SemaphoreType.DMA((count,)),
        ],
        compiler_params=params(collective_id),
        name="sum_all",
    )(x)


def sum_over_seq(part):
    return lax.psum_scatter(part.astype(BF16), "seq", scatter_dimension=0, tiled=True).astype(F32)


def per_device(
    hidden,
    lengths,
    w_input,
    w_forget,
    w_gate_out,
    w_output,
    norm_gain,
    gate_gain,
    glu_gain,
    lower_table,
    w_glu_gate,
    w_glu_up,
    w_glu_down,
    cotangent,
):
    seq_index = lax.axis_index("seq")
    fsdp_index = lax.axis_index("fsdp")
    groups = lax.axis_size("fsdp")
    _, rows, width = hidden.shape
    chans = w_input.shape[1]
    units = w_glu_gate.shape[1]
    tokens = groups * rows
    small_shape = (round_up(groups, 8), round_up(rows, 128))

    def to_small(value):
        return jnp.pad(
            value, ((0, small_shape[0] - value.shape[0]), (0, small_shape[1] - value.shape[1]))
        )

    def dot(left, right):
        return jnp.dot(left, right, preferred_element_type=F32)

    def dot_t(left, right):
        return lax.dot_general(left, right, (((1,), (1,)), ((), ())), preferred_element_type=F32)

    def over_tokens(left, right):
        return lax.dot_general(left, right, (((0,), (0,)), ((), ())), preferred_element_type=F32)

    cotangent_all = lax.all_gather(cotangent[0], "fsdp").reshape(tokens, width)

    hidden_f = hidden[0].astype(F32)
    scale_one = lax.rsqrt(jnp.mean(hidden_f * hidden_f, -1, keepdims=True) + epsilon)
    normed = (hidden_f * scale_one * norm_gain).astype(BF16)
    normed_all, _ = gather(normed, jnp.zeros((8, 128), F32), 0)
    normed_all = normed_all.reshape(tokens, width)
    in_raw = dot(normed_all, w_input).astype(BF16).reshape(groups, rows, chans)
    forget_raw = dot(normed_all, w_forget).astype(BF16).reshape(groups, rows, chans)
    gate_raw = dot(normed_all, w_gate_out)

    bounds_full = lower_bound(lower_table)
    bounds = lax.dynamic_slice_in_dim(bounds_full, fsdp_index * chans, chans)[None]
    seq_starts = jnp.cumsum(lengths, axis=1) - lengths
    places = seq_index * rows + jnp.arange(rows, dtype=jnp.int32)
    starts = jnp.any(places[None, :, None] == seq_starts[:, None, :], axis=-1)
    keep = jnp.where(starts, 0.0, 1.0).astype(F32)[:, :, None]
    state_b, before = forward_scan(in_raw, forget_raw, bounds, keep, 1)

    state_f = state_b.astype(F32).reshape(tokens, chans)
    gain_slice = lax.dynamic_slice_in_dim(gate_gain, fsdp_index * chans, chans)
    sigma_g = jax.nn.sigmoid(gate_raw)
    silu_gate = gate_raw * sigma_g
    out_raw = (state_f * gain_slice * silu_gate).astype(BF16)
    squares = jnp.sum(state_f * state_f, -1).reshape(groups, rows)
    mixed_part = dot(out_raw, w_output).astype(BF16).reshape(groups, rows, width)
    mixed_raw, square_sum = reduce_rows(mixed_part, to_small(squares), 2)
    state_scale = lax.rsqrt(square_sum[:groups, :rows] / width + epsilon)
    own_scale = lax.dynamic_slice_in_dim(state_scale, fsdp_index, 1, 0)[0][:, None]
    scale_g = state_scale.reshape(tokens, 1)
    middle = hidden_f + own_scale * mixed_raw
    scale_two = lax.rsqrt(jnp.mean(middle * middle, -1, keepdims=True) + epsilon)
    normed_two = (middle * scale_two * glu_gain).astype(BF16)
    normed_two_all, _ = gather(normed_two, jnp.zeros((8, 128), F32), 3)
    normed_two_all = normed_two_all.reshape(tokens, width)

    gate_val = dot(normed_two_all, w_glu_gate)
    up_val = dot(normed_two_all, w_glu_up)
    sigma_u = jax.nn.sigmoid(gate_val)
    silu_u = gate_val * sigma_u
    activity = (silu_u * up_val).astype(BF16)
    down_grad = sum_over_seq(over_tokens(cotangent_all, activity))
    d_act = dot_t(cotangent_all, w_glu_down)
    d_gate = (d_act * up_val * silu_slope(gate_val, sigma_u)).astype(BF16)
    d_up = (d_act * silu_u).astype(BF16)
    pair_grad = sum_over_seq(
        jnp.concatenate(
            [
                over_tokens(normed_two_all, d_gate).astype(BF16),
                over_tokens(normed_two_all, d_up).astype(BF16),
            ],
            1,
        )
    )
    d_two_part = (dot_t(d_gate, w_glu_gate) + dot_t(d_up, w_glu_up)).astype(BF16)
    no_small = jnp.zeros((8, 128), F32)
    d_normed_two, _ = reduce_rows(d_two_part.reshape(groups, rows, width), no_small, 4)
    glu_part = dot(activity, w_glu_down).astype(BF16).reshape(groups, rows, width)
    glu_result = lax.psum_scatter(glu_part, "fsdp", scatter_dimension=0, tiled=True)[0]
    output = (middle + glu_result.astype(F32)).astype(BF16)[None]

    cotangent_f = cotangent[0].astype(F32)
    scaled_two = glu_gain * d_normed_two
    d_middle = (
        cotangent_f
        + scale_two * scaled_two
        - middle * scale_two**3 * jnp.mean(scaled_two * middle, -1, keepdims=True)
    )
    d_glu_gain = jnp.sum(d_normed_two * middle * scale_two, 0)
    d_mixed = d_middle.astype(BF16)
    own_dot = jnp.sum(d_mixed.astype(F32) * mixed_raw, -1)[None]
    d_mixed_all, dots = gather(d_mixed, to_small(own_dot), 5)
    d_mixed_all = d_mixed_all.reshape(tokens, width)
    dot_rows = dots[:, 0, :rows].reshape(tokens, 1)

    d_out = dot_t(d_mixed_all, w_output)
    scaled_state = state_f * scale_g
    d_gain_slice = jnp.sum(d_out * scaled_state * silu_gate, 0)
    d_scaled = d_out * gain_slice * silu_gate
    d_gate_raw = (d_out * scaled_state * gain_slice * silu_slope(gate_raw, sigma_g)).astype(BF16)
    d_state = scale_g * d_scaled - state_f * (scale_g**3 * (dot_rows / width))
    d_state = d_state.astype(BF16).reshape(groups, rows, chans)
    d_in, d_forget_raw, d_bounds = backward_scan(
        d_state, in_raw, forget_raw, before, bounds, keep, 6
    )
    d_in = d_in.reshape(tokens, chans)
    d_forget_raw = d_forget_raw.reshape(tokens, chans)

    d_normed_part = dot_t(d_in, w_input) + dot_t(d_forget_raw, w_forget)
    d_normed_part = (d_normed_part + dot_t(d_gate_raw, w_gate_out)).astype(BF16)
    out_gate = (out_raw.astype(F32) * scale_g).astype(BF16)
    mixer_grad = sum_over_seq(
        jnp.concatenate(
            [
                over_tokens(d_mixed_all, out_gate).astype(BF16),
                over_tokens(normed_all, d_in).astype(BF16),
                over_tokens(normed_all, d_forget_raw).astype(BF16),
                over_tokens(normed_all, d_gate_raw).astype(BF16),
            ],
            1,
        )
    )
    d_normed, _ = reduce_rows(d_normed_part.reshape(groups, rows, width), no_small, 7)
    scaled_one = norm_gain * d_normed
    d_hidden = (
        d_middle
        + scale_one * scaled_one
        - hidden_f * scale_one**3 * jnp.mean(scaled_one * hidden_f, -1, keepdims=True)
    )
    d_norm_gain = jnp.sum(d_normed * hidden_f * scale_one, 0)
    d_gain_full = lax.dynamic_update_slice(
        jnp.zeros((width,), F32), d_gain_slice, (fsdp_index * chans,)
    )
    d_bounds_full = lax.dynamic_update_slice(
        jnp.zeros((width,), F32), d_bounds[0], (fsdp_index * chans,)
    )
    sums = jnp.stack([d_norm_gain, d_glu_gain, d_gain_full, d_bounds_full])
    totals = sum_all(sums.reshape(8, width // 2), 8).reshape(4, width)
    _, bounds_pull = jax.vjp(lower_bound, lower_table)
    d_table = bounds_pull(totals[3])[0]
    return (
        output,
        d_hidden.astype(BF16)[None],
        mixer_grad[:, chans : 2 * chans],
        mixer_grad[:, 2 * chans : 3 * chans],
        mixer_grad[:, 3 * chans :],
        mixer_grad[:, :chans].T,
        totals[0],
        totals[2],
        totals[1],
        d_table,
        pair_grad[:, :units],
        pair_grad[:, units:],
        down_grad.T,
    )


def copy_in(src, dst, sem):
    copy = pltpu.make_async_copy(src, dst, sem)
    copy.start()
    return copy


class Links:
    def __init__(self, send, recv):
        self.send, self.recv, self.used = send, recv, 0

    def start(self, src, dst, device):
        copy = remote(src, dst, self.send.at[self.used], self.recv.at[self.used], device)
        self.used += 1
        copy.start()
        return copy


class Locals:
    def __init__(self, sems):
        self.sems, self.used = sems, 0

    def start(self, src, dst):
        copy = copy_in(src, dst, self.sems.at[self.used])
        self.used += 1
        return copy


def row_slots(rows):
    half = rows // 2
    top = [pl.ds(k * rows, half) for k in range(4)]
    bottom = [pl.ds(k * rows + half, half) for k in range(4)]
    return top, bottom


def gather_start(links, src, dst, rows, s, fx, fy):
    half = rows // 2
    top, bottom = row_slots(rows)
    here = (pl.ds(0, half), pl.ds(half, half))
    return [
        links.start(src.at[here[0]], dst.at[top[1]], (s, fx)),
        links.start(src.at[here[1]], dst.at[bottom[2]], (s, fy)),
        links.start(src.at[here[1]], dst.at[bottom[1]], (s, fx)),
        links.start(src.at[here[0]], dst.at[top[2]], (s, fy)),
    ]


def gather_forward(links, own, dst, rows, s, fx, fy):
    top, bottom = row_slots(rows)
    own[0].wait_recv()
    on_y = links.start(dst.at[top[1]], dst.at[top[3]], (s, fy))
    own[1].wait_recv()
    on_x = links.start(dst.at[bottom[2]], dst.at[bottom[3]], (s, fx))
    return [on_y, on_x]


def gather_middle(own):
    own[2].wait_recv()
    own[3].wait_recv()


def gather_far(later):
    for copy in later:
        copy.wait_recv()


def sends_done(*lists):
    for copies in lists:
        for copy in copies:
            copy.wait_send()


def wait_all(*lists):
    for copies in lists:
        for copy in copies:
            copy.wait()


def reduce_start_far(links, part, from_x, from_y, rows, s, fx, fy):
    top, bottom = row_slots(rows)
    return [
        links.start(part.at[top[3]], from_x.at[0], (s, fx)),
        links.start(part.at[bottom[3]], from_y.at[0], (s, fy)),
    ]


def reduce_start_near(links, part, from_x, from_y, rows, s, fx, fy):
    top, bottom = row_slots(rows)
    return [
        links.start(part.at[top[1]], from_x.at[1], (s, fx)),
        links.start(part.at[bottom[2]], from_y.at[1], (s, fy)),
    ]


def reduce_pass(links, far, part, from_x, from_y, pass_x, pass_y, rows, s, fx, fy):
    top, bottom = row_slots(rows)
    far[0].wait_recv()
    pass_y[...] = (from_x[0].astype(F32) + part[top[2]].astype(F32)).astype(BF16)
    on_y = links.start(pass_y, from_y.at[2], (s, fy))
    far[1].wait_recv()
    pass_x[...] = (from_y[0].astype(F32) + part[bottom[1]].astype(F32)).astype(BF16)
    on_x = links.start(pass_x, from_x.at[2], (s, fx))
    return [on_y, on_x]


def mm(left, right):
    return jnp.dot(left, right, preferred_element_type=F32)


def mm_t(left, right):
    return lax.dot_general(left, right, (((1,), (1,)), ((), ())), preferred_element_type=F32)


def tile(n, width):
    return pl.ds(pl.multiple_of(n * width, width), width)


def bounds_slice(table, first, count):
    rows = table[:, pl.ds(pl.multiple_of(first, 128), count)]
    powers = jnp.exp(rows - jnp.max(rows, 0, keepdims=True))
    return jnp.sum(powers[1 : LAYER + 1], 0, keepdims=True) / jnp.sum(powers, 0, keepdims=True)


def keep_rows(lengths, group, first, rows):
    places = first + lax.broadcasted_iota(jnp.int32, (rows, 128), 0)
    start = jnp.int32(0)
    keep = jnp.where(places == start, 0.0, 1.0)
    for i in range(lengths.shape[1] - 1):
        start = start + lengths[group, i]
        keep = jnp.where(places == start, 0.0, keep)
    return keep.astype(F32)


def segment_totals(end_p, end_s, blocks, order):
    first, rest = order[0], order[1:]
    p_all = end_p[pl.ds(first, blocks, stride=8), :]
    s_all = end_s[pl.ds(first, blocks, stride=8), :]
    for j in rest:
        p_j = end_p[pl.ds(j, blocks, stride=8), :]
        s_all = end_s[pl.ds(j, blocks, stride=8), :] + p_j * s_all
        p_all = p_all * p_j
    return p_all, s_all


def spread_carry(carry, carr, end_p, end_s, blocks, order):
    for i, j in enumerate(order):
        carr[pl.ds(j, blocks, stride=8), :] = carry
        if i < 7:
            carry = end_s[pl.ds(j, blocks, stride=8), :] + end_p[pl.ds(j, blocks, stride=8), :] * carry


def mixer_kernel(
    n_seq,
    lengths,
    hidden,
    cot,
    norm_gain,
    gate_gain,
    glu_gain,
    table,
    w_in,
    w_fg,
    w_gt,
    w_out,
    normed_half,
    cot_out,
    in_out,
    fg_out,
    gate_out,
    state_out,
    raw_out,
    before_out,
    scale_out,
    middle,
    two,
    wv,
    wo,
    rows_all,
    stage,
    in_ref,
    fg_ref,
    gate_ref,
    a_ref,
    b_ref,
    shifted,
    keep_ref,
    end_p,
    end_s,
    carr,
    total,
    gathered,
    state_ref,
    raw_ref,
    squares,
    squares_t,
    packed,
    squares_in,
    part,
    from_x,
    from_y,
    pass_x,
    pass_y,
    send,
    recv,
    exchange_send,
    exchange_recv,
    local_sems,
):
    rows, width = hidden.shape
    chans = w_in.shape[1]
    lanes_of = [slice(c, c + 128) for c in range(0, chans, 128)]
    count = len(lanes_of)
    blocks = 4 * count
    step_len = rows // 8
    s, f, fx, fy, fd = plane()
    groups = [f, fx, fy, fd]
    links, local = Links(send, recv), Locals(local_sems)

    weights = [
        local.start(w, wv.at[:, pl.ds(i * chans, chans)]) for i, w in enumerate((w_in, w_fg, w_gt))
    ]
    weights.append(local.start(w_out, wo))
    barrier = pltpu.get_barrier_semaphore()
    peers = [(s, fx), (s, fy), (s, fd)] + seq_peers(n_seq)
    for peer in peers:
        pl.semaphore_signal(barrier, inc=1, device_id=peer, device_id_type=MESH)

    def norm_rows(i, _):
        at = pl.ds(pl.multiple_of(i * 16, 16), 16)
        value = hidden[at].astype(F32)
        scale = lax.rsqrt(jnp.mean(value * value, -1, keepdims=True) + epsilon)
        rows_all[at] = (value * scale * norm_gain[...]).astype(BF16)
        return 0

    lax.fori_loop(0, rows // 16, norm_rows, 0)
    pl.semaphore_wait(barrier, len(peers))
    own = gather_start(links, rows_all, rows_all, rows, s, fx, fy)
    bound = bounds_slice(table, f * chans, chans)
    for k in range(4):
        keep_ref[k] = keep_rows(lengths, groups[k], s * rows, rows)
    squares[...] = jnp.zeros_like(squares)
    squares_t[...] = jnp.zeros_like(squares_t)
    for copy in weights[:3]:
        copy.wait()

    def project(first, slots):
        def tile_of(n, _):
            cols = tile(n, 256)
            stage[: slots * rows, cols] = mm(
                rows_all[first * rows : (first + slots) * rows], wv[:, cols]
            )
            return 0

        lax.fori_loop(0, 3 * chans // 256, tile_of, 0)
        for k in range(slots):
            at = slice(k * rows, (k + 1) * rows)
            for c, lanes in enumerate(lanes_of):
                n = (first + k) * count + c
                value = stage[at, lanes].astype(BF16)
                in_ref[first + k, :, lanes] = value
                value = value.astype(F32)
                raw = stage[at, chans + c * 128 : chans + (c + 1) * 128].astype(BF16)
                fg_ref[first + k, :, lanes] = raw
                edge = bound[:, lanes]
                forget = edge + (1.0 - edge) * jax.nn.sigmoid(raw.astype(F32))
                a_ref[n] = forget * keep_ref[first + k]
                b_ref[n] = value * jax.nn.sigmoid(value) * (1.0 - forget)
            gate_ref[first + k] = stage[at, 2 * chans :]

    project(0, 1)
    later = gather_forward(links, own, rows_all, rows, s, fx, fy)
    gather_middle(own)
    project(1, 2)
    gather_far(later)
    cot_own = gather_start(links, cot, cot_out, rows, s, fx, fy)
    core = s % 2
    swaps, outs = swap_columns(
        links, local, rows_all, normed_half, n_seq, core, (s + 1 - 2 * core, f)
    )
    outs.append(local.start(cot, cot_out.at[pl.ds(0, rows)]))
    project(3, 1)
    outs += [
        local.start(in_ref, in_out),
        local.start(fg_ref, fg_out),
        local.start(gate_ref, gate_out),
    ]

    def scan_step(i, carry):
        new = []
        at = pl.ds(i, 8, stride=step_len)
        for n, (product, state) in enumerate(carry):
            a = a_ref[n, at, :]
            state = a * state + b_ref[n, at, :]
            product = product * a
            a_ref[n, at, :] = product
            b_ref[n, at, :] = state
            new.append((product, state))
        return tuple(new)

    start = tuple((jnp.ones((8, 128), F32), jnp.zeros((8, 128), F32)) for _ in range(blocks))
    ends = lax.fori_loop(0, step_len, scan_step, start)
    for n, (product, state) in enumerate(ends):
        end_p[8 * n : 8 * n + 8] = product
        end_s[8 * n : 8 * n + 8] = state
    p_all, s_all = segment_totals(end_p, end_s, blocks, range(8))
    total[:blocks] = p_all
    total[blocks:] = s_all
    copies = start_exchange(total, gathered, exchange_send, exchange_recv, n_seq)
    wait_all(copies)
    carry = jnp.zeros((blocks, 128), F32)
    for j in range(n_seq - 1):
        carry = jnp.where(j < s, gathered[j, blocks:] + gathered[j, :blocks] * carry, carry)
    for n in range(blocks):
        shifted[n, 0:1] = carry[n : n + 1]
    spread_carry(carry, carr, end_p, end_s, blocks, range(8))

    def finish(n, _):
        enter_state = carr[pl.ds(pl.multiple_of(n * 8, 8), 8)]
        for i in range(step_len):
            at = pl.ds(i, 8, stride=step_len)
            state = b_ref[n, at, :] + a_ref[n, at, :] * enter_state
            b_ref[n, at, :] = state
            shifted[n, pl.ds(i + 1, 8, stride=step_len), :] = state
        return 0

    lax.fori_loop(0, blocks, finish, 0)
    outs.append(local.start(shifted.at[:, pl.ds(0, rows)], before_out))

    lane = lax.broadcasted_iota(jnp.int32, (rows, 128), 1)
    for k in (3, 1, 2, 0):
        square = jnp.zeros((rows, 1), F32)
        for c, lanes in enumerate(lanes_of):
            state_b = b_ref[k * count + c].astype(BF16)
            state_ref[k, :, lanes] = state_b
            state = state_b.astype(F32)
            square = square + jnp.sum(state * state, -1, keepdims=True)
            gate = gate_ref[k, :, lanes]
            gain = gate_gain[:, pl.ds(pl.multiple_of(f * chans + c * 128, 128), 128)]
            raw_ref[k * rows : (k + 1) * rows, lanes] = (
                state * gain * gate * jax.nn.sigmoid(gate)
            ).astype(BF16)
        squares[:rows] = jnp.where(lane == groups[k], square, squares[:rows])
    packed[...] = squares[...].T[:8]
    square_copies = [
        links.start(packed, squares_in.at[i], (s, peer)) for i, peer in enumerate((fx, fy, fd))
    ]
    outs += [local.start(state_ref, state_out), local.start(raw_ref, raw_out)]
    cot_later = gather_forward(links, cot_own, cot_out, rows, s, fx, fy)
    weights[3].wait()

    def output_part(first, slots):
        at = slice(first * rows, (first + slots) * rows)

        def tile_of(n, _):
            cols = tile(n, 512)
            part[at, cols] = mm(raw_ref[at], wo[:, cols]).astype(BF16)
            return 0

        lax.fori_loop(0, width // 512, tile_of, 0)

    output_part(3, 1)
    far = reduce_start_far(links, part, from_x, from_y, rows, s, fx, fy)
    output_part(1, 2)
    near = reduce_start_near(links, part, from_x, from_y, rows, s, fx, fy)
    output_part(0, 1)
    passed = reduce_pass(links, far, part, from_x, from_y, pass_x, pass_y, rows, s, fx, fy)
    for copy in square_copies:
        copy.wait_recv()
    all_squares = (packed[...] + squares_in[0]) + (squares_in[1] + squares_in[2])
    squares_t[:8] = lax.rsqrt(all_squares / width + epsilon)
    scales = squares_t[...].T[:rows]
    for k in range(4):
        scale_out[k] = jnp.sum(jnp.where(lane == groups[k], scales, 0.0), -1, keepdims=True)
    for copy in near + passed:
        copy.wait_recv()
    half = rows // 2
    for first, one, other in ((0, from_x.at[1], from_y.at[2]), (half, from_y.at[1], from_x.at[2])):

        def sum_rows(i, _):
            here = pl.ds(pl.multiple_of(i * 16, 16), 16)
            at = pl.ds(pl.multiple_of(first + i * 16, 16), 16)
            mixed = part[at].astype(F32) + one[here].astype(F32) + other[here].astype(F32)
            value = hidden[at].astype(F32) + scale_out[0, at] * mixed
            middle[at] = value
            scale = lax.rsqrt(jnp.mean(value * value, -1, keepdims=True) + epsilon)
            two[at] = (value * scale * glu_gain[...]).astype(BF16)
            return 0

        lax.fori_loop(0, half // 16, sum_rows, 0)
    gather_middle(cot_own)
    gather_far(cot_later)
    sends_done(own, later, cot_own, cot_later, square_copies, far, near, passed)
    wait_all(swaps, outs)


def mixer_forward(lengths, hidden, cot, gains, table, weights, collective_id):
    n_seq = lax.axis_size("seq")
    rows, width = hidden.shape
    chans = weights[0].shape[1]
    blocks = 4 * chans // 128
    tokens = 4 * rows
    half = rows // 2
    shape = jax.ShapeDtypeStruct
    wide = shape((tokens, width), BF16)
    narrow = shape((4, rows, chans), BF16)
    long_rows = round_up(rows, 128)
    return pl.pallas_call(
        functools.partial(mixer_kernel, n_seq),
        out_shape=(
            shape((2, tokens, width // 2), BF16),
            wide,
            narrow,
            narrow,
            shape((4, rows, chans), F32),
            narrow,
            shape((tokens, chans), BF16),
            shape((blocks, rows, 128), F32),
            shape((4, rows, 1), F32),
            shape((rows, width), F32),
            shape((rows, width), BF16),
        ),
        in_specs=[pl.BlockSpec(memory_space=pltpu.SMEM), VMEM, VMEM, VMEM, VMEM, VMEM, VMEM]
        + [ANY] * 4,
        out_specs=(ANY,) * 8 + (VMEM,) * 3,
        scratch_shapes=[
            pltpu.VMEM((width, 3 * chans), BF16),
            pltpu.VMEM((chans, width), BF16),
            pltpu.VMEM((tokens, width), BF16),
            pltpu.VMEM((2 * rows, 3 * chans), F32),
            pltpu.VMEM((4, rows, chans), BF16),
            pltpu.VMEM((4, rows, chans), BF16),
            pltpu.VMEM((4, rows, chans), F32),
            pltpu.VMEM((blocks, rows, 128), F32),
            pltpu.VMEM((blocks, rows, 128), F32),
            pltpu.VMEM((blocks, rows + 8, 128), F32),
            pltpu.VMEM((4, rows, 128), F32),
            pltpu.VMEM((8 * blocks, 128), F32),
            pltpu.VMEM((8 * blocks, 128), F32),
            pltpu.VMEM((8 * blocks, 128), F32),
            pltpu.VMEM((2 * blocks, 128), F32),
            pltpu.VMEM((n_seq, 2 * blocks, 128), F32),
            pltpu.VMEM((4, rows, chans), BF16),
            pltpu.VMEM((tokens, chans), BF16),
            pltpu.VMEM((long_rows, 128), F32),
            pltpu.VMEM((128, long_rows), F32),
            pltpu.VMEM((8, long_rows), F32),
            pltpu.VMEM((3, 8, long_rows), F32),
            pltpu.VMEM((tokens, width), BF16),
            pltpu.VMEM((3, half, width), BF16),
            pltpu.VMEM((3, half, width), BF16),
            pltpu.VMEM((half, width), BF16),
            pltpu.VMEM((half, width), BF16),
            pltpu.SemaphoreType.DMA((21 + n_seq // 2,)),
            pltpu.SemaphoreType.DMA((21 + n_seq // 2,)),
            pltpu.SemaphoreType.DMA((n_seq,)),
            pltpu.SemaphoreType.DMA((n_seq,)),
            pltpu.SemaphoreType.DMA((11 + n_seq // 2,)),
        ],
        compiler_params=params(collective_id),
        name="mixer_forward",
    )(lengths, hidden, cot, *gains, table, *weights)


def swap_columns(links, local, src, dst, n_seq, core, mate):
    part = src.shape[1] // n_seq
    copies, stays = [], []
    for z in range(n_seq // 2):
        to = pl.ds(z * part, part)
        theirs = pl.ds(pl.multiple_of((2 * z + 1 - core) * part, part), part)
        ours = pl.ds(pl.multiple_of((2 * z + core) * part, part), part)
        copies.append(links.start(src.at[:, theirs], dst.at[1, :, to], mate))
        stays.append(local.start(src.at[:, ours], dst.at[0, :, to]))
    return copies, stays


def glu_kernel(
    n_seq,
    two,
    cot_all,
    w_gate,
    w_up,
    w_down,
    two_half,
    cot_half,
    act_pair,
    gate_pair,
    up_pair,
    wv,
    wd,
    cot_ref,
    two_ref,
    d_act,
    stage,
    act,
    d_gate,
    d_up,
    send,
    recv,
    local_sems,
):
    rows = two.shape[0]
    units = w_gate.shape[1]
    s, f, fx, fy, fd = plane()
    core = s % 2
    mate = (s + 1 - 2 * core, f)
    links, local = Links(send, recv), Locals(local_sems)
    loads = [local.start(w_down, wd), local.start(cot_all, cot_ref)]
    two_ref[:rows] = two[...]
    enter([(s, fx), (s, fy), mate])
    own = gather_start(links, two_ref, two_ref, rows, s, fx, fy)
    wait_all(loads)
    loads = [
        local.start(w_gate, wv.at[:, pl.ds(0, units)]),
        local.start(w_up, wv.at[:, pl.ds(units, units)]),
    ]
    swaps, stays = swap_columns(links, local, cot_ref, cot_half, n_seq, core, mate)

    def act_tile(n, _):
        cols = tile(n, 256)
        d_act[:, cols] = mm_t(cot_ref[...], wd[cols])
        return 0

    lax.fori_loop(0, units // 256, act_tile, 0)
    if units % 256:
        rest = slice(units // 256 * 256, units)
        d_act[:, rest] = mm_t(cot_ref[...], wd[rest])
    later = gather_forward(links, own, two_ref, rows, s, fx, fy)
    wait_all(loads)

    def slots(first, number, swap=True):
        nonlocal swaps, stays
        base = first * rows

        def tile_of(n, _):
            cols = tile(n, 256)
            stage[: number * rows, cols] = mm(two_ref[base : base + number * rows], wv[:, cols])
            return 0

        lax.fori_loop(0, 2 * units // 256, tile_of, 0)

        def rows_of(i, _):
            at = pl.ds(pl.multiple_of(i * 16, 16), 16)
            to = pl.ds(pl.multiple_of(base + i * 16, 16), 16)
            gate, up = stage[at, :units], stage[at, units:]
            sigma = jax.nn.sigmoid(gate)
            silu = gate * sigma
            act[to] = (silu * up).astype(BF16)
            d = d_act[to]
            d_gate[to] = (d * up * silu_slope(gate, sigma)).astype(BF16)
            d_up[to] = (d * silu).astype(BF16)
            return 0

        cuts = number * rows // 2
        for first_row in (0, cuts):
            lax.fori_loop(first_row // 16, (first_row + cuts) // 16, rows_of, 0)
            at = pl.ds(base + first_row, cuts)
            for src, dst in ((act, act_pair), (d_gate, gate_pair), (d_up, up_pair)):
                stays = stays + [local.start(src.at[at], dst.at[0, at])]
                if swap:
                    swaps = swaps + [links.start(src.at[at], dst.at[1, at], mate)]

    slots(0, 1)
    gather_middle(own)
    slots(1, 2)
    gather_far(later)
    more, keeps = swap_columns(links, local, two_ref, two_half, n_seq, core, mate)
    slots(3, 1, False)
    sends_done(own, later)
    wait_all(swaps, stays, more, keeps)


def glu(two, cot_all, w_gate, w_up, w_down, collective_id):
    n_seq = lax.axis_size("seq")
    rows, width = two.shape
    units = w_gate.shape[1]
    tokens = 4 * rows
    shape = jax.ShapeDtypeStruct
    half = shape((2, tokens, width // 2), BF16)
    pair = shape((2, tokens, units), BF16)
    remote_count = 6 + n_seq + 12
    return pl.pallas_call(
        functools.partial(glu_kernel, n_seq),
        out_shape=(half, half, pair, pair, pair),
        in_specs=[VMEM] + [ANY] * 4,
        out_specs=(ANY,) * 5,
        scratch_shapes=[
            pltpu.VMEM((width, 2 * units), BF16),
            pltpu.VMEM((units, width), BF16),
            pltpu.VMEM((tokens, width), BF16),
            pltpu.VMEM((tokens, width), BF16),
            pltpu.VMEM((tokens, units), F32),
            pltpu.VMEM((2 * rows, 2 * units), F32),
            pltpu.VMEM((tokens, units), BF16),
            pltpu.VMEM((tokens, units), BF16),
            pltpu.VMEM((tokens, units), BF16),
            pltpu.SemaphoreType.DMA((remote_count,)),
            pltpu.SemaphoreType.DMA((remote_count,)),
            pltpu.SemaphoreType.DMA((4 + n_seq + 18,)),
        ],
        compiler_params=params(collective_id),
        name="glu",
    )(two, cot_all, w_gate, w_up, w_down)


class ZLine:
    def __init__(self, part, buf, sems, n_seq, width, lag, ahead, store=None, leave=None):
        self.part, self.buf, self.width, self.lag, self.ahead = part, buf, width, lag, ahead
        self.send_up, self.recv_up, self.send_down, self.recv_down = sems[:4]
        self.store, self.leave = store, leave
        self.s, self.f = lax.axis_index("seq"), lax.axis_index("fsdp")
        self.n_seq, self.nz = n_seq, n_seq // 2
        self.z = self.s // 2
        self.block = part.shape[0] // self.nz
        self.chunks = part.shape[1] // width
        self.steps = (self.nz - 1) * self.chunks
        self.calls = self.steps + lag * (self.nz - 2)

    def rows(self, t):
        return pl.ds(pl.multiple_of(t * self.block, self.block), self.block)

    def move(self, up, k, j):
        t = self.nz - 1 - k if up else k
        landing = t + 1 if up else t
        cols = tile(j, self.width)
        slot = k * self.chunks + j
        peer = lax.rem(self.s + (2 if up else self.n_seq - 2), self.n_seq)
        send, recv = (
            (self.send_up, self.recv_up) if up else (self.send_down, self.recv_down)
        )
        return remote(
            self.part.at[self.rows(t), cols],
            self.buf.at[self.rows(landing), cols],
            send.at[slot],
            recv.at[slot],
            (peer, self.f),
        )

    def feed(self, q):
        inside = q < self.steps
        q = jnp.minimum(q, self.steps - 1)
        k = q // self.chunks
        j = q - k * self.chunks

        @pl.when(inside & (self.z == 0))
        def _():
            self.move(True, k, j).start()

        @pl.when(inside & (self.z == self.nz - 1))
        def _():
            self.move(False, k, j).start()

    def nth(self, i):
        return jnp.where(self.z < self.nz // 2, self.nz - 1 - i, i)

    def load(self, local, src, first, last):
        order = [self.rows(self.nth(i)) for i in range(first, last)]
        return [local.start(src.at[at], self.part.at[at]) for at in order]

    def feed_first(self):
        def step(q, _):
            self.feed(q)
            return 0

        lax.fori_loop(0, self.ahead, step, 0)

    def serve_one(self, up, q):
        z, nz = self.z, self.nz
        hops = z if up else nz - 1 - z
        q = q - self.lag * (hops - 1)
        inside = (hops >= 1) & (q >= 0) & (q < self.steps)
        q = jnp.clip(q, 0, self.steps - 1)
        k = q // self.chunks
        j = q - k * self.chunks
        left = nz - 1 - k - hops
        cols = tile(j, self.width)

        @pl.when(inside & (left >= 0))
        def _():
            self.move(up, k, j).wait_recv()

        @pl.when(inside & (left > 0))
        def _():
            t = nz - 1 - k if up else k
            landing = t + 1 if up else t
            own = self.part[self.rows(t), cols].astype(F32)
            came = self.buf[self.rows(landing), cols].astype(F32)
            self.part[self.rows(t), cols] = (own + came).astype(BF16)
            self.move(up, k, j).start()

    def serve(self, q, done=False):
        self.serve_one(True, q)
        self.serve_one(False, q)
        if done:
            j = q - (self.nz - 2) * self.chunks

            @pl.when((j >= 0) & (j < self.chunks))
            def _():
                self.finish(j)

    def serve_range(self, first, last, done=False):
        def step(q, _):
            self.feed(q + self.ahead)
            self.serve(q, done)
            return 0

        lax.fori_loop(first, last, step, 0)

    def finish(self, j):
        cols = tile(j, self.width)
        above = self.buf[self.rows(self.z), cols].astype(F32)
        below = self.buf[self.rows(self.z + 1), cols].astype(F32)
        own = self.part[self.rows(self.z), cols].astype(F32)
        own = own + jnp.where(self.z < self.nz - 1, above, 0.0)
        self.store(j, own + jnp.where(self.z > 0, below, 0.0))
        self.leave(j, True)

    def drain(self):
        for k in range(self.nz - 1):
            for up in (True, False):
                hops = self.z if up else self.nz - 1 - self.z

                @pl.when(hops < self.nz - 1 - k)
                def _():
                    def step(j, _):
                        self.move(up, k, j).wait_send()
                        return 0

                    lax.fori_loop(0, self.chunks, step, 0)

        def left(j, _):
            self.leave(j, False)
            return 0

        lax.fori_loop(0, self.chunks, left, 0)


def start_or_wait(copy, start):
    if start:
        copy.start()
    else:
        copy.wait()


def line_sems(n_seq, columns, width):
    count = (n_seq // 2 - 1) * (columns // width)
    leave = pltpu.SemaphoreType.DMA((columns // width,))
    return [pltpu.SemaphoreType.DMA((count,)) for _ in range(4)] + [leave]


def z_peers(n_seq):
    s = lax.axis_index("seq")
    f = lax.axis_index("fsdp")
    return [(lax.rem(s + 2 * k, n_seq), f) for k in range(1, n_seq // 2)]


def mm_tokens(left, right):
    return lax.dot_general(left, right, (((0,), (0,)), ((), ())), preferred_element_type=F32)


def down_kernel(
    n_seq,
    cot_half,
    act_pair,
    two_half,
    gate_pair,
    up_pair,
    w_gate,
    w_up,
    d_two_out,
    pair_part,
    down_out,
    d_two,
    cot_ref,
    act_ref,
    two_ref,
    gate_ref,
    up_ref,
    wg,
    wu,
    part,
    buf,
    rows_part,
    from_x,
    from_y,
    pass_x,
    pass_y,
    pair_ref,
    down_ref,
    send,
    recv,
    local_sems,
    *line,
):
    rows, width = d_two.shape
    units = act_pair.shape[1]
    s, f, fx, fy, fd = plane()
    links, local = Links(send, recv), Locals(local_sems)
    core = s % 2
    mate = (s + 1 - 2 * core, f)
    tokens = 4 * rows
    near_rows, far_own = pl.ds(0, 2 * tokens - rows), pl.ds(3 * rows, rows)
    far_mate = pl.ds(2 * tokens - rows, rows)
    loads = [local.start(act_pair.at[near_rows], act_ref.at[near_rows])]
    enter([(s, fx), (s, fy), mate] + z_peers(n_seq))
    swaps = [links.start(act_pair.at[far_own], act_ref.at[far_mate], mate)]

    def store(j, value):
        down_ref[tile(j, 128)] = value.T

    def leave(j, start):
        at = tile(j, 128)
        copy = pltpu.make_async_copy(down_ref.at[at], down_out.at[at], line[4].at[j])
        start_or_wait(copy, start)

    z_sum = ZLine(part, buf, line, n_seq, 128, 3, 11, store, leave)
    block = z_sum.block
    tiles_in = [
        local.start(cot_half.at[:, at], cot_ref.at[:, at])
        for at in (tile(z_sum.nth(i), block) for i in range(z_sum.nz))
    ]
    wait_all(loads, tiles_in[:1])
    swaps[0].wait_recv()
    swaps += [
        links.start(src.at[far_own], dst.at[far_mate], mate)
        for src, dst in ((gate_pair, gate_ref), (up_pair, up_ref))
    ]
    loads = [
        local.start(src, dst)
        for src, dst in (
            (w_gate, wg),
            (w_up, wu),
            (gate_pair.at[near_rows], gate_ref.at[near_rows]),
            (up_pair.at[near_rows], up_ref.at[near_rows]),
            (two_half, two_ref),
        )
    ]

    def down_tile(i, _):
        t = z_sum.nth(i)
        part[z_sum.rows(t)] = mm_tokens(cot_ref[:, tile(t, block)], act_ref[...]).astype(BF16)
        return 0

    down_tile(jnp.int32(0), 0)
    z_sum.feed_first()
    wait_all(tiles_in[1:])
    lax.fori_loop(1, z_sum.nz, down_tile, 0)
    wait_all(loads)
    for copy in swaps[1:]:
        copy.wait_recv()

    def two_part(first, slots, base):
        at = slice(first * rows, (first + slots) * rows)

        def tile_of(n, _):
            cols = tile(n, 512)
            total = mm_t(gate_ref[at], wg[cols]) + mm_t(up_ref[at], wu[cols])
            rows_part[at, cols] = total.astype(BF16)
            z_sum.feed(base + n + z_sum.ahead)
            z_sum.serve(base + n)
            return 0

        lax.fori_loop(0, width // 512, tile_of, 0)

    count = width // 512
    two_part(3, 1, 0)
    far = reduce_start_far(links, rows_part, from_x, from_y, rows, s, fx, fy)
    two_part(1, 2, count)
    near = reduce_start_near(links, rows_part, from_x, from_y, rows, s, fx, fy)
    two_part(0, 1, 2 * count)
    served = 3 * count

    def pair_tiles(right, first, base):
        def tile_of(t, _):
            pair_ref[z_sum.rows(t), pl.ds(first, units)] = mm_tokens(
                two_ref[:, tile(t, block)], right[...]
            ).astype(BF16)
            z_sum.serve_range(base + 2 * t, base + 2 * t + 2, True)
            return 0

        lax.fori_loop(0, z_sum.nz, tile_of, 0)

    pair_tiles(gate_ref, 0, served)
    served += 2 * z_sum.nz
    passed = reduce_pass(links, far, rows_part, from_x, from_y, pass_x, pass_y, rows, s, fx, fy)
    pair_tiles(up_ref, units, served)
    served += 2 * z_sum.nz
    stay = local.start(pair_ref, pair_part)
    for copy in near + passed:
        copy.wait_recv()
    half = rows // 2
    d_two[:half] = rows_part[:half].astype(F32) + from_x[1].astype(F32) + from_y[2].astype(F32)
    d_two[half:] = rows_part[half:rows].astype(F32) + from_y[1].astype(F32) + from_x[2].astype(F32)
    early = local.start(d_two, d_two_out)
    z_sum.serve_range(served, z_sum.calls, True)
    z_sum.drain()
    sends_done(swaps, far, near, passed)
    wait_all([stay, early])


def down_sum(cot_half, act_pair, two_half, gate_pair, up_pair, w_gate, w_up, collective_id):
    n_seq = lax.axis_size("seq")
    tokens, units = act_pair.shape
    width = w_gate.shape[0]
    rows = tokens // 8
    half = (rows // 2, width)
    own = cot_half.shape[1]
    block = width // n_seq
    shape = jax.ShapeDtypeStruct
    return pl.pallas_call(
        functools.partial(down_kernel, n_seq),
        out_shape=(
            shape((rows, width), F32),
            shape((own, 2 * units), BF16),
            shape((units, block), F32),
        ),
        in_specs=[ANY] * 7,
        out_specs=(ANY, ANY, ANY),
        scratch_shapes=[
            pltpu.VMEM((rows, width), F32),
            pltpu.VMEM((tokens, own), BF16),
            pltpu.VMEM((tokens, units), BF16),
            pltpu.VMEM((tokens, own), BF16),
            pltpu.VMEM((tokens, units), BF16),
            pltpu.VMEM((tokens, units), BF16),
            pltpu.VMEM((width, units), BF16),
            pltpu.VMEM((width, units), BF16),
            pltpu.VMEM((own, units), BF16),
            pltpu.VMEM((own + block, units), BF16),
            pltpu.VMEM((tokens // 2, width), BF16),
            pltpu.VMEM((3,) + half, BF16),
            pltpu.VMEM((3,) + half, BF16),
            pltpu.VMEM(half, BF16),
            pltpu.VMEM(half, BF16),
            pltpu.VMEM((own, 2 * units), BF16),
            pltpu.VMEM((units, block), F32),
            pltpu.SemaphoreType.DMA((9,)),
            pltpu.SemaphoreType.DMA((9,)),
            pltpu.SemaphoreType.DMA((8 + n_seq // 2,)),
        ]
        + line_sems(n_seq, units, 128),
        compiler_params=params(collective_id),
        name="down_sum",
    )(cot_half, act_pair, two_half, gate_pair, up_pair, w_gate, w_up)


class TotalsFromAbove:
    def __init__(self, total, gathered, send, recv, n_seq):
        self.total, self.gathered, self.send, self.recv = total, gathered, send, recv
        self.s, self.f = lax.axis_index("seq"), lax.axis_index("fsdp")
        self.nz = n_seq // 2
        self.z, self.core = self.s // 2, self.s % 2
        self.mate = (2 * self.z + 1 - self.core, self.f)

    def down(self, sender, target):
        return remote(
            self.total,
            self.gathered.at[2 * sender + self.core],
            self.send.at[target],
            self.recv.at[2 * sender + self.core],
            (2 * target + self.core, self.f),
        )

    def across(self, sender, core):
        slot = 2 * sender + core
        return remote(
            self.gathered.at[slot],
            self.gathered.at[slot],
            self.send.at[self.nz + sender],
            self.recv.at[slot],
            self.mate,
        )

    def to_mate(self, core):
        slot = 2 * self.z + core
        return remote(
            self.total,
            self.gathered.at[slot],
            self.send.at[2 * self.nz],
            self.recv.at[slot],
            self.mate,
        )

    def start(self):
        self.to_mate(self.core).start()
        for target in range(self.nz - 1):

            @pl.when(target < self.z)
            def _():
                self.down(self.z, target).start()

    def relay(self):
        for sender in range(1, self.nz):

            @pl.when(sender > self.z)
            def _():
                self.down(sender, self.z).wait_recv()
                self.across(sender, self.core).start()

    def wait(self):
        self.to_mate(1 - self.core).wait_recv()
        for sender in range(1, self.nz):

            @pl.when(sender > self.z)
            def _():
                self.across(sender, 1 - self.core).wait_recv()

    def drain(self):
        self.to_mate(self.core).wait_send()
        for z in range(self.nz):

            @pl.when(z < self.z)
            def _():
                self.down(self.z, z).wait_send()

            @pl.when(z > self.z)
            def _():
                self.across(z, self.core).wait_send()


def pair_kernel(
    n_seq,
    lengths,
    hidden,
    cot,
    glu_gain,
    gate_gain,
    table,
    scale_g,
    d_two,
    middle,
    pair_part,
    w_out,
    w_in,
    w_fg,
    w_gt,
    gate_raw,
    state_b,
    out_raw,
    in_raw,
    fg_raw,
    before_in,
    normed_half,
    pair_grad,
    mixer_part,
    rows_out,
    sums_ref,
    d_glu_gain,
    d_gain,
    d_bounds,
    d_normed,
    d_middle,
    pair_ref,
    part,
    buf,
    wo,
    wv,
    mixed_all,
    mixed_mate,
    normed_ref,
    d_proj,
    out_gate,
    gate_ref,
    state_ref,
    raw_ref,
    in_ref,
    fg_ref,
    before,
    p_ref,
    q_ref,
    stage,
    rows_part,
    from_x,
    from_y,
    pass_x,
    pass_y,
    dots,
    keep_ref,
    end_p,
    end_s,
    carr,
    total,
    gathered,
    send,
    recv,
    exchange_send,
    exchange_recv,
    local_sems,
    tile_sems,
    *line,
):
    rows, width = hidden.shape
    chans = w_in.shape[1]
    tokens = 4 * rows
    lanes_of = [slice(c, c + 128) for c in range(0, chans, 128)]
    count = len(lanes_of)
    blocks = 4 * count
    step_len = rows // 8
    s, f, fx, fy, fd = plane()
    groups = [f, fx, fy, fd]
    core = s % 2
    mate = (s + 1 - 2 * core, f)
    links, local = Links(send, recv), Locals(local_sems)

    def store(j, value):
        pair_ref[:, tile(j, 256)] = value

    def leave(j, start):
        at = tile(j, 256)
        copy = pltpu.make_async_copy(pair_ref.at[:, at], pair_grad.at[:, at], line[4].at[j])
        start_or_wait(copy, start)

    z_sum = ZLine(part, buf, line, n_seq, 256, 2, 7, store, leave)
    blocks_in = z_sum.load(local, pair_part, 0, 1)
    rows_in = [local.start(d_two, d_middle), local.start(middle, d_normed)]
    enter([(s, fx), (s, fy), (s, fd)] + seq_peers(n_seq))
    blocks_in[0].wait()
    z_sum.feed_first()
    blocks_in = z_sum.load(local, pair_part, 1, z_sum.nz)
    loads = [local.start(w_out, wo)]
    loads += [
        local.start(src, dst)
        for src, dst in (
            (gate_raw, gate_ref),
            (state_b, state_ref),
            (out_raw, raw_ref),
            (in_raw, in_ref),
            (fg_raw, fg_ref),
            (before_in, before),
        )
    ]
    weights = [
        local.start(w, wv.at[:, pl.ds(i * chans, chans)]) for i, w in enumerate((w_in, w_fg, w_gt))
    ]
    weights.append(local.start(normed_half, normed_ref))
    served = 0

    def serve(number):
        nonlocal served
        z_sum.serve_range(served, served + number)
        served += number

    d_glu_gain[...] = jnp.zeros_like(d_glu_gain)
    wait_all(rows_in, blocks_in)

    def middle_rows(i, _):
        at = pl.ds(pl.multiple_of(i * 16, 16), 16)
        value, came = d_normed[at], d_middle[at]
        scale = lax.rsqrt(jnp.mean(value * value, -1, keepdims=True) + epsilon)
        scaled = glu_gain[...] * came
        mean = jnp.mean(scaled * value, -1, keepdims=True)
        grad = cot[at].astype(F32) + scale * scaled - value * (scale**3 * mean)
        d_middle[at] = grad
        grad_b = grad.astype(BF16)
        mixed_all[at] = grad_b
        own_dot = jnp.sum(
            grad_b.astype(F32) * (value - hidden[at].astype(F32)), -1, keepdims=True
        )
        dots[0, at] = jnp.broadcast_to(own_dot, (16, 128))
        d_glu_gain[...] += jnp.sum(came * value * scale, 0, keepdims=True)
        return 0

    lax.fori_loop(0, rows // 16, middle_rows, 0)
    outs = [local.start(d_middle, rows_out.at[pl.ds(rows, rows)])]
    own = gather_start(links, mixed_all, mixed_all, rows, s, fx, fy)
    dot_copies = [
        links.start(dots.at[0], dots.at[k], (s, peer)) for k, peer in ((1, fx), (2, fy), (3, fd))
    ]
    bound = bounds_slice(table, f * chans, chans)
    for k in range(4):
        keep_ref[k] = keep_rows(lengths, groups[k], s * rows, rows)
    d_gain[...] = jnp.zeros_like(d_gain)
    serve(1)
    for copy in loads:
        copy.wait()

    def out_rows(first, slots):
        stage[: slots * rows] = mm_t(mixed_all[first * rows : (first + slots) * rows], wo[...])
        for i in range(slots):
            k = first + i
            scale = scale_g[k]
            for c, lanes in enumerate(lanes_of):
                n = k * count + c
                gain = gate_gain[:, pl.ds(pl.multiple_of(f * chans + c * 128, 128), 128)]
                d_out = stage[i * rows : (i + 1) * rows, lanes]
                gate = gate_ref[k, :, lanes]
                sigma = jax.nn.sigmoid(gate)
                silu = gate * sigma
                state = state_ref[k, :, lanes].astype(F32)
                weighed = d_out * (state * scale)
                d_gain[:, lanes] += jnp.sum(weighed * silu, 0, keepdims=True)
                at = slice(k * rows, (k + 1) * rows)
                d_proj[at, 2 * chans + c * 128 : 2 * chans + (c + 1) * 128] = (
                    weighed * gain * silu_slope(gate, sigma)
                ).astype(BF16)
                out_gate[at, lanes] = (raw_ref[at, lanes].astype(F32) * scale).astype(BF16)
                d_state = scale * (d_out * gain * silu) - state * (
                    scale * scale * (dots[k] / width)
                )
                q_ref[n] = d_state.astype(BF16).astype(F32)
                edge = bound[:, lanes]
                forget = edge + (1.0 - edge) * jax.nn.sigmoid(fg_ref[k, :, lanes].astype(F32))
                p_ref[n] = forget * keep_ref[k]

    out_rows(0, 1)
    later = gather_forward(links, own, mixed_all, rows, s, fx, fy)
    serve(2)
    gather_middle(own)
    for copy in dot_copies:
        copy.wait_recv()
    out_rows(1, 2)
    serve(3)
    gather_far(later)
    out_rows(3, 1)
    serve(2)
    own_rows, mate_rows = pl.ds(0, tokens), pl.ds(tokens, tokens)
    last = pl.ds(2 * chans, chans)
    swaps = [
        links.start(out_gate.at[own_rows], out_gate.at[mate_rows], mate),
        links.start(d_proj.at[own_rows, last], d_proj.at[mate_rows, last], mate),
    ]
    wide = z_sum.block
    for t in range(n_seq // 2):
        theirs = pl.ds(pl.multiple_of((2 * t + 1 - core) * wide, wide), wide)
        swaps.append(
            links.start(mixed_all.at[:, theirs], mixed_mate.at[:, pl.ds(t * wide, wide)], mate)
        )

    def scan_step(i, carry):
        new = []
        at = pl.ds(step_len - 1 - i, 8, stride=step_len)
        for n, (product, message) in enumerate(carry):
            a = p_ref[n, at, :]
            acc = q_ref[n, at, :] + message
            p_ref[n, at, :] = product
            q_ref[n, at, :] = acc
            new.append((product * a, a * acc))
        return tuple(new)

    start = tuple((jnp.ones((8, 128), F32), jnp.zeros((8, 128), F32)) for _ in range(blocks))
    ends = lax.fori_loop(0, step_len, scan_step, start)
    for n, (product, message) in enumerate(ends):
        end_p[8 * n : 8 * n + 8] = product
        end_s[8 * n : 8 * n + 8] = message
    p_all, s_all = segment_totals(end_p, end_s, blocks, range(7, -1, -1))
    total[:blocks] = p_all
    total[blocks:] = s_all
    above = TotalsFromAbove(total, gathered, exchange_send, exchange_recv, n_seq)
    above.start()
    serve(2)
    above.relay()
    serve(2)
    above.wait()
    carry = jnp.zeros((blocks, 128), F32)
    for j in range(n_seq - 1, 0, -1):
        carry = jnp.where(j > s, gathered[j, blocks:] + gathered[j, :blocks] * carry, carry)
    spread_carry(carry, carr, end_p, end_s, blocks, range(7, -1, -1))

    def finish(n, _):
        enter_state = carr[pl.ds(pl.multiple_of(n * 8, 8), 8)]
        for i in range(step_len):
            at = pl.ds(i, 8, stride=step_len)
            q_ref[n, at, :] = q_ref[n, at, :] + p_ref[n, at, :] * enter_state
        return 0

    lax.fori_loop(0, blocks, finish, 0)
    d_bounds[...] = jnp.zeros_like(d_bounds)
    for k in range(4):
        at = slice(k * rows, (k + 1) * rows)
        for c, lanes in enumerate(lanes_of):
            acc = q_ref[k * count + c]
            edge = bound[:, lanes]
            sigma_f = jax.nn.sigmoid(fg_ref[k, :, lanes].astype(F32))
            forget = edge + (1.0 - edge) * sigma_f
            value = in_ref[k, :, lanes].astype(F32)
            sigma_i = jax.nn.sigmoid(value)
            d_forget = acc * (before[k * count + c] * keep_ref[k] - value * sigma_i)
            d_proj[at, lanes] = (acc * (1.0 - forget) * silu_slope(value, sigma_i)).astype(BF16)
            d_sigma = d_forget * (1.0 - sigma_f)
            d_proj[at, chans + c * 128 : chans + (c + 1) * 128] = (
                d_sigma * (1.0 - edge) * sigma_f
            ).astype(BF16)
            d_bounds[:, lanes] += jnp.sum(d_sigma, 0, keepdims=True)
    first = pl.ds(0, 2 * chans)
    swaps.append(links.start(d_proj.at[own_rows, first], d_proj.at[mate_rows, first], mate))
    serve(2)
    for copy in weights:
        copy.wait()

    def normed_part(first_slot, slots):
        at = slice(first_slot * rows, (first_slot + slots) * rows)

        def tile_of(n, _):
            cols = tile(n, 512)
            rows_part[at, cols] = mm_t(d_proj[at], wv[cols]).astype(BF16)
            return 0

        lax.fori_loop(0, width // 512, tile_of, 0)

    normed_part(3, 1)
    far = reduce_start_far(links, rows_part, from_x, from_y, rows, s, fx, fy)
    normed_part(1, 2)
    near = reduce_start_near(links, rows_part, from_x, from_y, rows, s, fx, fy)
    normed_part(0, 1)
    serve(3)
    for copy in swaps:
        copy.wait_recv()

    def tile_out(t):
        slot = lax.rem(t, 2)
        return pltpu.make_async_copy(
            wo.at[tile(slot, wide)], mixer_part.at[z_sum.rows(t)], tile_sems.at[slot]
        )

    def mixer_tile(t, _):
        @pl.when(t >= 2)
        def _():
            tile_out(t - 2).wait()

        at = tile(lax.rem(t, 2), wide)
        ours = mixed_all[:, tile(2 * t + core, wide)]
        out_part = mm_tokens(ours, out_gate[:tokens])
        out_part = out_part + mm_tokens(mixed_mate[:, tile(t, wide)], out_gate[tokens:])
        wo[at, :chans] = out_part.astype(BF16)
        wo[at, chans:] = mm_tokens(normed_ref[:, tile(t, wide)], d_proj[...]).astype(BF16)
        tile_out(t).start()
        return 0

    lax.fori_loop(0, 1, mixer_tile, 0)
    passed = reduce_pass(links, far, rows_part, from_x, from_y, pass_x, pass_y, rows, s, fx, fy)
    serve(2)
    lax.fori_loop(1, z_sum.nz, mixer_tile, 0)
    serve(3)
    for copy in near + passed:
        copy.wait_recv()
    half = rows // 2
    d_normed[:half] = rows_part[:half].astype(F32) + from_x[1].astype(F32) + from_y[2].astype(F32)
    d_normed[half:] = (
        rows_part[half:rows].astype(F32) + from_y[1].astype(F32) + from_x[2].astype(F32)
    )
    outs.append(local.start(d_normed, rows_out.at[pl.ds(0, rows)]))
    sums_ref[...] = jnp.zeros_like(sums_ref)
    sums_ref[0:1] = d_glu_gain[...]
    sums_ref[1:2, :chans] = d_gain[...]
    sums_ref[2:3, :chans] = d_bounds[...]
    outs.append(local.start(sums_ref, rows_out.at[pl.ds(2 * rows, 8)]))
    z_sum.serve_range(served, z_sum.calls, True)
    z_sum.drain()
    above.drain()
    sends_done(own, later, dot_copies, swaps, far, near, passed)
    for t in range(z_sum.nz - 2, z_sum.nz):
        tile_out(jnp.int32(t)).wait()
    wait_all(outs)


def pair_sum(
    lengths, own_rows, gains, table, scale_g, float_rows, pair_part, weights, saved, normed_half, cid
):
    n_seq = lax.axis_size("seq")
    rows, width = own_rows[0].shape
    chans = weights[1].shape[1]
    own, columns = pair_part.shape
    tokens = 4 * rows
    blocks = 4 * chans // 128
    block = width // n_seq
    half = (rows // 2, width)
    shape = jax.ShapeDtypeStruct
    count = 18 + n_seq // 2
    return pl.pallas_call(
        functools.partial(pair_kernel, n_seq),
        out_shape=(
            shape((block, columns), F32),
            shape((own, 4 * chans), BF16),
            shape((2 * rows + 8, width), F32),
        ),
        in_specs=[pl.BlockSpec(memory_space=pltpu.SMEM)] + [VMEM] * 6 + [ANY] * 14,
        out_specs=(ANY,) * 3,
        scratch_shapes=[
            pltpu.VMEM((8, width), F32),
            pltpu.VMEM((1, width), F32),
            pltpu.VMEM((1, chans), F32),
            pltpu.VMEM((1, chans), F32),
            pltpu.VMEM((rows, width), F32),
            pltpu.VMEM((rows, width), F32),
            pltpu.VMEM((block, columns), F32),
            pltpu.VMEM((own, columns), BF16),
            pltpu.VMEM((own + block, columns), BF16),
            pltpu.VMEM((chans, width), BF16),
            pltpu.VMEM((width, 3 * chans), BF16),
            pltpu.VMEM((tokens, width), BF16),
            pltpu.VMEM((tokens, width // 2), BF16),
            pltpu.VMEM((2 * tokens, width // 2), BF16),
            pltpu.VMEM((2 * tokens, 3 * chans), BF16),
            pltpu.VMEM((2 * tokens, chans), BF16),
            pltpu.VMEM((4, rows, chans), F32),
            pltpu.VMEM((4, rows, chans), BF16),
            pltpu.VMEM((tokens, chans), BF16),
            pltpu.VMEM((4, rows, chans), BF16),
            pltpu.VMEM((4, rows, chans), BF16),
            pltpu.VMEM((blocks, rows, 128), F32),
            pltpu.VMEM((blocks, rows, 128), F32),
            pltpu.VMEM((blocks, rows, 128), F32),
            pltpu.VMEM((2 * rows, chans), F32),
            pltpu.VMEM((tokens, width), BF16),
            pltpu.VMEM((3,) + half, BF16),
            pltpu.VMEM((3,) + half, BF16),
            pltpu.VMEM(half, BF16),
            pltpu.VMEM(half, BF16),
            pltpu.VMEM((4, rows, 128), F32),
            pltpu.VMEM((4, rows, 128), F32),
            pltpu.VMEM((8 * blocks, 128), F32),
            pltpu.VMEM((8 * blocks, 128), F32),
            pltpu.VMEM((8 * blocks, 128), F32),
            pltpu.VMEM((2 * blocks, 128), F32),
            pltpu.VMEM((n_seq, 2 * blocks, 128), F32),
            pltpu.SemaphoreType.DMA((count,)),
            pltpu.SemaphoreType.DMA((count,)),
            pltpu.SemaphoreType.DMA((n_seq + 1,)),
            pltpu.SemaphoreType.DMA((n_seq,)),
            pltpu.SemaphoreType.DMA((16 + n_seq // 2,)),
            pltpu.SemaphoreType.DMA((2,)),
        ]
        + line_sems(n_seq, columns, 256),
        compiler_params=params(cid),
        name="pair_sum",
    )(
        lengths,
        *own_rows,
        *gains,
        table,
        scale_g,
        *float_rows,
        pair_part,
        *weights,
        *saved,
        normed_half,
    )


def final_kernel(
    n_seq,
    n_fsdp,
    hidden,
    norm_gain,
    table,
    float_rows,
    middle_in,
    mixer_part,
    act_pair,
    w_down,
    output_out,
    d_hidden_out,
    out_grad,
    rest_grad,
    norm_out,
    glu_out,
    gate_out,
    d_table,
    sums_ref,
    d_normed,
    d_middle,
    middle,
    output,
    d_hidden,
    out_ref,
    rest_ref,
    part,
    buf,
    act,
    wd,
    rows_part,
    from_x,
    from_y,
    pass_x,
    pass_y,
    norm_sum,
    bounds_out,
    terms,
    quarters_in,
    terms_q,
    from_mate,
    terms_chip,
    over_seq,
    along_sum,
    over_fsdp,
    send,
    recv,
    local_sems,
    *line,
):
    rows, width = hidden.shape
    chans = out_grad.shape[0]
    tokens = 4 * rows
    s, f, fx, fy, fd = plane()
    links, local = Links(send, recv), Locals(local_sems)
    head = chans // 256

    def store(j, value):
        @pl.when(j < head)
        def _():
            out_ref[tile(j, 256)] = value.T

        @pl.when(j >= head)
        def _():
            rest_ref[:, tile(j - head, 256)] = value

    def leave(j, start):
        @pl.when(j < head)
        def _():
            at = tile(j, 256)
            copy = pltpu.make_async_copy(out_ref.at[at], out_grad.at[at], line[4].at[j])
            start_or_wait(copy, start)

        @pl.when(j >= head)
        def _():
            at = tile(j - head, 256)
            copy = pltpu.make_async_copy(rest_ref.at[:, at], rest_grad.at[:, at], line[4].at[j])
            start_or_wait(copy, start)

    z_sum = ZLine(part, buf, line, n_seq, 256, 2, 6, store, leave)
    blocks_in = z_sum.load(local, mixer_part, 0, 1)
    along = seq_peers(n_seq)
    across = [(s, fx), (s, fy), (s, fd)]
    enter(across + along)
    blocks_in[0].wait()
    z_sum.feed_first()
    loads = [local.start(act_pair.at[pl.ds(0, tokens)], act), local.start(w_down, wd)]
    blocks_in = z_sum.load(local, mixer_part, 1, z_sum.nz)
    rows_in = [
        local.start(src, dst)
        for src, dst in (
            (float_rows.at[pl.ds(0, rows)], d_normed),
            (float_rows.at[pl.ds(rows, rows)], d_middle),
            (float_rows.at[pl.ds(2 * rows, 8)], sums_ref),
            (middle_in, middle),
        )
    ]
    served = 0

    def serve(number):
        nonlocal served
        z_sum.serve_range(served, served + number)
        served += number

    norm_sum[...] = jnp.zeros_like(norm_sum)

    def hidden_rows(i, _):
        at = pl.ds(pl.multiple_of(i * 16, 16), 16)
        value, came = hidden[at].astype(F32), d_normed[at]
        scale = lax.rsqrt(jnp.mean(value * value, -1, keepdims=True) + epsilon)
        scaled = norm_gain[...] * came
        mean = jnp.mean(scaled * value, -1, keepdims=True)
        d_hidden[at] = (d_middle[at] + scale * scaled - value * (scale**3 * mean)).astype(BF16)
        norm_sum[...] += jnp.sum(came * value * scale, 0, keepdims=True)
        return 0

    wait_all(loads)

    def glu_part(first, slots):
        at = slice(first * rows, (first + slots) * rows)

        def tile_of(n, _):
            cols = tile(n, 512)
            rows_part[at, cols] = mm(act[at], wd[:, cols]).astype(BF16)
            return 0

        lax.fori_loop(0, width // 512, tile_of, 0)

    glu_part(3, 1)
    far = reduce_start_far(links, rows_part, from_x, from_y, rows, s, fx, fy)
    glu_part(1, 2)
    near = reduce_start_near(links, rows_part, from_x, from_y, rows, s, fx, fy)
    glu_part(0, 1)
    wait_all(blocks_in, rows_in)
    serve(2)
    lax.fori_loop(0, rows // 16, hidden_rows, 0)
    terms[...] = jnp.zeros_like(terms)
    for q in range(4):
        terms[q, 0:1] = norm_sum[:, q * chans : (q + 1) * chans]
        terms[q, 1:2] = sums_ref[0:1, q * chans : (q + 1) * chans]
    quarter_copies = [
        links.start(terms.at[peer], quarters_in.at[k], (s, peer))
        for k, peer in enumerate((fx, fy, fd))
    ]
    serve(1)
    passed = reduce_pass(links, far, rows_part, from_x, from_y, pass_x, pass_y, rows, s, fx, fy)
    serve(2)
    quarter = terms[pl.ds(f, 1)][0]
    for k, copy in enumerate(quarter_copies):
        copy.wait_recv()
        quarter = quarter + quarters_in[k]
    half = chans // 2
    for first, cols in ((0, slice(0, half)), (4, slice(half, chans))):
        terms_q[first : first + 2] = quarter[:2, cols]
        terms_q[first + 2 : first + 3] = sums_ref[1:2, cols]
        terms_q[first + 3 : first + 4] = sums_ref[2:3, cols]
    mate_copy = links.start(terms_q, from_mate, (s + 1 - 2 * (s % 2), f))
    serve(3)
    serve(2)
    for copy in near + passed:
        copy.wait_recv()
    middle_half = rows // 2
    for first, one, other in (
        (0, from_x.at[1], from_y.at[2]),
        (middle_half, from_y.at[1], from_x.at[2]),
    ):
        at = slice(first, first + middle_half)
        added = rows_part[at].astype(F32) + one[...].astype(F32) + other[...].astype(F32)
        output[at] = (middle[at] + added).astype(BF16)
    mate_copy.wait_recv()
    terms_chip[...] = terms_q[...] + from_mate[...]
    seq_copies = [
        links.start(terms_chip, over_seq.at[k], peer) for k, peer in enumerate(z_peers(n_seq))
    ]
    serve(3)
    total = terms_chip[...]
    for k, copy in enumerate(seq_copies):
        copy.wait_recv()
        total = total + over_seq[k]
    along_sum[...] = total
    fsdp_copies = [links.start(along_sum, over_fsdp.at[k], peer) for k, peer in enumerate(across)]
    serve(3)
    for copy in fsdp_copies:
        copy.wait_recv()
    for k, group in enumerate((f, fx, fy, fd)):
        total = along_sum[...] if k == 0 else over_fsdp[k - 1]
        for i in range(2):
            at = pl.ds(pl.multiple_of(group * chans + i * half, 128), half)
            for r, out in enumerate((norm_out, glu_out, gate_out, bounds_out)):
                out[:, at] = total[4 * i + r : 4 * i + r + 1]
    powers = jnp.exp(table[...] - jnp.max(table[...], 0, keepdims=True))
    soft = powers / jnp.sum(powers, 0, keepdims=True)
    row = lax.broadcasted_iota(jnp.int32, soft.shape, 0)
    chosen = jnp.where((row >= 1) & (row <= LAYER), 1.0, 0.0)
    bound = jnp.sum(soft * chosen, 0, keepdims=True)
    d_table[...] = soft * (chosen - bound) * bounds_out[...]
    outs = [local.start(output, output_out), local.start(d_hidden, d_hidden_out)]
    z_sum.serve_range(served, z_sum.calls, True)
    z_sum.drain()
    wait_all(outs)
    sends_done(far, near, passed, quarter_copies, [mate_copy], seq_copies, fsdp_copies)


def final_sum(hidden, norm_gain, table, float_rows, middle, mixer_part, act_pair, w_down, cid):
    n_seq, n_fsdp = lax.axis_size("seq"), lax.axis_size("fsdp")
    rows, width = hidden.shape
    own, columns = mixer_part.shape
    units = w_down.shape[0]
    chans = columns // 4
    tokens = 4 * rows
    block = width // n_seq
    half = (rows // 2, width)
    terms = (8, chans // 2)
    shape = jax.ShapeDtypeStruct
    count = 6 + n_seq // 2 + 2 * (n_fsdp - 1)
    return pl.pallas_call(
        functools.partial(final_kernel, n_seq, n_fsdp),
        out_shape=(
            shape((rows, width), BF16),
            shape((rows, width), BF16),
            shape((chans, block), F32),
            shape((block, 3 * chans), F32),
            shape((1, width), F32),
            shape((1, width), F32),
            shape((1, width), F32),
            shape(table.shape, F32),
        ),
        in_specs=[VMEM] * 3 + [ANY] * 5,
        out_specs=(ANY,) * 4 + (VMEM,) * 4,
        scratch_shapes=[
            pltpu.VMEM((8, width), F32),
            pltpu.VMEM((rows, width), F32),
            pltpu.VMEM((rows, width), F32),
            pltpu.VMEM((rows, width), F32),
            pltpu.VMEM((rows, width), BF16),
            pltpu.VMEM((rows, width), BF16),
            pltpu.VMEM((chans, block), F32),
            pltpu.VMEM((block, 3 * chans), F32),
            pltpu.VMEM((own, columns), BF16),
            pltpu.VMEM((own + block, columns), BF16),
            pltpu.VMEM((tokens, units), BF16),
            pltpu.VMEM((units, width), BF16),
            pltpu.VMEM((tokens, width), BF16),
            pltpu.VMEM((3,) + half, BF16),
            pltpu.VMEM((3,) + half, BF16),
            pltpu.VMEM(half, BF16),
            pltpu.VMEM(half, BF16),
            pltpu.VMEM((1, width), F32),
            pltpu.VMEM((1, width), F32),
            pltpu.VMEM((n_fsdp, 8, chans), F32),
            pltpu.VMEM((n_fsdp - 1, 8, chans), F32),
            pltpu.VMEM(terms, F32),
            pltpu.VMEM(terms, F32),
            pltpu.VMEM(terms, F32),
            pltpu.VMEM((n_seq // 2 - 1,) + terms, F32),
            pltpu.VMEM(terms, F32),
            pltpu.VMEM((n_fsdp - 1,) + terms, F32),
            pltpu.SemaphoreType.DMA((count,)),
            pltpu.SemaphoreType.DMA((count,)),
            pltpu.SemaphoreType.DMA((8 + n_seq // 2,)),
        ]
        + line_sems(n_seq, columns, 256),
        compiler_params=params(cid, 48),
        name="final_sum",
    )(hidden, norm_gain, table, float_rows, middle, mixer_part, act_pair, w_down)


def hand_over_kernel(count, pieces, *refs):
    sources, targets = refs[: len(refs) - 2 * count - 2], refs[len(refs) - 2 * count - 2 :]
    kept, arrived, left = targets[count : 2 * count], targets[2 * count], targets[2 * count + 1]
    loads, stores = [], []
    for n, (i, source, first, rows, column) in enumerate(pieces):
        at = pl.ds(first, rows)
        src = sources[source].at[at, pl.ds(column, kept[i].shape[1])]
        loads.append(copy_in(src, kept[i].at[at], arrived.at[n]))
    for n, (i, source, first, rows, column) in enumerate(pieces):
        at = pl.ds(first, rows)
        loads[n].wait()
        stores.append(copy_in(kept[i].at[at], targets[i].at[at], left.at[n]))
    for store in stores:
        store.wait()


def hand_over(arrays, wanted):
    pieces, shapes = [], []
    for i, (source, column, columns) in enumerate(wanted):
        x = arrays[source]
        height = x.shape[0]
        parts = max(1, height * columns * x.dtype.itemsize >> 18)
        parts = parts if height % (parts * 16) == 0 else 1
        rows = height // parts
        pieces += [(i, source, n * rows, rows, column) for n in range(parts)]
        shapes.append(((height, columns), x.dtype))
    return pl.pallas_call(
        functools.partial(hand_over_kernel, len(wanted), tuple(pieces)),
        out_shape=tuple(jax.ShapeDtypeStruct(*x) for x in shapes),
        in_specs=[ANY] * len(arrays),
        out_specs=(ANY,) * len(wanted),
        scratch_shapes=[pltpu.VMEM(*x) for x in shapes]
        + [pltpu.SemaphoreType.DMA((len(pieces),))] * 2,
        compiler_params=pltpu.CompilerParams(vmem_limit_bytes=16 << 20),
        name="hand_over",
    )(*arrays)


def plane_device(
    hidden,
    lengths,
    w_input,
    w_forget,
    w_gate_out,
    w_output,
    norm_gain,
    gate_gain,
    glu_gain,
    lower_table,
    w_glu_gate,
    w_glu_up,
    w_glu_down,
    cotangent,
):
    hidden, cotangent = hidden[0], cotangent[0]
    tokens = 4 * hidden.shape[0]
    gains = (norm_gain[None], gate_gain[None], glu_gain[None])
    (
        normed_half,
        cot_all,
        in_raw,
        fg_raw,
        gate_raw,
        state_b,
        out_raw,
        before,
        scale_g,
        middle,
        normed_two,
    ) = mixer_forward(
        lengths,
        hidden,
        cotangent,
        gains,
        lower_table,
        (w_input, w_forget, w_gate_out, w_output),
        0,
    )
    two_half, cot_half, act_pair, gate_pair, up_pair = glu(
        normed_two, cot_all, w_glu_gate, w_glu_up, w_glu_down, 1
    )
    d_normed_two, pair_part, down_grad = down_sum(
        *(x.reshape(2 * tokens, -1) for x in (cot_half, act_pair, two_half, gate_pair, up_pair)),
        w_glu_gate,
        w_glu_up,
        2,
    )
    pair_grad, mixer_part, float_rows = pair_sum(
        lengths,
        (hidden, cotangent),
        (gains[2], gains[1]),
        lower_table,
        scale_g,
        (d_normed_two, middle),
        pair_part,
        (w_output, w_input, w_forget, w_gate_out),
        (gate_raw, state_b, out_raw, in_raw, fg_raw, before),
        normed_half.reshape(2 * tokens, -1),
        3,
    )
    output, d_hidden, out_grad, rest_grad, *sums, d_table = final_sum(
        hidden,
        gains[0],
        lower_table,
        float_rows,
        middle,
        mixer_part,
        act_pair.reshape(2 * tokens, -1),
        w_glu_down,
        4,
    )
    width, chans, units = hidden.shape[1], w_input.shape[1], w_glu_gate.shape[1]
    block = down_grad.shape[1]
    (
        down_grad,
        gate_grad,
        up_grad,
        output,
        d_hidden,
        d_table,
        out_grad,
        in_grad,
        fg_grad,
        gt_grad,
        *sums,
    ) = hand_over(
        (down_grad, pair_grad, output, d_hidden, d_table, out_grad, rest_grad, *sums),
        (
            (0, 0, block),
            (1, 0, units),
            (1, units, units),
            (2, 0, width),
            (3, 0, width),
            (4, 0, width),
            (5, 0, block),
            (6, 0, chans),
            (6, chans, chans),
            (6, 2 * chans, chans),
            (7, 0, width),
            (8, 0, width),
            (9, 0, width),
        ),
    )
    return (
        output[None],
        d_hidden[None],
        in_grad,
        fg_grad,
        gt_grad,
        out_grad,
        sums[0][0],
        sums[2][0],
        sums[1][0],
        d_table,
        gate_grad,
        up_grad,
        down_grad,
    )


def fits_plane(mesh):
    return mesh.shape["fsdp"] == 4 and mesh.shape["seq"] % 2 == 0


def solution(mesh):
    rows_spec = P("fsdp", "seq", None)
    columns = P(None, "fsdp")
    placed = (
        rows_spec,
        P(),
        columns,
        columns,
        columns,
        P("fsdp", None),
        P(),
        P(),
        P(),
        P(),
        columns,
        columns,
        P("fsdp", None),
        rows_spec,
    )
    by_rows, by_columns = P("seq", "fsdp"), P("fsdp", "seq")
    return jax.shard_map(
        plane_device if fits_plane(mesh) else per_device,
        mesh=mesh,
        in_specs=placed,
        out_specs=(
            rows_spec,
            rows_spec,
            by_rows,
            by_rows,
            by_rows,
            by_columns,
            P(),
            P(),
            P(),
            P(),
            by_rows,
            by_rows,
            by_columns,
        ),
        check_vma=False,
    )
```
